32 devices in a mesh: clip: 4 (over x, core), seq: 8 (over z, y).
Axes of the slice: x: 2, y: 2, z: 4, core: 2. Of those that a mesh axis runs over, the one named last changes fastest.
Arguments:
- tokens: bfloat16 [8, 1024, 768], P('clip', 'seq'), may hold values from -6 to 6
- lengths: int32 [8], P('clip'), may hold values from 716 to 1024, as said below
- attn_in: bfloat16 [2, 768, 2304], replicated, may hold values from -0.21875 to 0.21875
- in_bias: float32 [2, 1536], replicated, may hold values from -1.25 to 1.25
- attn_out: bfloat16 [2, 768, 768], replicated, may hold values from -0.875 to 0.875
- out_bias: float32 [2, 768], replicated, may hold values from -1.25 to 1.25
- ffn_in: bfloat16 [2, 768, 3072], replicated, may hold values from -0.21875 to 0.21875
- ffn_in_bias: float32 [2, 3072], replicated, may hold values from -1.25 to 1.25
- ffn_out: bfloat16 [2, 3072, 768], replicated, may hold values from -0.109375 to 0.109375
- ffn_out_bias: float32 [2, 768], replicated, may hold values from -1.25 to 1.25
- norm_gain: float32 [2, 2, 768], replicated, may hold values from 0.5 to 1.5
- norm_bias: float32 [2, 2, 768], replicated, may hold values from -1.25 to 1.25
- cotangent: bfloat16 [8, 1024, 768], P('clip', 'seq'), may hold values from -8 to 8
Outputs:
- out_tokens: bfloat16 [8, 1024, 768], P('clip', 'seq')
- grad_tokens: bfloat16 [8, 1024, 768], P('clip', 'seq')
- grad_attn_in: float32 [2, 768, 2304], P(None, 'clip', 'seq')
- grad_in_bias: float32 [2, 1536], P(None, 'seq')
- grad_attn_out: float32 [2, 768, 768], P(None, 'clip', 'seq')
- grad_out_bias: float32 [2, 768], P(None, 'seq')
- grad_ffn_in: float32 [2, 768, 3072], P(None, 'clip', 'seq')
- grad_ffn_in_bias: float32 [2, 3072], P(None, 'seq')
- grad_ffn_out: float32 [2, 3072, 768], P(None, 'clip', 'seq')
- grad_ffn_out_bias: float32 [2, 768], P(None, 'seq')
- grad_norm_gain: float32 [2, 2, 768], P(None, None, 'seq')
- grad_norm_bias: float32 [2, 2, 768], P(None, None, 'seq')
The draws below stay inside these ranges and needn't reach their ends.
Inputs may be any that keep to these rules, and one draw needn't show every extreme that they name: `lengths`: in each aligned run of 2 clips one clip is exactly 1024 frames long.
All inputs are finite; a program needn't handle non-finite values.
Results may differ from the reference program's by a relative error of at most 0.018.
Values may be sent and summed in bfloat16 or wider, within the bound.
A program may use at most 320 MiB of HBM per device.

```python
import math
import jax
import jax.numpy as jnp
from jax import lax

D = 768
HEADS = 12
HEAD_DIM = 64
FF = 3072
LAYERS = 2
LEN = 1024
CL = 2
CLIPS = 8


def draw_lengths(key, part):
    key = jax.random.fold_in(key, 11)
    base_key, pick_key = jax.random.split(key)
    base = jax.random.randint(base_key, (CLIPS,), LEN * 7 // 10, LEN + 1)
    chosen = jax.random.randint(pick_key, (CLIPS // CL, 1), 0, CL)
    full_clip = (jnp.arange(CL, dtype=jnp.int32)[None, :] == chosen).reshape(CLIPS)
    return jnp.where(full_clip, LEN, base).astype(jnp.int32)


def spiked(array, stream_key, source, target, blocks, factor):
    owner, partner = [(jnp.arange(array.shape[axis_at]) // (array.shape[axis_at] // blocks)).reshape([-1 if axis == axis_at else 1 for axis in range(array.ndim)]) for axis_at in (source, target)]
    chosen = jax.random.permutation(stream_key, blocks)[partner]
    strong = (owner == chosen) | (owner == (partner + blocks // 2) % blocks)
    return jnp.where(strong, factor * array, array)


def block_scale(stream_key, dims, cuts, least, top_value):
    loudness = 1.0
    for axis_at, shards_of in cuts:
        steps = jax.random.uniform(jax.random.fold_in(jax.random.fold_in(stream_key, 6), axis_at), (shards_of,), jnp.float32, least / len(cuts), top_value / len(cuts))
        loudness = loudness * jnp.repeat(jnp.exp(steps), dims[axis_at] // shards_of).reshape((-1,) + (1,) * (len(dims) - 1 - axis_at))
    return loudness


def gaussian(key, extent, deviation, limit, shards=(), kind=jnp.bfloat16):
    drawn = deviation * jax.random.normal(key, extent, jnp.float32)
    if shards:
        drawn = drawn * block_scale(key, extent, shards, -0.22, 0.18)
    return jnp.clip(drawn, -limit, limit).astype(kind)


def bell_draw_with(rng, dims, scale, reach, pieces, heavy, held_as=jnp.bfloat16):
    values = scale * jax.random.normal(rng, dims, jnp.float32)
    if pieces:
        values = values * block_scale(rng, dims, pieces, -0.22, 0.18)
    return jnp.clip(spiked(values, jax.random.fold_in(rng, 3), *heavy), -reach, reach).astype(held_as)


def setup_inputs(seed: int = 0) -> dict:
    key_of = jax.random.split(jax.random.key(seed), 14)
    return {
        "tokens": gaussian(key_of[0], (CLIPS, LEN, D), 1.0, 6.0, ((0, 4), (1, 8))),
        "lengths": draw_lengths(jax.random.fold_in(key_of[13], 71), 0),
        "attn_in": gaussian(key_of[2], (LAYERS, D, 3 * D), D ** -0.5, 0.21875),
        "in_bias": gaussian(key_of[3], (LAYERS, 2 * D), 0.2, 1.25, (), jnp.float32),
        "attn_out": gaussian(key_of[4], (LAYERS, D, D), (D // 16) ** -0.5, 0.875),
        "out_bias": gaussian(key_of[5], (LAYERS, D), 0.2, 1.25, (), jnp.float32),
        "ffn_in": gaussian(key_of[6], (LAYERS, D, FF), D ** -0.5, 0.21875),
        "ffn_in_bias": gaussian(key_of[7], (LAYERS, FF), 0.2, 1.25, (), jnp.float32),
        "ffn_out": gaussian(key_of[8], (LAYERS, FF, D), FF ** -0.5, 0.109375),
        "ffn_out_bias": gaussian(key_of[9], (LAYERS, D), 0.2, 1.25, (), jnp.float32),
        "norm_gain": jnp.clip(1.0 + 0.1 * jax.random.normal(key_of[10], (LAYERS, 2, D), jnp.float32), 0.5, 1.5),
        "norm_bias": gaussian(key_of[11], (LAYERS, 2, D), 0.2, 1.25, (), jnp.float32),
        "cotangent": bell_draw_with(key_of[12], (CLIPS, LEN, D), 1.0, 8.0, ((0, 4), (1, 8)), (1, 2, 8, 2.0)),
    }


@jax.custom_vjp
def low(v):
    return lax.optimization_barrier(v.astype(jnp.bfloat16)).astype(jnp.float32)

@jax.custom_vjp
def low_back(v):
    return v

def low_keep(v):
    return (low(v), None)

def low_pass(kept, grad):
    return (grad,)

def back_keep(v):
    return (v, None)

def back_low(kept, grad):
    return (low(grad),)
low.defvjp(low_keep, low_pass)
low_back.defvjp(back_keep, back_low)
HIGH = lax.Precision.HIGHEST

def layer_norm(values, gain, shift):
    center = values - lax.optimization_barrier(jnp.mean(values, -1, keepdims=True))
    spread = lax.optimization_barrier(jnp.mean(center * center, -1, keepdims=True))
    return center * lax.rsqrt(spread + 1e-05) * gain + shift

def gelu_exact(values):
    return jax.nn.gelu(values, approximate=False)

def encoder_block(state, weights, valid):
    w_in, b_in, w_out, b_out, w_up, b_up, w_down, b_down, gains, shifts = weights
    groups, slots, width = state.shape
    shape4 = (groups, slots, HEADS, HEAD_DIM)
    low_in = low(state)
    mixed = jnp.einsum('gtd,de->gte', low_in, w_in, precision=HIGH)
    queries = low(low_back(mixed[..., :width] + b_in[:width]))
    keys = low(low_back(mixed[..., width:2 * width]))
    values = low(low_back(mixed[..., 2 * width:] + b_in[width:]))
    scores = jnp.einsum('gqhd,gkhd->ghqk', queries.reshape(shape4), keys.reshape(shape4), precision=HIGH)
    scores = low_back(scores * HEAD_DIM ** (-0.5))
    scores = jnp.where(valid[:, None, None, :], scores, -1e+30)
    probs = low(jax.nn.softmax(scores, axis=-1))
    attended = jnp.einsum('ghqk,gkhd->gqhd', probs, values.reshape(shape4), precision=HIGH)
    attended = low(low_back(attended.reshape(groups, slots, width)))
    branch = low_back(jnp.einsum('gtd,de->gte', attended, w_out, precision=HIGH) + b_out)
    hidden = layer_norm(state + branch, gains[0], shifts[0])
    inner = low_back(jnp.einsum('gtd,df->gtf', low(hidden), w_up, precision=HIGH) + b_up)
    active = low(gelu_exact(inner))
    second = low_back(jnp.einsum('gtf,fd->gtd', active, w_down, precision=HIGH) + b_down)
    return layer_norm(hidden + second, gains[1], shifts[1])

def reference(tokens, lengths, attn_in, in_bias, attn_out, out_bias, ffn_in, ffn_in_bias, ffn_out, ffn_out_bias, norm_gain, norm_bias, cotangent):
    weights = tuple((w.astype(jnp.float32) for w in (attn_in, in_bias, attn_out, out_bias, ffn_in, ffn_in_bias, ffn_out, ffn_out_bias, norm_gain, norm_bias)))
    group = math.gcd(CLIPS, 4)
    rounds = CLIPS // group

    def network(state, params, valid):
        for layer in range(LAYERS):
            state = encoder_block(state, tuple((w[layer] for w in params)), valid)
        return state

    def advance(totals, inputs):
        frames, counts, grad_out = inputs
        valid = jnp.arange(LEN, dtype=jnp.int32)[None, :] < counts[:, None]

        def apply_net(state, params):
            return network(state, params, valid)
        result, pull = jax.vjp(apply_net, frames.astype(jnp.float32), weights)
        grad_state, grad_params = pull(grad_out.astype(jnp.float32))
        totals = tuple((a + b for a, b in zip(totals, grad_params)))
        return (totals, (result.astype(jnp.bfloat16), grad_state.astype(jnp.bfloat16)))
    start = tuple((jnp.zeros_like(w) for w in weights))
    inputs = (tokens.reshape(rounds, group, LEN, D), lengths.reshape(rounds, group), cotangent.reshape(rounds, group, LEN, D))
    totals, (results, grad_states) = lax.scan(advance, start, inputs)
    return (results.reshape(CLIPS, LEN, D), grad_states.reshape(CLIPS, LEN, D), totals[0], totals[1], totals[2], totals[3], totals[4], totals[5], totals[6], totals[7], totals[8], totals[9])
```

```python
import functools

import jax
import jax.numpy as jnp
from jax import lax
from jax.experimental import pallas as pl
from jax.experimental.pallas import tpu as pltpu
from jax.sharding import PartitionSpec as P

HEADS = 12
HEAD_DIM = 64
CORES = 2
LANES = 128
SCALE = HEAD_DIM**-0.5
SQRT_HALF = 0.5**0.5
GAUSS = 0.3989422804014327
EPS = 1e-05
VMEM = 56 * 1024 * 1024

f32 = jnp.float32
b16 = jnp.bfloat16


def dot(a, b):
    return lax.dot_general(a, b, (((1,), (0,)), ((), ())), preferred_element_type=f32)


def dot_nt(a, b):
    return lax.dot_general(a, b, (((1,), (1,)), ((), ())), preferred_element_type=f32)


def dot_tn(a, b):
    return lax.dot_general(a, b, (((0,), (0,)), ((), ())), preferred_element_type=f32)


def norm_parts(values):
    center = values - jnp.mean(values, -1, keepdims=True)
    inverse = lax.rsqrt(jnp.mean(center * center, -1, keepdims=True) + EPS)
    return center * inverse, inverse


def norm_back(values, gain, grad):
    unit, inverse = norm_parts(values)
    scaled = grad * gain
    mean_one = jnp.mean(scaled, -1, keepdims=True)
    mean_two = jnp.mean(scaled * unit, -1, keepdims=True)
    back = inverse * (scaled - mean_one - unit * mean_two)
    return back, jnp.sum(grad * unit, 0, keepdims=True), jnp.sum(grad, 0, keepdims=True)


def whole_spec(shape):
    zeros = (0,) * len(shape)
    return pl.BlockSpec(shape, lambda g, c: zeros)


def call(kernel, core, grid, ins, outs, scratch, flops, moved):
    in_specs = [pl.BlockSpec(block, lambda g, c, at=at: at(g, c[0])) for unused, block, at in ins]
    out_specs = [pl.BlockSpec(block, lambda g, c, at=at: at(g, c[0])) for s, d, block, at in outs]
    return pl.pallas_call(
        kernel,
        grid_spec=pltpu.PrefetchScalarGridSpec(
            num_scalar_prefetch=1,
            grid=(grid,),
            in_specs=in_specs,
            out_specs=out_specs,
            scratch_shapes=scratch,
        ),
        out_shape=[jax.ShapeDtypeStruct(shape, dtype) for shape, dtype, b, at in outs],
        compiler_params=pltpu.CompilerParams(
            dimension_semantics=("arbitrary",), vmem_limit_bytes=VMEM
        ),
        cost_estimate=pl.CostEstimate(flops=flops, bytes_accessed=moved, transcendentals=0),
    )(core, *[array for array, b, at in ins])


def all_of(array):
    zeros = (0,) * array.ndim
    return (array, array.shape, lambda g, c: zeros)


def full(shape, dtype):
    zeros = (0,) * len(shape)
    return (shape, dtype, shape, lambda g, c: zeros)


def attend_kernel(
    core_ref, x_ref, mask_ref, wq_ref, wk_ref, wv_ref, bq_ref, bv_ref, wo_ref,
    q_ref, k_ref, v_ref, o_ref, ot_ref, lse_ref, part_ref, acc_ref,
):
    step = pl.program_id(0)
    rows = q_ref.shape[0]
    tile = min(256, rows)
    everything = x_ref[...]
    query = dot(everything[:rows], wq_ref[0]) + bq_ref[0]
    query = (query.astype(b16) * SCALE).astype(b16)
    key = dot(everything, wk_ref[0]).astype(b16)
    value = (dot(everything, wv_ref[0]) + bv_ref[0]).astype(b16)
    q_ref[...] = query
    k_ref[...] = key
    v_ref[...] = value
    query_t = query.astype(f32).T.astype(b16)
    value_t = value.astype(f32).T.astype(b16)
    keyed = jnp.concatenate([key, mask_ref[...]], 1)
    first_row = (lax.broadcasted_iota(jnp.int32, (LANES, tile), 0) == 0).astype(f32).astype(b16)
    empty = jnp.zeros((HEAD_DIM, tile), b16)
    for head in range(2):
        here = slice(head * HEAD_DIM, (head + 1) * HEAD_DIM)
        for start in range(0, rows, tile):
            part = query_t[here, start : start + tile]
            pieces = [part, empty] if head == 0 else [empty, part]
            scores = dot(keyed, jnp.concatenate(pieces + [first_row], 0))
            top = jnp.max(scores, 0, keepdims=True)
            weights = jnp.exp(scores - top)
            total = jnp.sum(weights, 0, keepdims=True)
            attended = dot(value_t[here], weights.astype(b16)) / total
            ot_ref[here, start : start + tile] = attended
            lse_ref[0, head : head + 1, start : start + tile] = top + jnp.log(total)
    attended = ot_ref[...].T.astype(b16)
    o_ref[...] = attended
    mixed = dot(attended, wo_ref[0])

    @pl.when(step == 0)
    def first():
        acc_ref[...] = mixed

    @pl.when(step > 0)
    def later():
        acc_ref[...] += mixed

    @pl.when(step == pl.num_programs(0) - 1)
    def last():
        part_ref[...] = acc_ref[...].astype(b16)


def attend(core, layer, x_all, mask, rows, attn_in, in_bias, attn_out):
    count, width = x_all.shape
    half = width // CORES
    pairs = half // LANES

    def columns(kind):
        return ((1, width, LANES), lambda g, c: (layer, 0, (kind * CORES + c) * pairs + g))

    def biases(kind):
        return ((1, 1, LANES), lambda g, c: (layer, 0, (kind * CORES + c) * pairs + g))

    lane_block = lambda g, c: (0, g)
    return call(
        attend_kernel, core, pairs,
        [
            all_of(x_all), all_of(mask),
            (attn_in, *columns(0)), (attn_in, *columns(1)), (attn_in, *columns(2)),
            (in_bias, *biases(0)), (in_bias, *biases(1)),
            (attn_out, (1, LANES, width), lambda g, c: (layer, c * pairs + g, 0)),
        ],
        [
            ((rows, half), b16, (rows, LANES), lane_block),
            ((count, half), b16, (count, LANES), lane_block),
            ((count, half), b16, (count, LANES), lane_block),
            ((rows, half), b16, (rows, LANES), lane_block),
            ((half, rows), f32, (LANES, rows), lambda g, c: (g, 0)),
            ((pairs, 8, rows), f32, (1, 8, rows), lambda g, c: (g, 0, 0)),
            full((rows, width), b16),
        ],
        [pltpu.VMEM((rows, width), f32)],
        8 * 10**9, 10**7,
    )


def feed_kernel(
    core_ref, x_ref, p0_ref, p1_ref, bo_ref, gain_ref, shift_ref, up_ref, bup_ref, down_ref,
    z_ref, h_ref, hr_ref, hrt_ref, act_ref, slope_ref, part_ref, acc_ref,
):
    step = pl.program_id(0)

    @pl.when(step == 0)
    def first():
        summed = x_ref[...].astype(f32) + (p0_ref[...].astype(f32) + p1_ref[...].astype(f32)) + bo_ref[0]
        z_ref[...] = summed
        unit, unused = norm_parts(summed)
        hidden = unit * gain_ref[0] + shift_ref[0]
        h_ref[...] = hidden
        low = hidden.astype(b16)
        hr_ref[...] = low
        hrt_ref[...] = low.astype(f32).T.astype(b16)
        acc_ref[...] = jnp.zeros_like(acc_ref)

    inner = dot(hr_ref[...], up_ref[0]) + bup_ref[0]
    phi = 0.5 + 0.5 * lax.erf(inner * SQRT_HALF)
    active = (inner * phi).astype(b16)
    slope_ref[...] = (phi + inner * (GAUSS * jnp.exp(-0.5 * inner * inner))).astype(b16)
    act_ref[...] = active
    acc_ref[...] += dot(active, down_ref[0])

    @pl.when(step == pl.num_programs(0) - 1)
    def last():
        part_ref[...] = acc_ref[...].astype(b16)


def hidden_tiles(ffn, tile):
    per = ffn // 4 // tile
    return 2 * per, lambda g, c: (2 * (g // per) + c) * per + g % per


def feed(core, layer, x, p0, p1, out_bias, gain, shift, ffn_in, ffn_in_bias, ffn_out):
    rows, width = x.shape
    ffn = ffn_in.shape[2]
    tile = 256
    steps, at = hidden_tiles(ffn, tile)
    half = ffn // CORES
    return call(
        feed_kernel, core, steps,
        [
            all_of(x), all_of(p0), all_of(p1),
            (out_bias, (1, 1, width), lambda g, c: (layer, 0, 0)),
            (gain, (1, 1, width), lambda g, c: (2 * layer, 0, 0)),
            (shift, (1, 1, width), lambda g, c: (2 * layer, 0, 0)),
            (ffn_in, (1, width, tile), lambda g, c: (layer, 0, at(g, c))),
            (ffn_in_bias, (1, 1, tile), lambda g, c: (layer, 0, at(g, c))),
            (ffn_out, (1, tile, width), lambda g, c: (layer, at(g, c), 0)),
        ],
        [
            full((rows, width), f32), full((rows, width), f32), full((rows, width), b16),
            full((width, rows), b16),
            ((rows, half), b16, (rows, tile), lambda g, c: (0, g)),
            ((rows, half), b16, (rows, tile), lambda g, c: (0, g)),
            full((rows, width), b16),
        ],
        [pltpu.VMEM((rows, width), f32)],
        5 * 10**9, 10**7,
    )


def norm_kernel(core_ref, h_ref, p0_ref, p1_ref, b_ref, gain_ref, shift_ref, z_ref, y_ref, low_ref):
    summed = h_ref[...] + (p0_ref[...].astype(f32) + p1_ref[...].astype(f32)) + b_ref[0]
    z_ref[...] = summed
    unit, unused = norm_parts(summed)
    result = unit * gain_ref[0] + shift_ref[0]
    y_ref[...] = result
    low_ref[...] = result.astype(b16)


def norm(core, layer, h, p0, p1, bias, gain, shift):
    rows, width = h.shape
    return call(
        norm_kernel, core, 1,
        [
            all_of(h), all_of(p0), all_of(p1),
            (bias, (1, 1, width), lambda g, c: (layer, 0, 0)),
            (gain, (1, 1, width), lambda g, c: (2 * layer + 1, 0, 0)),
            (shift, (1, 1, width), lambda g, c: (2 * layer + 1, 0, 0)),
        ],
        [full((rows, width), f32), full((rows, width), f32), full((rows, width), b16)],
        [],
        10**7, 10**7,
    )


def feed_back_kernel(
    core_ref, z_ref, dy_ref, more_ref, gain_ref, slope_ref, up_ref, down_ref,
    dz_ref, dft_ref, small_ref, du_ref, dub_ref, part_ref, low_ref, acc_ref,
):
    step = pl.program_id(0)

    @pl.when(step == 0)
    def first():
        grad = dy_ref[...].astype(f32) + more_ref[...].astype(f32)
        back, gain_grad, shift_grad = norm_back(z_ref[...], gain_ref[0], grad)
        dz_ref[...] = back
        low = back.astype(b16)
        low_ref[...] = low
        wide = low.astype(f32)
        dft_ref[...] = wide.T.astype(b16)
        small_ref[0:1, :] = gain_grad
        small_ref[1:2, :] = shift_grad
        small_ref[2:3, :] = jnp.sum(wide, 0, keepdims=True)
        acc_ref[...] = jnp.zeros_like(acc_ref)

    grad = dot_nt(low_ref[...], down_ref[0]) * slope_ref[...].astype(f32)
    low = grad.astype(b16)
    du_ref[...] = low
    dub_ref[0:1, :] = jnp.sum(low.astype(f32), 0, keepdims=True)
    acc_ref[...] += dot_nt(low, up_ref[0])

    @pl.when(step == pl.num_programs(0) - 1)
    def last():
        part_ref[...] = acc_ref[...].astype(b16)


def feed_back(core, layer, z, dy, more, gain, slope, ffn_in, ffn_out):
    rows, width = z.shape
    ffn = ffn_in.shape[2]
    tile = 256
    steps, at = hidden_tiles(ffn, tile)
    half = ffn // CORES
    return call(
        feed_back_kernel, core, steps,
        [
            all_of(z), all_of(dy), all_of(more),
            (gain, (1, 1, width), lambda g, c: (2 * layer + 1, 0, 0)),
            (slope, (rows, tile), lambda g, c: (0, g)),
            (ffn_in, (1, width, tile), lambda g, c: (layer, 0, at(g, c))),
            (ffn_out, (1, tile, width), lambda g, c: (layer, at(g, c), 0)),
        ],
        [
            full((rows, width), f32), full((width, rows), b16), full((8, width), f32),
            ((rows, half), b16, (rows, tile), lambda g, c: (0, g)),
            ((8, half), f32, (8, tile), lambda g, c: (0, g)),
            full((rows, width), b16),
        ],
        [pltpu.VMEM((rows, width), b16), pltpu.VMEM((rows, width), f32)],
        5 * 10**9, 10**7,
    )


def attend_back_kernel(
    core_ref, dz_ref, p0_ref, p1_ref, z_ref, gain_ref, mask_ref,
    q_ref, k_ref, v_ref, ot_ref, lse_ref, wq_ref, wk_ref, wv_ref, wo_ref,
    dz1_ref, dat_ref, small_ref, dq_ref, dk_ref, dv_ref, dqb_ref, dvb_ref, part_ref,
    low_ref, acc_ref, dk_acc, dv_acc, dqt_ref,
):
    step = pl.program_id(0)
    rows = q_ref.shape[0]
    tile = min(256, rows)

    @pl.when(step == 0)
    def first():
        grad = dz_ref[...] + (p0_ref[...].astype(f32) + p1_ref[...].astype(f32))
        back, gain_grad, shift_grad = norm_back(z_ref[...], gain_ref[0], grad)
        dz1_ref[...] = back
        low = back.astype(b16)
        low_ref[...] = low
        wide = low.astype(f32)
        dat_ref[...] = wide.T.astype(b16)
        small_ref[0:1, :] = gain_grad
        small_ref[1:2, :] = shift_grad
        small_ref[2:3, :] = jnp.sum(wide, 0, keepdims=True)
        acc_ref[...] = jnp.zeros_like(acc_ref)

    query = q_ref[...]
    key = k_ref[...]
    value = v_ref[...]
    outgrad = dot_nt(low_ref[...], wo_ref[0]).astype(b16)
    outgrad_t = outgrad.astype(f32).T.astype(b16)
    query_t = query.astype(f32).T.astype(b16)
    key_t = key.astype(f32).T.astype(b16)
    keyed = jnp.concatenate([key, mask_ref[...]], 1)
    first_row = (lax.broadcasted_iota(jnp.int32, (LANES, tile), 0) == 0).astype(f32).astype(b16)
    empty = jnp.zeros((HEAD_DIM, tile), b16)
    lane_head = lax.broadcasted_iota(jnp.int32, (rows, LANES), 1) // HEAD_DIM
    for head in range(2):
        here = slice(head * HEAD_DIM, (head + 1) * HEAD_DIM)
        mine = (lane_head == head).astype(f32)
        query_mine = (query.astype(f32) * mine).astype(b16)
        outgrad_mine = (outgrad.astype(f32) * mine).astype(b16)
        for start in range(0, rows, tile):
            now = slice(start, start + tile)
            piece = query_t[here, now]
            pieces = [piece, empty] if head == 0 else [empty, piece]
            scores = dot(keyed, jnp.concatenate(pieces + [first_row], 0))
            probs = jnp.exp(scores - lse_ref[0, head : head + 1, now])
            piece = outgrad_t[here, now]
            pieces = [piece, empty] if head == 0 else [empty, piece]
            grads = dot(value, jnp.concatenate(pieces, 0))
            delta = jnp.sum(piece.astype(f32) * ot_ref[here, now], 0, keepdims=True)
            score_grads = (probs * (grads - delta)).astype(b16)
            value_part = dot(probs.astype(b16), outgrad_mine[now])
            key_part = dot(score_grads, query_mine[now])
            if head == 0 and start == 0:
                dv_acc[...] = value_part
                dk_acc[...] = key_part
            else:
                dv_acc[...] += value_part
                dk_acc[...] += key_part
            dqt_ref[here, now] = dot(key_t[here], score_grads)
    dq = (dqt_ref[...].T * SCALE).astype(b16)
    dk = dk_acc[...].astype(b16)
    dv = dv_acc[...].astype(b16)
    dq_ref[...] = dq
    dk_ref[...] = dk
    dv_ref[...] = dv
    dqb_ref[0:1, :] = jnp.sum(dq.astype(f32), 0, keepdims=True)
    dvb_ref[0:1, :] = jnp.sum(dv.astype(f32), 0, keepdims=True)
    acc_ref[...] += dot_nt(dk, wk_ref[0]) + dot_nt(dv, wv_ref[0])
    acc_ref[:rows] += dot_nt(dq, wq_ref[0])

    @pl.when(step == pl.num_programs(0) - 1)
    def last():
        part_ref[...] = acc_ref[...].astype(b16)


def attend_back(core, layer, dz, p0, p1, z, gain, mask, kept, attn_in, attn_out):
    q, k, v, ot, lse = kept
    rows, width = z.shape
    count = k.shape[0]
    half = width // CORES
    pairs = half // LANES

    def columns(kind):
        return ((1, width, LANES), lambda g, c: (layer, 0, (kind * CORES + c) * pairs + g))

    lane_block = lambda g, c: (0, g)
    return call(
        attend_back_kernel, core, pairs,
        [
            all_of(dz), all_of(p0), all_of(p1), all_of(z),
            (gain, (1, 1, width), lambda g, c: (2 * layer, 0, 0)),
            all_of(mask),
            (q, (rows, LANES), lane_block), (k, (count, LANES), lane_block),
            (v, (count, LANES), lane_block), (ot, (LANES, rows), lambda g, c: (g, 0)),
            (lse, (1, 8, rows), lambda g, c: (g, 0, 0)),
            (attn_in, *columns(0)), (attn_in, *columns(1)), (attn_in, *columns(2)),
            (attn_out, (1, LANES, width), lambda g, c: (layer, c * pairs + g, 0)),
        ],
        [
            full((rows, width), f32), full((width, rows), b16), full((8, width), f32),
            ((rows, half), b16, (rows, LANES), lane_block),
            ((count, half), b16, (count, LANES), lane_block),
            ((count, half), b16, (count, LANES), lane_block),
            ((8, half), f32, (8, LANES), lane_block),
            ((8, half), f32, (8, LANES), lane_block),
            full((count, width), b16),
        ],
        [
            pltpu.VMEM((rows, width), b16), pltpu.VMEM((count, width), f32),
            pltpu.VMEM((count, LANES), f32), pltpu.VMEM((count, LANES), f32),
            pltpu.VMEM((LANES, rows), f32),
        ],
        16 * 10**9, 2 * 10**7,
    )


def down_grad_kernel(core_ref, dft_ref, act_ref, out_ref):
    out = dot(dft_ref[...], act_ref[...]).astype(b16)
    out_ref[...] = out.reshape(out_ref.shape)


def down_grad(core, dft, act, lines, posts, cols):
    rows = dft.shape[1]
    hidden = act.shape[1] // CORES
    return call(
        down_grad_kernel, core, CORES * posts,
        [
            (dft, (lines * cols, rows), lambda g, c: (g % posts, 0)),
            (act, (rows, hidden), lambda g, c: (0, g // posts)),
        ],
        [(
            (CORES, lines, posts, cols, hidden), b16, (1, lines, 1, cols, hidden),
            lambda g, c: (g // posts, 0, g % posts, 0, 0),
        )],
        [],
        2 * 10**9, 10**7,
    )[0]


def up_grad_kernel(core_ref, top_ref, low_ref, own_ref, sib_ref, out_ref):
    lhs = jnp.concatenate([top_ref[...], low_ref[...]], 0)
    mine = pl.program_id(0) % 2 == 0

    @pl.when(mine)
    def own():
        out_ref[...] = dot(lhs, own_ref[...]).astype(b16).reshape(out_ref.shape)

    @pl.when(jnp.logical_not(mine))
    def sib():
        out_ref[...] = dot(lhs, sib_ref[...]).astype(b16).reshape(out_ref.shape)


def up_grad(core, hrt, du_own, du_sib, lines, posts, depth, cols):
    rows = hrt.shape[1]

    def place(g, c):
        kind = g % 2
        return ((g // 2) // lines, kind + c - 2 * kind * c, (g // 2) % lines)

    def out_at(g, c):
        block, who, line = place(g, c)
        return (0, line, 2 * block + who, 0, 0)

    return call(
        up_grad_kernel, core, lines * posts,
        [
            (hrt, (depth, rows), lambda g, c: (c, 0)),
            (hrt, (depth, rows), lambda g, c: (2 + c, 0)),
            (du_own, (rows, cols), lambda g, c: (0, g // 2)),
            (du_sib, (rows, cols), lambda g, c: (0, g // 2)),
        ],
        [(
            (CORES, lines, posts, depth, cols), b16, (CORES, 1, 1, depth, cols), out_at,
        )],
        [],
        2 * 10**9, 10**7,
    )[0]


def in_grad_kernel(
    core_ref, dq_ref, dqs_ref, dk_ref, dks_ref, dv_ref, dvs_ref, x_ref, dat_ref, or_ref,
    out_ref, proj_ref,
):
    core = core_ref[0]
    half = dq_ref.shape[1]
    everything = x_ref[...]
    parts = ((dq_ref, dqs_ref), (dk_ref, dks_ref), (dv_ref, dvs_ref))
    for kind, pair in enumerate(parts):
        for who, ref in enumerate(pair):
            owner = core if who == 0 else 1 - core
            at = pl.multiple_of((2 * kind + owner) * half, half)
            piece = ref[...]
            out_ref[pl.ds(at, half), :] = dot_tn(piece, everything[: piece.shape[0]]).astype(b16)
    proj_ref[...] = dot(dat_ref[...], or_ref[...]).astype(b16)


def in_grad(core, dq, dqs, dk, dks, dv, dvs, x_mine, dat, or_mine):
    half = dq.shape[1]
    width = dat.shape[0]
    arrays = (dq, dqs, dk, dks, dv, dvs, x_mine, dat, or_mine)
    return call(
        in_grad_kernel, core, 1, [all_of(array) for array in arrays],
        [full((6 * half, x_mine.shape[1]), b16), full((width, x_mine.shape[1]), b16)],
        [],
        5 * 10**9, 10**7,
    )


def build(mesh):
    clip_size, seq_size = mesh.shape["clip"], mesh.shape["seq"]
    columns = clip_size // CORES

    def shards(
        tokens, lengths, attn_in, in_bias, attn_out, out_bias, ffn_in, ffn_in_bias,
        ffn_out, ffn_out_bias, norm_gain, norm_bias, cotangent,
    ):
        held, slots, width = tokens.shape
        layers = attn_in.shape[0]
        ffn = ffn_in.shape[2]
        half = width // CORES
        quarter = ffn // 4
        posts = held * CORES
        lines = seq_size // posts
        rows = posts * slots
        count = rows * lines
        depth = width // clip_size
        aligned = columns == 2 and (ffn // seq_size) % LANES == 0

        clip_at = lax.axis_index("clip")
        seq_at = lax.axis_index("seq")
        core = clip_at % CORES
        column = clip_at // CORES
        post = seq_at // lines
        line = seq_at % lines
        core_arg = jnp.reshape(core, (1,)).astype(jnp.int32)
        parity = post % held

        def swap(array):
            pairs = [(at, at ^ 1) for at in range(clip_size)]
            return jax.tree.map(lambda a: lax.ppermute(a, "clip", pairs), array)

        def along_column(array, shift):
            pairs = [
                (at, ((at // CORES + shift) % columns) * CORES + at % CORES)
                for at in range(clip_size)
            ]
            return lax.ppermute(array, "clip", pairs)

        def along_line(array, shift):
            pairs = [
                (at, at // lines * lines + (at % lines + shift) % lines) for at in range(seq_size)
            ]
            return lax.ppermute(array, "seq", pairs)

        def along_post(array, shift):
            pairs = [
                (at, (at // lines + shift) % posts * lines + at % lines) for at in range(seq_size)
            ]
            return lax.ppermute(array, "seq", pairs)

        def shuffle_pairs(turn):
            pairs = []
            for col in range(columns):
                for cor in range(CORES):
                    for pos in range(posts):
                        for lin in range(lines):
                            source = (col * CORES + cor) * seq_size + pos * lines + lin
                            goal = (col * CORES + pos // held) * seq_size
                            goal += (held * cor + (pos + turn) % held) * lines + lin
                            pairs.append((source, goal))
            return pairs

        def to_rows(blocks):
            got = []
            for turn in range(held):
                piece = lax.dynamic_index_in_dim(blocks, (post + turn) % held, 0, False)
                got.append(lax.ppermute(piece, ("clip", "seq"), shuffle_pairs(turn)))
            return jnp.concatenate(got, 0)

        def from_rows(mine):
            got = []
            for turn in range(held):
                pairs = [(goal, source) for source, goal in shuffle_pairs(turn)]
                piece = mine[turn * slots : (turn + 1) * slots]
                got.append(lax.ppermute(piece, ("clip", "seq"), pairs))
            order = [jnp.stack([got[(at - turn) % held] for at in range(held)]) for turn in range(held)]
            result = order[0]
            for turn in range(1, held):
                result = jnp.where(parity == turn, order[turn], result)
            return result

        def joined(mine, other):
            return jnp.where(
                core == 0, jnp.concatenate([mine, other], 0), jnp.concatenate([other, mine], 0)
            )

        def half_of(array, which):
            return lax.dynamic_slice_in_dim(array, which * (rows // CORES), rows // CORES, 0)

        def gather_lines(mine):
            pieces = []
            for shift in range(1, lines):
                came = along_line(mine, shift)
                pieces.append(joined(came, swap(came)))
            return pieces

        sibling_lengths = swap(lengths)
        both_lengths = jnp.where(
            core == 0,
            jnp.concatenate([lengths, sibling_lengths]),
            jnp.concatenate([sibling_lengths, lengths]),
        )
        length = lax.dynamic_index_in_dim(both_lengths, post, 0, False)
        shift = jnp.arange(lines)[:, None, None, None]
        who = jnp.arange(CORES)[None, :, None, None]
        turn = jnp.arange(held)[None, None, :, None]
        slot = jnp.arange(slots)[None, None, None, :]
        source_post = held * who + (parity + turn) % held
        source_line = (line - shift) % lines
        position = ((source_post * lines + source_line) * slots + slot).reshape(count)
        lane = jnp.arange(LANES)[None, :]
        mask = jnp.where((lane == 0) & (position >= length)[:, None], -1e30, 0.0).astype(b16)

        in_bias3 = in_bias.reshape(layers, 1, -1)
        out_bias3 = out_bias.reshape(layers, 1, -1)
        up_bias3 = ffn_in_bias.reshape(layers, 1, -1)
        down_bias3 = ffn_out_bias.reshape(layers, 1, -1)
        gain3 = norm_gain.reshape(layers * 2, 1, -1)
        shift3 = norm_bias.reshape(layers * 2, 1, -1)

        my_tokens = to_rows(tokens)
        my_cotangent = to_rows(cotangent)
        own = joined(my_tokens, swap(my_tokens))
        state = own
        mine = my_tokens
        kept = []
        for layer in range(layers):
            x_all = jnp.concatenate([own] + gather_lines(mine), 0)
            q, k, v, attended, attended_t, lse, part = attend(
                core_arg, layer, x_all, mask, rows, attn_in, in_bias3, attn_out
            )
            first_sum, hidden, low, low_t, active, slope, part_two = feed(
                core_arg, layer, state, part, swap(part), out_bias3, gain3, shift3,
                ffn_in, up_bias3, ffn_out,
            )
            second_sum, state, own = norm(
                core_arg, layer, hidden, part_two, swap(part_two), down_bias3, gain3, shift3
            )
            mine = half_of(own, core)
            kept.append((x_all, (q, k, v, attended_t, lse), attended, first_sum, low_t, low, active, slope, second_sum))
        out_tokens = from_rows(mine)

        def quarters(array, axis):
            size = depth
            shape = array.shape[:axis] + (columns, CORES, size)
            split = array.reshape(shape)
            return jnp.where(core == 0, split[..., 0, :], split[..., 1, :]).reshape(array.shape[:axis] + (-1,))

        def pick(array, at):
            return lax.dynamic_index_in_dim(array, at, 0, False)

        def scatter(array, at, size, move):
            total = pick(array, at).astype(f32)
            for step in range(1, size):
                total = total + move(pick(array, (at + step) % size), step).astype(f32)
            return total

        grad = joined(my_cotangent, swap(my_cotangent))
        more = jnp.zeros_like(grad)
        grads = [None] * layers
        smalls = [None] * layers
        for layer in range(layers - 1, -1, -1):
            x_all, attend_kept, attended, first_sum, low_t, low, active, slope, second_sum = kept[layer]
            dz2, df_t, small_two, du, du_sums, part = feed_back(
                core_arg, layer, second_sum, grad, more, gain3, slope, ffn_in, ffn_out
            )
            du_sibling = swap(du)
            dz1, da_t, small_one, dq, dk, dv, dq_sums, dv_sums, dx = attend_back(
                core_arg, layer, dz2, part, swap(part), first_sum, gain3, mask, attend_kept,
                attn_in, attn_out,
            )
            blocks = dx.reshape(lines, CORES, rows // CORES, width)
            keep = lax.dynamic_index_in_dim(blocks, core, 1, False)
            came = swap(lax.dynamic_index_in_dim(blocks, 1 - core, 1, False))
            summed = keep.astype(f32) + came.astype(f32)
            total = summed[0]
            for step in range(1, lines):
                total = total + along_line(summed[step].astype(b16), lines - step).astype(f32)
            if layer > 0:
                low_total = total.astype(b16)
                more = joined(low_total, swap(low_total))
                grad = dz1
            else:
                grad_tokens = from_rows((total + half_of(dz1, core)).astype(b16))

            dq_s, dk_s, dv_s = swap((dq, dk, dv))
            if aligned:
                depth_in = ffn // seq_size
                down = down_grad(core_arg, df_t, active, lines, posts, width // seq_size)
                up = up_grad(core_arg, low_t, du, du_sibling, lines, posts, depth, depth_in)
                attended_sibling = swap(attended)
                features = joined_lanes = jnp.where(
                    core == 0,
                    jnp.concatenate([attended[:, :depth], attended_sibling[:, :depth]], 1),
                    jnp.concatenate([attended_sibling[:, depth:], attended[:, depth:]], 1),
                )
                into, proj = in_grad(
                    core_arg, dq, dq_s, dk, dk_s, dv, dv_s, quarters(x_all, 1), da_t, features
                )

                def column_first(array):
                    array = scatter(array, column, columns, along_column).astype(b16)
                    array = scatter(array, line, lines, along_line).astype(b16)
                    return scatter(array, post, posts, along_post)

                def line_first(array):
                    size = array.shape[0] // seq_size
                    array = array.reshape(posts, lines, size, columns * depth)
                    array = scatter(jnp.swapaxes(array, 0, 1), line, lines, along_line).astype(b16)
                    array = scatter(array, post, posts, along_post).astype(b16)
                    array = jnp.stack([array[:, at * depth : (at + 1) * depth] for at in range(columns)])
                    return scatter(array, column, columns, along_column).T

                matrices = (
                    line_first(into), line_first(proj), column_first(up), column_first(down).T,
                )
            else:
                def spread(array):
                    array = lax.psum_scatter(
                        array.astype(b16), "seq", scatter_dimension=1, tiled=True
                    ).astype(b16)
                    return lax.psum_scatter(
                        array, "clip", scatter_dimension=0, tiled=True
                    ).astype(f32)

                into = [
                    jnp.concatenate([jnp.where(core == 0, a, b), jnp.where(core == 0, b, a)], 1)
                    for a, b in (
                        (dot_tn(x_all[:rows], dq), dot_tn(x_all[:rows], dq_s)),
                        (dot_tn(x_all, dk), dot_tn(x_all, dk_s)),
                        (dot_tn(x_all, dv), dot_tn(x_all, dv_s)),
                    )
                ]
                proj = jnp.zeros((CORES, half, width), f32)
                proj = lax.dynamic_update_slice_in_dim(proj, dot(da_t, attended).T[None], core, 0)
                up = jnp.zeros((2, CORES, width, quarter), f32)
                own_up = dot(low_t, du).reshape(width, 2, 1, quarter).transpose(1, 2, 0, 3)
                up = lax.dynamic_update_slice_in_dim(up, own_up, core, 1)
                down = jnp.zeros((2, CORES, quarter, width), f32)
                own_down = dot(df_t, active).T.reshape(2, 1, quarter, width)
                down = lax.dynamic_update_slice_in_dim(down, own_down, core, 1)
                matrices = (
                    spread(jnp.concatenate(into, 1) * 0.5),
                    spread(proj.reshape(width, width)),
                    spread(up.transpose(2, 0, 1, 3).reshape(width, ffn)),
                    spread(down.reshape(ffn, width)),
                )
            grads[layer] = matrices

            in_sums = jnp.zeros((2, CORES, half), f32)
            own_sums = jnp.stack([dq_sums[:1], dv_sums[:1]])
            in_sums = lax.dynamic_update_slice_in_dim(in_sums, own_sums, core, 1)
            up_sums = jnp.zeros((2, CORES, quarter), f32)
            up_sums = lax.dynamic_update_slice_in_dim(
                up_sums, du_sums[0].reshape(2, 1, quarter), core, 1
            )
            smalls[layer] = jnp.concatenate([
                in_sums.reshape(-1), up_sums.reshape(-1),
                0.5 * small_one[2], 0.5 * small_two[2],
                0.5 * small_one[0], 0.5 * small_two[0], 0.5 * small_one[1], 0.5 * small_two[1],
            ])

        summed = lax.psum(jnp.stack(smalls), ("clip", "seq"))

        def share(start, size):
            piece = summed[:, start : start + size]
            return lax.dynamic_slice_in_dim(piece, seq_at * (size // seq_size), size // seq_size, 1)

        at = 2 * width + ffn
        matrices = [jnp.stack([grads[layer][which] for layer in range(layers)]) for which in range(4)]
        return (
            out_tokens,
            grad_tokens,
            matrices[0],
            share(0, 2 * width),
            matrices[1],
            share(at, width),
            matrices[2],
            share(2 * width, ffn),
            matrices[3],
            share(at + width, width),
            jnp.stack([share(at + 2 * width, width), share(at + 3 * width, width)], 1),
            jnp.stack([share(at + 4 * width, width), share(at + 5 * width, width)], 1),
        )

    return shards


def solution(mesh):
    rowed = P("clip", "seq", None)
    in_specs = (rowed, P("clip")) + (P(),) * 10 + (rowed,)
    out_specs = (
        rowed,
        rowed,
        P(None, "clip", "seq"),
        P(None, "seq"),
        P(None, "clip", "seq"),
        P(None, "seq"),
        P(None, "clip", "seq"),
        P(None, "seq"),
        P(None, "clip", "seq"),
        P(None, "seq"),
        P(None, None, "seq"),
        P(None, None, "seq"),
    )
    return jax.shard_map(
        build(mesh), mesh=mesh, in_specs=in_specs, out_specs=out_specs, check_vma=False
    )
```

```python
import functools

import jax
import jax.numpy as jnp
from jax import lax
from jax.experimental import pallas as pl
from jax.experimental.pallas import tpu as pltpu
from jax.sharding import PartitionSpec as P

HEADS = 12
HEAD_DIM = 64
CORES = 2
LANES = 128
SCALE = HEAD_DIM**-0.5
SQRT_HALF = 0.5**0.5
GAUSS = 0.3989422804014327
EPS = 1e-05
VMEM = 56 * 1024 * 1024

f32 = jnp.float32
b16 = jnp.bfloat16


def dot(a, b):
    return lax.dot_general(a, b, (((1,), (0,)), ((), ())), preferred_element_type=f32)


def dot_nt(a, b):
    return lax.dot_general(a, b, (((1,), (1,)), ((), ())), preferred_element_type=f32)


def dot_tn(a, b):
    return lax.dot_general(a, b, (((0,), (0,)), ((), ())), preferred_element_type=f32)


def norm_parts(values):
    center = values - jnp.mean(values, -1, keepdims=True)
    inverse = lax.rsqrt(jnp.mean(center * center, -1, keepdims=True) + EPS)
    return center * inverse, inverse


def norm_back(unit, inverse, gain, grad):
    scaled = grad * gain
    mean_one = jnp.mean(scaled, -1, keepdims=True)
    mean_two = jnp.mean(scaled * unit, -1, keepdims=True)
    back = inverse * (scaled - mean_one - unit * mean_two)
    return back, jnp.sum(grad * unit, 0, keepdims=True), jnp.sum(grad, 0, keepdims=True)


def after(array, *others):
    return lax.optimization_barrier((array,) + others)[0]


def call(kernel, core, grid, ins, outs, scratch, flops, moved):
    in_specs = [pl.BlockSpec(block, lambda g, c, at=at: at(g, c[0])) for unused, block, at in ins]
    out_specs = [pl.BlockSpec(block, lambda g, c, at=at: at(g, c[0])) for s, d, block, at in outs]
    return pl.pallas_call(
        kernel,
        grid_spec=pltpu.PrefetchScalarGridSpec(
            num_scalar_prefetch=1,
            grid=(grid,),
            in_specs=in_specs,
            out_specs=out_specs,
            scratch_shapes=scratch,
        ),
        out_shape=[jax.ShapeDtypeStruct(shape, dtype) for shape, dtype, b, at in outs],
        compiler_params=pltpu.CompilerParams(
            dimension_semantics=("arbitrary",), vmem_limit_bytes=VMEM
        ),
        cost_estimate=pl.CostEstimate(flops=flops, bytes_accessed=moved, transcendentals=0),
    )(core, *[array for array, b, at in ins])


def all_of(array):
    zeros = (0,) * array.ndim
    return (array, array.shape, lambda g, c: zeros)


def full(shape, dtype):
    zeros = (0,) * len(shape)
    return (shape, dtype, shape, lambda g, c: zeros)


def attend_kernel(
    core_ref, x_ref, mask_ref, wq_ref, wk_ref, wv_ref, bq_ref, bv_ref, wo_ref,
    q_ref, k_ref, v_ref, o_ref, ot_ref, lse_ref, part_ref, acc_ref,
):
    step = pl.program_id(0)
    rows = q_ref.shape[0]
    tile = min(256, rows)
    everything = x_ref[...]
    query = dot(everything[:rows], wq_ref[0]) + bq_ref[0]
    query = (query.astype(b16) * SCALE).astype(b16)
    key = dot(everything, wk_ref[0]).astype(b16)
    value = (dot(everything, wv_ref[0]) + bv_ref[0]).astype(b16)
    q_ref[...] = query
    k_ref[...] = key
    v_ref[...] = value
    query_t = query.astype(f32).T.astype(b16)
    value_t = value.astype(f32).T.astype(b16)
    keyed = jnp.concatenate([key, mask_ref[...]], 1)
    first_row = (lax.broadcasted_iota(jnp.int32, (LANES, tile), 0) == 0).astype(f32).astype(b16)
    empty = jnp.zeros((HEAD_DIM, tile), b16)
    for head in range(2):
        here = slice(head * HEAD_DIM, (head + 1) * HEAD_DIM)
        for start in range(0, rows, tile):
            part = query_t[here, start : start + tile]
            pieces = [part, empty] if head == 0 else [empty, part]
            scores = dot(keyed, jnp.concatenate(pieces + [first_row], 0))
            top = jnp.max(scores, 0, keepdims=True)
            weights = jnp.exp(scores - top)
            total = jnp.sum(weights, 0, keepdims=True)
            attended = dot(value_t[here], weights.astype(b16)) / total
            ot_ref[here, start : start + tile] = attended
            lse_ref[0, head : head + 1, start : start + tile] = top + jnp.log(total)
    attended = ot_ref[...].T.astype(b16)
    o_ref[...] = attended
    mixed = dot(attended, wo_ref[0])

    @pl.when(step == 0)
    def first():
        acc_ref[...] = mixed

    @pl.when(step > 0)
    def later():
        acc_ref[...] += mixed

    @pl.when(step == pl.num_programs(0) - 1)
    def last():
        part_ref[...] = acc_ref[...].astype(b16)


def attend(core, layer, x_all, mask, rows, attn_in, in_bias, attn_out):
    count, width = x_all.shape
    half = width // CORES
    pairs = half // LANES

    def columns(kind):
        return ((1, width, LANES), lambda g, c: (layer, 0, (kind * CORES + c) * pairs + g))

    def biases(kind):
        return ((1, 1, LANES), lambda g, c: (layer, 0, (kind * CORES + c) * pairs + g))

    lane_block = lambda g, c: (0, g)
    return call(
        attend_kernel, core, pairs,
        [
            all_of(x_all), all_of(mask),
            (attn_in, *columns(0)), (attn_in, *columns(1)), (attn_in, *columns(2)),
            (in_bias, *biases(0)), (in_bias, *biases(1)),
            (attn_out, (1, LANES, width), lambda g, c: (layer, c * pairs + g, 0)),
        ],
        [
            ((rows, half), b16, (rows, LANES), lane_block),
            ((count, half), b16, (count, LANES), lane_block),
            ((count, half), b16, (count, LANES), lane_block),
            ((rows, half), b16, (rows, LANES), lane_block),
            ((half, rows), f32, (LANES, rows), lambda g, c: (g, 0)),
            ((pairs, 8, rows), f32, (1, 8, rows), lambda g, c: (g, 0, 0)),
            full((rows, width), b16),
        ],
        [pltpu.VMEM((rows, width), f32)],
        8 * 10**9, 10**7,
    )


def feed_kernel(
    core_ref, x_ref, p0_ref, p1_ref, bo_ref, gain_ref, shift_ref, up_ref, bup_ref, down_ref,
    z_ref, h_ref, hr_ref, hrt_ref, act_ref, slope_ref, part_ref, acc_ref,
):
    step = pl.program_id(0)

    @pl.when(step == 0)
    def first():
        summed = x_ref[...].astype(f32) + (p0_ref[...].astype(f32) + p1_ref[...].astype(f32)) + bo_ref[0]
        z_ref[...] = summed
        unit, unused = norm_parts(summed)
        hidden = unit * gain_ref[0] + shift_ref[0]
        h_ref[...] = hidden
        low = hidden.astype(b16)
        hr_ref[...] = low
        hrt_ref[...] = low.astype(f32).T.astype(b16)
        acc_ref[...] = jnp.zeros_like(acc_ref)

    inner = dot(hr_ref[...], up_ref[0]) + bup_ref[0]
    phi = 0.5 + 0.5 * lax.erf(inner * SQRT_HALF)
    active = (inner * phi).astype(b16)
    slope_ref[...] = (phi + inner * (GAUSS * jnp.exp(-0.5 * inner * inner))).astype(b16)
    act_ref[...] = active
    acc_ref[...] += dot(active, down_ref[0])

    @pl.when(step == pl.num_programs(0) - 1)
    def last():
        part_ref[...] = acc_ref[...].astype(b16)


def hidden_tiles(ffn, tile):
    per = ffn // 4 // tile
    return 2 * per, lambda g, c: (2 * (g // per) + c) * per + g % per


def feed(core, layer, x, p0, p1, out_bias, gain, shift, ffn_in, ffn_in_bias, ffn_out):
    rows, width = x.shape
    ffn = ffn_in.shape[2]
    tile = 256
    steps, at = hidden_tiles(ffn, tile)
    half = ffn // CORES
    return call(
        feed_kernel, core, steps,
        [
            all_of(x), all_of(p0), all_of(p1),
            (out_bias, (1, 1, width), lambda g, c: (layer, 0, 0)),
            (gain, (1, 1, width), lambda g, c: (2 * layer, 0, 0)),
            (shift, (1, 1, width), lambda g, c: (2 * layer, 0, 0)),
            (ffn_in, (1, width, tile), lambda g, c: (layer, 0, at(g, c))),
            (ffn_in_bias, (1, 1, tile), lambda g, c: (layer, 0, at(g, c))),
            (ffn_out, (1, tile, width), lambda g, c: (layer, at(g, c), 0)),
        ],
        [
            full((rows, width), f32), full((rows, width), f32), full((rows, width), b16),
            full((width, rows), b16),
            ((rows, half), b16, (rows, tile), lambda g, c: (0, g)),
            ((rows, half), b16, (rows, tile), lambda g, c: (0, g)),
            full((rows, width), b16),
        ],
        [pltpu.VMEM((rows, width), f32)],
        5 * 10**9, 10**7,
    )


def norm_kernel(core_ref, h_ref, p0_ref, p1_ref, b_ref, gain_ref, shift_ref, z_ref, y_ref, low_ref):
    summed = h_ref[...] + (p0_ref[...].astype(f32) + p1_ref[...].astype(f32)) + b_ref[0]
    z_ref[...] = summed
    unit, unused = norm_parts(summed)
    result = unit * gain_ref[0] + shift_ref[0]
    y_ref[...] = result
    low_ref[...] = result.astype(b16)


def norm(core, layer, h, p0, p1, bias, gain, shift):
    rows, width = h.shape
    return call(
        norm_kernel, core, 1,
        [
            all_of(h), all_of(p0), all_of(p1),
            (bias, (1, 1, width), lambda g, c: (layer, 0, 0)),
            (gain, (1, 1, width), lambda g, c: (2 * layer + 1, 0, 0)),
            (shift, (1, 1, width), lambda g, c: (2 * layer + 1, 0, 0)),
        ],
        [full((rows, width), f32), full((rows, width), f32), full((rows, width), b16)],
        [],
        10**7, 10**7,
    )


def feed_back_kernel(
    fresh, core_ref, z_ref, p0_ref, p1_ref, bias_ref, shift_ref, dy_ref, more_ref, gain_ref,
    slope_ref, up_ref, down_ref,
    y_ref, dz_ref, dft_ref, small_ref, du_ref, dub_ref, part_ref, low_ref, acc_ref,
):
    step = pl.program_id(0)

    @pl.when(step == 0)
    def first():
        summed = z_ref[...]
        gain = gain_ref[0]
        if fresh:
            grad = dy_ref[...].astype(f32)
            summed = summed + (p0_ref[...].astype(f32) + p1_ref[...].astype(f32)) + bias_ref[0]
        else:
            grad = dy_ref[...] + more_ref[...].astype(f32)
        unit, inverse = norm_parts(summed)
        if fresh:
            y_ref[...] = (unit * gain + shift_ref[0]).astype(b16)
        back, gain_grad, shift_grad = norm_back(unit, inverse, gain, grad)
        dz_ref[...] = back
        low = back.astype(b16)
        low_ref[...] = low
        wide = low.astype(f32)
        dft_ref[...] = wide.T.astype(b16)
        small_ref[0:1, :] = gain_grad
        small_ref[1:2, :] = shift_grad
        small_ref[2:3, :] = jnp.sum(wide, 0, keepdims=True)
        acc_ref[...] = jnp.zeros_like(acc_ref)

    grad = dot_nt(low_ref[...], down_ref[0]) * slope_ref[...].astype(f32)
    low = grad.astype(b16)
    du_ref[...] = low
    dub_ref[0:1, :] = jnp.sum(low.astype(f32), 0, keepdims=True)
    acc_ref[...] += dot_nt(low, up_ref[0])

    @pl.when(step == pl.num_programs(0) - 1)
    def last():
        part_ref[...] = acc_ref[...].astype(b16)


def feed_back(core, layer, fresh, z, p0, p1, bias, shift, dy, more, gain, slope, ffn_in, ffn_out):
    rows, width = z.shape
    ffn = ffn_in.shape[2]
    tile = 256
    steps, at = hidden_tiles(ffn, tile)
    half = ffn // CORES
    return call(
        functools.partial(feed_back_kernel, fresh), core, steps,
        [
            all_of(z), all_of(p0), all_of(p1),
            (bias, (1, 1, width), lambda g, c: (layer, 0, 0)),
            (shift, (1, 1, width), lambda g, c: (2 * layer + 1, 0, 0)),
            all_of(dy), all_of(more),
            (gain, (1, 1, width), lambda g, c: (2 * layer + 1, 0, 0)),
            (slope, (rows, tile), lambda g, c: (0, g)),
            (ffn_in, (1, width, tile), lambda g, c: (layer, 0, at(g, c))),
            (ffn_out, (1, tile, width), lambda g, c: (layer, at(g, c), 0)),
        ],
        [
            full((rows, width) if fresh else (16, LANES), b16),
            full((rows, width), f32), full((width, rows), b16), full((8, width), f32),
            ((rows, half), b16, (rows, tile), lambda g, c: (0, g)),
            ((8, half), f32, (8, tile), lambda g, c: (0, g)),
            full((rows, width), b16),
        ],
        [pltpu.VMEM((rows, width), b16), pltpu.VMEM((rows, width), f32)],
        5 * 10**9, 10**7,
    )


def attend_back_kernel(
    core_ref, dz_ref, p0_ref, p1_ref, z_ref, gain_ref, mask_ref,
    q_ref, k_ref, v_ref, ot_ref, lse_ref, wq_ref, wk_ref, wv_ref, wo_ref,
    dz1_ref, dat_ref, small_ref, dq_ref, dk_ref, dv_ref, dqb_ref, dvb_ref, part_ref,
    low_ref, acc_ref, dk_acc, dv_acc, dqt_ref,
):
    step = pl.program_id(0)
    rows = q_ref.shape[0]
    tile = min(256, rows)

    @pl.when(step == 0)
    def first():
        grad = dz_ref[...] + (p0_ref[...].astype(f32) + p1_ref[...].astype(f32))
        unit, inverse = norm_parts(z_ref[...])
        back, gain_grad, shift_grad = norm_back(unit, inverse, gain_ref[0], grad)
        dz1_ref[...] = back
        low = back.astype(b16)
        low_ref[...] = low
        wide = low.astype(f32)
        dat_ref[...] = wide.T.astype(b16)
        small_ref[0:1, :] = gain_grad
        small_ref[1:2, :] = shift_grad
        small_ref[2:3, :] = jnp.sum(wide, 0, keepdims=True)
        acc_ref[...] = jnp.zeros_like(acc_ref)

    query = q_ref[...]
    key = k_ref[...]
    value = v_ref[...]
    outgrad = dot_nt(low_ref[...], wo_ref[0]).astype(b16)
    outgrad_t = outgrad.astype(f32).T.astype(b16)
    query_t = query.astype(f32).T.astype(b16)
    key_t = key.astype(f32).T.astype(b16)
    keyed = jnp.concatenate([key, mask_ref[...]], 1)
    first_row = (lax.broadcasted_iota(jnp.int32, (LANES, tile), 0) == 0).astype(f32).astype(b16)
    empty = jnp.zeros((HEAD_DIM, tile), b16)
    lane_head = lax.broadcasted_iota(jnp.int32, (rows, LANES), 1) // HEAD_DIM
    for head in range(2):
        here = slice(head * HEAD_DIM, (head + 1) * HEAD_DIM)
        mine = (lane_head == head).astype(f32)
        query_mine = (query.astype(f32) * mine).astype(b16)
        outgrad_mine = (outgrad.astype(f32) * mine).astype(b16)
        for start in range(0, rows, tile):
            now = slice(start, start + tile)
            piece = query_t[here, now]
            pieces = [piece, empty] if head == 0 else [empty, piece]
            scores = dot(keyed, jnp.concatenate(pieces + [first_row], 0))
            probs = jnp.exp(scores - lse_ref[0, head : head + 1, now])
            piece = outgrad_t[here, now]
            pieces = [piece, empty] if head == 0 else [empty, piece]
            grads = dot(value, jnp.concatenate(pieces, 0))
            delta = jnp.sum(piece.astype(f32) * ot_ref[here, now], 0, keepdims=True)
            score_grads = (probs * (grads - delta)).astype(b16)
            value_part = dot(probs.astype(b16), outgrad_mine[now])
            key_part = dot(score_grads, query_mine[now])
            if head == 0 and start == 0:
                dv_acc[...] = value_part
                dk_acc[...] = key_part
            else:
                dv_acc[...] += value_part
                dk_acc[...] += key_part
            dqt_ref[here, now] = dot(key_t[here], score_grads)
    dq = (dqt_ref[...].T * SCALE).astype(b16)
    dk = dk_acc[...].astype(b16)
    dv = dv_acc[...].astype(b16)
    dq_ref[...] = dq
    dk_ref[...] = dk
    dv_ref[...] = dv
    dqb_ref[0:1, :] = jnp.sum(dq.astype(f32), 0, keepdims=True)
    dvb_ref[0:1, :] = jnp.sum(dv.astype(f32), 0, keepdims=True)
    acc_ref[...] += dot_nt(dk, wk_ref[0]) + dot_nt(dv, wv_ref[0])
    acc_ref[:rows] += dot_nt(dq, wq_ref[0])

    @pl.when(step == pl.num_programs(0) - 1)
    def last():
        part_ref[...] = acc_ref[...].astype(b16)


def attend_back(core, layer, dz, p0, p1, z, gain, mask, kept, attn_in, attn_out):
    q, k, v, ot, lse = kept
    rows, width = z.shape
    count = k.shape[0]
    half = width // CORES
    pairs = half // LANES

    def columns(kind):
        return ((1, width, LANES), lambda g, c: (layer, 0, (kind * CORES + c) * pairs + g))

    lane_block = lambda g, c: (0, g)
    return call(
        attend_back_kernel, core, pairs,
        [
            all_of(dz), all_of(p0), all_of(p1), all_of(z),
            (gain, (1, 1, width), lambda g, c: (2 * layer, 0, 0)),
            all_of(mask),
            (q, (rows, LANES), lane_block), (k, (count, LANES), lane_block),
            (v, (count, LANES), lane_block), (ot, (LANES, rows), lambda g, c: (g, 0)),
            (lse, (1, 8, rows), lambda g, c: (g, 0, 0)),
            (attn_in, *columns(0)), (attn_in, *columns(1)), (attn_in, *columns(2)),
            (attn_out, (1, LANES, width), lambda g, c: (layer, c * pairs + g, 0)),
        ],
        [
            full((rows, width), f32), full((width, rows), b16), full((8, width), f32),
            ((rows, half), b16, (rows, LANES), lane_block),
            ((count, half), b16, (count, LANES), lane_block),
            ((count, half), b16, (count, LANES), lane_block),
            ((8, half), f32, (8, LANES), lane_block),
            ((8, half), f32, (8, LANES), lane_block),
            full((count, width), b16),
        ],
        [
            pltpu.VMEM((rows, width), b16), pltpu.VMEM((count, width), f32),
            pltpu.VMEM((count, LANES), f32), pltpu.VMEM((count, LANES), f32),
            pltpu.VMEM((LANES, rows), f32),
        ],
        16 * 10**9, 2 * 10**7,
    )


def down_grad_kernel(core_ref, dft_ref, act_ref, out_ref):
    out = dot(dft_ref[...], act_ref[...]).astype(b16)
    out_ref[...] = out.reshape(out_ref.shape)


def down_grad(core, dft, act, lines, posts, cols):
    rows = dft.shape[1]
    hidden = act.shape[1] // CORES
    return call(
        down_grad_kernel, core, CORES * posts,
        [
            (dft, (lines * cols, rows), lambda g, c: (g % posts, 0)),
            (act, (rows, hidden), lambda g, c: (0, g // posts)),
        ],
        [(
            (CORES, lines, posts, cols, hidden), b16, (1, lines, 1, cols, hidden),
            lambda g, c: (g // posts, 0, g % posts, 0, 0),
        )],
        [],
        2 * 10**9, 10**7,
    )[0]


def up_grad_kernel(core_ref, top_ref, low_ref, own_ref, sib_ref, out_ref):
    lhs = jnp.concatenate([top_ref[...], low_ref[...]], 0)
    mine = pl.program_id(0) % 2 == 0

    @pl.when(mine)
    def own():
        out_ref[...] = dot(lhs, own_ref[...]).astype(b16).reshape(out_ref.shape)

    @pl.when(jnp.logical_not(mine))
    def sib():
        out_ref[...] = dot(lhs, sib_ref[...]).astype(b16).reshape(out_ref.shape)


def up_grad(core, hrt, du_own, du_sib, lines, posts, depth, cols):
    rows = hrt.shape[1]

    def place(g, c):
        kind = g % 2
        return ((g // 2) // lines, kind + c - 2 * kind * c, (g // 2) % lines)

    def out_at(g, c):
        block, who, line = place(g, c)
        return (0, line, 2 * block + who, 0, 0)

    return call(
        up_grad_kernel, core, lines * posts,
        [
            (hrt, (depth, rows), lambda g, c: (c, 0)),
            (hrt, (depth, rows), lambda g, c: (2 + c, 0)),
            (du_own, (rows, cols), lambda g, c: (0, g // 2)),
            (du_sib, (rows, cols), lambda g, c: (0, g // 2)),
        ],
        [(
            (CORES, lines, posts, depth, cols), b16, (CORES, 1, 1, depth, cols), out_at,
        )],
        [],
        2 * 10**9, 10**7,
    )[0]


def in_grad_kernel(
    core_ref, dq_ref, dqs_ref, dk_ref, dks_ref, dv_ref, dvs_ref, x_ref, dat_ref, or_ref, out_ref
):
    core = core_ref[0]
    half = dq_ref.shape[1]
    unit = out_ref.shape[1] // 4
    units = half // unit
    everything = x_ref[...]
    parts = ((dq_ref, dqs_ref), (dk_ref, dks_ref), (dv_ref, dvs_ref))
    for kind, pair in enumerate(parts):
        for who, ref in enumerate(pair):
            owner = core if who == 0 else 1 - core
            piece = ref[...]
            result = dot_tn(piece, everything[: piece.shape[0]]).astype(b16)
            for at in range(units):
                place = (2 * kind + owner) * units + at
                where = pl.multiple_of(place % 3 * unit, unit)
                out_ref[place // 3, pl.ds(where, unit), :] = result[at * unit : (at + 1) * unit]
    result = dot(dat_ref[...], or_ref[...]).astype(b16)
    for at in range(out_ref.shape[0]):
        out_ref[at, 3 * unit :, :] = result[at * unit : (at + 1) * unit]


def in_grad(core, dq, dqs, dk, dks, dv, dvs, x_mine, dat, or_mine, blocks):
    width = dat.shape[0]
    arrays = (dq, dqs, dk, dks, dv, dvs, x_mine, dat, or_mine)
    return call(
        in_grad_kernel, core, 1, [all_of(array) for array in arrays],
        [full((blocks, 4 * width // blocks, x_mine.shape[1]), b16)],
        [],
        5 * 10**9, 10**7,
    )[0]


def build(mesh):
    clip_size, seq_size = mesh.shape["clip"], mesh.shape["seq"]
    columns = clip_size // CORES

    def shards(
        tokens, lengths, attn_in, in_bias, attn_out, out_bias, ffn_in, ffn_in_bias,
        ffn_out, ffn_out_bias, norm_gain, norm_bias, cotangent,
    ):
        held, slots, width = tokens.shape
        layers = attn_in.shape[0]
        ffn = ffn_in.shape[2]
        half = width // CORES
        quarter = ffn // 4
        posts = held * CORES
        lines = seq_size // posts
        rows = posts * slots
        count = rows * lines
        depth = width // clip_size
        aligned = columns == 2 and (ffn // seq_size) % LANES == 0

        clip_at = lax.axis_index("clip")
        seq_at = lax.axis_index("seq")
        core = clip_at % CORES
        column = clip_at // CORES
        post = seq_at // lines
        line = seq_at % lines
        core_arg = jnp.reshape(core, (1,)).astype(jnp.int32)
        parity = post % held

        def swap(array):
            pairs = [(at, at ^ 1) for at in range(clip_size)]
            return jax.tree.map(lambda a: lax.ppermute(a, "clip", pairs), array)

        def along_column(array, shift):
            pairs = [
                (at, ((at // CORES + shift) % columns) * CORES + at % CORES)
                for at in range(clip_size)
            ]
            return lax.ppermute(array, "clip", pairs)

        def along_line(array, shift):
            pairs = [
                (at, at // lines * lines + (at % lines + shift) % lines) for at in range(seq_size)
            ]
            return lax.ppermute(array, "seq", pairs)

        def along_post(array, shift):
            pairs = [
                (at, (at // lines + shift) % posts * lines + at % lines) for at in range(seq_size)
            ]
            return lax.ppermute(array, "seq", pairs)

        def shuffle_pairs(turn):
            pairs = []
            for col in range(columns):
                for cor in range(CORES):
                    for pos in range(posts):
                        for lin in range(lines):
                            source = (col * CORES + cor) * seq_size + pos * lines + lin
                            goal = (col * CORES + pos // held) * seq_size
                            goal += (held * cor + (pos + turn) % held) * lines + lin
                            pairs.append((source, goal))
            return pairs

        def to_rows(blocks):
            got = []
            for turn in range(held):
                piece = lax.dynamic_index_in_dim(blocks, (post + turn) % held, 0, False)
                got.append(lax.ppermute(piece, ("clip", "seq"), shuffle_pairs(turn)))
            return jnp.concatenate(got, 0)

        def from_rows(mine):
            got = []
            for turn in range(held):
                pairs = [(goal, source) for source, goal in shuffle_pairs(turn)]
                piece = mine[turn * slots : (turn + 1) * slots]
                got.append(lax.ppermute(piece, ("clip", "seq"), pairs))
            order = [jnp.stack([got[(at - turn) % held] for at in range(held)]) for turn in range(held)]
            result = order[0]
            for turn in range(1, held):
                result = jnp.where(parity == turn, order[turn], result)
            return result

        def joined(mine, other):
            return jnp.where(
                core == 0, jnp.concatenate([mine, other], 0), jnp.concatenate([other, mine], 0)
            )

        def half_of(array, which):
            return lax.dynamic_slice_in_dim(array, which * (rows // CORES), rows // CORES, 0)

        def gather_lines(mine):
            pieces = []
            for shift in range(1, lines):
                came = along_line(mine, shift)
                pieces.append(joined(came, swap(came)))
            return pieces

        sibling_lengths = swap(lengths)
        both_lengths = jnp.where(
            core == 0,
            jnp.concatenate([lengths, sibling_lengths]),
            jnp.concatenate([sibling_lengths, lengths]),
        )
        length = lax.dynamic_index_in_dim(both_lengths, post, 0, False)
        shift = jnp.arange(lines)[:, None, None, None]
        who = jnp.arange(CORES)[None, :, None, None]
        turn = jnp.arange(held)[None, None, :, None]
        slot = jnp.arange(slots)[None, None, None, :]
        source_post = held * who + (parity + turn) % held
        source_line = (line - shift) % lines
        position = ((source_post * lines + source_line) * slots + slot).reshape(count)
        lane = jnp.arange(LANES)[None, :]
        mask = jnp.where((lane == 0) & (position >= length)[:, None], -1e30, 0.0).astype(b16)

        in_bias3 = in_bias.reshape(layers, 1, -1)
        out_bias3 = out_bias.reshape(layers, 1, -1)
        up_bias3 = ffn_in_bias.reshape(layers, 1, -1)
        down_bias3 = ffn_out_bias.reshape(layers, 1, -1)
        gain3 = norm_gain.reshape(layers * 2, 1, -1)
        shift3 = norm_bias.reshape(layers * 2, 1, -1)

        my_tokens = to_rows(tokens)
        own = joined(my_tokens, swap(my_tokens))
        state = own
        mine = my_tokens
        kept = []
        for layer in range(layers):
            x_all = jnp.concatenate([own] + gather_lines(mine), 0)
            q, k, v, attended, attended_t, lse, part = attend(
                core_arg, layer, x_all, mask, rows, attn_in, in_bias3, attn_out
            )
            if layer == 0:
                my_cotangent = to_rows(after(cotangent, part))
            first_sum, hidden, low, low_t, active, slope, part_two = feed(
                core_arg, layer, state, part, swap(part), out_bias3, gain3, shift3,
                ffn_in, up_bias3, ffn_out,
            )
            attended_sibling = swap(after(attended, part_two))
            second = (hidden, part_two, swap(part_two))
            if layer < layers - 1:
                second_sum, state, own = norm(
                    core_arg, layer, *second, down_bias3, gain3, shift3
                )
                second = (second_sum, part_two, part_two)
                mine = half_of(own, core)
            kept.append(
                (x_all, (q, k, v, attended_t, lse), attended, attended_sibling, first_sum,
                 low_t, low, active, slope, second)
            )

        def quarters(array):
            split = array.reshape(array.shape[0], columns, CORES, depth)
            return jnp.where(core == 0, split[:, :, 0], split[:, :, 1]).reshape(array.shape[0], -1)

        def pick(array, at):
            return lax.dynamic_index_in_dim(array, at, 0, False)

        class Chain:
            def __init__(self, array, steps):
                self.steps = steps
                self.launch(array)

            def launch(self, array):
                (at, size, move, before), *self.steps = self.steps
                array = before(array)
                self.pieces = [pick(array, at)]
                for step in range(1, size):
                    self.pieces.append(move(pick(array, (at + step) % size), step))

            def land(self, gate=None):
                pieces = self.pieces
                if gate is not None:
                    pieces = lax.optimization_barrier(tuple(pieces) + (gate,))[:-1]
                total = pieces[0].astype(f32)
                for piece in pieces[1:]:
                    total = total + piece.astype(f32)
                return total

            def advance(self, gate=None):
                if not self.steps:
                    return
                self.launch(self.land(gate).astype(b16))

        def same(array):
            return array

        to_column = (column, columns, along_column)
        to_line = (line, lines, along_line)
        to_post = (post, posts, along_post)
        column_first = [(*to_column, same), (*to_line, same), (*to_post, same)]

        def by_line(array):
            return jnp.swapaxes(array.reshape(posts, lines, *array.shape[1:]), 0, 1)

        def by_column(array):
            return jnp.stack([array[:, at * depth : (at + 1) * depth] for at in range(columns)])

        line_first = [(*to_line, by_line), (*to_post, same), (*to_column, by_column)]

        def all_sum(array):
            total = array + swap(array)
            for size, move in ((columns, along_column), (lines, along_line), (posts, along_post)):
                moved = [move(total, step) for step in range(1, size)]
                for piece in moved:
                    total = total + piece
            return total

        def line_sum(dx):
            blocks = dx.reshape(lines, CORES, rows // CORES, width)
            keep = lax.dynamic_index_in_dim(blocks, core, 1, False)
            came = swap(lax.dynamic_index_in_dim(blocks, 1 - core, 1, False))
            summed = keep.astype(f32) + came.astype(f32)
            moved = [
                along_line(summed[step].astype(b16), lines - step) for step in range(1, lines)
            ]
            return summed, moved

        def spread(array):
            array = lax.psum_scatter(
                array.astype(b16), "seq", scatter_dimension=1, tiled=True
            ).astype(b16)
            return lax.psum_scatter(array, "clip", scatter_dimension=0, tiled=True).astype(f32)

        grad = joined(my_cotangent, swap(my_cotangent))
        more = grad
        chains = [None] * layers
        smalls = [None] * layers
        seq_cols, seq_ffn = width // seq_size, ffn // seq_size
        for layer in range(layers - 1, -1, -1):
            (x_all, attend_kept, attended, attended_sibling, first_sum, low_t, low, active, slope,
             second) = kept[layer]
            fresh = layer == layers - 1
            result, dz2, df_t, small_two, du, du_sums, part = feed_back(
                core_arg, layer, fresh, *second, down_bias3, shift3, grad, more, gain3, slope,
                ffn_in, ffn_out,
            )
            if fresh:
                out_tokens = from_rows(half_of(after(result, part), core))
            part_sibling = swap(part)
            du_sibling = swap(du)
            if aligned:
                down = down_grad(core_arg, df_t, active, lines, posts, seq_cols)
                down_chain = Chain(down, column_first)
                if not fresh:
                    for chain in chains[layer + 1]:
                        chain.advance(down)
                    up = up_grad(core_arg, low_t, du, du_sibling, lines, posts, depth, seq_ffn)
                    up_chain = Chain(up, column_first)
            dz1, da_t, small_one, dq, dk, dv, dq_sums, dv_sums, dx = attend_back(
                core_arg, layer, dz2, part, part_sibling, first_sum, gain3, mask, attend_kept,
                attn_in, attn_out,
            )
            summed, moved = line_sum(dx)
            dq_s, dk_s, dv_s = swap((dq, dk, dv))
            if aligned:
                if fresh:
                    up = up_grad(core_arg, low_t, du, after(du_sibling, dx), lines, posts, depth, seq_ffn)
                    up_chain = Chain(up, column_first)
                else:
                    for chain in chains[layer + 1]:
                        chain.advance(dx)
                down_chain.advance(dx)
                if not fresh:
                    up_chain.advance(dx)
                features = jnp.where(
                    core == 0,
                    jnp.concatenate([attended[:, :depth], attended_sibling[:, :depth]], 1),
                    jnp.concatenate([attended_sibling[:, depth:], attended[:, depth:]], 1),
                )
                into = in_grad(
                    core_arg, dq, dq_s, dk, dk_s, dv, dv_s, quarters(x_all), da_t, features,
                    seq_size,
                )
                chains[layer] = [Chain(into, line_first), up_chain, down_chain]
            else:
                into = [
                    jnp.concatenate([jnp.where(core == 0, a, b), jnp.where(core == 0, b, a)], 1)
                    for a, b in (
                        (dot_tn(x_all[:rows], dq), dot_tn(x_all[:rows], dq_s)),
                        (dot_tn(x_all, dk), dot_tn(x_all, dk_s)),
                        (dot_tn(x_all, dv), dot_tn(x_all, dv_s)),
                    )
                ]
                proj = jnp.zeros((CORES, half, width), f32)
                proj = lax.dynamic_update_slice_in_dim(proj, dot(da_t, attended).T[None], core, 0)
                up = jnp.zeros((2, CORES, width, quarter), f32)
                own_up = dot(low_t, du).reshape(width, 2, 1, quarter).transpose(1, 2, 0, 3)
                up = lax.dynamic_update_slice_in_dim(up, own_up, core, 1)
                down = jnp.zeros((2, CORES, quarter, width), f32)
                own_down = dot(df_t, active).T.reshape(2, 1, quarter, width)
                down = lax.dynamic_update_slice_in_dim(down, own_down, core, 1)
                chains[layer] = (
                    spread(jnp.concatenate(into, 1) * 0.5),
                    spread(proj.reshape(width, width)),
                    spread(up.transpose(2, 0, 1, 3).reshape(width, ffn)),
                    spread(down.reshape(ffn, width)),
                )

            total = summed[0]
            for piece in moved:
                total = total + piece.astype(f32)
            if layer > 0:
                low_total = total.astype(b16)
                more = joined(low_total, swap(low_total))
                grad = dz1
            else:
                grad_tokens = from_rows((total + half_of(dz1, core)).astype(b16))

            in_sums = jnp.zeros((2, CORES, half), f32)
            own_sums = jnp.stack([dq_sums[:1], dv_sums[:1]])
            in_sums = lax.dynamic_update_slice_in_dim(in_sums, own_sums, core, 1)
            up_sums = jnp.zeros((2, CORES, quarter), f32)
            up_sums = lax.dynamic_update_slice_in_dim(
                up_sums, du_sums[0].reshape(2, 1, quarter), core, 1
            )
            smalls[layer] = jnp.concatenate([
                in_sums.reshape(-1), up_sums.reshape(-1),
                0.5 * small_one[2], 0.5 * small_two[2],
                0.5 * small_one[0], 0.5 * small_two[0], 0.5 * small_one[1], 0.5 * small_two[1],
            ])

        summed = all_sum(jnp.stack(smalls))

        def share(start, size):
            piece = summed[:, start : start + size]
            return lax.dynamic_slice_in_dim(piece, seq_at * (size // seq_size), size // seq_size, 1)

        at = 2 * width + ffn
        if aligned:
            waiting = [chain for layer in range(layers) for chain in chains[layer]]
            while any(chain.steps for chain in waiting):
                for chain in waiting:
                    chain.advance()
            for layer in range(layers):
                into, up, down = (chain.land() for chain in chains[layer])
                into = into.T
                chains[layer] = (into[:, : 3 * seq_cols], into[:, 3 * seq_cols :], up, down.T)
        matrices = [jnp.stack([chains[layer][which] for layer in range(layers)]) for which in range(4)]
        return (
            out_tokens,
            grad_tokens,
            matrices[0],
            share(0, 2 * width),
            matrices[1],
            share(at, width),
            matrices[2],
            share(2 * width, ffn),
            matrices[3],
            share(at + width, width),
            jnp.stack([share(at + 2 * width, width), share(at + 3 * width, width)], 1),
            jnp.stack([share(at + 4 * width, width), share(at + 5 * width, width)], 1),
        )

    return shards


def solution(mesh):
    rowed = P("clip", "seq", None)
    in_specs = (rowed, P("clip")) + (P(),) * 10 + (rowed,)
    out_specs = (
        rowed,
        rowed,
        P(None, "clip", "seq"),
        P(None, "seq"),
        P(None, "clip", "seq"),
        P(None, "seq"),
        P(None, "clip", "seq"),
        P(None, "seq"),
        P(None, "clip", "seq"),
        P(None, "seq"),
        P(None, None, "seq"),
        P(None, None, "seq"),
    )
    return jax.shard_map(
        build(mesh), mesh=mesh, in_specs=in_specs, out_specs=out_specs, check_vma=False
    )
```

```python
from copy import copy as duplicate
import functools

import jax
import jax.numpy as jnp
from jax import lax
from jax.experimental import pallas as pl
from jax.experimental.pallas import tpu as pltpu
from jax.sharding import PartitionSpec as P

HEADS = 12
HEAD_DIM = 64
CORES = 2
LANES = 128
SCALE = HEAD_DIM**-0.5
SQRT_HALF = 0.5**0.5
GAUSS = 0.3989422804014327
EPS = 1e-05
VMEM = 56 * 1024 * 1024

f32 = jnp.float32
b16 = jnp.bfloat16


def dot(a, b):
    return lax.dot_general(a, b, (((1,), (0,)), ((), ())), preferred_element_type=f32)


def dot_nt(a, b):
    return lax.dot_general(a, b, (((1,), (1,)), ((), ())), preferred_element_type=f32)


def dot_tn(a, b):
    return lax.dot_general(a, b, (((0,), (0,)), ((), ())), preferred_element_type=f32)


def norm_parts(values):
    center = values - jnp.mean(values, -1, keepdims=True)
    inverse = lax.rsqrt(jnp.mean(center * center, -1, keepdims=True) + EPS)
    return center * inverse, inverse


def norm_back(unit, inverse, gain, grad):
    scaled = grad * gain
    mean_one = jnp.mean(scaled, -1, keepdims=True)
    mean_two = jnp.mean(scaled * unit, -1, keepdims=True)
    back = inverse * (scaled - mean_one - unit * mean_two)
    return back, jnp.sum(grad * unit, 0, keepdims=True), jnp.sum(grad, 0, keepdims=True)


def after(array, *others):
    return lax.optimization_barrier((array,) + others)[0]


def call(kernel, core, grid, ins, outs, scratch, flops, moved):
    in_specs = [pl.BlockSpec(block, lambda g, c, at=at: at(g, c[0])) for unused, block, at in ins]
    out_specs = [pl.BlockSpec(block, lambda g, c, at=at: at(g, c[0])) for s, d, block, at in outs]
    return pl.pallas_call(
        kernel,
        grid_spec=pltpu.PrefetchScalarGridSpec(
            num_scalar_prefetch=1,
            grid=(grid,),
            in_specs=in_specs,
            out_specs=out_specs,
            scratch_shapes=scratch,
        ),
        out_shape=[jax.ShapeDtypeStruct(shape, dtype) for shape, dtype, b, at in outs],
        compiler_params=pltpu.CompilerParams(
            dimension_semantics=("arbitrary",), vmem_limit_bytes=VMEM
        ),
        cost_estimate=pl.CostEstimate(flops=flops, bytes_accessed=moved, transcendentals=0),
    )(core, *[array for array, b, at in ins])


def all_of(array):
    zeros = (0,) * array.ndim
    return (array, array.shape, lambda g, c: zeros)


def full(shape, dtype):
    zeros = (0,) * len(shape)
    return (shape, dtype, shape, lambda g, c: zeros)


class Geometry:
    def __init__(self, mesh, tokens, ffn):
        self.clip_size, self.seq_size = mesh.shape["clip"], mesh.shape["seq"]
        self.columns = self.clip_size // CORES
        self.held, self.slots, self.width = tokens.shape
        self.ffn = ffn
        self.posts = self.held * CORES
        self.lines = self.seq_size // self.posts
        self.tile = CORES * self.slots
        self.rows = self.held * self.tile
        self.count = self.rows * self.lines
        self.half = self.width // CORES
        self.pairs = self.half // LANES
        self.heads = 2 * self.pairs
        self.quarter = ffn // 4
        self.depth = self.width // self.clip_size
        self.aligned = self.columns == 2 and (ffn // self.seq_size) % LANES == 0

    def locate(self):
        self.clip = lax.axis_index("clip")
        self.seq = lax.axis_index("seq")
        self.core = self.clip % CORES
        self.column = self.clip // CORES
        self.post = self.seq // self.lines
        self.line = self.seq % self.lines
        self.parity = self.post % self.held

    def sibling(self):
        return self.clip + 1 - 2 * self.core, self.seq

    def on_line(self, shift):
        return self.clip, self.post * self.lines + (self.line + shift) % self.lines

    def on_post(self, shift):
        return self.clip, (self.post + shift) % self.posts * self.lines + self.line

    def on_column(self, shift):
        return (self.column + shift) % self.columns * CORES + self.core, self.seq

    def goal(self, turn):
        post = self.held * self.core + (self.post + turn) % self.held
        return self.column * CORES + self.post // self.held, post * self.lines + self.line

    def origin(self, turn, who):
        post = self.held * who + (self.parity + turn) % self.held
        return self.column * CORES + self.post // self.held, post * self.lines + self.line

    def blocked(self, turn):
        return jnp.logical_and(self.post // self.held == self.core, turn == 0)


def remote(source, target, send, receive, device):
    return pltpu.make_async_remote_copy(
        src_ref=source, dst_ref=target, send_sem=send, recv_sem=receive,
        device_id=device, device_id_type=pl.DeviceIdType.MESH,
    )


def meet(geo, devices):
    barrier = pltpu.get_barrier_semaphore()
    total = 0
    for device in devices:
        other = jnp.logical_or(device[0] != geo.clip, device[1] != geo.seq)

        @pl.when(other)
        def greet(device=device):
            pl.semaphore_signal(
                barrier, inc=1, device_id=device, device_id_type=pl.DeviceIdType.MESH
            )

        total = total + other.astype(jnp.int32)
    pl.semaphore_wait(barrier, total)


def loop(count, body):
    def step(at, carry):
        body(at)
        return carry

    lax.fori_loop(0, count, step, 0)


def gelu_parts(inner):
    bell = jnp.exp(-0.5 * inner * inner)
    t = 1.0 / (1.0 + (0.3275911 * SQRT_HALF) * jnp.abs(inner))
    series = t * (0.5 * 0.254829592 + t * (0.5 * -0.284496736 + t * (
        0.5 * 1.421413741 + t * (0.5 * -1.453152027 + t * (0.5 * 1.061405429)))))
    tail = series * bell
    phi = jnp.where(inner >= 0.0, 1.0 - tail, tail)
    return phi, phi + inner * (GAUSS * bell)


KEPT = ("xall", "kx", "v", "q", "ot", "lse", "o", "z1", "hrt", "act", "slope", "z2")


def kept_shapes(geo):
    rows, width, half, count = geo.rows, geo.width, geo.half, geo.count
    return {
        "xall": ((count, width), b16),
        "kx": ((geo.pairs, count, 2 * LANES), b16),
        "v": ((count, half), b16),
        "q": ((rows, half), b16),
        "ot": ((half, rows), f32),
        "lse": ((geo.heads, 8, rows), f32),
        "o": ((rows, half), b16),
        "z1": ((rows, width), f32),
        "hrt": ((width, rows), b16),
        "act": ((rows, geo.ffn // CORES), b16),
        "slope": ((rows, geo.ffn // CORES), b16),
        "z2": ((rows, width), f32),
    }


def forward_kernel(geo, layers, *refs):
    refs = list(refs)

    def take(count):
        taken = refs[:count]
        del refs[:count]
        return taken

    tokens, cotangent, w_in, w_out, w_up, w_down = take(6)
    lens, in_bias, out_bias, up_bias, down_bias, gains, shifts = take(7)
    out_tokens, cot_rows = take(2)
    stored = [dict(zip(KEPT, take(len(KEPT)))) for unused in range(layers)]
    kept = [dict(zip(KEPT, take(len(KEPT)))) for unused in range(layers)]
    win, wout, wup, wdown = take(4)
    qx, vt, state, hidden, low_out, lens_there, psend, precv = take(8)
    (load_sem, save_sem, tok_sem, tok_send, tok_recv, cot_sem, cot_send, cot_recv, sib_send,
     sib_recv, line_send, line_recv, pass_send, pass_recv, part_send, part_recv, out_sem,
     out_send, out_recv, len_sem) = take(20)

    geo = duplicate(geo)
    geo.locate()
    core, tile, slots = geo.core, geo.tile, geo.slots
    held, lines, rows, width, half = geo.held, geo.lines, geo.rows, geo.width, geo.half
    quarter, pairs = geo.quarter, geo.pairs
    sibling = geo.sibling()

    loads = []
    for layer in range(layers):
        parts = [
            (w_in.at[layer, :, pl.ds(pl.multiple_of((kind * CORES + core) * half, half), half)],
             win.at[layer, kind])
            for kind in range(3)
        ]
        parts.append((w_out.at[layer, pl.ds(pl.multiple_of(core * half, half), half), :], wout.at[layer]))
        for block in range(2):
            at = pl.ds(pl.multiple_of((2 * block + core) * quarter, quarter), quarter)
            parts.append((w_up.at[layer, :, at], wup.at[layer, block]))
            parts.append((w_down.at[layer, at, :], wdown.at[layer, block]))
        loads.append([
            pltpu.make_async_copy(source, target, load_sem.at[layer, at])
            for at, (source, target) in enumerate(parts)
        ])
    for copy in loads[0]:
        copy.start()

    sources = [geo.origin(turn, who) for turn in range(held) for who in range(CORES)]
    goals = [geo.goal(turn) for turn in range(held)]
    goals = goals + [(device[0] + 1 - 2 * (device[0] % CORES), device[1]) for device in goals]
    near = [sibling] + [geo.on_line(shift) for shift in range(1, lines)]
    meet(geo, near + sources + goals)

    first = kept[0]["xall"]

    def block_at(turn, who, shift=0):
        start = shift * rows + turn * tile + who * slots
        return pl.ds(start if isinstance(start, int) else pl.multiple_of(start, slots), slots)

    def token_copies(turn, who):
        mine = tokens.at[(geo.post + turn) % held]
        place = first.at[block_at(turn, who)]
        own = pltpu.make_async_copy(mine, place, tok_sem.at[turn])
        return own, remote(mine, place, tok_send.at[turn], tok_recv.at[turn], geo.goal(turn))

    def token_start(turn):
        own, there = token_copies(turn, geo.post // held)
        pl.when(geo.blocked(turn))(own.start)
        pl.when(jnp.logical_not(geo.blocked(turn)))(there.start)

    def token_wait(turn):
        own, there = token_copies(turn, core)
        pl.when(geo.blocked(turn))(own.wait)
        pl.when(jnp.logical_not(geo.blocked(turn)))(there.wait)

    def to_sibling(array, turn, who, shift, send, receive):
        place = array.at[block_at(turn, who, shift)]
        return remote(place, place, send, receive, sibling)

    def to_line(layer, turn, shift):
        array = kept[layer]["xall"]
        source = array.at[block_at(turn, core)]
        target = array.at[block_at(turn, core, shift)]
        return remote(
            source, target, line_send.at[layer, turn, shift - 1], line_recv.at[layer, turn, shift - 1],
            geo.on_line(shift),
        )

    for turn in range(held):
        token_start(turn)
    len_copy = remote(lens, lens_there, len_sem.at[0], len_sem.at[1], sibling)
    len_copy.start()

    def clear(at):
        qx[at] = jnp.zeros(qx.shape[1:], b16)
        qx[at, LANES : LANES + 16, :] = (
            lax.broadcasted_iota(jnp.int32, (16, rows), 0) == 0
        ).astype(f32).astype(b16)

    loop(geo.heads, clear)
    len_copy.wait()
    lengths = jnp.where(geo.post // held == core, lens[...], lens_there[...])
    length = lengths[0:1, :]
    for clip in range(1, held):
        length = jnp.where(geo.parity == clip, lengths[clip : clip + 1, :], length)
    lane = lax.broadcasted_iota(jnp.int32, (slots, LANES), 1)
    slot = lax.broadcasted_iota(jnp.int32, (slots, LANES), 0)
    for shift in range(lines):
        for turn in range(held):
            for who in range(CORES):
                post = held * who + (geo.parity + turn) % held
                line = (geo.line + lines - shift) % lines
                outside = (post * lines + line) * slots + slot >= length
                mask = jnp.where(jnp.logical_and(lane == 0, outside), -1e30, 0.0).astype(b16)
                for layer in range(layers):
                    for pair in range(pairs):
                        kept[layer]["kx"][pair, block_at(turn, who, shift), LANES:] = mask

    for turn in range(held):
        token_wait(turn)
        to_sibling(first, turn, core, 0, sib_send.at[turn], sib_recv.at[turn]).start()
        for shift in range(1, lines):
            to_line(0, turn, shift).start()
    for copy in loads[0]:
        copy.wait()
    for copy in loads[1]:
        copy.start()

    def cot_copies(turn, flip):
        mine = cotangent.at[(geo.post + turn) % held]
        place = cot_rows.at[block_at(turn, geo.post // held)]
        goal = geo.goal(turn)
        if flip:
            goal = (goal[0] + 1 - 2 * (goal[0] % CORES), goal[1])
        own = pltpu.make_async_copy(mine, place, cot_sem.at[turn, flip])
        there = remote(
            mine, place, cot_send.at[turn, flip], cot_recv.at[turn, geo.post // held], goal
        )
        here = jnp.logical_and(goal[0] == geo.clip, goal[1] == geo.seq)
        return own, there, here

    def cot_start():
        for turn in range(held):
            for flip in range(CORES):
                own, there, here = cot_copies(turn, flip)
                pl.when(here)(own.start)
                pl.when(jnp.logical_not(here))(there.start)

    def cot_wait():
        for turn in range(held):
            for flip in range(CORES):
                own, there, here = cot_copies(turn, flip)
                pl.when(here)(own.wait)
                pl.when(jnp.logical_not(here))(there.wait_send)
            for who in range(CORES):
                source = geo.origin(turn, who)
                place = cot_rows.at[block_at(turn, who)]
                there = remote(
                    cotangent.at[0], place, cot_send.at[turn, 0], cot_recv.at[turn, who], source
                )
                here = jnp.logical_and(source[0] == geo.clip, source[1] == geo.seq)
                pl.when(jnp.logical_not(here))(there.wait_recv)

    def key_tile(layer, at):
        keep = kept[layer]
        now = pl.ds(pl.multiple_of(at, tile), tile)
        x = keep["xall"][now, :]
        key = dot(x, win[layer, 1]).astype(b16)
        for pair in range(pairs):
            keep["kx"][pair, now, :LANES] = key[:, pair * LANES : (pair + 1) * LANES]
        bias = in_bias[layer : layer + 1, pl.ds(pl.multiple_of(width + core * half, half), half)]
        value = (dot(x, win[layer, 2]) + bias).astype(b16)
        keep["v"][now, :] = value
        vt[:, now] = value.astype(f32).T.astype(b16)

    def query_tile(layer, at):
        keep = kept[layer]
        now = pl.ds(pl.multiple_of(at, tile), tile)
        bias = in_bias[layer : layer + 1, pl.ds(pl.multiple_of(core * half, half), half)]
        query = (dot(keep["xall"][now, :], win[layer, 0]) + bias).astype(b16)
        query = (query * SCALE).astype(b16)
        keep["q"][now, :] = query
        turned = query.astype(f32).T.astype(b16)
        for head in range(geo.heads):
            inside = head % 2 * HEAD_DIM
            qx[head, inside : inside + HEAD_DIM, now] = (
                turned[head * HEAD_DIM : (head + 1) * HEAD_DIM]
            )

    def attend_tile(layer, turn):
        keep = kept[layer]
        now = pl.ds(pl.multiple_of(turn * tile, tile), tile)

        def pair_step(pair):
            keys = keep["kx"][pair]
            for inside in range(2):
                head = 2 * pair + inside
                here = pl.ds(pl.multiple_of(head * HEAD_DIM, HEAD_DIM), HEAD_DIM)
                scores = dot(keys, qx[head, :, now])
                top = jnp.max(scores, 0, keepdims=True)
                weights = jnp.exp(scores - top)
                total = jnp.sum(weights, 0, keepdims=True)
                attended = dot(vt[here, :], weights.astype(b16)) / total
                keep["ot"][here, now] = attended
                keep["lse"][head, 0:1, now] = top + jnp.log(total)

        loop(pairs, pair_step)
        attended = keep["ot"][:, now].T.astype(b16)
        keep["o"][now, :] = attended
        share(2 * layer, turn, dot(attended, wout[layer]))

    def part_copy(which, turn):
        now = pl.ds(pl.multiple_of(turn * tile, tile), tile)
        return remote(
            psend.at[which, now, :], precv.at[which, now, :], part_send.at[which, turn],
            part_recv.at[which, turn], sibling,
        )

    def share(which, turn, part):
        now = pl.ds(pl.multiple_of(turn * tile, tile), tile)
        psend[which, now, :] = part.astype(b16)
        part_copy(which, turn).start()

    def collect(which, turn):
        now = pl.ds(pl.multiple_of(turn * tile, tile), tile)
        part_copy(which, turn).wait()
        return psend[which, now, :].astype(f32) + precv[which, now, :].astype(f32)

    def feed_tile(layer, turn):
        keep = kept[layer]
        now = pl.ds(pl.multiple_of(turn * tile, tile), tile)
        x = first[now, :].astype(f32) if layer == 0 else state[now, :]
        summed = x + collect(2 * layer, turn) + out_bias[layer : layer + 1, :]
        keep["z1"][now, :] = summed
        unit, unused = norm_parts(summed)
        normal = unit * gains[2 * layer : 2 * layer + 1, :] + shifts[2 * layer : 2 * layer + 1, :]
        hidden[now, :] = normal
        low = normal.astype(b16)
        keep["hrt"][:, now] = low.astype(f32).T.astype(b16)
        size = min(256, quarter)
        total = None
        for block in range(2):
            for start in range(0, quarter, size):
                at = block * quarter + start
                bias = up_bias[
                    layer : layer + 1,
                    pl.ds(pl.multiple_of((2 * block + core) * quarter + start, size), size),
                ]
                inner = dot(low, wup[layer, block, :, start : start + size]) + bias
                phi, slope = gelu_parts(inner)
                active = (inner * phi).astype(b16)
                keep["act"][now, at : at + size] = active
                keep["slope"][now, at : at + size] = slope.astype(b16)
            part = dot(keep["act"][now, block * quarter : (block + 1) * quarter], wdown[layer, block])
            total = part if total is None else total + part
        share(2 * layer + 1, turn, total)

    def norm_tile(layer, turn):
        keep = kept[layer]
        now = pl.ds(pl.multiple_of(turn * tile, tile), tile)
        summed = hidden[now, :] + collect(2 * layer + 1, turn) + down_bias[layer : layer + 1, :]
        keep["z2"][now, :] = summed
        unit, unused = norm_parts(summed)
        at = 2 * layer + 1
        result = unit * gains[at : at + 1, :] + shifts[at : at + 1, :]
        if layer < layers - 1:
            state[now, :] = result
            kept[layer + 1]["xall"][now, :] = result.astype(b16)
        else:
            low_out[now, :] = result.astype(b16)

    saves = []

    def save(layer, names):
        for name in names:
            copy = pltpu.make_async_copy(
                kept[layer][name], stored[layer][name], save_sem.at[layer, KEPT.index(name)]
            )
            copy.start()
            saves.append(copy)

    for layer in range(layers):
        x_all = kept[layer]["xall"]
        if layer == 0:
            for turn in range(held):
                to_sibling(x_all, turn, core, 0, sib_send.at[turn], sib_recv.at[turn]).wait_send()
                to_sibling(x_all, turn, 1 - core, 0, sib_send.at[turn], sib_recv.at[turn]).wait_recv()
                key_tile(layer, turn * tile)
                query_tile(layer, turn * tile)
        else:
            for copy in loads[layer]:
                copy.wait()

            def own_tile(turn):
                key_tile(layer, turn * tile)
                query_tile(layer, turn * tile)

            loop(held, own_tile)
        for shift in range(1, lines):
            for turn in range(held):
                to_line(layer, turn, shift).wait()
                to_sibling(
                    x_all, turn, core, shift,
                    pass_send.at[layer, turn, shift - 1], pass_recv.at[layer, turn, shift - 1],
                ).start()
        for shift in range(1, lines):
            for turn in range(held):
                send = pass_send.at[layer, turn, shift - 1]
                receive = pass_recv.at[layer, turn, shift - 1]
                to_sibling(x_all, turn, core, shift, send, receive).wait_send()
                to_sibling(x_all, turn, 1 - core, shift, send, receive).wait_recv()
                key_tile(layer, shift * rows + turn * tile)
        if layer == 0:
            cot_start()
        save(layer, ("xall", "kx", "v", "q"))
        loop(held, functools.partial(attend_tile, layer))
        save(layer, ("ot", "lse", "o"))
        loop(held, functools.partial(feed_tile, layer))
        save(layer, ("z1", "hrt", "act", "slope"))
        for turn in range(held):
            norm_tile(layer, turn)
            if layer < layers - 1:
                for shift in range(1, lines):
                    to_line(layer + 1, turn, shift).start()
        save(layer, ("z2",))

    def out_copies(turn, place):
        mine = low_out.at[block_at(turn, core)]
        own = pltpu.make_async_copy(mine, place, out_sem.at[turn])
        return own, remote(mine, place, out_send.at[turn], out_recv.at[turn], geo.origin(turn, core))

    for turn in range(held):
        own, there = out_copies(turn, out_tokens.at[geo.parity])
        pl.when(geo.blocked(turn))(own.start)
        pl.when(jnp.logical_not(geo.blocked(turn)))(there.start)
    cot_wait()
    for turn in range(held):
        own, there = out_copies(turn, out_tokens.at[(geo.post + turn) % held])
        pl.when(geo.blocked(turn))(own.wait)
        pl.when(jnp.logical_not(geo.blocked(turn)))(there.wait)
    for copy in saves:
        copy.wait()


def forward(geo, layers, tokens, cotangent, lens, weights, vectors):
    width, rows, half, ffn = geo.width, geo.rows, geo.half, geo.ffn
    shapes = kept_shapes(geo)
    any_spec = pl.BlockSpec(memory_space=pl.ANY)
    vmem_spec = pl.BlockSpec(memory_space=pltpu.VMEM)
    out_shape = [
        jax.ShapeDtypeStruct(tokens.shape, b16),
        jax.ShapeDtypeStruct((rows, width), b16),
    ]
    out_shape += [jax.ShapeDtypeStruct(*shapes[name]) for unused in range(layers) for name in KEPT]
    scratch = [pltpu.VMEM(*shapes[name]) for unused in range(layers) for name in KEPT]
    scratch += [
        pltpu.VMEM((layers, 3, width, half), b16),
        pltpu.VMEM((layers, half, width), b16),
        pltpu.VMEM((layers, 2, width, geo.quarter), b16),
        pltpu.VMEM((layers, 2, geo.quarter, width), b16),
        pltpu.VMEM((geo.heads, 2 * LANES, rows), b16),
        pltpu.VMEM((half, geo.count), b16),
        pltpu.VMEM((rows, width), f32),
        pltpu.VMEM((rows, width), f32),
        pltpu.VMEM((rows, width), b16),
        pltpu.VMEM(lens.shape, jnp.int32),
        pltpu.VMEM((2 * layers, rows, width), b16),
        pltpu.VMEM((2 * layers, rows, width), b16),
    ]
    held, lines = geo.held, max(geo.lines - 1, 1)
    dma = pltpu.SemaphoreType.DMA
    scratch += [dma(shape) for shape in (
        (layers, 8), (layers, len(KEPT)), (held,), (held,), (held,),
        (held, CORES), (held, CORES), (held, CORES), (held,), (held,),
        (layers, held, lines), (layers, held, lines), (layers, held, lines), (layers, held, lines),
        (2 * layers, held), (2 * layers, held), (held,), (held,), (held,), (2,),
    )]
    results = pl.pallas_call(
        functools.partial(forward_kernel, geo, layers),
        out_shape=out_shape,
        in_specs=[any_spec] * 6 + [vmem_spec] * 7,
        out_specs=[any_spec] * len(out_shape),
        scratch_shapes=scratch,
        compiler_params=pltpu.CompilerParams(
            collective_id=0, has_side_effects=True, vmem_limit_bytes=VMEM
        ),
        cost_estimate=pl.CostEstimate(flops=3 * 10**10, bytes_accessed=4 * 10**7, transcendentals=0),
    )(tokens, cotangent, *weights, lens, *vectors)
    count = len(KEPT)
    kept = [
        dict(zip(KEPT, results[2 + layer * count : 2 + (layer + 1) * count]))
        for layer in range(layers)
    ]
    return results[0], results[1], kept


def hidden_tiles(ffn, tile):
    per = ffn // 4 // tile
    return 2 * per, lambda g, c: (2 * (g // per) + c) * per + g % per


def feed_back_kernel(
    core_ref, z_ref, dy_ref, more_ref, gain_ref, slope_ref, up_ref, down_ref,
    dz_ref, dft_ref, small_ref, du_ref, dub_ref, part_ref, low_ref, acc_ref,
):
    step = pl.program_id(0)

    @pl.when(step == 0)
    def first():
        gain = gain_ref[0]
        grad = dy_ref[...].astype(f32) + more_ref[...].astype(f32)
        unit, inverse = norm_parts(z_ref[...])
        back, gain_grad, shift_grad = norm_back(unit, inverse, gain, grad)
        dz_ref[...] = back
        low = back.astype(b16)
        low_ref[...] = low
        wide = low.astype(f32)
        dft_ref[...] = wide.T.astype(b16)
        small_ref[0:1, :] = gain_grad
        small_ref[1:2, :] = shift_grad
        small_ref[2:3, :] = jnp.sum(wide, 0, keepdims=True)
        acc_ref[...] = jnp.zeros_like(acc_ref)

    grad = dot_nt(low_ref[...], down_ref[0]) * slope_ref[...].astype(f32)
    low = grad.astype(b16)
    du_ref[...] = low
    dub_ref[0:1, :] = jnp.sum(low.astype(f32), 0, keepdims=True)
    acc_ref[...] += dot_nt(low, up_ref[0])

    @pl.when(step == pl.num_programs(0) - 1)
    def last():
        part_ref[...] = acc_ref[...].astype(b16)


def feed_back(core, layer, z, dy, more, gain, slope, ffn_in, ffn_out):
    rows, width = z.shape
    ffn = ffn_in.shape[2]
    tile = 256
    steps, at = hidden_tiles(ffn, tile)
    half = ffn // CORES
    return call(
        feed_back_kernel, core, steps,
        [
            all_of(z), all_of(dy), all_of(more),
            (gain, (1, 1, width), lambda g, c: (2 * layer + 1, 0, 0)),
            (slope, (rows, tile), lambda g, c: (0, g)),
            (ffn_in, (1, width, tile), lambda g, c: (layer, 0, at(g, c))),
            (ffn_out, (1, tile, width), lambda g, c: (layer, at(g, c), 0)),
        ],
        [
            full((rows, width), f32), full((width, rows), b16), full((8, width), f32),
            ((rows, half), b16, (rows, tile), lambda g, c: (0, g)),
            ((8, half), f32, (8, tile), lambda g, c: (0, g)),
            full((rows, width), b16),
        ],
        [pltpu.VMEM((rows, width), b16), pltpu.VMEM((rows, width), f32)],
        5 * 10**9, 10**7,
    )


def attend_back_kernel(
    core_ref, dz_ref, p0_ref, p1_ref, z_ref, gain_ref,
    q_ref, k_ref, v_ref, ot_ref, lse_ref, wq_ref, wk_ref, wv_ref, wo_ref,
    dz1_ref, dat_ref, small_ref, dq_ref, dk_ref, dv_ref, dqb_ref, dvb_ref, part_ref,
    low_ref, acc_ref, dk_acc, dv_acc, dqt_ref,
):
    step = pl.program_id(0)
    rows = q_ref.shape[0]
    tile = min(256, rows)

    @pl.when(step == 0)
    def first():
        grad = dz_ref[...] + (p0_ref[...].astype(f32) + p1_ref[...].astype(f32))
        unit, inverse = norm_parts(z_ref[...])
        back, gain_grad, shift_grad = norm_back(unit, inverse, gain_ref[0], grad)
        dz1_ref[...] = back
        low = back.astype(b16)
        low_ref[...] = low
        wide = low.astype(f32)
        dat_ref[...] = wide.T.astype(b16)
        small_ref[0:1, :] = gain_grad
        small_ref[1:2, :] = shift_grad
        small_ref[2:3, :] = jnp.sum(wide, 0, keepdims=True)
        acc_ref[...] = jnp.zeros_like(acc_ref)

    query = q_ref[...]
    keyed = k_ref[0]
    key = keyed[:, :LANES]
    value = v_ref[...]
    outgrad = dot_nt(low_ref[...], wo_ref[0]).astype(b16)
    outgrad_t = outgrad.astype(f32).T.astype(b16)
    query_t = query.astype(f32).T.astype(b16)
    key_t = key.astype(f32).T.astype(b16)
    first_row = (lax.broadcasted_iota(jnp.int32, (LANES, tile), 0) == 0).astype(f32).astype(b16)
    empty = jnp.zeros((HEAD_DIM, tile), b16)
    lane_head = lax.broadcasted_iota(jnp.int32, (rows, LANES), 1) // HEAD_DIM
    for head in range(2):
        here = slice(head * HEAD_DIM, (head + 1) * HEAD_DIM)
        mine = (lane_head == head).astype(f32)
        query_mine = (query.astype(f32) * mine).astype(b16)
        outgrad_mine = (outgrad.astype(f32) * mine).astype(b16)
        for start in range(0, rows, tile):
            now = slice(start, start + tile)
            piece = query_t[here, now]
            pieces = [piece, empty] if head == 0 else [empty, piece]
            scores = dot(keyed, jnp.concatenate(pieces + [first_row], 0))
            probs = jnp.exp(scores - lse_ref[head, 0:1, now])
            piece = outgrad_t[here, now]
            pieces = [piece, empty] if head == 0 else [empty, piece]
            grads = dot(value, jnp.concatenate(pieces, 0))
            delta = jnp.sum(piece.astype(f32) * ot_ref[here, now], 0, keepdims=True)
            score_grads = (probs * (grads - delta)).astype(b16)
            value_part = dot(probs.astype(b16), outgrad_mine[now])
            key_part = dot(score_grads, query_mine[now])
            if head == 0 and start == 0:
                dv_acc[...] = value_part
                dk_acc[...] = key_part
            else:
                dv_acc[...] += value_part
                dk_acc[...] += key_part
            dqt_ref[here, now] = dot(key_t[here], score_grads)
    dq = (dqt_ref[...].T * SCALE).astype(b16)
    dk = dk_acc[...].astype(b16)
    dv = dv_acc[...].astype(b16)
    dq_ref[...] = dq
    dk_ref[...] = dk
    dv_ref[...] = dv
    dqb_ref[0:1, :] = jnp.sum(dq.astype(f32), 0, keepdims=True)
    dvb_ref[0:1, :] = jnp.sum(dv.astype(f32), 0, keepdims=True)
    acc_ref[...] += dot_nt(dk, wk_ref[0]) + dot_nt(dv, wv_ref[0])
    acc_ref[:rows] += dot_nt(dq, wq_ref[0])

    @pl.when(step == pl.num_programs(0) - 1)
    def last():
        part_ref[...] = acc_ref[...].astype(b16)


def attend_back(core, layer, dz, p0, p1, z, gain, kept, attn_in, attn_out):
    q, k, v, ot, lse = (kept[name] for name in ("q", "kx", "v", "ot", "lse"))
    rows, width = z.shape
    count = v.shape[0]
    half = width // CORES
    pairs = half // LANES

    def columns(kind):
        return ((1, width, LANES), lambda g, c: (layer, 0, (kind * CORES + c) * pairs + g))

    lane_block = lambda g, c: (0, g)
    return call(
        attend_back_kernel, core, pairs,
        [
            all_of(dz), all_of(p0), all_of(p1), all_of(z),
            (gain, (1, 1, width), lambda g, c: (2 * layer, 0, 0)),
            (q, (rows, LANES), lane_block), (k, (1, count, 2 * LANES), lambda g, c: (g, 0, 0)),
            (v, (count, LANES), lane_block), (ot, (LANES, rows), lambda g, c: (g, 0)),
            (lse, (2, 8, rows), lambda g, c: (g, 0, 0)),
            (attn_in, *columns(0)), (attn_in, *columns(1)), (attn_in, *columns(2)),
            (attn_out, (1, LANES, width), lambda g, c: (layer, c * pairs + g, 0)),
        ],
        [
            full((rows, width), f32), full((width, rows), b16), full((8, width), f32),
            ((rows, half), b16, (rows, LANES), lane_block),
            ((count, half), b16, (count, LANES), lane_block),
            ((count, half), b16, (count, LANES), lane_block),
            ((8, half), f32, (8, LANES), lane_block),
            ((8, half), f32, (8, LANES), lane_block),
            full((count, width), b16),
        ],
        [
            pltpu.VMEM((rows, width), b16), pltpu.VMEM((count, width), f32),
            pltpu.VMEM((count, LANES), f32), pltpu.VMEM((count, LANES), f32),
            pltpu.VMEM((LANES, rows), f32),
        ],
        16 * 10**9, 2 * 10**7,
    )


def down_grad_kernel(core_ref, dft_ref, act_ref, out_ref):
    out = dot(dft_ref[...], act_ref[...]).astype(b16)
    out_ref[...] = out.reshape(out_ref.shape)


def down_grad(core, dft, act, lines, posts, cols):
    rows = dft.shape[1]
    hidden = act.shape[1] // CORES
    return call(
        down_grad_kernel, core, CORES * posts,
        [
            (dft, (lines * cols, rows), lambda g, c: (g % posts, 0)),
            (act, (rows, hidden), lambda g, c: (0, g // posts)),
        ],
        [(
            (CORES, lines, posts, cols, hidden), b16, (1, lines, 1, cols, hidden),
            lambda g, c: (g // posts, 0, g % posts, 0, 0),
        )],
        [],
        2 * 10**9, 10**7,
    )[0]


def up_grad_kernel(core_ref, top_ref, low_ref, own_ref, sib_ref, out_ref):
    lhs = jnp.concatenate([top_ref[...], low_ref[...]], 0)
    mine = pl.program_id(0) % 2 == 0

    @pl.when(mine)
    def own():
        out_ref[...] = dot(lhs, own_ref[...]).astype(b16).reshape(out_ref.shape)

    @pl.when(jnp.logical_not(mine))
    def sib():
        out_ref[...] = dot(lhs, sib_ref[...]).astype(b16).reshape(out_ref.shape)


def up_grad(core, hrt, du_own, du_sib, lines, posts, depth, cols):
    rows = hrt.shape[1]

    def place(g, c):
        kind = g % 2
        return ((g // 2) // lines, kind + c - 2 * kind * c, (g // 2) % lines)

    def out_at(g, c):
        block, who, line = place(g, c)
        return (0, line, 2 * block + who, 0, 0)

    return call(
        up_grad_kernel, core, lines * posts,
        [
            (hrt, (depth, rows), lambda g, c: (c, 0)),
            (hrt, (depth, rows), lambda g, c: (2 + c, 0)),
            (du_own, (rows, cols), lambda g, c: (0, g // 2)),
            (du_sib, (rows, cols), lambda g, c: (0, g // 2)),
        ],
        [(
            (CORES, lines, posts, depth, cols), b16, (CORES, 1, 1, depth, cols), out_at,
        )],
        [],
        2 * 10**9, 10**7,
    )[0]


def in_grad_kernel(
    core_ref, dq_ref, dqs_ref, dk_ref, dks_ref, dv_ref, dvs_ref, x_ref, dat_ref, or_ref, out_ref
):
    core = core_ref[0]
    half = dq_ref.shape[1]
    unit = out_ref.shape[1] // 4
    units = half // unit
    everything = x_ref[...]
    parts = ((dq_ref, dqs_ref), (dk_ref, dks_ref), (dv_ref, dvs_ref))
    for kind, pair in enumerate(parts):
        for who, ref in enumerate(pair):
            owner = core if who == 0 else 1 - core
            piece = ref[...]
            result = dot_tn(piece, everything[: piece.shape[0]]).astype(b16)
            for at in range(units):
                place = (2 * kind + owner) * units + at
                where = pl.multiple_of(place % 3 * unit, unit)
                out_ref[place // 3, pl.ds(where, unit), :] = result[at * unit : (at + 1) * unit]
    result = dot(dat_ref[...], or_ref[...]).astype(b16)
    for at in range(out_ref.shape[0]):
        out_ref[at, 3 * unit :, :] = result[at * unit : (at + 1) * unit]


def in_grad(core, dq, dqs, dk, dks, dv, dvs, x_mine, dat, or_mine, blocks):
    width = dat.shape[0]
    arrays = (dq, dqs, dk, dks, dv, dvs, x_mine, dat, or_mine)
    return call(
        in_grad_kernel, core, 1, [all_of(array) for array in arrays],
        [full((blocks, 4 * width // blocks, x_mine.shape[1]), b16)],
        [],
        5 * 10**9, 10**7,
    )[0]


def build(mesh):
    clip_size, seq_size = mesh.shape["clip"], mesh.shape["seq"]
    columns = clip_size // CORES

    def shards(
        tokens, lengths, attn_in, in_bias, attn_out, out_bias, ffn_in, ffn_in_bias,
        ffn_out, ffn_out_bias, norm_gain, norm_bias, cotangent,
    ):
        layers = attn_in.shape[0]
        geo = Geometry(mesh, tokens, ffn_in.shape[2])
        geo.locate()
        held, slots, width, ffn = geo.held, geo.slots, geo.width, geo.ffn
        half, quarter, depth = geo.half, geo.quarter, geo.depth
        posts, lines, rows = geo.posts, geo.lines, geo.rows
        aligned = geo.aligned
        core, column, post, line, parity = geo.core, geo.column, geo.post, geo.line, geo.parity
        seq_at = geo.seq
        core_arg = jnp.reshape(core, (1,)).astype(jnp.int32)

        def swap(array):
            pairs = [(at, at ^ 1) for at in range(clip_size)]
            return jax.tree.map(lambda a: lax.ppermute(a, "clip", pairs), array)

        def along_column(array, shift):
            pairs = [
                (at, ((at // CORES + shift) % columns) * CORES + at % CORES)
                for at in range(clip_size)
            ]
            return lax.ppermute(array, "clip", pairs)

        def along_line(array, shift):
            pairs = [
                (at, at // lines * lines + (at % lines + shift) % lines) for at in range(seq_size)
            ]
            return lax.ppermute(array, "seq", pairs)

        def along_post(array, shift):
            pairs = [
                (at, (at // lines + shift) % posts * lines + at % lines) for at in range(seq_size)
            ]
            return lax.ppermute(array, "seq", pairs)

        def shuffle_pairs(turn):
            pairs = []
            for col in range(columns):
                for cor in range(CORES):
                    for pos in range(posts):
                        for lin in range(lines):
                            source = (col * CORES + cor) * seq_size + pos * lines + lin
                            goal = (col * CORES + pos // held) * seq_size
                            goal += (held * cor + (pos + turn) % held) * lines + lin
                            pairs.append((source, goal))
            return pairs

        def from_rows(mine):
            got = []
            for turn in range(held):
                pairs = [(goal, source) for source, goal in shuffle_pairs(turn)]
                piece = mine[turn]
                got.append(lax.ppermute(piece, ("clip", "seq"), pairs))
            order = [jnp.stack([got[(at - turn) % held] for at in range(held)]) for turn in range(held)]
            result = order[0]
            for turn in range(1, held):
                result = jnp.where(parity == turn, order[turn], result)
            return result

        def joined(mine, other):
            pair = jnp.where(core == 0, jnp.stack([mine, other], 1), jnp.stack([other, mine], 1))
            return pair.reshape(rows, width)

        def half_of(array, which):
            blocks = array.reshape(held, CORES, slots, width)
            return lax.dynamic_index_in_dim(blocks, which, 1, False)

        lens = jnp.zeros((8, LANES), jnp.int32) + jnp.pad(lengths, (0, 8 - held))[:, None]
        gains = norm_gain.reshape(layers * 2, width)
        gain3 = gains.reshape(layers * 2, 1, width)
        out_tokens, cot_rows, kept = forward(
            geo, layers, tokens, cotangent, lens, (attn_in, attn_out, ffn_in, ffn_out),
            (in_bias, out_bias, ffn_in_bias, ffn_out_bias, gains, norm_bias.reshape(layers * 2, width)),
        )

        def quarters(array):
            split = array.reshape(array.shape[0], columns, CORES, depth)
            return jnp.where(core == 0, split[:, :, 0], split[:, :, 1]).reshape(array.shape[0], -1)

        def pick(array, at):
            return lax.dynamic_index_in_dim(array, at, 0, False)

        class Chain:
            def __init__(self, array, steps):
                self.steps = steps
                self.launch(array)

            def launch(self, array):
                (at, size, move, before), *self.steps = self.steps
                array = before(array)
                self.pieces = [pick(array, at)]
                for step in range(1, size):
                    self.pieces.append(move(pick(array, (at + step) % size), step))

            def land(self, gate=None):
                pieces = self.pieces
                if gate is not None:
                    pieces = lax.optimization_barrier(tuple(pieces) + (gate,))[:-1]
                total = pieces[0].astype(f32)
                for piece in pieces[1:]:
                    total = total + piece.astype(f32)
                return total

            def advance(self, gate=None):
                if not self.steps:
                    return
                self.launch(self.land(gate).astype(b16))

        def same(array):
            return array

        to_column = (column, columns, along_column)
        to_line = (line, lines, along_line)
        to_post = (post, posts, along_post)
        column_first = [(*to_column, same), (*to_line, same), (*to_post, same)]

        def by_line(array):
            return jnp.swapaxes(array.reshape(posts, lines, *array.shape[1:]), 0, 1)

        def by_column(array):
            return jnp.stack([array[:, at * depth : (at + 1) * depth] for at in range(columns)])

        line_first = [(*to_line, by_line), (*to_post, same), (*to_column, by_column)]

        def all_sum(array):
            total = array + swap(array)
            for size, move in ((columns, along_column), (lines, along_line), (posts, along_post)):
                moved = [move(total, step) for step in range(1, size)]
                for piece in moved:
                    total = total + piece
            return total

        def line_sum(dx):
            blocks = dx.reshape(lines, held, CORES, slots, width)
            keep = lax.dynamic_index_in_dim(blocks, core, 2, False)
            came = swap(lax.dynamic_index_in_dim(blocks, 1 - core, 2, False))
            summed = keep.astype(f32) + came.astype(f32)
            moved = [
                along_line(summed[step].astype(b16), lines - step) for step in range(1, lines)
            ]
            return summed, moved

        def spread(array):
            array = lax.psum_scatter(
                array.astype(b16), "seq", scatter_dimension=1, tiled=True
            ).astype(b16)
            return lax.psum_scatter(array, "clip", scatter_dimension=0, tiled=True).astype(f32)

        grad = cot_rows
        more = jnp.zeros((rows, width), b16)
        chains = [None] * layers
        smalls = [None] * layers
        seq_cols, seq_ffn = width // seq_size, ffn // seq_size
        for layer in range(layers - 1, -1, -1):
            fresh = layer == layers - 1
            keep = kept[layer]
            x_all, attended, low_t, active = keep["xall"], keep["o"], keep["hrt"], keep["act"]
            attended_sibling = swap(attended)
            dz2, df_t, small_two, du, du_sums, part = feed_back(
                core_arg, layer, keep["z2"], grad, more, gain3, keep["slope"], ffn_in, ffn_out
            )
            part_sibling = swap(part)
            du_sibling = swap(du)
            if aligned:
                down = down_grad(core_arg, df_t, active, lines, posts, seq_cols)
                down_chain = Chain(down, column_first)
                if not fresh:
                    for chain in chains[layer + 1]:
                        chain.advance(down)
                    up = up_grad(core_arg, low_t, du, du_sibling, lines, posts, depth, seq_ffn)
                    up_chain = Chain(up, column_first)
            dz1, da_t, small_one, dq, dk, dv, dq_sums, dv_sums, dx = attend_back(
                core_arg, layer, dz2, part, part_sibling, keep["z1"], gain3, keep, attn_in,
                attn_out,
            )
            summed, moved = line_sum(dx)
            dq_s, dk_s, dv_s = swap((dq, dk, dv))
            if aligned:
                if fresh:
                    up = up_grad(core_arg, low_t, du, after(du_sibling, dx), lines, posts, depth, seq_ffn)
                    up_chain = Chain(up, column_first)
                else:
                    for chain in chains[layer + 1]:
                        chain.advance(dx)
                down_chain.advance(dx)
                if not fresh:
                    up_chain.advance(dx)
                features = jnp.where(
                    core == 0,
                    jnp.concatenate([attended[:, :depth], attended_sibling[:, :depth]], 1),
                    jnp.concatenate([attended_sibling[:, depth:], attended[:, depth:]], 1),
                )
                into = in_grad(
                    core_arg, dq, dq_s, dk, dk_s, dv, dv_s, quarters(x_all), da_t, features,
                    seq_size,
                )
                chains[layer] = [Chain(into, line_first), up_chain, down_chain]
            else:
                into = [
                    jnp.concatenate([jnp.where(core == 0, a, b), jnp.where(core == 0, b, a)], 1)
                    for a, b in (
                        (dot_tn(x_all[:rows], dq), dot_tn(x_all[:rows], dq_s)),
                        (dot_tn(x_all, dk), dot_tn(x_all, dk_s)),
                        (dot_tn(x_all, dv), dot_tn(x_all, dv_s)),
                    )
                ]
                proj = jnp.zeros((CORES, half, width), f32)
                proj = lax.dynamic_update_slice_in_dim(proj, dot(da_t, attended).T[None], core, 0)
                up = jnp.zeros((2, CORES, width, quarter), f32)
                own_up = dot(low_t, du).reshape(width, 2, 1, quarter).transpose(1, 2, 0, 3)
                up = lax.dynamic_update_slice_in_dim(up, own_up, core, 1)
                down = jnp.zeros((2, CORES, quarter, width), f32)
                own_down = dot(df_t, active).T.reshape(2, 1, quarter, width)
                down = lax.dynamic_update_slice_in_dim(down, own_down, core, 1)
                chains[layer] = (
                    spread(jnp.concatenate(into, 1) * 0.5),
                    spread(proj.reshape(width, width)),
                    spread(up.transpose(2, 0, 1, 3).reshape(width, ffn)),
                    spread(down.reshape(ffn, width)),
                )

            total = summed[0]
            for piece in moved:
                total = total + piece.astype(f32)
            if layer > 0:
                low_total = total.astype(b16)
                more = joined(low_total, swap(low_total))
                grad = dz1
            else:
                grad_tokens = from_rows((total + half_of(dz1, core)).astype(b16))

            in_sums = jnp.zeros((2, CORES, half), f32)
            own_sums = jnp.stack([dq_sums[:1], dv_sums[:1]])
            in_sums = lax.dynamic_update_slice_in_dim(in_sums, own_sums, core, 1)
            up_sums = jnp.zeros((2, CORES, quarter), f32)
            up_sums = lax.dynamic_update_slice_in_dim(
                up_sums, du_sums[0].reshape(2, 1, quarter), core, 1
            )
            smalls[layer] = jnp.concatenate([
                in_sums.reshape(-1), up_sums.reshape(-1),
                0.5 * small_one[2], 0.5 * small_two[2],
                0.5 * small_one[0], 0.5 * small_two[0], 0.5 * small_one[1], 0.5 * small_two[1],
            ])

        summed = all_sum(jnp.stack(smalls))

        def share(start, size):
            piece = summed[:, start : start + size]
            return lax.dynamic_slice_in_dim(piece, seq_at * (size // seq_size), size // seq_size, 1)

        at = 2 * width + ffn
        if aligned:
            waiting = [chain for layer in range(layers) for chain in chains[layer]]
            while any(chain.steps for chain in waiting):
                for chain in waiting:
                    chain.advance()
            for layer in range(layers):
                into, up, down = (chain.land() for chain in chains[layer])
                into = into.T
                chains[layer] = (into[:, : 3 * seq_cols], into[:, 3 * seq_cols :], up, down.T)
        matrices = [jnp.stack([chains[layer][which] for layer in range(layers)]) for which in range(4)]
        return (
            out_tokens,
            grad_tokens,
            matrices[0],
            share(0, 2 * width),
            matrices[1],
            share(at, width),
            matrices[2],
            share(2 * width, ffn),
            matrices[3],
            share(at + width, width),
            jnp.stack([share(at + 2 * width, width), share(at + 3 * width, width)], 1),
            jnp.stack([share(at + 4 * width, width), share(at + 5 * width, width)], 1),
        )

    return shards


def solution(mesh):
    rowed = P("clip", "seq", None)
    in_specs = (rowed, P("clip")) + (P(),) * 10 + (rowed,)
    out_specs = (
        rowed,
        rowed,
        P(None, "clip", "seq"),
        P(None, "seq"),
        P(None, "clip", "seq"),
        P(None, "seq"),
        P(None, "clip", "seq"),
        P(None, "seq"),
        P(None, "clip", "seq"),
        P(None, "seq"),
        P(None, None, "seq"),
        P(None, None, "seq"),
    )
    return jax.shard_map(
        build(mesh), mesh=mesh, in_specs=in_specs, out_specs=out_specs, check_vma=False
    )
```

```python
from copy import copy as duplicate
import functools

import jax
import jax.numpy as jnp
from jax import lax
from jax.experimental import pallas as pl
from jax.experimental.pallas import tpu as pltpu
from jax.sharding import PartitionSpec as P

HEADS = 12
HEAD_DIM = 64
CORES = 2
LANES = 128
SCALE = HEAD_DIM**-0.5
SQRT_HALF = 0.5**0.5
GAUSS = 0.3989422804014327
EPS = 1e-05
VMEM = 56 * 1024 * 1024
VMEM_BACK = 62 * 1024 * 1024

f32 = jnp.float32
b16 = jnp.bfloat16


def dot(a, b):
    return lax.dot_general(a, b, (((1,), (0,)), ((), ())), preferred_element_type=f32)


def dot_nt(a, b):
    return lax.dot_general(a, b, (((1,), (1,)), ((), ())), preferred_element_type=f32)


def dot_tn(a, b):
    return lax.dot_general(a, b, (((0,), (0,)), ((), ())), preferred_element_type=f32)


def norm_parts(values):
    center = values - jnp.mean(values, -1, keepdims=True)
    inverse = lax.rsqrt(jnp.mean(center * center, -1, keepdims=True) + EPS)
    return center * inverse, inverse


def norm_back(unit, inverse, gain, grad):
    scaled = grad * gain
    mean_one = jnp.mean(scaled, -1, keepdims=True)
    mean_two = jnp.mean(scaled * unit, -1, keepdims=True)
    back = inverse * (scaled - mean_one - unit * mean_two)
    return back, jnp.sum(grad * unit, 0, keepdims=True), jnp.sum(grad, 0, keepdims=True)


def call(kernel, core, grid, ins, outs, scratch, flops, moved):
    in_specs = [pl.BlockSpec(block, lambda g, c, at=at: at(g, c[0])) for unused, block, at in ins]
    out_specs = [pl.BlockSpec(block, lambda g, c, at=at: at(g, c[0])) for s, d, block, at in outs]
    return pl.pallas_call(
        kernel,
        grid_spec=pltpu.PrefetchScalarGridSpec(
            num_scalar_prefetch=1,
            grid=(grid,),
            in_specs=in_specs,
            out_specs=out_specs,
            scratch_shapes=scratch,
        ),
        out_shape=[jax.ShapeDtypeStruct(shape, dtype) for shape, dtype, b, at in outs],
        compiler_params=pltpu.CompilerParams(
            dimension_semantics=("arbitrary",), vmem_limit_bytes=VMEM
        ),
        cost_estimate=pl.CostEstimate(flops=flops, bytes_accessed=moved, transcendentals=0),
    )(core, *[array for array, b, at in ins])


def all_of(array):
    zeros = (0,) * array.ndim
    return (array, array.shape, lambda g, c: zeros)


def full(shape, dtype):
    zeros = (0,) * len(shape)
    return (shape, dtype, shape, lambda g, c: zeros)


class Geometry:
    def __init__(self, mesh, tokens, ffn):
        self.clip_size, self.seq_size = mesh.shape["clip"], mesh.shape["seq"]
        self.columns = self.clip_size // CORES
        self.held, self.slots, self.width = tokens.shape
        self.ffn = ffn
        self.posts = self.held * CORES
        self.lines = self.seq_size // self.posts
        self.tile = CORES * self.slots
        self.rows = self.held * self.tile
        self.count = self.rows * self.lines
        self.half = self.width // CORES
        self.pairs = self.half // LANES
        self.heads = 2 * self.pairs
        self.quarter = ffn // 4
        self.depth = self.width // self.clip_size
        self.aligned = self.columns == 2 and (ffn // self.seq_size) % LANES == 0

    def locate(self):
        self.clip = lax.axis_index("clip")
        self.seq = lax.axis_index("seq")
        self.core = self.clip % CORES
        self.column = self.clip // CORES
        self.post = self.seq // self.lines
        self.line = self.seq % self.lines
        self.parity = self.post % self.held

    def sibling(self):
        return self.clip + 1 - 2 * self.core, self.seq

    def on_line(self, shift):
        return self.clip, self.post * self.lines + (self.line + shift) % self.lines

    def on_post(self, shift):
        return self.clip, (self.post + shift) % self.posts * self.lines + self.line

    def on_column(self, shift):
        return (self.column + shift) % self.columns * CORES + self.core, self.seq

    def goal(self, turn):
        post = self.held * self.core + (self.post + turn) % self.held
        return self.column * CORES + self.post // self.held, post * self.lines + self.line

    def origin(self, turn, who):
        post = self.held * who + (self.parity + turn) % self.held
        return self.column * CORES + self.post // self.held, post * self.lines + self.line

    def blocked(self, turn):
        return jnp.logical_and(self.post // self.held == self.core, turn == 0)


def remote(source, target, send, receive, device):
    return pltpu.make_async_remote_copy(
        src_ref=source, dst_ref=target, send_sem=send, recv_sem=receive,
        device_id=device, device_id_type=pl.DeviceIdType.MESH,
    )


def meet(geo, devices):
    barrier = pltpu.get_barrier_semaphore()
    total = 0
    for device in devices:
        other = jnp.logical_or(device[0] != geo.clip, device[1] != geo.seq)

        @pl.when(other)
        def greet(device=device):
            pl.semaphore_signal(
                barrier, inc=1, device_id=device, device_id_type=pl.DeviceIdType.MESH
            )

        total = total + other.astype(jnp.int32)
    pl.semaphore_wait(barrier, total)


def loop(count, body):
    def step(at, carry):
        body(at)
        return carry

    lax.fori_loop(0, count, step, 0)


def gelu_parts(inner):
    bell = jnp.exp(-0.5 * inner * inner)
    t = 1.0 / (1.0 + (0.3275911 * SQRT_HALF) * jnp.abs(inner))
    series = t * (0.5 * 0.254829592 + t * (0.5 * -0.284496736 + t * (
        0.5 * 1.421413741 + t * (0.5 * -1.453152027 + t * (0.5 * 1.061405429)))))
    tail = series * bell
    phi = jnp.where(inner >= 0.0, 1.0 - tail, tail)
    return phi, phi + inner * (GAUSS * bell)


KEPT = ("xall", "kx", "v", "q", "ot", "lse", "o", "z1", "hrt", "act", "slope", "z2")


def kept_shapes(geo):
    rows, width, half, count = geo.rows, geo.width, geo.half, geo.count
    return {
        "xall": ((count, width), b16),
        "kx": ((geo.pairs, count, 2 * LANES), b16),
        "v": ((count, half), b16),
        "q": ((rows, half), b16),
        "ot": ((half, rows), f32),
        "lse": ((geo.heads, 8, rows), f32),
        "o": ((rows, half), b16),
        "z1": ((rows, width), f32),
        "hrt": ((width, rows), b16),
        "act": ((rows, geo.ffn // CORES), b16),
        "slope": ((rows, geo.ffn // CORES), b16),
        "z2": ((rows, width), f32),
    }


def forward_kernel(geo, layers, *refs):
    refs = list(refs)

    def take(count):
        taken = refs[:count]
        del refs[:count]
        return taken

    tokens, cotangent, w_in, w_out, w_up, w_down = take(6)
    lens, in_bias, out_bias, up_bias, down_bias, gains, shifts = take(7)
    out_tokens, cot_rows = take(2)
    stored = [dict(zip(KEPT, take(len(KEPT)))) for unused in range(layers)]
    kept = [dict(zip(KEPT, take(len(KEPT)))) for unused in range(layers)]
    win, wout, wup, wdown = take(4)
    qx, vt, state, hidden, low_out, lens_there, psend, precv = take(8)
    (load_sem, save_sem, tok_sem, tok_send, tok_recv, cot_sem, cot_send, cot_recv, sib_send,
     sib_recv, line_send, line_recv, pass_send, pass_recv, part_send, part_recv, out_sem,
     out_send, out_recv, len_sem) = take(20)

    geo = duplicate(geo)
    geo.locate()
    core, tile, slots = geo.core, geo.tile, geo.slots
    held, lines, rows, width, half = geo.held, geo.lines, geo.rows, geo.width, geo.half
    quarter, pairs = geo.quarter, geo.pairs
    sibling = geo.sibling()

    loads = []
    for layer in range(layers):
        parts = [
            (w_in.at[layer, :, pl.ds(pl.multiple_of((kind * CORES + core) * half, half), half)],
             win.at[layer, kind])
            for kind in range(3)
        ]
        parts.append((w_out.at[layer, pl.ds(pl.multiple_of(core * half, half), half), :], wout.at[layer]))
        for block in range(2):
            at = pl.ds(pl.multiple_of((2 * block + core) * quarter, quarter), quarter)
            parts.append((w_up.at[layer, :, at], wup.at[layer, block]))
            parts.append((w_down.at[layer, at, :], wdown.at[layer, block]))
        loads.append([
            pltpu.make_async_copy(source, target, load_sem.at[layer, at])
            for at, (source, target) in enumerate(parts)
        ])
    for copy in loads[0]:
        copy.start()

    sources = [geo.origin(turn, who) for turn in range(held) for who in range(CORES)]
    goals = [geo.goal(turn) for turn in range(held)]
    goals = goals + [(device[0] + 1 - 2 * (device[0] % CORES), device[1]) for device in goals]
    near = [sibling] + [geo.on_line(shift) for shift in range(1, lines)]
    meet(geo, near + sources + goals)

    first = kept[0]["xall"]

    def block_at(turn, who, shift=0):
        start = shift * rows + turn * tile + who * slots
        return pl.ds(start if isinstance(start, int) else pl.multiple_of(start, slots), slots)

    def token_copies(turn, who):
        mine = tokens.at[(geo.post + turn) % held]
        place = first.at[block_at(turn, who)]
        own = pltpu.make_async_copy(mine, place, tok_sem.at[turn])
        return own, remote(mine, place, tok_send.at[turn], tok_recv.at[turn], geo.goal(turn))

    def token_start(turn):
        own, there = token_copies(turn, geo.post // held)
        pl.when(geo.blocked(turn))(own.start)
        pl.when(jnp.logical_not(geo.blocked(turn)))(there.start)

    def token_wait(turn):
        own, there = token_copies(turn, core)
        pl.when(geo.blocked(turn))(own.wait)
        pl.when(jnp.logical_not(geo.blocked(turn)))(there.wait)

    def to_sibling(array, turn, who, shift, send, receive):
        place = array.at[block_at(turn, who, shift)]
        return remote(place, place, send, receive, sibling)

    def to_line(layer, turn, shift):
        array = kept[layer]["xall"]
        source = array.at[block_at(turn, core)]
        target = array.at[block_at(turn, core, shift)]
        return remote(
            source, target, line_send.at[layer, turn, shift - 1], line_recv.at[layer, turn, shift - 1],
            geo.on_line(shift),
        )

    for turn in range(held):
        token_start(turn)
    len_copy = remote(lens, lens_there, len_sem.at[0], len_sem.at[1], sibling)
    len_copy.start()

    def clear(at):
        qx[at] = jnp.zeros(qx.shape[1:], b16)
        qx[at, LANES : LANES + 16, :] = (
            lax.broadcasted_iota(jnp.int32, (16, rows), 0) == 0
        ).astype(f32).astype(b16)

    loop(geo.heads, clear)
    len_copy.wait()
    lengths = jnp.where(geo.post // held == core, lens[...], lens_there[...])
    length = lengths[0:1, :]
    for clip in range(1, held):
        length = jnp.where(geo.parity == clip, lengths[clip : clip + 1, :], length)
    lane = lax.broadcasted_iota(jnp.int32, (slots, LANES), 1)
    slot = lax.broadcasted_iota(jnp.int32, (slots, LANES), 0)
    for shift in range(lines):
        for turn in range(held):
            for who in range(CORES):
                post = held * who + (geo.parity + turn) % held
                line = (geo.line + lines - shift) % lines
                outside = (post * lines + line) * slots + slot >= length
                mask = jnp.where(jnp.logical_and(lane == 0, outside), -1e30, 0.0).astype(b16)
                for layer in range(layers):
                    for pair in range(pairs):
                        kept[layer]["kx"][pair, block_at(turn, who, shift), LANES:] = mask

    for turn in range(held):
        token_wait(turn)
        to_sibling(first, turn, core, 0, sib_send.at[turn], sib_recv.at[turn]).start()
        for shift in range(1, lines):
            to_line(0, turn, shift).start()
    for copy in loads[0]:
        copy.wait()
    for copy in loads[1]:
        copy.start()

    def cot_copies(turn, flip):
        mine = cotangent.at[(geo.post + turn) % held]
        place = cot_rows.at[block_at(turn, geo.post // held)]
        goal = geo.goal(turn)
        if flip:
            goal = (goal[0] + 1 - 2 * (goal[0] % CORES), goal[1])
        own = pltpu.make_async_copy(mine, place, cot_sem.at[turn, flip])
        there = remote(
            mine, place, cot_send.at[turn, flip], cot_recv.at[turn, geo.post // held], goal
        )
        here = jnp.logical_and(goal[0] == geo.clip, goal[1] == geo.seq)
        return own, there, here

    def cot_start():
        for turn in range(held):
            for flip in range(CORES):
                own, there, here = cot_copies(turn, flip)
                pl.when(here)(own.start)
                pl.when(jnp.logical_not(here))(there.start)

    def cot_wait():
        for turn in range(held):
            for flip in range(CORES):
                own, there, here = cot_copies(turn, flip)
                pl.when(here)(own.wait)
                pl.when(jnp.logical_not(here))(there.wait_send)
            for who in range(CORES):
                source = geo.origin(turn, who)
                place = cot_rows.at[block_at(turn, who)]
                there = remote(
                    cotangent.at[0], place, cot_send.at[turn, 0], cot_recv.at[turn, who], source
                )
                here = jnp.logical_and(source[0] == geo.clip, source[1] == geo.seq)
                pl.when(jnp.logical_not(here))(there.wait_recv)

    def key_tile(layer, at):
        keep = kept[layer]
        now = pl.ds(pl.multiple_of(at, tile), tile)
        x = keep["xall"][now, :]
        key = dot(x, win[layer, 1]).astype(b16)
        for pair in range(pairs):
            keep["kx"][pair, now, :LANES] = key[:, pair * LANES : (pair + 1) * LANES]
        bias = in_bias[layer : layer + 1, pl.ds(pl.multiple_of(width + core * half, half), half)]
        value = (dot(x, win[layer, 2]) + bias).astype(b16)
        keep["v"][now, :] = value
        vt[:, now] = value.astype(f32).T.astype(b16)

    def query_tile(layer, at):
        keep = kept[layer]
        now = pl.ds(pl.multiple_of(at, tile), tile)
        bias = in_bias[layer : layer + 1, pl.ds(pl.multiple_of(core * half, half), half)]
        query = (dot(keep["xall"][now, :], win[layer, 0]) + bias).astype(b16)
        query = (query * SCALE).astype(b16)
        keep["q"][now, :] = query
        turned = query.astype(f32).T.astype(b16)
        for head in range(geo.heads):
            inside = head % 2 * HEAD_DIM
            qx[head, inside : inside + HEAD_DIM, now] = (
                turned[head * HEAD_DIM : (head + 1) * HEAD_DIM]
            )

    def attend_tile(layer, turn):
        keep = kept[layer]
        now = pl.ds(pl.multiple_of(turn * tile, tile), tile)

        def pair_step(pair):
            keys = keep["kx"][pair]
            for inside in range(2):
                head = 2 * pair + inside
                here = pl.ds(pl.multiple_of(head * HEAD_DIM, HEAD_DIM), HEAD_DIM)
                scores = dot(keys, qx[head, :, now])
                top = jnp.max(scores, 0, keepdims=True)
                weights = jnp.exp(scores - top)
                total = jnp.sum(weights, 0, keepdims=True)
                attended = dot(vt[here, :], weights.astype(b16)) / total
                keep["ot"][here, now] = attended
                keep["lse"][head, 0:1, now] = top + jnp.log(total)

        loop(pairs, pair_step)
        attended = keep["ot"][:, now].T.astype(b16)
        keep["o"][now, :] = attended
        share(2 * layer, turn, dot(attended, wout[layer]))

    def part_copy(which, turn):
        now = pl.ds(pl.multiple_of(turn * tile, tile), tile)
        return remote(
            psend.at[which, now, :], precv.at[which, now, :], part_send.at[which, turn],
            part_recv.at[which, turn], sibling,
        )

    def share(which, turn, part):
        now = pl.ds(pl.multiple_of(turn * tile, tile), tile)
        psend[which, now, :] = part.astype(b16)
        part_copy(which, turn).start()

    def collect(which, turn):
        now = pl.ds(pl.multiple_of(turn * tile, tile), tile)
        part_copy(which, turn).wait()
        return psend[which, now, :].astype(f32) + precv[which, now, :].astype(f32)

    def feed_tile(layer, turn):
        keep = kept[layer]
        now = pl.ds(pl.multiple_of(turn * tile, tile), tile)
        x = first[now, :].astype(f32) if layer == 0 else state[now, :]
        summed = x + collect(2 * layer, turn) + out_bias[layer : layer + 1, :]
        keep["z1"][now, :] = summed
        unit, unused = norm_parts(summed)
        normal = unit * gains[2 * layer : 2 * layer + 1, :] + shifts[2 * layer : 2 * layer + 1, :]
        hidden[now, :] = normal
        low = normal.astype(b16)
        keep["hrt"][:, now] = low.astype(f32).T.astype(b16)
        size = min(256, quarter)
        total = None
        for block in range(2):
            for start in range(0, quarter, size):
                at = block * quarter + start
                bias = up_bias[
                    layer : layer + 1,
                    pl.ds(pl.multiple_of((2 * block + core) * quarter + start, size), size),
                ]
                inner = dot(low, wup[layer, block, :, start : start + size]) + bias
                phi, slope = gelu_parts(inner)
                active = (inner * phi).astype(b16)
                keep["act"][now, at : at + size] = active
                keep["slope"][now, at : at + size] = slope.astype(b16)
            part = dot(keep["act"][now, block * quarter : (block + 1) * quarter], wdown[layer, block])
            total = part if total is None else total + part
        share(2 * layer + 1, turn, total)

    def norm_tile(layer, turn):
        keep = kept[layer]
        now = pl.ds(pl.multiple_of(turn * tile, tile), tile)
        summed = hidden[now, :] + collect(2 * layer + 1, turn) + down_bias[layer : layer + 1, :]
        keep["z2"][now, :] = summed
        unit, unused = norm_parts(summed)
        at = 2 * layer + 1
        result = unit * gains[at : at + 1, :] + shifts[at : at + 1, :]
        if layer < layers - 1:
            state[now, :] = result
            kept[layer + 1]["xall"][now, :] = result.astype(b16)
        else:
            low_out[now, :] = result.astype(b16)

    saves = []

    def save(layer, names):
        for name in names:
            copy = pltpu.make_async_copy(
                kept[layer][name], stored[layer][name], save_sem.at[layer, KEPT.index(name)]
            )
            copy.start()
            saves.append(copy)

    for layer in range(layers):
        x_all = kept[layer]["xall"]
        if layer == 0:
            for turn in range(held):
                to_sibling(x_all, turn, core, 0, sib_send.at[turn], sib_recv.at[turn]).wait_send()
                to_sibling(x_all, turn, 1 - core, 0, sib_send.at[turn], sib_recv.at[turn]).wait_recv()
                key_tile(layer, turn * tile)
                query_tile(layer, turn * tile)
        else:
            for copy in loads[layer]:
                copy.wait()

            def own_tile(turn):
                key_tile(layer, turn * tile)
                query_tile(layer, turn * tile)

            loop(held, own_tile)
        for shift in range(1, lines):
            for turn in range(held):
                to_line(layer, turn, shift).wait()
                to_sibling(
                    x_all, turn, core, shift,
                    pass_send.at[layer, turn, shift - 1], pass_recv.at[layer, turn, shift - 1],
                ).start()
        for shift in range(1, lines):
            for turn in range(held):
                send = pass_send.at[layer, turn, shift - 1]
                receive = pass_recv.at[layer, turn, shift - 1]
                to_sibling(x_all, turn, core, shift, send, receive).wait_send()
                to_sibling(x_all, turn, 1 - core, shift, send, receive).wait_recv()
                key_tile(layer, shift * rows + turn * tile)
        if layer == 0:
            cot_start()
        save(layer, ("xall", "kx", "v", "q"))
        loop(held, functools.partial(attend_tile, layer))
        save(layer, ("ot", "lse", "o"))
        loop(held, functools.partial(feed_tile, layer))
        save(layer, ("z1", "hrt", "act", "slope"))
        for turn in range(held):
            norm_tile(layer, turn)
            if layer < layers - 1:
                for shift in range(1, lines):
                    to_line(layer + 1, turn, shift).start()
        save(layer, ("z2",))

    def out_copies(turn, place):
        mine = low_out.at[block_at(turn, core)]
        own = pltpu.make_async_copy(mine, place, out_sem.at[turn])
        return own, remote(mine, place, out_send.at[turn], out_recv.at[turn], geo.origin(turn, core))

    for turn in range(held):
        own, there = out_copies(turn, out_tokens.at[geo.parity])
        pl.when(geo.blocked(turn))(own.start)
        pl.when(jnp.logical_not(geo.blocked(turn)))(there.start)
    cot_wait()
    for turn in range(held):
        own, there = out_copies(turn, out_tokens.at[(geo.post + turn) % held])
        pl.when(geo.blocked(turn))(own.wait)
        pl.when(jnp.logical_not(geo.blocked(turn)))(there.wait)
    for copy in saves:
        copy.wait()


def forward(geo, layers, tokens, cotangent, lens, weights, vectors):
    width, rows, half, ffn = geo.width, geo.rows, geo.half, geo.ffn
    shapes = kept_shapes(geo)
    any_spec = pl.BlockSpec(memory_space=pl.ANY)
    vmem_spec = pl.BlockSpec(memory_space=pltpu.VMEM)
    out_shape = [
        jax.ShapeDtypeStruct(tokens.shape, b16),
        jax.ShapeDtypeStruct((rows, width), b16),
    ]
    out_shape += [jax.ShapeDtypeStruct(*shapes[name]) for unused in range(layers) for name in KEPT]
    scratch = [pltpu.VMEM(*shapes[name]) for unused in range(layers) for name in KEPT]
    scratch += [
        pltpu.VMEM((layers, 3, width, half), b16),
        pltpu.VMEM((layers, half, width), b16),
        pltpu.VMEM((layers, 2, width, geo.quarter), b16),
        pltpu.VMEM((layers, 2, geo.quarter, width), b16),
        pltpu.VMEM((geo.heads, 2 * LANES, rows), b16),
        pltpu.VMEM((half, geo.count), b16),
        pltpu.VMEM((rows, width), f32),
        pltpu.VMEM((rows, width), f32),
        pltpu.VMEM((rows, width), b16),
        pltpu.VMEM(lens.shape, jnp.int32),
        pltpu.VMEM((2 * layers, rows, width), b16),
        pltpu.VMEM((2 * layers, rows, width), b16),
    ]
    held, lines = geo.held, max(geo.lines - 1, 1)
    dma = pltpu.SemaphoreType.DMA
    scratch += [dma(shape) for shape in (
        (layers, 8), (layers, len(KEPT)), (held,), (held,), (held,),
        (held, CORES), (held, CORES), (held, CORES), (held,), (held,),
        (layers, held, lines), (layers, held, lines), (layers, held, lines), (layers, held, lines),
        (2 * layers, held), (2 * layers, held), (held,), (held,), (held,), (2,),
    )]
    results = pl.pallas_call(
        functools.partial(forward_kernel, geo, layers),
        out_shape=out_shape,
        in_specs=[any_spec] * 6 + [vmem_spec] * 7,
        out_specs=[any_spec] * len(out_shape),
        scratch_shapes=scratch,
        compiler_params=pltpu.CompilerParams(
            collective_id=0, has_side_effects=True, vmem_limit_bytes=VMEM
        ),
        cost_estimate=pl.CostEstimate(flops=3 * 10**10, bytes_accessed=4 * 10**7, transcendentals=0),
    )(tokens, cotangent, *weights, lens, *vectors)
    count = len(KEPT)
    kept = [
        dict(zip(KEPT, results[2 + layer * count : 2 + (layer + 1) * count]))
        for layer in range(layers)
    ]
    return results[0], results[1], kept


QUERY_BIAS, VALUE_BIAS, UP_BIAS, OUT_BIAS, DOWN_BIAS, GAIN, SHIFT = 0, 1, 2, 6, 7, 8, 10
SUMS = 16
UP, DOWN = 0, 1


def backward_kernel(geo, layers, *refs):
    refs = list(refs)

    def take(count):
        taken = refs[:count]
        del refs[:count]
        return taken

    cot_rows, w_in, w_out, w_up, w_down = take(5)
    stored = [dict(zip(KEPT, take(len(KEPT)))) for unused in range(layers)]
    (gains,) = take(1)
    grad_tokens, sums = take(2)
    if geo.aligned:
        feed_out, attend_out = take(2)
    else:
        plain = [take(6) for unused in range(layers)]
    keep = dict(zip(KEPT, take(len(KEPT))))
    win, wout, wup, wdown = take(4)
    (o_there, low_grad, turned, du_there, psend, precv, do, qx, dox, dq, dk, dv, dq_there,
     dk_there, dv_there, dk_acc, dv_acc, dqt, mine_dx, dx_send, dx_recv, line_dx, line_in,
     tok_low) = take(24)
    (load_sem, o_send, o_recv, du_send, du_recv, part_send, part_recv, qkv_send, qkv_recv,
     dx_ssem, dx_rsem, line_send, line_recv, more_send, more_recv, tok_sem, tok_send,
     tok_recv, plain_sem) = take(19)
    if geo.aligned:
        (other, mine, from_x, from_y, from_z, a_mine, a_y, a_z, a_send, a_x, sum_in) = take(11)
        (fx_send, fx_recv, fy_send, fy_recv, fz_send, fz_recv, ay_send, ay_recv, az_send, az_recv,
         ax_send, ax_recv, sum_send, sum_recv) = take(14)
        (credit,) = take(1)

    geo = duplicate(geo)
    geo.locate()
    core, tile, slots = geo.core, geo.tile, geo.slots
    held, lines, rows, width, half = geo.held, geo.lines, geo.rows, geo.width, geo.half
    quarter, pairs, posts, depth = geo.quarter, geo.pairs, geo.posts, geo.depth
    post, line, column = geo.post, geo.line, geo.column
    sibling = geo.sibling()

    def tile_at(turn):
        return pl.ds(pl.multiple_of(turn * tile, tile), tile)

    def block_at(turn, who, shift=0):
        start = shift * rows + turn * tile + who * slots
        return pl.ds(start if isinstance(start, int) else pl.multiple_of(start, slots), slots)

    NAMES = KEPT + ("win", "wout", "wup", "wdown", "cot")

    def load_copies(layer, name):
        where = load_sem.at[layer, NAMES.index(name)]
        if name == "win":
            return [
                pltpu.make_async_copy(
                    w_in.at[layer, :, pl.ds(pl.multiple_of((kind * CORES + core) * half, half), half)],
                    win.at[kind], load_sem.at[layer, len(NAMES) + kind],
                )
                for kind in range(3)
            ]
        if name == "wout":
            at = pl.ds(pl.multiple_of(core * half, half), half)
            return [pltpu.make_async_copy(w_out.at[layer, at, :], wout, where)]
        if name in ("wup", "wdown"):
            copies = []
            for block in range(2):
                at = pl.ds(pl.multiple_of((2 * block + core) * quarter, quarter), quarter)
                slot = len(NAMES) + 3 + 2 * (name == "wdown") + block
                if name == "wup":
                    pair = w_up.at[layer, :, at], wup.at[block]
                else:
                    pair = w_down.at[layer, at, :], wdown.at[block]
                copies.append(pltpu.make_async_copy(*pair, load_sem.at[layer, slot]))
            return copies
        if name == "cot":
            return [pltpu.make_async_copy(cot_rows, low_grad, where)]
        return [pltpu.make_async_copy(stored[layer][name], keep[name], where)]

    def load(layer, *names):
        for name in names:
            for copy in load_copies(layer, name):
                copy.start()

    def loaded(layer, *names):
        for name in names:
            for copy in load_copies(layer, name):
                copy.wait()

    top = layers - 1
    load(top, "z2", "cot", "wdown", "slope", "wup", "act", "z1", "wout", "q", "kx", "v", "ot",
         "lse", "win", "hrt", "xall", "o")

    sources = [geo.origin(turn, who) for turn in range(held) for who in range(CORES)]
    goals = [geo.goal(turn) for turn in range(held)]
    near = [sibling] + [geo.on_line(shift) for shift in range(1, lines)]
    if geo.aligned:
        near += [geo.on_post(shift) for shift in range(1, posts)]
        near += [geo.on_column(shift) for shift in range(1, geo.columns)]
    goals = goals + [(device[0] + 1 - 2 * (device[0] % CORES), device[1]) for device in goals]
    meet(geo, near + sources + goals)

    def o_copy(layer):
        return remote(stored[layer]["o"], o_there.at[layer], o_send.at[layer], o_recv.at[layer], sibling)

    for layer in range(layers):
        o_copy(layer).start()

    def clear(at):
        qx[at] = jnp.zeros(qx.shape[1:], b16)
        qx[at, LANES : LANES + 16, :] = (
            lax.broadcasted_iota(jnp.int32, (16, rows), 0) == 0
        ).astype(f32).astype(b16)
        dox[at] = jnp.zeros(dox.shape[1:], b16)

    loop(2, clear)
    sums[...] = jnp.zeros_like(sums)

    def add_sum(layer, row, lanes, value):
        sums[layer, pl.ds(row, 1), lanes] += value

    everywhere = slice(None)


    def x_copy(layer, kind, z):
        return remote(
            other.at[kind, z], from_x.at[kind, z], fx_send.at[layer, kind, z],
            fx_recv.at[layer, kind, z], geo.on_column(1),
        )

    def y_copy(layer, kind, z, shift):
        return remote(
            mine.at[layer, kind, z, (line + shift) % lines], from_y.at[layer, kind, z, shift - 1],
            fy_send.at[layer, kind, z, shift - 1], fy_recv.at[layer, kind, z, shift - 1],
            geo.on_line(shift),
        )

    def z_copy(layer, kind, shift):
        return remote(
            mine.at[layer, kind, (post + shift) % posts, line], from_z.at[layer, kind, shift - 1],
            fz_send.at[layer, kind, shift - 1], fz_recv.at[layer, kind, shift - 1],
            geo.on_post(shift),
        )

    def land_x(layer, kind):
        def chunk(z):
            x_copy(layer, kind, z).wait()
            total = mine[layer, kind, z].astype(f32) + from_x[kind, z].astype(f32)
            mine[layer, kind, z] = total.astype(b16)
            for shift in range(1, lines):
                y_copy(layer, kind, z, shift).start()

        loop(posts, chunk)
        if layer > 0:
            device = geo.on_column(1)
            pl.semaphore_signal(
                credit.at[kind], inc=1, device_id=device, device_id_type=pl.DeviceIdType.MESH
            )

    def land_y(layer, kind):
        for step in range(posts):
            z = (post + step + 1) % posts
            total = mine[layer, kind, z, line].astype(f32)
            for shift in range(1, lines):
                y_copy(layer, kind, z, shift).wait()
                total = total + from_y[layer, kind, z, shift - 1].astype(f32)
            mine[layer, kind, z, line] = total.astype(b16)
            if step + 1 < posts:
                z_copy(layer, kind, step + 1).start()

    def land_z(layer, kind):
        total = mine[layer, kind, post, line].astype(f32)
        for shift in range(1, posts):
            z_copy(layer, kind, shift).wait()
            total = total + from_z[layer, kind, shift - 1].astype(f32)
        feed_out[layer, kind] = total

    def ay_copy(layer, z, shift):
        return remote(
            a_mine.at[(line + shift) % lines, z], a_y.at[layer, z, shift - 1],
            ay_send.at[layer, z, shift - 1], ay_recv.at[layer, z, shift - 1], geo.on_line(shift),
        )

    def az_copy(layer, shift):
        return remote(
            a_mine.at[line, (post + shift) % posts], a_z.at[layer, shift - 1],
            az_send.at[layer, shift - 1], az_recv.at[layer, shift - 1], geo.on_post(shift),
        )

    def ax_copy(layer):
        return remote(
            a_send.at[layer], a_x.at[layer], ax_send.at[layer], ax_recv.at[layer], geo.on_column(1)
        )

    def land_ay(layer):
        for step in range(posts):
            z = (post + step + 1) % posts
            total = a_mine[line, z].astype(f32)
            for shift in range(1, lines):
                ay_copy(layer, z, shift).wait()
                total = total + a_y[layer, z, shift - 1].astype(f32)
            a_mine[line, z] = total.astype(b16)
            if step + 1 < posts:
                az_copy(layer, step + 1).start()

    def land_az(layer):
        total = a_mine[line, post].astype(f32)
        for shift in range(1, posts):
            az_copy(layer, shift).wait()
            total = total + a_z[layer, shift - 1].astype(f32)
        low, high = total[:, :depth], total[:, depth:]
        attend_out[layer] = jnp.where(column == 0, low, high)
        a_send[layer] = jnp.where(column == 0, high, low).astype(b16)
        ax_copy(layer).start()

    def land_ax(layer):
        ax_copy(layer).wait()
        attend_out[layer] = attend_out[layer] + a_x[layer].astype(f32)


    def part_copy(layer, turn):
        return remote(
            psend.at[tile_at(turn), :], precv.at[tile_at(turn), :], part_send.at[layer, turn],
            part_recv.at[layer, turn], sibling,
        )

    def du_copy(layer, turn):
        return remote(
            keep["slope"].at[tile_at(turn), :], du_there.at[tile_at(turn), :],
            du_send.at[layer, turn], du_recv.at[layer, turn], sibling,
        )

    def norm_grads(layer, which, values, grad):
        at = 2 * layer + which
        unit, inverse = norm_parts(values)
        back, gain_grad, shift_grad = norm_back(unit, inverse, gains[at : at + 1, :], grad)
        add_sum(layer, GAIN + which, everywhere, gain_grad)
        add_sum(layer, SHIFT + which, everywhere, shift_grad)
        return back

    def feed_back_tile(layer, turn):
        now = tile_at(turn)
        grad = low_grad[now, :].astype(f32)
        if layer < top:
            grad = grad + keep["z1"][now, :]
        back = norm_grads(layer, 1, keep["z2"][now, :], grad)
        keep["z2"][now, :] = back
        low = back.astype(b16)
        wide = low.astype(f32)
        turned[:, now] = wide.T.astype(b16)
        add_sum(layer, DOWN_BIAS, everywhere, jnp.sum(wide, 0, keepdims=True))
        size = min(256, quarter)
        total = None
        for block in range(2):
            for start in range(0, quarter, size):
                lanes = slice(block * quarter + start, block * quarter + start + size)
                grads = dot_nt(low, wdown[block, start : start + size, :])
                grads = (grads * keep["slope"][now, lanes].astype(f32)).astype(b16)
                keep["slope"][now, lanes] = grads
                add_sum(
                    layer, UP_BIAS + 2 * block + core, slice(start, start + size),
                    jnp.sum(grads.astype(f32), 0, keepdims=True),
                )
            lanes = slice(block * quarter, (block + 1) * quarter)
            part = dot_nt(keep["slope"][now, lanes], wup[block])
            total = part if total is None else total + part
        psend[now, :] = total.astype(b16)
        part_copy(layer, turn).start()
        du_copy(layer, turn).start()

    def down_grads(layer, which, start):
        lanes = pl.ds(pl.multiple_of(which * quarter, quarter), quarter)
        cols = width // geo.seq_size

        def chunk(z):
            at = pl.ds(pl.multiple_of(z * lines * cols, lines * cols), lines * cols)
            result = dot(turned[at, :], keep["act"][:, lanes]).astype(b16)
            for row in range(lines):
                for piece in range(2):
                    block = result[
                        row * cols : (row + 1) * cols,
                        piece * quarter // 2 : (piece + 1) * quarter // 2,
                    ]
                    span = slice(piece * cols, (piece + 1) * cols)
                    if start:
                        other[DOWN, z, row, span, :] = block
                    else:
                        mine[layer, DOWN, z, row, span, :] = block
            if start:
                x_copy(layer, DOWN, z).start()

        loop(posts, chunk)

    def up_grads(layer, which, start):
        at = pl.ds(pl.multiple_of((which * CORES + core) * depth, depth), depth)
        left = keep["hrt"][at, :]
        size = quarter // lines
        for block in range(2):
            lanes = slice(block * quarter, (block + 1) * quarter)
            for there, array in ((0, keep["slope"]), (1, du_there)):
                z = 2 * block + core + there * (1 - 2 * core)
                result = dot(left, array[:, lanes]).astype(b16)
                for row in range(lines):
                    piece = result[:, row * size : (row + 1) * size]
                    if start:
                        other[UP, z, row] = piece
                    else:
                        mine[layer, UP, z, row] = piece
                if start:
                    x_copy(layer, UP, z).start()

    def feed_grads(layer, kind):
        make = down_grads if kind == DOWN else up_grads
        if layer < top:
            pl.semaphore_wait(credit.at[kind], 1)
        make(layer, 1 - column, True)
        make(layer, column, False)

    def proj_back_tile(layer, turn):
        now = tile_at(turn)
        part_copy(layer, turn).wait()
        grad = keep["z2"][now, :] + (psend[now, :].astype(f32) + precv[now, :].astype(f32))
        back = norm_grads(layer, 0, keep["z1"][now, :], grad)
        keep["z1"][now, :] = back
        low = back.astype(b16)
        wide = low.astype(f32)
        turned[:, now] = wide.T.astype(b16)
        add_sum(layer, OUT_BIAS, everywhere, jnp.sum(wide, 0, keepdims=True))
        do[now, :] = dot_nt(low, wout[...]).astype(b16)

    lane_head = lax.broadcasted_iota(jnp.int32, (tile, LANES), 1) // HEAD_DIM

    def attend_back_pair(layer, pair):
        lanes = pl.ds(pl.multiple_of(pair * LANES, LANES), LANES)
        keys = keep["kx"][pair]
        key_t = keys[:, :LANES].astype(f32).T.astype(b16)
        value = keep["v"][:, lanes]
        query_t = keep["q"][:, lanes].astype(f32).T.astype(b16)
        grad_t = do[:, lanes].astype(f32).T.astype(b16)
        for head in range(2):
            here = slice(head * HEAD_DIM, (head + 1) * HEAD_DIM)
            qx[head, here, :] = query_t[here]
            dox[head, here, :] = grad_t[here]
        dk_acc[...] = jnp.zeros_like(dk_acc)
        dv_acc[...] = jnp.zeros_like(dv_acc)

        def turn_step(turn):
            now = tile_at(turn)
            query = keep["q"][now, lanes].astype(f32)
            outgrad = do[now, lanes].astype(f32)
            for head in range(2):
                here = slice(head * HEAD_DIM, (head + 1) * HEAD_DIM)
                chosen = (lane_head == head).astype(f32)
                scores = dot(keys, qx[head, :, now])
                probs = jnp.exp(scores - keep["lse"][2 * pair + head, 0:1, now])
                grads = dot(value, dox[head, :, now])
                own = pl.ds(pl.multiple_of(pair * LANES + head * HEAD_DIM, HEAD_DIM), HEAD_DIM)
                delta = jnp.sum(
                    dox[head, here, now].astype(f32) * keep["ot"][own, now], 0, keepdims=True
                )
                score_grads = (probs * (grads - delta)).astype(b16)
                dv_acc[...] += dot(probs.astype(b16), (outgrad * chosen).astype(b16))
                dk_acc[...] += dot(score_grads, (query * chosen).astype(b16))
                dqt[here, now] = dot(key_t[here], score_grads)

        loop(held, turn_step)
        query_grad = (dqt[...].T * SCALE).astype(b16)
        value_grad = dv_acc[...].astype(b16)
        dq[:, lanes] = query_grad
        dk[:, lanes] = dk_acc[...].astype(b16)
        dv[:, lanes] = value_grad
        spot = pl.ds(pl.multiple_of(core * half + pair * LANES, LANES), LANES)
        add_sum(layer, QUERY_BIAS, spot, jnp.sum(query_grad.astype(f32), 0, keepdims=True))
        add_sum(layer, VALUE_BIAS, spot, jnp.sum(value_grad.astype(f32), 0, keepdims=True))

    def qkv_copies(layer):
        return [
            remote(source, target, qkv_send.at[layer, at], qkv_recv.at[layer, at], sibling)
            for at, (source, target) in enumerate(((dq, dq_there), (dk, dk_there), (dv, dv_there)))
        ]

    def dx_copy(layer, shift, turn):
        return remote(
            dx_send.at[shift * held + turn], dx_recv.at[shift * held + turn],
            dx_ssem.at[layer, shift * held + turn], dx_rsem.at[layer, shift * held + turn], sibling,
        )

    def dx_tile(layer, shift, turn):
        now = pl.ds(pl.multiple_of(shift * rows + turn * tile, tile), tile)
        total = dot_nt(dk[now, :], win[1]) + dot_nt(dv[now, :], win[2])
        if shift == 0:
            total = total + dot_nt(dq[now, :], win[0])
        first, second = total[:slots], total[slots:]
        mine_dx[shift * held + turn] = jnp.where(core == 0, first, second)
        dx_send[shift * held + turn] = jnp.where(core == 0, second, first).astype(b16)
        dx_copy(layer, shift, turn).start()

    def line_copy(layer, shift, turn):
        return remote(
            line_dx.at[shift - 1, turn], line_in.at[layer, shift - 1, turn],
            line_send.at[layer, shift - 1, turn], line_recv.at[layer, shift - 1, turn],
            geo.on_line(lines - shift),
        )

    def more_copy(layer, turn, who):
        place = low_grad.at[block_at(turn, who)]
        return remote(place, place, more_send.at[layer, turn], more_recv.at[layer, turn], sibling)

    def token_copies(turn, place):
        own = pltpu.make_async_copy(tok_low.at[turn], place, tok_sem.at[turn])
        there = remote(
            tok_low.at[turn], place, tok_send.at[turn], tok_recv.at[turn], geo.origin(turn, core)
        )
        return own, there

    def mine_lanes(x):
        cuts = [x[:, at * depth : (at + 1) * depth] for at in range(2 * CORES)]
        return jnp.where(
            core == 0, jnp.concatenate([cuts[0], cuts[2]], 1), jnp.concatenate([cuts[1], cuts[3]], 1)
        )

    def attend_grads(layer):
        unit = width // geo.seq_size
        units = half // unit
        x = mine_lanes(keep["xall"][...])
        for kind, pair in enumerate(((dq, dq_there), (dk, dk_there), (dv, dv_there))):
            for there, ref in enumerate(pair):
                owner = core + there * (1 - 2 * core)
                count = ref.shape[0]
                result = dot_tn(ref[...], x[:count]).astype(b16)
                for at in range(units):
                    index = (2 * kind + owner) * units + at
                    seq = index // 3
                    where = pl.ds(pl.multiple_of(index % 3 * unit, unit), unit)
                    a_mine[seq % lines, seq // lines, where, :] = result[at * unit : (at + 1) * unit]
        here, there = keep["o"][...], o_there[layer]
        features = jnp.where(
            core == 0,
            jnp.concatenate([here[:, :depth], there[:, :depth]], 1),
            jnp.concatenate([there[:, depth:], here[:, depth:]], 1),
        )
        result = dot(turned[...], features).astype(b16)
        for seq in range(geo.seq_size):
            a_mine[seq % lines, seq // lines, 3 * unit :, :] = result[seq * unit : (seq + 1) * unit]
        for z in range(posts):
            for shift in range(1, lines):
                ay_copy(layer, z, shift).start()

    def plain_out(layer, names):
        sources = {"du": keep["slope"], "dft": turned, "dat": turned, "dq": dq, "dk": dk, "dv": dv}
        order = ("du", "dft", "dat", "dq", "dk", "dv")
        copies = [
            pltpu.make_async_copy(sources[name], plain[layer][order.index(name)], plain_sem.at[order.index(name)])
            for name in names
        ]
        for copy in copies:
            copy.start()
        for copy in copies:
            copy.wait()

    for layer in range(layers - 1, -1, -1):
        last = layer == 0
        below = layer - 1
        if layer == top:
            loaded(layer, "cot")
        else:
            for turn in range(held):
                more_copy(layer + 1, turn, core).wait_send()
                more_copy(layer + 1, turn, 1 - core).wait_recv()
        loaded(layer, "z2", "wdown", "slope", "wup")
        loop(held, functools.partial(feed_back_tile, layer))
        if not last:
            load(below, "wdown", "wup")
        else:
            load(layer, "z1")
        loaded(layer, "act")
        if geo.aligned:
            if layer < top:
                land_x(layer + 1, UP)
                land_y(layer + 1, DOWN)
            feed_grads(layer, DOWN)
            if last:
                loaded(layer, "hrt")
                for turn in range(held):
                    du_copy(layer, turn).wait()
                feed_grads(layer, UP)
                land_ay(layer + 1)
        else:
            plain_out(layer, ("dft",))
        if not last:
            load(below, "act")
        loaded(layer, "z1", "wout")
        loop(held, functools.partial(proj_back_tile, layer))
        if not last:
            load(below, "wout", "z2")
        loaded(layer, "q", "kx", "v", "ot", "lse")
        loop(pairs, functools.partial(attend_back_pair, layer))
        if not last:
            load(below, "q", "kx", "v", "ot", "lse")
        for copy in qkv_copies(layer):
            copy.start()
        loaded(layer, "win")
        for shift in range(1, lines):
            loop(held, functools.partial(dx_tile, layer, shift))
        if geo.aligned and layer < top:
            land_y(layer + 1, UP)
            land_z(layer + 1, DOWN)
        for shift in range(1, lines):
            for turn in range(held):
                dx_copy(layer, shift, turn).wait()
                at = shift * held + turn
                line_dx[shift - 1, turn] = (mine_dx[at] + dx_recv[at].astype(f32)).astype(b16)
                line_copy(layer, shift, turn).start()
        loop(held, functools.partial(dx_tile, layer, 0))
        if not last:
            load(below, "win")
        if geo.aligned:
            if not last:
                loaded(layer, "hrt")
                for turn in range(held):
                    du_copy(layer, turn).wait()
                feed_grads(layer, UP)
            for copy in qkv_copies(layer):
                copy.wait()
            loaded(layer, "xall", "o")
            o_copy(layer).wait()
            if layer < top:
                land_az(layer + 1)
            attend_grads(layer)
            land_x(layer, DOWN)
        else:
            for turn in range(held):
                du_copy(layer, turn).wait()
            for copy in qkv_copies(layer):
                copy.wait()
            loaded(layer, "hrt", "xall", "o")
            o_copy(layer).wait()
            plain_out(layer, ("du", "dat", "dq", "dk", "dv"))
        if not last:
            load(below, "hrt", "slope", "xall", "o")
        for turn in range(held):
            dx_copy(layer, 0, turn).wait()
            total = mine_dx[turn] + dx_recv[turn].astype(f32)
            for shift in range(1, lines):
                line_copy(layer, shift, turn).wait()
                total = total + line_in[layer, shift - 1, turn].astype(f32)
            if not last:
                low_grad[block_at(turn, core), :] = total.astype(b16)
                more_copy(layer, turn, core).start()
            else:
                total = total + keep["z1"][block_at(turn, core), :]
                tok_low[turn] = total.astype(b16)
                own, there = token_copies(turn, grad_tokens.at[geo.parity])
                pl.when(geo.blocked(turn))(own.start)
                pl.when(jnp.logical_not(geo.blocked(turn)))(there.start)

    if geo.aligned:
        def sum_copy(hop, device):
            return remote(sums, sum_in.at[hop], sum_send.at[hop], sum_recv.at[hop], device)

        def sum_hop(first, devices):
            copies = [sum_copy(first + at, device) for at, device in enumerate(devices)]
            for copy in copies:
                copy.start()
            return copies

        def sum_land(first, copies):
            total = sums[...]
            for at, copy in enumerate(copies):
                copy.wait()
                total = total + sum_in[first + at]
            sums[...] = total

        halves = lax.broadcasted_iota(jnp.int32, sums.shape, 1) >= OUT_BIAS
        sums[...] = jnp.where(halves, 0.5 * sums[...], sums[...])
        moved = sum_hop(0, [sibling])
        land_z(1, UP)
        sum_land(0, moved)
        moved = sum_hop(1, [geo.on_column(1)])
        land_ax(1)
        land_y(0, DOWN)
        sum_land(1, moved)
        moved = sum_hop(2, [geo.on_line(shift) for shift in range(1, lines)])
        land_x(0, UP)
        sum_land(2, moved)
        moved = sum_hop(1 + lines, [geo.on_post(shift) for shift in range(1, posts)])
        land_ay(0)
        land_z(0, DOWN)
        sum_land(1 + lines, moved)
        land_y(0, UP)
        land_az(0)
        land_z(0, UP)
        land_ax(0)
    for turn in range(held):
        own, there = token_copies(turn, grad_tokens.at[(post + turn) % held])
        pl.when(geo.blocked(turn))(own.wait)
        pl.when(jnp.logical_not(geo.blocked(turn)))(there.wait)


def backward(geo, layers, cot_rows, weights, kept, gains):
    width, rows, half, ffn, count = geo.width, geo.rows, geo.half, geo.ffn, geo.count
    held, lines, posts, slots, quarter = geo.held, geo.lines, geo.posts, geo.slots, geo.quarter
    shapes = kept_shapes(geo)
    any_spec = pl.BlockSpec(memory_space=pl.ANY)
    vmem_spec = pl.BlockSpec(memory_space=pltpu.VMEM)
    unit = width // geo.seq_size
    out = [((held, slots, width), b16), ((layers, SUMS, width), f32)]
    out_specs = [any_spec, vmem_spec]
    if geo.aligned:
        out += [
            ((layers, 2, geo.depth, quarter // lines), f32),
            ((layers, 4 * unit, geo.depth), f32),
        ]
        out_specs += [vmem_spec] * 2
    else:
        for unused in range(layers):
            out += [
                ((rows, ffn // CORES), b16), ((width, rows), b16), ((width, rows), b16),
                ((rows, half), b16), ((count, half), b16), ((count, half), b16),
            ]
            out_specs += [any_spec] * 6
    vmem = pltpu.VMEM
    scratch = [vmem(*shapes[name]) for name in KEPT]
    scratch += [
        vmem((3, width, half), b16), vmem((half, width), b16),
        vmem((2, width, quarter), b16), vmem((2, quarter, width), b16),
        vmem((layers, rows, half), b16),
        vmem((rows, width), b16),
        vmem((width, rows), b16),
        vmem((rows, ffn // CORES), b16),
        vmem((rows, width), b16), vmem((rows, width), b16),
        vmem((rows, half), b16),
        vmem((2, 2 * LANES, rows), b16), vmem((2, LANES, rows), b16),
        vmem((rows, half), b16), vmem((count, half), b16), vmem((count, half), b16),
        vmem((rows, half), b16), vmem((count, half), b16), vmem((count, half), b16),
        vmem((count, LANES), f32), vmem((count, LANES), f32), vmem((LANES, rows), f32),
        vmem((lines * held, slots, width), f32),
        vmem((lines * held, slots, width), b16), vmem((lines * held, slots, width), b16),
        vmem((lines - 1, held, slots, width), b16),
        vmem((layers, lines - 1, held, slots, width), b16),
        vmem((held, slots, width), b16),
    ]
    dma = pltpu.SemaphoreType.DMA
    scratch += [dma(shape) for shape in (
        (layers, len(KEPT) + 12), (layers,), (layers,), (layers, held), (layers, held),
        (layers, held), (layers, held), (layers, 3), (layers, 3),
        (layers, lines * held), (layers, lines * held),
        (layers, lines - 1, held), (layers, lines - 1, held),
        (layers, held), (layers, held), (held,), (held,), (held,), (6,),
    )]
    if geo.aligned:
        block = (geo.depth, quarter // lines)
        cell = (4 * unit, 2 * geo.depth)
        hops = 1 + 1 + (lines - 1) + (posts - 1)
        scratch += [
            vmem((2, posts, lines, *block), b16), vmem((layers, 2, posts, lines, *block), b16),
            vmem((2, posts, lines, *block), b16),
            vmem((layers, 2, posts, lines - 1, *block), b16),
            vmem((layers, 2, posts - 1, *block), b16),
            vmem((lines, posts, *cell), b16),
            vmem((layers, posts, lines - 1, *cell), b16),
            vmem((layers, posts - 1, *cell), b16),
            vmem((layers, 4 * unit, geo.depth), b16), vmem((layers, 4 * unit, geo.depth), b16),
            vmem((hops, layers, SUMS, width), f32),
        ]
        scratch += [dma(shape) for shape in (
            (layers, 2, posts), (layers, 2, posts),
            (layers, 2, posts, lines - 1), (layers, 2, posts, lines - 1),
            (layers, 2, posts - 1), (layers, 2, posts - 1),
            (layers, posts, lines - 1), (layers, posts, lines - 1),
            (layers, posts - 1), (layers, posts - 1), (layers,), (layers,), (hops,), (hops,),
        )]
        scratch += [pltpu.SemaphoreType.REGULAR((2,))]
    stored = [kept[layer][name] for layer in range(layers) for name in KEPT]
    return pl.pallas_call(
        functools.partial(backward_kernel, geo, layers),
        out_shape=[jax.ShapeDtypeStruct(*shape) for shape in out],
        in_specs=[any_spec] * (5 + len(stored)) + [vmem_spec],
        out_specs=out_specs,
        scratch_shapes=scratch,
        compiler_params=pltpu.CompilerParams(
            collective_id=1, has_side_effects=True, vmem_limit_bytes=VMEM_BACK
        ),
        cost_estimate=pl.CostEstimate(flops=8 * 10**10, bytes_accessed=6 * 10**7, transcendentals=0),
    )(cot_rows, *weights, *stored, gains)


def finish_kernel(
    geo, core_ref, sums_ref, feed_ref, attend_ref,
    into_ref, in_bias_ref, proj_ref, out_bias_ref, up_ref, up_bias_ref, down_ref, down_bias_ref,
    gain_ref, shift_ref,
):
    seq = core_ref[0]
    layers = feed_ref.shape[0]
    unit = geo.width // geo.seq_size
    wide, span = 2 * unit, geo.ffn // geo.seq_size
    per_row, per_quarter = geo.width // wide, geo.quarter // span

    def turn(rows, amount):
        return pltpu.roll(rows, (geo.width - amount) % geo.width, 1)

    for layer in range(layers):
        up_ref[layer] = feed_ref[layer, UP]
        down = feed_ref[layer, DOWN]
        down_ref[layer] = jnp.concatenate([down[:unit], down[unit:]], 1).T
        both = attend_ref[layer].T
        into_ref[layer] = both[:, : 3 * unit]
        proj_ref[layer] = both[:, 3 * unit :]
        sums = sums_ref[layer]
        narrow = turn(sums, seq * unit)
        out_bias_ref[layer : layer + 1, :] = narrow[OUT_BIAS : OUT_BIAS + 1, :unit]
        down_bias_ref[layer : layer + 1, :] = narrow[DOWN_BIAS : DOWN_BIAS + 1, :unit]
        gain_ref[layer] = narrow[GAIN : GAIN + 2, :unit]
        shift_ref[layer] = narrow[SHIFT : SHIFT + 2, :unit]
        middle = turn(sums, seq % per_row * wide)
        first = middle[QUERY_BIAS : QUERY_BIAS + 1, :wide]
        second = middle[VALUE_BIAS : VALUE_BIAS + 1, :wide]
        in_bias_ref[layer : layer + 1, :] = jnp.where(seq < per_row, first, second)
        large = turn(sums, seq % per_quarter * span)
        chosen = large[UP_BIAS : UP_BIAS + 1, :span]
        for block in range(1, 4):
            chosen = jnp.where(
                seq // per_quarter == block, large[UP_BIAS + block : UP_BIAS + block + 1, :span], chosen
            )
        up_bias_ref[layer : layer + 1, :] = chosen


def finish(geo, layers, seq, sums, feed_out, attend_out):
    unit, width = geo.width // geo.seq_size, geo.width
    span = geo.ffn // geo.seq_size
    depth = geo.depth
    shapes = [
        (layers, depth, 3 * unit), (layers, 2 * unit), (layers, depth, unit), (layers, unit),
        (layers, depth, span), (layers, span), (layers, geo.ffn // geo.clip_size, unit),
        (layers, unit), (layers, 2, unit), (layers, 2, unit),
    ]
    return call(
        functools.partial(finish_kernel, geo), seq, 1,
        [all_of(sums), all_of(feed_out), all_of(attend_out)],
        [full(shape, f32) for shape in shapes], [], 10**7, 10**7,
    )


def build(mesh):
    clip_size, seq_size = mesh.shape["clip"], mesh.shape["seq"]

    def shards(
        tokens, lengths, attn_in, in_bias, attn_out, out_bias, ffn_in, ffn_in_bias,
        ffn_out, ffn_out_bias, norm_gain, norm_bias, cotangent,
    ):
        layers = attn_in.shape[0]
        geo = Geometry(mesh, tokens, ffn_in.shape[2])
        geo.locate()
        held, width, ffn, half, quarter = geo.held, geo.width, geo.ffn, geo.half, geo.quarter
        aligned, core = geo.aligned, geo.core
        seq_at = geo.seq

        lens = jnp.zeros((8, LANES), jnp.int32) + jnp.pad(lengths, (0, 8 - held))[:, None]
        gains = norm_gain.reshape(layers * 2, width)
        weights = (attn_in, attn_out, ffn_in, ffn_out)
        out_tokens, cot_rows, kept = forward(
            geo, layers, tokens, cotangent, lens, weights,
            (in_bias, out_bias, ffn_in_bias, ffn_out_bias, gains, norm_bias.reshape(layers * 2, width)),
        )
        grad_tokens, sums, *results = backward(geo, layers, cot_rows, weights, kept, gains)
        if aligned:
            seq_arg = jnp.reshape(seq_at, (1,)).astype(jnp.int32)
            return (out_tokens, grad_tokens, *finish(geo, layers, seq_arg, sums, *results))

        def swap(array):
            pairs = [(at, at ^ 1) for at in range(clip_size)]
            return lax.ppermute(array, "clip", pairs)

        def spread(array):
            array = lax.psum_scatter(
                array.astype(b16), "seq", scatter_dimension=1, tiled=True
            ).astype(b16)
            return lax.psum_scatter(array, "clip", scatter_dimension=0, tiled=True).astype(f32)

        matrices = []
        for layer in range(layers):
            du, df_t, da_t, dq, dk, dv = results[6 * layer : 6 * layer + 6]
            keep = kept[layer]
            x_all = keep["xall"]
            into = [
                jnp.concatenate([jnp.where(core == 0, a, b), jnp.where(core == 0, b, a)], 1)
                for a, b in (
                    (dot_tn(x_all[: array.shape[0]], array), dot_tn(x_all[: array.shape[0]], swap(array)))
                    for array in (dq, dk, dv)
                )
            ]
            proj = jnp.zeros((CORES, half, width), f32)
            proj = lax.dynamic_update_slice_in_dim(proj, dot(da_t, keep["o"]).T[None], core, 0)
            up = jnp.zeros((2, CORES, width, quarter), f32)
            own_up = dot(keep["hrt"], du).reshape(width, 2, 1, quarter).transpose(1, 2, 0, 3)
            up = lax.dynamic_update_slice_in_dim(up, own_up, core, 1)
            down = jnp.zeros((2, CORES, quarter, width), f32)
            own_down = dot(df_t, keep["act"]).T.reshape(2, 1, quarter, width)
            down = lax.dynamic_update_slice_in_dim(down, own_down, core, 1)
            matrices.append((
                spread(jnp.concatenate(into, 1) * 0.5),
                spread(proj.reshape(width, width)),
                spread(up.transpose(2, 0, 1, 3).reshape(width, ffn)),
                spread(down.reshape(ffn, width)),
            ))
        halves = jnp.arange(SUMS)[None, :, None] >= OUT_BIAS
        summed = lax.psum(jnp.where(halves, 0.5 * sums, sums), ("clip", "seq"))

        def share(row, count):
            piece = summed[:, row : row + count].reshape(layers, count * width)
            size = count * width // seq_size
            return lax.dynamic_slice_in_dim(piece, seq_at * size, size, 1)

        into, proj, up, down = (
            jnp.stack([matrices[layer][which] for layer in range(layers)]) for which in range(4)
        )
        return (
            out_tokens, grad_tokens, into, share(QUERY_BIAS, 2), proj, share(OUT_BIAS, 1),
            up, share(UP_BIAS, 4), down, share(DOWN_BIAS, 1),
            jnp.stack([share(GAIN, 1), share(GAIN + 1, 1)], 1),
            jnp.stack([share(SHIFT, 1), share(SHIFT + 1, 1)], 1),
        )

    return shards


def solution(mesh):
    rowed = P("clip", "seq", None)
    in_specs = (rowed, P("clip")) + (P(),) * 10 + (rowed,)
    out_specs = (
        rowed,
        rowed,
        P(None, "clip", "seq"),
        P(None, "seq"),
        P(None, "clip", "seq"),
        P(None, "seq"),
        P(None, "clip", "seq"),
        P(None, "seq"),
        P(None, "clip", "seq"),
        P(None, "seq"),
        P(None, None, "seq"),
        P(None, None, "seq"),
    )
    return jax.shard_map(
        build(mesh), mesh=mesh, in_specs=in_specs, out_specs=out_specs, check_vma=False
    )
```

```python
from copy import copy as duplicate
import functools

import jax
import jax.numpy as jnp
from jax import lax
from jax.experimental import pallas as pl
from jax.experimental.pallas import tpu as pltpu
from jax.sharding import PartitionSpec as P

HEADS = 12
HEAD_DIM = 64
CORES = 2
LANES = 128
SCALE = HEAD_DIM**-0.5
SQRT_HALF = 0.5**0.5
GAUSS = 0.3989422804014327
EPS = 1e-05
VMEM = 56 * 1024 * 1024
VMEM_BACK = 63 * 1024 * 1024

f32 = jnp.float32
b16 = jnp.bfloat16


def dot(a, b):
    return lax.dot_general(a, b, (((1,), (0,)), ((), ())), preferred_element_type=f32)


def dot_nt(a, b):
    return lax.dot_general(a, b, (((1,), (1,)), ((), ())), preferred_element_type=f32)


def dot_tn(a, b):
    return lax.dot_general(a, b, (((0,), (0,)), ((), ())), preferred_element_type=f32)


def norm_parts(values):
    center = values - jnp.mean(values, -1, keepdims=True)
    inverse = lax.rsqrt(jnp.mean(center * center, -1, keepdims=True) + EPS)
    return center * inverse, inverse


def norm_back(unit, inverse, gain, grad):
    scaled = grad * gain
    mean_one = jnp.mean(scaled, -1, keepdims=True)
    mean_two = jnp.mean(scaled * unit, -1, keepdims=True)
    back = inverse * (scaled - mean_one - unit * mean_two)
    return back, jnp.sum(grad * unit, 0, keepdims=True), jnp.sum(grad, 0, keepdims=True)


def call(kernel, core, grid, ins, outs, scratch, flops, moved):
    in_specs = [pl.BlockSpec(block, lambda g, c, at=at: at(g, c[0])) for unused, block, at in ins]
    out_specs = [pl.BlockSpec(block, lambda g, c, at=at: at(g, c[0])) for s, d, block, at in outs]
    return pl.pallas_call(
        kernel,
        grid_spec=pltpu.PrefetchScalarGridSpec(
            num_scalar_prefetch=1,
            grid=(grid,),
            in_specs=in_specs,
            out_specs=out_specs,
            scratch_shapes=scratch,
        ),
        out_shape=[jax.ShapeDtypeStruct(shape, dtype) for shape, dtype, b, at in outs],
        compiler_params=pltpu.CompilerParams(
            dimension_semantics=("arbitrary",), vmem_limit_bytes=VMEM
        ),
        cost_estimate=pl.CostEstimate(flops=flops, bytes_accessed=moved, transcendentals=0),
    )(core, *[array for array, b, at in ins])


def all_of(array):
    zeros = (0,) * array.ndim
    return (array, array.shape, lambda g, c: zeros)


def full(shape, dtype):
    zeros = (0,) * len(shape)
    return (shape, dtype, shape, lambda g, c: zeros)


class Geometry:
    def __init__(self, mesh, tokens, ffn):
        self.clip_size, self.seq_size = mesh.shape["clip"], mesh.shape["seq"]
        self.columns = self.clip_size // CORES
        self.held, self.slots, self.width = tokens.shape
        self.ffn = ffn
        self.posts = self.held * CORES
        self.lines = self.seq_size // self.posts
        self.tile = CORES * self.slots
        self.rows = self.held * self.tile
        self.count = self.rows * self.lines
        self.half = self.width // CORES
        self.pairs = self.half // LANES
        self.heads = 2 * self.pairs
        self.quarter = ffn // 4
        self.depth = self.width // self.clip_size
        self.aligned = self.columns == 2 and (ffn // self.seq_size) % LANES == 0

    def locate(self):
        self.clip = lax.axis_index("clip")
        self.seq = lax.axis_index("seq")
        self.core = self.clip % CORES
        self.column = self.clip // CORES
        self.post = self.seq // self.lines
        self.line = self.seq % self.lines
        self.parity = self.post % self.held

    def sibling(self):
        return self.clip + 1 - 2 * self.core, self.seq

    def on_line(self, shift):
        return self.clip, self.post * self.lines + (self.line + shift) % self.lines

    def on_post(self, shift):
        return self.clip, (self.post + shift) % self.posts * self.lines + self.line

    def on_column(self, shift):
        return (self.column + shift) % self.columns * CORES + self.core, self.seq

    def goal(self, turn):
        post = self.held * self.core + (self.post + turn) % self.held
        return self.column * CORES + self.post // self.held, post * self.lines + self.line

    def origin(self, turn, who):
        post = self.held * who + (self.parity + turn) % self.held
        return self.column * CORES + self.post // self.held, post * self.lines + self.line

    def blocked(self, turn):
        return jnp.logical_and(self.post // self.held == self.core, turn == 0)


def remote(source, target, send, receive, device):
    return pltpu.make_async_remote_copy(
        src_ref=source, dst_ref=target, send_sem=send, recv_sem=receive,
        device_id=device, device_id_type=pl.DeviceIdType.MESH,
    )


def meet(geo, devices):
    barrier = pltpu.get_barrier_semaphore()
    total = 0
    for device in devices:
        other = jnp.logical_or(device[0] != geo.clip, device[1] != geo.seq)

        @pl.when(other)
        def greet(device=device):
            pl.semaphore_signal(
                barrier, inc=1, device_id=device, device_id_type=pl.DeviceIdType.MESH
            )

        total = total + other.astype(jnp.int32)
    pl.semaphore_wait(barrier, total)


def loop(count, body):
    def step(at, carry):
        body(at)
        return carry

    lax.fori_loop(0, count, step, 0)


def gelu_parts(inner):
    bell = jnp.exp(-0.5 * inner * inner)
    t = 1.0 / (1.0 + (0.3275911 * SQRT_HALF) * jnp.abs(inner))
    series = t * (0.5 * 0.254829592 + t * (0.5 * -0.284496736 + t * (
        0.5 * 1.421413741 + t * (0.5 * -1.453152027 + t * (0.5 * 1.061405429)))))
    tail = series * bell
    phi = jnp.where(inner >= 0.0, 1.0 - tail, tail)
    return phi, phi + inner * (GAUSS * bell)


KEPT = ("xall", "kx", "v", "q", "ot", "lse", "o", "z1", "hrt", "act", "slope", "z2")


def kept_shapes(geo):
    rows, width, half, count = geo.rows, geo.width, geo.half, geo.count
    return {
        "xall": ((count, width), b16),
        "kx": ((geo.pairs, count, 2 * LANES), b16),
        "v": ((count, half), b16),
        "q": ((rows, half), b16),
        "ot": ((half, rows), f32),
        "lse": ((geo.heads, 8, rows), f32),
        "o": ((rows, half), b16),
        "z1": ((rows, width), f32),
        "hrt": ((width, rows), b16),
        "act": ((rows, geo.ffn // CORES), b16),
        "slope": ((rows, geo.ffn // CORES), b16),
        "z2": ((rows, width), f32),
    }


def forward_kernel(geo, layers, *refs):
    refs = list(refs)

    def take(count):
        taken = refs[:count]
        del refs[:count]
        return taken

    tokens, cotangent, w_in, w_out, w_up, w_down = take(6)
    lengths, in_bias, out_bias, up_bias, down_bias, gains, shifts = take(7)
    out_tokens, cot_rows = take(2)
    stored = [dict(zip(KEPT, take(len(KEPT)))) for unused in range(layers)]
    kept = [dict(zip(KEPT, take(len(KEPT)))) for unused in range(layers)]
    win, wout, wup, wdown = take(4)
    qx, vt, state, hidden, low_out, lens, lens_there, psend, precv, running = take(10)
    (load_sem, save_sem, tok_sem, tok_send, tok_recv, cot_sem, cot_send, cot_recv, sib_send,
     sib_recv, line_send, line_recv, pass_send, pass_recv, part_send, part_recv, out_sem,
     out_send, out_recv, len_sem) = take(20)

    geo = duplicate(geo)
    geo.locate()
    core, tile, slots = geo.core, geo.tile, geo.slots
    held, lines, rows, width, half = geo.held, geo.lines, geo.rows, geo.width, geo.half
    quarter, pairs = geo.quarter, geo.pairs
    sibling = geo.sibling()

    loads = []
    for layer in range(layers):
        parts = [
            (w_in.at[layer, :, pl.ds(pl.multiple_of((kind * CORES + core) * half, half), half)],
             win.at[layer, kind])
            for kind in range(3)
        ]
        parts.append((w_out.at[layer, pl.ds(pl.multiple_of(core * half, half), half), :], wout.at[layer]))
        for block in range(2):
            at = pl.ds(pl.multiple_of((2 * block + core) * quarter, quarter), quarter)
            parts.append((w_up.at[layer, :, at], wup.at[layer, block]))
            parts.append((w_down.at[layer, at, :], wdown.at[layer, block]))
        loads.append([
            pltpu.make_async_copy(source, target, load_sem.at[layer, at])
            for at, (source, target) in enumerate(parts)
        ])
    for copy in loads[0]:
        copy.start()

    sources = [geo.origin(turn, who) for turn in range(held) for who in range(CORES)]
    goals = [geo.goal(turn) for turn in range(held)]
    goals = goals + [(device[0] + 1 - 2 * (device[0] % CORES), device[1]) for device in goals]
    near = [sibling] + [geo.on_line(shift) for shift in range(1, lines)]
    meet(geo, near + sources + goals)

    first = kept[0]["xall"]

    def block_at(turn, who, shift=0):
        start = shift * rows + turn * tile + who * slots
        return pl.ds(start if isinstance(start, int) else pl.multiple_of(start, slots), slots)

    def token_copies(turn, who):
        mine = tokens.at[(geo.post + turn) % held]
        place = first.at[block_at(turn, who)]
        own = pltpu.make_async_copy(mine, place, tok_sem.at[turn])
        return own, remote(mine, place, tok_send.at[turn], tok_recv.at[turn], geo.goal(turn))

    def token_start(turn):
        own, there = token_copies(turn, geo.post // held)
        pl.when(geo.blocked(turn))(own.start)
        pl.when(jnp.logical_not(geo.blocked(turn)))(there.start)

    def token_wait(turn):
        own, there = token_copies(turn, core)
        pl.when(geo.blocked(turn))(own.wait)
        pl.when(jnp.logical_not(geo.blocked(turn)))(there.wait)

    def to_sibling(array, turn, who, shift, send, receive):
        place = array.at[block_at(turn, who, shift)]
        return remote(place, place, send, receive, sibling)

    def to_line(layer, turn, shift):
        array = kept[layer]["xall"]
        source = array.at[block_at(turn, core)]
        target = array.at[block_at(turn, core, shift)]
        return remote(
            source, target, line_send.at[layer, turn, shift - 1], line_recv.at[layer, turn, shift - 1],
            geo.on_line(shift),
        )

    for turn in range(held):
        token_start(turn)
    clip_row = lax.broadcasted_iota(jnp.int32, lens.shape, 0)
    filled = jnp.full(lens.shape, lengths[0], jnp.int32)
    for clip in range(1, held):
        filled = jnp.where(clip_row == clip, lengths[clip], filled)
    lens[...] = filled
    len_copy = remote(lens, lens_there, len_sem.at[0], len_sem.at[1], sibling)
    len_copy.start()

    def clear(at):
        qx[at] = jnp.zeros(qx.shape[1:], b16)
        qx[at, LANES : LANES + 16, :] = (
            lax.broadcasted_iota(jnp.int32, (16, rows), 0) == 0
        ).astype(f32).astype(b16)

    loop(geo.heads, clear)
    len_copy.wait()
    known = jnp.where(geo.post // held == core, lens[...], lens_there[...])
    length = known[0:1, :]
    for clip in range(1, held):
        length = jnp.where(geo.parity == clip, known[clip : clip + 1, :], length)
    lane = lax.broadcasted_iota(jnp.int32, (slots, LANES), 1)
    slot = lax.broadcasted_iota(jnp.int32, (slots, LANES), 0)
    for shift in range(lines):
        for turn in range(held):
            for who in range(CORES):
                post = held * who + (geo.parity + turn) % held
                line = (geo.line + lines - shift) % lines
                outside = (post * lines + line) * slots + slot >= length
                mask = jnp.where(jnp.logical_and(lane == 0, outside), -1e30, 0.0).astype(b16)
                for layer in range(layers):
                    for pair in range(pairs):
                        kept[layer]["kx"][pair, block_at(turn, who, shift), LANES:] = mask

    for turn in range(held):
        token_wait(turn)
        to_sibling(first, turn, core, 0, sib_send.at[turn], sib_recv.at[turn]).start()
        for shift in range(1, lines):
            to_line(0, turn, shift).start()
    for copy in loads[0]:
        copy.wait()
    for copy in loads[1]:
        copy.start()

    def cot_copies(turn, flip):
        mine = cotangent.at[(geo.post + turn) % held]
        place = cot_rows.at[block_at(turn, geo.post // held)]
        goal = geo.goal(turn)
        if flip:
            goal = (goal[0] + 1 - 2 * (goal[0] % CORES), goal[1])
        own = pltpu.make_async_copy(mine, place, cot_sem.at[turn, flip])
        there = remote(
            mine, place, cot_send.at[turn, flip], cot_recv.at[turn, geo.post // held], goal
        )
        here = jnp.logical_and(goal[0] == geo.clip, goal[1] == geo.seq)
        return own, there, here

    def cot_start():
        for turn in range(held):
            for flip in range(CORES):
                own, there, here = cot_copies(turn, flip)
                pl.when(here)(own.start)
                pl.when(jnp.logical_not(here))(there.start)

    def cot_wait():
        for turn in range(held):
            for flip in range(CORES):
                own, there, here = cot_copies(turn, flip)
                pl.when(here)(own.wait)
                pl.when(jnp.logical_not(here))(there.wait_send)
            for who in range(CORES):
                source = geo.origin(turn, who)
                place = cot_rows.at[block_at(turn, who)]
                there = remote(
                    cotangent.at[0], place, cot_send.at[turn, 0], cot_recv.at[turn, who], source
                )
                here = jnp.logical_and(source[0] == geo.clip, source[1] == geo.seq)
                pl.when(jnp.logical_not(here))(there.wait_recv)

    def key_tile(layer, at):
        keep = kept[layer]
        now = pl.ds(pl.multiple_of(at, tile), tile)
        x = keep["xall"][now, :]
        key = dot(x, win[layer, 1]).astype(b16)
        for pair in range(pairs):
            keep["kx"][pair, now, :LANES] = key[:, pair * LANES : (pair + 1) * LANES]
        bias = in_bias[layer : layer + 1, pl.ds(pl.multiple_of(width + core * half, half), half)]
        value = (dot(x, win[layer, 2]) + bias).astype(b16)
        keep["v"][now, :] = value
        vt[:, now] = value.astype(f32).T.astype(b16)

    def query_tile(layer, at):
        keep = kept[layer]
        now = pl.ds(pl.multiple_of(at, tile), tile)
        bias = in_bias[layer : layer + 1, pl.ds(pl.multiple_of(core * half, half), half)]
        query = (dot(keep["xall"][now, :], win[layer, 0]) + bias).astype(b16)
        query = (query * SCALE).astype(b16)
        keep["q"][now, :] = query
        turned = query.astype(f32).T.astype(b16)
        for head in range(geo.heads):
            inside = head % 2 * HEAD_DIM
            qx[head, inside : inside + HEAD_DIM, now] = (
                turned[head * HEAD_DIM : (head + 1) * HEAD_DIM]
            )

    def attend_block(layer, shift, turn):
        keep = kept[layer]
        now = pl.ds(pl.multiple_of(turn * tile, tile), tile)
        span = slice(shift * rows, (shift + 1) * rows)

        def pair_step(pair):
            for inside in range(2):
                head = 2 * pair + inside
                here = pl.ds(pl.multiple_of(head * HEAD_DIM, HEAD_DIM), HEAD_DIM)
                scores = dot(keep["kx"][pair, span, :], qx[head, :, now])
                top = jnp.max(scores, 0, keepdims=True)
                if shift > 0:
                    before = keep["lse"][head, 0:1, now]
                    top = jnp.maximum(top, before)
                    shrink = jnp.exp(before - top)
                weights = jnp.exp(scores - top)
                total = jnp.sum(weights, 0, keepdims=True)
                attended = dot(vt[here, span], weights.astype(b16))
                if shift > 0:
                    total = total + shrink * running[head, 0:1, now]
                    attended = attended + shrink * keep["ot"][here, now]
                if shift < lines - 1:
                    running[head, 0:1, now] = total
                    keep["ot"][here, now] = attended
                    keep["lse"][head, 0:1, now] = top
                else:
                    keep["ot"][here, now] = attended / total
                    keep["lse"][head, 0:1, now] = top + jnp.log(total)

        loop(pairs, pair_step)

    def project_tile(layer, turn):
        keep = kept[layer]
        now = pl.ds(pl.multiple_of(turn * tile, tile), tile)
        attended = keep["ot"][:, now].T.astype(b16)
        keep["o"][now, :] = attended
        share(2 * layer, turn, dot(attended, wout[layer]))

    def part_copy(which, turn):
        now = pl.ds(pl.multiple_of(turn * tile, tile), tile)
        return remote(
            psend.at[which, now, :], precv.at[which, now, :], part_send.at[which, turn],
            part_recv.at[which, turn], sibling,
        )

    def share(which, turn, part):
        now = pl.ds(pl.multiple_of(turn * tile, tile), tile)
        psend[which, now, :] = part.astype(b16)
        part_copy(which, turn).start()

    def collect(which, turn):
        now = pl.ds(pl.multiple_of(turn * tile, tile), tile)
        part_copy(which, turn).wait()
        return psend[which, now, :].astype(f32) + precv[which, now, :].astype(f32)

    def feed_tile(layer, turn):
        keep = kept[layer]
        now = pl.ds(pl.multiple_of(turn * tile, tile), tile)
        x = first[now, :].astype(f32) if layer == 0 else state[now, :]
        summed = x + collect(2 * layer, turn) + out_bias[layer : layer + 1, :]
        keep["z1"][now, :] = summed
        unit, unused = norm_parts(summed)
        normal = unit * gains[layer, 0:1, :] + shifts[layer, 0:1, :]
        hidden[now, :] = normal
        low = normal.astype(b16)
        keep["hrt"][:, now] = low.astype(f32).T.astype(b16)
        size = min(256, quarter)
        total = None
        for block in range(2):
            for start in range(0, quarter, size):
                at = block * quarter + start
                bias = up_bias[
                    layer : layer + 1,
                    pl.ds(pl.multiple_of((2 * block + core) * quarter + start, size), size),
                ]
                inner = dot(low, wup[layer, block, :, start : start + size]) + bias
                phi, slope = gelu_parts(inner)
                active = (inner * phi).astype(b16)
                keep["act"][now, at : at + size] = active
                keep["slope"][now, at : at + size] = slope.astype(b16)
            part = dot(keep["act"][now, block * quarter : (block + 1) * quarter], wdown[layer, block])
            total = part if total is None else total + part
        share(2 * layer + 1, turn, total)

    def norm_tile(layer, turn):
        keep = kept[layer]
        now = pl.ds(pl.multiple_of(turn * tile, tile), tile)
        summed = hidden[now, :] + collect(2 * layer + 1, turn) + down_bias[layer : layer + 1, :]
        keep["z2"][now, :] = summed
        unit, unused = norm_parts(summed)
        result = unit * gains[layer, 1:2, :] + shifts[layer, 1:2, :]
        if layer < layers - 1:
            state[now, :] = result
            kept[layer + 1]["xall"][now, :] = result.astype(b16)
        else:
            low_out[now, :] = result.astype(b16)

    saves = []

    def save(layer, names):
        for name in names:
            copy = pltpu.make_async_copy(
                kept[layer][name], stored[layer][name], save_sem.at[layer, KEPT.index(name)]
            )
            copy.start()
            saves.append(copy)

    for layer in range(layers):
        x_all = kept[layer]["xall"]
        if layer == 0:
            for turn in range(held):
                to_sibling(x_all, turn, core, 0, sib_send.at[turn], sib_recv.at[turn]).wait_send()
                to_sibling(x_all, turn, 1 - core, 0, sib_send.at[turn], sib_recv.at[turn]).wait_recv()
                key_tile(layer, turn * tile)
                query_tile(layer, turn * tile)
        else:
            for copy in loads[layer]:
                copy.wait()

            def own_tile(turn):
                key_tile(layer, turn * tile)
                query_tile(layer, turn * tile)

            loop(held, own_tile)
        for shift in range(lines):
            if shift > 0:
                for turn in range(held):
                    to_line(layer, turn, shift).wait()
                    to_sibling(
                        x_all, turn, core, shift,
                        pass_send.at[layer, turn, shift - 1], pass_recv.at[layer, turn, shift - 1],
                    ).start()
                for turn in range(held):
                    send = pass_send.at[layer, turn, shift - 1]
                    receive = pass_recv.at[layer, turn, shift - 1]
                    to_sibling(x_all, turn, core, shift, send, receive).wait_send()
                    to_sibling(x_all, turn, 1 - core, shift, send, receive).wait_recv()
                    key_tile(layer, shift * rows + turn * tile)
            if shift == lines - 1:
                save(layer, ("xall", "kx", "v", "q"))
                if layer == 0:
                    cot_start()

            def turn_step(turn):
                attend_block(layer, shift, turn)
                if shift == lines - 1:
                    project_tile(layer, turn)

            loop(held, turn_step)
        save(layer, ("ot", "lse", "o"))
        loop(held, functools.partial(feed_tile, layer))
        save(layer, ("z1", "hrt", "act", "slope"))
        for turn in range(held):
            norm_tile(layer, turn)
            if layer < layers - 1:
                for shift in range(1, lines):
                    to_line(layer + 1, turn, shift).start()
        save(layer, ("z2",))

    def out_copies(turn, place):
        mine = low_out.at[block_at(turn, core)]
        own = pltpu.make_async_copy(mine, place, out_sem.at[turn])
        return own, remote(mine, place, out_send.at[turn], out_recv.at[turn], geo.origin(turn, core))

    for turn in range(held):
        own, there = out_copies(turn, out_tokens.at[geo.parity])
        pl.when(geo.blocked(turn))(own.start)
        pl.when(jnp.logical_not(geo.blocked(turn)))(there.start)
    cot_wait()
    for turn in range(held):
        own, there = out_copies(turn, out_tokens.at[(geo.post + turn) % held])
        pl.when(geo.blocked(turn))(own.wait)
        pl.when(jnp.logical_not(geo.blocked(turn)))(there.wait)
    for copy in saves:
        copy.wait()


def forward(geo, layers, tokens, cotangent, lengths, weights, vectors):
    width, rows, half, ffn = geo.width, geo.rows, geo.half, geo.ffn
    shapes = kept_shapes(geo)
    any_spec = pl.BlockSpec(memory_space=pl.ANY)
    vmem_spec = pl.BlockSpec(memory_space=pltpu.VMEM)
    out_shape = [
        jax.ShapeDtypeStruct(tokens.shape, b16),
        jax.ShapeDtypeStruct((rows, width), b16),
    ]
    out_shape += [jax.ShapeDtypeStruct(*shapes[name]) for unused in range(layers) for name in KEPT]
    scratch = [pltpu.VMEM(*shapes[name]) for unused in range(layers) for name in KEPT]
    scratch += [
        pltpu.VMEM((layers, 3, width, half), b16),
        pltpu.VMEM((layers, half, width), b16),
        pltpu.VMEM((layers, 2, width, geo.quarter), b16),
        pltpu.VMEM((layers, 2, geo.quarter, width), b16),
        pltpu.VMEM((geo.heads, 2 * LANES, rows), b16),
        pltpu.VMEM((half, geo.count), b16),
        pltpu.VMEM((rows, width), f32),
        pltpu.VMEM((rows, width), f32),
        pltpu.VMEM((rows, width), b16),
        pltpu.VMEM((8, LANES), jnp.int32),
        pltpu.VMEM((8, LANES), jnp.int32),
        pltpu.VMEM((2 * layers, rows, width), b16),
        pltpu.VMEM((2 * layers, rows, width), b16),
        pltpu.VMEM((geo.heads, 8, rows), f32),
    ]
    held, lines = geo.held, max(geo.lines - 1, 1)
    dma = pltpu.SemaphoreType.DMA
    scratch += [dma(shape) for shape in (
        (layers, 8), (layers, len(KEPT)), (held,), (held,), (held,),
        (held, CORES), (held, CORES), (held, CORES), (held,), (held,),
        (layers, held, lines), (layers, held, lines), (layers, held, lines), (layers, held, lines),
        (2 * layers, held), (2 * layers, held), (held,), (held,), (held,), (2,),
    )]
    results = pl.pallas_call(
        functools.partial(forward_kernel, geo, layers),
        out_shape=out_shape,
        in_specs=[any_spec] * 6 + [pl.BlockSpec(memory_space=pltpu.SMEM)] + [vmem_spec] * 6,
        out_specs=[any_spec] * len(out_shape),
        scratch_shapes=scratch,
        compiler_params=pltpu.CompilerParams(
            collective_id=0, has_side_effects=True, vmem_limit_bytes=VMEM
        ),
        cost_estimate=pl.CostEstimate(flops=3 * 10**10, bytes_accessed=4 * 10**7, transcendentals=0),
    )(tokens, cotangent, *weights, lengths, *vectors)
    count = len(KEPT)
    kept = [
        dict(zip(KEPT, results[2 + layer * count : 2 + (layer + 1) * count]))
        for layer in range(layers)
    ]
    return results[0], results[1], kept


QUERY_BIAS, VALUE_BIAS, UP_BIAS, OUT_BIAS, DOWN_BIAS, GAIN, SHIFT = 0, 1, 2, 6, 7, 8, 10
SUMS = 16
UP, DOWN = 0, 1
INTO, PROJ = 0, 1


def backward_kernel(geo, layers, *refs):
    refs = list(refs)

    def take(count):
        taken = refs[:count]
        del refs[:count]
        return taken

    cot_rows, w_in, w_out, w_up, w_down = take(5)
    stored = [dict(zip(KEPT, take(len(KEPT)))) for unused in range(layers)]
    (gains,) = take(1)
    grad_tokens, sums = take(2)
    if geo.aligned:
        feed_out, attend_out = take(2)
    else:
        plain = [take(6) for unused in range(layers)]
    keep = dict(zip(KEPT, take(len(KEPT))))
    win, wout, wup, wdown = take(4)
    (o_there, low_grad, turned, du_there, psend, precv, do, qx, dox, dq, dk, dv, dq_there,
     dk_there, dv_there, probs_all, grads_all, do_stack, q_stack, dqt, mine_dx, dx_send, dx_recv, line_in) = take(24)
    (load_sem, o_send, o_recv, du_send, du_recv, part_send, part_recv, qkv_send, qkv_recv,
     dx_ssem, dx_rsem, line_send, line_recv, more_send, more_recv, tok_sem, tok_send,
     tok_recv, plain_sem) = take(19)
    if geo.aligned:
        (other, mine, from_x, from_y, from_z, into_cell, proj_cell, into_y, proj_y, into_z, proj_z,
         a_send, a_x, sum_in) = take(14)
        cells = [[into_cell] * layers, [proj_cell.at[layer] for layer in range(layers)]]
        cells_y, cells_z = (into_y, proj_y), (into_z, proj_z)
        (fx_send, fx_recv, fy_send, fy_recv, fz_send, fz_recv, ay_send, ay_recv, az_send, az_recv,
         ax_send, ax_recv, sum_send, sum_recv) = take(14)
        (credit,) = take(1)

    geo = duplicate(geo)
    geo.locate()
    core, tile, slots = geo.core, geo.tile, geo.slots
    held, lines, rows, width, half = geo.held, geo.lines, geo.rows, geo.width, geo.half
    quarter, pairs, posts, depth = geo.quarter, geo.pairs, geo.posts, geo.depth
    post, line, column = geo.post, geo.line, geo.column
    unit = width // geo.seq_size
    sibling = geo.sibling()

    def tile_at(turn):
        return pl.ds(pl.multiple_of(turn * tile, tile), tile)

    def block_at(turn, who, shift=0):
        start = shift * rows + turn * tile + who * slots
        return pl.ds(start if isinstance(start, int) else pl.multiple_of(start, slots), slots)

    NAMES = KEPT + ("win", "wout", "wup", "wdown", "cot")

    def load_copies(layer, name):
        where = load_sem.at[layer, NAMES.index(name)]
        if name == "win":
            return [
                pltpu.make_async_copy(
                    w_in.at[layer, :, pl.ds(pl.multiple_of((kind * CORES + core) * half, half), half)],
                    win.at[kind], load_sem.at[layer, len(NAMES) + kind],
                )
                for kind in range(3)
            ]
        if name == "wout":
            at = pl.ds(pl.multiple_of(core * half, half), half)
            return [pltpu.make_async_copy(w_out.at[layer, at, :], wout, where)]
        if name in ("wup", "wdown"):
            copies = []
            for block in range(2):
                at = pl.ds(pl.multiple_of((2 * block + core) * quarter, quarter), quarter)
                slot = len(NAMES) + 3 + 2 * (name == "wdown") + block
                if name == "wup":
                    pair = w_up.at[layer, :, at], wup.at[block]
                else:
                    pair = w_down.at[layer, at, :], wdown.at[block]
                copies.append(pltpu.make_async_copy(*pair, load_sem.at[layer, slot]))
            return copies
        if name == "hrt" and geo.aligned:
            return [
                pltpu.make_async_copy(
                    stored[layer][name].at[pl.ds(pl.multiple_of((2 * which + core) * depth, depth), depth), :],
                    keep[name].at[which * depth : (which + 1) * depth, :],
                    load_sem.at[layer, len(NAMES) + 7 + which],
                )
                for which in range(2)
            ]
        if name == "cot":
            return [pltpu.make_async_copy(cot_rows, low_grad, where)]
        return [pltpu.make_async_copy(stored[layer][name], keep[name], where)]

    def load(layer, *names):
        for name in names:
            for copy in load_copies(layer, name):
                copy.start()

    def loaded(layer, *names):
        for name in names:
            for copy in load_copies(layer, name):
                copy.wait()

    top = layers - 1
    load(top, "z2", "cot", "wdown", "slope", "wup", "act", "z1", "wout", "q", "kx", "v", "ot",
         "lse", "win", "hrt", "xall", "o")

    sources = [geo.origin(turn, who) for turn in range(held) for who in range(CORES)]
    goals = [geo.goal(turn) for turn in range(held)]
    near = [sibling] + [geo.on_line(shift) for shift in range(1, lines)]
    if geo.aligned:
        near += [geo.on_post(shift) for shift in range(1, posts)]
        near += [geo.on_column(shift) for shift in range(1, geo.columns)]
    goals = goals + [(device[0] + 1 - 2 * (device[0] % CORES), device[1]) for device in goals]
    meet(geo, near + sources + goals)

    def o_copy(layer):
        return remote(stored[layer]["o"], o_there, o_send.at[layer], o_recv.at[layer], sibling)

    def clear(at):
        qx[at] = jnp.zeros(qx.shape[1:], b16)
        qx[at, LANES : LANES + 16, :] = (
            lax.broadcasted_iota(jnp.int32, (16, rows), 0) == 0
        ).astype(f32).astype(b16)
        dox[at] = jnp.zeros(dox.shape[1:], b16)

    loop(2, clear)
    sums[...] = jnp.zeros_like(sums)

    def add_sum(layer, row, lanes, value):
        sums[layer, pl.ds(row, 1), lanes] += value

    everywhere = slice(None)


    def x_copy(layer, kind, z):
        return remote(
            other.at[kind, z], from_x.at[kind, z], fx_send.at[layer, kind, z],
            fx_recv.at[layer, kind, z], geo.on_column(1),
        )

    def y_copy(layer, kind, z, shift):
        return remote(
            mine.at[layer, kind, z, (line + shift) % lines], from_y.at[layer, kind, z, shift - 1],
            fy_send.at[layer, kind, z, shift - 1], fy_recv.at[layer, kind, z, shift - 1],
            geo.on_line(shift),
        )

    def z_copy(layer, kind, shift):
        return remote(
            mine.at[layer, kind, (post + shift) % posts, line], from_z.at[layer, kind, shift - 1],
            fz_send.at[layer, kind, shift - 1], fz_recv.at[layer, kind, shift - 1],
            geo.on_post(shift),
        )

    def order(step):
        return (post + step + 1) % posts

    def land_x(layer, kind, step):
        z = order(step)
        x_copy(layer, kind, z).wait()
        total = mine[layer, kind, z].astype(f32) + from_x[kind, z].astype(f32)
        mine[layer, kind, z] = total.astype(b16)
        for shift in range(1, lines):
            y_copy(layer, kind, z, shift).start()
        if layer > 0 and step == posts - 1:
            device = geo.on_column(1)
            pl.semaphore_signal(
                credit.at[kind], inc=1, device_id=device, device_id_type=pl.DeviceIdType.MESH
            )

    def land_y(layer, kind, step):
        z = order(step)
        total = mine[layer, kind, z, line].astype(f32)
        for shift in range(1, lines):
            y_copy(layer, kind, z, shift).wait()
            total = total + from_y[layer, kind, z, shift - 1].astype(f32)
        mine[layer, kind, z, line] = total.astype(b16)
        if step + 1 < posts:
            z_copy(layer, kind, step + 1).start()

    def land_z(layer, kind):
        total = mine[layer, kind, post, line].astype(f32)
        for shift in range(1, posts):
            z_copy(layer, kind, shift).wait()
            total = total + from_z[layer, kind, shift - 1].astype(f32)
        feed_out[layer, kind] = total

    def ay_copy(layer, kind, z, shift):
        return remote(
            cells[kind][layer].at[(line + shift) % lines, z], cells_y[kind].at[layer, z, shift - 1],
            ay_send.at[layer, kind, z, shift - 1], ay_recv.at[layer, kind, z, shift - 1],
            geo.on_line(shift),
        )

    def az_copy(layer, kind, shift):
        return remote(
            cells[kind][layer].at[line, (post + shift) % posts], cells_z[kind].at[layer, shift - 1],
            az_send.at[layer, kind, shift - 1], az_recv.at[layer, kind, shift - 1],
            geo.on_post(shift),
        )

    def ax_copy(layer, kind):
        span = slice(0, 3 * unit) if kind == INTO else slice(3 * unit, 4 * unit)
        return remote(
            a_send.at[layer, span], a_x.at[layer, span], ax_send.at[layer, kind],
            ax_recv.at[layer, kind], geo.on_column(1),
        )

    def send_ay(layer, kind):
        for step in range(posts):
            for shift in range(1, lines):
                ay_copy(layer, kind, order(step), shift).start()

    def land_ay(layer, kind, step):
        z = order(step)
        cell = cells[kind][layer]
        total = cell[line, z].astype(f32)
        for shift in range(1, lines):
            ay_copy(layer, kind, z, shift).wait()
            total = total + cells_y[kind][layer, z, shift - 1].astype(f32)
        cell[line, z] = total.astype(b16)
        if step + 1 < posts:
            az_copy(layer, kind, step + 1).start()

    def land_az(layer, kind):
        total = cells[kind][layer][line, post].astype(f32)
        for shift in range(1, posts):
            az_copy(layer, kind, shift).wait()
            total = total + cells_z[kind][layer, shift - 1].astype(f32)
        low, high = total[:, :depth], total[:, depth:]
        span = slice(0, 3 * unit) if kind == INTO else slice(3 * unit, 4 * unit)
        attend_out[layer, span] = jnp.where(column == 0, low, high)
        a_send[layer, span] = jnp.where(column == 0, high, low).astype(b16)
        ax_copy(layer, kind).start()

    def land_ax(layer, kind):
        ax_copy(layer, kind).wait()
        span = slice(0, 3 * unit) if kind == INTO else slice(3 * unit, 4 * unit)
        attend_out[layer, span] = attend_out[layer, span] + a_x[layer, span].astype(f32)

    work = []

    def plan(*tasks):
        for function, *given in tasks:
            work.append(functools.partial(function, *given))

    def progress(count):
        for unused in range(min(count, len(work))):
            work.pop(0)()

    def progress_past(function, *given):
        while any(task.func is function and task.args == given for task in work):
            work.pop(0)()


    def part_copy(layer, turn):
        return remote(
            psend.at[tile_at(turn), :], precv.at[tile_at(turn), :], part_send.at[layer, turn],
            part_recv.at[layer, turn], sibling,
        )

    def du_copy(layer, turn):
        return remote(
            keep["slope"].at[tile_at(turn), :], du_there.at[tile_at(turn), :],
            du_send.at[layer, turn], du_recv.at[layer, turn], sibling,
        )

    def norm_grads(layer, which, values, grad):
        unit, inverse = norm_parts(values)
        gain = gains[layer, which : which + 1, :]
        back, gain_grad, shift_grad = norm_back(unit, inverse, gain, grad)
        add_sum(layer, GAIN + which, everywhere, gain_grad)
        add_sum(layer, SHIFT + which, everywhere, shift_grad)
        return back

    def feed_back_tile(layer, turn):
        now = tile_at(turn)
        grad = low_grad[now, :].astype(f32)
        if layer < top:
            grad = grad + keep["z1"][now, :]
        back = norm_grads(layer, 1, keep["z2"][now, :], grad)
        keep["z2"][now, :] = back
        low = back.astype(b16)
        wide = low.astype(f32)
        turned[:, now] = wide.T.astype(b16)
        add_sum(layer, DOWN_BIAS, everywhere, jnp.sum(wide, 0, keepdims=True))
        size = min(256, quarter)
        total = None
        for block in range(2):
            for start in range(0, quarter, size):
                lanes = slice(block * quarter + start, block * quarter + start + size)
                grads = dot_nt(low, wdown[block, start : start + size, :])
                grads = (grads * keep["slope"][now, lanes].astype(f32)).astype(b16)
                keep["slope"][now, lanes] = grads
                add_sum(
                    layer, UP_BIAS + 2 * block + core, slice(start, start + size),
                    jnp.sum(grads.astype(f32), 0, keepdims=True),
                )
            lanes = slice(block * quarter, (block + 1) * quarter)
            part = dot_nt(keep["slope"][now, lanes], wup[block])
            total = part if total is None else total + part
        psend[now, :] = total.astype(b16)
        part_copy(layer, turn).start()
        du_copy(layer, turn).start()

    def down_grads(layer, which, start):
        lanes = pl.ds(pl.multiple_of(which * quarter, quarter), quarter)
        cols = width // geo.seq_size

        def chunk(step):
            z = order(step)
            at = pl.ds(pl.multiple_of(z * lines * cols, lines * cols), lines * cols)
            result = dot(turned[at, :], keep["act"][:, lanes]).astype(b16)
            for row in range(lines):
                for piece in range(2):
                    block = result[
                        row * cols : (row + 1) * cols,
                        piece * quarter // 2 : (piece + 1) * quarter // 2,
                    ]
                    span = slice(piece * cols, (piece + 1) * cols)
                    if start:
                        other[DOWN, z, row, span, :] = block
                    else:
                        mine[layer, DOWN, z, row, span, :] = block
            if start:
                x_copy(layer, DOWN, z).start()

        loop(posts, chunk)

    def up_grads(layer, which, start):
        left = keep["hrt"][pl.ds(pl.multiple_of(which * depth, depth), depth), :]
        size = quarter // lines
        for block in range(2):
            lanes = slice(block * quarter, (block + 1) * quarter)
            for there, array in ((0, keep["slope"]), (1, du_there)):
                z = 2 * block + core + there * (1 - 2 * core)
                result = dot(left, array[:, lanes]).astype(b16)
                for row in range(lines):
                    piece = result[:, row * size : (row + 1) * size]
                    if start:
                        other[UP, z, row] = piece
                    else:
                        mine[layer, UP, z, row] = piece
        if start:
            for step in range(posts):
                x_copy(layer, UP, order(step)).start()

    def feed_grads(layer, kind):
        make = down_grads if kind == DOWN else up_grads
        if layer < top:
            pl.semaphore_wait(credit.at[kind], 1)
        make(layer, 1 - column, True)
        make(layer, column, False)

    def proj_back_tile(layer, turn):
        now = tile_at(turn)
        part_copy(layer, turn).wait()
        grad = keep["z2"][now, :] + (psend[now, :].astype(f32) + precv[now, :].astype(f32))
        back = norm_grads(layer, 0, keep["z1"][now, :], grad)
        keep["z1"][now, :] = back
        low = back.astype(b16)
        wide = low.astype(f32)
        turned[:, now] = wide.T.astype(b16)
        add_sum(layer, OUT_BIAS, everywhere, jnp.sum(wide, 0, keepdims=True))
        do[now, :] = dot_nt(low, wout[...]).astype(b16)

    lane_head = lax.broadcasted_iota(jnp.int32, (tile, LANES), 1) // HEAD_DIM

    def attend_back_pair(layer, pair):
        lanes = pl.ds(pl.multiple_of(pair * LANES, LANES), LANES)
        key_t = keep["kx"][pair, :, :LANES].astype(f32).T.astype(b16)
        query_t = keep["q"][:, lanes].astype(f32).T.astype(b16)
        grad_t = do[:, lanes].astype(f32).T.astype(b16)
        for head in range(2):
            here = slice(head * HEAD_DIM, (head + 1) * HEAD_DIM)
            qx[head, here, :] = query_t[here]
            dox[head, here, :] = grad_t[here]

        def turn_step(turn):
            now = tile_at(turn)
            query = keep["q"][now, lanes].astype(f32)
            outgrad = do[now, lanes].astype(f32)
            for head in range(2):
                here = slice(head * HEAD_DIM, (head + 1) * HEAD_DIM)
                chosen = (lane_head == head).astype(f32)
                place = pl.ds(pl.multiple_of((2 * turn + head) * tile, tile), tile)
                do_stack[place, :] = (outgrad * chosen).astype(b16)
                q_stack[place, :] = (query * chosen).astype(b16)
                scores = dot(keep["kx"][pair], qx[head, :, now])
                probs = jnp.exp(scores - keep["lse"][2 * pair + head, 0:1, now])
                probs_all[:, place] = probs.astype(b16)
                grads = dot(keep["v"][:, lanes], dox[head, :, now])
                own = pl.ds(pl.multiple_of(pair * LANES + head * HEAD_DIM, HEAD_DIM), HEAD_DIM)
                delta = jnp.sum(
                    dox[head, here, now].astype(f32) * keep["ot"][own, now], 0, keepdims=True
                )
                score_grads = (probs * (grads - delta)).astype(b16)
                grads_all[:, place] = score_grads
                dqt[here, now] = dot(key_t[here], score_grads)

        loop(held, turn_step)
        query_grad = (dqt[...].T * SCALE).astype(b16)
        value_grad = dot(probs_all[...], do_stack[...]).astype(b16)
        dq[:, lanes] = query_grad
        dk[:, lanes] = dot(grads_all[...], q_stack[...]).astype(b16)
        dv[:, lanes] = value_grad
        spot = pl.ds(pl.multiple_of(core * half + pair * LANES, LANES), LANES)
        add_sum(layer, QUERY_BIAS, spot, jnp.sum(query_grad.astype(f32), 0, keepdims=True))
        add_sum(layer, VALUE_BIAS, spot, jnp.sum(value_grad.astype(f32), 0, keepdims=True))

    def qkv_copies(layer):
        return [
            remote(source, target, qkv_send.at[layer, at], qkv_recv.at[layer, at], sibling)
            for at, (source, target) in enumerate(((dq, dq_there), (dk, dk_there), (dv, dv_there)))
        ]

    def dx_copy(layer, shift, turn):
        return remote(
            dx_send.at[shift * held + turn], dx_recv.at[shift * held + turn],
            dx_ssem.at[layer, shift * held + turn], dx_rsem.at[layer, shift * held + turn], sibling,
        )

    def dx_tile(layer, shift, turn):
        now = pl.ds(pl.multiple_of(shift * rows + turn * tile, tile), tile)
        total = dot_nt(dk[now, :], win[1]) + dot_nt(dv[now, :], win[2])
        if shift == 0:
            total = total + dot_nt(dq[now, :], win[0])
        first, second = total[:slots], total[slots:]
        mine_dx[shift * held + turn] = jnp.where(core == 0, first, second).astype(b16)
        dx_send[shift * held + turn] = jnp.where(core == 0, second, first).astype(b16)
        dx_copy(layer, shift, turn).start()

    def line_copy(layer, shift, turn):
        return remote(
            dx_recv.at[shift * held + turn], line_in.at[layer, shift - 1, turn],
            line_send.at[layer, shift - 1, turn], line_recv.at[layer, shift - 1, turn],
            geo.on_line(lines - shift),
        )

    def more_copy(layer, turn, who):
        place = low_grad.at[block_at(turn, who)]
        return remote(place, place, more_send.at[layer, turn], more_recv.at[layer, turn], sibling)

    def token_copies(turn, place):
        own = pltpu.make_async_copy(low_grad.at[block_at(turn, core)], place, tok_sem.at[turn])
        there = remote(
            low_grad.at[block_at(turn, core)], place, tok_send.at[turn], tok_recv.at[turn],
            geo.origin(turn, core),
        )
        return own, there

    def mine_lanes(x):
        cuts = [x[:, at * depth : (at + 1) * depth] for at in range(2 * CORES)]
        return jnp.where(
            core == 0, jnp.concatenate([cuts[0], cuts[2]], 1), jnp.concatenate([cuts[1], cuts[3]], 1)
        )

    def into_grads(layer):
        units = half // unit
        x = mine_lanes(keep["xall"][...])
        for kind, pair in enumerate(((dq, dq_there), (dk, dk_there), (dv, dv_there))):
            for there, ref in enumerate(pair):
                owner = core + there * (1 - 2 * core)
                count = ref.shape[0]
                result = dot_tn(ref[...], x[:count]).astype(b16)
                for at in range(units):
                    index = (2 * kind + owner) * units + at
                    seq = index // 3
                    where = pl.ds(pl.multiple_of(index % 3 * unit, unit), unit)
                    into_cell[seq % lines, seq // lines, where, :] = result[at * unit : (at + 1) * unit]
        send_ay(layer, INTO)

    def proj_grads(layer):
        here, there = keep["o"][...], o_there[...]
        features = jnp.where(
            core == 0,
            jnp.concatenate([here[:, :depth], there[:, :depth]], 1),
            jnp.concatenate([there[:, depth:], here[:, depth:]], 1),
        )
        result = dot(turned[...], features).astype(b16)
        for seq in range(geo.seq_size):
            proj_cell[layer, seq % lines, seq // lines] = result[seq * unit : (seq + 1) * unit]
        send_ay(layer, PROJ)

    def plain_out(layer, names):
        sources = {"du": keep["slope"], "dft": turned, "dat": turned, "dq": dq, "dk": dk, "dv": dv}
        order = ("du", "dft", "dat", "dq", "dk", "dv")
        copies = [
            pltpu.make_async_copy(sources[name], plain[layer][order.index(name)], plain_sem.at[order.index(name)])
            for name in names
        ]
        for copy in copies:
            copy.start()
        for copy in copies:
            copy.wait()

    for layer in range(layers - 1, -1, -1):
        last = layer == 0
        below = layer - 1
        if layer == top:
            loaded(layer, "cot")
        else:
            for turn in range(held):
                more_copy(layer + 1, turn, core).wait_send()
                more_copy(layer + 1, turn, 1 - core).wait_recv()
        o_copy(layer).start()
        loaded(layer, "z2", "wdown", "slope", "wup")
        loop(held, functools.partial(feed_back_tile, layer))
        if not last:
            load(below, "wdown", "wup")
        else:
            load(layer, "z1")
        loaded(layer, "act")
        if geo.aligned:
            if layer < top:
                progress(3)
            feed_grads(layer, DOWN)
            landings = [(land_x, layer, DOWN, 0), (land_x, layer, DOWN, 1)]
            for step in range(posts):
                landings.append((land_y, layer, DOWN, step))
                if step + 2 < posts:
                    landings.append((land_x, layer, DOWN, step + 2))
            if last:
                progress(1)
                loaded(layer, "hrt")
                for turn in range(held):
                    du_copy(layer, turn).wait()
                feed_grads(layer, UP)
                progress(1)
            else:
                plan(*landings)
        else:
            plain_out(layer, ("dft",))
        if not last:
            load(below, "act")
        loaded(layer, "z1", "wout")
        loop(held, functools.partial(proj_back_tile, layer))
        if not last:
            load(below, "wout", "z2")
        if geo.aligned:
            loaded(layer, "o")
            o_copy(layer).wait()
            proj_grads(layer)
            if last:
                plan(
                    (land_x, 0, DOWN, 0), (land_ay, 1, INTO, 2), (land_x, 0, DOWN, 1),
                    (land_y, 1, UP, 0), (land_ay, 1, INTO, 3), (land_y, 1, UP, 1),
                    (land_x, 0, DOWN, 2), (land_y, 1, UP, 2), (land_x, 0, DOWN, 3),
                    (land_y, 1, UP, 3), (land_ay, 0, PROJ, 0), (land_ay, 0, PROJ, 1),
                    (land_az, 1, INTO), (land_ay, 0, PROJ, 2), (land_ay, 0, PROJ, 3),
                    (land_y, 0, DOWN, 0), (land_x, 0, UP, 0), (land_y, 0, DOWN, 1),
                    (land_z, 1, UP), (land_x, 0, UP, 1), (land_y, 0, DOWN, 2), (land_ax, 1, INTO),
                    (land_y, 0, DOWN, 3), (land_x, 0, UP, 2), (land_az, 0, PROJ),
                )
        loaded(layer, "q", "kx", "v", "ot", "lse")
        for pair in range(pairs):
            attend_back_pair(layer, pair)
            if geo.aligned:
                progress((1, 2, 2)[min(pair, 2)] if not last else 3)
                if not last and pair == pairs - 2:
                    loaded(layer, "hrt")
                    for turn in range(held):
                        du_copy(layer, turn).wait()
                    feed_grads(layer, UP)
        if not last:
            load(below, "q", "kx", "v", "ot", "lse")
        for copy in qkv_copies(layer):
            copy.start()
        loaded(layer, "win")
        for shift in range(1, lines):
            loop(held, functools.partial(dx_tile, layer, shift))
        if geo.aligned:
            progress(2)
        for shift in range(1, lines):
            for turn in range(held):
                dx_copy(layer, shift, turn).wait()
                at = shift * held + turn
                dx_recv[at] = (mine_dx[at].astype(f32) + dx_recv[at].astype(f32)).astype(b16)
                line_copy(layer, shift, turn).start()
        loop(held, functools.partial(dx_tile, layer, 0))
        if not last:
            load(below, "win")
        if geo.aligned:
            progress(1 if not last else 5)
            if last:
                progress_past(land_az, 1, INTO)
            for copy in qkv_copies(layer):
                copy.wait()
            loaded(layer, "xall")
            into_grads(layer)
            if not last:
                progress(len(work))
                plan(
                    (land_x, 1, UP, 0), (land_x, 1, UP, 1), (land_x, 1, UP, 2), (land_x, 1, UP, 3),
                    (land_z, 1, DOWN), (land_ay, 1, PROJ, 0), (land_ay, 1, PROJ, 1),
                    (land_ay, 1, PROJ, 2), (land_ay, 1, PROJ, 3), (land_ay, 1, INTO, 0),
                    (land_ay, 1, INTO, 1), (land_az, 1, PROJ), (land_ax, 1, PROJ),
                )
                progress(2)
        else:
            for turn in range(held):
                du_copy(layer, turn).wait()
            for copy in qkv_copies(layer):
                copy.wait()
            loaded(layer, "hrt", "xall", "o")
            o_copy(layer).wait()
            plain_out(layer, ("du", "dat", "dq", "dk", "dv"))
        if not last:
            load(below, "hrt", "slope", "xall", "o")
        for turn in range(held):
            dx_copy(layer, 0, turn).wait()
            total = mine_dx[turn].astype(f32) + dx_recv[turn].astype(f32)
            for shift in range(1, lines):
                line_copy(layer, shift, turn).wait()
                total = total + line_in[layer, shift - 1, turn].astype(f32)
            if not last:
                low_grad[block_at(turn, core), :] = total.astype(b16)
                more_copy(layer, turn, core).start()
            else:
                total = total + keep["z1"][block_at(turn, core), :]
                low_grad[block_at(turn, core), :] = total.astype(b16)
                own, there = token_copies(turn, grad_tokens.at[geo.parity])
                pl.when(geo.blocked(turn))(own.start)
                pl.when(jnp.logical_not(geo.blocked(turn)))(there.start)

    if geo.aligned:
        def sum_copy(hop, device):
            return remote(sums, sum_in.at[hop], sum_send.at[hop], sum_recv.at[hop], device)

        def sum_hop(first, devices):
            copies = [sum_copy(first + at, device) for at, device in enumerate(devices)]
            for copy in copies:
                copy.start()
            return copies

        def sum_land(first, copies):
            total = sums[...]
            for at, copy in enumerate(copies):
                copy.wait()
                total = total + sum_in[first + at]
            sums[...] = total

        halves = lax.broadcasted_iota(jnp.int32, sums.shape, 1) >= OUT_BIAS
        sums[...] = jnp.where(halves, 0.5 * sums[...], sums[...])
        moved = sum_hop(0, [sibling])
        progress(len(work))
        sum_land(0, moved)
        moved = sum_hop(1, [geo.on_column(1)])
        land_ay(0, INTO, 0)
        land_x(0, UP, 3)
        sum_land(1, moved)
        moved = sum_hop(2, [geo.on_line(shift) for shift in range(1, lines)])
        land_ay(0, INTO, 1)
        land_ax(0, PROJ)
        land_y(0, UP, 0)
        sum_land(2, moved)
        moved = sum_hop(1 + lines, [geo.on_post(shift) for shift in range(1, posts)])
        land_ay(0, INTO, 2)
        land_y(0, UP, 1)
        land_y(0, UP, 2)
        land_z(0, DOWN)
        sum_land(1 + lines, moved)
        land_ay(0, INTO, 3)
        land_y(0, UP, 3)
        land_az(0, INTO)
        land_z(0, UP)
        land_ax(0, INTO)
    for turn in range(held):
        own, there = token_copies(turn, grad_tokens.at[(post + turn) % held])
        pl.when(geo.blocked(turn))(own.wait)
        pl.when(jnp.logical_not(geo.blocked(turn)))(there.wait)


def backward(geo, layers, cot_rows, weights, kept, gains):
    width, rows, half, ffn, count = geo.width, geo.rows, geo.half, geo.ffn, geo.count
    held, lines, posts, slots, quarter = geo.held, geo.lines, geo.posts, geo.slots, geo.quarter
    shapes = kept_shapes(geo)
    any_spec = pl.BlockSpec(memory_space=pl.ANY)
    vmem_spec = pl.BlockSpec(memory_space=pltpu.VMEM)
    unit = width // geo.seq_size
    out = [((held, slots, width), b16), ((layers, SUMS, width), f32)]
    out_specs = [any_spec, vmem_spec]
    if geo.aligned:
        out += [
            ((layers, 2, geo.depth, quarter // lines), f32),
            ((layers, 4 * unit, geo.depth), f32),
        ]
        out_specs += [vmem_spec] * 2
    else:
        for unused in range(layers):
            out += [
                ((rows, ffn // CORES), b16), ((width, rows), b16), ((width, rows), b16),
                ((rows, half), b16), ((count, half), b16), ((count, half), b16),
            ]
            out_specs += [any_spec] * 6
    vmem = pltpu.VMEM
    if geo.aligned:
        shapes["hrt"] = (2 * geo.depth, rows), b16
    scratch = [vmem(*shapes[name]) for name in KEPT]
    scratch += [
        vmem((3, width, half), b16), vmem((half, width), b16),
        vmem((2, width, quarter), b16), vmem((2, quarter, width), b16),
        vmem((rows, half), b16),
        vmem((rows, width), b16),
        vmem((width, rows), b16),
        vmem((rows, ffn // CORES), b16),
        vmem((rows, width), b16), vmem((rows, width), b16),
        vmem((rows, half), b16),
        vmem((2, 2 * LANES, rows), b16), vmem((2, LANES, rows), b16),
        vmem((rows, half), b16), vmem((count, half), b16), vmem((count, half), b16),
        vmem((rows, half), b16), vmem((count, half), b16), vmem((count, half), b16),
        vmem((count, 2 * rows), b16), vmem((count, 2 * rows), b16),
        vmem((2 * rows, LANES), b16), vmem((2 * rows, LANES), b16), vmem((LANES, rows), f32),
        vmem((lines * held, slots, width), b16),
        vmem((lines * held, slots, width), b16), vmem((lines * held, slots, width), b16),
        vmem((layers, lines - 1, held, slots, width), b16),
    ]
    dma = pltpu.SemaphoreType.DMA
    scratch += [dma(shape) for shape in (
        (layers, len(KEPT) + 16), (layers,), (layers,), (layers, held), (layers, held),
        (layers, held), (layers, held), (layers, 3), (layers, 3),
        (layers, lines * held), (layers, lines * held),
        (layers, lines - 1, held), (layers, lines - 1, held),
        (layers, held), (layers, held), (held,), (held,), (held,), (6,),
    )]
    if geo.aligned:
        block = (geo.depth, quarter // lines)
        into, proj = (3 * unit, 2 * geo.depth), (unit, 2 * geo.depth)
        hops = 1 + 1 + (lines - 1) + (posts - 1)
        scratch += [
            vmem((2, posts, lines, *block), b16), vmem((layers, 2, posts, lines, *block), b16),
            vmem((2, posts, lines, *block), b16),
            vmem((layers, 2, posts, lines - 1, *block), b16),
            vmem((layers, 2, posts - 1, *block), b16),
            vmem((lines, posts, *into), b16), vmem((layers, lines, posts, *proj), b16),
            vmem((layers, posts, lines - 1, *into), b16), vmem((layers, posts, lines - 1, *proj), b16),
            vmem((layers, posts - 1, *into), b16), vmem((layers, posts - 1, *proj), b16),
            vmem((layers, 4 * unit, geo.depth), b16), vmem((layers, 4 * unit, geo.depth), b16),
            vmem((hops, layers, SUMS, width), f32),
        ]
        scratch += [dma(shape) for shape in (
            (layers, 2, posts), (layers, 2, posts),
            (layers, 2, posts, lines - 1), (layers, 2, posts, lines - 1),
            (layers, 2, posts - 1), (layers, 2, posts - 1),
            (layers, 2, posts, lines - 1), (layers, 2, posts, lines - 1),
            (layers, 2, posts - 1), (layers, 2, posts - 1), (layers, 2), (layers, 2),
            (hops,), (hops,),
        )]
        scratch += [pltpu.SemaphoreType.REGULAR((2,))]
    stored = [kept[layer][name] for layer in range(layers) for name in KEPT]
    return pl.pallas_call(
        functools.partial(backward_kernel, geo, layers),
        out_shape=[jax.ShapeDtypeStruct(*shape) for shape in out],
        in_specs=[any_spec] * (5 + len(stored)) + [vmem_spec],
        out_specs=out_specs,
        scratch_shapes=scratch,
        compiler_params=pltpu.CompilerParams(
            collective_id=1, has_side_effects=True, vmem_limit_bytes=VMEM_BACK
        ),
        cost_estimate=pl.CostEstimate(flops=8 * 10**10, bytes_accessed=6 * 10**7, transcendentals=0),
    )(cot_rows, *weights, *stored, gains)


def finish_kernel(
    geo, core_ref, sums_ref, feed_ref, attend_ref, out_in_ref, grad_in_ref,
    out_ref, grad_ref, into_ref, in_bias_ref, proj_ref, out_bias_ref, up_ref, up_bias_ref, down_ref, down_bias_ref,
    gain_ref, shift_ref,
):
    seq = core_ref[0]
    out_ref[...] = out_in_ref[...]
    grad_ref[...] = grad_in_ref[...]
    layers = feed_ref.shape[0]
    unit = geo.width // geo.seq_size
    wide, span = 2 * unit, geo.ffn // geo.seq_size
    per_row, per_quarter = geo.width // wide, geo.quarter // span

    def turn(rows, amount):
        return pltpu.roll(rows, (geo.width - amount) % geo.width, 1)

    for layer in range(layers):
        up_ref[layer] = feed_ref[layer, UP]
        down = feed_ref[layer, DOWN]
        down_ref[layer] = jnp.concatenate([down[:unit], down[unit:]], 1)
        both = attend_ref[layer].T
        into_ref[layer] = both[:, : 3 * unit]
        proj_ref[layer] = both[:, 3 * unit :]
        sums = sums_ref[layer]
        narrow = turn(sums, seq * unit)
        out_bias_ref[layer : layer + 1, :] = narrow[OUT_BIAS : OUT_BIAS + 1, :unit]
        down_bias_ref[layer : layer + 1, :] = narrow[DOWN_BIAS : DOWN_BIAS + 1, :unit]
        gain_ref[layer] = narrow[GAIN : GAIN + 2, :unit]
        shift_ref[layer] = narrow[SHIFT : SHIFT + 2, :unit]
        middle = turn(sums, seq % per_row * wide)
        first = middle[QUERY_BIAS : QUERY_BIAS + 1, :wide]
        second = middle[VALUE_BIAS : VALUE_BIAS + 1, :wide]
        in_bias_ref[layer : layer + 1, :] = jnp.where(seq < per_row, first, second)
        large = turn(sums, seq % per_quarter * span)
        chosen = large[UP_BIAS : UP_BIAS + 1, :span]
        for block in range(1, 4):
            chosen = jnp.where(
                seq // per_quarter == block, large[UP_BIAS + block : UP_BIAS + block + 1, :span], chosen
            )
        up_bias_ref[layer : layer + 1, :] = chosen


def finish(geo, layers, seq, sums, feed_out, attend_out, out_tokens, grad_tokens):
    unit, width = geo.width // geo.seq_size, geo.width
    span = geo.ffn // geo.seq_size
    depth = geo.depth
    shapes = [
        (layers, depth, 3 * unit), (layers, 2 * unit), (layers, depth, unit), (layers, unit),
        (layers, depth, span), (layers, span), (layers, unit, geo.ffn // geo.clip_size),
        (layers, unit), (layers, 2, unit), (layers, 2, unit),
    ]
    results = list(call(
        functools.partial(finish_kernel, geo), seq, 1,
        [all_of(array) for array in (sums, feed_out, attend_out, out_tokens, grad_tokens)],
        [full(out_tokens.shape, b16)] * 2 + [full(shape, f32) for shape in shapes], [],
        10**7, 10**7,
    ))
    results[8] = jnp.swapaxes(results[8], 1, 2)
    return results


def build(mesh):
    clip_size, seq_size = mesh.shape["clip"], mesh.shape["seq"]

    def shards(
        tokens, lengths, attn_in, in_bias, attn_out, out_bias, ffn_in, ffn_in_bias,
        ffn_out, ffn_out_bias, norm_gain, norm_bias, cotangent,
    ):
        layers = attn_in.shape[0]
        geo = Geometry(mesh, tokens, ffn_in.shape[2])
        geo.locate()
        held, width, ffn, half, quarter = geo.held, geo.width, geo.ffn, geo.half, geo.quarter
        aligned, core = geo.aligned, geo.core
        seq_at = geo.seq

        weights = (attn_in, attn_out, ffn_in, ffn_out)
        out_tokens, cot_rows, kept = forward(
            geo, layers, tokens, cotangent, lengths, weights,
            (in_bias, out_bias, ffn_in_bias, ffn_out_bias, norm_gain, norm_bias),
        )
        grad_tokens, sums, *results = backward(geo, layers, cot_rows, weights, kept, norm_gain)
        if aligned:
            seq_arg = jnp.reshape(seq_at, (1,)).astype(jnp.int32)
            return tuple(finish(geo, layers, seq_arg, sums, *results, out_tokens, grad_tokens))

        def swap(array):
            pairs = [(at, at ^ 1) for at in range(clip_size)]
            return lax.ppermute(array, "clip", pairs)

        def spread(array):
            array = lax.psum_scatter(
                array.astype(b16), "seq", scatter_dimension=1, tiled=True
            ).astype(b16)
            return lax.psum_scatter(array, "clip", scatter_dimension=0, tiled=True).astype(f32)

        matrices = []
        for layer in range(layers):
            du, df_t, da_t, dq, dk, dv = results[6 * layer : 6 * layer + 6]
            keep = kept[layer]
            x_all = keep["xall"]
            into = [
                jnp.concatenate([jnp.where(core == 0, a, b), jnp.where(core == 0, b, a)], 1)
                for a, b in (
                    (dot_tn(x_all[: array.shape[0]], array), dot_tn(x_all[: array.shape[0]], swap(array)))
                    for array in (dq, dk, dv)
                )
            ]
            proj = jnp.zeros((CORES, half, width), f32)
            proj = lax.dynamic_update_slice_in_dim(proj, dot(da_t, keep["o"]).T[None], core, 0)
            up = jnp.zeros((2, CORES, width, quarter), f32)
            own_up = dot(keep["hrt"], du).reshape(width, 2, 1, quarter).transpose(1, 2, 0, 3)
            up = lax.dynamic_update_slice_in_dim(up, own_up, core, 1)
            down = jnp.zeros((2, CORES, quarter, width), f32)
            own_down = dot(df_t, keep["act"]).T.reshape(2, 1, quarter, width)
            down = lax.dynamic_update_slice_in_dim(down, own_down, core, 1)
            matrices.append((
                spread(jnp.concatenate(into, 1) * 0.5),
                spread(proj.reshape(width, width)),
                spread(up.transpose(2, 0, 1, 3).reshape(width, ffn)),
                spread(down.reshape(ffn, width)),
            ))
        halves = jnp.arange(SUMS)[None, :, None] >= OUT_BIAS
        summed = lax.psum(jnp.where(halves, 0.5 * sums, sums), ("clip", "seq"))

        def share(row, count):
            piece = summed[:, row : row + count].reshape(layers, count * width)
            size = count * width // seq_size
            return lax.dynamic_slice_in_dim(piece, seq_at * size, size, 1)

        into, proj, up, down = (
            jnp.stack([matrices[layer][which] for layer in range(layers)]) for which in range(4)
        )
        return (
            out_tokens, grad_tokens, into, share(QUERY_BIAS, 2), proj, share(OUT_BIAS, 1),
            up, share(UP_BIAS, 4), down, share(DOWN_BIAS, 1),
            jnp.stack([share(GAIN, 1), share(GAIN + 1, 1)], 1),
            jnp.stack([share(SHIFT, 1), share(SHIFT + 1, 1)], 1),
        )

    return shards


def solution(mesh):
    rowed = P("clip", "seq", None)
    in_specs = (rowed, P("clip")) + (P(),) * 10 + (rowed,)
    out_specs = (
        rowed,
        rowed,
        P(None, "clip", "seq"),
        P(None, "seq"),
        P(None, "clip", "seq"),
        P(None, "seq"),
        P(None, "clip", "seq"),
        P(None, "seq"),
        P(None, "clip", "seq"),
        P(None, "seq"),
        P(None, None, "seq"),
        P(None, None, "seq"),
    )
    return jax.shard_map(
        build(mesh), mesh=mesh, in_specs=in_specs, out_specs=out_specs, check_vma=False
    )
```

```python
from copy import copy as duplicate
import functools

import jax
import jax.numpy as jnp
from jax import lax
from jax.experimental import pallas as pl
from jax.experimental.pallas import tpu as pltpu
from jax.sharding import PartitionSpec as P

HEADS = 12
HEAD_DIM = 64
CORES = 2
LANES = 128
SCALE = HEAD_DIM**-0.5
SQRT_HALF = 0.5**0.5
GAUSS = 0.3989422804014327
LOG2E = 1.4426950408889634
EPS = 1e-05
VMEM = 56 * 1024 * 1024
VMEM_BACK = 63 * 1024 * 1024

f32 = jnp.float32
b16 = jnp.bfloat16


def dot(a, b):
    return lax.dot_general(a, b, (((1,), (0,)), ((), ())), preferred_element_type=f32)


def dot_nt(a, b):
    return lax.dot_general(a, b, (((1,), (1,)), ((), ())), preferred_element_type=f32)


def dot_tn(a, b):
    return lax.dot_general(a, b, (((0,), (0,)), ((), ())), preferred_element_type=f32)


def norm_parts(values):
    center = values - jnp.mean(values, -1, keepdims=True)
    inverse = lax.rsqrt(jnp.mean(center * center, -1, keepdims=True) + EPS)
    return center * inverse, inverse


def norm_back(unit, inverse, gain, grad):
    scaled = grad * gain
    mean_one = jnp.mean(scaled, -1, keepdims=True)
    mean_two = jnp.mean(scaled * unit, -1, keepdims=True)
    back = inverse * (scaled - mean_one - unit * mean_two)
    return back, jnp.sum(grad * unit, 0, keepdims=True), jnp.sum(grad, 0, keepdims=True)


def call(kernel, core, grid, ins, outs, scratch, flops, moved):
    in_specs = [pl.BlockSpec(block, lambda g, c, at=at: at(g, c[0])) for unused, block, at in ins]
    out_specs = [pl.BlockSpec(block, lambda g, c, at=at: at(g, c[0])) for s, d, block, at in outs]
    return pl.pallas_call(
        kernel,
        grid_spec=pltpu.PrefetchScalarGridSpec(
            num_scalar_prefetch=1,
            grid=(grid,),
            in_specs=in_specs,
            out_specs=out_specs,
            scratch_shapes=scratch,
        ),
        out_shape=[jax.ShapeDtypeStruct(shape, dtype) for shape, dtype, b, at in outs],
        compiler_params=pltpu.CompilerParams(
            dimension_semantics=("arbitrary",), vmem_limit_bytes=VMEM
        ),
        cost_estimate=pl.CostEstimate(flops=flops, bytes_accessed=moved, transcendentals=0),
    )(core, *[array for array, b, at in ins])


def all_of(array):
    zeros = (0,) * array.ndim
    return (array, array.shape, lambda g, c: zeros)


def full(shape, dtype):
    zeros = (0,) * len(shape)
    return (shape, dtype, shape, lambda g, c: zeros)


class Geometry:
    def __init__(self, mesh, tokens, ffn):
        self.clip_size, self.seq_size = mesh.shape["clip"], mesh.shape["seq"]
        self.columns = self.clip_size // CORES
        self.held, self.slots, self.width = tokens.shape
        self.ffn = ffn
        self.posts = self.held * CORES
        self.lines = self.seq_size // self.posts
        self.tile = CORES * self.slots
        self.rows = self.held * self.tile
        self.count = self.rows * self.lines
        self.half = self.width // CORES
        self.pairs = self.half // LANES
        self.heads = 2 * self.pairs
        self.quarter = ffn // 4
        self.depth = self.width // self.clip_size
        self.aligned = self.columns == 2 and (ffn // self.seq_size) % LANES == 0

    def locate(self):
        self.clip = lax.axis_index("clip")
        self.seq = lax.axis_index("seq")
        self.core = self.clip % CORES
        self.column = self.clip // CORES
        self.post = self.seq // self.lines
        self.line = self.seq % self.lines
        self.parity = self.post % self.held

    def sibling(self):
        return self.clip + 1 - 2 * self.core, self.seq

    def on_line(self, shift):
        return self.clip, self.post * self.lines + (self.line + shift) % self.lines

    def on_post(self, shift):
        return self.clip, (self.post + shift) % self.posts * self.lines + self.line

    def on_column(self, shift):
        return (self.column + shift) % self.columns * CORES + self.core, self.seq

    def goal(self, turn):
        post = self.held * self.core + (self.post + turn) % self.held
        return self.column * CORES + self.post // self.held, post * self.lines + self.line

    def origin(self, turn, who):
        post = self.held * who + (self.parity + turn) % self.held
        return self.column * CORES + self.post // self.held, post * self.lines + self.line

    def blocked(self, turn):
        return jnp.logical_and(self.post // self.held == self.core, turn == 0)


def remote(source, target, send, receive, device):
    return pltpu.make_async_remote_copy(
        src_ref=source, dst_ref=target, send_sem=send, recv_sem=receive,
        device_id=device, device_id_type=pl.DeviceIdType.MESH,
    )


def meet(geo, devices):
    barrier = pltpu.get_barrier_semaphore()
    total = 0
    for device in devices:
        other = jnp.logical_or(device[0] != geo.clip, device[1] != geo.seq)

        @pl.when(other)
        def greet(device=device):
            pl.semaphore_signal(
                barrier, inc=1, device_id=device, device_id_type=pl.DeviceIdType.MESH
            )

        total = total + other.astype(jnp.int32)
    pl.semaphore_wait(barrier, total)


def loop(count, body):
    def step(at, carry):
        body(at)
        return carry

    lax.fori_loop(0, count, step, 0)


def gelu_parts(inner):
    bell = jnp.exp2((inner * inner) * (-0.5 * LOG2E))
    denominator = 1.0 + (0.3275911 * SQRT_HALF) * jnp.abs(inner)
    t = pl.reciprocal(denominator, approx=True)
    t = t * (2.0 - denominator * t)
    series = t * (0.5 * 0.254829592 + t * (0.5 * -0.284496736 + t * (
        0.5 * 1.421413741 + t * (0.5 * -1.453152027 + t * (0.5 * 1.061405429)))))
    tail = series * bell
    phi = jnp.where(inner >= 0.0, 1.0 - tail, tail)
    return phi, phi + inner * (GAUSS * bell)


KEPT = ("xall", "kx", "v", "q", "ot", "lse", "o", "z1", "hrt", "act", "slope", "z2")


def kept_shapes(geo):
    rows, width, half, count = geo.rows, geo.width, geo.half, geo.count
    return {
        "xall": ((count, width), b16),
        "kx": ((geo.pairs, count, 2 * LANES), b16),
        "v": ((count, half), b16),
        "q": ((rows, half), b16),
        "ot": ((half, rows), f32),
        "lse": ((geo.heads, 8, rows), f32),
        "o": ((rows, half), b16),
        "z1": ((rows, width), f32),
        "hrt": ((width, rows), b16),
        "act": ((rows, geo.ffn // CORES), b16),
        "slope": ((rows, geo.ffn // CORES), b16),
        "z2": ((rows, width), f32),
    }


def forward_kernel(geo, layers, *refs):
    refs = list(refs)

    def take(count):
        taken = refs[:count]
        del refs[:count]
        return taken

    tokens, cotangent, w_in, w_out, w_up, w_down = take(6)
    lengths, in_bias, out_bias, up_bias, down_bias, gains, shifts = take(7)
    out_tokens, cot_rows = take(2)
    stored = [dict(zip(KEPT, take(len(KEPT)))) for unused in range(layers)]
    kept = [dict(zip(KEPT, take(len(KEPT)))) for unused in range(layers)]
    win, wout, wup, wdown = take(4)
    qx, vt, state, hidden, low_out, lens, lens_there, psend, precv, running = take(10)
    (load_sem, save_sem, tok_sem, tok_send, tok_recv, cot_sem, cot_send, cot_recv, sib_send,
     sib_recv, line_send, line_recv, pass_send, pass_recv, part_send, part_recv, out_sem,
     out_send, out_recv, len_sem) = take(20)

    geo = duplicate(geo)
    geo.locate()
    core, tile, slots = geo.core, geo.tile, geo.slots
    held, lines, rows, width, half = geo.held, geo.lines, geo.rows, geo.width, geo.half
    quarter, pairs = geo.quarter, geo.pairs
    sibling = geo.sibling()

    loads = []
    for layer in range(layers):
        parts = [
            (w_in.at[layer, :, pl.ds(pl.multiple_of((kind * CORES + core) * half, half), half)],
             win.at[layer, kind])
            for kind in range(3)
        ]
        parts.append((w_out.at[layer, pl.ds(pl.multiple_of(core * half, half), half), :], wout.at[layer]))
        for block in range(2):
            at = pl.ds(pl.multiple_of((2 * block + core) * quarter, quarter), quarter)
            parts.append((w_up.at[layer, :, at], wup.at[layer, block]))
            parts.append((w_down.at[layer, at, :], wdown.at[layer, block]))
        loads.append([
            pltpu.make_async_copy(source, target, load_sem.at[layer, at])
            for at, (source, target) in enumerate(parts)
        ])
    for copy in loads[0]:
        copy.start()

    sources = [geo.origin(turn, who) for turn in range(held) for who in range(CORES)]
    goals = [geo.goal(turn) for turn in range(held)]
    goals = goals + [(device[0] + 1 - 2 * (device[0] % CORES), device[1]) for device in goals]
    near = [sibling] + [geo.on_line(shift) for shift in range(1, lines)]
    meet(geo, near + sources + goals)

    first = kept[0]["xall"]

    def block_at(turn, who, shift=0):
        start = shift * rows + turn * tile + who * slots
        return pl.ds(start if isinstance(start, int) else pl.multiple_of(start, slots), slots)

    def token_copies(turn, who):
        mine = tokens.at[(geo.post + turn) % held]
        place = first.at[block_at(turn, who)]
        own = pltpu.make_async_copy(mine, place, tok_sem.at[turn])
        return own, remote(mine, place, tok_send.at[turn], tok_recv.at[turn], geo.goal(turn))

    def token_start(turn):
        own, there = token_copies(turn, geo.post // held)
        pl.when(geo.blocked(turn))(own.start)
        pl.when(jnp.logical_not(geo.blocked(turn)))(there.start)

    def token_wait(turn):
        own, there = token_copies(turn, core)
        pl.when(geo.blocked(turn))(own.wait)
        pl.when(jnp.logical_not(geo.blocked(turn)))(there.wait)

    def to_sibling(array, turn, who, shift, send, receive):
        place = array.at[block_at(turn, who, shift)]
        return remote(place, place, send, receive, sibling)

    def to_line(layer, turn, shift):
        array = kept[layer]["xall"]
        source = array.at[block_at(turn, core)]
        target = array.at[block_at(turn, core, shift)]
        return remote(
            source, target, line_send.at[layer, turn, shift - 1], line_recv.at[layer, turn, shift - 1],
            geo.on_line(shift),
        )

    for turn in range(held):
        token_start(turn)
    clip_row = lax.broadcasted_iota(jnp.int32, lens.shape, 0)
    filled = jnp.full(lens.shape, lengths[0], jnp.int32)
    for clip in range(1, held):
        filled = jnp.where(clip_row == clip, lengths[clip], filled)
    lens[...] = filled
    len_copy = remote(lens, lens_there, len_sem.at[0], len_sem.at[1], sibling)
    len_copy.start()

    def clear(at):
        qx[at] = jnp.zeros(qx.shape[1:], b16)
        qx[at, LANES : LANES + 16, :] = (
            lax.broadcasted_iota(jnp.int32, (16, rows), 0) == 0
        ).astype(f32).astype(b16)

    loop(geo.heads, clear)
    len_copy.wait()
    known = jnp.where(geo.post // held == core, lens[...], lens_there[...])
    length = known[0:1, :]
    for clip in range(1, held):
        length = jnp.where(geo.parity == clip, known[clip : clip + 1, :], length)
    lane = lax.broadcasted_iota(jnp.int32, (slots, LANES), 1)
    slot = lax.broadcasted_iota(jnp.int32, (slots, LANES), 0)
    for shift in range(lines):
        for turn in range(held):
            for who in range(CORES):
                post = held * who + (geo.parity + turn) % held
                line = (geo.line + lines - shift) % lines
                outside = (post * lines + line) * slots + slot >= length
                mask = jnp.where(jnp.logical_and(lane == 0, outside), -1e30, 0.0).astype(b16)
                for layer in range(layers):
                    for pair in range(pairs):
                        kept[layer]["kx"][pair, block_at(turn, who, shift), LANES:] = mask

    for turn in range(held):
        token_wait(turn)
        to_sibling(first, turn, core, 0, sib_send.at[turn], sib_recv.at[turn]).start()
        for shift in range(1, lines):
            to_line(0, turn, shift).start()
    for copy in loads[0]:
        copy.wait()
    for copy in loads[1]:
        copy.start()

    def cot_copies(turn, flip):
        mine = cotangent.at[(geo.post + turn) % held]
        place = cot_rows.at[block_at(turn, geo.post // held)]
        goal = geo.goal(turn)
        if flip:
            goal = (goal[0] + 1 - 2 * (goal[0] % CORES), goal[1])
        own = pltpu.make_async_copy(mine, place, cot_sem.at[turn, flip])
        there = remote(
            mine, place, cot_send.at[turn, flip], cot_recv.at[turn, geo.post // held], goal
        )
        here = jnp.logical_and(goal[0] == geo.clip, goal[1] == geo.seq)
        return own, there, here

    def cot_start():
        for turn in range(held):
            for flip in range(CORES):
                own, there, here = cot_copies(turn, flip)
                pl.when(here)(own.start)
                pl.when(jnp.logical_not(here))(there.start)

    def cot_wait():
        for turn in range(held):
            for flip in range(CORES):
                own, there, here = cot_copies(turn, flip)
                pl.when(here)(own.wait)
                pl.when(jnp.logical_not(here))(there.wait_send)
            for who in range(CORES):
                source = geo.origin(turn, who)
                place = cot_rows.at[block_at(turn, who)]
                there = remote(
                    cotangent.at[0], place, cot_send.at[turn, 0], cot_recv.at[turn, who], source
                )
                here = jnp.logical_and(source[0] == geo.clip, source[1] == geo.seq)
                pl.when(jnp.logical_not(here))(there.wait_recv)

    def key_tile(layer, at):
        keep = kept[layer]
        now = pl.ds(pl.multiple_of(at, tile), tile)
        x = keep["xall"][now, :]
        key = dot(x, win[layer, 1]).astype(b16)
        for pair in range(pairs):
            keep["kx"][pair, now, :LANES] = key[:, pair * LANES : (pair + 1) * LANES]
        bias = in_bias[layer : layer + 1, pl.ds(pl.multiple_of(width + core * half, half), half)]
        value = (dot(x, win[layer, 2]) + bias).astype(b16)
        keep["v"][now, :] = value
        vt[:, now] = value.astype(f32).T.astype(b16)

    def query_tile(layer, at):
        keep = kept[layer]
        now = pl.ds(pl.multiple_of(at, tile), tile)
        bias = in_bias[layer : layer + 1, pl.ds(pl.multiple_of(core * half, half), half)]
        query = (dot(keep["xall"][now, :], win[layer, 0]) + bias).astype(b16)
        query = (query * SCALE).astype(b16)
        keep["q"][now, :] = query
        turned = query.astype(f32).T.astype(b16)
        for head in range(geo.heads):
            inside = head % 2 * HEAD_DIM
            qx[head, inside : inside + HEAD_DIM, now] = (
                turned[head * HEAD_DIM : (head + 1) * HEAD_DIM]
            )

    def attend_block(layer, shift, turn):
        keep = kept[layer]
        now = pl.ds(pl.multiple_of(turn * tile, tile), tile)
        span = slice(shift * rows, (shift + 1) * rows)

        size = min(256, rows)
        cuts = [slice(start, start + size) for start in range(shift * rows, (shift + 1) * rows, size)]

        def pair_step(pair):
            heads = [2 * pair, 2 * pair + 1]
            scores = [
                [dot(keep["kx"][pair, cut, :], qx[head, :, now]) for cut in cuts] for head in heads
            ]
            for head, pieces in zip(heads, scores):
                here = pl.ds(pl.multiple_of(head * HEAD_DIM, HEAD_DIM), HEAD_DIM)
                top = functools.reduce(
                    jnp.maximum, [jnp.max(piece, 0, keepdims=True) for piece in pieces]
                )
                if shift > 0:
                    before = keep["lse"][head, 0:1, now]
                    top = jnp.maximum(top, before)
                    shrink = jnp.exp(before - top)
                total = attended = None
                for piece, cut in zip(pieces, cuts):
                    weights = jnp.exp(piece - top)
                    sums = jnp.sum(weights, 0, keepdims=True)
                    values = dot(vt[here, cut], weights.astype(b16))
                    total = sums if total is None else total + sums
                    attended = values if attended is None else attended + values
                if shift > 0:
                    total = total + shrink * running[head, 0:1, now]
                    attended = attended + shrink * keep["ot"][here, now]
                if shift < lines - 1:
                    running[head, 0:1, now] = total
                    keep["ot"][here, now] = attended
                    keep["lse"][head, 0:1, now] = top
                else:
                    keep["ot"][here, now] = attended / total
                    keep["lse"][head, 0:1, now] = top + jnp.log(total)

        loop(pairs, pair_step)

    def project_tile(layer, turn):
        keep = kept[layer]
        now = pl.ds(pl.multiple_of(turn * tile, tile), tile)
        attended = keep["ot"][:, now].T.astype(b16)
        keep["o"][now, :] = attended
        share(2 * layer, turn, dot(attended, wout[layer]))

    def part_copy(which, turn):
        now = pl.ds(pl.multiple_of(turn * tile, tile), tile)
        return remote(
            psend.at[which, now, :], precv.at[which, now, :], part_send.at[which, turn],
            part_recv.at[which, turn], sibling,
        )

    def share(which, turn, part):
        now = pl.ds(pl.multiple_of(turn * tile, tile), tile)
        psend[which, now, :] = part.astype(b16)
        part_copy(which, turn).start()

    def collect(which, turn):
        now = pl.ds(pl.multiple_of(turn * tile, tile), tile)
        part_copy(which, turn).wait()
        return psend[which, now, :].astype(f32) + precv[which, now, :].astype(f32)

    def feed_tile(layer, turn):
        keep = kept[layer]
        now = pl.ds(pl.multiple_of(turn * tile, tile), tile)
        x = first[now, :].astype(f32) if layer == 0 else state[now, :]
        summed = x + collect(2 * layer, turn) + out_bias[layer : layer + 1, :]
        keep["z1"][now, :] = summed
        unit, unused = norm_parts(summed)
        normal = unit * gains[layer, 0:1, :] + shifts[layer, 0:1, :]
        hidden[now, :] = normal
        low = normal.astype(b16)
        keep["hrt"][:, now] = low.astype(f32).T.astype(b16)
        size = min(256, quarter)
        total = None
        for block in range(2):
            for start in range(0, quarter, size):
                at = block * quarter + start
                bias = up_bias[
                    layer : layer + 1,
                    pl.ds(pl.multiple_of((2 * block + core) * quarter + start, size), size),
                ]
                inner = dot(low, wup[layer, block, :, start : start + size]) + bias
                phi, slope = gelu_parts(inner)
                active = (inner * phi).astype(b16)
                keep["act"][now, at : at + size] = active
                keep["slope"][now, at : at + size] = slope.astype(b16)
            part = dot(keep["act"][now, block * quarter : (block + 1) * quarter], wdown[layer, block])
            total = part if total is None else total + part
        share(2 * layer + 1, turn, total)

    def norm_tile(layer, turn):
        keep = kept[layer]
        now = pl.ds(pl.multiple_of(turn * tile, tile), tile)
        summed = hidden[now, :] + collect(2 * layer + 1, turn) + down_bias[layer : layer + 1, :]
        keep["z2"][now, :] = summed
        unit, unused = norm_parts(summed)
        result = unit * gains[layer, 1:2, :] + shifts[layer, 1:2, :]
        if layer < layers - 1:
            state[now, :] = result
            kept[layer + 1]["xall"][now, :] = result.astype(b16)
        else:
            low_out[now, :] = result.astype(b16)

    saves = []

    def save(layer, names):
        for name in names:
            copy = pltpu.make_async_copy(
                kept[layer][name], stored[layer][name], save_sem.at[layer, KEPT.index(name)]
            )
            copy.start()
            saves.append(copy)

    for layer in range(layers):
        x_all = kept[layer]["xall"]
        if layer == 0:
            for turn in range(held):
                to_sibling(x_all, turn, core, 0, sib_send.at[turn], sib_recv.at[turn]).wait_send()
                to_sibling(x_all, turn, 1 - core, 0, sib_send.at[turn], sib_recv.at[turn]).wait_recv()
                key_tile(layer, turn * tile)
                query_tile(layer, turn * tile)
        else:
            for copy in loads[layer]:
                copy.wait()

            def own_tile(turn):
                key_tile(layer, turn * tile)
                query_tile(layer, turn * tile)

            loop(held, own_tile)
        for shift in range(lines):
            if shift > 0:
                for turn in range(held):
                    to_line(layer, turn, shift).wait()
                    to_sibling(
                        x_all, turn, core, shift,
                        pass_send.at[layer, turn, shift - 1], pass_recv.at[layer, turn, shift - 1],
                    ).start()
                for turn in range(held):
                    send = pass_send.at[layer, turn, shift - 1]
                    receive = pass_recv.at[layer, turn, shift - 1]
                    to_sibling(x_all, turn, core, shift, send, receive).wait_send()
                    to_sibling(x_all, turn, 1 - core, shift, send, receive).wait_recv()
                    key_tile(layer, shift * rows + turn * tile)
            if shift == lines - 1:
                save(layer, ("xall", "kx", "v", "q"))
                if layer == 0:
                    cot_start()

            def turn_step(turn):
                attend_block(layer, shift, turn)
                if shift == lines - 1:
                    project_tile(layer, turn)

            loop(held, turn_step)
        save(layer, ("ot", "lse", "o"))
        loop(held, functools.partial(feed_tile, layer))
        save(layer, ("z1", "hrt", "act", "slope"))
        for turn in range(held):
            norm_tile(layer, turn)
            if layer < layers - 1:
                for shift in range(1, lines):
                    to_line(layer + 1, turn, shift).start()
        save(layer, ("z2",))

    def out_copies(turn, place):
        mine = low_out.at[block_at(turn, core)]
        own = pltpu.make_async_copy(mine, place, out_sem.at[turn])
        return own, remote(mine, place, out_send.at[turn], out_recv.at[turn], geo.origin(turn, core))

    for turn in range(held):
        own, there = out_copies(turn, out_tokens.at[geo.parity])
        pl.when(geo.blocked(turn))(own.start)
        pl.when(jnp.logical_not(geo.blocked(turn)))(there.start)
    cot_wait()
    for turn in range(held):
        own, there = out_copies(turn, out_tokens.at[(geo.post + turn) % held])
        pl.when(geo.blocked(turn))(own.wait)
        pl.when(jnp.logical_not(geo.blocked(turn)))(there.wait)
    for copy in saves:
        copy.wait()


def forward(geo, layers, tokens, cotangent, lengths, weights, vectors):
    width, rows, half, ffn = geo.width, geo.rows, geo.half, geo.ffn
    shapes = kept_shapes(geo)
    any_spec = pl.BlockSpec(memory_space=pl.ANY)
    vmem_spec = pl.BlockSpec(memory_space=pltpu.VMEM)
    out_shape = [
        jax.ShapeDtypeStruct(tokens.shape, b16),
        jax.ShapeDtypeStruct((rows, width), b16),
    ]
    out_shape += [jax.ShapeDtypeStruct(*shapes[name]) for unused in range(layers) for name in KEPT]
    scratch = [pltpu.VMEM(*shapes[name]) for unused in range(layers) for name in KEPT]
    scratch += [
        pltpu.VMEM((layers, 3, width, half), b16),
        pltpu.VMEM((layers, half, width), b16),
        pltpu.VMEM((layers, 2, width, geo.quarter), b16),
        pltpu.VMEM((layers, 2, geo.quarter, width), b16),
        pltpu.VMEM((geo.heads, 2 * LANES, rows), b16),
        pltpu.VMEM((half, geo.count), b16),
        pltpu.VMEM((rows, width), f32),
        pltpu.VMEM((rows, width), f32),
        pltpu.VMEM((rows, width), b16),
        pltpu.VMEM((8, LANES), jnp.int32),
        pltpu.VMEM((8, LANES), jnp.int32),
        pltpu.VMEM((2 * layers, rows, width), b16),
        pltpu.VMEM((2 * layers, rows, width), b16),
        pltpu.VMEM((geo.heads, 8, rows), f32),
    ]
    held, lines = geo.held, max(geo.lines - 1, 1)
    dma = pltpu.SemaphoreType.DMA
    scratch += [dma(shape) for shape in (
        (layers, 8), (layers, len(KEPT)), (held,), (held,), (held,),
        (held, CORES), (held, CORES), (held, CORES), (held,), (held,),
        (layers, held, lines), (layers, held, lines), (layers, held, lines), (layers, held, lines),
        (2 * layers, held), (2 * layers, held), (held,), (held,), (held,), (2,),
    )]
    results = pl.pallas_call(
        functools.partial(forward_kernel, geo, layers),
        out_shape=out_shape,
        in_specs=[any_spec] * 6 + [pl.BlockSpec(memory_space=pltpu.SMEM)] + [vmem_spec] * 6,
        out_specs=[any_spec] * len(out_shape),
        scratch_shapes=scratch,
        compiler_params=pltpu.CompilerParams(
            collective_id=0, has_side_effects=True, vmem_limit_bytes=VMEM
        ),
        cost_estimate=pl.CostEstimate(flops=3 * 10**10, bytes_accessed=4 * 10**7, transcendentals=0),
    )(tokens, cotangent, *weights, lengths, *vectors)
    count = len(KEPT)
    kept = [
        dict(zip(KEPT, results[2 + layer * count : 2 + (layer + 1) * count]))
        for layer in range(layers)
    ]
    return results[0], results[1], kept


QUERY_BIAS, VALUE_BIAS, UP_BIAS, OUT_BIAS, DOWN_BIAS, GAIN, SHIFT = 0, 1, 2, 6, 7, 8, 10
SUMS = 16
UP, DOWN = 0, 1
INTO, PROJ = 0, 1
PAIRS = ("pair0", "pair1", "pair2")


def backward_kernel(geo, layers, *refs):
    refs = list(refs)

    def take(count):
        taken = refs[:count]
        del refs[:count]
        return taken

    cot_rows, w_in, w_out, w_up, w_down = take(5)
    stored = [dict(zip(KEPT, take(len(KEPT)))) for unused in range(layers)]
    (gains,) = take(1)
    grad_tokens, sums = take(2)
    if geo.aligned:
        feed_out, attend_out = take(2)
    else:
        plain = [take(6) for unused in range(layers)]
    keep = dict(zip(KEPT, take(len(KEPT))))
    win, wout, wup, wdown = take(4)
    (o_there, low_grad, turned, du_there, psend, precv, do, qx, dox, dq, dk, dv, dq_there,
     dk_there, dv_there, probs_all, grads_all, do_stack, q_stack, dqt, mine_dx, dx_send, dx_recv, line_in) = take(24)
    (load_sem, o_send, o_recv, du_send, du_recv, part_send, part_recv, qkv_send, qkv_recv,
     dx_ssem, dx_rsem, line_send, line_recv, more_send, more_recv, tok_sem, tok_send,
     tok_recv, plain_sem) = take(19)
    if geo.aligned:
        (other, mine, from_x, from_y, from_z, into_cell, proj_cell, into_y, proj_y, into_z, proj_z,
         a_send, a_x, sum_in) = take(14)
        cells = [[into_cell] * layers, [proj_cell.at[layer] for layer in range(layers)]]
        cells_y, cells_z = (into_y, proj_y), (into_z, proj_z)
        (fx_send, fx_recv, fy_send, fy_recv, fz_send, fz_recv, ay_send, ay_recv, az_send, az_recv,
         ax_send, ax_recv, sum_send, sum_recv) = take(14)
        (credit,) = take(1)

    geo = duplicate(geo)
    geo.locate()
    core, tile, slots = geo.core, geo.tile, geo.slots
    held, lines, rows, width, half = geo.held, geo.lines, geo.rows, geo.width, geo.half
    quarter, pairs, posts, depth = geo.quarter, geo.pairs, geo.posts, geo.depth
    post, line, column = geo.post, geo.line, geo.column
    unit = width // geo.seq_size
    sibling = geo.sibling()

    def tile_at(turn):
        return pl.ds(pl.multiple_of(turn * tile, tile), tile)

    def block_at(turn, who, shift=0):
        start = shift * rows + turn * tile + who * slots
        return pl.ds(start if isinstance(start, int) else pl.multiple_of(start, slots), slots)

    NAMES = KEPT + ("win", "wout", "wup", "wdown", "cot")

    def load_copies(layer, name):
        where = load_sem.at[layer, NAMES.index(name)]
        if name == "win":
            return [
                pltpu.make_async_copy(
                    w_in.at[layer, :, pl.ds(pl.multiple_of((kind * CORES + core) * half, half), half)],
                    win.at[kind], load_sem.at[layer, len(NAMES) + kind],
                )
                for kind in range(3)
            ]
        if name == "wout":
            at = pl.ds(pl.multiple_of(core * half, half), half)
            return [pltpu.make_async_copy(w_out.at[layer, at, :], wout, where)]
        if name in ("wup", "wdown"):
            copies = []
            for block in range(2):
                at = pl.ds(pl.multiple_of((2 * block + core) * quarter, quarter), quarter)
                slot = len(NAMES) + 3 + 2 * (name == "wdown") + block
                if name == "wup":
                    pair = w_up.at[layer, :, at], wup.at[block]
                else:
                    pair = w_down.at[layer, at, :], wdown.at[block]
                copies.append(pltpu.make_async_copy(*pair, load_sem.at[layer, slot]))
            return copies
        if name == "hrt" and geo.aligned:
            return [
                pltpu.make_async_copy(
                    stored[layer][name].at[pl.ds(pl.multiple_of((2 * which + core) * depth, depth), depth), :],
                    keep[name].at[which * depth : (which + 1) * depth, :],
                    load_sem.at[layer, len(NAMES) + 7 + which],
                )
                for which in range(2)
            ]
        if name == "cot":
            return [pltpu.make_async_copy(cot_rows, low_grad, where)]
        return [pltpu.make_async_copy(stored[layer][name], keep[name], where)]

    def load(layer, *names):
        for name in names:
            for copy in load_copies(layer, name):
                copy.start()

    def loaded(layer, *names):
        for name in names:
            for copy in load_copies(layer, name):
                copy.wait()

    top = layers - 1
    load(top, "z2", "cot", "wdown", "slope", "wup", "act", "z1", "wout", "q", "kx", "v", "ot",
         "lse", "win", "hrt", "xall", "o")

    sources = [geo.origin(turn, who) for turn in range(held) for who in range(CORES)]
    goals = [geo.goal(turn) for turn in range(held)]
    near = [sibling] + [geo.on_line(shift) for shift in range(1, lines)]
    if geo.aligned:
        near += [geo.on_post(shift) for shift in range(1, posts)]
        near += [geo.on_column(shift) for shift in range(1, geo.columns)]
    goals = goals + [(device[0] + 1 - 2 * (device[0] % CORES), device[1]) for device in goals]
    meet(geo, near + sources + goals)

    def o_copy(layer):
        return remote(stored[layer]["o"], o_there, o_send.at[layer], o_recv.at[layer], sibling)

    def clear(at):
        qx[at] = jnp.zeros(qx.shape[1:], b16)
        qx[at, LANES : LANES + 16, :] = (
            lax.broadcasted_iota(jnp.int32, (16, rows), 0) == 0
        ).astype(f32).astype(b16)
        dox[at] = jnp.zeros(dox.shape[1:], b16)

    loop(2, clear)
    sums[...] = jnp.zeros_like(sums)

    def add_sum(layer, row, lanes, value):
        sums[layer, pl.ds(row, 1), lanes] += value

    everywhere = slice(None)


    def x_copy(layer, kind, z):
        return remote(
            other.at[kind, z], from_x.at[kind, z], fx_send.at[layer, kind, z],
            fx_recv.at[layer, kind, z], geo.on_column(1),
        )

    def y_copy(layer, kind, z, shift):
        return remote(
            mine.at[layer, kind, z, (line + shift) % lines], from_y.at[layer, kind, z, shift - 1],
            fy_send.at[layer, kind, z, shift - 1], fy_recv.at[layer, kind, z, shift - 1],
            geo.on_line(shift),
        )

    def z_copy(layer, kind, shift):
        return remote(
            mine.at[layer, kind, (post + shift) % posts, line], from_z.at[layer, kind, shift - 1],
            fz_send.at[layer, kind, shift - 1], fz_recv.at[layer, kind, shift - 1],
            geo.on_post(shift),
        )

    def order(step):
        return (post + step + 1) % posts

    def land_x(layer, kind, step):
        z = order(step)
        x_copy(layer, kind, z).wait()
        total = mine[layer, kind, z].astype(f32) + from_x[kind, z].astype(f32)
        mine[layer, kind, z] = total.astype(b16)
        for shift in range(1, lines):
            y_copy(layer, kind, z, shift).start()
        if layer > 0 and step == posts - 1:
            device = geo.on_column(1)
            pl.semaphore_signal(
                credit.at[kind], inc=1, device_id=device, device_id_type=pl.DeviceIdType.MESH
            )

    def land_y(layer, kind, step):
        z = order(step)
        total = mine[layer, kind, z, line].astype(f32)
        for shift in range(1, lines):
            y_copy(layer, kind, z, shift).wait()
            total = total + from_y[layer, kind, z, shift - 1].astype(f32)
        mine[layer, kind, z, line] = total.astype(b16)
        if step + 1 < posts:
            z_copy(layer, kind, step + 1).start()

    def land_z(layer, kind):
        total = mine[layer, kind, post, line].astype(f32)
        for shift in range(1, posts):
            z_copy(layer, kind, shift).wait()
            total = total + from_z[layer, kind, shift - 1].astype(f32)
        feed_out[layer, kind] = total

    def ay_copy(layer, kind, z, shift):
        return remote(
            cells[kind][layer].at[(line + shift) % lines, z], cells_y[kind].at[layer, z, shift - 1],
            ay_send.at[layer, kind, z, shift - 1], ay_recv.at[layer, kind, z, shift - 1],
            geo.on_line(shift),
        )

    def az_copy(layer, kind, shift):
        return remote(
            cells[kind][layer].at[line, (post + shift) % posts], cells_z[kind].at[layer, shift - 1],
            az_send.at[layer, kind, shift - 1], az_recv.at[layer, kind, shift - 1],
            geo.on_post(shift),
        )

    def ax_copy(layer, kind):
        span = slice(0, 3 * unit) if kind == INTO else slice(3 * unit, 4 * unit)
        return remote(
            a_send.at[layer, span], a_x.at[layer, span], ax_send.at[layer, kind],
            ax_recv.at[layer, kind], geo.on_column(1),
        )

    def send_ay(layer, kind):
        for step in range(posts):
            for shift in range(1, lines):
                ay_copy(layer, kind, order(step), shift).start()

    def land_ay(layer, kind, step):
        z = order(step)
        cell = cells[kind][layer]
        total = cell[line, z].astype(f32)
        for shift in range(1, lines):
            ay_copy(layer, kind, z, shift).wait()
            total = total + cells_y[kind][layer, z, shift - 1].astype(f32)
        cell[line, z] = total.astype(b16)
        if step + 1 < posts:
            az_copy(layer, kind, step + 1).start()

    def land_az(layer, kind):
        total = cells[kind][layer][line, post].astype(f32)
        for shift in range(1, posts):
            az_copy(layer, kind, shift).wait()
            total = total + cells_z[kind][layer, shift - 1].astype(f32)
        low, high = total[:, :depth], total[:, depth:]
        span = slice(0, 3 * unit) if kind == INTO else slice(3 * unit, 4 * unit)
        attend_out[layer, span] = jnp.where(column == 0, low, high)
        a_send[layer, span] = jnp.where(column == 0, high, low).astype(b16)
        ax_copy(layer, kind).start()

    def land_ax(layer, kind):
        ax_copy(layer, kind).wait()
        span = slice(0, 3 * unit) if kind == INTO else slice(3 * unit, 4 * unit)
        attend_out[layer, span] = attend_out[layer, span] + a_x[layer, span].astype(f32)

    def sum_copies(layer, hop):
        near = ([sibling], [geo.on_line(shift) for shift in range(1, lines)],
                [geo.on_post(shift) for shift in range(1, posts)], [geo.on_column(1)])
        first = (0, 1, lines, lines + posts - 1)[hop]
        return [
            (remote(
                sums.at[layer], sum_in.at[layer, first + at], sum_send.at[layer, first + at],
                sum_recv.at[layer, first + at], device,
            ), first + at)
            for at, device in enumerate(near[hop])
        ]

    def start_sum(layer):
        shared = lax.broadcasted_iota(jnp.int32, sums.shape[1:], 0) >= OUT_BIAS
        sums[layer] = jnp.where(shared, 0.5 * sums[layer], sums[layer])
        for copy, unused in sum_copies(layer, 0):
            copy.start()

    def land_sum(layer, hop):
        total = sums[layer]
        for copy, at in sum_copies(layer, hop):
            copy.wait()
            total = total + sum_in[layer, at]
        sums[layer] = total
        if hop < 3:
            for copy, unused in sum_copies(layer, hop + 1):
                copy.start()

    schedule = {
        (1, "pair0"): (
            (land_x, 1, DOWN, 0), (land_ay, 1, PROJ, 0), (land_ay, 1, PROJ, 1),
        ),
        (1, "pair1"): (
            (land_ay, 1, PROJ, 2), (land_x, 1, DOWN, 1), (land_ay, 1, PROJ, 3),
            (land_y, 1, DOWN, 0),
        ),
        (1, "up"): (
            (land_x, 1, DOWN, 2),
        ),
        (1, "pair2"): (
            (land_az, 1, PROJ), (land_y, 1, DOWN, 1), (land_x, 1, DOWN, 3), (land_y, 1, DOWN, 2),
        ),
        (1, "own"): (
            (land_x, 1, UP, 0), (land_y, 1, DOWN, 3), (land_sum, 1, 0),
        ),
        (1, "into"): (
            (land_z, 1, DOWN), (land_x, 1, UP, 1),
        ),
        (0, "feed"): (
            (land_x, 1, UP, 2), (land_y, 1, UP, 0), (land_sum, 1, 1), (land_x, 1, UP, 3),
            (land_ax, 1, PROJ),
        ),
        (0, "down"): (
            (land_ay, 1, INTO, 0),
        ),
        (0, "up"): (
            (land_ay, 1, INTO, 1),
        ),
        (0, "proj"): (
            (land_ay, 1, INTO, 2),
        ),
        (0, "pair0"): (
            (land_sum, 1, 2), (land_x, 0, DOWN, 0), (land_ay, 1, INTO, 3), (land_x, 0, DOWN, 1),
            (land_y, 1, UP, 1),
        ),
        (0, "pair1"): (
            (land_y, 1, UP, 2), (land_x, 0, DOWN, 2), (land_y, 1, UP, 3), (land_ay, 0, PROJ, 0),
        ),
        (0, "pair2"): (
            (land_ay, 0, PROJ, 1), (land_ay, 0, PROJ, 2), (land_az, 1, INTO),
            (land_ay, 0, PROJ, 3), (land_x, 0, DOWN, 3),
        ),
        (0, "dx"): (
            (land_y, 0, DOWN, 0),
        ),
        (0, "own"): (
            (land_y, 0, DOWN, 1), (land_x, 0, UP, 0), (land_z, 1, UP), (land_y, 0, DOWN, 2),
            (land_sum, 0, 0),
        ),
        (0, "into"): (
            (land_y, 0, DOWN, 3), (land_x, 0, UP, 1), (land_az, 0, PROJ),
        ),
        (0, "end"): (
            (land_x, 0, UP, 2), (land_y, 0, UP, 0), (land_x, 0, UP, 3), (land_sum, 0, 1),
            (land_sum, 1, 3), (land_z, 0, DOWN), (land_ax, 1, INTO), (land_ax, 0, PROJ),
            (land_ay, 0, INTO, 0), (land_ay, 0, INTO, 1), (land_ay, 0, INTO, 2),
            (land_sum, 0, 2), (land_ay, 0, INTO, 3), (land_sum, 0, 3), (land_y, 0, UP, 1),
            (land_y, 0, UP, 2), (land_y, 0, UP, 3), (land_az, 0, INTO), (land_ax, 0, INTO),
            (land_z, 0, UP),
        ),
    }

    def progress(layer, phase):
        if geo.aligned:
            for function, *given in schedule.get((layer, phase), ()):
                function(*given)


    def part_copy(layer, turn):
        return remote(
            psend.at[tile_at(turn), :], precv.at[tile_at(turn), :], part_send.at[layer, turn],
            part_recv.at[layer, turn], sibling,
        )

    def du_copy(layer, turn):
        return remote(
            keep["slope"].at[tile_at(turn), :], du_there.at[tile_at(turn), :],
            du_send.at[layer, turn], du_recv.at[layer, turn], sibling,
        )

    def norm_grads(layer, which, values, grad):
        unit, inverse = norm_parts(values)
        gain = gains[layer, which : which + 1, :]
        back, gain_grad, shift_grad = norm_back(unit, inverse, gain, grad)
        add_sum(layer, GAIN + which, everywhere, gain_grad)
        add_sum(layer, SHIFT + which, everywhere, shift_grad)
        return back

    def feed_back_tile(layer, turn):
        now = tile_at(turn)
        grad = low_grad[now, :].astype(f32)
        if layer < top:
            grad = grad + keep["z1"][now, :]
        back = norm_grads(layer, 1, keep["z2"][now, :], grad)
        keep["z2"][now, :] = back
        low = back.astype(b16)
        wide = low.astype(f32)
        turned[:, now] = wide.T.astype(b16)
        add_sum(layer, DOWN_BIAS, everywhere, jnp.sum(wide, 0, keepdims=True))
        size = min(256, quarter)
        total = None
        for block in range(2):
            for start in range(0, quarter, size):
                lanes = slice(block * quarter + start, block * quarter + start + size)
                grads = dot_nt(low, wdown[block, start : start + size, :])
                grads = (grads * keep["slope"][now, lanes].astype(f32)).astype(b16)
                keep["slope"][now, lanes] = grads
                add_sum(
                    layer, UP_BIAS + 2 * block + core, slice(start, start + size),
                    jnp.sum(grads.astype(f32), 0, keepdims=True),
                )
            lanes = slice(block * quarter, (block + 1) * quarter)
            part = dot_nt(keep["slope"][now, lanes], wup[block])
            total = part if total is None else total + part
        psend[now, :] = total.astype(b16)
        part_copy(layer, turn).start()
        du_copy(layer, turn).start()

    def down_grads(layer, which, start):
        lanes = pl.ds(pl.multiple_of(which * quarter, quarter), quarter)
        cols = width // geo.seq_size

        def chunk(step):
            z = order(step)
            at = pl.ds(pl.multiple_of(z * lines * cols, lines * cols), lines * cols)
            result = dot(turned[at, :], keep["act"][:, lanes]).astype(b16)
            for row in range(lines):
                for piece in range(2):
                    block = result[
                        row * cols : (row + 1) * cols,
                        piece * quarter // 2 : (piece + 1) * quarter // 2,
                    ]
                    span = slice(piece * cols, (piece + 1) * cols)
                    if start:
                        other[DOWN, z, row, span, :] = block
                    else:
                        mine[layer, DOWN, z, row, span, :] = block
            if start:
                x_copy(layer, DOWN, z).start()

        loop(posts, chunk)

    def up_grads(layer, which, start):
        left = keep["hrt"][pl.ds(pl.multiple_of(which * depth, depth), depth), :]
        size = quarter // lines
        for block in range(2):
            lanes = slice(block * quarter, (block + 1) * quarter)
            for there, array in ((0, keep["slope"]), (1, du_there)):
                z = 2 * block + core + there * (1 - 2 * core)
                result = dot(left, array[:, lanes]).astype(b16)
                for row in range(lines):
                    piece = result[:, row * size : (row + 1) * size]
                    if start:
                        other[UP, z, row] = piece
                    else:
                        mine[layer, UP, z, row] = piece
        if start:
            for step in range(posts):
                x_copy(layer, UP, order(step)).start()

    def feed_grads(layer, kind):
        make = down_grads if kind == DOWN else up_grads
        if layer < top:
            pl.semaphore_wait(credit.at[kind], 1)
        make(layer, 1 - column, True)
        make(layer, column, False)

    def proj_back_tile(layer, turn):
        now = tile_at(turn)
        part_copy(layer, turn).wait()
        grad = keep["z2"][now, :] + (psend[now, :].astype(f32) + precv[now, :].astype(f32))
        back = norm_grads(layer, 0, keep["z1"][now, :], grad)
        keep["z1"][now, :] = back
        low = back.astype(b16)
        wide = low.astype(f32)
        turned[:, now] = wide.T.astype(b16)
        add_sum(layer, OUT_BIAS, everywhere, jnp.sum(wide, 0, keepdims=True))
        do[now, :] = dot_nt(low, wout[...]).astype(b16)

    lane_head = lax.broadcasted_iota(jnp.int32, (tile, LANES), 1) // HEAD_DIM

    def attend_back_pair(layer, pair):
        lanes = pl.ds(pl.multiple_of(pair * LANES, LANES), LANES)
        key_t = keep["kx"][pair, :, :LANES].astype(f32).T.astype(b16)
        query_t = keep["q"][:, lanes].astype(f32).T.astype(b16)
        grad_t = do[:, lanes].astype(f32).T.astype(b16)
        for head in range(2):
            here = slice(head * HEAD_DIM, (head + 1) * HEAD_DIM)
            qx[head, here, :] = query_t[here]
            dox[head, here, :] = grad_t[here]

        def turn_step(turn):
            now = tile_at(turn)
            query = keep["q"][now, lanes].astype(f32)
            outgrad = do[now, lanes].astype(f32)
            for head in range(2):
                here = slice(head * HEAD_DIM, (head + 1) * HEAD_DIM)
                chosen = (lane_head == head).astype(f32)
                place = pl.ds(pl.multiple_of((2 * turn + head) * tile, tile), tile)
                do_stack[place, :] = (outgrad * chosen).astype(b16)
                q_stack[place, :] = (query * chosen).astype(b16)
                scores = dot(keep["kx"][pair], qx[head, :, now])
                probs = jnp.exp(scores - keep["lse"][2 * pair + head, 0:1, now])
                probs_all[:, place] = probs.astype(b16)
                grads = dot(keep["v"][:, lanes], dox[head, :, now])
                own = pl.ds(pl.multiple_of(pair * LANES + head * HEAD_DIM, HEAD_DIM), HEAD_DIM)
                delta = jnp.sum(
                    dox[head, here, now].astype(f32) * keep["ot"][own, now], 0, keepdims=True
                )
                score_grads = (probs * (grads - delta)).astype(b16)
                grads_all[:, place] = score_grads
                dqt[here, now] = dot(key_t[here], score_grads)

        loop(held, turn_step)
        query_grad = (dqt[...].T * SCALE).astype(b16)
        value_grad = dot(probs_all[...], do_stack[...]).astype(b16)
        dq[:, lanes] = query_grad
        dk[:, lanes] = dot(grads_all[...], q_stack[...]).astype(b16)
        dv[:, lanes] = value_grad
        spot = pl.ds(pl.multiple_of(core * half + pair * LANES, LANES), LANES)
        add_sum(layer, QUERY_BIAS, spot, jnp.sum(query_grad.astype(f32), 0, keepdims=True))
        add_sum(layer, VALUE_BIAS, spot, jnp.sum(value_grad.astype(f32), 0, keepdims=True))

    def qkv_copies(layer):
        return [
            remote(source, target, qkv_send.at[layer, at], qkv_recv.at[layer, at], sibling)
            for at, (source, target) in enumerate(((dq, dq_there), (dk, dk_there), (dv, dv_there)))
        ]

    def dx_copy(layer, shift, turn):
        return remote(
            dx_send.at[shift * held + turn], dx_recv.at[shift * held + turn],
            dx_ssem.at[layer, shift * held + turn], dx_rsem.at[layer, shift * held + turn], sibling,
        )

    def dx_tile(layer, shift, turn):
        now = pl.ds(pl.multiple_of(shift * rows + turn * tile, tile), tile)
        total = dot_nt(dk[now, :], win[1]) + dot_nt(dv[now, :], win[2])
        if shift == 0:
            total = total + dot_nt(dq[now, :], win[0])
        first, second = total[:slots], total[slots:]
        mine_dx[shift * held + turn] = jnp.where(core == 0, first, second).astype(b16)
        dx_send[shift * held + turn] = jnp.where(core == 0, second, first).astype(b16)
        dx_copy(layer, shift, turn).start()

    def line_copy(layer, shift, turn):
        return remote(
            dx_recv.at[shift * held + turn], line_in.at[layer, shift - 1, turn],
            line_send.at[layer, shift - 1, turn], line_recv.at[layer, shift - 1, turn],
            geo.on_line(lines - shift),
        )

    def more_copy(layer, turn, who):
        place = low_grad.at[block_at(turn, who)]
        return remote(place, place, more_send.at[layer, turn], more_recv.at[layer, turn], sibling)

    def token_copies(turn, place):
        own = pltpu.make_async_copy(low_grad.at[block_at(turn, core)], place, tok_sem.at[turn])
        there = remote(
            low_grad.at[block_at(turn, core)], place, tok_send.at[turn], tok_recv.at[turn],
            geo.origin(turn, core),
        )
        return own, there

    def mine_lanes(x):
        cuts = [x[:, at * depth : (at + 1) * depth] for at in range(2 * CORES)]
        return jnp.where(
            core == 0, jnp.concatenate([cuts[0], cuts[2]], 1), jnp.concatenate([cuts[1], cuts[3]], 1)
        )

    def into_grads(layer):
        units = half // unit
        x = mine_lanes(keep["xall"][...])
        for kind, pair in enumerate(((dq, dq_there), (dk, dk_there), (dv, dv_there))):
            for there, ref in enumerate(pair):
                owner = core + there * (1 - 2 * core)
                count = ref.shape[0]
                result = dot_tn(ref[...], x[:count]).astype(b16)
                for at in range(units):
                    index = (2 * kind + owner) * units + at
                    seq = index // 3
                    where = pl.ds(pl.multiple_of(index % 3 * unit, unit), unit)
                    into_cell[seq % lines, seq // lines, where, :] = result[at * unit : (at + 1) * unit]
        send_ay(layer, INTO)

    def proj_grads(layer):
        here, there = keep["o"][...], o_there[...]
        features = jnp.where(
            core == 0,
            jnp.concatenate([here[:, :depth], there[:, :depth]], 1),
            jnp.concatenate([there[:, depth:], here[:, depth:]], 1),
        )
        result = dot(turned[...], features).astype(b16)
        for seq in range(geo.seq_size):
            proj_cell[layer, seq % lines, seq // lines] = result[seq * unit : (seq + 1) * unit]
        send_ay(layer, PROJ)

    def plain_out(layer, names):
        sources = {"du": keep["slope"], "dft": turned, "dat": turned, "dq": dq, "dk": dk, "dv": dv}
        order = ("du", "dft", "dat", "dq", "dk", "dv")
        copies = [
            pltpu.make_async_copy(sources[name], plain[layer][order.index(name)], plain_sem.at[order.index(name)])
            for name in names
        ]
        for copy in copies:
            copy.start()
        for copy in copies:
            copy.wait()

    for layer in range(layers - 1, -1, -1):
        last = layer == 0
        below = layer - 1
        if layer == top:
            loaded(layer, "cot")
        else:
            for turn in range(held):
                more_copy(layer + 1, turn, core).wait_send()
                more_copy(layer + 1, turn, 1 - core).wait_recv()
        o_copy(layer).start()
        loaded(layer, "z2", "wdown", "slope", "wup")
        loop(held, functools.partial(feed_back_tile, layer))
        progress(layer, "feed")
        if not last:
            load(below, "wdown", "wup")
        else:
            load(layer, "z1")
        loaded(layer, "act")
        if geo.aligned:
            feed_grads(layer, DOWN)
            progress(layer, "down")
            if last:
                loaded(layer, "hrt")
                for turn in range(held):
                    du_copy(layer, turn).wait()
                feed_grads(layer, UP)
                progress(layer, "up")
        else:
            plain_out(layer, ("dft",))
        if not last:
            load(below, "act")
        loaded(layer, "z1", "wout")
        loop(held, functools.partial(proj_back_tile, layer))
        progress(layer, "proj")
        if not last:
            load(below, "wout", "z2")
        if geo.aligned:
            loaded(layer, "o")
            o_copy(layer).wait()
            proj_grads(layer)
        loaded(layer, "q", "kx", "v", "ot", "lse")
        for pair in range(pairs):
            attend_back_pair(layer, pair)
            progress(layer, PAIRS[pair])
            if geo.aligned and not last and pair == pairs - 2:
                loaded(layer, "hrt")
                for turn in range(held):
                    du_copy(layer, turn).wait()
                feed_grads(layer, UP)
                progress(layer, "up")
        if not last:
            load(below, "q", "kx", "v", "ot", "lse")
        for copy in qkv_copies(layer):
            copy.start()
        if geo.aligned:
            start_sum(layer)
        loaded(layer, "win")
        for shift in range(1, lines):
            loop(held, functools.partial(dx_tile, layer, shift))
        progress(layer, "dx")
        for shift in range(1, lines):
            for turn in range(held):
                dx_copy(layer, shift, turn).wait()
                at = shift * held + turn
                dx_recv[at] = (mine_dx[at].astype(f32) + dx_recv[at].astype(f32)).astype(b16)
                line_copy(layer, shift, turn).start()
        loop(held, functools.partial(dx_tile, layer, 0))
        progress(layer, "own")
        if not last:
            load(below, "win")
        if geo.aligned:
            for copy in qkv_copies(layer):
                copy.wait()
            loaded(layer, "xall")
            into_grads(layer)
            progress(layer, "into")
        else:
            for turn in range(held):
                du_copy(layer, turn).wait()
            for copy in qkv_copies(layer):
                copy.wait()
            loaded(layer, "hrt", "xall", "o")
            o_copy(layer).wait()
            plain_out(layer, ("du", "dat", "dq", "dk", "dv"))
        if not last:
            load(below, "hrt", "slope", "xall", "o")
        for turn in range(held):
            dx_copy(layer, 0, turn).wait()
            total = mine_dx[turn].astype(f32) + dx_recv[turn].astype(f32)
            for shift in range(1, lines):
                line_copy(layer, shift, turn).wait()
                total = total + line_in[layer, shift - 1, turn].astype(f32)
            if not last:
                low_grad[block_at(turn, core), :] = total.astype(b16)
                more_copy(layer, turn, core).start()
            else:
                total = total + keep["z1"][block_at(turn, core), :]
                low_grad[block_at(turn, core), :] = total.astype(b16)
                own, there = token_copies(turn, grad_tokens.at[geo.parity])
                pl.when(geo.blocked(turn))(own.start)
                pl.when(jnp.logical_not(geo.blocked(turn)))(there.start)

    progress(0, "end")
    for turn in range(held):
        own, there = token_copies(turn, grad_tokens.at[(post + turn) % held])
        pl.when(geo.blocked(turn))(own.wait)
        pl.when(jnp.logical_not(geo.blocked(turn)))(there.wait)


def backward(geo, layers, cot_rows, weights, kept, gains):
    width, rows, half, ffn, count = geo.width, geo.rows, geo.half, geo.ffn, geo.count
    held, lines, posts, slots, quarter = geo.held, geo.lines, geo.posts, geo.slots, geo.quarter
    shapes = kept_shapes(geo)
    any_spec = pl.BlockSpec(memory_space=pl.ANY)
    vmem_spec = pl.BlockSpec(memory_space=pltpu.VMEM)
    unit = width // geo.seq_size
    out = [((held, slots, width), b16), ((layers, SUMS, width), f32)]
    out_specs = [any_spec, vmem_spec]
    if geo.aligned:
        out += [
            ((layers, 2, geo.depth, quarter // lines), f32),
            ((layers, 4 * unit, geo.depth), f32),
        ]
        out_specs += [vmem_spec] * 2
    else:
        for unused in range(layers):
            out += [
                ((rows, ffn // CORES), b16), ((width, rows), b16), ((width, rows), b16),
                ((rows, half), b16), ((count, half), b16), ((count, half), b16),
            ]
            out_specs += [any_spec] * 6
    vmem = pltpu.VMEM
    if geo.aligned:
        shapes["hrt"] = (2 * geo.depth, rows), b16
    scratch = [vmem(*shapes[name]) for name in KEPT]
    scratch += [
        vmem((3, width, half), b16), vmem((half, width), b16),
        vmem((2, width, quarter), b16), vmem((2, quarter, width), b16),
        vmem((rows, half), b16),
        vmem((rows, width), b16),
        vmem((width, rows), b16),
        vmem((rows, ffn // CORES), b16),
        vmem((rows, width), b16), vmem((rows, width), b16),
        vmem((rows, half), b16),
        vmem((2, 2 * LANES, rows), b16), vmem((2, LANES, rows), b16),
        vmem((rows, half), b16), vmem((count, half), b16), vmem((count, half), b16),
        vmem((rows, half), b16), vmem((count, half), b16), vmem((count, half), b16),
        vmem((count, 2 * rows), b16), vmem((count, 2 * rows), b16),
        vmem((2 * rows, LANES), b16), vmem((2 * rows, LANES), b16), vmem((LANES, rows), f32),
        vmem((lines * held, slots, width), b16),
        vmem((lines * held, slots, width), b16), vmem((lines * held, slots, width), b16),
        vmem((layers, lines - 1, held, slots, width), b16),
    ]
    dma = pltpu.SemaphoreType.DMA
    scratch += [dma(shape) for shape in (
        (layers, len(KEPT) + 16), (layers,), (layers,), (layers, held), (layers, held),
        (layers, held), (layers, held), (layers, 3), (layers, 3),
        (layers, lines * held), (layers, lines * held),
        (layers, lines - 1, held), (layers, lines - 1, held),
        (layers, held), (layers, held), (held,), (held,), (held,), (6,),
    )]
    if geo.aligned:
        block = (geo.depth, quarter // lines)
        into, proj = (3 * unit, 2 * geo.depth), (unit, 2 * geo.depth)
        hops = 1 + 1 + (lines - 1) + (posts - 1)
        scratch += [
            vmem((2, posts, lines, *block), b16), vmem((layers, 2, posts, lines, *block), b16),
            vmem((2, posts, lines, *block), b16),
            vmem((layers, 2, posts, lines - 1, *block), b16),
            vmem((layers, 2, posts - 1, *block), b16),
            vmem((lines, posts, *into), b16), vmem((layers, lines, posts, *proj), b16),
            vmem((layers, posts, lines - 1, *into), b16), vmem((layers, posts, lines - 1, *proj), b16),
            vmem((layers, posts - 1, *into), b16), vmem((layers, posts - 1, *proj), b16),
            vmem((layers, 4 * unit, geo.depth), b16), vmem((layers, 4 * unit, geo.depth), b16),
            vmem((layers, hops, SUMS, width), f32),
        ]
        scratch += [dma(shape) for shape in (
            (layers, 2, posts), (layers, 2, posts),
            (layers, 2, posts, lines - 1), (layers, 2, posts, lines - 1),
            (layers, 2, posts - 1), (layers, 2, posts - 1),
            (layers, 2, posts, lines - 1), (layers, 2, posts, lines - 1),
            (layers, 2, posts - 1), (layers, 2, posts - 1), (layers, 2), (layers, 2),
            (layers, hops), (layers, hops),
        )]
        scratch += [pltpu.SemaphoreType.REGULAR((2,))]
    stored = [kept[layer][name] for layer in range(layers) for name in KEPT]
    return pl.pallas_call(
        functools.partial(backward_kernel, geo, layers),
        out_shape=[jax.ShapeDtypeStruct(*shape) for shape in out],
        in_specs=[any_spec] * (5 + len(stored)) + [vmem_spec],
        out_specs=out_specs,
        scratch_shapes=scratch,
        compiler_params=pltpu.CompilerParams(
            collective_id=1, has_side_effects=True, vmem_limit_bytes=VMEM_BACK
        ),
        cost_estimate=pl.CostEstimate(flops=8 * 10**10, bytes_accessed=6 * 10**7, transcendentals=0),
    )(cot_rows, *weights, *stored, gains)


def finish_kernel(
    geo, core_ref, sums_ref, feed_ref, attend_ref, out_in_ref, grad_in_ref,
    out_ref, grad_ref, into_ref, in_bias_ref, proj_ref, out_bias_ref, up_ref, up_bias_ref, down_ref, down_bias_ref,
    gain_ref, shift_ref,
):
    seq = core_ref[0]
    out_ref[...] = out_in_ref[...]
    grad_ref[...] = grad_in_ref[...]
    layers = feed_ref.shape[0]
    unit = geo.width // geo.seq_size
    wide, span = 2 * unit, geo.ffn // geo.seq_size
    per_row, per_quarter = geo.width // wide, geo.quarter // span

    def turn(rows, amount):
        return pltpu.roll(rows, (geo.width - amount) % geo.width, 1)

    for layer in range(layers):
        up_ref[layer] = feed_ref[layer, UP]
        down = feed_ref[layer, DOWN]
        down_ref[layer] = jnp.concatenate([down[:unit], down[unit:]], 1)
        both = attend_ref[layer].T
        into_ref[layer] = both[:, : 3 * unit]
        proj_ref[layer] = both[:, 3 * unit :]
        sums = sums_ref[layer]
        narrow = turn(sums, seq * unit)
        out_bias_ref[layer : layer + 1, :] = narrow[OUT_BIAS : OUT_BIAS + 1, :unit]
        down_bias_ref[layer : layer + 1, :] = narrow[DOWN_BIAS : DOWN_BIAS + 1, :unit]
        gain_ref[layer] = narrow[GAIN : GAIN + 2, :unit]
        shift_ref[layer] = narrow[SHIFT : SHIFT + 2, :unit]
        middle = turn(sums, seq % per_row * wide)
        first = middle[QUERY_BIAS : QUERY_BIAS + 1, :wide]
        second = middle[VALUE_BIAS : VALUE_BIAS + 1, :wide]
        in_bias_ref[layer : layer + 1, :] = jnp.where(seq < per_row, first, second)
        large = turn(sums, seq % per_quarter * span)
        chosen = large[UP_BIAS : UP_BIAS + 1, :span]
        for block in range(1, 4):
            chosen = jnp.where(
                seq // per_quarter == block, large[UP_BIAS + block : UP_BIAS + block + 1, :span], chosen
            )
        up_bias_ref[layer : layer + 1, :] = chosen


def finish(geo, layers, seq, sums, feed_out, attend_out, out_tokens, grad_tokens):
    unit, width = geo.width // geo.seq_size, geo.width
    span = geo.ffn // geo.seq_size
    depth = geo.depth
    shapes = [
        (layers, depth, 3 * unit), (layers, 2 * unit), (layers, depth, unit), (layers, unit),
        (layers, depth, span), (layers, span), (layers, unit, geo.ffn // geo.clip_size),
        (layers, unit), (layers, 2, unit), (layers, 2, unit),
    ]
    results = list(call(
        functools.partial(finish_kernel, geo), seq, 1,
        [all_of(array) for array in (sums, feed_out, attend_out, out_tokens, grad_tokens)],
        [full(out_tokens.shape, b16)] * 2 + [full(shape, f32) for shape in shapes], [],
        10**7, 10**7,
    ))
    results[8] = jnp.swapaxes(results[8], 1, 2)
    return results


def build(mesh):
    clip_size, seq_size = mesh.shape["clip"], mesh.shape["seq"]

    def shards(
        tokens, lengths, attn_in, in_bias, attn_out, out_bias, ffn_in, ffn_in_bias,
        ffn_out, ffn_out_bias, norm_gain, norm_bias, cotangent,
    ):
        layers = attn_in.shape[0]
        geo = Geometry(mesh, tokens, ffn_in.shape[2])
        geo.locate()
        held, width, ffn, half, quarter = geo.held, geo.width, geo.ffn, geo.half, geo.quarter
        aligned, core = geo.aligned, geo.core
        seq_at = geo.seq

        weights = (attn_in, attn_out, ffn_in, ffn_out)
        out_tokens, cot_rows, kept = forward(
            geo, layers, tokens, cotangent, lengths, weights,
            (in_bias, out_bias, ffn_in_bias, ffn_out_bias, norm_gain, norm_bias),
        )
        grad_tokens, sums, *results = backward(geo, layers, cot_rows, weights, kept, norm_gain)
        if aligned:
            seq_arg = jnp.reshape(seq_at, (1,)).astype(jnp.int32)
            return tuple(finish(geo, layers, seq_arg, sums, *results, out_tokens, grad_tokens))

        def swap(array):
            pairs = [(at, at ^ 1) for at in range(clip_size)]
            return lax.ppermute(array, "clip", pairs)

        def spread(array):
            array = lax.psum_scatter(
                array.astype(b16), "seq", scatter_dimension=1, tiled=True
            ).astype(b16)
            return lax.psum_scatter(array, "clip", scatter_dimension=0, tiled=True).astype(f32)

        matrices = []
        for layer in range(layers):
            du, df_t, da_t, dq, dk, dv = results[6 * layer : 6 * layer + 6]
            keep = kept[layer]
            x_all = keep["xall"]
            into = [
                jnp.concatenate([jnp.where(core == 0, a, b), jnp.where(core == 0, b, a)], 1)
                for a, b in (
                    (dot_tn(x_all[: array.shape[0]], array), dot_tn(x_all[: array.shape[0]], swap(array)))
                    for array in (dq, dk, dv)
                )
            ]
            proj = jnp.zeros((CORES, half, width), f32)
            proj = lax.dynamic_update_slice_in_dim(proj, dot(da_t, keep["o"]).T[None], core, 0)
            up = jnp.zeros((2, CORES, width, quarter), f32)
            own_up = dot(keep["hrt"], du).reshape(width, 2, 1, quarter).transpose(1, 2, 0, 3)
            up = lax.dynamic_update_slice_in_dim(up, own_up, core, 1)
            down = jnp.zeros((2, CORES, quarter, width), f32)
            own_down = dot(df_t, keep["act"]).T.reshape(2, 1, quarter, width)
            down = lax.dynamic_update_slice_in_dim(down, own_down, core, 1)
            matrices.append((
                spread(jnp.concatenate(into, 1) * 0.5),
                spread(proj.reshape(width, width)),
                spread(up.transpose(2, 0, 1, 3).reshape(width, ffn)),
                spread(down.reshape(ffn, width)),
            ))
        halves = jnp.arange(SUMS)[None, :, None] >= OUT_BIAS
        summed = lax.psum(jnp.where(halves, 0.5 * sums, sums), ("clip", "seq"))

        def share(row, count):
            piece = summed[:, row : row + count].reshape(layers, count * width)
            size = count * width // seq_size
            return lax.dynamic_slice_in_dim(piece, seq_at * size, size, 1)

        into, proj, up, down = (
            jnp.stack([matrices[layer][which] for layer in range(layers)]) for which in range(4)
        )
        return (
            out_tokens, grad_tokens, into, share(QUERY_BIAS, 2), proj, share(OUT_BIAS, 1),
            up, share(UP_BIAS, 4), down, share(DOWN_BIAS, 1),
            jnp.stack([share(GAIN, 1), share(GAIN + 1, 1)], 1),
            jnp.stack([share(SHIFT, 1), share(SHIFT + 1, 1)], 1),
        )

    return shards


def solution(mesh):
    rowed = P("clip", "seq", None)
    in_specs = (rowed, P("clip")) + (P(),) * 10 + (rowed,)
    out_specs = (
        rowed,
        rowed,
        P(None, "clip", "seq"),
        P(None, "seq"),
        P(None, "clip", "seq"),
        P(None, "seq"),
        P(None, "clip", "seq"),
        P(None, "seq"),
        P(None, "clip", "seq"),
        P(None, "seq"),
        P(None, None, "seq"),
        P(None, None, "seq"),
    )
    return jax.shard_map(
        build(mesh), mesh=mesh, in_specs=in_specs, out_specs=out_specs, check_vma=False
    )
```

```python
from copy import copy as duplicate
import functools

import jax
import jax.numpy as jnp
from jax import lax
from jax.experimental import pallas as pl
from jax.experimental.pallas import tpu as pltpu
from jax.sharding import PartitionSpec as P

HEADS = 12
HEAD_DIM = 64
CORES = 2
LANES = 128
SCALE = HEAD_DIM**-0.5
SQRT_HALF = 0.5**0.5
GAUSS = 0.3989422804014327
LOG2E = 1.4426950408889634
EPS = 1e-05
VMEM = 56 * 1024 * 1024
VMEM_BACK = 63 * 1024 * 1024

f32 = jnp.float32
b16 = jnp.bfloat16


def dot(a, b):
    return lax.dot_general(a, b, (((1,), (0,)), ((), ())), preferred_element_type=f32)


def dot_nt(a, b):
    return lax.dot_general(a, b, (((1,), (1,)), ((), ())), preferred_element_type=f32)


def dot_tn(a, b):
    return lax.dot_general(a, b, (((0,), (0,)), ((), ())), preferred_element_type=f32)


def norm_parts(values):
    center = values - jnp.mean(values, -1, keepdims=True)
    inverse = lax.rsqrt(jnp.mean(center * center, -1, keepdims=True) + EPS)
    return center * inverse, inverse


def norm_back(unit, inverse, gain, grad):
    scaled = grad * gain
    mean_one = jnp.mean(scaled, -1, keepdims=True)
    mean_two = jnp.mean(scaled * unit, -1, keepdims=True)
    back = inverse * (scaled - mean_one - unit * mean_two)
    return back, jnp.sum(grad * unit, 0, keepdims=True), jnp.sum(grad, 0, keepdims=True)


def call(kernel, core, grid, ins, outs, scratch, flops, moved):
    in_specs = [pl.BlockSpec(block, lambda g, c, at=at: at(g, c[0])) for unused, block, at in ins]
    out_specs = [pl.BlockSpec(block, lambda g, c, at=at: at(g, c[0])) for s, d, block, at in outs]
    return pl.pallas_call(
        kernel,
        grid_spec=pltpu.PrefetchScalarGridSpec(
            num_scalar_prefetch=1,
            grid=(grid,),
            in_specs=in_specs,
            out_specs=out_specs,
            scratch_shapes=scratch,
        ),
        out_shape=[jax.ShapeDtypeStruct(shape, dtype) for shape, dtype, b, at in outs],
        compiler_params=pltpu.CompilerParams(
            dimension_semantics=("arbitrary",), vmem_limit_bytes=VMEM
        ),
        cost_estimate=pl.CostEstimate(flops=flops, bytes_accessed=moved, transcendentals=0),
    )(core, *[array for array, b, at in ins])


def all_of(array):
    zeros = (0,) * array.ndim
    return (array, array.shape, lambda g, c: zeros)


def full(shape, dtype):
    zeros = (0,) * len(shape)
    return (shape, dtype, shape, lambda g, c: zeros)


class Geometry:
    def __init__(self, mesh, tokens, ffn):
        self.clip_size, self.seq_size = mesh.shape["clip"], mesh.shape["seq"]
        self.columns = self.clip_size // CORES
        self.held, self.slots, self.width = tokens.shape
        self.ffn = ffn
        self.posts = self.held * CORES
        self.lines = self.seq_size // self.posts
        self.tile = CORES * self.slots
        self.rows = self.held * self.tile
        self.count = self.rows * self.lines
        self.half = self.width // CORES
        self.pairs = self.half // LANES
        self.heads = 2 * self.pairs
        self.quarter = ffn // 4
        self.depth = self.width // self.clip_size
        self.aligned = self.columns == 2 and (ffn // self.seq_size) % LANES == 0

    def locate(self):
        self.clip = lax.axis_index("clip")
        self.seq = lax.axis_index("seq")
        self.core = self.clip % CORES
        self.column = self.clip // CORES
        self.post = self.seq // self.lines
        self.line = self.seq % self.lines
        self.parity = self.post % self.held

    def sibling(self):
        return self.clip + 1 - 2 * self.core, self.seq

    def on_line(self, shift):
        return self.clip, self.post * self.lines + (self.line + shift) % self.lines

    def on_post(self, shift):
        return self.clip, (self.post + shift) % self.posts * self.lines + self.line

    def on_column(self, shift):
        return (self.column + shift) % self.columns * CORES + self.core, self.seq

    def goal(self, turn):
        post = self.held * self.core + (self.post + turn) % self.held
        return self.column * CORES + self.post // self.held, post * self.lines + self.line

    def origin(self, turn, who):
        post = self.held * who + (self.parity + turn) % self.held
        return self.column * CORES + self.post // self.held, post * self.lines + self.line

    def blocked(self, turn):
        return jnp.logical_and(self.post // self.held == self.core, turn == 0)


def remote(source, target, send, receive, device):
    return pltpu.make_async_remote_copy(
        src_ref=source, dst_ref=target, send_sem=send, recv_sem=receive,
        device_id=device, device_id_type=pl.DeviceIdType.MESH,
    )


def meet(geo, devices):
    barrier = pltpu.get_barrier_semaphore()
    total = 0
    for device in devices:
        other = jnp.logical_or(device[0] != geo.clip, device[1] != geo.seq)

        @pl.when(other)
        def greet(device=device):
            pl.semaphore_signal(
                barrier, inc=1, device_id=device, device_id_type=pl.DeviceIdType.MESH
            )

        total = total + other.astype(jnp.int32)
    pl.semaphore_wait(barrier, total)


def loop(count, body):
    def step(at, carry):
        body(at)
        return carry

    lax.fori_loop(0, count, step, 0)


def gelu_parts(inner):
    bell = jnp.exp2((inner * inner) * (-0.5 * LOG2E))
    phi = 0.5 + 0.5 * lax.erf(inner * SQRT_HALF)
    return phi, phi + inner * (GAUSS * bell)


KEPT = ("xall", "kx", "v", "q", "ot", "lse", "o", "z1", "hrt", "act", "slope", "z2")


def kept_shapes(geo):
    rows, width, half, count = geo.rows, geo.width, geo.half, geo.count
    return {
        "xall": ((count, width), b16),
        "kx": ((geo.pairs, count, 2 * LANES), b16),
        "v": ((count, half), b16),
        "q": ((rows, half), b16),
        "ot": ((half, rows), f32),
        "lse": ((geo.heads, 8, rows), f32),
        "o": ((rows, half), b16),
        "z1": ((rows, width), f32),
        "hrt": ((width, rows), b16),
        "act": ((rows, geo.ffn // CORES), b16),
        "slope": ((rows, geo.ffn // CORES), b16),
        "z2": ((rows, width), f32),
    }


def forward_kernel(geo, layers, *refs):
    refs = list(refs)

    def take(count):
        taken = refs[:count]
        del refs[:count]
        return taken

    tokens, cotangent, w_in, w_out, w_up, w_down = take(6)
    lengths, in_bias, out_bias, up_bias, down_bias, gains, shifts = take(7)
    out_tokens, cot_rows = take(2)
    stored = [dict(zip(KEPT, take(len(KEPT)))) for unused in range(layers)]
    kept = [dict(zip(KEPT, take(len(KEPT)))) for unused in range(layers)]
    wq, wkv, wout, wup, wdown = take(5)
    qx, vt, state, hidden, low_out, lens, lens_there, psend, precv, running = take(10)
    (load_sem, save_sem, tok_sem, tok_send, tok_recv, cot_sem, cot_send, cot_recv, sib_send,
     sib_recv, line_send, line_recv, pass_send, pass_recv, part_send, part_recv, out_sem,
     out_send, out_recv, len_sem) = take(20)

    geo = duplicate(geo)
    geo.locate()
    core, tile, slots = geo.core, geo.tile, geo.slots
    held, lines, rows, width, half = geo.held, geo.lines, geo.rows, geo.width, geo.half
    quarter, pairs = geo.quarter, geo.pairs
    sibling = geo.sibling()

    loads = []
    for layer in range(layers):
        targets = (wq.at[layer], wkv.at[layer, :, :half], wkv.at[layer, :, half:])
        parts = [
            (w_in.at[layer, :, pl.ds(pl.multiple_of((kind * CORES + core) * half, half), half)],
             targets[kind])
            for kind in range(3)
        ]
        parts.append((w_out.at[layer, pl.ds(pl.multiple_of(core * half, half), half), :], wout.at[layer]))
        for block in range(2):
            at = pl.ds(pl.multiple_of((2 * block + core) * quarter, quarter), quarter)
            span = slice(block * quarter, (block + 1) * quarter)
            parts.append((w_up.at[layer, :, at], wup.at[layer, :, span]))
            parts.append((w_down.at[layer, at, :], wdown.at[layer, span, :]))
        loads.append([
            pltpu.make_async_copy(source, target, load_sem.at[layer, at])
            for at, (source, target) in enumerate(parts)
        ])
    for copy in loads[0]:
        copy.start()

    sources = [geo.origin(turn, who) for turn in range(held) for who in range(CORES)]
    goals = [geo.goal(turn) for turn in range(held)]
    goals = goals + [(device[0] + 1 - 2 * (device[0] % CORES), device[1]) for device in goals]
    near = [sibling] + [geo.on_line(shift) for shift in range(1, lines)]
    meet(geo, near + sources + goals)

    first = kept[0]["xall"]

    def block_at(turn, who, shift=0):
        start = shift * rows + turn * tile + who * slots
        return pl.ds(start if isinstance(start, int) else pl.multiple_of(start, slots), slots)

    def token_copies(turn, who):
        mine = tokens.at[(geo.post + turn) % held]
        place = first.at[block_at(turn, who)]
        own = pltpu.make_async_copy(mine, place, tok_sem.at[turn])
        return own, remote(mine, place, tok_send.at[turn], tok_recv.at[turn], geo.goal(turn))

    def token_start(turn):
        own, there = token_copies(turn, geo.post // held)
        pl.when(geo.blocked(turn))(own.start)
        pl.when(jnp.logical_not(geo.blocked(turn)))(there.start)

    def token_wait(turn):
        own, there = token_copies(turn, core)
        pl.when(geo.blocked(turn))(own.wait)
        pl.when(jnp.logical_not(geo.blocked(turn)))(there.wait)

    def to_sibling(array, turn, who, shift, send, receive):
        place = array.at[block_at(turn, who, shift)]
        return remote(place, place, send, receive, sibling)

    def to_line(layer, turn, shift):
        array = kept[layer]["xall"]
        source = array.at[block_at(turn, core)]
        target = array.at[block_at(turn, core, shift)]
        return remote(
            source, target, line_send.at[layer, turn, shift - 1], line_recv.at[layer, turn, shift - 1],
            geo.on_line(shift),
        )

    for turn in range(held):
        token_start(turn)
    clip_row = lax.broadcasted_iota(jnp.int32, lens.shape, 0)
    filled = jnp.full(lens.shape, lengths[0], jnp.int32)
    for clip in range(1, held):
        filled = jnp.where(clip_row == clip, lengths[clip], filled)
    lens[...] = filled
    len_copy = remote(lens, lens_there, len_sem.at[0], len_sem.at[1], sibling)
    len_copy.start()

    def clear(at):
        qx[at] = jnp.zeros(qx.shape[1:], b16)
        qx[at, LANES : LANES + 16, :] = (
            lax.broadcasted_iota(jnp.int32, (16, rows), 0) == 0
        ).astype(f32).astype(b16)

    loop(geo.heads, clear)
    len_copy.wait()
    known = jnp.where(geo.post // held == core, lens[...], lens_there[...])
    length = known[0:1, :]
    for clip in range(1, held):
        length = jnp.where(geo.parity == clip, known[clip : clip + 1, :], length)
    lane = lax.broadcasted_iota(jnp.int32, (slots, LANES), 1)
    slot = lax.broadcasted_iota(jnp.int32, (slots, LANES), 0)
    for shift in range(lines):
        for turn in range(held):
            for who in range(CORES):
                post = held * who + (geo.parity + turn) % held
                line = (geo.line + lines - shift) % lines
                outside = (post * lines + line) * slots + slot >= length
                mask = jnp.where(jnp.logical_and(lane == 0, outside), -1e30, 0.0).astype(b16)
                for layer in range(layers):
                    for pair in range(pairs):
                        kept[layer]["kx"][pair, block_at(turn, who, shift), LANES:] = mask

    for turn in range(held):
        token_wait(turn)
        to_sibling(first, turn, core, 0, sib_send.at[turn], sib_recv.at[turn]).start()
        for shift in range(1, lines):
            to_line(0, turn, shift).start()
    for copy in loads[0]:
        copy.wait()
    for copy in loads[1]:
        copy.start()

    def cot_copies(turn, flip):
        mine = cotangent.at[(geo.post + turn) % held]
        place = cot_rows.at[block_at(turn, geo.post // held)]
        goal = geo.goal(turn)
        if flip:
            goal = (goal[0] + 1 - 2 * (goal[0] % CORES), goal[1])
        own = pltpu.make_async_copy(mine, place, cot_sem.at[turn, flip])
        there = remote(
            mine, place, cot_send.at[turn, flip], cot_recv.at[turn, geo.post // held], goal
        )
        here = jnp.logical_and(goal[0] == geo.clip, goal[1] == geo.seq)
        return own, there, here

    def cot_start():
        for turn in range(held):
            for flip in range(CORES):
                own, there, here = cot_copies(turn, flip)
                pl.when(here)(own.start)
                pl.when(jnp.logical_not(here))(there.start)

    def cot_wait():
        for turn in range(held):
            for flip in range(CORES):
                own, there, here = cot_copies(turn, flip)
                pl.when(here)(own.wait)
                pl.when(jnp.logical_not(here))(there.wait_send)
            for who in range(CORES):
                source = geo.origin(turn, who)
                place = cot_rows.at[block_at(turn, who)]
                there = remote(
                    cotangent.at[0], place, cot_send.at[turn, 0], cot_recv.at[turn, who], source
                )
                here = jnp.logical_and(source[0] == geo.clip, source[1] == geo.seq)
                pl.when(jnp.logical_not(here))(there.wait_recv)

    def key_tile(layer, at):
        keep = kept[layer]
        now = pl.ds(pl.multiple_of(at, tile), tile)
        both = dot(keep["xall"][now, :], wkv[layer])
        key = both[:, :half].astype(b16)
        for pair in range(pairs):
            keep["kx"][pair, now, :LANES] = key[:, pair * LANES : (pair + 1) * LANES]
        bias = in_bias[layer : layer + 1, pl.ds(pl.multiple_of(width + core * half, half), half)]
        value = (both[:, half:] + bias).astype(b16)
        keep["v"][now, :] = value
        vt[:, now] = value.astype(f32).T.astype(b16)

    def query_tile(layer, at):
        keep = kept[layer]
        now = pl.ds(pl.multiple_of(at, tile), tile)
        bias = in_bias[layer : layer + 1, pl.ds(pl.multiple_of(core * half, half), half)]
        query = (dot(keep["xall"][now, :], wq[layer]) + bias).astype(b16)
        query = (query * SCALE).astype(b16)
        keep["q"][now, :] = query
        turned = query.astype(f32).T.astype(b16)
        for head in range(geo.heads):
            inside = head % 2 * HEAD_DIM
            qx[head, inside : inside + HEAD_DIM, now] = (
                turned[head * HEAD_DIM : (head + 1) * HEAD_DIM]
            )

    def attend_block(layer, shift, turn):
        keep = kept[layer]
        now = pl.ds(pl.multiple_of(turn * tile, tile), tile)
        span = slice(shift * rows, (shift + 1) * rows)

        size = min(256, rows)
        cuts = [slice(start, start + size) for start in range(shift * rows, (shift + 1) * rows, size)]

        def pair_step(pair):
            heads = [2 * pair, 2 * pair + 1]
            scores = [
                [dot(keep["kx"][pair, cut, :], qx[head, :, now]) for cut in cuts] for head in heads
            ]
            for head, pieces in zip(heads, scores):
                here = pl.ds(pl.multiple_of(head * HEAD_DIM, HEAD_DIM), HEAD_DIM)
                top = functools.reduce(
                    jnp.maximum, [jnp.max(piece, 0, keepdims=True) for piece in pieces]
                )
                if shift > 0:
                    before = keep["lse"][head, 0:1, now]
                    top = jnp.maximum(top, before)
                    shrink = jnp.exp(before - top)
                total = attended = None
                for piece, cut in zip(pieces, cuts):
                    weights = jnp.exp(piece - top)
                    sums = jnp.sum(weights, 0, keepdims=True)
                    values = dot(vt[here, cut], weights.astype(b16))
                    total = sums if total is None else total + sums
                    attended = values if attended is None else attended + values
                if shift > 0:
                    total = total + shrink * running[head, 0:1, now]
                    attended = attended + shrink * keep["ot"][here, now]
                if shift < lines - 1:
                    running[head, 0:1, now] = total
                    keep["ot"][here, now] = attended
                    keep["lse"][head, 0:1, now] = top
                else:
                    keep["ot"][here, now] = attended / total
                    keep["lse"][head, 0:1, now] = top + jnp.log(total)

        loop(pairs, pair_step)

    def project_tile(layer, turn):
        keep = kept[layer]
        now = pl.ds(pl.multiple_of(turn * tile, tile), tile)
        attended = keep["ot"][:, now].T.astype(b16)
        keep["o"][now, :] = attended
        share(2 * layer, turn, dot(attended, wout[layer]))

    def part_copy(which, turn):
        now = pl.ds(pl.multiple_of(turn * tile, tile), tile)
        return remote(
            psend.at[which, now, :], precv.at[which, now, :], part_send.at[which, turn],
            part_recv.at[which, turn], sibling,
        )

    def share(which, turn, part):
        now = pl.ds(pl.multiple_of(turn * tile, tile), tile)
        psend[which, now, :] = part.astype(b16)
        part_copy(which, turn).start()

    def collect(which, turn):
        now = pl.ds(pl.multiple_of(turn * tile, tile), tile)
        part_copy(which, turn).wait()
        return psend[which, now, :].astype(f32) + precv[which, now, :].astype(f32)

    def feed_tile(layer, turn):
        keep = kept[layer]
        now = pl.ds(pl.multiple_of(turn * tile, tile), tile)
        x = first[now, :].astype(f32) if layer == 0 else state[now, :]
        summed = x + collect(2 * layer, turn) + out_bias[layer : layer + 1, :]
        keep["z1"][now, :] = summed
        unit, unused = norm_parts(summed)
        normal = unit * gains[layer, 0:1, :] + shifts[layer, 0:1, :]
        hidden[now, :] = normal
        low = normal.astype(b16)
        keep["hrt"][:, now] = low.astype(f32).T.astype(b16)
        size = min(256, quarter)
        for at in range(0, 2 * quarter, size):
            block, start = at // quarter, at % quarter
            bias = up_bias[
                layer : layer + 1,
                pl.ds(pl.multiple_of((2 * block + core) * quarter + start, size), size),
            ]
            inner = dot(low, wup[layer, :, at : at + size]) + bias
            phi, slope = gelu_parts(inner)
            keep["act"][now, at : at + size] = (inner * phi).astype(b16)
            keep["slope"][now, at : at + size] = slope.astype(b16)
        total = dot(keep["act"][now, :], wdown[layer])
        share(2 * layer + 1, turn, total)

    def norm_tile(layer, turn):
        keep = kept[layer]
        now = pl.ds(pl.multiple_of(turn * tile, tile), tile)
        summed = hidden[now, :] + collect(2 * layer + 1, turn) + down_bias[layer : layer + 1, :]
        keep["z2"][now, :] = summed
        unit, unused = norm_parts(summed)
        result = unit * gains[layer, 1:2, :] + shifts[layer, 1:2, :]
        if layer < layers - 1:
            state[now, :] = result
            kept[layer + 1]["xall"][now, :] = result.astype(b16)
        else:
            low_out[now, :] = result.astype(b16)

    saves = []

    def save(layer, names):
        for name in names:
            copy = pltpu.make_async_copy(
                kept[layer][name], stored[layer][name], save_sem.at[layer, KEPT.index(name)]
            )
            copy.start()
            saves.append(copy)

    for layer in range(layers):
        x_all = kept[layer]["xall"]
        if layer == 0:
            for turn in range(held):
                to_sibling(x_all, turn, core, 0, sib_send.at[turn], sib_recv.at[turn]).wait_send()
                to_sibling(x_all, turn, 1 - core, 0, sib_send.at[turn], sib_recv.at[turn]).wait_recv()
                key_tile(layer, turn * tile)
                query_tile(layer, turn * tile)
        else:
            for copy in loads[layer]:
                copy.wait()

            def own_tile(turn):
                key_tile(layer, turn * tile)
                query_tile(layer, turn * tile)

            loop(held, own_tile)
        for shift in range(lines):
            if shift > 0:
                for turn in range(held):
                    to_line(layer, turn, shift).wait()
                    to_sibling(
                        x_all, turn, core, shift,
                        pass_send.at[layer, turn, shift - 1], pass_recv.at[layer, turn, shift - 1],
                    ).start()
                for turn in range(held):
                    send = pass_send.at[layer, turn, shift - 1]
                    receive = pass_recv.at[layer, turn, shift - 1]
                    to_sibling(x_all, turn, core, shift, send, receive).wait_send()
                    to_sibling(x_all, turn, 1 - core, shift, send, receive).wait_recv()
                    key_tile(layer, shift * rows + turn * tile)
            if shift == lines - 1:
                save(layer, ("xall", "kx", "v", "q"))
                if layer == 0:
                    cot_start()

            def turn_step(turn):
                attend_block(layer, shift, turn)
                if shift == lines - 1:
                    project_tile(layer, turn)

            loop(held, turn_step)
        save(layer, ("ot", "lse", "o"))
        loop(held, functools.partial(feed_tile, layer))
        save(layer, ("z1", "hrt", "act", "slope"))
        for turn in range(held):
            norm_tile(layer, turn)
            if layer < layers - 1:
                for shift in range(1, lines):
                    to_line(layer + 1, turn, shift).start()
        save(layer, ("z2",))

    def out_copies(turn, place):
        mine = low_out.at[block_at(turn, core)]
        own = pltpu.make_async_copy(mine, place, out_sem.at[turn])
        return own, remote(mine, place, out_send.at[turn], out_recv.at[turn], geo.origin(turn, core))

    for turn in range(held):
        own, there = out_copies(turn, out_tokens.at[geo.parity])
        pl.when(geo.blocked(turn))(own.start)
        pl.when(jnp.logical_not(geo.blocked(turn)))(there.start)
    cot_wait()
    for turn in range(held):
        own, there = out_copies(turn, out_tokens.at[(geo.post + turn) % held])
        pl.when(geo.blocked(turn))(own.wait)
        pl.when(jnp.logical_not(geo.blocked(turn)))(there.wait)
    for copy in saves:
        copy.wait()


def forward(geo, layers, tokens, cotangent, lengths, weights, vectors):
    width, rows, half, ffn = geo.width, geo.rows, geo.half, geo.ffn
    shapes = kept_shapes(geo)
    any_spec = pl.BlockSpec(memory_space=pl.ANY)
    vmem_spec = pl.BlockSpec(memory_space=pltpu.VMEM)
    out_shape = [
        jax.ShapeDtypeStruct(tokens.shape, b16),
        jax.ShapeDtypeStruct((rows, width), b16),
    ]
    out_shape += [jax.ShapeDtypeStruct(*shapes[name]) for unused in range(layers) for name in KEPT]
    scratch = [pltpu.VMEM(*shapes[name]) for unused in range(layers) for name in KEPT]
    scratch += [
        pltpu.VMEM((layers, width, half), b16),
        pltpu.VMEM((layers, width, 2 * half), b16),
        pltpu.VMEM((layers, half, width), b16),
        pltpu.VMEM((layers, width, 2 * geo.quarter), b16),
        pltpu.VMEM((layers, 2 * geo.quarter, width), b16),
        pltpu.VMEM((geo.heads, 2 * LANES, rows), b16),
        pltpu.VMEM((half, geo.count), b16),
        pltpu.VMEM((rows, width), f32),
        pltpu.VMEM((rows, width), f32),
        pltpu.VMEM((rows, width), b16),
        pltpu.VMEM((8, LANES), jnp.int32),
        pltpu.VMEM((8, LANES), jnp.int32),
        pltpu.VMEM((2 * layers, rows, width), b16),
        pltpu.VMEM((2 * layers, rows, width), b16),
        pltpu.VMEM((geo.heads, 8, rows), f32),
    ]
    held, lines = geo.held, max(geo.lines - 1, 1)
    dma = pltpu.SemaphoreType.DMA
    scratch += [dma(shape) for shape in (
        (layers, 8), (layers, len(KEPT)), (held,), (held,), (held,),
        (held, CORES), (held, CORES), (held, CORES), (held,), (held,),
        (layers, held, lines), (layers, held, lines), (layers, held, lines), (layers, held, lines),
        (2 * layers, held), (2 * layers, held), (held,), (held,), (held,), (2,),
    )]
    results = pl.pallas_call(
        functools.partial(forward_kernel, geo, layers),
        out_shape=out_shape,
        in_specs=[any_spec] * 6 + [pl.BlockSpec(memory_space=pltpu.SMEM)] + [vmem_spec] * 6,
        out_specs=[any_spec] * len(out_shape),
        scratch_shapes=scratch,
        compiler_params=pltpu.CompilerParams(
            collective_id=0, has_side_effects=True, vmem_limit_bytes=VMEM
        ),
        cost_estimate=pl.CostEstimate(flops=3 * 10**10, bytes_accessed=4 * 10**7, transcendentals=0),
    )(tokens, cotangent, *weights, lengths, *vectors)
    count = len(KEPT)
    kept = [
        dict(zip(KEPT, results[2 + layer * count : 2 + (layer + 1) * count]))
        for layer in range(layers)
    ]
    return results[0], results[1], kept


QUERY_BIAS, VALUE_BIAS, UP_BIAS, OUT_BIAS, DOWN_BIAS, GAIN, SHIFT = 0, 1, 2, 6, 7, 8, 10
SUMS = 16
UP, DOWN = 0, 1
INTO, PROJ = 0, 1
PAIRS = ("pair0", "pair1", "pair2")


def backward_kernel(geo, layers, *refs):
    refs = list(refs)

    def take(count):
        taken = refs[:count]
        del refs[:count]
        return taken

    cot_rows, w_in, w_out, w_up, w_down = take(5)
    stored = [dict(zip(KEPT, take(len(KEPT)))) for unused in range(layers)]
    (gains,) = take(1)
    grad_tokens, sums = take(2)
    if geo.aligned:
        feed_out, attend_out = take(2)
    else:
        plain = [take(6) for unused in range(layers)]
    keep = dict(zip(KEPT, take(len(KEPT))))
    wq, wkv, wout, wup, wdown = take(5)
    (o_there, low_grad, turned, du_there, psend, precv, do, qx, dox, dq, dkv, dq_there,
     dkv_there, probs_all, grads_all, do_stack, q_stack, dqt, mine_dx, dx_send, dx_recv, line_in) = take(22)
    (load_sem, o_send, o_recv, du_send, du_recv, part_send, part_recv, qkv_send, qkv_recv,
     dx_ssem, dx_rsem, line_send, line_recv, more_send, more_recv, tok_sem, tok_send,
     tok_recv, plain_sem) = take(19)
    if geo.aligned:
        (other, mine, from_x, y_first, y_last, z_first, z_last, into_cell, proj_cell, into_y, proj_y, into_z, proj_z,
         a_send, a_x, sum_in) = take(16)
        from_y, from_z = (y_first, y_last), (z_first, z_last)
        cells = [[into_cell] * layers, [proj_cell.at[layer] for layer in range(layers)]]
        cells_y, cells_z = (into_y, proj_y), (into_z, proj_z)
        (fx_send, fx_recv, fy_send, fy_recv, fz_send, fz_recv, ay_send, ay_recv, az_send, az_recv,
         ax_send, ax_recv, sum_send, sum_recv) = take(14)
        (credit,) = take(1)

    geo = duplicate(geo)
    geo.locate()
    core, tile, slots = geo.core, geo.tile, geo.slots
    held, lines, rows, width, half = geo.held, geo.lines, geo.rows, geo.width, geo.half
    quarter, pairs, posts, depth = geo.quarter, geo.pairs, geo.posts, geo.depth
    post, line, column = geo.post, geo.line, geo.column
    unit = width // geo.seq_size
    sibling = geo.sibling()

    def tile_at(turn):
        return pl.ds(pl.multiple_of(turn * tile, tile), tile)

    def block_at(turn, who, shift=0):
        start = shift * rows + turn * tile + who * slots
        return pl.ds(start if isinstance(start, int) else pl.multiple_of(start, slots), slots)

    NAMES = KEPT + ("win", "wout", "wup", "wdown", "cot")

    def load_copies(layer, name):
        where = load_sem.at[layer, NAMES.index(name)]
        if name == "win":
            targets = (wq, wkv.at[:, :half], wkv.at[:, half:])
            return [
                pltpu.make_async_copy(
                    w_in.at[layer, :, pl.ds(pl.multiple_of((kind * CORES + core) * half, half), half)],
                    targets[kind], load_sem.at[layer, len(NAMES) + kind],
                )
                for kind in range(3)
            ]
        if name == "wout":
            at = pl.ds(pl.multiple_of(core * half, half), half)
            return [pltpu.make_async_copy(w_out.at[layer, at, :], wout, where)]
        if name in ("wup", "wdown"):
            copies = []
            for block in range(2):
                at = pl.ds(pl.multiple_of((2 * block + core) * quarter, quarter), quarter)
                slot = len(NAMES) + 3 + 2 * (name == "wdown") + block
                if name == "wup":
                    pair = w_up.at[layer, :, at], wup.at[:, block * quarter : (block + 1) * quarter]
                else:
                    pair = w_down.at[layer, at, :], wdown.at[block * quarter : (block + 1) * quarter, :]
                copies.append(pltpu.make_async_copy(*pair, load_sem.at[layer, slot]))
            return copies
        if name == "hrt" and geo.aligned:
            return [
                pltpu.make_async_copy(
                    stored[layer][name].at[pl.ds(pl.multiple_of((2 * which + core) * depth, depth), depth), :],
                    keep[name].at[which * depth : (which + 1) * depth, :],
                    load_sem.at[layer, len(NAMES) + 7 + which],
                )
                for which in range(2)
            ]
        if name == "cot":
            return [pltpu.make_async_copy(cot_rows, low_grad, where)]
        return [pltpu.make_async_copy(stored[layer][name], keep[name], where)]

    def load(layer, *names):
        for name in names:
            for copy in load_copies(layer, name):
                copy.start()

    def loaded(layer, *names):
        for name in names:
            for copy in load_copies(layer, name):
                copy.wait()

    top = layers - 1
    load(top, "z2", "cot", "wdown", "slope", "wup", "act", "z1", "wout", "q", "kx", "v", "ot",
         "lse", "win", "hrt", "xall", "o")

    sources = [geo.origin(turn, who) for turn in range(held) for who in range(CORES)]
    goals = [geo.goal(turn) for turn in range(held)]
    near = [sibling] + [geo.on_line(shift) for shift in range(1, lines)]
    if geo.aligned:
        near += [geo.on_post(shift) for shift in range(1, posts)]
        near += [geo.on_column(shift) for shift in range(1, geo.columns)]
    goals = goals + [(device[0] + 1 - 2 * (device[0] % CORES), device[1]) for device in goals]
    meet(geo, near + sources + goals)

    def o_copy(layer):
        return remote(stored[layer]["o"], o_there, o_send.at[layer], o_recv.at[layer], sibling)

    def clear(at):
        qx[at] = jnp.zeros(qx.shape[1:], b16)
        qx[at, LANES : LANES + 16, :] = (
            lax.broadcasted_iota(jnp.int32, (16, rows), 0) == 0
        ).astype(f32).astype(b16)
        dox[at] = jnp.zeros(dox.shape[1:], b16)

    loop(2, clear)
    sums[...] = jnp.zeros_like(sums)

    def add_sum(layer, row, lanes, value):
        sums[layer, pl.ds(row, 1), lanes] += value

    everywhere = slice(None)


    def x_copy(layer, kind, z):
        return remote(
            other.at[kind, z], from_x.at[kind, z], fx_send.at[layer, kind, z],
            fx_recv.at[layer, kind, z], geo.on_column(1),
        )

    pair_post = post + 1 - 2 * (post % 2)
    far_post = (post + 2) % posts

    def order(step):
        return (pair_post + step // 2 * (far_post - pair_post) + step % 2 * 2) % posts

    def at_post(which):
        return geo.clip, which * lines + line

    def y_copy(layer, kind, z, shift):
        there = from_y[layer].at[kind, shift - 1] if layer else from_y[layer].at[kind, z, shift - 1]
        at = 0 if layer else z
        return remote(
            mine.at[layer, kind, z, (line + shift) % lines], there,
            fy_send.at[layer, kind, at, shift - 1], fy_recv.at[layer, kind, at, shift - 1],
            geo.on_line(shift),
        )

    def z_copy(layer, kind, hop):
        block = mine.at[layer, kind, order(hop)]
        return remote(
            block if layer else block.at[line], from_z[layer].at[kind, hop],
            fz_send.at[layer, kind, hop], fz_recv.at[layer, kind, hop],
            at_post(far_post if hop == 2 else pair_post),
        )

    def land_x(layer, kind, step):
        z = order(step)
        x_copy(layer, kind, z).wait()
        total = mine[layer, kind, z].astype(f32) + from_x[kind, z].astype(f32)
        mine[layer, kind, z] = total.astype(b16)
        if layer == 0:
            for shift in range(1, lines):
                y_copy(layer, kind, z, shift).start()
            return
        if step < 2:
            z_copy(layer, kind, step).start()
        if step == posts - 1:
            device = geo.on_column(1)
            pl.semaphore_signal(
                credit.at[kind], inc=1, device_id=device, device_id_type=pl.DeviceIdType.MESH
            )

    def land_y(layer, kind, step):
        z = order(step)
        total = mine[layer, kind, z, line].astype(f32)
        for shift in range(1, lines):
            y_copy(layer, kind, z, shift).wait()
            total = total + from_y[layer][kind, z, shift - 1].astype(f32)
        mine[layer, kind, z, line] = total.astype(b16)
        if step < 2:
            z_copy(layer, kind, step).start()

    def land_near(layer, kind):
        z_copy(layer, kind, 1).wait()
        here = (layer, kind, far_post) if layer else (layer, kind, far_post, line)
        total = mine[here].astype(f32) + from_z[layer][kind, 1].astype(f32)
        mine[here] = total.astype(b16)
        z_copy(layer, kind, 2).start()

    def land_far(layer, kind):
        here = (layer, kind, post) if layer else (layer, kind, post, line)
        total = mine[here].astype(f32)
        for hop in (0, 2):
            z_copy(layer, kind, hop).wait()
            total = total + from_z[layer][kind, hop].astype(f32)
        if layer == 0:
            feed_out[layer, kind] = total
            return
        mine[here] = total.astype(b16)
        for shift in range(1, lines):
            y_copy(layer, kind, post, shift).start()

    def land_end(layer, kind):
        total = mine[layer, kind, post, line].astype(f32)
        for shift in range(1, lines):
            y_copy(layer, kind, post, shift).wait()
            total = total + from_y[layer][kind, shift - 1].astype(f32)
        feed_out[layer, kind] = total

    def ay_copy(layer, kind, z, shift):
        return remote(
            cells[kind][layer].at[(line + shift) % lines, z], cells_y[kind].at[layer, z, shift - 1],
            ay_send.at[layer, kind, z, shift - 1], ay_recv.at[layer, kind, z, shift - 1],
            geo.on_line(shift),
        )

    def az_copy(layer, kind, hop):
        return remote(
            cells[kind][layer].at[line, order(hop)], cells_z[kind].at[layer, hop],
            az_send.at[layer, kind, hop], az_recv.at[layer, kind, hop],
            at_post(far_post if hop == 2 else pair_post),
        )

    def ax_copy(layer, kind):
        span = slice(0, 3 * unit) if kind == INTO else slice(3 * unit, 4 * unit)
        return remote(
            a_send.at[layer, span], a_x.at[layer, span], ax_send.at[layer, kind],
            ax_recv.at[layer, kind], geo.on_column(1),
        )

    def send_ay(layer, kind):
        for step in range(posts):
            for shift in range(1, lines):
                ay_copy(layer, kind, order(step), shift).start()

    def land_ay(layer, kind, step):
        z = order(step)
        cell = cells[kind][layer]
        total = cell[line, z].astype(f32)
        for shift in range(1, lines):
            ay_copy(layer, kind, z, shift).wait()
            total = total + cells_y[kind][layer, z, shift - 1].astype(f32)
        cell[line, z] = total.astype(b16)
        if step < 2:
            az_copy(layer, kind, step).start()

    def land_anear(layer, kind):
        cell = cells[kind][layer]
        az_copy(layer, kind, 1).wait()
        total = cell[line, far_post].astype(f32) + cells_z[kind][layer, 1].astype(f32)
        cell[line, far_post] = total.astype(b16)
        az_copy(layer, kind, 2).start()

    def land_afar(layer, kind):
        total = cells[kind][layer][line, post].astype(f32)
        for hop in (0, 2):
            az_copy(layer, kind, hop).wait()
            total = total + cells_z[kind][layer, hop].astype(f32)
        low, high = total[:, :depth], total[:, depth:]
        span = slice(0, 3 * unit) if kind == INTO else slice(3 * unit, 4 * unit)
        attend_out[layer, span] = jnp.where(column == 0, low, high)
        a_send[layer, span] = jnp.where(column == 0, high, low).astype(b16)
        ax_copy(layer, kind).start()

    def land_ax(layer, kind):
        ax_copy(layer, kind).wait()
        span = slice(0, 3 * unit) if kind == INTO else slice(3 * unit, 4 * unit)
        attend_out[layer, span] = attend_out[layer, span] + a_x[layer, span].astype(f32)

    def sum_copies(layer, hop):
        near = ([sibling], [geo.on_line(shift) for shift in range(1, lines)],
                [at_post(pair_post)], [at_post(far_post)], [geo.on_column(1)])
        first = (0, 1, lines, lines + 1, lines + 2)[hop]
        return [
            (remote(
                sums.at[layer], sum_in.at[layer, first + at], sum_send.at[layer, first + at],
                sum_recv.at[layer, first + at], device,
            ), first + at)
            for at, device in enumerate(near[hop])
        ]

    def start_sum(layer):
        shared = lax.broadcasted_iota(jnp.int32, sums.shape[1:], 0) >= OUT_BIAS
        sums[layer] = jnp.where(shared, 0.5 * sums[layer], sums[layer])
        for copy, unused in sum_copies(layer, 0):
            copy.start()

    def land_sum(layer, hop):
        total = sums[layer]
        for copy, at in sum_copies(layer, hop):
            copy.wait()
            total = total + sum_in[layer, at]
        sums[layer] = total
        if hop < 4:
            for copy, unused in sum_copies(layer, hop + 1):
                copy.start()

    schedule = {
        (1, "pair0"): (
            (land_x, 1, DOWN, 0), (land_ay, 1, PROJ, 0),
        ),
        (1, "pair1"): (
            (land_ay, 1, PROJ, 1), (land_ay, 1, PROJ, 2), (land_ay, 1, PROJ, 3),
            (land_x, 1, DOWN, 1),
        ),
        (1, "pair2"): (
            (land_x, 1, DOWN, 2), (land_anear, 1, PROJ),
        ),
        (1, "dx"): (
            (land_x, 1, DOWN, 3),
        ),
        (1, "own"): (
            (land_near, 1, DOWN), (land_afar, 1, PROJ), (land_sum, 1, 0), (land_x, 1, UP, 0),
        ),
        (0, "feed"): (
            (land_x, 1, UP, 1), (land_sum, 1, 1), (land_x, 1, UP, 2), (land_ay, 1, INTO, 0),
            (land_far, 1, DOWN),
        ),
        (0, "down"): (
            (land_x, 1, UP, 3), (land_ax, 1, PROJ), (land_ay, 1, INTO, 1),
        ),
        (0, "proj"): (
            (land_ay, 1, INTO, 2), (land_near, 1, UP), (land_sum, 1, 2),
        ),
        (0, "pair0"): (
            (land_x, 0, DOWN, 0), (land_ay, 1, INTO, 3), (land_end, 1, DOWN),
            (land_ay, 0, PROJ, 0), (land_x, 0, DOWN, 1), (land_ay, 0, PROJ, 1),
            (land_anear, 1, INTO),
        ),
        (0, "pair1"): (
            (land_ay, 0, PROJ, 2), (land_ay, 0, PROJ, 3), (land_x, 0, DOWN, 2),
            (land_y, 0, DOWN, 0),
        ),
        (0, "pair2"): (
            (land_far, 1, UP), (land_y, 0, DOWN, 1), (land_sum, 1, 3), (land_anear, 0, PROJ),
            (land_x, 0, DOWN, 3), (land_y, 0, DOWN, 2),
        ),
        (0, "own"): (
            (land_x, 0, UP, 0), (land_afar, 1, INTO), (land_end, 1, UP), (land_near, 0, DOWN),
            (land_sum, 0, 0), (land_afar, 0, PROJ), (land_y, 0, DOWN, 3), (land_x, 0, UP, 1),
        ),
        (0, "end"): (
            (land_x, 0, UP, 2), (land_far, 0, DOWN), (land_y, 0, UP, 0), (land_sum, 0, 1),
            (land_x, 0, UP, 3), (land_sum, 1, 4), (land_y, 0, UP, 1), (land_ax, 1, INTO),
            (land_ax, 0, PROJ), (land_ay, 0, INTO, 0), (land_sum, 0, 2), (land_ay, 0, INTO, 1),
            (land_ay, 0, INTO, 2), (land_sum, 0, 3), (land_sum, 0, 4), (land_ay, 0, INTO, 3),
            (land_anear, 0, INTO), (land_y, 0, UP, 2), (land_near, 0, UP), (land_y, 0, UP, 3),
            (land_afar, 0, INTO), (land_ax, 0, INTO), (land_far, 0, UP),
        ),
    }

    def progress(layer, phase):
        if geo.aligned:
            for function, *given in schedule.get((layer, phase), ()):
                function(*given)


    def part_copy(layer, turn):
        return remote(
            psend.at[tile_at(turn), :], precv.at[tile_at(turn), :], part_send.at[layer, turn],
            part_recv.at[layer, turn], sibling,
        )

    def du_copy(layer, turn):
        return remote(
            keep["slope"].at[tile_at(turn), :], du_there.at[tile_at(turn), :],
            du_send.at[layer, turn], du_recv.at[layer, turn], sibling,
        )

    def norm_grads(layer, which, values, grad):
        unit, inverse = norm_parts(values)
        gain = gains[layer, which : which + 1, :]
        back, gain_grad, shift_grad = norm_back(unit, inverse, gain, grad)
        add_sum(layer, GAIN + which, everywhere, gain_grad)
        add_sum(layer, SHIFT + which, everywhere, shift_grad)
        return back

    def feed_back_tile(layer, turn):
        now = tile_at(turn)
        grad = low_grad[now, :].astype(f32)
        if layer < top:
            grad = grad + keep["z1"][now, :]
        back = norm_grads(layer, 1, keep["z2"][now, :], grad)
        keep["z2"][now, :] = back
        low = back.astype(b16)
        wide = low.astype(f32)
        turned[:, now] = wide.T.astype(b16)
        add_sum(layer, DOWN_BIAS, everywhere, jnp.sum(wide, 0, keepdims=True))
        size = min(256, quarter)
        for at in range(0, 2 * quarter, size):
            block, start = at // quarter, at % quarter
            lanes = slice(at, at + size)
            grads = dot_nt(low, wdown[lanes, :])
            grads = (grads * keep["slope"][now, lanes].astype(f32)).astype(b16)
            keep["slope"][now, lanes] = grads
            add_sum(
                layer, UP_BIAS + 2 * block + core, slice(start, start + size),
                jnp.sum(grads.astype(f32), 0, keepdims=True),
            )
        total = dot_nt(keep["slope"][now, :], wup[...])
        psend[now, :] = total.astype(b16)
        part_copy(layer, turn).start()
        du_copy(layer, turn).start()

    def down_grads(layer, which, start):
        lanes = pl.ds(pl.multiple_of(which * quarter, quarter), quarter)
        cols = width // geo.seq_size

        def chunk(step):
            z = order(step)
            at = pl.ds(pl.multiple_of(z * lines * cols, lines * cols), lines * cols)
            result = dot(turned[at, :], keep["act"][:, lanes]).astype(b16)
            for row in range(lines):
                for piece in range(2):
                    block = result[
                        row * cols : (row + 1) * cols,
                        piece * quarter // 2 : (piece + 1) * quarter // 2,
                    ]
                    span = slice(piece * cols, (piece + 1) * cols)
                    if start:
                        other[DOWN, z, row, span, :] = block
                    else:
                        mine[layer, DOWN, z, row, span, :] = block
            if start:
                x_copy(layer, DOWN, z).start()

        loop(posts, chunk)

    def up_grads(layer, which, start):
        left = keep["hrt"][pl.ds(pl.multiple_of(which * depth, depth), depth), :]
        size = quarter // lines
        for block in range(2):
            lanes = slice(block * quarter, (block + 1) * quarter)
            for there, array in ((0, keep["slope"]), (1, du_there)):
                z = 2 * block + core + there * (1 - 2 * core)
                result = dot(left, array[:, lanes]).astype(b16)
                for row in range(lines):
                    piece = result[:, row * size : (row + 1) * size]
                    if start:
                        other[UP, z, row] = piece
                    else:
                        mine[layer, UP, z, row] = piece
        if start:
            for step in range(posts):
                x_copy(layer, UP, order(step)).start()

    def feed_grads(layer, kind):
        make = down_grads if kind == DOWN else up_grads
        if layer < top:
            pl.semaphore_wait(credit.at[kind], 1)
        make(layer, 1 - column, True)
        make(layer, column, False)

    def proj_back_tile(layer, turn):
        now = tile_at(turn)
        part_copy(layer, turn).wait()
        grad = keep["z2"][now, :] + (psend[now, :].astype(f32) + precv[now, :].astype(f32))
        back = norm_grads(layer, 0, keep["z1"][now, :], grad)
        keep["z1"][now, :] = back
        low = back.astype(b16)
        wide = low.astype(f32)
        turned[:, now] = wide.T.astype(b16)
        add_sum(layer, OUT_BIAS, everywhere, jnp.sum(wide, 0, keepdims=True))
        do[now, :] = dot_nt(low, wout[...]).astype(b16)

    lane_head = lax.broadcasted_iota(jnp.int32, (tile, LANES), 1) // HEAD_DIM

    def attend_back_pair(layer, pair):
        lanes = pl.ds(pl.multiple_of(pair * LANES, LANES), LANES)
        key_t = keep["kx"][pair, :, :LANES].astype(f32).T.astype(b16)
        query_t = keep["q"][:, lanes].astype(f32).T.astype(b16)
        grad_t = do[:, lanes].astype(f32).T.astype(b16)
        for head in range(2):
            here = slice(head * HEAD_DIM, (head + 1) * HEAD_DIM)
            qx[head, here, :] = query_t[here]
            dox[head, here, :] = grad_t[here]

        def turn_step(turn):
            now = tile_at(turn)
            query = keep["q"][now, lanes].astype(f32)
            outgrad = do[now, lanes].astype(f32)
            for head in range(2):
                here = slice(head * HEAD_DIM, (head + 1) * HEAD_DIM)
                chosen = (lane_head == head).astype(f32)
                place = pl.ds(pl.multiple_of((2 * turn + head) * tile, tile), tile)
                do_stack[place, :] = (outgrad * chosen).astype(b16)
                q_stack[place, :] = (query * chosen).astype(b16)
                scores = dot(keep["kx"][pair], qx[head, :, now])
                probs = jnp.exp(scores - keep["lse"][2 * pair + head, 0:1, now])
                probs_all[:, place] = probs.astype(b16)
                grads = dot(keep["v"][:, lanes], dox[head, :, now])
                own = pl.ds(pl.multiple_of(pair * LANES + head * HEAD_DIM, HEAD_DIM), HEAD_DIM)
                delta = jnp.sum(
                    dox[head, here, now].astype(f32) * keep["ot"][own, now], 0, keepdims=True
                )
                score_grads = (probs * (grads - delta)).astype(b16)
                grads_all[:, place] = score_grads
                dqt[here, now] = dot(key_t[here], score_grads)

        loop(held, turn_step)
        query_grad = (dqt[...].T * SCALE).astype(b16)
        value_grad = dot(probs_all[...], do_stack[...]).astype(b16)
        dq[:, lanes] = query_grad
        dkv[:, lanes] = dot(grads_all[...], q_stack[...]).astype(b16)
        dkv[:, pl.ds(pl.multiple_of(half + pair * LANES, LANES), LANES)] = value_grad
        spot = pl.ds(pl.multiple_of(core * half + pair * LANES, LANES), LANES)
        add_sum(layer, QUERY_BIAS, spot, jnp.sum(query_grad.astype(f32), 0, keepdims=True))
        add_sum(layer, VALUE_BIAS, spot, jnp.sum(value_grad.astype(f32), 0, keepdims=True))

    def qkv_copies(layer):
        return [
            remote(source, target, qkv_send.at[layer, at], qkv_recv.at[layer, at], sibling)
            for at, (source, target) in enumerate(((dq, dq_there), (dkv, dkv_there)))
        ]

    def dx_copy(layer, shift, turn):
        return remote(
            dx_send.at[shift * held + turn], dx_recv.at[shift * held + turn],
            dx_ssem.at[layer, shift * held + turn], dx_rsem.at[layer, shift * held + turn], sibling,
        )

    def dx_tile(layer, shift, turn):
        now = pl.ds(pl.multiple_of(shift * rows + turn * tile, tile), tile)
        total = dot_nt(dkv[now, :], wkv[...])
        if shift == 0:
            total = total + dot_nt(dq[now, :], wq[...])
        first, second = total[:slots], total[slots:]
        mine_dx[shift * held + turn] = jnp.where(core == 0, first, second).astype(b16)
        dx_send[shift * held + turn] = jnp.where(core == 0, second, first).astype(b16)
        dx_copy(layer, shift, turn).start()

    def line_copy(layer, shift, turn):
        return remote(
            dx_recv.at[shift * held + turn], line_in.at[layer, shift - 1, turn],
            line_send.at[layer, shift - 1, turn], line_recv.at[layer, shift - 1, turn],
            geo.on_line(lines - shift),
        )

    def more_copy(layer, turn, who):
        place = low_grad.at[block_at(turn, who)]
        return remote(place, place, more_send.at[layer, turn], more_recv.at[layer, turn], sibling)

    def token_copies(turn, place):
        own = pltpu.make_async_copy(low_grad.at[block_at(turn, core)], place, tok_sem.at[turn])
        there = remote(
            low_grad.at[block_at(turn, core)], place, tok_send.at[turn], tok_recv.at[turn],
            geo.origin(turn, core),
        )
        return own, there

    def mine_lanes(x):
        cuts = [x[:, at * depth : (at + 1) * depth] for at in range(2 * CORES)]
        return jnp.where(
            core == 0, jnp.concatenate([cuts[0], cuts[2]], 1), jnp.concatenate([cuts[1], cuts[3]], 1)
        )

    def into_grads(layer):
        units = half // unit
        x = mine_lanes(keep["xall"][...])
        for first, pair in ((0, (dq, dq_there)), (1, (dkv, dkv_there))):
            for there, ref in enumerate(pair):
                owner = core + there * (1 - 2 * core)
                count = ref.shape[0]
                result = dot_tn(ref[...], x[:count]).astype(b16)
                for at in range(result.shape[0] // unit):
                    kind = first + at // units
                    index = (2 * kind + owner) * units + at % units
                    seq = index // 3
                    where = pl.ds(pl.multiple_of(index % 3 * unit, unit), unit)
                    into_cell[seq % lines, seq // lines, where, :] = result[at * unit : (at + 1) * unit]
        send_ay(layer, INTO)

    def proj_grads(layer):
        here, there = keep["o"][...], o_there[...]
        features = jnp.where(
            core == 0,
            jnp.concatenate([here[:, :depth], there[:, :depth]], 1),
            jnp.concatenate([there[:, depth:], here[:, depth:]], 1),
        )
        result = dot(turned[...], features).astype(b16)
        for seq in range(geo.seq_size):
            proj_cell[layer, seq % lines, seq // lines] = result[seq * unit : (seq + 1) * unit]
        send_ay(layer, PROJ)

    def plain_out(layer, names):
        sources = {"du": keep["slope"], "dft": turned, "dat": turned, "dq": dq, "dk": dkv.at[:, :half], "dv": dkv.at[:, half:]}
        order = ("du", "dft", "dat", "dq", "dk", "dv")
        copies = [
            pltpu.make_async_copy(sources[name], plain[layer][order.index(name)], plain_sem.at[order.index(name)])
            for name in names
        ]
        for copy in copies:
            copy.start()
        for copy in copies:
            copy.wait()

    for layer in range(layers - 1, -1, -1):
        last = layer == 0
        below = layer - 1
        if layer == top:
            loaded(layer, "cot")
        else:
            for turn in range(held):
                more_copy(layer + 1, turn, core).wait_send()
                more_copy(layer + 1, turn, 1 - core).wait_recv()
        o_copy(layer).start()
        loaded(layer, "z2", "wdown", "slope", "wup")
        loop(held, functools.partial(feed_back_tile, layer))
        progress(layer, "feed")
        if not last:
            load(below, "wdown", "wup")
        else:
            load(layer, "z1")
        loaded(layer, "act")
        if geo.aligned:
            feed_grads(layer, DOWN)
            progress(layer, "down")
            if last:
                loaded(layer, "hrt")
                for turn in range(held):
                    du_copy(layer, turn).wait()
                feed_grads(layer, UP)
                progress(layer, "up")
        else:
            plain_out(layer, ("dft",))
        if not last:
            load(below, "act")
        loaded(layer, "z1", "wout")
        loop(held, functools.partial(proj_back_tile, layer))
        progress(layer, "proj")
        if not last:
            load(below, "wout", "z2")
        if geo.aligned:
            loaded(layer, "o")
            o_copy(layer).wait()
            proj_grads(layer)
        loaded(layer, "q", "kx", "v", "ot", "lse")
        for pair in range(pairs):
            attend_back_pair(layer, pair)
            progress(layer, PAIRS[pair])
            if geo.aligned and not last and pair == pairs - 2:
                loaded(layer, "hrt")
                for turn in range(held):
                    du_copy(layer, turn).wait()
                feed_grads(layer, UP)
                progress(layer, "up")
        if not last:
            load(below, "q", "kx", "v", "ot", "lse")
        for copy in qkv_copies(layer):
            copy.start()
        if geo.aligned:
            start_sum(layer)
        loaded(layer, "win")
        for shift in range(1, lines):
            loop(held, functools.partial(dx_tile, layer, shift))
        progress(layer, "dx")
        for shift in range(1, lines):
            for turn in range(held):
                dx_copy(layer, shift, turn).wait()
                at = shift * held + turn
                dx_recv[at] = (mine_dx[at].astype(f32) + dx_recv[at].astype(f32)).astype(b16)
                line_copy(layer, shift, turn).start()
        loop(held, functools.partial(dx_tile, layer, 0))
        progress(layer, "own")
        if not last:
            load(below, "win")
        if geo.aligned:
            for copy in qkv_copies(layer):
                copy.wait()
            loaded(layer, "xall")
            into_grads(layer)
            progress(layer, "into")
        else:
            for turn in range(held):
                du_copy(layer, turn).wait()
            for copy in qkv_copies(layer):
                copy.wait()
            loaded(layer, "hrt", "xall", "o")
            o_copy(layer).wait()
            plain_out(layer, ("du", "dat", "dq", "dk", "dv"))
        if not last:
            load(below, "hrt", "slope", "xall", "o")
        for turn in range(held):
            dx_copy(layer, 0, turn).wait()
            total = mine_dx[turn].astype(f32) + dx_recv[turn].astype(f32)
            for shift in range(1, lines):
                line_copy(layer, shift, turn).wait()
                total = total + line_in[layer, shift - 1, turn].astype(f32)
            if not last:
                low_grad[block_at(turn, core), :] = total.astype(b16)
                more_copy(layer, turn, core).start()
            else:
                total = total + keep["z1"][block_at(turn, core), :]
                low_grad[block_at(turn, core), :] = total.astype(b16)
                own, there = token_copies(turn, grad_tokens.at[geo.parity])
                pl.when(geo.blocked(turn))(own.start)
                pl.when(jnp.logical_not(geo.blocked(turn)))(there.start)

    progress(0, "end")
    for turn in range(held):
        own, there = token_copies(turn, grad_tokens.at[(post + turn) % held])
        pl.when(geo.blocked(turn))(own.wait)
        pl.when(jnp.logical_not(geo.blocked(turn)))(there.wait)


def backward(geo, layers, cot_rows, weights, kept, gains):
    width, rows, half, ffn, count = geo.width, geo.rows, geo.half, geo.ffn, geo.count
    held, lines, posts, slots, quarter = geo.held, geo.lines, geo.posts, geo.slots, geo.quarter
    shapes = kept_shapes(geo)
    any_spec = pl.BlockSpec(memory_space=pl.ANY)
    vmem_spec = pl.BlockSpec(memory_space=pltpu.VMEM)
    unit = width // geo.seq_size
    out = [((held, slots, width), b16), ((layers, SUMS, width), f32)]
    out_specs = [any_spec, vmem_spec]
    if geo.aligned:
        out += [
            ((layers, 2, geo.depth, quarter // lines), f32),
            ((layers, 4 * unit, geo.depth), f32),
        ]
        out_specs += [vmem_spec] * 2
    else:
        for unused in range(layers):
            out += [
                ((rows, ffn // CORES), b16), ((width, rows), b16), ((width, rows), b16),
                ((rows, half), b16), ((count, half), b16), ((count, half), b16),
            ]
            out_specs += [any_spec] * 6
    vmem = pltpu.VMEM
    if geo.aligned:
        shapes["hrt"] = (2 * geo.depth, rows), b16
    scratch = [vmem(*shapes[name]) for name in KEPT]
    scratch += [
        vmem((width, half), b16), vmem((width, 2 * half), b16), vmem((half, width), b16),
        vmem((width, 2 * quarter), b16), vmem((2 * quarter, width), b16),
        vmem((rows, half), b16),
        vmem((rows, width), b16),
        vmem((width, rows), b16),
        vmem((rows, ffn // CORES), b16),
        vmem((rows, width), b16), vmem((rows, width), b16),
        vmem((rows, half), b16),
        vmem((2, 2 * LANES, rows), b16), vmem((2, LANES, rows), b16),
        vmem((rows, half), b16), vmem((count, 2 * half), b16),
        vmem((rows, half), b16), vmem((count, 2 * half), b16),
        vmem((count, 2 * rows), b16), vmem((count, 2 * rows), b16),
        vmem((2 * rows, LANES), b16), vmem((2 * rows, LANES), b16), vmem((LANES, rows), f32),
        vmem((lines * held, slots, width), b16),
        vmem((lines * held, slots, width), b16), vmem((lines * held, slots, width), b16),
        vmem((layers, lines - 1, held, slots, width), b16),
    ]
    dma = pltpu.SemaphoreType.DMA
    scratch += [dma(shape) for shape in (
        (layers, len(KEPT) + 16), (layers,), (layers,), (layers, held), (layers, held),
        (layers, held), (layers, held), (layers, 3), (layers, 3),
        (layers, lines * held), (layers, lines * held),
        (layers, lines - 1, held), (layers, lines - 1, held),
        (layers, held), (layers, held), (held,), (held,), (held,), (6,),
    )]
    if geo.aligned:
        block = (geo.depth, quarter // lines)
        into, proj = (3 * unit, 2 * geo.depth), (unit, 2 * geo.depth)
        hops = lines + 3
        scratch += [
            vmem((2, posts, lines, *block), b16), vmem((layers, 2, posts, lines, *block), b16),
            vmem((2, posts, lines, *block), b16),
            vmem((2, posts, lines - 1, *block), b16), vmem((2, lines - 1, *block), b16),
            vmem((2, 3, *block), b16), vmem((2, 3, lines, *block), b16),
            vmem((lines, posts, *into), b16), vmem((layers, lines, posts, *proj), b16),
            vmem((layers, posts, lines - 1, *into), b16), vmem((layers, posts, lines - 1, *proj), b16),
            vmem((layers, 3, *into), b16), vmem((layers, 3, *proj), b16),
            vmem((layers, 4 * unit, geo.depth), b16), vmem((layers, 4 * unit, geo.depth), b16),
            vmem((layers, hops, SUMS, width), f32),
        ]
        scratch += [dma(shape) for shape in (
            (layers, 2, posts), (layers, 2, posts),
            (layers, 2, posts, lines - 1), (layers, 2, posts, lines - 1),
            (layers, 2, 3), (layers, 2, 3),
            (layers, 2, posts, lines - 1), (layers, 2, posts, lines - 1),
            (layers, 2, 3), (layers, 2, 3), (layers, 2), (layers, 2),
            (layers, hops), (layers, hops),
        )]
        scratch += [pltpu.SemaphoreType.REGULAR((2,))]
    stored = [kept[layer][name] for layer in range(layers) for name in KEPT]
    return pl.pallas_call(
        functools.partial(backward_kernel, geo, layers),
        out_shape=[jax.ShapeDtypeStruct(*shape) for shape in out],
        in_specs=[any_spec] * (5 + len(stored)) + [vmem_spec],
        out_specs=out_specs,
        scratch_shapes=scratch,
        compiler_params=pltpu.CompilerParams(
            collective_id=1, has_side_effects=True, vmem_limit_bytes=VMEM_BACK
        ),
        cost_estimate=pl.CostEstimate(flops=8 * 10**10, bytes_accessed=6 * 10**7, transcendentals=0),
    )(cot_rows, *weights, *stored, gains)


def finish_kernel(
    geo, core_ref, sums_ref, feed_ref, attend_ref, out_in_ref, grad_in_ref,
    out_ref, grad_ref, into_ref, in_bias_ref, proj_ref, out_bias_ref, up_ref, up_bias_ref, down_ref, down_bias_ref,
    gain_ref, shift_ref,
):
    seq = core_ref[0]
    out_ref[...] = out_in_ref[...]
    grad_ref[...] = grad_in_ref[...]
    layers = feed_ref.shape[0]
    unit = geo.width // geo.seq_size
    wide, span = 2 * unit, geo.ffn // geo.seq_size
    per_row, per_quarter = geo.width // wide, geo.quarter // span

    def turn(rows, amount):
        return pltpu.roll(rows, (geo.width - amount) % geo.width, 1)

    for layer in range(layers):
        up_ref[layer] = feed_ref[layer, UP]
        down = feed_ref[layer, DOWN]
        down_ref[layer] = jnp.concatenate([down[:unit], down[unit:]], 1)
        both = attend_ref[layer].T
        into_ref[layer] = both[:, : 3 * unit]
        proj_ref[layer] = both[:, 3 * unit :]
        sums = sums_ref[layer]
        narrow = turn(sums, seq * unit)
        out_bias_ref[layer : layer + 1, :] = narrow[OUT_BIAS : OUT_BIAS + 1, :unit]
        down_bias_ref[layer : layer + 1, :] = narrow[DOWN_BIAS : DOWN_BIAS + 1, :unit]
        gain_ref[layer] = narrow[GAIN : GAIN + 2, :unit]
        shift_ref[layer] = narrow[SHIFT : SHIFT + 2, :unit]
        middle = turn(sums, seq % per_row * wide)
        first = middle[QUERY_BIAS : QUERY_BIAS + 1, :wide]
        second = middle[VALUE_BIAS : VALUE_BIAS + 1, :wide]
        in_bias_ref[layer : layer + 1, :] = jnp.where(seq < per_row, first, second)
        large = turn(sums, seq % per_quarter * span)
        chosen = large[UP_BIAS : UP_BIAS + 1, :span]
        for block in range(1, 4):
            chosen = jnp.where(
                seq // per_quarter == block, large[UP_BIAS + block : UP_BIAS + block + 1, :span], chosen
            )
        up_bias_ref[layer : layer + 1, :] = chosen


def finish(geo, layers, seq, sums, feed_out, attend_out, out_tokens, grad_tokens):
    unit, width = geo.width // geo.seq_size, geo.width
    span = geo.ffn // geo.seq_size
    depth = geo.depth
    shapes = [
        (layers, depth, 3 * unit), (layers, 2 * unit), (layers, depth, unit), (layers, unit),
        (layers, depth, span), (layers, span), (layers, unit, geo.ffn // geo.clip_size),
        (layers, unit), (layers, 2, unit), (layers, 2, unit),
    ]
    results = list(call(
        functools.partial(finish_kernel, geo), seq, 1,
        [all_of(array) for array in (sums, feed_out, attend_out, out_tokens, grad_tokens)],
        [full(out_tokens.shape, b16)] * 2 + [full(shape, f32) for shape in shapes], [],
        10**7, 10**7,
    ))
    results[8] = jnp.swapaxes(results[8], 1, 2)
    return results


def build(mesh):
    clip_size, seq_size = mesh.shape["clip"], mesh.shape["seq"]

    def shards(
        tokens, lengths, attn_in, in_bias, attn_out, out_bias, ffn_in, ffn_in_bias,
        ffn_out, ffn_out_bias, norm_gain, norm_bias, cotangent,
    ):
        layers = attn_in.shape[0]
        geo = Geometry(mesh, tokens, ffn_in.shape[2])
        geo.locate()
        held, width, ffn, half, quarter = geo.held, geo.width, geo.ffn, geo.half, geo.quarter
        aligned, core = geo.aligned, geo.core
        seq_at = geo.seq

        weights = (attn_in, attn_out, ffn_in, ffn_out)
        out_tokens, cot_rows, kept = forward(
            geo, layers, tokens, cotangent, lengths, weights,
            (in_bias, out_bias, ffn_in_bias, ffn_out_bias, norm_gain, norm_bias),
        )
        grad_tokens, sums, *results = backward(geo, layers, cot_rows, weights, kept, norm_gain)
        if aligned:
            seq_arg = jnp.reshape(seq_at, (1,)).astype(jnp.int32)
            return tuple(finish(geo, layers, seq_arg, sums, *results, out_tokens, grad_tokens))

        def swap(array):
            pairs = [(at, at ^ 1) for at in range(clip_size)]
            return lax.ppermute(array, "clip", pairs)

        def spread(array):
            array = lax.psum_scatter(
                array.astype(b16), "seq", scatter_dimension=1, tiled=True
            ).astype(b16)
            return lax.psum_scatter(array, "clip", scatter_dimension=0, tiled=True).astype(f32)

        matrices = []
        for layer in range(layers):
            du, df_t, da_t, dq, dk, dv = results[6 * layer : 6 * layer + 6]
            keep = kept[layer]
            x_all = keep["xall"]
            into = [
                jnp.concatenate([jnp.where(core == 0, a, b), jnp.where(core == 0, b, a)], 1)
                for a, b in (
                    (dot_tn(x_all[: array.shape[0]], array), dot_tn(x_all[: array.shape[0]], swap(array)))
                    for array in (dq, dk, dv)
                )
            ]
            proj = jnp.zeros((CORES, half, width), f32)
            proj = lax.dynamic_update_slice_in_dim(proj, dot(da_t, keep["o"]).T[None], core, 0)
            up = jnp.zeros((2, CORES, width, quarter), f32)
            own_up = dot(keep["hrt"], du).reshape(width, 2, 1, quarter).transpose(1, 2, 0, 3)
            up = lax.dynamic_update_slice_in_dim(up, own_up, core, 1)
            down = jnp.zeros((2, CORES, quarter, width), f32)
            own_down = dot(df_t, keep["act"]).T.reshape(2, 1, quarter, width)
            down = lax.dynamic_update_slice_in_dim(down, own_down, core, 1)
            matrices.append((
                spread(jnp.concatenate(into, 1) * 0.5),
                spread(proj.reshape(width, width)),
                spread(up.transpose(2, 0, 1, 3).reshape(width, ffn)),
                spread(down.reshape(ffn, width)),
            ))
        halves = jnp.arange(SUMS)[None, :, None] >= OUT_BIAS
        summed = lax.psum(jnp.where(halves, 0.5 * sums, sums), ("clip", "seq"))

        def share(row, count):
            piece = summed[:, row : row + count].reshape(layers, count * width)
            size = count * width // seq_size
            return lax.dynamic_slice_in_dim(piece, seq_at * size, size, 1)

        into, proj, up, down = (
            jnp.stack([matrices[layer][which] for layer in range(layers)]) for which in range(4)
        )
        return (
            out_tokens, grad_tokens, into, share(QUERY_BIAS, 2), proj, share(OUT_BIAS, 1),
            up, share(UP_BIAS, 4), down, share(DOWN_BIAS, 1),
            jnp.stack([share(GAIN, 1), share(GAIN + 1, 1)], 1),
            jnp.stack([share(SHIFT, 1), share(SHIFT + 1, 1)], 1),
        )

    return shards


def solution(mesh):
    rowed = P("clip", "seq", None)
    in_specs = (rowed, P("clip")) + (P(),) * 10 + (rowed,)
    out_specs = (
        rowed,
        rowed,
        P(None, "clip", "seq"),
        P(None, "seq"),
        P(None, "clip", "seq"),
        P(None, "seq"),
        P(None, "clip", "seq"),
        P(None, "seq"),
        P(None, "clip", "seq"),
        P(None, "seq"),
        P(None, None, "seq"),
        P(None, None, "seq"),
    )
    return jax.shard_map(
        build(mesh), mesh=mesh, in_specs=in_specs, out_specs=out_specs, check_vma=False
    )
```

```python
from copy import copy as duplicate
import functools

import jax
import jax.numpy as jnp
from jax import lax
from jax.experimental import pallas as pl
from jax.experimental.pallas import tpu as pltpu
from jax.sharding import PartitionSpec as P

HEADS = 12
HEAD_DIM = 64
CORES = 2
LANES = 128
SCALE = HEAD_DIM**-0.5
SQRT_HALF = 0.5**0.5
GAUSS = 0.3989422804014327
LOG2E = 1.4426950408889634
EPS = 1e-05
VMEM = 56 * 1024 * 1024
VMEM_BACK = 63 * 1024 * 1024

f32 = jnp.float32
b16 = jnp.bfloat16


def dot(a, b):
    return lax.dot_general(a, b, (((1,), (0,)), ((), ())), preferred_element_type=f32)


def dot_nt(a, b):
    return lax.dot_general(a, b, (((1,), (1,)), ((), ())), preferred_element_type=f32)


def dot_tn(a, b):
    return lax.dot_general(a, b, (((0,), (0,)), ((), ())), preferred_element_type=f32)


def norm_parts(values):
    center = values - jnp.mean(values, -1, keepdims=True)
    inverse = lax.rsqrt(jnp.mean(center * center, -1, keepdims=True) + EPS)
    return center * inverse, inverse


def norm_back(unit, inverse, gain, grad):
    scaled = grad * gain
    mean_one = jnp.mean(scaled, -1, keepdims=True)
    mean_two = jnp.mean(scaled * unit, -1, keepdims=True)
    back = inverse * (scaled - mean_one - unit * mean_two)
    return back, jnp.sum(grad * unit, 0, keepdims=True), jnp.sum(grad, 0, keepdims=True)


def call(kernel, core, grid, ins, outs, scratch, flops, moved):
    in_specs = [pl.BlockSpec(block, lambda g, c, at=at: at(g, c[0])) for unused, block, at in ins]
    out_specs = [pl.BlockSpec(block, lambda g, c, at=at: at(g, c[0])) for s, d, block, at in outs]
    return pl.pallas_call(
        kernel,
        grid_spec=pltpu.PrefetchScalarGridSpec(
            num_scalar_prefetch=1,
            grid=(grid,),
            in_specs=in_specs,
            out_specs=out_specs,
            scratch_shapes=scratch,
        ),
        out_shape=[jax.ShapeDtypeStruct(shape, dtype) for shape, dtype, b, at in outs],
        compiler_params=pltpu.CompilerParams(
            dimension_semantics=("arbitrary",), vmem_limit_bytes=VMEM
        ),
        cost_estimate=pl.CostEstimate(flops=flops, bytes_accessed=moved, transcendentals=0),
    )(core, *[array for array, b, at in ins])


def all_of(array):
    zeros = (0,) * array.ndim
    return (array, array.shape, lambda g, c: zeros)


def full(shape, dtype):
    zeros = (0,) * len(shape)
    return (shape, dtype, shape, lambda g, c: zeros)


class Geometry:
    def __init__(self, mesh, tokens, ffn):
        self.clip_size, self.seq_size = mesh.shape["clip"], mesh.shape["seq"]
        self.columns = self.clip_size // CORES
        self.held, self.slots, self.width = tokens.shape
        self.ffn = ffn
        self.posts = self.held * CORES
        self.lines = self.seq_size // self.posts
        self.tile = CORES * self.slots
        self.rows = self.held * self.tile
        self.count = self.rows * self.lines
        self.half = self.width // CORES
        self.pairs = self.half // LANES
        self.heads = 2 * self.pairs
        self.quarter = ffn // 4
        self.depth = self.width // self.clip_size
        self.aligned = self.columns == 2 and (ffn // self.seq_size) % LANES == 0

    def locate(self):
        self.clip = lax.axis_index("clip")
        self.seq = lax.axis_index("seq")
        self.core = self.clip % CORES
        self.column = self.clip // CORES
        self.post = self.seq // self.lines
        self.line = self.seq % self.lines
        self.parity = self.post % self.held

    def sibling(self):
        return self.clip + 1 - 2 * self.core, self.seq

    def on_line(self, shift):
        return self.clip, self.post * self.lines + (self.line + shift) % self.lines

    def on_post(self, shift):
        return self.clip, (self.post + shift) % self.posts * self.lines + self.line

    def on_column(self, shift):
        return (self.column + shift) % self.columns * CORES + self.core, self.seq

    def goal(self, turn):
        post = self.held * self.core + (self.post + turn) % self.held
        return self.column * CORES + self.post // self.held, post * self.lines + self.line

    def origin(self, turn, who):
        post = self.held * who + (self.parity + turn) % self.held
        return self.column * CORES + self.post // self.held, post * self.lines + self.line

    def blocked(self, turn):
        return jnp.logical_and(self.post // self.held == self.core, turn == 0)


def remote(source, target, send, receive, device):
    return pltpu.make_async_remote_copy(
        src_ref=source, dst_ref=target, send_sem=send, recv_sem=receive,
        device_id=device, device_id_type=pl.DeviceIdType.MESH,
    )


def meet(geo, devices):
    barrier = pltpu.get_barrier_semaphore()
    total = 0
    for device in devices:
        other = jnp.logical_or(device[0] != geo.clip, device[1] != geo.seq)

        @pl.when(other)
        def greet(device=device):
            pl.semaphore_signal(
                barrier, inc=1, device_id=device, device_id_type=pl.DeviceIdType.MESH
            )

        total = total + other.astype(jnp.int32)
    pl.semaphore_wait(barrier, total)


def loop(count, body):
    def step(at, carry):
        body(at)
        return carry

    lax.fori_loop(0, count, step, 0)


def gelu_parts(inner):
    bell = jnp.exp2((inner * inner) * (-0.5 * LOG2E))
    phi = 0.5 + 0.5 * lax.erf(inner * SQRT_HALF)
    return phi, phi + inner * (GAUSS * bell)


KEPT = ("xall", "kx", "v", "q", "ot", "lse", "o", "z1", "hrt", "act", "slope", "z2")


def kept_shapes(geo):
    rows, width, half, count = geo.rows, geo.width, geo.half, geo.count
    return {
        "xall": ((count, width), b16),
        "kx": ((geo.pairs, count, 2 * LANES), b16),
        "v": ((count, half), b16),
        "q": ((rows, half), b16),
        "ot": ((half, rows), f32),
        "lse": ((geo.heads, 8, rows), f32),
        "o": ((rows, half), b16),
        "z1": ((rows, width), f32),
        "hrt": ((width, rows), b16),
        "act": ((rows, geo.ffn // CORES), b16),
        "slope": ((rows, geo.ffn // CORES), b16),
        "z2": ((rows, width), f32),
    }


def forward_kernel(geo, layers, *refs):
    refs = list(refs)

    def take(count):
        taken = refs[:count]
        del refs[:count]
        return taken

    tokens, cotangent, w_in, w_out, w_up, w_down = take(6)
    lengths, in_bias, out_bias, up_bias, down_bias, gains, shifts = take(7)
    out_tokens, cot_rows = take(2)
    stored = [dict(zip(KEPT, take(len(KEPT)))) for unused in range(layers)]
    kept = [dict(zip(KEPT, take(len(KEPT)))) for unused in range(layers)]
    wq, wkv, wout, wup, wdown = take(5)
    qx, vt, state, hidden, low_out, lens, lens_there, psend, precv, running = take(10)
    (load_sem, save_sem, tok_sem, tok_send, tok_recv, cot_sem, cot_send, cot_recv, sib_send,
     sib_recv, line_send, line_recv, pass_send, pass_recv, part_send, part_recv, out_sem,
     out_send, out_recv, len_sem) = take(20)

    geo = duplicate(geo)
    geo.locate()
    core, tile, slots = geo.core, geo.tile, geo.slots
    held, lines, rows, width, half = geo.held, geo.lines, geo.rows, geo.width, geo.half
    quarter, pairs = geo.quarter, geo.pairs
    sibling = geo.sibling()

    loads = []
    for layer in range(layers):
        targets = (wq.at[layer], wkv.at[layer, :, :half], wkv.at[layer, :, half:])
        parts = [
            (w_in.at[layer, :, pl.ds(pl.multiple_of((kind * CORES + core) * half, half), half)],
             targets[kind])
            for kind in range(3)
        ]
        parts.append((w_out.at[layer, pl.ds(pl.multiple_of(core * half, half), half), :], wout.at[layer]))
        for block in range(2):
            at = pl.ds(pl.multiple_of((2 * block + core) * quarter, quarter), quarter)
            span = slice(block * quarter, (block + 1) * quarter)
            parts.append((w_up.at[layer, :, at], wup.at[layer, :, span]))
            parts.append((w_down.at[layer, at, :], wdown.at[layer, span, :]))
        loads.append([
            pltpu.make_async_copy(source, target, load_sem.at[layer, at])
            for at, (source, target) in enumerate(parts)
        ])
    for copy in loads[0]:
        copy.start()

    sources = [geo.origin(turn, who) for turn in range(held) for who in range(CORES)]
    goals = [geo.goal(turn) for turn in range(held)]
    goals = goals + [(device[0] + 1 - 2 * (device[0] % CORES), device[1]) for device in goals]
    near = [sibling] + [geo.on_line(shift) for shift in range(1, lines)]
    meet(geo, near + sources + goals)

    first = kept[0]["xall"]

    def block_at(turn, who, shift=0):
        start = shift * rows + turn * tile + who * slots
        return pl.ds(start if isinstance(start, int) else pl.multiple_of(start, slots), slots)

    def token_copies(turn, who):
        mine = tokens.at[(geo.post + turn) % held]
        place = first.at[block_at(turn, who)]
        own = pltpu.make_async_copy(mine, place, tok_sem.at[turn])
        return own, remote(mine, place, tok_send.at[turn], tok_recv.at[turn], geo.goal(turn))

    def token_start(turn):
        own, there = token_copies(turn, geo.post // held)
        pl.when(geo.blocked(turn))(own.start)
        pl.when(jnp.logical_not(geo.blocked(turn)))(there.start)

    def token_wait(turn):
        own, there = token_copies(turn, core)
        pl.when(geo.blocked(turn))(own.wait)
        pl.when(jnp.logical_not(geo.blocked(turn)))(there.wait)

    def to_sibling(array, turn, who, shift, send, receive):
        place = array.at[block_at(turn, who, shift)]
        return remote(place, place, send, receive, sibling)

    def to_line(layer, turn, shift):
        array = kept[layer]["xall"]
        source = array.at[block_at(turn, core)]
        target = array.at[block_at(turn, core, shift)]
        return remote(
            source, target, line_send.at[layer, turn, shift - 1], line_recv.at[layer, turn, shift - 1],
            geo.on_line(shift),
        )

    for turn in range(held):
        token_start(turn)
    clip_row = lax.broadcasted_iota(jnp.int32, lens.shape, 0)
    filled = jnp.full(lens.shape, lengths[0], jnp.int32)
    for clip in range(1, held):
        filled = jnp.where(clip_row == clip, lengths[clip], filled)
    lens[...] = filled
    len_copy = remote(lens, lens_there, len_sem.at[0], len_sem.at[1], sibling)
    len_copy.start()

    def clear(at):
        qx[at] = jnp.zeros(qx.shape[1:], b16)
        qx[at, LANES : LANES + 16, :] = (
            lax.broadcasted_iota(jnp.int32, (16, rows), 0) == 0
        ).astype(f32).astype(b16)

    loop(geo.heads, clear)
    len_copy.wait()
    known = jnp.where(geo.post // held == core, lens[...], lens_there[...])
    length = known[0:1, :]
    for clip in range(1, held):
        length = jnp.where(geo.parity == clip, known[clip : clip + 1, :], length)
    lane = lax.broadcasted_iota(jnp.int32, (slots, LANES), 1)
    slot = lax.broadcasted_iota(jnp.int32, (slots, LANES), 0)
    for shift in range(lines):
        for turn in range(held):
            for who in range(CORES):
                post = held * who + (geo.parity + turn) % held
                line = (geo.line + lines - shift) % lines
                outside = (post * lines + line) * slots + slot >= length
                mask = jnp.where(jnp.logical_and(lane == 0, outside), -1e30, 0.0)
                mask = jnp.where(jnp.logical_and(lane > 0, lane < 4), 1.0, mask).astype(b16)
                for layer in range(layers):
                    for pair in range(pairs):
                        kept[layer]["kx"][pair, block_at(turn, who, shift), LANES:] = mask

    for turn in range(held):
        token_wait(turn)
        to_sibling(first, turn, core, 0, sib_send.at[turn], sib_recv.at[turn]).start()
        for shift in range(1, lines):
            to_line(0, turn, shift).start()
    for copy in loads[0]:
        copy.wait()
    for copy in loads[1]:
        copy.start()

    def cot_copies(turn, flip):
        mine = cotangent.at[(geo.post + turn) % held]
        place = cot_rows.at[block_at(turn, geo.post // held)]
        goal = geo.goal(turn)
        if flip:
            goal = (goal[0] + 1 - 2 * (goal[0] % CORES), goal[1])
        own = pltpu.make_async_copy(mine, place, cot_sem.at[turn, flip])
        there = remote(
            mine, place, cot_send.at[turn, flip], cot_recv.at[turn, geo.post // held], goal
        )
        here = jnp.logical_and(goal[0] == geo.clip, goal[1] == geo.seq)
        return own, there, here

    def cot_start():
        for turn in range(held):
            for flip in range(CORES):
                own, there, here = cot_copies(turn, flip)
                pl.when(here)(own.start)
                pl.when(jnp.logical_not(here))(there.start)

    def cot_wait():
        for turn in range(held):
            for flip in range(CORES):
                own, there, here = cot_copies(turn, flip)
                pl.when(here)(own.wait)
                pl.when(jnp.logical_not(here))(there.wait_send)
            for who in range(CORES):
                source = geo.origin(turn, who)
                place = cot_rows.at[block_at(turn, who)]
                there = remote(
                    cotangent.at[0], place, cot_send.at[turn, 0], cot_recv.at[turn, who], source
                )
                here = jnp.logical_and(source[0] == geo.clip, source[1] == geo.seq)
                pl.when(jnp.logical_not(here))(there.wait_recv)

    def key_tile(layer, at):
        keep = kept[layer]
        now = pl.ds(pl.multiple_of(at, tile), tile)
        both = dot(keep["xall"][now, :], wkv[layer])
        key = both[:, :half].astype(b16)
        for pair in range(pairs):
            keep["kx"][pair, now, :LANES] = key[:, pair * LANES : (pair + 1) * LANES]
        bias = in_bias[layer : layer + 1, pl.ds(pl.multiple_of(width + core * half, half), half)]
        value = (both[:, half:] + bias).astype(b16)
        keep["v"][now, :] = value
        vt[:, now] = value.astype(f32).T.astype(b16)

    def query_tile(layer, at):
        keep = kept[layer]
        now = pl.ds(pl.multiple_of(at, tile), tile)
        bias = in_bias[layer : layer + 1, pl.ds(pl.multiple_of(core * half, half), half)]
        query = (dot(keep["xall"][now, :], wq[layer]) + bias).astype(b16)
        query = (query * SCALE).astype(b16)
        keep["q"][now, :] = query
        turned = query.astype(f32).T.astype(b16)
        for head in range(geo.heads):
            inside = head % 2 * HEAD_DIM
            qx[head, inside : inside + HEAD_DIM, now] = (
                turned[head * HEAD_DIM : (head + 1) * HEAD_DIM]
            )

    def attend_block(layer, shift):
        keep = kept[layer]
        span = slice(shift * rows, (shift + 1) * rows)

        size = min(256, rows)
        cuts = [slice(start, start + size) for start in range(shift * rows, (shift + 1) * rows, size)]

        def pair_step(pair):
            heads = [2 * pair, 2 * pair + 1]
            scores = [
                [dot(keep["kx"][pair, cut, :], qx[head]) for cut in cuts] for head in heads
            ]
            for head, pieces in zip(heads, scores):
                here = pl.ds(pl.multiple_of(head * HEAD_DIM, HEAD_DIM), HEAD_DIM)
                top = functools.reduce(
                    jnp.maximum, [jnp.max(piece, 0, keepdims=True) for piece in pieces]
                )
                if shift > 0:
                    before = keep["lse"][head, 0:1, :]
                    top = jnp.maximum(top, before)
                    shrink = jnp.exp(before - top)
                total = attended = None
                for piece, cut in zip(pieces, cuts):
                    weights = jnp.exp(piece - top)
                    sums = jnp.sum(weights, 0, keepdims=True)
                    values = dot(vt[here, cut], weights.astype(b16))
                    total = sums if total is None else total + sums
                    attended = values if attended is None else attended + values
                if shift > 0:
                    total = total + shrink * running[head, 0:1, :]
                    attended = attended + shrink * keep["ot"][here, :]
                if shift < lines - 1:
                    running[head, 0:1, :] = total
                    keep["ot"][here, :] = attended
                    keep["lse"][head, 0:1, :] = top
                else:
                    keep["ot"][here, :] = attended / total
                    keep["lse"][head, 0:1, :] = top + jnp.log(total)

        loop(pairs, pair_step)

    def project_tile(layer, turn):
        keep = kept[layer]
        now = pl.ds(pl.multiple_of(turn * tile, tile), tile)
        attended = keep["ot"][:, now].T.astype(b16)
        keep["o"][now, :] = attended
        share(2 * layer, turn, dot(attended, wout[layer]))

    def part_copy(which, turn):
        now = pl.ds(pl.multiple_of(turn * tile, tile), tile)
        return remote(
            psend.at[which, now, :], precv.at[which, now, :], part_send.at[which, turn],
            part_recv.at[which, turn], sibling,
        )

    def share(which, turn, part):
        now = pl.ds(pl.multiple_of(turn * tile, tile), tile)
        psend[which, now, :] = part.astype(b16)
        part_copy(which, turn).start()

    def collect(which, turn):
        now = pl.ds(pl.multiple_of(turn * tile, tile), tile)
        part_copy(which, turn).wait()
        return psend[which, now, :].astype(f32) + precv[which, now, :].astype(f32)

    def feed_tile(layer, turn):
        keep = kept[layer]
        now = pl.ds(pl.multiple_of(turn * tile, tile), tile)
        x = first[now, :].astype(f32) if layer == 0 else state[now, :]
        summed = x + collect(2 * layer, turn) + out_bias[layer : layer + 1, :]
        keep["z1"][now, :] = summed
        unit, unused = norm_parts(summed)
        normal = unit * gains[layer, 0:1, :] + shifts[layer, 0:1, :]
        hidden[now, :] = normal
        low = normal.astype(b16)
        keep["hrt"][:, now] = low.astype(f32).T.astype(b16)
        size = min(256, quarter)
        for at in range(0, 2 * quarter, size):
            block, start = at // quarter, at % quarter
            bias = up_bias[
                layer : layer + 1,
                pl.ds(pl.multiple_of((2 * block + core) * quarter + start, size), size),
            ]
            inner = dot(low, wup[layer, :, at : at + size]) + bias
            phi, slope = gelu_parts(inner)
            keep["act"][now, at : at + size] = (inner * phi).astype(b16)
            keep["slope"][now, at : at + size] = slope.astype(b16)
        total = dot(keep["act"][now, :], wdown[layer])
        share(2 * layer + 1, turn, total)

    def norm_tile(layer, turn):
        keep = kept[layer]
        now = pl.ds(pl.multiple_of(turn * tile, tile), tile)
        summed = hidden[now, :] + collect(2 * layer + 1, turn) + down_bias[layer : layer + 1, :]
        keep["z2"][now, :] = summed
        unit, unused = norm_parts(summed)
        result = unit * gains[layer, 1:2, :] + shifts[layer, 1:2, :]
        if layer < layers - 1:
            state[now, :] = result
            kept[layer + 1]["xall"][now, :] = result.astype(b16)
        else:
            low_out[now, :] = result.astype(b16)

    saves = []

    def save(layer, names):
        for name in names:
            copy = pltpu.make_async_copy(
                kept[layer][name], stored[layer][name], save_sem.at[layer, KEPT.index(name)]
            )
            copy.start()
            saves.append(copy)

    for layer in range(layers):
        x_all = kept[layer]["xall"]
        if layer == 0:
            for turn in range(held):
                to_sibling(x_all, turn, core, 0, sib_send.at[turn], sib_recv.at[turn]).wait_send()
                to_sibling(x_all, turn, 1 - core, 0, sib_send.at[turn], sib_recv.at[turn]).wait_recv()
                key_tile(layer, turn * tile)
                query_tile(layer, turn * tile)
        else:
            for copy in loads[layer]:
                copy.wait()

            def own_tile(turn):
                key_tile(layer, turn * tile)
                query_tile(layer, turn * tile)

            loop(held, own_tile)
        for shift in range(lines):
            if shift > 0:
                for turn in range(held):
                    to_line(layer, turn, shift).wait()
                    to_sibling(
                        x_all, turn, core, shift,
                        pass_send.at[layer, turn, shift - 1], pass_recv.at[layer, turn, shift - 1],
                    ).start()
                for turn in range(held):
                    send = pass_send.at[layer, turn, shift - 1]
                    receive = pass_recv.at[layer, turn, shift - 1]
                    to_sibling(x_all, turn, core, shift, send, receive).wait_send()
                    to_sibling(x_all, turn, 1 - core, shift, send, receive).wait_recv()
                    key_tile(layer, shift * rows + turn * tile)
            if shift == lines - 1:
                save(layer, ("xall", "kx", "v", "q"))
                if layer == 0:
                    cot_start()

            attend_block(layer, shift)
        loop(held, functools.partial(project_tile, layer))
        save(layer, ("ot", "lse", "o"))
        loop(held, functools.partial(feed_tile, layer))
        save(layer, ("z1", "hrt", "act", "slope"))
        for turn in range(held):
            norm_tile(layer, turn)
            if layer < layers - 1:
                for shift in range(1, lines):
                    to_line(layer + 1, turn, shift).start()
        save(layer, ("z2",))

    def out_copies(turn, place):
        mine = low_out.at[block_at(turn, core)]
        own = pltpu.make_async_copy(mine, place, out_sem.at[turn])
        return own, remote(mine, place, out_send.at[turn], out_recv.at[turn], geo.origin(turn, core))

    for turn in range(held):
        own, there = out_copies(turn, out_tokens.at[geo.parity])
        pl.when(geo.blocked(turn))(own.start)
        pl.when(jnp.logical_not(geo.blocked(turn)))(there.start)
    cot_wait()
    for turn in range(held):
        own, there = out_copies(turn, out_tokens.at[(geo.post + turn) % held])
        pl.when(geo.blocked(turn))(own.wait)
        pl.when(jnp.logical_not(geo.blocked(turn)))(there.wait)
    for copy in saves:
        copy.wait()


def forward(geo, layers, tokens, cotangent, lengths, weights, vectors):
    width, rows, half, ffn = geo.width, geo.rows, geo.half, geo.ffn
    shapes = kept_shapes(geo)
    any_spec = pl.BlockSpec(memory_space=pl.ANY)
    vmem_spec = pl.BlockSpec(memory_space=pltpu.VMEM)
    out_shape = [
        jax.ShapeDtypeStruct(tokens.shape, b16),
        jax.ShapeDtypeStruct((rows, width), b16),
    ]
    out_shape += [jax.ShapeDtypeStruct(*shapes[name]) for unused in range(layers) for name in KEPT]
    scratch = [pltpu.VMEM(*shapes[name]) for unused in range(layers) for name in KEPT]
    scratch += [
        pltpu.VMEM((layers, width, half), b16),
        pltpu.VMEM((layers, width, 2 * half), b16),
        pltpu.VMEM((layers, half, width), b16),
        pltpu.VMEM((layers, width, 2 * geo.quarter), b16),
        pltpu.VMEM((layers, 2 * geo.quarter, width), b16),
        pltpu.VMEM((geo.heads, 2 * LANES, rows), b16),
        pltpu.VMEM((half, geo.count), b16),
        pltpu.VMEM((rows, width), f32),
        pltpu.VMEM((rows, width), f32),
        pltpu.VMEM((rows, width), b16),
        pltpu.VMEM((8, LANES), jnp.int32),
        pltpu.VMEM((8, LANES), jnp.int32),
        pltpu.VMEM((2 * layers, rows, width), b16),
        pltpu.VMEM((2 * layers, rows, width), b16),
        pltpu.VMEM((geo.heads, 8, rows), f32),
    ]
    held, lines = geo.held, max(geo.lines - 1, 1)
    dma = pltpu.SemaphoreType.DMA
    scratch += [dma(shape) for shape in (
        (layers, 8), (layers, len(KEPT)), (held,), (held,), (held,),
        (held, CORES), (held, CORES), (held, CORES), (held,), (held,),
        (layers, held, lines), (layers, held, lines), (layers, held, lines), (layers, held, lines),
        (2 * layers, held), (2 * layers, held), (held,), (held,), (held,), (2,),
    )]
    results = pl.pallas_call(
        functools.partial(forward_kernel, geo, layers),
        out_shape=out_shape,
        in_specs=[any_spec] * 6 + [pl.BlockSpec(memory_space=pltpu.SMEM)] + [vmem_spec] * 6,
        out_specs=[any_spec] * len(out_shape),
        scratch_shapes=scratch,
        compiler_params=pltpu.CompilerParams(
            collective_id=0, has_side_effects=True, vmem_limit_bytes=VMEM
        ),
        cost_estimate=pl.CostEstimate(flops=3 * 10**10, bytes_accessed=4 * 10**7, transcendentals=0),
    )(tokens, cotangent, *weights, lengths, *vectors)
    count = len(KEPT)
    kept = [
        dict(zip(KEPT, results[2 + layer * count : 2 + (layer + 1) * count]))
        for layer in range(layers)
    ]
    return results[0], results[1], kept


QUERY_BIAS, VALUE_BIAS, UP_BIAS, OUT_BIAS, DOWN_BIAS, GAIN, SHIFT = 0, 1, 2, 6, 7, 8, 10
SUMS = 16
UP, DOWN = 0, 1
INTO, PROJ = 0, 1
PAIRS = ("pair0", "pair1", "pair2")
UP_AFTER = (None, 0)


def backward_kernel(geo, layers, *refs):
    refs = list(refs)

    def take(count):
        taken = refs[:count]
        del refs[:count]
        return taken

    cot_rows, w_in, w_out, w_up, w_down = take(5)
    stored = [dict(zip(KEPT, take(len(KEPT)))) for unused in range(layers)]
    (gains,) = take(1)
    grad_tokens, sums = take(2)
    if geo.aligned:
        feed_out, attend_out = take(2)
    else:
        plain = [take(6) for unused in range(layers)]
    keep = dict(zip(KEPT, take(len(KEPT))))
    wq, wkv, wout, wup, wdown = take(5)
    (o_there, low_grad, turned, du_there, psend, precv, do, qx, dox, dq, dkv, dq_there,
     dkv_there, probs_all, grads_all, do_stack, q_stack, dqt, mine_dx, dx_send, dx_recv, line_in) = take(22)
    (load_sem, o_send, o_recv, du_send, du_recv, part_send, part_recv, qkv_send, qkv_recv,
     dx_ssem, dx_rsem, line_send, line_recv, more_send, more_recv, tok_sem, tok_send,
     tok_recv, plain_sem) = take(19)
    if geo.aligned:
        (other, mine, from_x, y_first, y_last, z_first, z_last, into_cell, proj_cell, into_y, proj_y, into_z, proj_z,
         a_send, a_x, sum_in) = take(16)
        from_y, from_z = (y_first, y_last), (z_first, z_last)
        cells = [[into_cell] * layers, [proj_cell.at[layer] for layer in range(layers)]]
        cells_y, cells_z = (into_y, proj_y), (into_z, proj_z)
        (fx_send, fx_recv, fy_send, fy_recv, fz_send, fz_recv, ay_send, ay_recv, az_send, az_recv,
         ax_send, ax_recv, sum_send, sum_recv) = take(14)
        (credit,) = take(1)

    geo = duplicate(geo)
    geo.locate()
    core, tile, slots = geo.core, geo.tile, geo.slots
    held, lines, rows, width, half = geo.held, geo.lines, geo.rows, geo.width, geo.half
    quarter, pairs, posts, depth = geo.quarter, geo.pairs, geo.posts, geo.depth
    post, line, column = geo.post, geo.line, geo.column
    unit = width // geo.seq_size
    sibling = geo.sibling()

    def tile_at(turn):
        return pl.ds(pl.multiple_of(turn * tile, tile), tile)

    def block_at(turn, who, shift=0):
        start = shift * rows + turn * tile + who * slots
        return pl.ds(start if isinstance(start, int) else pl.multiple_of(start, slots), slots)

    NAMES = KEPT + ("win", "wout", "wup", "wdown", "cot")

    def load_copies(layer, name):
        where = load_sem.at[layer, NAMES.index(name)]
        if name == "win":
            targets = (wq, wkv.at[:, :half], wkv.at[:, half:])
            return [
                pltpu.make_async_copy(
                    w_in.at[layer, :, pl.ds(pl.multiple_of((kind * CORES + core) * half, half), half)],
                    targets[kind], load_sem.at[layer, len(NAMES) + kind],
                )
                for kind in range(3)
            ]
        if name == "wout":
            at = pl.ds(pl.multiple_of(core * half, half), half)
            return [pltpu.make_async_copy(w_out.at[layer, at, :], wout, where)]
        if name in ("wup", "wdown"):
            copies = []
            for block in range(2):
                at = pl.ds(pl.multiple_of((2 * block + core) * quarter, quarter), quarter)
                slot = len(NAMES) + 3 + 2 * (name == "wdown") + block
                if name == "wup":
                    pair = w_up.at[layer, :, at], wup.at[:, block * quarter : (block + 1) * quarter]
                else:
                    pair = w_down.at[layer, at, :], wdown.at[block * quarter : (block + 1) * quarter, :]
                copies.append(pltpu.make_async_copy(*pair, load_sem.at[layer, slot]))
            return copies
        if name == "hrt" and geo.aligned:
            return [
                pltpu.make_async_copy(
                    stored[layer][name].at[pl.ds(pl.multiple_of((2 * which + core) * depth, depth), depth), :],
                    keep[name].at[which * depth : (which + 1) * depth, :],
                    load_sem.at[layer, len(NAMES) + 7 + which],
                )
                for which in range(2)
            ]
        if name == "cot":
            return [pltpu.make_async_copy(cot_rows, low_grad, where)]
        return [pltpu.make_async_copy(stored[layer][name], keep[name], where)]

    def load(layer, *names):
        for name in names:
            for copy in load_copies(layer, name):
                copy.start()

    def loaded(layer, *names):
        for name in names:
            for copy in load_copies(layer, name):
                copy.wait()

    top = layers - 1
    load(top, "z2", "cot", "wdown", "slope", "wup", "act", "z1", "wout", "q", "kx", "v", "ot",
         "lse", "win", "hrt", "xall", "o")

    sources = [geo.origin(turn, who) for turn in range(held) for who in range(CORES)]
    goals = [geo.goal(turn) for turn in range(held)]
    near = [sibling] + [geo.on_line(shift) for shift in range(1, lines)]
    if geo.aligned:
        near += [geo.on_post(shift) for shift in range(1, posts)]
        near += [geo.on_column(shift) for shift in range(1, geo.columns)]
    goals = goals + [(device[0] + 1 - 2 * (device[0] % CORES), device[1]) for device in goals]
    meet(geo, near + sources + goals)

    def o_copy(layer):
        return remote(stored[layer]["o"], o_there, o_send.at[layer], o_recv.at[layer], sibling)

    def clear(at):
        qx[at] = jnp.zeros(qx.shape[1:], b16)
        dox[at] = jnp.zeros(dox.shape[1:], b16)

    loop(2, clear)
    sums[...] = jnp.zeros_like(sums)

    def add_sum(layer, row, lanes, value):
        sums[layer, pl.ds(row, 1), lanes] += value

    everywhere = slice(None)


    def x_copy(layer, kind, z):
        return remote(
            other.at[kind, z], from_x.at[kind, z], fx_send.at[layer, kind, z],
            fx_recv.at[layer, kind, z], geo.on_column(1),
        )

    pair_post = post + 1 - 2 * (post % 2)
    far_post = (post + 2) % posts

    def order(step):
        return (pair_post + step // 2 * (far_post - pair_post) + step % 2 * 2) % posts

    def at_post(which):
        return geo.clip, which * lines + line

    def y_copy(layer, kind, z, shift):
        there = from_y[layer].at[kind, shift - 1] if layer else from_y[layer].at[kind, z, shift - 1]
        at = 0 if layer else z
        return remote(
            mine.at[layer, kind, z, (line + shift) % lines], there,
            fy_send.at[layer, kind, at, shift - 1], fy_recv.at[layer, kind, at, shift - 1],
            geo.on_line(shift),
        )

    def z_copy(layer, kind, hop):
        block = mine.at[layer, kind, order(hop)]
        return remote(
            block if layer else block.at[line], from_z[layer].at[kind, hop],
            fz_send.at[layer, kind, hop], fz_recv.at[layer, kind, hop],
            at_post(far_post if hop == 2 else pair_post),
        )

    def land_x(layer, kind, step):
        z = order(step)
        x_copy(layer, kind, z).wait()
        total = mine[layer, kind, z].astype(f32) + from_x[kind, z].astype(f32)
        mine[layer, kind, z] = total.astype(b16)
        if layer == 0:
            for shift in range(1, lines):
                y_copy(layer, kind, z, shift).start()
            return
        if step < 2:
            z_copy(layer, kind, step).start()
        if step == posts - 1:
            device = geo.on_column(1)
            pl.semaphore_signal(
                credit.at[kind], inc=1, device_id=device, device_id_type=pl.DeviceIdType.MESH
            )

    def land_y(layer, kind, step):
        z = order(step)
        total = mine[layer, kind, z, line].astype(f32)
        for shift in range(1, lines):
            y_copy(layer, kind, z, shift).wait()
            total = total + from_y[layer][kind, z, shift - 1].astype(f32)
        mine[layer, kind, z, line] = total.astype(b16)
        if step < 2:
            z_copy(layer, kind, step).start()

    def land_near(layer, kind):
        z_copy(layer, kind, 1).wait()
        here = (layer, kind, far_post) if layer else (layer, kind, far_post, line)
        total = mine[here].astype(f32) + from_z[layer][kind, 1].astype(f32)
        mine[here] = total.astype(b16)
        z_copy(layer, kind, 2).start()

    def land_far(layer, kind):
        here = (layer, kind, post) if layer else (layer, kind, post, line)
        total = mine[here].astype(f32)
        for hop in (0, 2):
            z_copy(layer, kind, hop).wait()
            total = total + from_z[layer][kind, hop].astype(f32)
        if layer == 0:
            feed_out[layer, kind] = total
            return
        mine[here] = total.astype(b16)
        for shift in range(1, lines):
            y_copy(layer, kind, post, shift).start()

    def land_end(layer, kind):
        total = mine[layer, kind, post, line].astype(f32)
        for shift in range(1, lines):
            y_copy(layer, kind, post, shift).wait()
            total = total + from_y[layer][kind, shift - 1].astype(f32)
        feed_out[layer, kind] = total

    def ay_copy(layer, kind, z, shift):
        return remote(
            cells[kind][layer].at[(line + shift) % lines, z], cells_y[kind].at[layer, z, shift - 1],
            ay_send.at[layer, kind, z, shift - 1], ay_recv.at[layer, kind, z, shift - 1],
            geo.on_line(shift),
        )

    def az_copy(layer, kind, hop):
        return remote(
            cells[kind][layer].at[line, order(hop)], cells_z[kind].at[layer, hop],
            az_send.at[layer, kind, hop], az_recv.at[layer, kind, hop],
            at_post(far_post if hop == 2 else pair_post),
        )

    def ax_copy(layer, kind):
        span = slice(0, 3 * unit) if kind == INTO else slice(3 * unit, 4 * unit)
        return remote(
            a_send.at[layer, span], a_x.at[layer, span], ax_send.at[layer, kind],
            ax_recv.at[layer, kind], geo.on_column(1),
        )

    def send_ay(layer, kind):
        for step in range(posts):
            for shift in range(1, lines):
                ay_copy(layer, kind, order(step), shift).start()

    def land_ay(layer, kind, step):
        z = order(step)
        cell = cells[kind][layer]
        total = cell[line, z].astype(f32)
        for shift in range(1, lines):
            ay_copy(layer, kind, z, shift).wait()
            total = total + cells_y[kind][layer, z, shift - 1].astype(f32)
        cell[line, z] = total.astype(b16)
        if step < 2:
            az_copy(layer, kind, step).start()

    def land_anear(layer, kind):
        cell = cells[kind][layer]
        az_copy(layer, kind, 1).wait()
        total = cell[line, far_post].astype(f32) + cells_z[kind][layer, 1].astype(f32)
        cell[line, far_post] = total.astype(b16)
        az_copy(layer, kind, 2).start()

    def land_afar(layer, kind):
        total = cells[kind][layer][line, post].astype(f32)
        for hop in (0, 2):
            az_copy(layer, kind, hop).wait()
            total = total + cells_z[kind][layer, hop].astype(f32)
        low, high = total[:, :depth], total[:, depth:]
        span = slice(0, 3 * unit) if kind == INTO else slice(3 * unit, 4 * unit)
        attend_out[layer, span] = jnp.where(column == 0, low, high)
        a_send[layer, span] = jnp.where(column == 0, high, low).astype(b16)
        ax_copy(layer, kind).start()

    def land_ax(layer, kind):
        ax_copy(layer, kind).wait()
        span = slice(0, 3 * unit) if kind == INTO else slice(3 * unit, 4 * unit)
        attend_out[layer, span] = attend_out[layer, span] + a_x[layer, span].astype(f32)

    def sum_copies(layer, hop):
        near = ([sibling], [geo.on_line(shift) for shift in range(1, lines)],
                [at_post(pair_post)], [at_post(far_post)], [geo.on_column(1)])
        first = (0, 1, lines, lines + 1, lines + 2)[hop]
        return [
            (remote(
                sums.at[layer], sum_in.at[layer, first + at], sum_send.at[layer, first + at],
                sum_recv.at[layer, first + at], device,
            ), first + at)
            for at, device in enumerate(near[hop])
        ]

    def start_sum(layer):
        shared = lax.broadcasted_iota(jnp.int32, sums.shape[1:], 0) >= OUT_BIAS
        sums[layer] = jnp.where(shared, 0.5 * sums[layer], sums[layer])
        for copy, unused in sum_copies(layer, 0):
            copy.start()

    def land_sum(layer, hop):
        total = sums[layer]
        for copy, at in sum_copies(layer, hop):
            copy.wait()
            total = total + sum_in[layer, at]
        sums[layer] = total
        if hop < 4:
            for copy, unused in sum_copies(layer, hop + 1):
                copy.start()

    schedule = {
        (1, "pair0"): (
            (land_ay, 1, PROJ, 0),
        ),
        (1, "up"): (
            (land_ay, 1, PROJ, 1),
        ),
        (1, "pair1"): (
            (land_ay, 1, PROJ, 2), (land_anear, 1, PROJ), (land_x, 1, DOWN, 1),
        ),
        (1, "dx"): (
            (land_x, 1, DOWN, 0),
        ),
        (1, "own"): (
            (land_ay, 1, PROJ, 3), (land_x, 1, DOWN, 2), (land_x, 1, DOWN, 3), (land_sum, 1, 0),
            (land_near, 1, DOWN),
        ),
        (1, "into"): (
            (land_x, 1, UP, 0),
        ),
        (0, "feed"): (
            (land_sum, 1, 1), (land_x, 1, UP, 1), (land_ay, 1, INTO, 0),
        ),
        (0, "down"): (
            (land_far, 1, DOWN), (land_afar, 1, PROJ), (land_x, 1, UP, 2), (land_ay, 1, INTO, 1),
            (land_sum, 1, 2), (land_x, 1, UP, 3),
        ),
        (0, "proj"): (
            (land_ay, 1, INTO, 2),
        ),
        (0, "pair0"): (
            (land_end, 1, DOWN), (land_near, 1, UP), (land_x, 0, DOWN, 0), (land_ay, 1, INTO, 3),
            (land_ay, 0, PROJ, 0), (land_x, 0, DOWN, 1),
        ),
        (0, "pair1"): (
            (land_sum, 1, 3), (land_ay, 0, PROJ, 2), (land_anear, 1, INTO), (land_x, 0, DOWN, 2),
            (land_ay, 0, PROJ, 3), (land_ay, 0, PROJ, 1),
        ),
        (0, "pair2"): (
            (land_y, 0, DOWN, 1), (land_x, 0, DOWN, 3), (land_y, 0, DOWN, 0),
        ),
        (0, "dx"): (
            (land_ax, 1, PROJ), (land_far, 1, UP), (land_y, 0, DOWN, 2),
        ),
        (0, "own"): (
            (land_y, 0, DOWN, 3), (land_near, 0, DOWN), (land_x, 0, UP, 0),
            (land_anear, 0, PROJ), (land_sum, 0, 0), (land_end, 1, UP), (land_afar, 1, INTO),
        ),
        (0, "into"): (
            (land_x, 0, UP, 1),
        ),
        (0, "end"): (
            (land_far, 0, DOWN), (land_y, 0, UP, 0), (land_x, 0, UP, 2), (land_x, 0, UP, 3),
            (land_sum, 0, 1), (land_sum, 1, 4), (land_ay, 0, INTO, 0), (land_ay, 0, INTO, 1),
            (land_afar, 0, PROJ), (land_ay, 0, INTO, 2), (land_sum, 0, 2), (land_ax, 1, INTO),
            (land_anear, 0, INTO), (land_ay, 0, INTO, 3), (land_sum, 0, 3), (land_sum, 0, 4),
            (land_y, 0, UP, 1), (land_ax, 0, PROJ), (land_y, 0, UP, 2), (land_near, 0, UP),
            (land_afar, 0, INTO), (land_ax, 0, INTO), (land_y, 0, UP, 3), (land_far, 0, UP),
        ),
    }

    def progress(layer, phase):
        if geo.aligned:
            for function, *given in schedule.get((layer, phase), ()):
                function(*given)


    def part_copy(layer, turn):
        return remote(
            psend.at[tile_at(turn), :], precv.at[tile_at(turn), :], part_send.at[layer, turn],
            part_recv.at[layer, turn], sibling,
        )

    def du_copy(layer, turn):
        return remote(
            keep["slope"].at[tile_at(turn), :], du_there.at[tile_at(turn), :],
            du_send.at[layer, turn], du_recv.at[layer, turn], sibling,
        )

    def norm_grads(layer, which, values, grad):
        unit, inverse = norm_parts(values)
        gain = gains[layer, which : which + 1, :]
        back, gain_grad, shift_grad = norm_back(unit, inverse, gain, grad)
        add_sum(layer, GAIN + which, everywhere, gain_grad)
        add_sum(layer, SHIFT + which, everywhere, shift_grad)
        return back

    def feed_back_tile(layer, turn):
        now = tile_at(turn)
        grad = low_grad[now, :].astype(f32)
        if layer < top:
            grad = grad + keep["z1"][now, :]
        back = norm_grads(layer, 1, keep["z2"][now, :], grad)
        keep["z2"][now, :] = back
        low = back.astype(b16)
        wide = low.astype(f32)
        turned[:, now] = wide.T.astype(b16)
        add_sum(layer, DOWN_BIAS, everywhere, jnp.sum(wide, 0, keepdims=True))
        size = min(256, quarter)
        for at in range(0, 2 * quarter, size):
            block, start = at // quarter, at % quarter
            lanes = slice(at, at + size)
            grads = dot_nt(low, wdown[lanes, :])
            grads = (grads * keep["slope"][now, lanes].astype(f32)).astype(b16)
            keep["slope"][now, lanes] = grads
            add_sum(
                layer, UP_BIAS + 2 * block + core, slice(start, start + size),
                jnp.sum(grads.astype(f32), 0, keepdims=True),
            )
        total = dot_nt(keep["slope"][now, :], wup[...])
        psend[now, :] = total.astype(b16)
        part_copy(layer, turn).start()
        du_copy(layer, turn).start()

    def down_grads(layer, which, start):
        lanes = pl.ds(pl.multiple_of(which * quarter, quarter), quarter)
        size = lines * unit

        def chunk(at):
            steps = (2 * at, 2 * at + 1)
            left = [
                turned[pl.ds(pl.multiple_of(order(step) * size, size), size), :] for step in steps
            ]
            result = dot(jnp.concatenate(left, 0), keep["act"][:, lanes]).astype(b16)
            for index, step in enumerate(steps):
                z = order(step)
                for row in range(lines):
                    top = index * size + row * unit
                    for piece in range(2):
                        block = result[
                            top : top + unit, piece * quarter // 2 : (piece + 1) * quarter // 2
                        ]
                        span = slice(piece * unit, (piece + 1) * unit)
                        if start:
                            other[DOWN, z, row, span, :] = block
                        else:
                            mine[layer, DOWN, z, row, span, :] = block
                if start:
                    x_copy(layer, DOWN, z).start()

        loop(posts // 2, chunk)

    def up_grads(layer):
        left = [
            keep["hrt"][pl.ds(pl.multiple_of(which * depth, depth), depth), :]
            for which in (1 - column, column)
        ]
        left = jnp.concatenate(left, 0)
        size = quarter // lines
        for block in range(2):
            lanes = slice(block * quarter, (block + 1) * quarter)
            for there, array in ((0, keep["slope"]), (1, du_there)):
                z = 2 * block + core + there * (1 - 2 * core)
                result = dot(left, array[:, lanes]).astype(b16)
                for row in range(lines):
                    span = slice(row * size, (row + 1) * size)
                    other[UP, z, row] = result[:depth, span]
                    mine[layer, UP, z, row] = result[depth:, span]
        for step in range(posts):
            x_copy(layer, UP, order(step)).start()

    def feed_grads(layer, kind):
        if layer < top:
            pl.semaphore_wait(credit.at[kind], 1)
        if kind == UP:
            loaded(layer, "hrt")
            for turn in range(held):
                du_copy(layer, turn).wait()
            up_grads(layer)
        else:
            down_grads(layer, 1 - column, True)
            down_grads(layer, column, False)

    def proj_back_tile(layer, turn):
        now = tile_at(turn)
        part_copy(layer, turn).wait()
        grad = keep["z2"][now, :] + (psend[now, :].astype(f32) + precv[now, :].astype(f32))
        back = norm_grads(layer, 0, keep["z1"][now, :], grad)
        keep["z1"][now, :] = back
        low = back.astype(b16)
        wide = low.astype(f32)
        turned[:, now] = wide.T.astype(b16)
        add_sum(layer, OUT_BIAS, everywhere, jnp.sum(wide, 0, keepdims=True))
        do[now, :] = dot_nt(low, wout[...]).astype(b16)

    lane_head = lax.broadcasted_iota(jnp.int32, (tile, LANES), 1) // HEAD_DIM

    def attend_back_pair(layer, pair):
        lanes = pl.ds(pl.multiple_of(pair * LANES, LANES), LANES)
        key_t = keep["kx"][pair, :, :LANES].astype(f32).T.astype(b16)
        query_t = keep["q"][:, lanes].astype(f32).T.astype(b16)
        grad_t = do[:, lanes].astype(f32).T.astype(b16)
        for head in range(2):
            here = slice(head * HEAD_DIM, (head + 1) * HEAD_DIM)
            qx[head, here, :] = query_t[here]
            dox[head, here, :] = grad_t[here]
            rest = -keep["lse"][2 * pair + head, 0:1, :]
            row = lax.broadcasted_iota(jnp.int32, (16, rows), 0)
            extra = jnp.where(row == 0, 1.0, 0.0)
            for part in range(1, 4):
                piece = rest.astype(b16).astype(f32)
                rest = rest - piece
                extra = jnp.where(row == part, piece, extra)
            qx[head, LANES : LANES + 16, :] = extra.astype(b16)

        def turn_step(turn):
            now = tile_at(turn)
            query = keep["q"][now, lanes].astype(f32)
            outgrad = do[now, lanes].astype(f32)
            for head in range(2):
                here = slice(head * HEAD_DIM, (head + 1) * HEAD_DIM)
                chosen = (lane_head == head).astype(f32)
                place = pl.ds(pl.multiple_of((2 * turn + head) * tile, tile), tile)
                do_stack[place, :] = (outgrad * chosen).astype(b16)
                q_stack[place, :] = (query * chosen).astype(b16)
                scores = dot(keep["kx"][pair], qx[head, :, now])
                probs = jnp.exp(scores)
                probs_all[:, place] = probs.astype(b16)
                grads = dot(keep["v"][:, lanes], dox[head, :, now])
                own = pl.ds(pl.multiple_of(pair * LANES + head * HEAD_DIM, HEAD_DIM), HEAD_DIM)
                delta = jnp.sum(
                    dox[head, here, now].astype(f32) * keep["ot"][own, now], 0, keepdims=True
                )
                score_grads = (probs * (grads - delta)).astype(b16)
                grads_all[:, place] = score_grads
                dqt[here, now] = dot(key_t[here], score_grads)

        loop(held, turn_step)
        query_grad = (dqt[...].T * SCALE).astype(b16)
        value_grad = dot(probs_all[...], do_stack[...]).astype(b16)
        dq[:, lanes] = query_grad
        dkv[:, lanes] = dot(grads_all[...], q_stack[...]).astype(b16)
        dkv[:, pl.ds(pl.multiple_of(half + pair * LANES, LANES), LANES)] = value_grad
        spot = pl.ds(pl.multiple_of(core * half + pair * LANES, LANES), LANES)
        add_sum(layer, QUERY_BIAS, spot, jnp.sum(query_grad.astype(f32), 0, keepdims=True))
        add_sum(layer, VALUE_BIAS, spot, jnp.sum(value_grad.astype(f32), 0, keepdims=True))

    def qkv_copies(layer):
        return [
            remote(source, target, qkv_send.at[layer, at], qkv_recv.at[layer, at], sibling)
            for at, (source, target) in enumerate(((dq, dq_there), (dkv, dkv_there)))
        ]

    def dx_copy(layer, shift, turn):
        return remote(
            dx_send.at[shift * held + turn], dx_recv.at[shift * held + turn],
            dx_ssem.at[layer, shift * held + turn], dx_rsem.at[layer, shift * held + turn], sibling,
        )

    def dx_tile(layer, shift, turn):
        now = pl.ds(pl.multiple_of(shift * rows + turn * tile, tile), tile)
        total = dot_nt(dkv[now, :], wkv[...])
        if shift == 0:
            total = total + dot_nt(dq[now, :], wq[...])
        first, second = total[:slots], total[slots:]
        mine_dx[shift * held + turn] = jnp.where(core == 0, first, second).astype(b16)
        dx_send[shift * held + turn] = jnp.where(core == 0, second, first).astype(b16)
        dx_copy(layer, shift, turn).start()

    def line_copy(layer, shift, turn):
        return remote(
            dx_recv.at[shift * held + turn], line_in.at[layer, shift - 1, turn],
            line_send.at[layer, shift - 1, turn], line_recv.at[layer, shift - 1, turn],
            geo.on_line(lines - shift),
        )

    def more_copy(layer, turn, who):
        place = low_grad.at[block_at(turn, who)]
        return remote(place, place, more_send.at[layer, turn], more_recv.at[layer, turn], sibling)

    def token_copies(turn, place):
        own = pltpu.make_async_copy(low_grad.at[block_at(turn, core)], place, tok_sem.at[turn])
        there = remote(
            low_grad.at[block_at(turn, core)], place, tok_send.at[turn], tok_recv.at[turn],
            geo.origin(turn, core),
        )
        return own, there

    def mine_lanes(x):
        cuts = [x[:, at * depth : (at + 1) * depth] for at in range(2 * CORES)]
        return jnp.where(
            core == 0, jnp.concatenate([cuts[0], cuts[2]], 1), jnp.concatenate([cuts[1], cuts[3]], 1)
        )

    def into_grads(layer):
        units = half // unit
        x = mine_lanes(keep["xall"][...])
        for first, pair in ((0, (dq, dq_there)), (1, (dkv, dkv_there))):
            for there, ref in enumerate(pair):
                owner = core + there * (1 - 2 * core)
                count = ref.shape[0]
                result = dot_tn(ref[...], x[:count]).astype(b16)
                for at in range(result.shape[0] // unit):
                    kind = first + at // units
                    index = (2 * kind + owner) * units + at % units
                    seq = index // 3
                    where = pl.ds(pl.multiple_of(index % 3 * unit, unit), unit)
                    into_cell[seq % lines, seq // lines, where, :] = result[at * unit : (at + 1) * unit]
        send_ay(layer, INTO)

    def proj_grads(layer):
        here, there = keep["o"][...], o_there[...]
        features = jnp.where(
            core == 0,
            jnp.concatenate([here[:, :depth], there[:, :depth]], 1),
            jnp.concatenate([there[:, depth:], here[:, depth:]], 1),
        )
        result = dot(turned[...], features).astype(b16)
        for seq in range(geo.seq_size):
            proj_cell[layer, seq % lines, seq // lines] = result[seq * unit : (seq + 1) * unit]
        send_ay(layer, PROJ)

    def plain_out(layer, names):
        sources = {"du": keep["slope"], "dft": turned, "dat": turned, "dq": dq, "dk": dkv.at[:, :half], "dv": dkv.at[:, half:]}
        order = ("du", "dft", "dat", "dq", "dk", "dv")
        copies = [
            pltpu.make_async_copy(sources[name], plain[layer][order.index(name)], plain_sem.at[order.index(name)])
            for name in names
        ]
        for copy in copies:
            copy.start()
        for copy in copies:
            copy.wait()

    for layer in range(layers - 1, -1, -1):
        last = layer == 0
        below = layer - 1
        if layer == top:
            loaded(layer, "cot")
        else:
            for turn in range(held):
                more_copy(layer + 1, turn, core).wait_send()
                more_copy(layer + 1, turn, 1 - core).wait_recv()
        o_copy(layer).start()
        loaded(layer, "z2", "wdown", "slope", "wup")
        loop(held, functools.partial(feed_back_tile, layer))
        progress(layer, "feed")
        if not last:
            load(below, "wdown", "wup")
        else:
            load(layer, "z1")
        loaded(layer, "act")
        if geo.aligned:
            feed_grads(layer, DOWN)
            progress(layer, "down")
            if UP_AFTER[layer] is None:
                feed_grads(layer, UP)
                progress(layer, "up")
        else:
            plain_out(layer, ("dft",))
        if not last:
            load(below, "act")
        loaded(layer, "z1", "wout")
        loop(held, functools.partial(proj_back_tile, layer))
        progress(layer, "proj")
        if not last:
            load(below, "wout", "z2")
        if geo.aligned:
            loaded(layer, "o")
            o_copy(layer).wait()
            proj_grads(layer)
        loaded(layer, "q", "kx", "v", "ot", "lse")
        for pair in range(pairs):
            attend_back_pair(layer, pair)
            progress(layer, PAIRS[pair])
            if geo.aligned and pair == UP_AFTER[layer]:
                feed_grads(layer, UP)
                progress(layer, "up")
        if not last:
            load(below, "q", "kx", "v", "ot", "lse")
        for copy in qkv_copies(layer):
            copy.start()
        if geo.aligned:
            start_sum(layer)
        loaded(layer, "win")
        for shift in range(1, lines):
            loop(held, functools.partial(dx_tile, layer, shift))
        progress(layer, "dx")
        for shift in range(1, lines):
            for turn in range(held):
                dx_copy(layer, shift, turn).wait()
                at = shift * held + turn
                dx_recv[at] = (mine_dx[at].astype(f32) + dx_recv[at].astype(f32)).astype(b16)
                line_copy(layer, shift, turn).start()
        loop(held, functools.partial(dx_tile, layer, 0))
        progress(layer, "own")
        if not last:
            load(below, "win")
        if geo.aligned:
            for copy in qkv_copies(layer):
                copy.wait()
            loaded(layer, "xall")
            into_grads(layer)
            progress(layer, "into")
        else:
            for turn in range(held):
                du_copy(layer, turn).wait()
            for copy in qkv_copies(layer):
                copy.wait()
            loaded(layer, "hrt", "xall", "o")
            o_copy(layer).wait()
            plain_out(layer, ("du", "dat", "dq", "dk", "dv"))
        if not last:
            load(below, "hrt", "slope", "xall", "o")
        for turn in range(held):
            dx_copy(layer, 0, turn).wait()
            total = mine_dx[turn].astype(f32) + dx_recv[turn].astype(f32)
            for shift in range(1, lines):
                line_copy(layer, shift, turn).wait()
                total = total + line_in[layer, shift - 1, turn].astype(f32)
            if not last:
                low_grad[block_at(turn, core), :] = total.astype(b16)
                more_copy(layer, turn, core).start()
            else:
                total = total + keep["z1"][block_at(turn, core), :]
                low_grad[block_at(turn, core), :] = total.astype(b16)
                own, there = token_copies(turn, grad_tokens.at[geo.parity])
                pl.when(geo.blocked(turn))(own.start)
                pl.when(jnp.logical_not(geo.blocked(turn)))(there.start)

    progress(0, "end")
    for turn in range(held):
        own, there = token_copies(turn, grad_tokens.at[(post + turn) % held])
        pl.when(geo.blocked(turn))(own.wait)
        pl.when(jnp.logical_not(geo.blocked(turn)))(there.wait)


def backward(geo, layers, cot_rows, weights, kept, gains):
    width, rows, half, ffn, count = geo.width, geo.rows, geo.half, geo.ffn, geo.count
    held, lines, posts, slots, quarter = geo.held, geo.lines, geo.posts, geo.slots, geo.quarter
    shapes = kept_shapes(geo)
    any_spec = pl.BlockSpec(memory_space=pl.ANY)
    vmem_spec = pl.BlockSpec(memory_space=pltpu.VMEM)
    unit = width // geo.seq_size
    out = [((held, slots, width), b16), ((layers, SUMS, width), f32)]
    out_specs = [any_spec, vmem_spec]
    if geo.aligned:
        out += [
            ((layers, 2, geo.depth, quarter // lines), f32),
            ((layers, 4 * unit, geo.depth), f32),
        ]
        out_specs += [vmem_spec] * 2
    else:
        for unused in range(layers):
            out += [
                ((rows, ffn // CORES), b16), ((width, rows), b16), ((width, rows), b16),
                ((rows, half), b16), ((count, half), b16), ((count, half), b16),
            ]
            out_specs += [any_spec] * 6
    vmem = pltpu.VMEM
    if geo.aligned:
        shapes["hrt"] = (2 * geo.depth, rows), b16
    scratch = [vmem(*shapes[name]) for name in KEPT]
    scratch += [
        vmem((width, half), b16), vmem((width, 2 * half), b16), vmem((half, width), b16),
        vmem((width, 2 * quarter), b16), vmem((2 * quarter, width), b16),
        vmem((rows, half), b16),
        vmem((rows, width), b16),
        vmem((width, rows), b16),
        vmem((rows, ffn // CORES), b16),
        vmem((rows, width), b16), vmem((rows, width), b16),
        vmem((rows, half), b16),
        vmem((2, 2 * LANES, rows), b16), vmem((2, LANES, rows), b16),
        vmem((rows, half), b16), vmem((count, 2 * half), b16),
        vmem((rows, half), b16), vmem((count, 2 * half), b16),
        vmem((count, 2 * rows), b16), vmem((count, 2 * rows), b16),
        vmem((2 * rows, LANES), b16), vmem((2 * rows, LANES), b16), vmem((LANES, rows), f32),
        vmem((lines * held, slots, width), b16),
        vmem((lines * held, slots, width), b16), vmem((lines * held, slots, width), b16),
        vmem((layers, lines - 1, held, slots, width), b16),
    ]
    dma = pltpu.SemaphoreType.DMA
    scratch += [dma(shape) for shape in (
        (layers, len(KEPT) + 16), (layers,), (layers,), (layers, held), (layers, held),
        (layers, held), (layers, held), (layers, 3), (layers, 3),
        (layers, lines * held), (layers, lines * held),
        (layers, lines - 1, held), (layers, lines - 1, held),
        (layers, held), (layers, held), (held,), (held,), (held,), (6,),
    )]
    if geo.aligned:
        block = (geo.depth, quarter // lines)
        into, proj = (3 * unit, 2 * geo.depth), (unit, 2 * geo.depth)
        hops = lines + 3
        scratch += [
            vmem((2, posts, lines, *block), b16), vmem((layers, 2, posts, lines, *block), b16),
            vmem((2, posts, lines, *block), b16),
            vmem((2, posts, lines - 1, *block), b16), vmem((2, lines - 1, *block), b16),
            vmem((2, 3, *block), b16), vmem((2, 3, lines, *block), b16),
            vmem((lines, posts, *into), b16), vmem((layers, lines, posts, *proj), b16),
            vmem((layers, posts, lines - 1, *into), b16), vmem((layers, posts, lines - 1, *proj), b16),
            vmem((layers, 3, *into), b16), vmem((layers, 3, *proj), b16),
            vmem((layers, 4 * unit, geo.depth), b16), vmem((layers, 4 * unit, geo.depth), b16),
            vmem((layers, hops, SUMS, width), f32),
        ]
        scratch += [dma(shape) for shape in (
            (layers, 2, posts), (layers, 2, posts),
            (layers, 2, posts, lines - 1), (layers, 2, posts, lines - 1),
            (layers, 2, 3), (layers, 2, 3),
            (layers, 2, posts, lines - 1), (layers, 2, posts, lines - 1),
            (layers, 2, 3), (layers, 2, 3), (layers, 2), (layers, 2),
            (layers, hops), (layers, hops),
        )]
        scratch += [pltpu.SemaphoreType.REGULAR((2,))]
    stored = [kept[layer][name] for layer in range(layers) for name in KEPT]
    return pl.pallas_call(
        functools.partial(backward_kernel, geo, layers),
        out_shape=[jax.ShapeDtypeStruct(*shape) for shape in out],
        in_specs=[any_spec] * (5 + len(stored)) + [vmem_spec],
        out_specs=out_specs,
        scratch_shapes=scratch,
        compiler_params=pltpu.CompilerParams(
            collective_id=1, has_side_effects=True, vmem_limit_bytes=VMEM_BACK
        ),
        cost_estimate=pl.CostEstimate(flops=8 * 10**10, bytes_accessed=6 * 10**7, transcendentals=0),
    )(cot_rows, *weights, *stored, gains)


def finish_kernel(
    geo, core_ref, sums_ref, feed_ref, attend_ref, out_in_ref, grad_in_ref,
    out_ref, grad_ref, into_ref, in_bias_ref, proj_ref, out_bias_ref, up_ref, up_bias_ref, down_ref, down_bias_ref,
    gain_ref, shift_ref,
):
    seq = core_ref[0]
    out_ref[...] = out_in_ref[...]
    grad_ref[...] = grad_in_ref[...]
    layers = feed_ref.shape[0]
    unit = geo.width // geo.seq_size
    wide, span = 2 * unit, geo.ffn // geo.seq_size
    per_row, per_quarter = geo.width // wide, geo.quarter // span

    def turn(rows, amount):
        return pltpu.roll(rows, (geo.width - amount) % geo.width, 1)

    for layer in range(layers):
        up_ref[layer] = feed_ref[layer, UP]
        down = feed_ref[layer, DOWN]
        down_ref[layer] = jnp.concatenate([down[:unit], down[unit:]], 1)
        both = attend_ref[layer].T
        into_ref[layer] = both[:, : 3 * unit]
        proj_ref[layer] = both[:, 3 * unit :]
        sums = sums_ref[layer]
        narrow = turn(sums, seq * unit)
        out_bias_ref[layer : layer + 1, :] = narrow[OUT_BIAS : OUT_BIAS + 1, :unit]
        down_bias_ref[layer : layer + 1, :] = narrow[DOWN_BIAS : DOWN_BIAS + 1, :unit]
        gain_ref[layer] = narrow[GAIN : GAIN + 2, :unit]
        shift_ref[layer] = narrow[SHIFT : SHIFT + 2, :unit]
        middle = turn(sums, seq % per_row * wide)
        first = middle[QUERY_BIAS : QUERY_BIAS + 1, :wide]
        second = middle[VALUE_BIAS : VALUE_BIAS + 1, :wide]
        in_bias_ref[layer : layer + 1, :] = jnp.where(seq < per_row, first, second)
        large = turn(sums, seq % per_quarter * span)
        chosen = large[UP_BIAS : UP_BIAS + 1, :span]
        for block in range(1, 4):
            chosen = jnp.where(
                seq // per_quarter == block, large[UP_BIAS + block : UP_BIAS + block + 1, :span], chosen
            )
        up_bias_ref[layer : layer + 1, :] = chosen


def finish(geo, layers, seq, sums, feed_out, attend_out, out_tokens, grad_tokens):
    unit, width = geo.width // geo.seq_size, geo.width
    span = geo.ffn // geo.seq_size
    depth = geo.depth
    shapes = [
        (layers, depth, 3 * unit), (layers, 2 * unit), (layers, depth, unit), (layers, unit),
        (layers, depth, span), (layers, span), (layers, unit, geo.ffn // geo.clip_size),
        (layers, unit), (layers, 2, unit), (layers, 2, unit),
    ]
    results = list(call(
        functools.partial(finish_kernel, geo), seq, 1,
        [all_of(array) for array in (sums, feed_out, attend_out, out_tokens, grad_tokens)],
        [full(out_tokens.shape, b16)] * 2 + [full(shape, f32) for shape in shapes], [],
        10**7, 10**7,
    ))
    results[8] = jnp.swapaxes(results[8], 1, 2)
    return results


def build(mesh):
    clip_size, seq_size = mesh.shape["clip"], mesh.shape["seq"]

    def shards(
        tokens, lengths, attn_in, in_bias, attn_out, out_bias, ffn_in, ffn_in_bias,
        ffn_out, ffn_out_bias, norm_gain, norm_bias, cotangent,
    ):
        layers = attn_in.shape[0]
        geo = Geometry(mesh, tokens, ffn_in.shape[2])
        geo.locate()
        held, width, ffn, half, quarter = geo.held, geo.width, geo.ffn, geo.half, geo.quarter
        aligned, core = geo.aligned, geo.core
        seq_at = geo.seq

        weights = (attn_in, attn_out, ffn_in, ffn_out)
        out_tokens, cot_rows, kept = forward(
            geo, layers, tokens, cotangent, lengths, weights,
            (in_bias, out_bias, ffn_in_bias, ffn_out_bias, norm_gain, norm_bias),
        )
        grad_tokens, sums, *results = backward(geo, layers, cot_rows, weights, kept, norm_gain)
        if aligned:
            seq_arg = jnp.reshape(seq_at, (1,)).astype(jnp.int32)
            return tuple(finish(geo, layers, seq_arg, sums, *results, out_tokens, grad_tokens))

        def swap(array):
            pairs = [(at, at ^ 1) for at in range(clip_size)]
            return lax.ppermute(array, "clip", pairs)

        def spread(array):
            array = lax.psum_scatter(
                array.astype(b16), "seq", scatter_dimension=1, tiled=True
            ).astype(b16)
            return lax.psum_scatter(array, "clip", scatter_dimension=0, tiled=True).astype(f32)

        matrices = []
        for layer in range(layers):
            du, df_t, da_t, dq, dk, dv = results[6 * layer : 6 * layer + 6]
            keep = kept[layer]
            x_all = keep["xall"]
            into = [
                jnp.concatenate([jnp.where(core == 0, a, b), jnp.where(core == 0, b, a)], 1)
                for a, b in (
                    (dot_tn(x_all[: array.shape[0]], array), dot_tn(x_all[: array.shape[0]], swap(array)))
                    for array in (dq, dk, dv)
                )
            ]
            proj = jnp.zeros((CORES, half, width), f32)
            proj = lax.dynamic_update_slice_in_dim(proj, dot(da_t, keep["o"]).T[None], core, 0)
            up = jnp.zeros((2, CORES, width, quarter), f32)
            own_up = dot(keep["hrt"], du).reshape(width, 2, 1, quarter).transpose(1, 2, 0, 3)
            up = lax.dynamic_update_slice_in_dim(up, own_up, core, 1)
            down = jnp.zeros((2, CORES, quarter, width), f32)
            own_down = dot(df_t, keep["act"]).T.reshape(2, 1, quarter, width)
            down = lax.dynamic_update_slice_in_dim(down, own_down, core, 1)
            matrices.append((
                spread(jnp.concatenate(into, 1) * 0.5),
                spread(proj.reshape(width, width)),
                spread(up.transpose(2, 0, 1, 3).reshape(width, ffn)),
                spread(down.reshape(ffn, width)),
            ))
        halves = jnp.arange(SUMS)[None, :, None] >= OUT_BIAS
        summed = lax.psum(jnp.where(halves, 0.5 * sums, sums), ("clip", "seq"))

        def share(row, count):
            piece = summed[:, row : row + count].reshape(layers, count * width)
            size = count * width // seq_size
            return lax.dynamic_slice_in_dim(piece, seq_at * size, size, 1)

        into, proj, up, down = (
            jnp.stack([matrices[layer][which] for layer in range(layers)]) for which in range(4)
        )
        return (
            out_tokens, grad_tokens, into, share(QUERY_BIAS, 2), proj, share(OUT_BIAS, 1),
            up, share(UP_BIAS, 4), down, share(DOWN_BIAS, 1),
            jnp.stack([share(GAIN, 1), share(GAIN + 1, 1)], 1),
            jnp.stack([share(SHIFT, 1), share(SHIFT + 1, 1)], 1),
        )

    return shards


def solution(mesh):
    rowed = P("clip", "seq", None)
    in_specs = (rowed, P("clip")) + (P(),) * 10 + (rowed,)
    out_specs = (
        rowed,
        rowed,
        P(None, "clip", "seq"),
        P(None, "seq"),
        P(None, "clip", "seq"),
        P(None, "seq"),
        P(None, "clip", "seq"),
        P(None, "seq"),
        P(None, "clip", "seq"),
        P(None, "seq"),
        P(None, None, "seq"),
        P(None, None, "seq"),
    )
    return jax.shard_map(
        build(mesh), mesh=mesh, in_specs=in_specs, out_specs=out_specs, check_vma=False
    )
```

```python
from copy import copy as duplicate
import functools

import jax
import jax.numpy as jnp
from jax import lax
from jax.experimental import pallas as pl
from jax.experimental.pallas import tpu as pltpu
from jax.sharding import PartitionSpec as P

HEADS = 12
HEAD_DIM = 64
CORES = 2
LANES = 128
SCALE = HEAD_DIM**-0.5
SQRT_HALF = 0.5**0.5
GAUSS = 0.3989422804014327
LOG2E = 1.4426950408889634
EPS = 1e-05
VMEM = 56 * 1024 * 1024
VMEM_BACK = 63 * 1024 * 1024

f32 = jnp.float32
b16 = jnp.bfloat16


def dot(a, b):
    return lax.dot_general(a, b, (((1,), (0,)), ((), ())), preferred_element_type=f32)


def dot_nt(a, b):
    return lax.dot_general(a, b, (((1,), (1,)), ((), ())), preferred_element_type=f32)


def dot_tn(a, b):
    return lax.dot_general(a, b, (((0,), (0,)), ((), ())), preferred_element_type=f32)


def norm_parts(values):
    center = values - jnp.mean(values, -1, keepdims=True)
    inverse = lax.rsqrt(jnp.mean(center * center, -1, keepdims=True) + EPS)
    return center * inverse, inverse


def norm_back(unit, inverse, gain, grad):
    scaled = grad * gain
    mean_one = jnp.mean(scaled, -1, keepdims=True)
    mean_two = jnp.mean(scaled * unit, -1, keepdims=True)
    back = inverse * (scaled - mean_one - unit * mean_two)
    return back, jnp.sum(grad * unit, 0, keepdims=True), jnp.sum(grad, 0, keepdims=True)


def call(kernel, core, grid, ins, outs, scratch, flops, moved):
    in_specs = [pl.BlockSpec(block, lambda g, c, at=at: at(g, c[0])) for unused, block, at in ins]
    out_specs = [pl.BlockSpec(block, lambda g, c, at=at: at(g, c[0])) for s, d, block, at in outs]
    return pl.pallas_call(
        kernel,
        grid_spec=pltpu.PrefetchScalarGridSpec(
            num_scalar_prefetch=1,
            grid=(grid,),
            in_specs=in_specs,
            out_specs=out_specs,
            scratch_shapes=scratch,
        ),
        out_shape=[jax.ShapeDtypeStruct(shape, dtype) for shape, dtype, b, at in outs],
        compiler_params=pltpu.CompilerParams(
            dimension_semantics=("arbitrary",), vmem_limit_bytes=VMEM
        ),
        cost_estimate=pl.CostEstimate(flops=flops, bytes_accessed=moved, transcendentals=0),
    )(core, *[array for array, b, at in ins])


def all_of(array):
    zeros = (0,) * array.ndim
    return (array, array.shape, lambda g, c: zeros)


def full(shape, dtype):
    zeros = (0,) * len(shape)
    return (shape, dtype, shape, lambda g, c: zeros)


class Geometry:
    def __init__(self, mesh, tokens, ffn):
        self.clip_size, self.seq_size = mesh.shape["clip"], mesh.shape["seq"]
        self.columns = self.clip_size // CORES
        self.held, self.slots, self.width = tokens.shape
        self.ffn = ffn
        self.posts = self.held * CORES
        self.lines = self.seq_size // self.posts
        self.tile = CORES * self.slots
        self.rows = self.held * self.tile
        self.count = self.rows * self.lines
        self.half = self.width // CORES
        self.pairs = self.half // LANES
        self.heads = 2 * self.pairs
        self.quarter = ffn // 4
        self.depth = self.width // self.clip_size
        self.aligned = self.columns == 2 and (ffn // self.seq_size) % LANES == 0

    def locate(self):
        self.clip = lax.axis_index("clip")
        self.seq = lax.axis_index("seq")
        self.core = self.clip % CORES
        self.column = self.clip // CORES
        self.post = self.seq // self.lines
        self.line = self.seq % self.lines
        self.parity = self.post % self.held

    def sibling(self):
        return self.clip + 1 - 2 * self.core, self.seq

    def on_line(self, shift):
        return self.clip, self.post * self.lines + (self.line + shift) % self.lines

    def on_post(self, shift):
        return self.clip, (self.post + shift) % self.posts * self.lines + self.line

    def on_column(self, shift):
        return (self.column + shift) % self.columns * CORES + self.core, self.seq

    def goal(self, turn):
        post = self.held * self.core + (self.post + turn) % self.held
        return self.column * CORES + self.post // self.held, post * self.lines + self.line

    def origin(self, turn, who):
        post = self.held * who + (self.parity + turn) % self.held
        return self.column * CORES + self.post // self.held, post * self.lines + self.line

    def blocked(self, turn):
        return jnp.logical_and(self.post // self.held == self.core, turn == 0)


def remote(source, target, send, receive, device):
    return pltpu.make_async_remote_copy(
        src_ref=source, dst_ref=target, send_sem=send, recv_sem=receive,
        device_id=device, device_id_type=pl.DeviceIdType.MESH,
    )


def meet(geo, devices):
    barrier = pltpu.get_barrier_semaphore()
    total = 0
    for device in devices:
        other = jnp.logical_or(device[0] != geo.clip, device[1] != geo.seq)

        @pl.when(other)
        def greet(device=device):
            pl.semaphore_signal(
                barrier, inc=1, device_id=device, device_id_type=pl.DeviceIdType.MESH
            )

        total = total + other.astype(jnp.int32)
    pl.semaphore_wait(barrier, total)


def loop(count, body):
    def step(at, carry):
        body(at)
        return carry

    lax.fori_loop(0, count, step, 0)


def gelu_parts(inner):
    bell = jnp.exp2((inner * inner) * (-0.5 * LOG2E))
    phi = 0.5 + 0.5 * lax.erf(inner * SQRT_HALF)
    return phi, phi + inner * (GAUSS * bell)


KEPT = ("xall", "kx", "v", "q", "ot", "lse", "o", "z1", "hrt", "act", "slope", "z2")


def kept_shapes(geo):
    rows, width, half, count = geo.rows, geo.width, geo.half, geo.count
    return {
        "xall": ((count, width), b16),
        "kx": ((geo.pairs, count, 2 * LANES), b16),
        "v": ((count, half), b16),
        "q": ((rows, half), b16),
        "ot": ((half, rows), f32),
        "lse": ((geo.heads, 8, rows), f32),
        "o": ((rows, half), b16),
        "z1": ((rows, width), f32),
        "hrt": ((width, rows), b16),
        "act": ((rows, geo.ffn // CORES), b16),
        "slope": ((rows, geo.ffn // CORES), b16),
        "z2": ((rows, width), f32),
    }


def forward_kernel(geo, layers, *refs):
    refs = list(refs)

    def take(count):
        taken = refs[:count]
        del refs[:count]
        return taken

    tokens, cotangent, w_in, w_out, w_up, w_down = take(6)
    lengths, in_bias, out_bias, up_bias, down_bias, gains, shifts = take(7)
    (cot_rows,) = take(1)
    stored = [dict(zip(KEPT, take(len(KEPT)))) for unused in range(layers)]
    kept = [dict(zip(KEPT, take(len(KEPT)))) for unused in range(layers)]
    wq, wkv, wout, wup, wdown = take(5)
    qx, vt, state, hidden, lens, lens_there, psend, precv, running = take(9)
    (load_sem, save_sem, tok_sem, tok_send, tok_recv, cot_sem, cot_send, cot_recv, sib_send,
     sib_recv, line_send, line_recv, pass_send, pass_recv, part_send, part_recv,
     len_sem) = take(17)

    geo = duplicate(geo)
    geo.locate()
    core, tile, slots = geo.core, geo.tile, geo.slots
    held, lines, rows, width, half = geo.held, geo.lines, geo.rows, geo.width, geo.half
    quarter, pairs = geo.quarter, geo.pairs
    sibling = geo.sibling()

    loads = []
    for layer in range(layers):
        targets = (wq.at[layer], wkv.at[layer, :, :half], wkv.at[layer, :, half:])
        parts = [
            (w_in.at[layer, :, pl.ds(pl.multiple_of((kind * CORES + core) * half, half), half)],
             targets[kind])
            for kind in range(3)
        ]
        parts.append((w_out.at[layer, pl.ds(pl.multiple_of(core * half, half), half), :], wout.at[layer]))
        for block in range(2):
            at = pl.ds(pl.multiple_of((2 * block + core) * quarter, quarter), quarter)
            span = slice(block * quarter, (block + 1) * quarter)
            parts.append((w_up.at[layer, :, at], wup.at[layer, :, span]))
            parts.append((w_down.at[layer, at, :], wdown.at[layer, span, :]))
        loads.append([
            pltpu.make_async_copy(source, target, load_sem.at[layer, at])
            for at, (source, target) in enumerate(parts)
        ])
    for copy in loads[0]:
        copy.start()

    sources = [geo.origin(turn, who) for turn in range(held) for who in range(CORES)]
    goals = [geo.goal(turn) for turn in range(held)]
    goals = goals + [(device[0] + 1 - 2 * (device[0] % CORES), device[1]) for device in goals]
    near = [sibling] + [geo.on_line(shift) for shift in range(1, lines)]
    meet(geo, near + sources + goals)

    first = kept[0]["xall"]

    def block_at(turn, who, shift=0):
        start = shift * rows + turn * tile + who * slots
        return pl.ds(start if isinstance(start, int) else pl.multiple_of(start, slots), slots)

    def token_copies(turn, who):
        mine = tokens.at[(geo.post + turn) % held]
        place = first.at[block_at(turn, who)]
        own = pltpu.make_async_copy(mine, place, tok_sem.at[turn])
        return own, remote(mine, place, tok_send.at[turn], tok_recv.at[turn], geo.goal(turn))

    def token_start(turn):
        own, there = token_copies(turn, geo.post // held)
        pl.when(geo.blocked(turn))(own.start)
        pl.when(jnp.logical_not(geo.blocked(turn)))(there.start)

    def token_wait(turn):
        own, there = token_copies(turn, core)
        pl.when(geo.blocked(turn))(own.wait)
        pl.when(jnp.logical_not(geo.blocked(turn)))(there.wait)

    def to_sibling(array, turn, who, shift, send, receive):
        place = array.at[block_at(turn, who, shift)]
        return remote(place, place, send, receive, sibling)

    def to_line(layer, turn, shift):
        array = kept[layer]["xall"]
        source = array.at[block_at(turn, core)]
        target = array.at[block_at(turn, core, shift)]
        return remote(
            source, target, line_send.at[layer, turn, shift - 1], line_recv.at[layer, turn, shift - 1],
            geo.on_line(shift),
        )

    for turn in range(held):
        token_start(turn)
    clip_row = lax.broadcasted_iota(jnp.int32, lens.shape, 0)
    filled = jnp.full(lens.shape, lengths[0], jnp.int32)
    for clip in range(1, held):
        filled = jnp.where(clip_row == clip, lengths[clip], filled)
    lens[...] = filled
    len_copy = remote(lens, lens_there, len_sem.at[0], len_sem.at[1], sibling)
    len_copy.start()

    def clear(at):
        qx[at] = jnp.zeros(qx.shape[1:], b16)
        qx[at, LANES : LANES + 16, :] = (
            lax.broadcasted_iota(jnp.int32, (16, rows), 0) == 0
        ).astype(f32).astype(b16)

    loop(geo.heads, clear)
    len_copy.wait()
    known = jnp.where(geo.post // held == core, lens[...], lens_there[...])
    length = known[0:1, :]
    for clip in range(1, held):
        length = jnp.where(geo.parity == clip, known[clip : clip + 1, :], length)
    lane = lax.broadcasted_iota(jnp.int32, (slots, LANES), 1)
    slot = lax.broadcasted_iota(jnp.int32, (slots, LANES), 0)
    for shift in range(lines):
        for turn in range(held):
            for who in range(CORES):
                post = held * who + (geo.parity + turn) % held
                line = (geo.line + lines - shift) % lines
                outside = (post * lines + line) * slots + slot >= length
                mask = jnp.where(jnp.logical_and(lane == 0, outside), -1e30, 0.0)
                mask = jnp.where(jnp.logical_and(lane > 0, lane < 4), 1.0, mask).astype(b16)
                for layer in range(layers):
                    for pair in range(pairs):
                        kept[layer]["kx"][pair, block_at(turn, who, shift), LANES:] = mask

    for turn in range(held):
        token_wait(turn)
        to_sibling(first, turn, core, 0, sib_send.at[turn], sib_recv.at[turn]).start()
        for shift in range(1, lines):
            to_line(0, turn, shift).start()
    for copy in loads[0]:
        copy.wait()
    for copy in loads[1]:
        copy.start()

    def cot_copies(turn, flip):
        mine = cotangent.at[(geo.post + turn) % held]
        place = cot_rows.at[block_at(turn, geo.post // held)]
        goal = geo.goal(turn)
        if flip:
            goal = (goal[0] + 1 - 2 * (goal[0] % CORES), goal[1])
        own = pltpu.make_async_copy(mine, place, cot_sem.at[turn, flip])
        there = remote(
            mine, place, cot_send.at[turn, flip], cot_recv.at[turn, geo.post // held], goal
        )
        here = jnp.logical_and(goal[0] == geo.clip, goal[1] == geo.seq)
        return own, there, here

    def cot_start():
        for turn in range(held):
            for flip in range(CORES):
                own, there, here = cot_copies(turn, flip)
                pl.when(here)(own.start)
                pl.when(jnp.logical_not(here))(there.start)

    def cot_wait():
        for turn in range(held):
            for flip in range(CORES):
                own, there, here = cot_copies(turn, flip)
                pl.when(here)(own.wait)
                pl.when(jnp.logical_not(here))(there.wait_send)
            for who in range(CORES):
                source = geo.origin(turn, who)
                place = cot_rows.at[block_at(turn, who)]
                there = remote(
                    cotangent.at[0], place, cot_send.at[turn, 0], cot_recv.at[turn, who], source
                )
                here = jnp.logical_and(source[0] == geo.clip, source[1] == geo.seq)
                pl.when(jnp.logical_not(here))(there.wait_recv)

    def key_tile(layer, at):
        keep = kept[layer]
        now = pl.ds(pl.multiple_of(at, tile), tile)
        both = dot(keep["xall"][now, :], wkv[layer])
        key = both[:, :half].astype(b16)
        for pair in range(pairs):
            keep["kx"][pair, now, :LANES] = key[:, pair * LANES : (pair + 1) * LANES]
        bias = in_bias[layer : layer + 1, pl.ds(pl.multiple_of(width + core * half, half), half)]
        value = (both[:, half:] + bias).astype(b16)
        keep["v"][now, :] = value
        vt[:, now] = value.astype(f32).T.astype(b16)

    def query_tile(layer, at):
        keep = kept[layer]
        now = pl.ds(pl.multiple_of(at, tile), tile)
        bias = in_bias[layer : layer + 1, pl.ds(pl.multiple_of(core * half, half), half)]
        query = (dot(keep["xall"][now, :], wq[layer]) + bias).astype(b16)
        query = (query * SCALE).astype(b16)
        keep["q"][now, :] = query
        turned = query.astype(f32).T.astype(b16)
        for head in range(geo.heads):
            inside = head % 2 * HEAD_DIM
            qx[head, inside : inside + HEAD_DIM, now] = (
                turned[head * HEAD_DIM : (head + 1) * HEAD_DIM]
            )

    def attend_block(layer, shift):
        keep = kept[layer]
        span = slice(shift * rows, (shift + 1) * rows)

        size = min(256, rows)
        cuts = [slice(start, start + size) for start in range(shift * rows, (shift + 1) * rows, size)]

        def pair_step(pair):
            heads = [2 * pair, 2 * pair + 1]
            scores = [
                [dot(keep["kx"][pair, cut, :], qx[head]) for cut in cuts] for head in heads
            ]
            for head, pieces in zip(heads, scores):
                here = pl.ds(pl.multiple_of(head * HEAD_DIM, HEAD_DIM), HEAD_DIM)
                top = functools.reduce(
                    jnp.maximum, [jnp.max(piece, 0, keepdims=True) for piece in pieces]
                )
                if shift > 0:
                    before = keep["lse"][head, 0:1, :]
                    top = jnp.maximum(top, before)
                    shrink = jnp.exp(before - top)
                total = attended = None
                for piece, cut in zip(pieces, cuts):
                    weights = jnp.exp(piece - top)
                    sums = jnp.sum(weights, 0, keepdims=True)
                    values = dot(vt[here, cut], weights.astype(b16))
                    total = sums if total is None else total + sums
                    attended = values if attended is None else attended + values
                if shift > 0:
                    total = total + shrink * running[head, 0:1, :]
                    attended = attended + shrink * keep["ot"][here, :]
                if shift < lines - 1:
                    running[head, 0:1, :] = total
                    keep["ot"][here, :] = attended
                    keep["lse"][head, 0:1, :] = top
                else:
                    keep["ot"][here, :] = attended / total
                    keep["lse"][head, 0:1, :] = top + jnp.log(total)

        loop(pairs, pair_step)

    def project_tile(layer, turn):
        keep = kept[layer]
        now = pl.ds(pl.multiple_of(turn * tile, tile), tile)
        attended = keep["ot"][:, now].T.astype(b16)
        keep["o"][now, :] = attended
        share(2 * layer, turn, dot(attended, wout[layer]))

    def part_copy(which, turn):
        now = pl.ds(pl.multiple_of(turn * tile, tile), tile)
        return remote(
            psend.at[which, now, :], precv.at[which, now, :], part_send.at[which, turn],
            part_recv.at[which, turn], sibling,
        )

    def share(which, turn, part):
        now = pl.ds(pl.multiple_of(turn * tile, tile), tile)
        psend[which, now, :] = part.astype(b16)
        part_copy(which, turn).start()

    def collect(which, turn):
        now = pl.ds(pl.multiple_of(turn * tile, tile), tile)
        part_copy(which, turn).wait()
        return psend[which, now, :].astype(f32) + precv[which, now, :].astype(f32)

    def feed_tile(layer, turn):
        keep = kept[layer]
        now = pl.ds(pl.multiple_of(turn * tile, tile), tile)
        x = first[now, :].astype(f32) if layer == 0 else state[now, :]
        summed = x + collect(2 * layer, turn) + out_bias[layer : layer + 1, :]
        keep["z1"][now, :] = summed
        unit, unused = norm_parts(summed)
        normal = unit * gains[layer, 0:1, :] + shifts[layer, 0:1, :]
        hidden[now, :] = normal
        low = normal.astype(b16)
        keep["hrt"][:, now] = low.astype(f32).T.astype(b16)
        size = min(256, quarter)
        for at in range(0, 2 * quarter, size):
            block, start = at // quarter, at % quarter
            bias = up_bias[
                layer : layer + 1,
                pl.ds(pl.multiple_of((2 * block + core) * quarter + start, size), size),
            ]
            inner = dot(low, wup[layer, :, at : at + size]) + bias
            phi, slope = gelu_parts(inner)
            keep["act"][now, at : at + size] = (inner * phi).astype(b16)
            keep["slope"][now, at : at + size] = slope.astype(b16)
        total = dot(keep["act"][now, :], wdown[layer])
        share(2 * layer + 1, turn, total)

    def norm_tile(layer, turn):
        keep = kept[layer]
        now = pl.ds(pl.multiple_of(turn * tile, tile), tile)
        summed = hidden[now, :] + collect(2 * layer + 1, turn) + down_bias[layer : layer + 1, :]
        keep["z2"][now, :] = summed
        if layer < layers - 1:
            unit, unused = norm_parts(summed)
            result = unit * gains[layer, 1:2, :] + shifts[layer, 1:2, :]
            state[now, :] = result
            kept[layer + 1]["xall"][now, :] = result.astype(b16)

    saves = []

    def save(layer, names):
        for name in names:
            copy = pltpu.make_async_copy(
                kept[layer][name], stored[layer][name], save_sem.at[layer, KEPT.index(name)]
            )
            copy.start()
            saves.append(copy)

    for layer in range(layers):
        x_all = kept[layer]["xall"]
        if layer == 0:
            for turn in range(held):
                to_sibling(x_all, turn, core, 0, sib_send.at[turn], sib_recv.at[turn]).wait_send()
                to_sibling(x_all, turn, 1 - core, 0, sib_send.at[turn], sib_recv.at[turn]).wait_recv()
                key_tile(layer, turn * tile)
                query_tile(layer, turn * tile)
        else:
            for copy in loads[layer]:
                copy.wait()

            def own_tile(turn):
                key_tile(layer, turn * tile)
                query_tile(layer, turn * tile)

            loop(held, own_tile)
        for shift in range(lines):
            if shift > 0:
                for turn in range(held):
                    to_line(layer, turn, shift).wait()
                    to_sibling(
                        x_all, turn, core, shift,
                        pass_send.at[layer, turn, shift - 1], pass_recv.at[layer, turn, shift - 1],
                    ).start()
                for turn in range(held):
                    send = pass_send.at[layer, turn, shift - 1]
                    receive = pass_recv.at[layer, turn, shift - 1]
                    to_sibling(x_all, turn, core, shift, send, receive).wait_send()
                    to_sibling(x_all, turn, 1 - core, shift, send, receive).wait_recv()
                    key_tile(layer, shift * rows + turn * tile)
            if shift == lines - 1:
                save(layer, ("xall", "kx", "v", "q"))
                if layer == 0:
                    cot_start()

            attend_block(layer, shift)
        loop(held, functools.partial(project_tile, layer))
        save(layer, ("ot", "lse", "o"))
        loop(held, functools.partial(feed_tile, layer))
        save(layer, ("z1", "hrt", "act", "slope"))
        for turn in range(held):
            norm_tile(layer, turn)
            if layer < layers - 1:
                for shift in range(1, lines):
                    to_line(layer + 1, turn, shift).start()
        save(layer, ("z2",))

    cot_wait()
    for copy in saves:
        copy.wait()


def forward(geo, layers, tokens, cotangent, lengths, weights, vectors):
    width, rows, half, ffn = geo.width, geo.rows, geo.half, geo.ffn
    shapes = kept_shapes(geo)
    any_spec = pl.BlockSpec(memory_space=pl.ANY)
    vmem_spec = pl.BlockSpec(memory_space=pltpu.VMEM)
    out_shape = [
        jax.ShapeDtypeStruct((rows, width), b16),
    ]
    out_shape += [jax.ShapeDtypeStruct(*shapes[name]) for unused in range(layers) for name in KEPT]
    scratch = [pltpu.VMEM(*shapes[name]) for unused in range(layers) for name in KEPT]
    scratch += [
        pltpu.VMEM((layers, width, half), b16),
        pltpu.VMEM((layers, width, 2 * half), b16),
        pltpu.VMEM((layers, half, width), b16),
        pltpu.VMEM((layers, width, 2 * geo.quarter), b16),
        pltpu.VMEM((layers, 2 * geo.quarter, width), b16),
        pltpu.VMEM((geo.heads, 2 * LANES, rows), b16),
        pltpu.VMEM((half, geo.count), b16),
        pltpu.VMEM((rows, width), f32),
        pltpu.VMEM((rows, width), f32),
        pltpu.VMEM((8, LANES), jnp.int32),
        pltpu.VMEM((8, LANES), jnp.int32),
        pltpu.VMEM((2 * layers, rows, width), b16),
        pltpu.VMEM((2 * layers, rows, width), b16),
        pltpu.VMEM((geo.heads, 8, rows), f32),
    ]
    held, lines = geo.held, max(geo.lines - 1, 1)
    dma = pltpu.SemaphoreType.DMA
    scratch += [dma(shape) for shape in (
        (layers, 8), (layers, len(KEPT)), (held,), (held,), (held,),
        (held, CORES), (held, CORES), (held, CORES), (held,), (held,),
        (layers, held, lines), (layers, held, lines), (layers, held, lines), (layers, held, lines),
        (2 * layers, held), (2 * layers, held), (2,),
    )]
    results = pl.pallas_call(
        functools.partial(forward_kernel, geo, layers),
        out_shape=out_shape,
        in_specs=[any_spec] * 6 + [pl.BlockSpec(memory_space=pltpu.SMEM)] + [vmem_spec] * 6,
        out_specs=[any_spec] * len(out_shape),
        scratch_shapes=scratch,
        compiler_params=pltpu.CompilerParams(
            collective_id=0, has_side_effects=True, vmem_limit_bytes=VMEM
        ),
        cost_estimate=pl.CostEstimate(flops=3 * 10**10, bytes_accessed=4 * 10**7, transcendentals=0),
    )(tokens, cotangent, *weights, lengths, *vectors)
    count = len(KEPT)
    kept = [
        dict(zip(KEPT, results[1 + layer * count : 1 + (layer + 1) * count]))
        for layer in range(layers)
    ]
    return results[0], kept


QUERY_BIAS, VALUE_BIAS, UP_BIAS, OUT_BIAS, DOWN_BIAS, GAIN, SHIFT = 0, 1, 2, 6, 7, 8, 10
SUMS = 16
UP, DOWN = 0, 1
INTO, PROJ = 0, 1
PAIRS = ("pair0", "pair1", "pair2")
UP_AFTER = (None, 0)


def backward_kernel(geo, layers, *refs):
    refs = list(refs)

    def take(count):
        taken = refs[:count]
        del refs[:count]
        return taken

    cot_rows, w_in, w_out, w_up, w_down = take(5)
    stored = [dict(zip(KEPT, take(len(KEPT)))) for unused in range(layers)]
    gains, shifts = take(2)
    out_tokens, grad_tokens, sums = take(3)
    if geo.aligned:
        feed_out, attend_out = take(2)
    else:
        plain = [take(6) for unused in range(layers)]
    keep = dict(zip(KEPT, take(len(KEPT))))
    wq, wkv, wout, wup, wdown = take(5)
    (o_there, low_grad, turned, du_there, psend, precv, do, qx, dox, dq, dkv, dq_there,
     dkv_there, probs_all, grads_all, do_stack, q_stack, dqt, mine_dx, dx_recv, line_in) = take(21)
    out_low = mine_dx
    (load_sem, o_send, o_recv, du_send, du_recv, part_send, part_recv, qkv_send, qkv_recv,
     dx_ssem, dx_rsem, line_send, line_recv, more_send, more_recv, tok_sem, tok_send,
     tok_recv, plain_sem, out_sem, out_send, out_recv) = take(22)
    if geo.aligned:
        (other, mine, from_x, y_first, y_last, z_first, z_last, into_cell, proj_cell, into_y, proj_y, into_z, proj_z,
         a_send, a_x, sum_in) = take(16)
        from_y, from_z = (y_first, y_last), (z_first, z_last)
        cells = [[into_cell] * layers, [proj_cell.at[layer] for layer in range(layers)]]
        cells_z = (into_z, proj_z)
        (fx_send, fx_recv, fy_send, fy_recv, fz_send, fz_recv, ay_send, ay_recv, az_send, az_recv,
         ax_send, ax_recv, sum_send, sum_recv) = take(14)
        credit, into_credit = take(2)

    geo = duplicate(geo)
    geo.locate()
    core, tile, slots = geo.core, geo.tile, geo.slots
    held, lines, rows, width, half = geo.held, geo.lines, geo.rows, geo.width, geo.half
    quarter, pairs, posts, depth = geo.quarter, geo.pairs, geo.posts, geo.depth
    post, line, column = geo.post, geo.line, geo.column
    unit = width // geo.seq_size
    sibling = geo.sibling()

    def tile_at(turn):
        return pl.ds(pl.multiple_of(turn * tile, tile), tile)

    def block_at(turn, who, shift=0):
        start = shift * rows + turn * tile + who * slots
        return pl.ds(start if isinstance(start, int) else pl.multiple_of(start, slots), slots)

    NAMES = KEPT + ("win", "wout", "wup", "wdown", "cot")

    def load_copies(layer, name):
        where = load_sem.at[layer, NAMES.index(name)]
        if name == "win":
            targets = (wq, wkv.at[:, :half], wkv.at[:, half:])
            return [
                pltpu.make_async_copy(
                    w_in.at[layer, :, pl.ds(pl.multiple_of((kind * CORES + core) * half, half), half)],
                    targets[kind], load_sem.at[layer, len(NAMES) + kind],
                )
                for kind in range(3)
            ]
        if name == "wout":
            at = pl.ds(pl.multiple_of(core * half, half), half)
            return [pltpu.make_async_copy(w_out.at[layer, at, :], wout, where)]
        if name in ("wup", "wdown"):
            copies = []
            for block in range(2):
                at = pl.ds(pl.multiple_of((2 * block + core) * quarter, quarter), quarter)
                slot = len(NAMES) + 3 + 2 * (name == "wdown") + block
                if name == "wup":
                    pair = w_up.at[layer, :, at], wup.at[:, block * quarter : (block + 1) * quarter]
                else:
                    pair = w_down.at[layer, at, :], wdown.at[block * quarter : (block + 1) * quarter, :]
                copies.append(pltpu.make_async_copy(*pair, load_sem.at[layer, slot]))
            return copies
        if name == "hrt" and geo.aligned:
            return [
                pltpu.make_async_copy(
                    stored[layer][name].at[pl.ds(pl.multiple_of((2 * which + core) * depth, depth), depth), :],
                    keep[name].at[which * depth : (which + 1) * depth, :],
                    load_sem.at[layer, len(NAMES) + 7 + which],
                )
                for which in range(2)
            ]
        if name == "cot":
            return [pltpu.make_async_copy(cot_rows, low_grad, where)]
        return [pltpu.make_async_copy(stored[layer][name], keep[name], where)]

    def load(layer, *names):
        for name in names:
            for copy in load_copies(layer, name):
                copy.start()

    def loaded(layer, *names):
        for name in names:
            for copy in load_copies(layer, name):
                copy.wait()

    top = layers - 1
    load(top, "z2", "cot", "wdown", "slope", "wup", "act", "z1", "wout", "q", "kx", "v", "ot",
         "lse", "win", "hrt", "xall", "o")

    sources = [geo.origin(turn, who) for turn in range(held) for who in range(CORES)]
    goals = [geo.goal(turn) for turn in range(held)]
    near = [sibling] + [geo.on_line(shift) for shift in range(1, lines)]
    if geo.aligned:
        near += [geo.on_post(shift) for shift in range(1, posts)]
        near += [geo.on_column(shift) for shift in range(1, geo.columns)]
    goals = goals + [(device[0] + 1 - 2 * (device[0] % CORES), device[1]) for device in goals]
    meet(geo, near + sources + goals)

    def o_copy(layer):
        return remote(stored[layer]["o"], o_there, o_send.at[layer], o_recv.at[layer], sibling)

    def clear(at):
        qx[at] = jnp.zeros(qx.shape[1:], b16)
        dox[at] = jnp.zeros(dox.shape[1:], b16)

    loop(2, clear)
    sums[...] = jnp.zeros_like(sums)

    def add_sum(layer, row, lanes, value):
        sums[layer, pl.ds(row, 1), lanes] += value

    everywhere = slice(None)


    def x_copy(layer, kind, z):
        return remote(
            other.at[kind, z], from_x.at[kind, z], fx_send.at[layer, kind, z],
            fx_recv.at[layer, kind, z], geo.on_column(1),
        )

    pair_post = post + 1 - 2 * (post % 2)
    far_post = (post + 2) % posts

    landed = {}

    def all_landed(hop, kind):
        landed[hop, kind] = landed.get((hop, kind), 0) + 1
        return landed[hop, kind] == posts

    def order(step):
        return (pair_post + step // 2 * (far_post - pair_post) + step % 2 * 2) % posts

    def at_post(which):
        return geo.clip, which * lines + line

    def y_copy(layer, kind, z, shift):
        there = from_y[layer].at[kind, shift - 1] if layer else from_y[layer].at[kind, z, shift - 1]
        at = 0 if layer else z
        return remote(
            mine.at[layer, kind, z, (line + shift) % lines], there,
            fy_send.at[layer, kind, at, shift - 1], fy_recv.at[layer, kind, at, shift - 1],
            geo.on_line(shift),
        )

    def z_copy(layer, kind, hop):
        block = mine.at[layer, kind, order(hop)]
        return remote(
            block if layer else block.at[line], from_z[layer].at[kind, hop],
            fz_send.at[layer, kind, hop], fz_recv.at[layer, kind, hop],
            at_post(far_post if hop == 2 else pair_post),
        )

    def land_x(layer, kind, step):
        z = order(step)
        x_copy(layer, kind, z).wait()
        total = mine[layer, kind, z].astype(f32) + from_x[kind, z].astype(f32)
        mine[layer, kind, z] = total.astype(b16)
        if layer == 0:
            for shift in range(1, lines):
                y_copy(layer, kind, z, shift).start()
            return
        if step < 2:
            z_copy(layer, kind, step).start()
        if all_landed("x", kind):
            device = geo.on_column(1)
            pl.semaphore_signal(
                credit.at[kind], inc=1, device_id=device, device_id_type=pl.DeviceIdType.MESH
            )

    def land_y(layer, kind, step):
        z = order(step)
        total = mine[layer, kind, z, line].astype(f32)
        for shift in range(1, lines):
            y_copy(layer, kind, z, shift).wait()
            total = total + from_y[layer][kind, z, shift - 1].astype(f32)
        mine[layer, kind, z, line] = total.astype(b16)
        if step < 2:
            z_copy(layer, kind, step).start()

    def land_near(layer, kind):
        z_copy(layer, kind, 1).wait()
        here = (layer, kind, far_post) if layer else (layer, kind, far_post, line)
        total = mine[here].astype(f32) + from_z[layer][kind, 1].astype(f32)
        mine[here] = total.astype(b16)
        z_copy(layer, kind, 2).start()

    def land_far(layer, kind):
        here = (layer, kind, post) if layer else (layer, kind, post, line)
        total = mine[here].astype(f32)
        for hop in (0, 2):
            z_copy(layer, kind, hop).wait()
            total = total + from_z[layer][kind, hop].astype(f32)
        if layer == 0:
            feed_out[layer, kind] = total
            return
        mine[here] = total.astype(b16)
        for shift in range(1, lines):
            y_copy(layer, kind, post, shift).start()

    def land_end(layer, kind):
        total = mine[layer, kind, post, line].astype(f32)
        for shift in range(1, lines):
            y_copy(layer, kind, post, shift).wait()
            total = total + from_y[layer][kind, shift - 1].astype(f32)
        feed_out[layer, kind] = total

    def landing(layer, kind, z, shift):
        if kind == INTO:
            return into_y.at[z, shift - 1]
        return proj_y.at[layer, z, shift - 1]

    def ay_copy(layer, kind, z, shift):
        return remote(
            cells[kind][layer].at[(line + shift) % lines, z], landing(layer, kind, z, shift),
            ay_send.at[layer, kind, z, shift - 1], ay_recv.at[layer, kind, z, shift - 1],
            geo.on_line(shift),
        )

    def az_copy(layer, kind, hop):
        return remote(
            cells[kind][layer].at[line, order(hop)], cells_z[kind].at[layer, hop],
            az_send.at[layer, kind, hop], az_recv.at[layer, kind, hop],
            at_post(far_post if hop == 2 else pair_post),
        )

    def ax_copy(layer, kind):
        span = slice(0, 3 * unit) if kind == INTO else slice(3 * unit, 4 * unit)
        return remote(
            a_send.at[layer, span], a_x.at[layer, span], ax_send.at[layer, kind],
            ax_recv.at[layer, kind], geo.on_column(1),
        )

    def send_ay(layer, kind):
        if layer < top and kind == INTO:
            pl.semaphore_wait(into_credit, lines - 1)
        for step in range(posts):
            for shift in range(1, lines):
                ay_copy(layer, kind, order(step), shift).start()

    def land_ay(layer, kind, step):
        z = order(step)
        cell = cells[kind][layer]
        total = cell[line, z].astype(f32)
        for shift in range(1, lines):
            ay_copy(layer, kind, z, shift).wait()
            total = total + landing(layer, kind, z, shift)[...].astype(f32)
        cell[line, z] = total.astype(b16)
        if step < 2:
            az_copy(layer, kind, step).start()

        if layer > 0 and kind == INTO and all_landed("into", kind):
            for shift in range(1, lines):
                pl.semaphore_signal(
                    into_credit, inc=1, device_id=geo.on_line(shift),
                    device_id_type=pl.DeviceIdType.MESH,
                )

    def land_anear(layer, kind):
        cell = cells[kind][layer]
        az_copy(layer, kind, 1).wait()
        total = cell[line, far_post].astype(f32) + cells_z[kind][layer, 1].astype(f32)
        cell[line, far_post] = total.astype(b16)
        az_copy(layer, kind, 2).start()

    def land_afar(layer, kind):
        total = cells[kind][layer][line, post].astype(f32)
        for hop in (0, 2):
            az_copy(layer, kind, hop).wait()
            total = total + cells_z[kind][layer, hop].astype(f32)
        low, high = total[:, :depth], total[:, depth:]
        span = slice(0, 3 * unit) if kind == INTO else slice(3 * unit, 4 * unit)
        attend_out[layer, span] = jnp.where(column == 0, low, high)
        a_send[layer, span] = jnp.where(column == 0, high, low).astype(b16)
        ax_copy(layer, kind).start()

    def land_ax(layer, kind):
        ax_copy(layer, kind).wait()
        span = slice(0, 3 * unit) if kind == INTO else slice(3 * unit, 4 * unit)
        attend_out[layer, span] = attend_out[layer, span] + a_x[layer, span].astype(f32)

    def sum_copies(layer, hop):
        near = ([sibling], [geo.on_line(shift) for shift in range(1, lines)],
                [at_post(pair_post)], [at_post(far_post)], [geo.on_column(1)])
        first = (0, 1, lines, lines + 1, lines + 2)[hop]
        return [
            (remote(
                sums.at[layer], sum_in.at[layer, first + at], sum_send.at[layer, first + at],
                sum_recv.at[layer, first + at], device,
            ), first + at)
            for at, device in enumerate(near[hop])
        ]

    def start_sum(layer):
        shared = lax.broadcasted_iota(jnp.int32, sums.shape[1:], 0) >= OUT_BIAS
        sums[layer] = jnp.where(shared, 0.5 * sums[layer], sums[layer])
        for copy, unused in sum_copies(layer, 0):
            copy.start()

    def land_sum(layer, hop):
        total = sums[layer]
        for copy, at in sum_copies(layer, hop):
            copy.wait()
            total = total + sum_in[layer, at]
        sums[layer] = total
        if hop < 4:
            for copy, unused in sum_copies(layer, hop + 1):
                copy.start()

    schedule = {
        (1, "pair0"): (
            (land_ay, 1, PROJ, 0),
        ),
        (1, "up"): (
            (land_ay, 1, PROJ, 1),
        ),
        (1, "pair1"): (
            (land_ay, 1, PROJ, 2), (land_anear, 1, PROJ), (land_x, 1, DOWN, 1),
        ),
        (1, "dx"): (
            (land_x, 1, DOWN, 0),
        ),
        (1, "own"): (
            (land_ay, 1, PROJ, 3), (land_x, 1, DOWN, 2), (land_x, 1, DOWN, 3), (land_sum, 1, 0),
            (land_near, 1, DOWN),
        ),
        (1, "into"): (
            (land_x, 1, UP, 0),
        ),
        (0, "feed"): (
            (land_sum, 1, 1), (land_x, 1, UP, 1), (land_ay, 1, INTO, 0),
        ),
        (0, "down"): (
            (land_far, 1, DOWN), (land_afar, 1, PROJ), (land_x, 1, UP, 2), (land_ay, 1, INTO, 1),
            (land_sum, 1, 2), (land_x, 1, UP, 3),
        ),
        (0, "proj"): (
            (land_ay, 1, INTO, 2),
        ),
        (0, "pair0"): (
            (land_end, 1, DOWN), (land_near, 1, UP), (land_x, 0, DOWN, 0), (land_ay, 1, INTO, 3),
            (land_ay, 0, PROJ, 0), (land_x, 0, DOWN, 1),
        ),
        (0, "pair1"): (
            (land_sum, 1, 3), (land_ay, 0, PROJ, 2), (land_anear, 1, INTO), (land_x, 0, DOWN, 2),
            (land_ay, 0, PROJ, 3), (land_ay, 0, PROJ, 1),
        ),
        (0, "pair2"): (
            (land_y, 0, DOWN, 1), (land_x, 0, DOWN, 3), (land_y, 0, DOWN, 0),
        ),
        (0, "dx"): (
            (land_ax, 1, PROJ), (land_far, 1, UP), (land_y, 0, DOWN, 2),
        ),
        (0, "own"): (
            (land_y, 0, DOWN, 3), (land_near, 0, DOWN), (land_x, 0, UP, 0),
            (land_anear, 0, PROJ), (land_sum, 0, 0), (land_end, 1, UP), (land_afar, 1, INTO),
        ),
        (0, "into"): (
            (land_x, 0, UP, 1),
        ),
        (0, "end"): (
            (land_far, 0, DOWN), (land_y, 0, UP, 0), (land_x, 0, UP, 2), (land_x, 0, UP, 3),
            (land_sum, 0, 1), (land_sum, 1, 4), (land_ay, 0, INTO, 0), (land_ay, 0, INTO, 1),
            (land_afar, 0, PROJ), (land_ay, 0, INTO, 2), (land_sum, 0, 2), (land_ax, 1, INTO),
            (land_anear, 0, INTO), (land_ay, 0, INTO, 3), (land_sum, 0, 3), (land_sum, 0, 4),
            (land_y, 0, UP, 1), (land_ax, 0, PROJ), (land_y, 0, UP, 2), (land_near, 0, UP),
            (land_afar, 0, INTO), (land_ax, 0, INTO), (land_y, 0, UP, 3), (land_far, 0, UP),
        ),
    }

    def progress(layer, phase):
        if geo.aligned:
            for function, *given in schedule.get((layer, phase), ()):
                function(*given)


    def part_copy(layer, turn):
        return remote(
            psend.at[tile_at(turn), :], precv.at[tile_at(turn), :], part_send.at[layer, turn],
            part_recv.at[layer, turn], sibling,
        )

    def du_copy(layer, turn):
        return remote(
            keep["slope"].at[tile_at(turn), :], du_there.at[tile_at(turn), :],
            du_send.at[layer, turn], du_recv.at[layer, turn], sibling,
        )

    def out_copies(turn, place):
        own = pltpu.make_async_copy(out_low.at[turn], place, out_sem.at[turn])
        there = remote(
            out_low.at[turn], place, out_send.at[turn], out_recv.at[turn], geo.origin(turn, core)
        )
        return own, there

    def send_home(copies, turn, target):
        own, there = copies(turn, target.at[geo.parity])
        pl.when(geo.blocked(turn))(own.start)
        pl.when(jnp.logical_not(geo.blocked(turn)))(there.start)

    def wait_home(copies, turn, target):
        own, there = copies(turn, target.at[(post + turn) % held])
        pl.when(geo.blocked(turn))(own.wait)
        pl.when(jnp.logical_not(geo.blocked(turn)))(there.wait)

    def norm_grads(layer, which, values, grad, turn):
        unit, inverse = norm_parts(values)
        gain = gains[layer, which : which + 1, :]
        if layer == top and which == 1:
            result = unit * gain + shifts[layer, which : which + 1, :]
            out_low[turn] = jnp.where(core == 0, result[:slots], result[slots:]).astype(b16)
            send_home(out_copies, turn, out_tokens)
        back, gain_grad, shift_grad = norm_back(unit, inverse, gain, grad)
        add_sum(layer, GAIN + which, everywhere, gain_grad)
        add_sum(layer, SHIFT + which, everywhere, shift_grad)
        return back

    def feed_back_tile(layer, turn):
        now = tile_at(turn)
        grad = low_grad[now, :].astype(f32)
        if layer < top:
            grad = grad + keep["z1"][now, :]
        back = norm_grads(layer, 1, keep["z2"][now, :], grad, turn)
        keep["z2"][now, :] = back
        low = back.astype(b16)
        wide = low.astype(f32)
        turned[:, now] = wide.T.astype(b16)
        add_sum(layer, DOWN_BIAS, everywhere, jnp.sum(wide, 0, keepdims=True))
        size = min(256, quarter)
        for at in range(0, 2 * quarter, size):
            block, start = at // quarter, at % quarter
            lanes = slice(at, at + size)
            grads = dot_nt(low, wdown[lanes, :])
            grads = (grads * keep["slope"][now, lanes].astype(f32)).astype(b16)
            keep["slope"][now, lanes] = grads
            add_sum(
                layer, UP_BIAS + 2 * block + core, slice(start, start + size),
                jnp.sum(grads.astype(f32), 0, keepdims=True),
            )
        total = dot_nt(keep["slope"][now, :], wup[...])
        psend[now, :] = total.astype(b16)
        part_copy(layer, turn).start()
        du_copy(layer, turn).start()

    def down_grads(layer, which, start):
        lanes = pl.ds(pl.multiple_of(which * quarter, quarter), quarter)
        size = lines * unit

        def chunk(at):
            steps = (2 * at, 2 * at + 1)
            left = [
                turned[pl.ds(pl.multiple_of(order(step) * size, size), size), :] for step in steps
            ]
            result = dot(jnp.concatenate(left, 0), keep["act"][:, lanes]).astype(b16)
            for index, step in enumerate(steps):
                z = order(step)
                for row in range(lines):
                    top = index * size + row * unit
                    for piece in range(2):
                        block = result[
                            top : top + unit, piece * quarter // 2 : (piece + 1) * quarter // 2
                        ]
                        span = slice(piece * unit, (piece + 1) * unit)
                        if start:
                            other[DOWN, z, row, span, :] = block
                        else:
                            mine[layer, DOWN, z, row, span, :] = block
                if start:
                    x_copy(layer, DOWN, z).start()

        loop(posts // 2, chunk)

    def up_grads(layer):
        left = [
            keep["hrt"][pl.ds(pl.multiple_of(which * depth, depth), depth), :]
            for which in (1 - column, column)
        ]
        left = jnp.concatenate(left, 0)
        size = quarter // lines
        for block in range(2):
            lanes = slice(block * quarter, (block + 1) * quarter)
            for there, array in ((0, keep["slope"]), (1, du_there)):
                z = 2 * block + core + there * (1 - 2 * core)
                result = dot(left, array[:, lanes]).astype(b16)
                for row in range(lines):
                    span = slice(row * size, (row + 1) * size)
                    other[UP, z, row] = result[:depth, span]
                    mine[layer, UP, z, row] = result[depth:, span]
        for step in range(posts):
            x_copy(layer, UP, order(step)).start()

    def feed_grads(layer, kind):
        if layer < top:
            pl.semaphore_wait(credit.at[kind], 1)
        if kind == UP:
            loaded(layer, "hrt")
            for turn in range(held):
                du_copy(layer, turn).wait()
            up_grads(layer)
        else:
            down_grads(layer, 1 - column, True)
            down_grads(layer, column, False)

    def proj_back_tile(layer, turn):
        now = tile_at(turn)
        part_copy(layer, turn).wait()
        grad = keep["z2"][now, :] + (psend[now, :].astype(f32) + precv[now, :].astype(f32))
        back = norm_grads(layer, 0, keep["z1"][now, :], grad, turn)
        keep["z1"][now, :] = back
        low = back.astype(b16)
        wide = low.astype(f32)
        turned[:, now] = wide.T.astype(b16)
        add_sum(layer, OUT_BIAS, everywhere, jnp.sum(wide, 0, keepdims=True))
        do[now, :] = dot_nt(low, wout[...]).astype(b16)

    lane_head = lax.broadcasted_iota(jnp.int32, (tile, LANES), 1) // HEAD_DIM

    def attend_back_pair(layer, pair):
        lanes = pl.ds(pl.multiple_of(pair * LANES, LANES), LANES)
        key_t = keep["kx"][pair, :, :LANES].astype(f32).T.astype(b16)
        query_t = keep["q"][:, lanes].astype(f32).T.astype(b16)
        grad_t = do[:, lanes].astype(f32).T.astype(b16)
        for head in range(2):
            here = slice(head * HEAD_DIM, (head + 1) * HEAD_DIM)
            qx[head, here, :] = query_t[here]
            dox[head, here, :] = grad_t[here]
            rest = -keep["lse"][2 * pair + head, 0:1, :]
            row = lax.broadcasted_iota(jnp.int32, (16, rows), 0)
            extra = jnp.where(row == 0, 1.0, 0.0)
            for part in range(1, 4):
                piece = rest.astype(b16).astype(f32)
                rest = rest - piece
                extra = jnp.where(row == part, piece, extra)
            qx[head, LANES : LANES + 16, :] = extra.astype(b16)

        def turn_step(turn):
            now = tile_at(turn)
            query = keep["q"][now, lanes].astype(f32)
            outgrad = do[now, lanes].astype(f32)
            for head in range(2):
                here = slice(head * HEAD_DIM, (head + 1) * HEAD_DIM)
                chosen = (lane_head == head).astype(f32)
                place = pl.ds(pl.multiple_of((2 * turn + head) * tile, tile), tile)
                do_stack[place, :] = (outgrad * chosen).astype(b16)
                q_stack[place, :] = (query * chosen).astype(b16)
                scores = dot(keep["kx"][pair], qx[head, :, now])
                probs = jnp.exp(scores)
                probs_all[:, place] = probs.astype(b16)
                grads = dot(keep["v"][:, lanes], dox[head, :, now])
                own = pl.ds(pl.multiple_of(pair * LANES + head * HEAD_DIM, HEAD_DIM), HEAD_DIM)
                delta = jnp.sum(
                    dox[head, here, now].astype(f32) * keep["ot"][own, now], 0, keepdims=True
                )
                score_grads = (probs * (grads - delta)).astype(b16)
                grads_all[:, place] = score_grads
                dqt[here, now] = dot(key_t[here], score_grads)

        loop(held, turn_step)
        query_grad = (dqt[...].T * SCALE).astype(b16)
        value_grad = dot(probs_all[...], do_stack[...]).astype(b16)
        dq[:, lanes] = query_grad
        dkv[:, lanes] = dot(grads_all[...], q_stack[...]).astype(b16)
        dkv[:, pl.ds(pl.multiple_of(half + pair * LANES, LANES), LANES)] = value_grad
        spot = pl.ds(pl.multiple_of(core * half + pair * LANES, LANES), LANES)
        add_sum(layer, QUERY_BIAS, spot, jnp.sum(query_grad.astype(f32), 0, keepdims=True))
        add_sum(layer, VALUE_BIAS, spot, jnp.sum(value_grad.astype(f32), 0, keepdims=True))

    def qkv_copies(layer):
        return [
            remote(source, target, qkv_send.at[layer, at], qkv_recv.at[layer, at], sibling)
            for at, (source, target) in enumerate(((dq, dq_there), (dkv, dkv_there)))
        ]

    def dx_send(shift, turn):
        start = pl.multiple_of((shift * held + turn) * slots, slots)
        return psend.at[pl.ds(start, slots), :]

    def dx_copy(layer, shift, turn):
        return remote(
            dx_send(shift, turn), dx_recv.at[shift * held + turn],
            dx_ssem.at[layer, shift * held + turn], dx_rsem.at[layer, shift * held + turn], sibling,
        )

    def dx_tile(layer, shift, turn):
        now = pl.ds(pl.multiple_of(shift * rows + turn * tile, tile), tile)
        total = dot_nt(dkv[now, :], wkv[...])
        if shift == 0:
            total = total + dot_nt(dq[now, :], wq[...])
        first, second = total[:slots], total[slots:]
        mine_dx[shift * held + turn] = jnp.where(core == 0, first, second).astype(b16)
        dx_send(shift, turn)[...] = jnp.where(core == 0, second, first).astype(b16)
        dx_copy(layer, shift, turn).start()

    def line_copy(layer, shift, turn):
        return remote(
            dx_recv.at[shift * held + turn], line_in.at[layer, shift - 1, turn],
            line_send.at[layer, shift - 1, turn], line_recv.at[layer, shift - 1, turn],
            geo.on_line(lines - shift),
        )

    def more_copy(layer, turn, who):
        place = low_grad.at[block_at(turn, who)]
        return remote(place, place, more_send.at[layer, turn], more_recv.at[layer, turn], sibling)

    def token_copies(turn, place):
        own = pltpu.make_async_copy(low_grad.at[block_at(turn, core)], place, tok_sem.at[turn])
        there = remote(
            low_grad.at[block_at(turn, core)], place, tok_send.at[turn], tok_recv.at[turn],
            geo.origin(turn, core),
        )
        return own, there

    def mine_lanes(x):
        cuts = [x[:, at * depth : (at + 1) * depth] for at in range(2 * CORES)]
        return jnp.where(
            core == 0, jnp.concatenate([cuts[0], cuts[2]], 1), jnp.concatenate([cuts[1], cuts[3]], 1)
        )

    def into_grads(layer):
        units = half // unit
        x = mine_lanes(keep["xall"][...])
        for first, pair in ((0, (dq, dq_there)), (1, (dkv, dkv_there))):
            for there, ref in enumerate(pair):
                owner = core + there * (1 - 2 * core)
                count = ref.shape[0]
                result = dot_tn(ref[...], x[:count]).astype(b16)
                for at in range(result.shape[0] // unit):
                    kind = first + at // units
                    index = (2 * kind + owner) * units + at % units
                    seq = index // 3
                    where = pl.ds(pl.multiple_of(index % 3 * unit, unit), unit)
                    into_cell[seq % lines, seq // lines, where, :] = result[at * unit : (at + 1) * unit]
        send_ay(layer, INTO)

    def proj_grads(layer):
        here, there = keep["o"][...], o_there[...]
        features = jnp.where(
            core == 0,
            jnp.concatenate([here[:, :depth], there[:, :depth]], 1),
            jnp.concatenate([there[:, depth:], here[:, depth:]], 1),
        )
        result = dot(turned[...], features).astype(b16)
        for seq in range(geo.seq_size):
            proj_cell[layer, seq % lines, seq // lines] = result[seq * unit : (seq + 1) * unit]
        send_ay(layer, PROJ)

    def plain_out(layer, names):
        sources = {"du": keep["slope"], "dft": turned, "dat": turned, "dq": dq, "dk": dkv.at[:, :half], "dv": dkv.at[:, half:]}
        order = ("du", "dft", "dat", "dq", "dk", "dv")
        copies = [
            pltpu.make_async_copy(sources[name], plain[layer][order.index(name)], plain_sem.at[order.index(name)])
            for name in names
        ]
        for copy in copies:
            copy.start()
        for copy in copies:
            copy.wait()

    for layer in range(layers - 1, -1, -1):
        last = layer == 0
        below = layer - 1
        if layer == top:
            loaded(layer, "cot")
        else:
            for turn in range(held):
                more_copy(layer + 1, turn, core).wait_send()
                more_copy(layer + 1, turn, 1 - core).wait_recv()
        o_copy(layer).start()
        loaded(layer, "z2", "wdown", "slope", "wup")
        loop(held, functools.partial(feed_back_tile, layer))
        progress(layer, "feed")
        if not last:
            load(below, "wdown", "wup")
        else:
            load(layer, "z1")
        loaded(layer, "act")
        if geo.aligned:
            feed_grads(layer, DOWN)
            progress(layer, "down")
            if UP_AFTER[layer] is None:
                feed_grads(layer, UP)
                progress(layer, "up")
        else:
            plain_out(layer, ("dft",))
        if not last:
            load(below, "act")
        loaded(layer, "z1", "wout")
        loop(held, functools.partial(proj_back_tile, layer))
        progress(layer, "proj")
        if not last:
            load(below, "wout", "z2")
        if geo.aligned:
            loaded(layer, "o")
            o_copy(layer).wait()
            proj_grads(layer)
        loaded(layer, "q", "kx", "v", "ot", "lse")

        def pair_step(pair):
            attend_back_pair(layer, pair)
            for index in range(pairs if geo.aligned else 0):

                @pl.when(pair == index)
                def after_pair(index=index):
                    progress(layer, PAIRS[index])
                    if index == UP_AFTER[layer]:
                        feed_grads(layer, UP)
                        progress(layer, "up")

        loop(pairs, pair_step)
        if not last:
            load(below, "q", "kx", "v", "ot", "lse")
        for copy in qkv_copies(layer):
            copy.start()
        if geo.aligned:
            start_sum(layer)
        loaded(layer, "win")
        if layer == top:
            for turn in range(held):
                wait_home(out_copies, turn, out_tokens)
        for shift in range(1, lines):
            loop(held, functools.partial(dx_tile, layer, shift))
        progress(layer, "dx")
        for shift in range(1, lines):
            for turn in range(held):
                dx_copy(layer, shift, turn).wait()
                at = shift * held + turn
                dx_recv[at] = (mine_dx[at].astype(f32) + dx_recv[at].astype(f32)).astype(b16)
                line_copy(layer, shift, turn).start()
        loop(held, functools.partial(dx_tile, layer, 0))
        progress(layer, "own")
        if not last:
            load(below, "win")
        if geo.aligned:
            for copy in qkv_copies(layer):
                copy.wait()
            loaded(layer, "xall")
            into_grads(layer)
            progress(layer, "into")
        else:
            for turn in range(held):
                du_copy(layer, turn).wait()
            for copy in qkv_copies(layer):
                copy.wait()
            loaded(layer, "hrt", "xall", "o")
            o_copy(layer).wait()
            plain_out(layer, ("du", "dat", "dq", "dk", "dv"))
        if not last:
            load(below, "hrt", "slope", "xall", "o")
        for turn in range(held):
            dx_copy(layer, 0, turn).wait()
            total = mine_dx[turn].astype(f32) + dx_recv[turn].astype(f32)
            for shift in range(1, lines):
                line_copy(layer, shift, turn).wait()
                total = total + line_in[layer, shift - 1, turn].astype(f32)
            if not last:
                low_grad[block_at(turn, core), :] = total.astype(b16)
                more_copy(layer, turn, core).start()
            else:
                total = total + keep["z1"][block_at(turn, core), :]
                low_grad[block_at(turn, core), :] = total.astype(b16)
                send_home(token_copies, turn, grad_tokens)

    progress(0, "end")
    for turn in range(held):
        wait_home(token_copies, turn, grad_tokens)


def backward(geo, layers, cot_rows, weights, kept, gains, shifts):
    width, rows, half, ffn, count = geo.width, geo.rows, geo.half, geo.ffn, geo.count
    held, lines, posts, slots, quarter = geo.held, geo.lines, geo.posts, geo.slots, geo.quarter
    shapes = kept_shapes(geo)
    any_spec = pl.BlockSpec(memory_space=pl.ANY)
    vmem_spec = pl.BlockSpec(memory_space=pltpu.VMEM)
    unit = width // geo.seq_size
    out = [((held, slots, width), b16)] * 2 + [((layers, SUMS, width), f32)]
    out_specs = [any_spec] * 2 + [vmem_spec]
    if geo.aligned:
        out += [
            ((layers, 2, geo.depth, quarter // lines), f32),
            ((layers, 4 * unit, geo.depth), f32),
        ]
        out_specs += [vmem_spec] * 2
    else:
        for unused in range(layers):
            out += [
                ((rows, ffn // CORES), b16), ((width, rows), b16), ((width, rows), b16),
                ((rows, half), b16), ((count, half), b16), ((count, half), b16),
            ]
            out_specs += [any_spec] * 6
    vmem = pltpu.VMEM
    if geo.aligned:
        shapes["hrt"] = (2 * geo.depth, rows), b16
    scratch = [vmem(*shapes[name]) for name in KEPT]
    scratch += [
        vmem((width, half), b16), vmem((width, 2 * half), b16), vmem((half, width), b16),
        vmem((width, 2 * quarter), b16), vmem((2 * quarter, width), b16),
        vmem((rows, half), b16),
        vmem((rows, width), b16),
        vmem((width, rows), b16),
        vmem((rows, ffn // CORES), b16),
        vmem((max(rows, lines * held * slots), width), b16), vmem((rows, width), b16),
        vmem((rows, half), b16),
        vmem((2, 2 * LANES, rows), b16), vmem((2, LANES, rows), b16),
        vmem((rows, half), b16), vmem((count, 2 * half), b16),
        vmem((rows, half), b16), vmem((count, 2 * half), b16),
        vmem((count, 2 * rows), b16), vmem((count, 2 * rows), b16),
        vmem((2 * rows, LANES), b16), vmem((2 * rows, LANES), b16), vmem((LANES, rows), f32),
        vmem((lines * held, slots, width), b16), vmem((lines * held, slots, width), b16),
        vmem((layers, lines - 1, held, slots, width), b16),
    ]
    dma = pltpu.SemaphoreType.DMA
    scratch += [dma(shape) for shape in (
        (layers, len(KEPT) + 16), (layers,), (layers,), (layers, held), (layers, held),
        (layers, held), (layers, held), (layers, 3), (layers, 3),
        (layers, lines * held), (layers, lines * held),
        (layers, lines - 1, held), (layers, lines - 1, held),
        (layers, held), (layers, held), (held,), (held,), (held,), (6,),
        (held,), (held,), (held,),
    )]
    if geo.aligned:
        block = (geo.depth, quarter // lines)
        into, proj = (3 * unit, 2 * geo.depth), (unit, 2 * geo.depth)
        hops = lines + 3
        scratch += [
            vmem((2, posts, lines, *block), b16), vmem((layers, 2, posts, lines, *block), b16),
            vmem((2, posts, lines, *block), b16),
            vmem((2, posts, lines - 1, *block), b16), vmem((2, lines - 1, *block), b16),
            vmem((2, 3, *block), b16), vmem((2, 3, lines, *block), b16),
            vmem((lines, posts, *into), b16), vmem((layers, lines, posts, *proj), b16),
            vmem((posts, lines - 1, *into), b16), vmem((layers, posts, lines - 1, *proj), b16),
            vmem((layers, 3, *into), b16), vmem((layers, 3, *proj), b16),
            vmem((layers, 4 * unit, geo.depth), b16), vmem((layers, 4 * unit, geo.depth), b16),
            vmem((layers, hops, SUMS, width), f32),
        ]
        scratch += [dma(shape) for shape in (
            (layers, 2, posts), (layers, 2, posts),
            (layers, 2, posts, lines - 1), (layers, 2, posts, lines - 1),
            (layers, 2, 3), (layers, 2, 3),
            (layers, 2, posts, lines - 1), (layers, 2, posts, lines - 1),
            (layers, 2, 3), (layers, 2, 3), (layers, 2), (layers, 2),
            (layers, hops), (layers, hops),
        )]
        scratch += [pltpu.SemaphoreType.REGULAR((2,)), pltpu.SemaphoreType.REGULAR]
    stored = [kept[layer][name] for layer in range(layers) for name in KEPT]
    return pl.pallas_call(
        functools.partial(backward_kernel, geo, layers),
        out_shape=[jax.ShapeDtypeStruct(*shape) for shape in out],
        in_specs=[any_spec] * (5 + len(stored)) + [vmem_spec] * 2,
        out_specs=out_specs,
        scratch_shapes=scratch,
        compiler_params=pltpu.CompilerParams(
            collective_id=1, has_side_effects=True, vmem_limit_bytes=VMEM_BACK
        ),
        cost_estimate=pl.CostEstimate(flops=8 * 10**10, bytes_accessed=6 * 10**7, transcendentals=0),
    )(cot_rows, *weights, *stored, gains, shifts)


def finish_kernel(
    geo, core_ref, sums_ref, feed_ref, attend_ref, out_in_ref, grad_in_ref,
    out_ref, grad_ref, into_ref, in_bias_ref, proj_ref, out_bias_ref, up_ref, up_bias_ref, down_ref, down_bias_ref,
    gain_ref, shift_ref,
):
    seq = core_ref[0]
    out_ref[...] = out_in_ref[...]
    grad_ref[...] = grad_in_ref[...]
    layers = feed_ref.shape[0]
    unit = geo.width // geo.seq_size
    wide, span = 2 * unit, geo.ffn // geo.seq_size
    per_row, per_quarter = geo.width // wide, geo.quarter // span

    def turn(rows, amount):
        return pltpu.roll(rows, (geo.width - amount) % geo.width, 1)

    for layer in range(layers):
        up_ref[layer] = feed_ref[layer, UP]
        down = feed_ref[layer, DOWN]
        down_ref[layer] = jnp.concatenate([down[:unit], down[unit:]], 1)
        both = attend_ref[layer].T
        into_ref[layer] = both[:, : 3 * unit]
        proj_ref[layer] = both[:, 3 * unit :]
        sums = sums_ref[layer]
        narrow = turn(sums, seq * unit)
        out_bias_ref[layer : layer + 1, :] = narrow[OUT_BIAS : OUT_BIAS + 1, :unit]
        down_bias_ref[layer : layer + 1, :] = narrow[DOWN_BIAS : DOWN_BIAS + 1, :unit]
        gain_ref[layer] = narrow[GAIN : GAIN + 2, :unit]
        shift_ref[layer] = narrow[SHIFT : SHIFT + 2, :unit]
        middle = turn(sums, seq % per_row * wide)
        first = middle[QUERY_BIAS : QUERY_BIAS + 1, :wide]
        second = middle[VALUE_BIAS : VALUE_BIAS + 1, :wide]
        in_bias_ref[layer : layer + 1, :] = jnp.where(seq < per_row, first, second)
        large = turn(sums, seq % per_quarter * span)
        chosen = large[UP_BIAS : UP_BIAS + 1, :span]
        for block in range(1, 4):
            chosen = jnp.where(
                seq // per_quarter == block, large[UP_BIAS + block : UP_BIAS + block + 1, :span], chosen
            )
        up_bias_ref[layer : layer + 1, :] = chosen


def finish(geo, layers, seq, sums, feed_out, attend_out, out_tokens, grad_tokens):
    unit, width = geo.width // geo.seq_size, geo.width
    span = geo.ffn // geo.seq_size
    depth = geo.depth
    shapes = [
        (layers, depth, 3 * unit), (layers, 2 * unit), (layers, depth, unit), (layers, unit),
        (layers, depth, span), (layers, span), (layers, unit, geo.ffn // geo.clip_size),
        (layers, unit), (layers, 2, unit), (layers, 2, unit),
    ]
    results = list(call(
        functools.partial(finish_kernel, geo), seq, 1,
        [all_of(array) for array in (sums, feed_out, attend_out, out_tokens, grad_tokens)],
        [full(out_tokens.shape, b16)] * 2 + [full(shape, f32) for shape in shapes], [],
        10**7, 10**7,
    ))
    results[8] = jnp.swapaxes(results[8], 1, 2)
    return results


def build(mesh):
    clip_size, seq_size = mesh.shape["clip"], mesh.shape["seq"]

    def shards(
        tokens, lengths, attn_in, in_bias, attn_out, out_bias, ffn_in, ffn_in_bias,
        ffn_out, ffn_out_bias, norm_gain, norm_bias, cotangent,
    ):
        layers = attn_in.shape[0]
        geo = Geometry(mesh, tokens, ffn_in.shape[2])
        geo.locate()
        held, width, ffn, half, quarter = geo.held, geo.width, geo.ffn, geo.half, geo.quarter
        aligned, core = geo.aligned, geo.core
        seq_at = geo.seq

        weights = (attn_in, attn_out, ffn_in, ffn_out)
        cot_rows, kept = forward(
            geo, layers, tokens, cotangent, lengths, weights,
            (in_bias, out_bias, ffn_in_bias, ffn_out_bias, norm_gain, norm_bias),
        )
        out_tokens, grad_tokens, sums, *results = backward(
            geo, layers, cot_rows, weights, kept, norm_gain, norm_bias
        )
        if aligned:
            seq_arg = jnp.reshape(seq_at, (1,)).astype(jnp.int32)
            return tuple(finish(geo, layers, seq_arg, sums, *results, out_tokens, grad_tokens))

        def swap(array):
            pairs = [(at, at ^ 1) for at in range(clip_size)]
            return lax.ppermute(array, "clip", pairs)

        def spread(array):
            array = lax.psum_scatter(
                array.astype(b16), "seq", scatter_dimension=1, tiled=True
            ).astype(b16)
            return lax.psum_scatter(array, "clip", scatter_dimension=0, tiled=True).astype(f32)

        matrices = []
        for layer in range(layers):
            du, df_t, da_t, dq, dk, dv = results[6 * layer : 6 * layer + 6]
            keep = kept[layer]
            x_all = keep["xall"]
            into = [
                jnp.concatenate([jnp.where(core == 0, a, b), jnp.where(core == 0, b, a)], 1)
                for a, b in (
                    (dot_tn(x_all[: array.shape[0]], array), dot_tn(x_all[: array.shape[0]], swap(array)))
                    for array in (dq, dk, dv)
                )
            ]
            proj = jnp.zeros((CORES, half, width), f32)
            proj = lax.dynamic_update_slice_in_dim(proj, dot(da_t, keep["o"]).T[None], core, 0)
            up = jnp.zeros((2, CORES, width, quarter), f32)
            own_up = dot(keep["hrt"], du).reshape(width, 2, 1, quarter).transpose(1, 2, 0, 3)
            up = lax.dynamic_update_slice_in_dim(up, own_up, core, 1)
            down = jnp.zeros((2, CORES, quarter, width), f32)
            own_down = dot(df_t, keep["act"]).T.reshape(2, 1, quarter, width)
            down = lax.dynamic_update_slice_in_dim(down, own_down, core, 1)
            matrices.append((
                spread(jnp.concatenate(into, 1) * 0.5),
                spread(proj.reshape(width, width)),
                spread(up.transpose(2, 0, 1, 3).reshape(width, ffn)),
                spread(down.reshape(ffn, width)),
            ))
        halves = jnp.arange(SUMS)[None, :, None] >= OUT_BIAS
        summed = lax.psum(jnp.where(halves, 0.5 * sums, sums), ("clip", "seq"))

        def share(row, count):
            piece = summed[:, row : row + count].reshape(layers, count * width)
            size = count * width // seq_size
            return lax.dynamic_slice_in_dim(piece, seq_at * size, size, 1)

        into, proj, up, down = (
            jnp.stack([matrices[layer][which] for layer in range(layers)]) for which in range(4)
        )
        return (
            out_tokens, grad_tokens, into, share(QUERY_BIAS, 2), proj, share(OUT_BIAS, 1),
            up, share(UP_BIAS, 4), down, share(DOWN_BIAS, 1),
            jnp.stack([share(GAIN, 1), share(GAIN + 1, 1)], 1),
            jnp.stack([share(SHIFT, 1), share(SHIFT + 1, 1)], 1),
        )

    return shards


def solution(mesh):
    rowed = P("clip", "seq", None)
    in_specs = (rowed, P("clip")) + (P(),) * 10 + (rowed,)
    out_specs = (
        rowed,
        rowed,
        P(None, "clip", "seq"),
        P(None, "seq"),
        P(None, "clip", "seq"),
        P(None, "seq"),
        P(None, "clip", "seq"),
        P(None, "seq"),
        P(None, "clip", "seq"),
        P(None, "seq"),
        P(None, None, "seq"),
        P(None, None, "seq"),
    )
    return jax.shard_map(
        build(mesh), mesh=mesh, in_specs=in_specs, out_specs=out_specs, check_vma=False
    )
```

```python
from copy import copy as duplicate
import functools

import jax
import jax.numpy as jnp
from jax import lax
from jax.experimental import pallas as pl
from jax.experimental.pallas import tpu as pltpu
from jax.sharding import PartitionSpec as P

HEADS = 12
HEAD_DIM = 64
CORES = 2
LANES = 128
SCALE = HEAD_DIM**-0.5
SQRT_HALF = 0.5**0.5
GAUSS = 0.3989422804014327
LOG2E = 1.4426950408889634
EPS = 1e-05
VMEM = 56 * 1024 * 1024
VMEM_BACK = 63 * 1024 * 1024

f32 = jnp.float32
b16 = jnp.bfloat16


def dot(a, b):
    return lax.dot_general(a, b, (((1,), (0,)), ((), ())), preferred_element_type=f32)


def dot_nt(a, b):
    return lax.dot_general(a, b, (((1,), (1,)), ((), ())), preferred_element_type=f32)


def dot_tn(a, b):
    return lax.dot_general(a, b, (((0,), (0,)), ((), ())), preferred_element_type=f32)


def norm_parts(values):
    center = values - jnp.mean(values, -1, keepdims=True)
    inverse = lax.rsqrt(jnp.mean(center * center, -1, keepdims=True) + EPS)
    return center * inverse, inverse


def norm_back(unit, inverse, gain, grad):
    scaled = grad * gain
    mean_one = jnp.mean(scaled, -1, keepdims=True)
    mean_two = jnp.mean(scaled * unit, -1, keepdims=True)
    back = inverse * (scaled - mean_one - unit * mean_two)
    return back, jnp.sum(grad * unit, 0, keepdims=True), jnp.sum(grad, 0, keepdims=True)


def call(kernel, core, grid, ins, outs, scratch, flops, moved):
    in_specs = [pl.BlockSpec(block, lambda g, c, at=at: at(g, c[0])) for unused, block, at in ins]
    out_specs = [pl.BlockSpec(block, lambda g, c, at=at: at(g, c[0])) for s, d, block, at in outs]
    return pl.pallas_call(
        kernel,
        grid_spec=pltpu.PrefetchScalarGridSpec(
            num_scalar_prefetch=1,
            grid=(grid,),
            in_specs=in_specs,
            out_specs=out_specs,
            scratch_shapes=scratch,
        ),
        out_shape=[jax.ShapeDtypeStruct(shape, dtype) for shape, dtype, b, at in outs],
        compiler_params=pltpu.CompilerParams(
            dimension_semantics=("arbitrary",), vmem_limit_bytes=VMEM
        ),
        cost_estimate=pl.CostEstimate(flops=flops, bytes_accessed=moved, transcendentals=0),
    )(core, *[array for array, b, at in ins])


def all_of(array):
    zeros = (0,) * array.ndim
    return (array, array.shape, lambda g, c: zeros)


def full(shape, dtype):
    zeros = (0,) * len(shape)
    return (shape, dtype, shape, lambda g, c: zeros)


class Geometry:
    def __init__(self, mesh, tokens, ffn):
        self.clip_size, self.seq_size = mesh.shape["clip"], mesh.shape["seq"]
        self.columns = self.clip_size // CORES
        self.held, self.slots, self.width = tokens.shape
        self.ffn = ffn
        self.posts = self.held * CORES
        self.lines = self.seq_size // self.posts
        self.tile = CORES * self.slots
        self.rows = self.held * self.tile
        self.count = self.rows * self.lines
        self.half = self.width // CORES
        self.pairs = self.half // LANES
        self.heads = 2 * self.pairs
        self.quarter = ffn // 4
        self.depth = self.width // self.clip_size
        self.aligned = self.columns == 2 and (ffn // self.seq_size) % LANES == 0

    def locate(self):
        self.clip = lax.axis_index("clip")
        self.seq = lax.axis_index("seq")
        self.core = self.clip % CORES
        self.column = self.clip // CORES
        self.post = self.seq // self.lines
        self.line = self.seq % self.lines
        self.parity = self.post % self.held

    def sibling(self):
        return self.clip + 1 - 2 * self.core, self.seq

    def on_line(self, shift):
        return self.clip, self.post * self.lines + (self.line + shift) % self.lines

    def on_post(self, shift):
        return self.clip, (self.post + shift) % self.posts * self.lines + self.line

    def on_column(self, shift):
        return (self.column + shift) % self.columns * CORES + self.core, self.seq

    def goal(self, turn):
        post = self.held * self.core + (self.post + turn) % self.held
        return self.column * CORES + self.post // self.held, post * self.lines + self.line

    def origin(self, turn, who):
        post = self.held * who + (self.parity + turn) % self.held
        return self.column * CORES + self.post // self.held, post * self.lines + self.line

    def blocked(self, turn):
        return jnp.logical_and(self.post // self.held == self.core, turn == 0)


def remote(source, target, send, receive, device):
    return pltpu.make_async_remote_copy(
        src_ref=source, dst_ref=target, send_sem=send, recv_sem=receive,
        device_id=device, device_id_type=pl.DeviceIdType.MESH,
    )


def meet(geo, devices):
    barrier = pltpu.get_barrier_semaphore()
    total = 0
    for device in devices:
        other = jnp.logical_or(device[0] != geo.clip, device[1] != geo.seq)

        @pl.when(other)
        def greet(device=device):
            pl.semaphore_signal(
                barrier, inc=1, device_id=device, device_id_type=pl.DeviceIdType.MESH
            )

        total = total + other.astype(jnp.int32)
    pl.semaphore_wait(barrier, total)


def loop(count, body):
    def step(at, carry):
        body(at)
        return carry

    lax.fori_loop(0, count, step, 0)


def gelu_parts(inner):
    bell = jnp.exp2((inner * inner) * (-0.5 * LOG2E))
    phi = 0.5 + 0.5 * lax.erf(inner * SQRT_HALF)
    return phi, phi + inner * (GAUSS * bell)


KEPT = ("xall", "kx", "v", "q", "ot", "lse", "o", "z1", "hrt", "act", "slope", "z2")


def kept_shapes(geo):
    rows, width, half, count = geo.rows, geo.width, geo.half, geo.count
    return {
        "xall": ((count, width), b16),
        "kx": ((geo.pairs, count, 2 * LANES), b16),
        "v": ((count, half), b16),
        "q": ((rows, half), b16),
        "ot": ((half, rows), f32),
        "lse": ((geo.heads, 8, rows), f32),
        "o": ((rows, half), b16),
        "z1": ((rows, width), f32),
        "hrt": ((width, rows), b16),
        "act": ((rows, geo.ffn // CORES), b16),
        "slope": ((rows, geo.ffn // CORES), b16),
        "z2": ((rows, width), f32),
    }


def forward_kernel(geo, layers, *refs):
    refs = list(refs)

    def take(count):
        taken = refs[:count]
        del refs[:count]
        return taken

    tokens, cotangent, w_in, w_out, w_up, w_down = take(6)
    lengths, in_bias, out_bias, up_bias, down_bias, gains, shifts = take(7)
    (cot_rows,) = take(1)
    stored = [dict(zip(KEPT, take(len(KEPT)))) for unused in range(layers)]
    kept = [dict(zip(KEPT, take(len(KEPT)))) for unused in range(layers)]
    wq, wkv, wout, wup, wdown = take(5)
    qx, vt, state, hidden, lens, lens_there, psend, precv, running = take(9)
    (load_sem, save_sem, tok_sem, tok_send, tok_recv, cot_sem, cot_send, cot_recv, sib_send,
     sib_recv, line_send, line_recv, pass_send, pass_recv, part_send, part_recv,
     len_sem) = take(17)

    geo = duplicate(geo)
    geo.locate()
    core, tile, slots = geo.core, geo.tile, geo.slots
    held, lines, rows, width, half = geo.held, geo.lines, geo.rows, geo.width, geo.half
    quarter, pairs = geo.quarter, geo.pairs
    sibling = geo.sibling()

    loads = []
    for layer in range(layers):
        targets = (wq.at[layer], wkv.at[layer, :, :half], wkv.at[layer, :, half:])
        parts = [
            (w_in.at[layer, :, pl.ds(pl.multiple_of((kind * CORES + core) * half, half), half)],
             targets[kind])
            for kind in range(3)
        ]
        parts.append((w_out.at[layer, pl.ds(pl.multiple_of(core * half, half), half), :], wout.at[layer]))
        for block in range(2):
            at = pl.ds(pl.multiple_of((2 * block + core) * quarter, quarter), quarter)
            span = slice(block * quarter, (block + 1) * quarter)
            parts.append((w_up.at[layer, :, at], wup.at[layer, :, span]))
            parts.append((w_down.at[layer, at, :], wdown.at[layer, span, :]))
        loads.append([
            pltpu.make_async_copy(source, target, load_sem.at[layer, at])
            for at, (source, target) in enumerate(parts)
        ])
    for copy in loads[0]:
        copy.start()

    sources = [geo.origin(turn, who) for turn in range(held) for who in range(CORES)]
    goals = [geo.goal(turn) for turn in range(held)]
    goals = goals + [(device[0] + 1 - 2 * (device[0] % CORES), device[1]) for device in goals]
    near = [sibling] + [geo.on_line(shift) for shift in range(1, lines)]
    meet(geo, near + sources + goals)

    first = kept[0]["xall"]

    def block_at(turn, who, shift=0):
        start = shift * rows + turn * tile + who * slots
        return pl.ds(start if isinstance(start, int) else pl.multiple_of(start, slots), slots)

    def token_copies(turn, who):
        mine = tokens.at[(geo.post + turn) % held]
        place = first.at[block_at(turn, who)]
        own = pltpu.make_async_copy(mine, place, tok_sem.at[turn])
        return own, remote(mine, place, tok_send.at[turn], tok_recv.at[turn], geo.goal(turn))

    def token_start(turn):
        own, there = token_copies(turn, geo.post // held)
        pl.when(geo.blocked(turn))(own.start)
        pl.when(jnp.logical_not(geo.blocked(turn)))(there.start)

    def token_wait(turn):
        own, there = token_copies(turn, core)
        pl.when(geo.blocked(turn))(own.wait)
        pl.when(jnp.logical_not(geo.blocked(turn)))(there.wait)

    def to_sibling(array, turn, who, shift, send, receive):
        place = array.at[block_at(turn, who, shift)]
        return remote(place, place, send, receive, sibling)

    def to_line(layer, turn, shift):
        array = kept[layer]["xall"]
        source = array.at[block_at(turn, core)]
        target = array.at[block_at(turn, core, shift)]
        return remote(
            source, target, line_send.at[layer, turn, shift - 1], line_recv.at[layer, turn, shift - 1],
            geo.on_line(shift),
        )

    for turn in range(held):
        token_start(turn)
    clip_row = lax.broadcasted_iota(jnp.int32, lens.shape, 0)
    filled = jnp.full(lens.shape, lengths[0], jnp.int32)
    for clip in range(1, held):
        filled = jnp.where(clip_row == clip, lengths[clip], filled)
    lens[...] = filled
    len_copy = remote(lens, lens_there, len_sem.at[0], len_sem.at[1], sibling)
    len_copy.start()

    def clear(at):
        qx[at] = jnp.zeros(qx.shape[1:], b16)
        qx[at, LANES : LANES + 16, :] = (
            lax.broadcasted_iota(jnp.int32, (16, rows), 0) == 0
        ).astype(f32).astype(b16)

    loop(geo.heads, clear)
    len_copy.wait()
    known = jnp.where(geo.post // held == core, lens[...], lens_there[...])
    length = known[0:1, :]
    for clip in range(1, held):
        length = jnp.where(geo.parity == clip, known[clip : clip + 1, :], length)
    lane = lax.broadcasted_iota(jnp.int32, (slots, LANES), 1)
    slot = lax.broadcasted_iota(jnp.int32, (slots, LANES), 0)
    for shift in range(lines):
        for turn in range(held):
            for who in range(CORES):
                post = held * who + (geo.parity + turn) % held
                line = (geo.line + lines - shift) % lines
                outside = (post * lines + line) * slots + slot >= length
                mask = jnp.where(jnp.logical_and(lane == 0, outside), -1e30, 0.0)
                mask = jnp.where(jnp.logical_and(lane > 0, lane < 4), 1.0, mask).astype(b16)
                for layer in range(layers):
                    for pair in range(pairs):
                        kept[layer]["kx"][pair, block_at(turn, who, shift), LANES:] = mask

    for turn in range(held):
        token_wait(turn)
        to_sibling(first, turn, core, 0, sib_send.at[turn], sib_recv.at[turn]).start()
        for shift in range(1, lines):
            to_line(0, turn, shift).start()
    for copy in loads[0]:
        copy.wait()
    for copy in loads[1]:
        copy.start()

    def cot_copies(turn, flip):
        mine = cotangent.at[(geo.post + turn) % held]
        place = cot_rows.at[block_at(turn, geo.post // held)]
        goal = geo.goal(turn)
        if flip:
            goal = (goal[0] + 1 - 2 * (goal[0] % CORES), goal[1])
        own = pltpu.make_async_copy(mine, place, cot_sem.at[turn, flip])
        there = remote(
            mine, place, cot_send.at[turn, flip], cot_recv.at[turn, geo.post // held], goal
        )
        here = jnp.logical_and(goal[0] == geo.clip, goal[1] == geo.seq)
        return own, there, here

    def cot_start():
        for turn in range(held):
            for flip in range(CORES):
                own, there, here = cot_copies(turn, flip)
                pl.when(here)(own.start)
                pl.when(jnp.logical_not(here))(there.start)

    def cot_wait():
        for turn in range(held):
            for flip in range(CORES):
                own, there, here = cot_copies(turn, flip)
                pl.when(here)(own.wait)
                pl.when(jnp.logical_not(here))(there.wait_send)
            for who in range(CORES):
                source = geo.origin(turn, who)
                place = cot_rows.at[block_at(turn, who)]
                there = remote(
                    cotangent.at[0], place, cot_send.at[turn, 0], cot_recv.at[turn, who], source
                )
                here = jnp.logical_and(source[0] == geo.clip, source[1] == geo.seq)
                pl.when(jnp.logical_not(here))(there.wait_recv)

    def key_tile(layer, at):
        keep = kept[layer]
        now = pl.ds(pl.multiple_of(at, tile), tile)
        both = dot(keep["xall"][now, :], wkv[layer])
        key = both[:, :half].astype(b16)
        for pair in range(pairs):
            keep["kx"][pair, now, :LANES] = key[:, pair * LANES : (pair + 1) * LANES]
        bias = in_bias[layer : layer + 1, pl.ds(pl.multiple_of(width + core * half, half), half)]
        value = (both[:, half:] + bias).astype(b16)
        keep["v"][now, :] = value
        vt[:, now] = value.astype(f32).T.astype(b16)

    def query_tile(layer, at):
        keep = kept[layer]
        now = pl.ds(pl.multiple_of(at, tile), tile)
        bias = in_bias[layer : layer + 1, pl.ds(pl.multiple_of(core * half, half), half)]
        query = (dot(keep["xall"][now, :], wq[layer]) + bias).astype(b16)
        query = (query * SCALE).astype(b16)
        keep["q"][now, :] = query
        turned = (query.astype(f32) * LOG2E).T.astype(b16)
        for head in range(geo.heads):
            inside = head % 2 * HEAD_DIM
            qx[head, inside : inside + HEAD_DIM, now] = (
                turned[head * HEAD_DIM : (head + 1) * HEAD_DIM]
            )

    def attend_block(layer, shift):
        keep = kept[layer]
        span = slice(shift * rows, (shift + 1) * rows)

        size = min(256, rows)
        cuts = [slice(start, start + size) for start in range(shift * rows, (shift + 1) * rows, size)]

        def pair_step(pair):
            heads = [2 * pair, 2 * pair + 1]
            scores = [
                [dot(keep["kx"][pair, cut, :], qx[head]) for cut in cuts] for head in heads
            ]
            for head, pieces in zip(heads, scores):
                here = pl.ds(pl.multiple_of(head * HEAD_DIM, HEAD_DIM), HEAD_DIM)
                top = functools.reduce(
                    jnp.maximum, [jnp.max(piece, 0, keepdims=True) for piece in pieces]
                )
                if shift > 0:
                    before = keep["lse"][head, 0:1, :]
                    top = jnp.maximum(top, before)
                    shrink = jnp.exp2(before - top)
                total = attended = None
                for piece, cut in zip(pieces, cuts):
                    weights = jnp.exp2(piece - top)
                    sums = jnp.sum(weights, 0, keepdims=True)
                    values = dot(vt[here, cut], weights.astype(b16))
                    total = sums if total is None else total + sums
                    attended = values if attended is None else attended + values
                if shift > 0:
                    total = total + shrink * running[head, 0:1, :]
                    attended = attended + shrink * keep["ot"][here, :]
                if shift < lines - 1:
                    running[head, 0:1, :] = total
                    keep["ot"][here, :] = attended
                    keep["lse"][head, 0:1, :] = top
                else:
                    keep["ot"][here, :] = attended / total
                    keep["lse"][head, 0:1, :] = top + jnp.log(total) * LOG2E

        loop(pairs, pair_step)

    def project_tile(layer, turn):
        keep = kept[layer]
        now = pl.ds(pl.multiple_of(turn * tile, tile), tile)
        attended = keep["ot"][:, now].T.astype(b16)
        keep["o"][now, :] = attended
        share(2 * layer, turn, dot(attended, wout[layer]))

    def part_copy(which, turn):
        now = pl.ds(pl.multiple_of(turn * tile, tile), tile)
        return remote(
            psend.at[which, now, :], precv.at[which, now, :], part_send.at[which, turn],
            part_recv.at[which, turn], sibling,
        )

    def share(which, turn, part):
        now = pl.ds(pl.multiple_of(turn * tile, tile), tile)
        psend[which, now, :] = part.astype(b16)
        part_copy(which, turn).start()

    def collect(which, turn):
        now = pl.ds(pl.multiple_of(turn * tile, tile), tile)
        part_copy(which, turn).wait()
        return psend[which, now, :].astype(f32) + precv[which, now, :].astype(f32)

    def feed_tile(layer, turn):
        keep = kept[layer]
        now = pl.ds(pl.multiple_of(turn * tile, tile), tile)
        x = first[now, :].astype(f32) if layer == 0 else state[now, :]
        summed = x + collect(2 * layer, turn) + out_bias[layer : layer + 1, :]
        keep["z1"][now, :] = summed
        unit, unused = norm_parts(summed)
        normal = unit * gains[layer, 0:1, :] + shifts[layer, 0:1, :]
        hidden[now, :] = normal
        low = normal.astype(b16)
        keep["hrt"][:, now] = low.astype(f32).T.astype(b16)
        size = min(256, quarter)
        for at in range(0, 2 * quarter, size):
            block, start = at // quarter, at % quarter
            bias = up_bias[
                layer : layer + 1,
                pl.ds(pl.multiple_of((2 * block + core) * quarter + start, size), size),
            ]
            inner = dot(low, wup[layer, :, at : at + size]) + bias
            phi, slope = gelu_parts(inner)
            keep["act"][now, at : at + size] = (inner * phi).astype(b16)
            keep["slope"][now, at : at + size] = slope.astype(b16)
        total = dot(keep["act"][now, :], wdown[layer])
        share(2 * layer + 1, turn, total)

    def norm_tile(layer, turn):
        keep = kept[layer]
        now = pl.ds(pl.multiple_of(turn * tile, tile), tile)
        summed = hidden[now, :] + collect(2 * layer + 1, turn) + down_bias[layer : layer + 1, :]
        keep["z2"][now, :] = summed
        if layer < layers - 1:
            unit, unused = norm_parts(summed)
            result = unit * gains[layer, 1:2, :] + shifts[layer, 1:2, :]
            state[now, :] = result
            kept[layer + 1]["xall"][now, :] = result.astype(b16)

    saves = []

    def save(layer, names):
        for name in names:
            copy = pltpu.make_async_copy(
                kept[layer][name], stored[layer][name], save_sem.at[layer, KEPT.index(name)]
            )
            copy.start()
            saves.append(copy)

    for layer in range(layers):
        x_all = kept[layer]["xall"]
        if layer == 0:
            for turn in range(held):
                to_sibling(x_all, turn, core, 0, sib_send.at[turn], sib_recv.at[turn]).wait_send()
                to_sibling(x_all, turn, 1 - core, 0, sib_send.at[turn], sib_recv.at[turn]).wait_recv()
                key_tile(layer, turn * tile)
                query_tile(layer, turn * tile)
        for shift in range(lines):
            if shift > 0:
                for turn in range(held):
                    to_line(layer, turn, shift).wait()
                    to_sibling(
                        x_all, turn, core, shift,
                        pass_send.at[layer, turn, shift - 1], pass_recv.at[layer, turn, shift - 1],
                    ).start()
                for turn in range(held):
                    send = pass_send.at[layer, turn, shift - 1]
                    receive = pass_recv.at[layer, turn, shift - 1]
                    to_sibling(x_all, turn, core, shift, send, receive).wait_send()
                    to_sibling(x_all, turn, 1 - core, shift, send, receive).wait_recv()
                    key_tile(layer, shift * rows + turn * tile)
            if shift == lines - 1:
                save(layer, ("xall", "kx", "v", "q"))
                if layer == 0:
                    cot_start()

            attend_block(layer, shift)
        loop(held, functools.partial(project_tile, layer))
        save(layer, ("ot", "lse", "o"))
        loop(held, functools.partial(feed_tile, layer))
        save(layer, ("z1", "hrt", "act", "slope"))
        for turn in range(held):
            norm_tile(layer, turn)
            if layer < layers - 1:
                for shift in range(1, lines):
                    to_line(layer + 1, turn, shift).start()
                if turn == 0:
                    for copy in loads[layer + 1]:
                        copy.wait()
                key_tile(layer + 1, turn * tile)
                query_tile(layer + 1, turn * tile)
        save(layer, ("z2",))

    cot_wait()
    for copy in saves:
        copy.wait()


def forward(geo, layers, tokens, cotangent, lengths, weights, vectors):
    width, rows, half, ffn = geo.width, geo.rows, geo.half, geo.ffn
    shapes = kept_shapes(geo)
    any_spec = pl.BlockSpec(memory_space=pl.ANY)
    vmem_spec = pl.BlockSpec(memory_space=pltpu.VMEM)
    out_shape = [
        jax.ShapeDtypeStruct((rows, width), b16),
    ]
    out_shape += [jax.ShapeDtypeStruct(*shapes[name]) for unused in range(layers) for name in KEPT]
    scratch = [pltpu.VMEM(*shapes[name]) for unused in range(layers) for name in KEPT]
    scratch += [
        pltpu.VMEM((layers, width, half), b16),
        pltpu.VMEM((layers, width, 2 * half), b16),
        pltpu.VMEM((layers, half, width), b16),
        pltpu.VMEM((layers, width, 2 * geo.quarter), b16),
        pltpu.VMEM((layers, 2 * geo.quarter, width), b16),
        pltpu.VMEM((geo.heads, 2 * LANES, rows), b16),
        pltpu.VMEM((half, geo.count), b16),
        pltpu.VMEM((rows, width), f32),
        pltpu.VMEM((rows, width), f32),
        pltpu.VMEM((8, LANES), jnp.int32),
        pltpu.VMEM((8, LANES), jnp.int32),
        pltpu.VMEM((2 * layers, rows, width), b16),
        pltpu.VMEM((2 * layers, rows, width), b16),
        pltpu.VMEM((geo.heads, 8, rows), f32),
    ]
    held, lines = geo.held, max(geo.lines - 1, 1)
    dma = pltpu.SemaphoreType.DMA
    scratch += [dma(shape) for shape in (
        (layers, 8), (layers, len(KEPT)), (held,), (held,), (held,),
        (held, CORES), (held, CORES), (held, CORES), (held,), (held,),
        (layers, held, lines), (layers, held, lines), (layers, held, lines), (layers, held, lines),
        (2 * layers, held), (2 * layers, held), (2,),
    )]
    results = pl.pallas_call(
        functools.partial(forward_kernel, geo, layers),
        out_shape=out_shape,
        in_specs=[any_spec] * 6 + [pl.BlockSpec(memory_space=pltpu.SMEM)] + [vmem_spec] * 6,
        out_specs=[any_spec] * len(out_shape),
        scratch_shapes=scratch,
        compiler_params=pltpu.CompilerParams(
            collective_id=0, has_side_effects=True, vmem_limit_bytes=VMEM
        ),
        cost_estimate=pl.CostEstimate(flops=3 * 10**10, bytes_accessed=4 * 10**7, transcendentals=0),
    )(tokens, cotangent, *weights, lengths, *vectors)
    count = len(KEPT)
    kept = [
        dict(zip(KEPT, results[1 + layer * count : 1 + (layer + 1) * count]))
        for layer in range(layers)
    ]
    return results[0], kept


QUERY_BIAS, VALUE_BIAS, UP_BIAS, OUT_BIAS, DOWN_BIAS, GAIN, SHIFT = 0, 1, 2, 6, 7, 8, 10
SUMS = 16
UP, DOWN = 0, 1
INTO, PROJ = 0, 1
PAIRS = ("pair0", "pair1", "pair2")
UP_AFTER = (1, 1)


def backward_kernel(geo, layers, *refs):
    refs = list(refs)

    def take(count):
        taken = refs[:count]
        del refs[:count]
        return taken

    cot_rows, w_in, w_out, w_up, w_down = take(5)
    stored = [dict(zip(KEPT, take(len(KEPT)))) for unused in range(layers)]
    gains, shifts = take(2)
    out_tokens, grad_tokens, sums = take(3)
    if geo.aligned:
        feed_out, attend_out = take(2)
    else:
        plain = [take(6) for unused in range(layers)]
    keep = dict(zip(KEPT, take(len(KEPT))))
    wq, wkv, wout, wup, wdown = take(5)
    (o_there, low_grad, turned, du_there, psend, precv, do, qx, dox, dq, dkv, dq_there,
     dkv_there, probs_all, grads_all, do_stack, q_stack, dqt, mine_dx, dx_recv, line_in) = take(21)
    out_low = mine_dx
    (load_sem, o_send, o_recv, du_send, du_recv, part_send, part_recv, qkv_send, qkv_recv,
     dx_ssem, dx_rsem, line_send, line_recv, more_send, more_recv, tok_sem, tok_send,
     tok_recv, plain_sem, out_sem, out_send, out_recv) = take(22)
    if geo.aligned:
        (other, mine, from_x, y_first, y_last, z_first, z_last, into_cell, proj_cell, into_y, proj_y, into_z, proj_z,
         a_send, a_x, sum_in) = take(16)
        from_y, from_z = (y_first, y_last), (z_first, z_last)
        cells = [[into_cell] * layers, [proj_cell.at[layer] for layer in range(layers)]]
        cells_z = (into_z, proj_z)
        (fx_send, fx_recv, fy_send, fy_recv, fz_send, fz_recv, ay_send, ay_recv, az_send, az_recv,
         ax_send, ax_recv, sum_send, sum_recv) = take(14)
        credit, into_credit = take(2)

    geo = duplicate(geo)
    geo.locate()
    core, tile, slots = geo.core, geo.tile, geo.slots
    held, lines, rows, width, half = geo.held, geo.lines, geo.rows, geo.width, geo.half
    quarter, pairs, posts, depth = geo.quarter, geo.pairs, geo.posts, geo.depth
    post, line, column = geo.post, geo.line, geo.column
    unit = width // geo.seq_size
    sibling = geo.sibling()

    def tile_at(turn):
        return pl.ds(pl.multiple_of(turn * tile, tile), tile)

    def block_at(turn, who, shift=0):
        start = shift * rows + turn * tile + who * slots
        return pl.ds(start if isinstance(start, int) else pl.multiple_of(start, slots), slots)

    NAMES = KEPT + ("win", "wout", "wup", "wdown", "cot")

    def load_copies(layer, name):
        where = load_sem.at[layer, NAMES.index(name)]
        if name == "win":
            targets = (wq, wkv.at[:, :half], wkv.at[:, half:])
            return [
                pltpu.make_async_copy(
                    w_in.at[layer, :, pl.ds(pl.multiple_of((kind * CORES + core) * half, half), half)],
                    targets[kind], load_sem.at[layer, len(NAMES) + kind],
                )
                for kind in range(3)
            ]
        if name == "wout":
            at = pl.ds(pl.multiple_of(core * half, half), half)
            return [pltpu.make_async_copy(w_out.at[layer, at, :], wout, where)]
        if name in ("wup", "wdown"):
            copies = []
            for block in range(2):
                at = pl.ds(pl.multiple_of((2 * block + core) * quarter, quarter), quarter)
                slot = len(NAMES) + 3 + 2 * (name == "wdown") + block
                if name == "wup":
                    pair = w_up.at[layer, :, at], wup.at[:, block * quarter : (block + 1) * quarter]
                else:
                    pair = w_down.at[layer, at, :], wdown.at[block * quarter : (block + 1) * quarter, :]
                copies.append(pltpu.make_async_copy(*pair, load_sem.at[layer, slot]))
            return copies
        if name == "hrt" and geo.aligned:
            return [
                pltpu.make_async_copy(
                    stored[layer][name].at[pl.ds(pl.multiple_of((2 * which + core) * depth, depth), depth), :],
                    keep[name].at[which * depth : (which + 1) * depth, :],
                    load_sem.at[layer, len(NAMES) + 7 + which],
                )
                for which in range(2)
            ]
        if name == "cot":
            return [pltpu.make_async_copy(cot_rows, low_grad, where)]
        return [pltpu.make_async_copy(stored[layer][name], keep[name], where)]

    def load(layer, *names):
        for name in names:
            for copy in load_copies(layer, name):
                copy.start()

    def loaded(layer, *names):
        for name in names:
            for copy in load_copies(layer, name):
                copy.wait()

    top = layers - 1
    load(top, "z2", "cot", "wdown", "slope", "wup", "act", "z1", "wout", "q", "kx", "v", "ot",
         "lse", "win", "hrt", "xall", "o")

    sources = [geo.origin(turn, who) for turn in range(held) for who in range(CORES)]
    goals = [geo.goal(turn) for turn in range(held)]
    near = [sibling] + [geo.on_line(shift) for shift in range(1, lines)]
    if geo.aligned:
        near += [geo.on_post(shift) for shift in range(1, posts)]
        near += [geo.on_column(shift) for shift in range(1, geo.columns)]
    goals = goals + [(device[0] + 1 - 2 * (device[0] % CORES), device[1]) for device in goals]
    meet(geo, near + sources + goals)

    def o_copy(layer):
        return remote(stored[layer]["o"], o_there, o_send.at[layer], o_recv.at[layer], sibling)

    def clear(at):
        qx[at] = jnp.zeros(qx.shape[1:], b16)
        dox[at] = jnp.zeros(dox.shape[1:], b16)

    loop(2, clear)
    sums[...] = jnp.zeros_like(sums)

    def add_sum(layer, row, lanes, value):
        sums[layer, pl.ds(row, 1), lanes] += value

    everywhere = slice(None)


    def x_copy(layer, kind, z):
        return remote(
            other.at[kind, z], from_x.at[kind, z], fx_send.at[layer, kind, z],
            fx_recv.at[layer, kind, z], geo.on_column(1),
        )

    pair_post = post + 1 - 2 * (post % 2)
    far_post = (post + 2) % posts

    landed = {}

    def all_landed(hop, kind):
        landed[hop, kind] = landed.get((hop, kind), 0) + 1
        return landed[hop, kind] == posts

    def order(step):
        return (pair_post + step // 2 * (far_post - pair_post) + step % 2 * 2) % posts

    def at_post(which):
        return geo.clip, which * lines + line

    def y_copy(layer, kind, z, shift):
        there = from_y[layer].at[kind, shift - 1] if layer else from_y[layer].at[kind, z, shift - 1]
        at = 0 if layer else z
        return remote(
            mine.at[layer, kind, z, (line + shift) % lines], there,
            fy_send.at[layer, kind, at, shift - 1], fy_recv.at[layer, kind, at, shift - 1],
            geo.on_line(shift),
        )

    def z_copy(layer, kind, hop):
        block = mine.at[layer, kind, order(hop)]
        return remote(
            block if layer else block.at[line], from_z[layer].at[kind, hop],
            fz_send.at[layer, kind, hop], fz_recv.at[layer, kind, hop],
            at_post(far_post if hop == 2 else pair_post),
        )

    def land_x(layer, kind, step):
        z = order(step)
        x_copy(layer, kind, z).wait()
        total = mine[layer, kind, z].astype(f32) + from_x[kind, z].astype(f32)
        mine[layer, kind, z] = total.astype(b16)
        if layer == 0:
            for shift in range(1, lines):
                y_copy(layer, kind, z, shift).start()
            return
        if step < 2:
            z_copy(layer, kind, step).start()
        if all_landed("x", kind):
            device = geo.on_column(1)
            pl.semaphore_signal(
                credit.at[kind], inc=1, device_id=device, device_id_type=pl.DeviceIdType.MESH
            )

    def land_y(layer, kind, step):
        z = order(step)
        total = mine[layer, kind, z, line].astype(f32)
        for shift in range(1, lines):
            y_copy(layer, kind, z, shift).wait()
            total = total + from_y[layer][kind, z, shift - 1].astype(f32)
        mine[layer, kind, z, line] = total.astype(b16)
        if step < 2:
            z_copy(layer, kind, step).start()

    def land_near(layer, kind):
        z_copy(layer, kind, 1).wait()
        here = (layer, kind, far_post) if layer else (layer, kind, far_post, line)
        total = mine[here].astype(f32) + from_z[layer][kind, 1].astype(f32)
        mine[here] = total.astype(b16)
        z_copy(layer, kind, 2).start()

    def land_far(layer, kind):
        here = (layer, kind, post) if layer else (layer, kind, post, line)
        total = mine[here].astype(f32)
        for hop in (0, 2):
            z_copy(layer, kind, hop).wait()
            total = total + from_z[layer][kind, hop].astype(f32)
        if layer == 0:
            feed_out[layer, kind] = total
            return
        mine[here] = total.astype(b16)
        for shift in range(1, lines):
            y_copy(layer, kind, post, shift).start()

    def land_end(layer, kind):
        total = mine[layer, kind, post, line].astype(f32)
        for shift in range(1, lines):
            y_copy(layer, kind, post, shift).wait()
            total = total + from_y[layer][kind, shift - 1].astype(f32)
        feed_out[layer, kind] = total

    def landing(layer, kind, z, shift):
        if kind == INTO:
            return into_y.at[z, shift - 1]
        return proj_y.at[layer, z, shift - 1]

    def ay_copy(layer, kind, z, shift):
        return remote(
            cells[kind][layer].at[(line + shift) % lines, z], landing(layer, kind, z, shift),
            ay_send.at[layer, kind, z, shift - 1], ay_recv.at[layer, kind, z, shift - 1],
            geo.on_line(shift),
        )

    def az_copy(layer, kind, hop):
        return remote(
            cells[kind][layer].at[line, order(hop)], cells_z[kind].at[layer, hop],
            az_send.at[layer, kind, hop], az_recv.at[layer, kind, hop],
            at_post(far_post if hop == 2 else pair_post),
        )

    def ax_copy(layer, kind):
        span = slice(0, 3 * unit) if kind == INTO else slice(3 * unit, 4 * unit)
        return remote(
            a_send.at[layer, span], a_x.at[layer, span], ax_send.at[layer, kind],
            ax_recv.at[layer, kind], geo.on_column(1),
        )

    def send_ay(layer, kind):
        if layer < top and kind == INTO:
            pl.semaphore_wait(into_credit, lines - 1)
        for step in range(posts):
            for shift in range(1, lines):
                ay_copy(layer, kind, order(step), shift).start()

    def land_ay(layer, kind, step):
        z = order(step)
        cell = cells[kind][layer]
        total = cell[line, z].astype(f32)
        for shift in range(1, lines):
            ay_copy(layer, kind, z, shift).wait()
            total = total + landing(layer, kind, z, shift)[...].astype(f32)
        cell[line, z] = total.astype(b16)
        if step < 2:
            az_copy(layer, kind, step).start()

        if layer > 0 and kind == INTO and all_landed("into", kind):
            for shift in range(1, lines):
                pl.semaphore_signal(
                    into_credit, inc=1, device_id=geo.on_line(shift),
                    device_id_type=pl.DeviceIdType.MESH,
                )

    def land_anear(layer, kind):
        cell = cells[kind][layer]
        az_copy(layer, kind, 1).wait()
        total = cell[line, far_post].astype(f32) + cells_z[kind][layer, 1].astype(f32)
        cell[line, far_post] = total.astype(b16)
        az_copy(layer, kind, 2).start()

    def land_afar(layer, kind):
        total = cells[kind][layer][line, post].astype(f32)
        for hop in (0, 2):
            az_copy(layer, kind, hop).wait()
            total = total + cells_z[kind][layer, hop].astype(f32)
        low, high = total[:, :depth], total[:, depth:]
        span = slice(0, 3 * unit) if kind == INTO else slice(3 * unit, 4 * unit)
        attend_out[layer, span] = jnp.where(column == 0, low, high)
        a_send[layer, span] = jnp.where(column == 0, high, low).astype(b16)
        ax_copy(layer, kind).start()

    def land_ax(layer, kind):
        ax_copy(layer, kind).wait()
        span = slice(0, 3 * unit) if kind == INTO else slice(3 * unit, 4 * unit)
        attend_out[layer, span] = attend_out[layer, span] + a_x[layer, span].astype(f32)

    def sum_copies(layer, hop):
        near = ([sibling], [geo.on_line(shift) for shift in range(1, lines)],
                [at_post(pair_post)], [at_post(far_post)], [geo.on_column(1)])
        first = (0, 1, lines, lines + 1, lines + 2)[hop]
        return [
            (remote(
                sums.at[layer], sum_in.at[layer, first + at], sum_send.at[layer, first + at],
                sum_recv.at[layer, first + at], device,
            ), first + at)
            for at, device in enumerate(near[hop])
        ]

    def start_sum(layer):
        shared = lax.broadcasted_iota(jnp.int32, sums.shape[1:], 0) >= OUT_BIAS
        sums[layer] = jnp.where(shared, 0.5 * sums[layer], sums[layer])
        for copy, unused in sum_copies(layer, 0):
            copy.start()

    def land_sum(layer, hop):
        total = sums[layer]
        for copy, at in sum_copies(layer, hop):
            copy.wait()
            total = total + sum_in[layer, at]
        sums[layer] = total
        if hop < 4:
            for copy, unused in sum_copies(layer, hop + 1):
                copy.start()

    schedule = {
        (1, "pair1"): (
            (land_x, 1, DOWN, 1),
        ),
        (1, "dx"): (
            (land_x, 1, DOWN, 2), (land_near, 1, DOWN),
        ),
        (1, "own"): (
            (land_sum, 1, 0), (land_x, 1, DOWN, 0), (land_ay, 1, PROJ, 2), (land_x, 1, UP, 0),
        ),
        (1, "into"): (
            (land_x, 1, DOWN, 3), (land_x, 1, UP, 1), (land_ay, 1, PROJ, 0),
            (land_ay, 1, PROJ, 3),
        ),
        (0, "feed"): (
            (land_sum, 1, 1), (land_ay, 1, INTO, 0),
        ),
        (0, "down"): (
            (land_x, 1, UP, 3), (land_ay, 1, INTO, 1),
        ),
        (0, "proj"): (
            (land_ay, 1, INTO, 2),
        ),
        (0, "pair0"): (
            (land_sum, 1, 2), (land_ay, 1, INTO, 3), (land_ay, 0, PROJ, 0),
            (land_ay, 0, PROJ, 1), (land_x, 0, DOWN, 0),
        ),
        (0, "pair1"): (
            (land_ay, 0, PROJ, 2), (land_anear, 1, INTO), (land_ay, 0, PROJ, 3),
            (land_x, 0, DOWN, 1), (land_y, 0, DOWN, 0), (land_anear, 0, PROJ),
            (land_x, 0, DOWN, 2), (land_ay, 1, PROJ, 1), (land_far, 1, DOWN), (land_x, 1, UP, 2),
        ),
        (0, "pair2"): (
            (land_x, 0, DOWN, 3), (land_y, 0, DOWN, 1), (land_y, 0, DOWN, 2), (land_sum, 1, 3),
            (land_near, 1, UP),
        ),
        (0, "dx"): (
            (land_x, 0, UP, 0), (land_afar, 1, INTO), (land_end, 1, DOWN), (land_anear, 1, PROJ),
        ),
        (0, "own"): (
            (land_near, 0, DOWN), (land_y, 0, DOWN, 3), (land_afar, 0, PROJ), (land_y, 0, UP, 0),
            (land_sum, 0, 0), (land_x, 0, UP, 1),
        ),
        (0, "end"): (
            (land_afar, 1, PROJ), (land_far, 0, DOWN), (land_sum, 0, 1), (land_sum, 0, 2),
            (land_ay, 0, INTO, 1), (land_x, 0, UP, 2), (land_ax, 1, PROJ), (land_far, 1, UP),
            (land_y, 0, UP, 1), (land_x, 0, UP, 3), (land_sum, 1, 4), (land_ax, 0, PROJ),
            (land_ay, 0, INTO, 0), (land_ay, 0, INTO, 2), (land_anear, 0, INTO),
            (land_ax, 1, INTO), (land_sum, 0, 3), (land_ay, 0, INTO, 3), (land_y, 0, UP, 2),
            (land_near, 0, UP), (land_sum, 0, 4), (land_end, 1, UP), (land_afar, 0, INTO),
            (land_ax, 0, INTO), (land_y, 0, UP, 3), (land_far, 0, UP),
        ),
    }

    def progress(layer, phase):
        if geo.aligned:
            for function, *given in schedule.get((layer, phase), ()):
                function(*given)


    def part_copy(layer, turn):
        return remote(
            psend.at[tile_at(turn), :], precv.at[tile_at(turn), :], part_send.at[layer, turn],
            part_recv.at[layer, turn], sibling,
        )

    def du_copy(layer, turn):
        return remote(
            keep["slope"].at[tile_at(turn), :], du_there.at[tile_at(turn), :],
            du_send.at[layer, turn], du_recv.at[layer, turn], sibling,
        )

    def out_copies(turn, place):
        own = pltpu.make_async_copy(out_low.at[turn], place, out_sem.at[turn])
        there = remote(
            out_low.at[turn], place, out_send.at[turn], out_recv.at[turn], geo.origin(turn, core)
        )
        return own, there

    def send_home(copies, turn, target):
        own, there = copies(turn, target.at[geo.parity])
        pl.when(geo.blocked(turn))(own.start)
        pl.when(jnp.logical_not(geo.blocked(turn)))(there.start)

    def wait_home(copies, turn, target):
        own, there = copies(turn, target.at[(post + turn) % held])
        pl.when(geo.blocked(turn))(own.wait)
        pl.when(jnp.logical_not(geo.blocked(turn)))(there.wait)

    def norm_grads(layer, which, values, grad, turn):
        unit, inverse = norm_parts(values)
        gain = gains[layer, which : which + 1, :]
        if layer == top and which == 1:
            result = unit * gain + shifts[layer, which : which + 1, :]
            out_low[turn] = jnp.where(core == 0, result[:slots], result[slots:]).astype(b16)
            send_home(out_copies, turn, out_tokens)
        back, gain_grad, shift_grad = norm_back(unit, inverse, gain, grad)
        add_sum(layer, GAIN + which, everywhere, gain_grad)
        add_sum(layer, SHIFT + which, everywhere, shift_grad)
        return back

    def feed_back_tile(layer, turn):
        now = tile_at(turn)
        grad = low_grad[now, :].astype(f32)
        if layer < top:
            grad = grad + keep["z1"][now, :]
        back = norm_grads(layer, 1, keep["z2"][now, :], grad, turn)
        keep["z2"][now, :] = back
        low = back.astype(b16)
        wide = low.astype(f32)
        turned[:, now] = wide.T.astype(b16)
        add_sum(layer, DOWN_BIAS, everywhere, jnp.sum(wide, 0, keepdims=True))
        size = min(256, quarter)
        for at in range(0, 2 * quarter, size):
            block, start = at // quarter, at % quarter
            lanes = slice(at, at + size)
            grads = dot_nt(low, wdown[lanes, :])
            grads = (grads * keep["slope"][now, lanes].astype(f32)).astype(b16)
            keep["slope"][now, lanes] = grads
            add_sum(
                layer, UP_BIAS + 2 * block + core, slice(start, start + size),
                jnp.sum(grads.astype(f32), 0, keepdims=True),
            )
        total = dot_nt(keep["slope"][now, :], wup[...])
        psend[now, :] = total.astype(b16)
        part_copy(layer, turn).start()
        du_copy(layer, turn).start()

    def down_grads(layer, which, start):
        lanes = pl.ds(pl.multiple_of(which * quarter, quarter), quarter)
        size = lines * unit

        def chunk(at):
            steps = (2 * at, 2 * at + 1)
            left = [
                turned[pl.ds(pl.multiple_of(order(step) * size, size), size), :] for step in steps
            ]
            result = dot(jnp.concatenate(left, 0), keep["act"][:, lanes]).astype(b16)
            for index, step in enumerate(steps):
                z = order(step)
                for row in range(lines):
                    top = index * size + row * unit
                    for piece in range(2):
                        block = result[
                            top : top + unit, piece * quarter // 2 : (piece + 1) * quarter // 2
                        ]
                        span = slice(piece * unit, (piece + 1) * unit)
                        if start:
                            other[DOWN, z, row, span, :] = block
                        else:
                            mine[layer, DOWN, z, row, span, :] = block
                if start:
                    x_copy(layer, DOWN, z).start()

        loop(posts // 2, chunk)

    def up_grads(layer):
        left = [
            keep["hrt"][pl.ds(pl.multiple_of(which * depth, depth), depth), :]
            for which in (1 - column, column)
        ]
        left = jnp.concatenate(left, 0)
        size = quarter // lines
        for block in range(2):
            lanes = slice(block * quarter, (block + 1) * quarter)
            for there, array in ((0, keep["slope"]), (1, du_there)):
                z = 2 * block + core + there * (1 - 2 * core)
                result = dot(left, array[:, lanes]).astype(b16)
                for row in range(lines):
                    span = slice(row * size, (row + 1) * size)
                    other[UP, z, row] = result[:depth, span]
                    mine[layer, UP, z, row] = result[depth:, span]
        for step in range(posts):
            x_copy(layer, UP, order(step)).start()

    def feed_grads(layer, kind):
        if layer < top:
            pl.semaphore_wait(credit.at[kind], 1)
        if kind == UP:
            loaded(layer, "hrt")
            for turn in range(held):
                du_copy(layer, turn).wait()
            up_grads(layer)
        else:
            down_grads(layer, 1 - column, True)
            down_grads(layer, column, False)

    def proj_back_tile(layer, turn):
        now = tile_at(turn)
        part_copy(layer, turn).wait()
        grad = keep["z2"][now, :] + (psend[now, :].astype(f32) + precv[now, :].astype(f32))
        back = norm_grads(layer, 0, keep["z1"][now, :], grad, turn)
        keep["z1"][now, :] = back
        low = back.astype(b16)
        wide = low.astype(f32)
        turned[:, now] = wide.T.astype(b16)
        add_sum(layer, OUT_BIAS, everywhere, jnp.sum(wide, 0, keepdims=True))
        do[now, :] = dot_nt(low, wout[...]).astype(b16)

    lane_head = lax.broadcasted_iota(jnp.int32, (tile, LANES), 1) // HEAD_DIM

    def attend_back_pair(layer, pair):
        lanes = pl.ds(pl.multiple_of(pair * LANES, LANES), LANES)
        key_t = keep["kx"][pair, :, :LANES].astype(f32).T.astype(b16)
        query_t = (keep["q"][:, lanes].astype(f32) * LOG2E).T.astype(b16)
        grad_t = do[:, lanes].astype(f32).T.astype(b16)
        for head in range(2):
            here = slice(head * HEAD_DIM, (head + 1) * HEAD_DIM)
            qx[head, here, :] = query_t[here]
            dox[head, here, :] = grad_t[here]
            rest = -keep["lse"][2 * pair + head, 0:1, :]
            row = lax.broadcasted_iota(jnp.int32, (16, rows), 0)
            extra = jnp.where(row == 0, 1.0, 0.0)
            for part in range(1, 4):
                piece = rest.astype(b16).astype(f32)
                rest = rest - piece
                extra = jnp.where(row == part, piece, extra)
            qx[head, LANES : LANES + 16, :] = extra.astype(b16)

        def turn_step(turn):
            now = tile_at(turn)
            query = keep["q"][now, lanes].astype(f32)
            outgrad = do[now, lanes].astype(f32)
            for head in range(2):
                here = slice(head * HEAD_DIM, (head + 1) * HEAD_DIM)
                chosen = (lane_head == head).astype(f32)
                place = pl.ds(pl.multiple_of((2 * turn + head) * tile, tile), tile)
                do_stack[place, :] = (outgrad * chosen).astype(b16)
                q_stack[place, :] = (query * chosen).astype(b16)
                scores = dot(keep["kx"][pair], qx[head, :, now])
                probs = jnp.exp2(scores)
                probs_all[:, place] = probs.astype(b16)
                grads = dot(keep["v"][:, lanes], dox[head, :, now])
                own = pl.ds(pl.multiple_of(pair * LANES + head * HEAD_DIM, HEAD_DIM), HEAD_DIM)
                delta = jnp.sum(
                    dox[head, here, now].astype(f32) * keep["ot"][own, now], 0, keepdims=True
                )
                score_grads = (probs * (grads - delta)).astype(b16)
                grads_all[:, place] = score_grads
                dqt[here, now] = dot(key_t[here], score_grads)

        loop(held, turn_step)
        query_grad = (dqt[...].T * SCALE).astype(b16)
        value_grad = dot(probs_all[...], do_stack[...]).astype(b16)
        dq[:, lanes] = query_grad
        dkv[:, lanes] = dot(grads_all[...], q_stack[...]).astype(b16)
        dkv[:, pl.ds(pl.multiple_of(half + pair * LANES, LANES), LANES)] = value_grad
        spot = pl.ds(pl.multiple_of(core * half + pair * LANES, LANES), LANES)
        add_sum(layer, QUERY_BIAS, spot, jnp.sum(query_grad.astype(f32), 0, keepdims=True))
        add_sum(layer, VALUE_BIAS, spot, jnp.sum(value_grad.astype(f32), 0, keepdims=True))

    def qkv_copies(layer):
        return [
            remote(source, target, qkv_send.at[layer, at], qkv_recv.at[layer, at], sibling)
            for at, (source, target) in enumerate(((dq, dq_there), (dkv, dkv_there)))
        ]

    def dx_send(shift, turn):
        start = pl.multiple_of((shift * held + turn) * slots, slots)
        return psend.at[pl.ds(start, slots), :]

    def dx_copy(layer, shift, turn):
        return remote(
            dx_send(shift, turn), dx_recv.at[shift * held + turn],
            dx_ssem.at[layer, shift * held + turn], dx_rsem.at[layer, shift * held + turn], sibling,
        )

    def dx_tile(layer, shift, turn):
        now = pl.ds(pl.multiple_of(shift * rows + turn * tile, tile), tile)
        total = dot_nt(dkv[now, :], wkv[...])
        if shift == 0:
            total = total + dot_nt(dq[now, :], wq[...])
        first, second = total[:slots], total[slots:]
        mine_dx[shift * held + turn] = jnp.where(core == 0, first, second).astype(b16)
        dx_send(shift, turn)[...] = jnp.where(core == 0, second, first).astype(b16)
        dx_copy(layer, shift, turn).start()

    def line_copy(layer, shift, turn):
        return remote(
            dx_recv.at[shift * held + turn], line_in.at[layer, shift - 1, turn],
            line_send.at[layer, shift - 1, turn], line_recv.at[layer, shift - 1, turn],
            geo.on_line(lines - shift),
        )

    def more_copy(layer, turn, who):
        place = low_grad.at[block_at(turn, who)]
        return remote(place, place, more_send.at[layer, turn], more_recv.at[layer, turn], sibling)

    def token_copies(turn, place):
        own = pltpu.make_async_copy(low_grad.at[block_at(turn, core)], place, tok_sem.at[turn])
        there = remote(
            low_grad.at[block_at(turn, core)], place, tok_send.at[turn], tok_recv.at[turn],
            geo.origin(turn, core),
        )
        return own, there

    def mine_lanes(x):
        cuts = [x[:, at * depth : (at + 1) * depth] for at in range(2 * CORES)]
        return jnp.where(
            core == 0, jnp.concatenate([cuts[0], cuts[2]], 1), jnp.concatenate([cuts[1], cuts[3]], 1)
        )

    def into_grads(layer):
        units = half // unit
        x = mine_lanes(keep["xall"][...])
        for first, pair in ((0, (dq, dq_there)), (1, (dkv, dkv_there))):
            for there, ref in enumerate(pair):
                owner = core + there * (1 - 2 * core)
                count = ref.shape[0]
                result = dot_tn(ref[...], x[:count]).astype(b16)
                for at in range(result.shape[0] // unit):
                    kind = first + at // units
                    index = (2 * kind + owner) * units + at % units
                    seq = index // 3
                    where = pl.ds(pl.multiple_of(index % 3 * unit, unit), unit)
                    into_cell[seq % lines, seq // lines, where, :] = result[at * unit : (at + 1) * unit]
        send_ay(layer, INTO)

    def proj_grads(layer):
        here, there = keep["o"][...], o_there[...]
        features = jnp.where(
            core == 0,
            jnp.concatenate([here[:, :depth], there[:, :depth]], 1),
            jnp.concatenate([there[:, depth:], here[:, depth:]], 1),
        )
        result = dot(turned[...], features).astype(b16)
        for seq in range(geo.seq_size):
            proj_cell[layer, seq % lines, seq // lines] = result[seq * unit : (seq + 1) * unit]
        send_ay(layer, PROJ)

    def plain_out(layer, names):
        sources = {"du": keep["slope"], "dft": turned, "dat": turned, "dq": dq, "dk": dkv.at[:, :half], "dv": dkv.at[:, half:]}
        order = ("du", "dft", "dat", "dq", "dk", "dv")
        copies = [
            pltpu.make_async_copy(sources[name], plain[layer][order.index(name)], plain_sem.at[order.index(name)])
            for name in names
        ]
        for copy in copies:
            copy.start()
        for copy in copies:
            copy.wait()

    for layer in range(layers - 1, -1, -1):
        last = layer == 0
        below = layer - 1
        if layer == top:
            loaded(layer, "cot")
        else:
            for turn in range(held):
                more_copy(layer + 1, turn, core).wait_send()
                more_copy(layer + 1, turn, 1 - core).wait_recv()
        o_copy(layer).start()
        loaded(layer, "z2", "wdown", "slope", "wup")
        loop(held, functools.partial(feed_back_tile, layer))
        progress(layer, "feed")
        if not last:
            load(below, "wdown", "wup")
        else:
            load(layer, "z1")
        loaded(layer, "act")
        if geo.aligned:
            feed_grads(layer, DOWN)
            progress(layer, "down")
            if UP_AFTER[layer] is None:
                feed_grads(layer, UP)
                progress(layer, "up")
        else:
            plain_out(layer, ("dft",))
        if not last:
            load(below, "act")
        loaded(layer, "z1", "wout")
        loop(held, functools.partial(proj_back_tile, layer))
        progress(layer, "proj")
        if not last:
            load(below, "wout", "z2")
        if geo.aligned:
            loaded(layer, "o")
            o_copy(layer).wait()
            proj_grads(layer)
        loaded(layer, "q", "kx", "v", "ot", "lse")

        def pair_step(pair):
            attend_back_pair(layer, pair)
            for index in range(pairs if geo.aligned else 0):

                @pl.when(pair == index)
                def after_pair(index=index):
                    progress(layer, PAIRS[index])
                    if index == UP_AFTER[layer]:
                        feed_grads(layer, UP)
                        progress(layer, "up")

        loop(pairs, pair_step)
        if not last:
            load(below, "q", "kx", "v", "ot", "lse")
        for copy in qkv_copies(layer):
            copy.start()
        if geo.aligned:
            start_sum(layer)
        loaded(layer, "win")
        if layer == top:
            for turn in range(held):
                wait_home(out_copies, turn, out_tokens)
        for shift in range(1, lines):
            loop(held, functools.partial(dx_tile, layer, shift))
        progress(layer, "dx")
        for shift in range(1, lines):
            for turn in range(held):
                dx_copy(layer, shift, turn).wait()
                at = shift * held + turn
                dx_recv[at] = (mine_dx[at].astype(f32) + dx_recv[at].astype(f32)).astype(b16)
                line_copy(layer, shift, turn).start()
        loop(held, functools.partial(dx_tile, layer, 0))
        progress(layer, "own")
        if not last:
            load(below, "win")
        if geo.aligned:
            for copy in qkv_copies(layer):
                copy.wait()
            loaded(layer, "xall")
            into_grads(layer)
            progress(layer, "into")
        else:
            for turn in range(held):
                du_copy(layer, turn).wait()
            for copy in qkv_copies(layer):
                copy.wait()
            loaded(layer, "hrt", "xall", "o")
            o_copy(layer).wait()
            plain_out(layer, ("du", "dat", "dq", "dk", "dv"))
        if not last:
            load(below, "hrt", "slope", "xall", "o")
        for turn in range(held):
            dx_copy(layer, 0, turn).wait()
            total = mine_dx[turn].astype(f32) + dx_recv[turn].astype(f32)
            for shift in range(1, lines):
                line_copy(layer, shift, turn).wait()
                total = total + line_in[layer, shift - 1, turn].astype(f32)
            if not last:
                low_grad[block_at(turn, core), :] = total.astype(b16)
                more_copy(layer, turn, core).start()
            else:
                total = total + keep["z1"][block_at(turn, core), :]
                low_grad[block_at(turn, core), :] = total.astype(b16)
                send_home(token_copies, turn, grad_tokens)

    progress(0, "end")
    for turn in range(held):
        wait_home(token_copies, turn, grad_tokens)


def backward(geo, layers, cot_rows, weights, kept, gains, shifts):
    width, rows, half, ffn, count = geo.width, geo.rows, geo.half, geo.ffn, geo.count
    held, lines, posts, slots, quarter = geo.held, geo.lines, geo.posts, geo.slots, geo.quarter
    shapes = kept_shapes(geo)
    any_spec = pl.BlockSpec(memory_space=pl.ANY)
    vmem_spec = pl.BlockSpec(memory_space=pltpu.VMEM)
    unit = width // geo.seq_size
    out = [((held, slots, width), b16)] * 2 + [((layers, SUMS, width), f32)]
    out_specs = [any_spec] * 2 + [vmem_spec]
    if geo.aligned:
        out += [
            ((layers, 2, geo.depth, quarter // lines), f32),
            ((layers, 4 * unit, geo.depth), f32),
        ]
        out_specs += [vmem_spec] * 2
    else:
        for unused in range(layers):
            out += [
                ((rows, ffn // CORES), b16), ((width, rows), b16), ((width, rows), b16),
                ((rows, half), b16), ((count, half), b16), ((count, half), b16),
            ]
            out_specs += [any_spec] * 6
    vmem = pltpu.VMEM
    if geo.aligned:
        shapes["hrt"] = (2 * geo.depth, rows), b16
    scratch = [vmem(*shapes[name]) for name in KEPT]
    scratch += [
        vmem((width, half), b16), vmem((width, 2 * half), b16), vmem((half, width), b16),
        vmem((width, 2 * quarter), b16), vmem((2 * quarter, width), b16),
        vmem((rows, half), b16),
        vmem((rows, width), b16),
        vmem((width, rows), b16),
        vmem((rows, ffn // CORES), b16),
        vmem((max(rows, lines * held * slots), width), b16), vmem((rows, width), b16),
        vmem((rows, half), b16),
        vmem((2, 2 * LANES, rows), b16), vmem((2, LANES, rows), b16),
        vmem((rows, half), b16), vmem((count, 2 * half), b16),
        vmem((rows, half), b16), vmem((count, 2 * half), b16),
        vmem((count, 2 * rows), b16), vmem((count, 2 * rows), b16),
        vmem((2 * rows, LANES), b16), vmem((2 * rows, LANES), b16), vmem((LANES, rows), f32),
        vmem((lines * held, slots, width), b16), vmem((lines * held, slots, width), b16),
        vmem((layers, lines - 1, held, slots, width), b16),
    ]
    dma = pltpu.SemaphoreType.DMA
    scratch += [dma(shape) for shape in (
        (layers, len(KEPT) + 16), (layers,), (layers,), (layers, held), (layers, held),
        (layers, held), (layers, held), (layers, 3), (layers, 3),
        (layers, lines * held), (layers, lines * held),
        (layers, lines - 1, held), (layers, lines - 1, held),
        (layers, held), (layers, held), (held,), (held,), (held,), (6,),
        (held,), (held,), (held,),
    )]
    if geo.aligned:
        block = (geo.depth, quarter // lines)
        into, proj = (3 * unit, 2 * geo.depth), (unit, 2 * geo.depth)
        hops = lines + 3
        scratch += [
            vmem((2, posts, lines, *block), b16), vmem((layers, 2, posts, lines, *block), b16),
            vmem((2, posts, lines, *block), b16),
            vmem((2, posts, lines - 1, *block), b16), vmem((2, lines - 1, *block), b16),
            vmem((2, 3, *block), b16), vmem((2, 3, lines, *block), b16),
            vmem((lines, posts, *into), b16), vmem((layers, lines, posts, *proj), b16),
            vmem((posts, lines - 1, *into), b16), vmem((layers, posts, lines - 1, *proj), b16),
            vmem((layers, 3, *into), b16), vmem((layers, 3, *proj), b16),
            vmem((layers, 4 * unit, geo.depth), b16), vmem((layers, 4 * unit, geo.depth), b16),
            vmem((layers, hops, SUMS, width), f32),
        ]
        scratch += [dma(shape) for shape in (
            (layers, 2, posts), (layers, 2, posts),
            (layers, 2, posts, lines - 1), (layers, 2, posts, lines - 1),
            (layers, 2, 3), (layers, 2, 3),
            (layers, 2, posts, lines - 1), (layers, 2, posts, lines - 1),
            (layers, 2, 3), (layers, 2, 3), (layers, 2), (layers, 2),
            (layers, hops), (layers, hops),
        )]
        scratch += [pltpu.SemaphoreType.REGULAR((2,)), pltpu.SemaphoreType.REGULAR]
    stored = [kept[layer][name] for layer in range(layers) for name in KEPT]
    return pl.pallas_call(
        functools.partial(backward_kernel, geo, layers),
        out_shape=[jax.ShapeDtypeStruct(*shape) for shape in out],
        in_specs=[any_spec] * (5 + len(stored)) + [vmem_spec] * 2,
        out_specs=out_specs,
        scratch_shapes=scratch,
        compiler_params=pltpu.CompilerParams(
            collective_id=1, has_side_effects=True, vmem_limit_bytes=VMEM_BACK
        ),
        cost_estimate=pl.CostEstimate(flops=8 * 10**10, bytes_accessed=6 * 10**7, transcendentals=0),
    )(cot_rows, *weights, *stored, gains, shifts)


def finish_kernel(
    geo, core_ref, sums_ref, feed_ref, attend_ref, out_in_ref, grad_in_ref,
    out_ref, grad_ref, into_ref, in_bias_ref, proj_ref, out_bias_ref, up_ref, up_bias_ref, down_ref, down_bias_ref,
    gain_ref, shift_ref,
):
    seq = core_ref[0]
    out_ref[...] = out_in_ref[...]
    grad_ref[...] = grad_in_ref[...]
    layers = feed_ref.shape[0]
    unit = geo.width // geo.seq_size
    wide, span = 2 * unit, geo.ffn // geo.seq_size
    per_row, per_quarter = geo.width // wide, geo.quarter // span

    def turn(rows, amount):
        return pltpu.roll(rows, (geo.width - amount) % geo.width, 1)

    for layer in range(layers):
        up_ref[layer] = feed_ref[layer, UP]
        down = feed_ref[layer, DOWN]
        down_ref[layer] = jnp.concatenate([down[:unit], down[unit:]], 1)
        both = attend_ref[layer].T
        into_ref[layer] = both[:, : 3 * unit]
        proj_ref[layer] = both[:, 3 * unit :]
        sums = sums_ref[layer]
        narrow = turn(sums, seq * unit)
        out_bias_ref[layer : layer + 1, :] = narrow[OUT_BIAS : OUT_BIAS + 1, :unit]
        down_bias_ref[layer : layer + 1, :] = narrow[DOWN_BIAS : DOWN_BIAS + 1, :unit]
        gain_ref[layer] = narrow[GAIN : GAIN + 2, :unit]
        shift_ref[layer] = narrow[SHIFT : SHIFT + 2, :unit]
        middle = turn(sums, seq % per_row * wide)
        first = middle[QUERY_BIAS : QUERY_BIAS + 1, :wide]
        second = middle[VALUE_BIAS : VALUE_BIAS + 1, :wide]
        in_bias_ref[layer : layer + 1, :] = jnp.where(seq < per_row, first, second)
        large = turn(sums, seq % per_quarter * span)
        chosen = large[UP_BIAS : UP_BIAS + 1, :span]
        for block in range(1, 4):
            chosen = jnp.where(
                seq // per_quarter == block, large[UP_BIAS + block : UP_BIAS + block + 1, :span], chosen
            )
        up_bias_ref[layer : layer + 1, :] = chosen


def finish(geo, layers, seq, sums, feed_out, attend_out, out_tokens, grad_tokens):
    unit, width = geo.width // geo.seq_size, geo.width
    span = geo.ffn // geo.seq_size
    depth = geo.depth
    shapes = [
        (layers, depth, 3 * unit), (layers, 2 * unit), (layers, depth, unit), (layers, unit),
        (layers, depth, span), (layers, span), (layers, unit, geo.ffn // geo.clip_size),
        (layers, unit), (layers, 2, unit), (layers, 2, unit),
    ]
    results = list(call(
        functools.partial(finish_kernel, geo), seq, 1,
        [all_of(array) for array in (sums, feed_out, attend_out, out_tokens, grad_tokens)],
        [full(out_tokens.shape, b16)] * 2 + [full(shape, f32) for shape in shapes], [],
        10**7, 10**7,
    ))
    results[8] = jnp.swapaxes(results[8], 1, 2)
    return results


def build(mesh):
    clip_size, seq_size = mesh.shape["clip"], mesh.shape["seq"]

    def shards(
        tokens, lengths, attn_in, in_bias, attn_out, out_bias, ffn_in, ffn_in_bias,
        ffn_out, ffn_out_bias, norm_gain, norm_bias, cotangent,
    ):
        layers = attn_in.shape[0]
        geo = Geometry(mesh, tokens, ffn_in.shape[2])
        geo.locate()
        held, width, ffn, half, quarter = geo.held, geo.width, geo.ffn, geo.half, geo.quarter
        aligned, core = geo.aligned, geo.core
        seq_at = geo.seq

        weights = (attn_in, attn_out, ffn_in, ffn_out)
        cot_rows, kept = forward(
            geo, layers, tokens, cotangent, lengths, weights,
            (in_bias, out_bias, ffn_in_bias, ffn_out_bias, norm_gain, norm_bias),
        )
        out_tokens, grad_tokens, sums, *results = backward(
            geo, layers, cot_rows, weights, kept, norm_gain, norm_bias
        )
        if aligned:
            seq_arg = jnp.reshape(seq_at, (1,)).astype(jnp.int32)
            return tuple(finish(geo, layers, seq_arg, sums, *results, out_tokens, grad_tokens))

        def swap(array):
            pairs = [(at, at ^ 1) for at in range(clip_size)]
            return lax.ppermute(array, "clip", pairs)

        def spread(array):
            array = lax.psum_scatter(
                array.astype(b16), "seq", scatter_dimension=1, tiled=True
            ).astype(b16)
            return lax.psum_scatter(array, "clip", scatter_dimension=0, tiled=True).astype(f32)

        matrices = []
        for layer in range(layers):
            du, df_t, da_t, dq, dk, dv = results[6 * layer : 6 * layer + 6]
            keep = kept[layer]
            x_all = keep["xall"]
            into = [
                jnp.concatenate([jnp.where(core == 0, a, b), jnp.where(core == 0, b, a)], 1)
                for a, b in (
                    (dot_tn(x_all[: array.shape[0]], array), dot_tn(x_all[: array.shape[0]], swap(array)))
                    for array in (dq, dk, dv)
                )
            ]
            proj = jnp.zeros((CORES, half, width), f32)
            proj = lax.dynamic_update_slice_in_dim(proj, dot(da_t, keep["o"]).T[None], core, 0)
            up = jnp.zeros((2, CORES, width, quarter), f32)
            own_up = dot(keep["hrt"], du).reshape(width, 2, 1, quarter).transpose(1, 2, 0, 3)
            up = lax.dynamic_update_slice_in_dim(up, own_up, core, 1)
            down = jnp.zeros((2, CORES, quarter, width), f32)
            own_down = dot(df_t, keep["act"]).T.reshape(2, 1, quarter, width)
            down = lax.dynamic_update_slice_in_dim(down, own_down, core, 1)
            matrices.append((
                spread(jnp.concatenate(into, 1) * 0.5),
                spread(proj.reshape(width, width)),
                spread(up.transpose(2, 0, 1, 3).reshape(width, ffn)),
                spread(down.reshape(ffn, width)),
            ))
        halves = jnp.arange(SUMS)[None, :, None] >= OUT_BIAS
        summed = lax.psum(jnp.where(halves, 0.5 * sums, sums), ("clip", "seq"))

        def share(row, count):
            piece = summed[:, row : row + count].reshape(layers, count * width)
            size = count * width // seq_size
            return lax.dynamic_slice_in_dim(piece, seq_at * size, size, 1)

        into, proj, up, down = (
            jnp.stack([matrices[layer][which] for layer in range(layers)]) for which in range(4)
        )
        return (
            out_tokens, grad_tokens, into, share(QUERY_BIAS, 2), proj, share(OUT_BIAS, 1),
            up, share(UP_BIAS, 4), down, share(DOWN_BIAS, 1),
            jnp.stack([share(GAIN, 1), share(GAIN + 1, 1)], 1),
            jnp.stack([share(SHIFT, 1), share(SHIFT + 1, 1)], 1),
        )

    return shards


def solution(mesh):
    rowed = P("clip", "seq", None)
    in_specs = (rowed, P("clip")) + (P(),) * 10 + (rowed,)
    out_specs = (
        rowed,
        rowed,
        P(None, "clip", "seq"),
        P(None, "seq"),
        P(None, "clip", "seq"),
        P(None, "seq"),
        P(None, "clip", "seq"),
        P(None, "seq"),
        P(None, "clip", "seq"),
        P(None, "seq"),
        P(None, None, "seq"),
        P(None, None, "seq"),
    )
    return jax.shard_map(
        build(mesh), mesh=mesh, in_specs=in_specs, out_specs=out_specs, check_vma=False
    )
```

```python
from copy import copy as duplicate
import functools

import jax
import jax.numpy as jnp
from jax import lax
from jax.experimental import pallas as pl
from jax.experimental.pallas import tpu as pltpu
from jax.sharding import PartitionSpec as P

HEADS = 12
HEAD_DIM = 64
CORES = 2
LANES = 128
SCALE = HEAD_DIM**-0.5
SQRT_HALF = 0.5**0.5
GAUSS = 0.3989422804014327
LOG2E = 1.4426950408889634
EPS = 1e-05
VMEM = 56 * 1024 * 1024
VMEM_BACK = 63 * 1024 * 1024

f32 = jnp.float32
b16 = jnp.bfloat16


def dot(a, b):
    return lax.dot_general(a, b, (((1,), (0,)), ((), ())), preferred_element_type=f32)


def dot_nt(a, b):
    return lax.dot_general(a, b, (((1,), (1,)), ((), ())), preferred_element_type=f32)


def dot_tn(a, b):
    return lax.dot_general(a, b, (((0,), (0,)), ((), ())), preferred_element_type=f32)


def norm_parts(values):
    center = values - jnp.mean(values, -1, keepdims=True)
    inverse = lax.rsqrt(jnp.mean(center * center, -1, keepdims=True) + EPS)
    return center * inverse, inverse


def norm_back(unit, inverse, gain, grad):
    scaled = grad * gain
    mean_one = jnp.mean(scaled, -1, keepdims=True)
    mean_two = jnp.mean(scaled * unit, -1, keepdims=True)
    back = inverse * (scaled - mean_one - unit * mean_two)
    return back, jnp.sum(grad * unit, 0, keepdims=True), jnp.sum(grad, 0, keepdims=True)


def call(kernel, core, grid, ins, outs, scratch, flops, moved):
    in_specs = [pl.BlockSpec(block, lambda g, c, at=at: at(g, c[0])) for unused, block, at in ins]
    out_specs = [pl.BlockSpec(block, lambda g, c, at=at: at(g, c[0])) for s, d, block, at in outs]
    return pl.pallas_call(
        kernel,
        grid_spec=pltpu.PrefetchScalarGridSpec(
            num_scalar_prefetch=1,
            grid=(grid,),
            in_specs=in_specs,
            out_specs=out_specs,
            scratch_shapes=scratch,
        ),
        out_shape=[jax.ShapeDtypeStruct(shape, dtype) for shape, dtype, b, at in outs],
        compiler_params=pltpu.CompilerParams(
            dimension_semantics=("arbitrary",), vmem_limit_bytes=VMEM
        ),
        cost_estimate=pl.CostEstimate(flops=flops, bytes_accessed=moved, transcendentals=0),
    )(core, *[array for array, b, at in ins])


def all_of(array):
    zeros = (0,) * array.ndim
    return (array, array.shape, lambda g, c: zeros)


def full(shape, dtype):
    zeros = (0,) * len(shape)
    return (shape, dtype, shape, lambda g, c: zeros)


class Geometry:
    def __init__(self, mesh, tokens, ffn):
        self.clip_size, self.seq_size = mesh.shape["clip"], mesh.shape["seq"]
        self.columns = self.clip_size // CORES
        self.held, self.slots, self.width = tokens.shape
        self.ffn = ffn
        self.posts = self.held * CORES
        self.lines = self.seq_size // self.posts
        self.tile = CORES * self.slots
        self.rows = self.held * self.tile
        self.count = self.rows * self.lines
        self.half = self.width // CORES
        self.pairs = self.half // LANES
        self.heads = 2 * self.pairs
        self.quarter = ffn // 4
        self.depth = self.width // self.clip_size
        self.aligned = self.columns == 2 and (ffn // self.seq_size) % LANES == 0

    def locate(self):
        self.clip = lax.axis_index("clip")
        self.seq = lax.axis_index("seq")
        self.core = self.clip % CORES
        self.column = self.clip // CORES
        self.post = self.seq // self.lines
        self.line = self.seq % self.lines
        self.parity = self.post % self.held

    def sibling(self):
        return self.clip + 1 - 2 * self.core, self.seq

    def on_line(self, shift):
        return self.clip, self.post * self.lines + (self.line + shift) % self.lines

    def on_post(self, shift):
        return self.clip, (self.post + shift) % self.posts * self.lines + self.line

    def on_column(self, shift):
        return (self.column + shift) % self.columns * CORES + self.core, self.seq

    def goal(self, turn):
        post = self.held * self.core + (self.post + turn) % self.held
        return self.column * CORES + self.post // self.held, post * self.lines + self.line

    def origin(self, turn, who):
        post = self.held * who + (self.parity + turn) % self.held
        return self.column * CORES + self.post // self.held, post * self.lines + self.line

    def blocked(self, turn):
        return jnp.logical_and(self.post // self.held == self.core, turn == 0)


def remote(source, target, send, receive, device):
    return pltpu.make_async_remote_copy(
        src_ref=source, dst_ref=target, send_sem=send, recv_sem=receive,
        device_id=device, device_id_type=pl.DeviceIdType.MESH,
    )


def meet(geo, devices):
    barrier = pltpu.get_barrier_semaphore()
    total = 0
    for device in devices:
        other = jnp.logical_or(device[0] != geo.clip, device[1] != geo.seq)

        @pl.when(other)
        def greet(device=device):
            pl.semaphore_signal(
                barrier, inc=1, device_id=device, device_id_type=pl.DeviceIdType.MESH
            )

        total = total + other.astype(jnp.int32)
    pl.semaphore_wait(barrier, total)


def loop(count, body):
    def step(at, carry):
        body(at)
        return carry

    lax.fori_loop(0, count, step, 0)


def gelu_parts(inner):
    bell = jnp.exp2((inner * inner) * (-0.5 * LOG2E))
    phi = 0.5 + 0.5 * lax.erf(inner * SQRT_HALF)
    return phi, phi + inner * (GAUSS * bell)


KEPT = ("xall", "kx", "v", "q", "ot", "lse", "o", "z1", "hrt", "act", "slope", "z2")


def kept_shapes(geo):
    rows, width, half, count = geo.rows, geo.width, geo.half, geo.count
    return {
        "xall": ((count, width), b16),
        "kx": ((geo.pairs, count, 2 * LANES), b16),
        "v": ((count, half), b16),
        "q": ((rows, half), b16),
        "ot": ((half, rows), f32),
        "lse": ((geo.heads, 8, rows), f32),
        "o": ((rows, half), b16),
        "z1": ((rows, width), f32),
        "hrt": ((width, rows), b16),
        "act": ((rows, geo.ffn // CORES), b16),
        "slope": ((rows, geo.ffn // CORES), b16),
        "z2": ((rows, width), f32),
    }


def forward_kernel(geo, layers, *refs):
    refs = list(refs)

    def take(count):
        taken = refs[:count]
        del refs[:count]
        return taken

    tokens, cotangent, w_in, w_out, w_up, w_down = take(6)
    lengths, in_bias, out_bias, up_bias, down_bias, gains, shifts = take(7)
    (cot_rows,) = take(1)
    stored = [dict(zip(KEPT, take(len(KEPT)))) for unused in range(layers)]
    kept = [dict(zip(KEPT, take(len(KEPT)))) for unused in range(layers)]
    wq, wkv, wout, wup, wdown = take(5)
    qx, vt, state, hidden, lens, lens_there, psend, precv, running = take(9)
    (load_sem, save_sem, tok_sem, tok_send, tok_recv, cot_sem, cot_send, cot_recv, sib_send,
     sib_recv, line_send, line_recv, pass_send, pass_recv, part_send, part_recv,
     len_sem) = take(17)

    geo = duplicate(geo)
    geo.locate()
    core, tile, slots = geo.core, geo.tile, geo.slots
    held, lines, rows, width, half = geo.held, geo.lines, geo.rows, geo.width, geo.half
    quarter, pairs = geo.quarter, geo.pairs
    sibling = geo.sibling()

    loads = []
    for layer in range(layers):
        targets = (wq.at[layer], wkv.at[layer, :, :half], wkv.at[layer, :, half:])
        parts = [
            (w_in.at[layer, :, pl.ds(pl.multiple_of((kind * CORES + core) * half, half), half)],
             targets[kind])
            for kind in range(3)
        ]
        parts.append((w_out.at[layer, pl.ds(pl.multiple_of(core * half, half), half), :], wout.at[layer]))
        for block in range(2):
            at = pl.ds(pl.multiple_of((2 * block + core) * quarter, quarter), quarter)
            span = slice(block * quarter, (block + 1) * quarter)
            parts.append((w_up.at[layer, :, at], wup.at[layer, :, span]))
            parts.append((w_down.at[layer, at, :], wdown.at[layer, span, :]))
        loads.append([
            pltpu.make_async_copy(source, target, load_sem.at[layer, at])
            for at, (source, target) in enumerate(parts)
        ])
    for copy in loads[0]:
        copy.start()

    sources = [geo.origin(turn, who) for turn in range(held) for who in range(CORES)]
    goals = [geo.goal(turn) for turn in range(held)]
    goals = goals + [(device[0] + 1 - 2 * (device[0] % CORES), device[1]) for device in goals]
    near = [sibling] + [geo.on_line(shift) for shift in range(1, lines)]
    meet(geo, near + sources + goals)

    first = kept[0]["xall"]

    def block_at(turn, who, shift=0):
        start = shift * rows + turn * tile + who * slots
        return pl.ds(start if isinstance(start, int) else pl.multiple_of(start, slots), slots)

    def token_copies(turn, who):
        mine = tokens.at[(geo.post + turn) % held]
        place = first.at[block_at(turn, who)]
        own = pltpu.make_async_copy(mine, place, tok_sem.at[turn])
        return own, remote(mine, place, tok_send.at[turn], tok_recv.at[turn], geo.goal(turn))

    def token_start(turn):
        own, there = token_copies(turn, geo.post // held)
        pl.when(geo.blocked(turn))(own.start)
        pl.when(jnp.logical_not(geo.blocked(turn)))(there.start)

    def token_wait(turn):
        own, there = token_copies(turn, core)
        pl.when(geo.blocked(turn))(own.wait)
        pl.when(jnp.logical_not(geo.blocked(turn)))(there.wait)

    def to_sibling(array, turn, who, shift, send, receive):
        place = array.at[block_at(turn, who, shift)]
        return remote(place, place, send, receive, sibling)

    def to_line(layer, turn, shift):
        array = kept[layer]["xall"]
        source = array.at[block_at(turn, core)]
        target = array.at[block_at(turn, core, shift)]
        return remote(
            source, target, line_send.at[layer, turn, shift - 1], line_recv.at[layer, turn, shift - 1],
            geo.on_line(shift),
        )

    for turn in range(held):
        token_start(turn)
    clip_row = lax.broadcasted_iota(jnp.int32, lens.shape, 0)
    filled = jnp.full(lens.shape, lengths[0], jnp.int32)
    for clip in range(1, held):
        filled = jnp.where(clip_row == clip, lengths[clip], filled)
    lens[...] = filled
    len_copy = remote(lens, lens_there, len_sem.at[0], len_sem.at[1], sibling)
    len_copy.start()

    def clear(at):
        qx[at] = jnp.zeros(qx.shape[1:], b16)
        qx[at, LANES : LANES + 16, :] = (
            lax.broadcasted_iota(jnp.int32, (16, rows), 0) == 0
        ).astype(f32).astype(b16)

    loop(geo.heads, clear)
    len_copy.wait()
    known = jnp.where(geo.post // held == core, lens[...], lens_there[...])
    length = known[0:1, :]
    for clip in range(1, held):
        length = jnp.where(geo.parity == clip, known[clip : clip + 1, :], length)
    lane = lax.broadcasted_iota(jnp.int32, (slots, LANES), 1)
    slot = lax.broadcasted_iota(jnp.int32, (slots, LANES), 0)
    for shift in range(lines):
        for turn in range(held):
            for who in range(CORES):
                post = held * who + (geo.parity + turn) % held
                line = (geo.line + lines - shift) % lines
                outside = (post * lines + line) * slots + slot >= length
                mask = jnp.where(jnp.logical_and(lane == 0, outside), -1e30, 0.0)
                mask = jnp.where(jnp.logical_and(lane > 0, lane < 4), 1.0, mask).astype(b16)
                for layer in range(layers):
                    for pair in range(pairs):
                        kept[layer]["kx"][pair, block_at(turn, who, shift), LANES:] = mask

    for turn in range(held):
        token_wait(turn)
        to_sibling(first, turn, core, 0, sib_send.at[turn], sib_recv.at[turn]).start()
        for shift in range(1, lines):
            to_line(0, turn, shift).start()
    for copy in loads[0]:
        copy.wait()
    for copy in loads[1]:
        copy.start()

    def cot_copies(turn, flip):
        mine = cotangent.at[(geo.post + turn) % held]
        place = cot_rows.at[block_at(turn, geo.post // held)]
        goal = geo.goal(turn)
        if flip:
            goal = (goal[0] + 1 - 2 * (goal[0] % CORES), goal[1])
        own = pltpu.make_async_copy(mine, place, cot_sem.at[turn, flip])
        there = remote(
            mine, place, cot_send.at[turn, flip], cot_recv.at[turn, geo.post // held], goal
        )
        here = jnp.logical_and(goal[0] == geo.clip, goal[1] == geo.seq)
        return own, there, here

    def cot_start():
        for turn in range(held):
            for flip in range(CORES):
                own, there, here = cot_copies(turn, flip)
                pl.when(here)(own.start)
                pl.when(jnp.logical_not(here))(there.start)

    def cot_wait():
        for turn in range(held):
            for flip in range(CORES):
                own, there, here = cot_copies(turn, flip)
                pl.when(here)(own.wait)
                pl.when(jnp.logical_not(here))(there.wait_send)
            for who in range(CORES):
                source = geo.origin(turn, who)
                place = cot_rows.at[block_at(turn, who)]
                there = remote(
                    cotangent.at[0], place, cot_send.at[turn, 0], cot_recv.at[turn, who], source
                )
                here = jnp.logical_and(source[0] == geo.clip, source[1] == geo.seq)
                pl.when(jnp.logical_not(here))(there.wait_recv)

    def key_tile(layer, at):
        keep = kept[layer]
        now = pl.ds(pl.multiple_of(at, tile), tile)
        both = dot(keep["xall"][now, :], wkv[layer])
        key = both[:, :half].astype(b16)
        for pair in range(pairs):
            keep["kx"][pair, now, :LANES] = key[:, pair * LANES : (pair + 1) * LANES]
        bias = in_bias[layer : layer + 1, pl.ds(pl.multiple_of(width + core * half, half), half)]
        value = (both[:, half:] + bias).astype(b16)
        keep["v"][now, :] = value
        vt[:, now] = value.astype(f32).T.astype(b16)

    def query_tile(layer, at):
        keep = kept[layer]
        now = pl.ds(pl.multiple_of(at, tile), tile)
        bias = in_bias[layer : layer + 1, pl.ds(pl.multiple_of(core * half, half), half)]
        query = (dot(keep["xall"][now, :], wq[layer]) + bias).astype(b16)
        query = (query * SCALE).astype(b16)
        keep["q"][now, :] = query
        turned = (query.astype(f32) * LOG2E).T.astype(b16)
        for head in range(geo.heads):
            inside = head % 2 * HEAD_DIM
            qx[head, inside : inside + HEAD_DIM, now] = (
                turned[head * HEAD_DIM : (head + 1) * HEAD_DIM]
            )

    def attend_block(layer, shift):
        keep = kept[layer]
        span = slice(shift * rows, (shift + 1) * rows)

        size = min(256, rows)
        cuts = [slice(start, start + size) for start in range(shift * rows, (shift + 1) * rows, size)]

        def pair_step(pair):
            heads = [2 * pair, 2 * pair + 1]
            scores = [
                [dot(keep["kx"][pair, cut, :], qx[head]) for cut in cuts] for head in heads
            ]
            for head, pieces in zip(heads, scores):
                here = pl.ds(pl.multiple_of(head * HEAD_DIM, HEAD_DIM), HEAD_DIM)
                top = functools.reduce(
                    jnp.maximum, [jnp.max(piece, 0, keepdims=True) for piece in pieces]
                )
                if shift > 0:
                    before = keep["lse"][head, 0:1, :]
                    top = jnp.maximum(top, before)
                    shrink = jnp.exp2(before - top)
                total = attended = None
                for piece, cut in zip(pieces, cuts):
                    weights = jnp.exp2(piece - top)
                    sums = jnp.sum(weights, 0, keepdims=True)
                    values = dot(vt[here, cut], weights.astype(b16))
                    total = sums if total is None else total + sums
                    attended = values if attended is None else attended + values
                if shift > 0:
                    total = total + shrink * running[head, 0:1, :]
                    attended = attended + shrink * keep["ot"][here, :]
                if shift < lines - 1:
                    running[head, 0:1, :] = total
                    keep["ot"][here, :] = attended
                    keep["lse"][head, 0:1, :] = top
                else:
                    keep["ot"][here, :] = attended / total
                    keep["lse"][head, 0:1, :] = top + jnp.log(total) * LOG2E

        loop(pairs, pair_step)

    def project_tile(layer, turn):
        keep = kept[layer]
        now = pl.ds(pl.multiple_of(turn * tile, tile), tile)
        attended = keep["ot"][:, now].T.astype(b16)
        keep["o"][now, :] = attended
        share(2 * layer, turn, dot(attended, wout[layer]))

    def part_copy(which, turn):
        now = pl.ds(pl.multiple_of(turn * tile, tile), tile)
        return remote(
            psend.at[which, now, :], precv.at[which, now, :], part_send.at[which, turn],
            part_recv.at[which, turn], sibling,
        )

    def share(which, turn, part):
        now = pl.ds(pl.multiple_of(turn * tile, tile), tile)
        psend[which, now, :] = part.astype(b16)
        part_copy(which, turn).start()

    def collect(which, turn):
        now = pl.ds(pl.multiple_of(turn * tile, tile), tile)
        part_copy(which, turn).wait()
        return psend[which, now, :].astype(f32) + precv[which, now, :].astype(f32)

    def feed_tile(layer, turn):
        keep = kept[layer]
        now = pl.ds(pl.multiple_of(turn * tile, tile), tile)
        x = first[now, :].astype(f32) if layer == 0 else state[now, :]
        summed = x + collect(2 * layer, turn) + out_bias[layer : layer + 1, :]
        keep["z1"][now, :] = summed
        unit, unused = norm_parts(summed)
        normal = unit * gains[layer, 0:1, :] + shifts[layer, 0:1, :]
        hidden[now, :] = normal
        low = normal.astype(b16)
        keep["hrt"][:, now] = low.astype(f32).T.astype(b16)
        size = min(256, quarter)
        for at in range(0, 2 * quarter, size):
            block, start = at // quarter, at % quarter
            bias = up_bias[
                layer : layer + 1,
                pl.ds(pl.multiple_of((2 * block + core) * quarter + start, size), size),
            ]
            inner = dot(low, wup[layer, :, at : at + size]) + bias
            phi, slope = gelu_parts(inner)
            keep["act"][now, at : at + size] = (inner * phi).astype(b16)
            keep["slope"][now, at : at + size] = slope.astype(b16)
        total = dot(keep["act"][now, :], wdown[layer])
        share(2 * layer + 1, turn, total)

    def norm_tile(layer, turn):
        keep = kept[layer]
        now = pl.ds(pl.multiple_of(turn * tile, tile), tile)
        summed = hidden[now, :] + collect(2 * layer + 1, turn) + down_bias[layer : layer + 1, :]
        keep["z2"][now, :] = summed
        if layer < layers - 1:
            unit, unused = norm_parts(summed)
            result = unit * gains[layer, 1:2, :] + shifts[layer, 1:2, :]
            state[now, :] = result
            kept[layer + 1]["xall"][now, :] = result.astype(b16)

    saves = []

    def save(layer, names):
        for name in names:
            copy = pltpu.make_async_copy(
                kept[layer][name], stored[layer][name], save_sem.at[layer, KEPT.index(name)]
            )
            copy.start()
            saves.append(copy)

    for layer in range(layers):
        x_all = kept[layer]["xall"]
        if layer == 0:
            for turn in range(held):
                to_sibling(x_all, turn, core, 0, sib_send.at[turn], sib_recv.at[turn]).wait_send()
                to_sibling(x_all, turn, 1 - core, 0, sib_send.at[turn], sib_recv.at[turn]).wait_recv()
                key_tile(layer, turn * tile)
                query_tile(layer, turn * tile)
        for shift in range(lines):
            if shift > 0:
                for turn in range(held):
                    to_line(layer, turn, shift).wait()
                    to_sibling(
                        x_all, turn, core, shift,
                        pass_send.at[layer, turn, shift - 1], pass_recv.at[layer, turn, shift - 1],
                    ).start()
                for turn in range(held):
                    send = pass_send.at[layer, turn, shift - 1]
                    receive = pass_recv.at[layer, turn, shift - 1]
                    to_sibling(x_all, turn, core, shift, send, receive).wait_send()
                    to_sibling(x_all, turn, 1 - core, shift, send, receive).wait_recv()
                    key_tile(layer, shift * rows + turn * tile)
            if shift == lines - 1:
                save(layer, ("xall", "kx", "v", "q"))
                if layer == 0:
                    cot_start()

            attend_block(layer, shift)
        loop(held, functools.partial(project_tile, layer))
        save(layer, ("ot", "lse", "o"))
        loop(held, functools.partial(feed_tile, layer))
        save(layer, ("z1", "hrt", "act", "slope"))
        for turn in range(held):
            norm_tile(layer, turn)
            if layer < layers - 1:
                for shift in range(1, lines):
                    to_line(layer + 1, turn, shift).start()
                if turn == 0:
                    for copy in loads[layer + 1]:
                        copy.wait()
                key_tile(layer + 1, turn * tile)
                query_tile(layer + 1, turn * tile)
        save(layer, ("z2",))

    cot_wait()
    for copy in saves:
        copy.wait()


def forward(geo, layers, tokens, cotangent, lengths, weights, vectors):
    width, rows, half, ffn = geo.width, geo.rows, geo.half, geo.ffn
    shapes = kept_shapes(geo)
    any_spec = pl.BlockSpec(memory_space=pl.ANY)
    vmem_spec = pl.BlockSpec(memory_space=pltpu.VMEM)
    out_shape = [
        jax.ShapeDtypeStruct((rows, width), b16),
    ]
    out_shape += [jax.ShapeDtypeStruct(*shapes[name]) for unused in range(layers) for name in KEPT]
    scratch = [pltpu.VMEM(*shapes[name]) for unused in range(layers) for name in KEPT]
    scratch += [
        pltpu.VMEM((layers, width, half), b16),
        pltpu.VMEM((layers, width, 2 * half), b16),
        pltpu.VMEM((layers, half, width), b16),
        pltpu.VMEM((layers, width, 2 * geo.quarter), b16),
        pltpu.VMEM((layers, 2 * geo.quarter, width), b16),
        pltpu.VMEM((geo.heads, 2 * LANES, rows), b16),
        pltpu.VMEM((half, geo.count), b16),
        pltpu.VMEM((rows, width), f32),
        pltpu.VMEM((rows, width), f32),
        pltpu.VMEM((8, LANES), jnp.int32),
        pltpu.VMEM((8, LANES), jnp.int32),
        pltpu.VMEM((2 * layers, rows, width), b16),
        pltpu.VMEM((2 * layers, rows, width), b16),
        pltpu.VMEM((geo.heads, 8, rows), f32),
    ]
    held, lines = geo.held, max(geo.lines - 1, 1)
    dma = pltpu.SemaphoreType.DMA
    scratch += [dma(shape) for shape in (
        (layers, 8), (layers, len(KEPT)), (held,), (held,), (held,),
        (held, CORES), (held, CORES), (held, CORES), (held,), (held,),
        (layers, held, lines), (layers, held, lines), (layers, held, lines), (layers, held, lines),
        (2 * layers, held), (2 * layers, held), (2,),
    )]
    results = pl.pallas_call(
        functools.partial(forward_kernel, geo, layers),
        out_shape=out_shape,
        in_specs=[any_spec] * 6 + [pl.BlockSpec(memory_space=pltpu.SMEM)] + [vmem_spec] * 6,
        out_specs=[any_spec] * len(out_shape),
        scratch_shapes=scratch,
        compiler_params=pltpu.CompilerParams(
            collective_id=0, has_side_effects=True, vmem_limit_bytes=VMEM
        ),
        cost_estimate=pl.CostEstimate(flops=3 * 10**10, bytes_accessed=4 * 10**7, transcendentals=0),
    )(tokens, cotangent, *weights, lengths, *vectors)
    count = len(KEPT)
    kept = [
        dict(zip(KEPT, results[1 + layer * count : 1 + (layer + 1) * count]))
        for layer in range(layers)
    ]
    return results[0], kept


QUERY_BIAS, VALUE_BIAS, UP_BIAS, OUT_BIAS, DOWN_BIAS, GAIN, SHIFT = 0, 1, 2, 6, 7, 8, 10
SUMS = 16
UP, DOWN = 0, 1
INTO, PROJ = 0, 1
PAIRS = ("pair0", "pair1", "pair2")
UP_AFTER = (1, 1)


def backward_kernel(geo, layers, *refs):
    refs = list(refs)

    def take(count):
        taken = refs[:count]
        del refs[:count]
        return taken

    cot_rows, w_in, w_out, w_up, w_down = take(5)
    stored = [dict(zip(KEPT, take(len(KEPT)))) for unused in range(layers)]
    gains, shifts = take(2)
    out_tokens, grad_tokens, sums = take(3)
    if geo.aligned:
        feed_out, attend_out = take(2)
    else:
        plain = [take(6) for unused in range(layers)]
    keep = dict(zip(KEPT, take(len(KEPT))))
    wq, wkv, wout, wup, wdown = take(5)
    (o_there, low_grad, turned, du_there, psend, precv, do, qx, dox, dq, dkv, dq_there,
     dkv_there, probs_all, grads_all, do_stack, q_stack, dqt, mine_dx, dx_recv, line_in) = take(21)
    out_low = mine_dx
    (load_sem, o_send, o_recv, du_send, du_recv, part_send, part_recv, qkv_send, qkv_recv,
     dx_ssem, dx_rsem, line_send, line_recv, more_send, more_recv, tok_sem, tok_send,
     tok_recv, plain_sem, out_sem, out_send, out_recv) = take(22)
    if geo.aligned:
        (other, mine, from_x, y_first, y_last, z_first, z_last, into_cell, proj_cell, into_y, proj_y, into_z, proj_z,
         a_send, a_x, sum_in) = take(16)
        from_y, from_z = (y_first, y_last), (z_first, z_last)
        cells = [[into_cell] * layers, [proj_cell.at[layer] for layer in range(layers)]]
        cells_z = (into_z, proj_z)
        (fx_send, fx_recv, fy_send, fy_recv, fz_send, fz_recv, ay_send, ay_recv, az_send, az_recv,
         ax_send, ax_recv, sum_send, sum_recv) = take(14)
        credit, into_credit = take(2)

    geo = duplicate(geo)
    geo.locate()
    core, tile, slots = geo.core, geo.tile, geo.slots
    held, lines, rows, width, half = geo.held, geo.lines, geo.rows, geo.width, geo.half
    quarter, pairs, posts, depth = geo.quarter, geo.pairs, geo.posts, geo.depth
    post, line, column = geo.post, geo.line, geo.column
    unit = width // geo.seq_size
    sibling = geo.sibling()

    def tile_at(turn):
        return pl.ds(pl.multiple_of(turn * tile, tile), tile)

    def block_at(turn, who, shift=0):
        start = shift * rows + turn * tile + who * slots
        return pl.ds(start if isinstance(start, int) else pl.multiple_of(start, slots), slots)

    NAMES = KEPT + ("win", "wout", "wup", "wdown", "cot")

    def load_copies(layer, name):
        where = load_sem.at[layer, NAMES.index(name)]
        if name == "win":
            targets = (wq, wkv.at[:, :half], wkv.at[:, half:])
            return [
                pltpu.make_async_copy(
                    w_in.at[layer, :, pl.ds(pl.multiple_of((kind * CORES + core) * half, half), half)],
                    targets[kind], load_sem.at[layer, len(NAMES) + kind],
                )
                for kind in range(3)
            ]
        if name == "wout":
            at = pl.ds(pl.multiple_of(core * half, half), half)
            return [pltpu.make_async_copy(w_out.at[layer, at, :], wout, where)]
        if name in ("wup", "wdown"):
            copies = []
            for block in range(2):
                at = pl.ds(pl.multiple_of((2 * block + core) * quarter, quarter), quarter)
                slot = len(NAMES) + 3 + 2 * (name == "wdown") + block
                if name == "wup":
                    pair = w_up.at[layer, :, at], wup.at[:, block * quarter : (block + 1) * quarter]
                else:
                    pair = w_down.at[layer, at, :], wdown.at[block * quarter : (block + 1) * quarter, :]
                copies.append(pltpu.make_async_copy(*pair, load_sem.at[layer, slot]))
            return copies
        if name == "hrt" and geo.aligned:
            return [
                pltpu.make_async_copy(
                    stored[layer][name].at[pl.ds(pl.multiple_of((2 * which + core) * depth, depth), depth), :],
                    keep[name].at[which * depth : (which + 1) * depth, :],
                    load_sem.at[layer, len(NAMES) + 7 + which],
                )
                for which in range(2)
            ]
        if name == "cot":
            return [pltpu.make_async_copy(cot_rows, low_grad, where)]
        return [pltpu.make_async_copy(stored[layer][name], keep[name], where)]

    def load(layer, *names):
        for name in names:
            for copy in load_copies(layer, name):
                copy.start()

    def loaded(layer, *names):
        for name in names:
            for copy in load_copies(layer, name):
                copy.wait()

    top = layers - 1
    load(top, "z2", "cot", "wdown", "slope", "wup", "act", "z1", "wout", "q", "kx", "v", "ot",
         "lse", "win", "hrt", "xall", "o")

    sources = [geo.origin(turn, who) for turn in range(held) for who in range(CORES)]
    goals = [geo.goal(turn) for turn in range(held)]
    near = [sibling] + [geo.on_line(shift) for shift in range(1, lines)]
    if geo.aligned:
        near += [geo.on_post(shift) for shift in range(1, posts)]
        near += [geo.on_column(shift) for shift in range(1, geo.columns)]
    goals = goals + [(device[0] + 1 - 2 * (device[0] % CORES), device[1]) for device in goals]
    meet(geo, near + sources + goals)

    def o_copy(layer):
        return remote(stored[layer]["o"], o_there, o_send.at[layer], o_recv.at[layer], sibling)

    def clear(at):
        qx[at] = jnp.zeros(qx.shape[1:], b16)
        dox[at] = jnp.zeros(dox.shape[1:], b16)

    loop(2, clear)
    sums[...] = jnp.zeros_like(sums)

    def add_sum(layer, row, lanes, value):
        sums[layer, pl.ds(row, 1), lanes] += value

    everywhere = slice(None)


    def x_copy(layer, kind, z):
        return remote(
            other.at[kind, z], from_x.at[kind, z], fx_send.at[layer, kind, z],
            fx_recv.at[layer, kind, z], geo.on_column(1),
        )

    pair_post = post + 1 - 2 * (post % 2)
    far_post = (post + 2) % posts

    landed = {}

    def all_landed(hop, kind):
        landed[hop, kind] = landed.get((hop, kind), 0) + 1
        return landed[hop, kind] == posts

    def order(step):
        return (pair_post + step // 2 * (far_post - pair_post) + step % 2 * 2) % posts

    def at_post(which):
        return geo.clip, which * lines + line

    def y_copy(layer, kind, z, shift):
        there = from_y[layer].at[kind, shift - 1] if layer else from_y[layer].at[kind, z, shift - 1]
        at = 0 if layer else z
        return remote(
            mine.at[layer, kind, z, (line + shift) % lines], there,
            fy_send.at[layer, kind, at, shift - 1], fy_recv.at[layer, kind, at, shift - 1],
            geo.on_line(shift),
        )

    def z_copy(layer, kind, hop):
        block = mine.at[layer, kind, order(hop)]
        return remote(
            block if layer else block.at[line], from_z[layer].at[kind, hop],
            fz_send.at[layer, kind, hop], fz_recv.at[layer, kind, hop],
            at_post(far_post if hop == 2 else pair_post),
        )

    def land_x(layer, kind, step):
        z = order(step)
        x_copy(layer, kind, z).wait()
        total = mine[layer, kind, z].astype(f32) + from_x[kind, z].astype(f32)
        mine[layer, kind, z] = total.astype(b16)
        if layer == 0:
            for shift in range(1, lines):
                y_copy(layer, kind, z, shift).start()
            return
        if step < 2:
            z_copy(layer, kind, step).start()
        if all_landed("x", kind):
            device = geo.on_column(1)
            pl.semaphore_signal(
                credit.at[kind], inc=1, device_id=device, device_id_type=pl.DeviceIdType.MESH
            )

    def land_y(layer, kind, step):
        z = order(step)
        total = mine[layer, kind, z, line].astype(f32)
        for shift in range(1, lines):
            y_copy(layer, kind, z, shift).wait()
            total = total + from_y[layer][kind, z, shift - 1].astype(f32)
        mine[layer, kind, z, line] = total.astype(b16)
        if step < 2:
            z_copy(layer, kind, step).start()

    def land_near(layer, kind):
        z_copy(layer, kind, 1).wait()
        here = (layer, kind, far_post) if layer else (layer, kind, far_post, line)
        total = mine[here].astype(f32) + from_z[layer][kind, 1].astype(f32)
        mine[here] = total.astype(b16)
        z_copy(layer, kind, 2).start()

    def land_far(layer, kind):
        here = (layer, kind, post) if layer else (layer, kind, post, line)
        total = mine[here].astype(f32)
        for hop in (0, 2):
            z_copy(layer, kind, hop).wait()
            total = total + from_z[layer][kind, hop].astype(f32)
        if layer == 0:
            feed_out[layer, kind] = total
            return
        mine[here] = total.astype(b16)
        for shift in range(1, lines):
            y_copy(layer, kind, post, shift).start()

    def land_end(layer, kind):
        total = mine[layer, kind, post, line].astype(f32)
        for shift in range(1, lines):
            y_copy(layer, kind, post, shift).wait()
            total = total + from_y[layer][kind, shift - 1].astype(f32)
        feed_out[layer, kind] = total

    def landing(layer, kind, z, shift):
        if kind == INTO:
            return into_y.at[z, shift - 1]
        return proj_y.at[layer, z, shift - 1]

    def ay_copy(layer, kind, z, shift):
        return remote(
            cells[kind][layer].at[(line + shift) % lines, z], landing(layer, kind, z, shift),
            ay_send.at[layer, kind, z, shift - 1], ay_recv.at[layer, kind, z, shift - 1],
            geo.on_line(shift),
        )

    def az_copy(layer, kind, hop):
        return remote(
            cells[kind][layer].at[line, order(hop)], cells_z[kind].at[layer, hop],
            az_send.at[layer, kind, hop], az_recv.at[layer, kind, hop],
            at_post(far_post if hop == 2 else pair_post),
        )

    def ax_copy(layer, kind):
        span = slice(0, 3 * unit) if kind == INTO else slice(3 * unit, 4 * unit)
        return remote(
            a_send.at[layer, span], a_x.at[layer, span], ax_send.at[layer, kind],
            ax_recv.at[layer, kind], geo.on_column(1),
        )

    def send_ay(layer, kind):
        if layer < top and kind == INTO:
            pl.semaphore_wait(into_credit, lines - 1)
        for step in range(posts):
            for shift in range(1, lines):
                ay_copy(layer, kind, order(step), shift).start()

    def land_ay(layer, kind, step):
        z = order(step)
        cell = cells[kind][layer]
        total = cell[line, z].astype(f32)
        for shift in range(1, lines):
            ay_copy(layer, kind, z, shift).wait()
            total = total + landing(layer, kind, z, shift)[...].astype(f32)
        cell[line, z] = total.astype(b16)
        if step < 2:
            az_copy(layer, kind, step).start()

        if layer > 0 and kind == INTO and all_landed("into", kind):
            for shift in range(1, lines):
                pl.semaphore_signal(
                    into_credit, inc=1, device_id=geo.on_line(shift),
                    device_id_type=pl.DeviceIdType.MESH,
                )

    def land_anear(layer, kind):
        cell = cells[kind][layer]
        az_copy(layer, kind, 1).wait()
        total = cell[line, far_post].astype(f32) + cells_z[kind][layer, 1].astype(f32)
        cell[line, far_post] = total.astype(b16)
        az_copy(layer, kind, 2).start()

    def land_afar(layer, kind):
        total = cells[kind][layer][line, post].astype(f32)
        for hop in (0, 2):
            az_copy(layer, kind, hop).wait()
            total = total + cells_z[kind][layer, hop].astype(f32)
        low, high = total[:, :depth], total[:, depth:]
        span = slice(0, 3 * unit) if kind == INTO else slice(3 * unit, 4 * unit)
        attend_out[layer, span] = jnp.where(column == 0, low, high)
        a_send[layer, span] = jnp.where(column == 0, high, low).astype(b16)
        ax_copy(layer, kind).start()

    def land_ax(layer, kind):
        ax_copy(layer, kind).wait()
        span = slice(0, 3 * unit) if kind == INTO else slice(3 * unit, 4 * unit)
        attend_out[layer, span] = attend_out[layer, span] + a_x[layer, span].astype(f32)

    def sum_copies(layer, hop):
        near = ([sibling], [geo.on_line(shift) for shift in range(1, lines)],
                [at_post(pair_post)], [at_post(far_post)], [geo.on_column(1)])
        first = (0, 1, lines, lines + 1, lines + 2)[hop]
        return [
            (remote(
                sums.at[layer], sum_in.at[layer, first + at], sum_send.at[layer, first + at],
                sum_recv.at[layer, first + at], device,
            ), first + at)
            for at, device in enumerate(near[hop])
        ]

    def start_sum(layer):
        shared = lax.broadcasted_iota(jnp.int32, sums.shape[1:], 0) >= OUT_BIAS
        sums[layer] = jnp.where(shared, 0.5 * sums[layer], sums[layer])
        for copy, unused in sum_copies(layer, 0):
            copy.start()

    def land_sum(layer, hop):
        total = sums[layer]
        for copy, at in sum_copies(layer, hop):
            copy.wait()
            total = total + sum_in[layer, at]
        sums[layer] = total
        if hop < 4:
            for copy, unused in sum_copies(layer, hop + 1):
                copy.start()

    schedule = {
        (1, "pair0"): (
            (land_x, 1, DOWN, 0),
        ),
        (1, "dx"): (
            (land_ay, 1, PROJ, 1), (land_ay, 1, PROJ, 2), (land_x, 1, DOWN, 1),
        ),
        (1, "into"): (
            (land_ay, 1, PROJ, 0), (land_x, 1, DOWN, 2), (land_near, 1, DOWN),
            (land_x, 1, UP, 0), (land_x, 1, DOWN, 3),
        ),
        (0, "feed"): (
            (land_ay, 1, INTO, 0), (land_x, 1, UP, 1),
        ),
        (0, "down"): (
            (land_sum, 1, 0),
        ),
        (0, "proj"): (
            (land_ay, 1, INTO, 2), (land_ay, 1, INTO, 1),
        ),
        (0, "pair0"): (
            (land_x, 1, UP, 2), (land_ay, 1, INTO, 3), (land_sum, 1, 1), (land_far, 1, DOWN),
            (land_near, 1, UP),
        ),
        (0, "pair1"): (
            (land_x, 0, DOWN, 0), (land_x, 1, UP, 3), (land_ay, 0, PROJ, 2),
            (land_anear, 1, INTO),
        ),
        (0, "up"): (
            (land_x, 0, DOWN, 1), (land_ay, 0, PROJ, 1),
        ),
        (0, "pair2"): (
            (land_x, 0, DOWN, 2), (land_anear, 1, PROJ), (land_ay, 1, PROJ, 3),
            (land_y, 0, DOWN, 1), (land_ay, 0, PROJ, 0),
        ),
        (0, "dx"): (
            (land_far, 1, UP), (land_sum, 0, 0), (land_y, 0, DOWN, 2), (land_anear, 0, PROJ),
        ),
        (0, "own"): (
            (land_sum, 1, 2), (land_sum, 0, 1), (land_near, 0, DOWN), (land_afar, 1, INTO),
        ),
        (0, "end"): (
            (land_ay, 0, INTO, 0), (land_end, 1, UP), (land_afar, 1, PROJ),
            (land_ay, 0, INTO, 1), (land_ay, 0, INTO, 2), (land_x, 0, UP, 1), (land_sum, 1, 3),
            (land_x, 0, UP, 2), (land_sum, 0, 2), (land_x, 0, DOWN, 3), (land_end, 1, DOWN),
            (land_ax, 1, INTO), (land_anear, 0, INTO), (land_y, 0, UP, 1), (land_x, 0, UP, 0),
            (land_sum, 0, 3), (land_x, 0, UP, 3), (land_ay, 0, PROJ, 3), (land_y, 0, DOWN, 0),
            (land_ax, 1, PROJ), (land_ay, 0, INTO, 3), (land_y, 0, UP, 2), (land_sum, 1, 4),
            (land_afar, 0, PROJ), (land_near, 0, UP), (land_afar, 0, INTO), (land_y, 0, UP, 0),
            (land_ax, 0, PROJ), (land_y, 0, DOWN, 3), (land_far, 0, DOWN), (land_sum, 0, 4),
            (land_y, 0, UP, 3), (land_ax, 0, INTO), (land_far, 0, UP),
        ),
    }

    def progress(layer, phase):
        if geo.aligned:
            for function, *given in schedule.get((layer, phase), ()):
                function(*given)


    def part_copy(layer, turn):
        return remote(
            psend.at[tile_at(turn), :], precv.at[tile_at(turn), :], part_send.at[layer, turn],
            part_recv.at[layer, turn], sibling,
        )

    def du_copy(layer, turn):
        return remote(
            keep["slope"].at[tile_at(turn), :], du_there.at[tile_at(turn), :],
            du_send.at[layer, turn], du_recv.at[layer, turn], sibling,
        )

    def out_copies(turn, place):
        own = pltpu.make_async_copy(out_low.at[turn], place, out_sem.at[turn])
        there = remote(
            out_low.at[turn], place, out_send.at[turn], out_recv.at[turn], geo.origin(turn, core)
        )
        return own, there

    def send_home(copies, turn, target):
        own, there = copies(turn, target.at[geo.parity])
        pl.when(geo.blocked(turn))(own.start)
        pl.when(jnp.logical_not(geo.blocked(turn)))(there.start)

    def wait_home(copies, turn, target):
        own, there = copies(turn, target.at[(post + turn) % held])
        pl.when(geo.blocked(turn))(own.wait)
        pl.when(jnp.logical_not(geo.blocked(turn)))(there.wait)

    def norm_grads(layer, which, values, grad, turn):
        unit, inverse = norm_parts(values)
        gain = gains[layer, which : which + 1, :]
        if layer == top and which == 1:
            result = unit * gain + shifts[layer, which : which + 1, :]
            out_low[turn] = jnp.where(core == 0, result[:slots], result[slots:]).astype(b16)
            send_home(out_copies, turn, out_tokens)
        back, gain_grad, shift_grad = norm_back(unit, inverse, gain, grad)
        add_sum(layer, GAIN + which, everywhere, gain_grad)
        add_sum(layer, SHIFT + which, everywhere, shift_grad)
        return back

    def feed_back_tile(layer, turn):
        now = tile_at(turn)
        grad = low_grad[now, :].astype(f32)
        if layer < top:
            grad = grad + keep["z1"][now, :]
        back = norm_grads(layer, 1, keep["z2"][now, :], grad, turn)
        keep["z2"][now, :] = back
        low = back.astype(b16)
        wide = low.astype(f32)
        turned[:, now] = wide.T.astype(b16)
        add_sum(layer, DOWN_BIAS, everywhere, jnp.sum(wide, 0, keepdims=True))
        size = min(256, quarter)
        for at in range(0, 2 * quarter, size):
            block, start = at // quarter, at % quarter
            lanes = slice(at, at + size)
            grads = dot_nt(low, wdown[lanes, :])
            grads = (grads * keep["slope"][now, lanes].astype(f32)).astype(b16)
            keep["slope"][now, lanes] = grads
            add_sum(
                layer, UP_BIAS + 2 * block + core, slice(start, start + size),
                jnp.sum(grads.astype(f32), 0, keepdims=True),
            )
        total = dot_nt(keep["slope"][now, :], wup[...])
        psend[now, :] = total.astype(b16)
        part_copy(layer, turn).start()
        du_copy(layer, turn).start()

    def down_grads(layer, which, start):
        lanes = pl.ds(pl.multiple_of(which * quarter, quarter), quarter)
        size = lines * unit

        def chunk(at):
            steps = (2 * at, 2 * at + 1)
            left = [
                turned[pl.ds(pl.multiple_of(order(step) * size, size), size), :] for step in steps
            ]
            result = dot(jnp.concatenate(left, 0), keep["act"][:, lanes]).astype(b16)
            for index, step in enumerate(steps):
                z = order(step)
                for row in range(lines):
                    top = index * size + row * unit
                    for piece in range(2):
                        block = result[
                            top : top + unit, piece * quarter // 2 : (piece + 1) * quarter // 2
                        ]
                        span = slice(piece * unit, (piece + 1) * unit)
                        if start:
                            other[DOWN, z, row, span, :] = block
                        else:
                            mine[layer, DOWN, z, row, span, :] = block
                if start:
                    x_copy(layer, DOWN, z).start()

        loop(posts // 2, chunk)

    def up_grads(layer):
        left = [
            keep["hrt"][pl.ds(pl.multiple_of(which * depth, depth), depth), :]
            for which in (1 - column, column)
        ]
        left = jnp.concatenate(left, 0)
        size = quarter // lines
        for block in range(2):
            lanes = slice(block * quarter, (block + 1) * quarter)
            for there, array in ((0, keep["slope"]), (1, du_there)):
                z = 2 * block + core + there * (1 - 2 * core)
                result = dot(left, array[:, lanes]).astype(b16)
                for row in range(lines):
                    span = slice(row * size, (row + 1) * size)
                    other[UP, z, row] = result[:depth, span]
                    mine[layer, UP, z, row] = result[depth:, span]
        for step in range(posts):
            x_copy(layer, UP, order(step)).start()

    def feed_grads(layer, kind):
        if layer < top:
            pl.semaphore_wait(credit.at[kind], 1)
        if kind == UP:
            loaded(layer, "hrt")
            for turn in range(held):
                du_copy(layer, turn).wait()
            up_grads(layer)
        else:
            down_grads(layer, 1 - column, True)
            down_grads(layer, column, False)

    def proj_back_tile(layer, turn):
        now = tile_at(turn)
        part_copy(layer, turn).wait()
        grad = keep["z2"][now, :] + (psend[now, :].astype(f32) + precv[now, :].astype(f32))
        back = norm_grads(layer, 0, keep["z1"][now, :], grad, turn)
        keep["z1"][now, :] = back
        low = back.astype(b16)
        wide = low.astype(f32)
        turned[:, now] = wide.T.astype(b16)
        add_sum(layer, OUT_BIAS, everywhere, jnp.sum(wide, 0, keepdims=True))
        do[now, :] = dot_nt(low, wout[...]).astype(b16)

    lane_head = lax.broadcasted_iota(jnp.int32, (tile, LANES), 1) // HEAD_DIM

    def attend_back_pair(layer, pair):
        lanes = pl.ds(pl.multiple_of(pair * LANES, LANES), LANES)
        key_t = keep["kx"][pair, :, :LANES].astype(f32).T.astype(b16)
        query_t = (keep["q"][:, lanes].astype(f32) * LOG2E).T.astype(b16)
        grad_t = do[:, lanes].astype(f32).T.astype(b16)
        for head in range(2):
            here = slice(head * HEAD_DIM, (head + 1) * HEAD_DIM)
            qx[head, here, :] = query_t[here]
            dox[head, here, :] = grad_t[here]
            rest = -keep["lse"][2 * pair + head, 0:1, :]
            row = lax.broadcasted_iota(jnp.int32, (16, rows), 0)
            extra = jnp.where(row == 0, 1.0, 0.0)
            for part in range(1, 4):
                piece = rest.astype(b16).astype(f32)
                rest = rest - piece
                extra = jnp.where(row == part, piece, extra)
            qx[head, LANES : LANES + 16, :] = extra.astype(b16)

        def turn_step(turn):
            now = tile_at(turn)
            query = keep["q"][now, lanes].astype(f32)
            outgrad = do[now, lanes].astype(f32)
            for head in range(2):
                here = slice(head * HEAD_DIM, (head + 1) * HEAD_DIM)
                chosen = (lane_head == head).astype(f32)
                place = pl.ds(pl.multiple_of((2 * turn + head) * tile, tile), tile)
                do_stack[place, :] = (outgrad * chosen).astype(b16)
                q_stack[place, :] = (query * chosen).astype(b16)
                scores = dot(keep["kx"][pair], qx[head, :, now])
                probs = jnp.exp2(scores)
                probs_all[:, place] = probs.astype(b16)
                grads = dot(keep["v"][:, lanes], dox[head, :, now])
                own = pl.ds(pl.multiple_of(pair * LANES + head * HEAD_DIM, HEAD_DIM), HEAD_DIM)
                delta = jnp.sum(
                    dox[head, here, now].astype(f32) * keep["ot"][own, now], 0, keepdims=True
                )
                score_grads = (probs * (grads - delta)).astype(b16)
                grads_all[:, place] = score_grads
                dqt[here, now] = dot(key_t[here], score_grads)

        loop(held, turn_step)
        query_grad = (dqt[...].T * SCALE).astype(b16)
        value_grad = dot(probs_all[...], do_stack[...]).astype(b16)
        dq[:, lanes] = query_grad
        dkv[:, lanes] = dot(grads_all[...], q_stack[...]).astype(b16)
        dkv[:, pl.ds(pl.multiple_of(half + pair * LANES, LANES), LANES)] = value_grad
        spot = pl.ds(pl.multiple_of(core * half + pair * LANES, LANES), LANES)
        add_sum(layer, QUERY_BIAS, spot, jnp.sum(query_grad.astype(f32), 0, keepdims=True))
        add_sum(layer, VALUE_BIAS, spot, jnp.sum(value_grad.astype(f32), 0, keepdims=True))

    def qkv_copies(layer):
        return [
            remote(source, target, qkv_send.at[layer, at], qkv_recv.at[layer, at], sibling)
            for at, (source, target) in enumerate(((dq, dq_there), (dkv, dkv_there)))
        ]

    def dx_send(shift, turn):
        start = pl.multiple_of((shift * held + turn) * slots, slots)
        return psend.at[pl.ds(start, slots), :]

    def dx_copy(layer, shift, turn):
        return remote(
            dx_send(shift, turn), dx_recv.at[shift * held + turn],
            dx_ssem.at[layer, shift * held + turn], dx_rsem.at[layer, shift * held + turn], sibling,
        )

    def dx_tile(layer, shift, turn):
        now = pl.ds(pl.multiple_of(shift * rows + turn * tile, tile), tile)
        total = dot_nt(dkv[now, :], wkv[...])
        if shift == 0:
            total = total + dot_nt(dq[now, :], wq[...])
        first, second = total[:slots], total[slots:]
        mine_dx[shift * held + turn] = jnp.where(core == 0, first, second).astype(b16)
        dx_send(shift, turn)[...] = jnp.where(core == 0, second, first).astype(b16)
        dx_copy(layer, shift, turn).start()

    def line_copy(layer, shift, turn):
        return remote(
            dx_recv.at[shift * held + turn], line_in.at[layer, shift - 1, turn],
            line_send.at[layer, shift - 1, turn], line_recv.at[layer, shift - 1, turn],
            geo.on_line(lines - shift),
        )

    def more_copy(layer, turn, who):
        place = low_grad.at[block_at(turn, who)]
        return remote(place, place, more_send.at[layer, turn], more_recv.at[layer, turn], sibling)

    def token_copies(turn, place):
        own = pltpu.make_async_copy(low_grad.at[block_at(turn, core)], place, tok_sem.at[turn])
        there = remote(
            low_grad.at[block_at(turn, core)], place, tok_send.at[turn], tok_recv.at[turn],
            geo.origin(turn, core),
        )
        return own, there

    def mine_lanes(x):
        cuts = [x[:, at * depth : (at + 1) * depth] for at in range(2 * CORES)]
        return jnp.where(
            core == 0, jnp.concatenate([cuts[0], cuts[2]], 1), jnp.concatenate([cuts[1], cuts[3]], 1)
        )

    def into_grads(layer):
        units = half // unit
        x = mine_lanes(keep["xall"][...])
        for first, pair in ((0, (dq, dq_there)), (1, (dkv, dkv_there))):
            for there, ref in enumerate(pair):
                owner = core + there * (1 - 2 * core)
                count = ref.shape[0]
                result = dot_tn(ref[...], x[:count]).astype(b16)
                for at in range(result.shape[0] // unit):
                    kind = first + at // units
                    index = (2 * kind + owner) * units + at % units
                    seq = index // 3
                    where = pl.ds(pl.multiple_of(index % 3 * unit, unit), unit)
                    into_cell[seq % lines, seq // lines, where, :] = result[at * unit : (at + 1) * unit]
        send_ay(layer, INTO)

    def proj_grads(layer):
        here, there = keep["o"][...], o_there[...]
        features = jnp.where(
            core == 0,
            jnp.concatenate([here[:, :depth], there[:, :depth]], 1),
            jnp.concatenate([there[:, depth:], here[:, depth:]], 1),
        )
        result = dot(turned[...], features).astype(b16)
        for seq in range(geo.seq_size):
            proj_cell[layer, seq % lines, seq // lines] = result[seq * unit : (seq + 1) * unit]
        send_ay(layer, PROJ)

    def plain_out(layer, names):
        sources = {"du": keep["slope"], "dft": turned, "dat": turned, "dq": dq, "dk": dkv.at[:, :half], "dv": dkv.at[:, half:]}
        order = ("du", "dft", "dat", "dq", "dk", "dv")
        copies = [
            pltpu.make_async_copy(sources[name], plain[layer][order.index(name)], plain_sem.at[order.index(name)])
            for name in names
        ]
        for copy in copies:
            copy.start()
        for copy in copies:
            copy.wait()

    for layer in range(layers - 1, -1, -1):
        last = layer == 0
        below = layer - 1
        if layer == top:
            loaded(layer, "cot")
        else:
            for turn in range(held):
                more_copy(layer + 1, turn, core).wait_send()
                more_copy(layer + 1, turn, 1 - core).wait_recv()
        o_copy(layer).start()
        loaded(layer, "z2", "wdown", "slope", "wup")
        loop(held, functools.partial(feed_back_tile, layer))
        progress(layer, "feed")
        if not last:
            load(below, "wdown", "wup")
        else:
            load(layer, "z1")
        loaded(layer, "act")
        if geo.aligned:
            feed_grads(layer, DOWN)
            progress(layer, "down")
            if UP_AFTER[layer] is None:
                feed_grads(layer, UP)
                progress(layer, "up")
        else:
            plain_out(layer, ("dft",))
        if not last:
            load(below, "act")
        loaded(layer, "z1", "wout")
        loop(held, functools.partial(proj_back_tile, layer))
        progress(layer, "proj")
        if not last:
            load(below, "wout", "z2")
        if geo.aligned:
            loaded(layer, "o")
            o_copy(layer).wait()
            proj_grads(layer)
        loaded(layer, "q", "kx", "v", "ot", "lse")

        def pair_step(pair):
            attend_back_pair(layer, pair)
            for index in range(pairs if geo.aligned else 0):

                @pl.when(pair == index)
                def after_pair(index=index):
                    progress(layer, PAIRS[index])
                    if index == UP_AFTER[layer]:
                        feed_grads(layer, UP)
                        progress(layer, "up")

        loop(pairs, pair_step)
        if not last:
            load(below, "q", "kx", "v", "ot", "lse")
        for copy in qkv_copies(layer):
            copy.start()
        if geo.aligned:
            start_sum(layer)
        loaded(layer, "win")
        if layer == top:
            for turn in range(held):
                wait_home(out_copies, turn, out_tokens)
        for shift in range(1, lines):
            loop(held, functools.partial(dx_tile, layer, shift))
        progress(layer, "dx")
        for shift in range(1, lines):
            for turn in range(held):
                dx_copy(layer, shift, turn).wait()
                at = shift * held + turn
                dx_recv[at] = (mine_dx[at].astype(f32) + dx_recv[at].astype(f32)).astype(b16)
                line_copy(layer, shift, turn).start()
        loop(held, functools.partial(dx_tile, layer, 0))
        progress(layer, "own")
        if not last:
            load(below, "win")
        if geo.aligned:
            for copy in qkv_copies(layer):
                copy.wait()
            loaded(layer, "xall")
            into_grads(layer)
            progress(layer, "into")
        else:
            for turn in range(held):
                du_copy(layer, turn).wait()
            for copy in qkv_copies(layer):
                copy.wait()
            loaded(layer, "hrt", "xall", "o")
            o_copy(layer).wait()
            plain_out(layer, ("du", "dat", "dq", "dk", "dv"))
        if not last:
            load(below, "hrt", "slope", "xall", "o")
        for turn in range(held):
            dx_copy(layer, 0, turn).wait()
            total = mine_dx[turn].astype(f32) + dx_recv[turn].astype(f32)
            for shift in range(1, lines):
                line_copy(layer, shift, turn).wait()
                total = total + line_in[layer, shift - 1, turn].astype(f32)
            if not last:
                low_grad[block_at(turn, core), :] = total.astype(b16)
                more_copy(layer, turn, core).start()
            else:
                total = total + keep["z1"][block_at(turn, core), :]
                low_grad[block_at(turn, core), :] = total.astype(b16)
                send_home(token_copies, turn, grad_tokens)

    progress(0, "end")
    for turn in range(held):
        wait_home(token_copies, turn, grad_tokens)


def backward(geo, layers, cot_rows, weights, kept, gains, shifts):
    width, rows, half, ffn, count = geo.width, geo.rows, geo.half, geo.ffn, geo.count
    held, lines, posts, slots, quarter = geo.held, geo.lines, geo.posts, geo.slots, geo.quarter
    shapes = kept_shapes(geo)
    any_spec = pl.BlockSpec(memory_space=pl.ANY)
    vmem_spec = pl.BlockSpec(memory_space=pltpu.VMEM)
    unit = width // geo.seq_size
    out = [((held, slots, width), b16)] * 2 + [((layers, SUMS, width), f32)]
    out_specs = [any_spec] * 2 + [vmem_spec]
    if geo.aligned:
        out += [
            ((layers, 2, geo.depth, quarter // lines), f32),
            ((layers, 4 * unit, geo.depth), f32),
        ]
        out_specs += [vmem_spec] * 2
    else:
        for unused in range(layers):
            out += [
                ((rows, ffn // CORES), b16), ((width, rows), b16), ((width, rows), b16),
                ((rows, half), b16), ((count, half), b16), ((count, half), b16),
            ]
            out_specs += [any_spec] * 6
    vmem = pltpu.VMEM
    if geo.aligned:
        shapes["hrt"] = (2 * geo.depth, rows), b16
    scratch = [vmem(*shapes[name]) for name in KEPT]
    scratch += [
        vmem((width, half), b16), vmem((width, 2 * half), b16), vmem((half, width), b16),
        vmem((width, 2 * quarter), b16), vmem((2 * quarter, width), b16),
        vmem((rows, half), b16),
        vmem((rows, width), b16),
        vmem((width, rows), b16),
        vmem((rows, ffn // CORES), b16),
        vmem((max(rows, lines * held * slots), width), b16), vmem((rows, width), b16),
        vmem((rows, half), b16),
        vmem((2, 2 * LANES, rows), b16), vmem((2, LANES, rows), b16),
        vmem((rows, half), b16), vmem((count, 2 * half), b16),
        vmem((rows, half), b16), vmem((count, 2 * half), b16),
        vmem((count, 2 * rows), b16), vmem((count, 2 * rows), b16),
        vmem((2 * rows, LANES), b16), vmem((2 * rows, LANES), b16), vmem((LANES, rows), f32),
        vmem((lines * held, slots, width), b16), vmem((lines * held, slots, width), b16),
        vmem((layers, lines - 1, held, slots, width), b16),
    ]
    dma = pltpu.SemaphoreType.DMA
    scratch += [dma(shape) for shape in (
        (layers, len(KEPT) + 16), (layers,), (layers,), (layers, held), (layers, held),
        (layers, held), (layers, held), (layers, 3), (layers, 3),
        (layers, lines * held), (layers, lines * held),
        (layers, lines - 1, held), (layers, lines - 1, held),
        (layers, held), (layers, held), (held,), (held,), (held,), (6,),
        (held,), (held,), (held,),
    )]
    if geo.aligned:
        block = (geo.depth, quarter // lines)
        into, proj = (3 * unit, 2 * geo.depth), (unit, 2 * geo.depth)
        hops = lines + 3
        scratch += [
            vmem((2, posts, lines, *block), b16), vmem((layers, 2, posts, lines, *block), b16),
            vmem((2, posts, lines, *block), b16),
            vmem((2, posts, lines - 1, *block), b16), vmem((2, lines - 1, *block), b16),
            vmem((2, 3, *block), b16), vmem((2, 3, lines, *block), b16),
            vmem((lines, posts, *into), b16), vmem((layers, lines, posts, *proj), b16),
            vmem((posts, lines - 1, *into), b16), vmem((layers, posts, lines - 1, *proj), b16),
            vmem((layers, 3, *into), b16), vmem((layers, 3, *proj), b16),
            vmem((layers, 4 * unit, geo.depth), b16), vmem((layers, 4 * unit, geo.depth), b16),
            vmem((layers, hops, SUMS, width), f32),
        ]
        scratch += [dma(shape) for shape in (
            (layers, 2, posts), (layers, 2, posts),
            (layers, 2, posts, lines - 1), (layers, 2, posts, lines - 1),
            (layers, 2, 3), (layers, 2, 3),
            (layers, 2, posts, lines - 1), (layers, 2, posts, lines - 1),
            (layers, 2, 3), (layers, 2, 3), (layers, 2), (layers, 2),
            (layers, hops), (layers, hops),
        )]
        scratch += [pltpu.SemaphoreType.REGULAR((2,)), pltpu.SemaphoreType.REGULAR]
    stored = [kept[layer][name] for layer in range(layers) for name in KEPT]
    return pl.pallas_call(
        functools.partial(backward_kernel, geo, layers),
        out_shape=[jax.ShapeDtypeStruct(*shape) for shape in out],
        in_specs=[any_spec] * (5 + len(stored)) + [vmem_spec] * 2,
        out_specs=out_specs,
        scratch_shapes=scratch,
        compiler_params=pltpu.CompilerParams(
            collective_id=1, has_side_effects=True, vmem_limit_bytes=VMEM_BACK
        ),
        cost_estimate=pl.CostEstimate(flops=8 * 10**10, bytes_accessed=6 * 10**7, transcendentals=0),
    )(cot_rows, *weights, *stored, gains, shifts)


def finish_kernel(
    geo, core_ref, sums_ref, feed_ref, attend_ref, out_in_ref, grad_in_ref,
    out_ref, grad_ref, into_ref, in_bias_ref, proj_ref, out_bias_ref, up_ref, up_bias_ref, down_ref, down_bias_ref,
    gain_ref, shift_ref,
):
    seq = core_ref[0]
    out_ref[...] = out_in_ref[...]
    grad_ref[...] = grad_in_ref[...]
    layers = feed_ref.shape[0]
    unit = geo.width // geo.seq_size
    wide, span = 2 * unit, geo.ffn // geo.seq_size
    per_row, per_quarter = geo.width // wide, geo.quarter // span

    def turn(rows, amount):
        return pltpu.roll(rows, (geo.width - amount) % geo.width, 1)

    for layer in range(layers):
        up_ref[layer] = feed_ref[layer, UP]
        down = feed_ref[layer, DOWN]
        down_ref[layer] = jnp.concatenate([down[:unit], down[unit:]], 1)
        both = attend_ref[layer].T
        into_ref[layer] = both[:, : 3 * unit]
        proj_ref[layer] = both[:, 3 * unit :]
        sums = sums_ref[layer]
        narrow = turn(sums, seq * unit)
        out_bias_ref[layer : layer + 1, :] = narrow[OUT_BIAS : OUT_BIAS + 1, :unit]
        down_bias_ref[layer : layer + 1, :] = narrow[DOWN_BIAS : DOWN_BIAS + 1, :unit]
        gain_ref[layer] = narrow[GAIN : GAIN + 2, :unit]
        shift_ref[layer] = narrow[SHIFT : SHIFT + 2, :unit]
        middle = turn(sums, seq % per_row * wide)
        first = middle[QUERY_BIAS : QUERY_BIAS + 1, :wide]
        second = middle[VALUE_BIAS : VALUE_BIAS + 1, :wide]
        in_bias_ref[layer : layer + 1, :] = jnp.where(seq < per_row, first, second)
        large = turn(sums, seq % per_quarter * span)
        chosen = large[UP_BIAS : UP_BIAS + 1, :span]
        for block in range(1, 4):
            chosen = jnp.where(
                seq // per_quarter == block, large[UP_BIAS + block : UP_BIAS + block + 1, :span], chosen
            )
        up_bias_ref[layer : layer + 1, :] = chosen


def finish(geo, layers, seq, sums, feed_out, attend_out, out_tokens, grad_tokens):
    unit, width = geo.width // geo.seq_size, geo.width
    span = geo.ffn // geo.seq_size
    depth = geo.depth
    shapes = [
        (layers, depth, 3 * unit), (layers, 2 * unit), (layers, depth, unit), (layers, unit),
        (layers, depth, span), (layers, span), (layers, unit, geo.ffn // geo.clip_size),
        (layers, unit), (layers, 2, unit), (layers, 2, unit),
    ]
    results = list(call(
        functools.partial(finish_kernel, geo), seq, 1,
        [all_of(array) for array in (sums, feed_out, attend_out, out_tokens, grad_tokens)],
        [full(out_tokens.shape, b16)] * 2 + [full(shape, f32) for shape in shapes], [],
        10**7, 10**7,
    ))
    results[8] = jnp.swapaxes(results[8], 1, 2)
    return results


def build(mesh):
    clip_size, seq_size = mesh.shape["clip"], mesh.shape["seq"]

    def shards(
        tokens, lengths, attn_in, in_bias, attn_out, out_bias, ffn_in, ffn_in_bias,
        ffn_out, ffn_out_bias, norm_gain, norm_bias, cotangent,
    ):
        layers = attn_in.shape[0]
        geo = Geometry(mesh, tokens, ffn_in.shape[2])
        geo.locate()
        held, width, ffn, half, quarter = geo.held, geo.width, geo.ffn, geo.half, geo.quarter
        aligned, core = geo.aligned, geo.core
        seq_at = geo.seq

        weights = (attn_in, attn_out, ffn_in, ffn_out)
        cot_rows, kept = forward(
            geo, layers, tokens, cotangent, lengths, weights,
            (in_bias, out_bias, ffn_in_bias, ffn_out_bias, norm_gain, norm_bias),
        )
        out_tokens, grad_tokens, sums, *results = backward(
            geo, layers, cot_rows, weights, kept, norm_gain, norm_bias
        )
        if aligned:
            seq_arg = jnp.reshape(seq_at, (1,)).astype(jnp.int32)
            return tuple(finish(geo, layers, seq_arg, sums, *results, out_tokens, grad_tokens))

        def swap(array):
            pairs = [(at, at ^ 1) for at in range(clip_size)]
            return lax.ppermute(array, "clip", pairs)

        def spread(array):
            array = lax.psum_scatter(
                array.astype(b16), "seq", scatter_dimension=1, tiled=True
            ).astype(b16)
            return lax.psum_scatter(array, "clip", scatter_dimension=0, tiled=True).astype(f32)

        matrices = []
        for layer in range(layers):
            du, df_t, da_t, dq, dk, dv = results[6 * layer : 6 * layer + 6]
            keep = kept[layer]
            x_all = keep["xall"]
            into = [
                jnp.concatenate([jnp.where(core == 0, a, b), jnp.where(core == 0, b, a)], 1)
                for a, b in (
                    (dot_tn(x_all[: array.shape[0]], array), dot_tn(x_all[: array.shape[0]], swap(array)))
                    for array in (dq, dk, dv)
                )
            ]
            proj = jnp.zeros((CORES, half, width), f32)
            proj = lax.dynamic_update_slice_in_dim(proj, dot(da_t, keep["o"]).T[None], core, 0)
            up = jnp.zeros((2, CORES, width, quarter), f32)
            own_up = dot(keep["hrt"], du).reshape(width, 2, 1, quarter).transpose(1, 2, 0, 3)
            up = lax.dynamic_update_slice_in_dim(up, own_up, core, 1)
            down = jnp.zeros((2, CORES, quarter, width), f32)
            own_down = dot(df_t, keep["act"]).T.reshape(2, 1, quarter, width)
            down = lax.dynamic_update_slice_in_dim(down, own_down, core, 1)
            matrices.append((
                spread(jnp.concatenate(into, 1) * 0.5),
                spread(proj.reshape(width, width)),
                spread(up.transpose(2, 0, 1, 3).reshape(width, ffn)),
                spread(down.reshape(ffn, width)),
            ))
        halves = jnp.arange(SUMS)[None, :, None] >= OUT_BIAS
        summed = lax.psum(jnp.where(halves, 0.5 * sums, sums), ("clip", "seq"))

        def share(row, count):
            piece = summed[:, row : row + count].reshape(layers, count * width)
            size = count * width // seq_size
            return lax.dynamic_slice_in_dim(piece, seq_at * size, size, 1)

        into, proj, up, down = (
            jnp.stack([matrices[layer][which] for layer in range(layers)]) for which in range(4)
        )
        return (
            out_tokens, grad_tokens, into, share(QUERY_BIAS, 2), proj, share(OUT_BIAS, 1),
            up, share(UP_BIAS, 4), down, share(DOWN_BIAS, 1),
            jnp.stack([share(GAIN, 1), share(GAIN + 1, 1)], 1),
            jnp.stack([share(SHIFT, 1), share(SHIFT + 1, 1)], 1),
        )

    return shards


def solution(mesh):
    rowed = P("clip", "seq", None)
    in_specs = (rowed, P("clip")) + (P(),) * 10 + (rowed,)
    out_specs = (
        rowed,
        rowed,
        P(None, "clip", "seq"),
        P(None, "seq"),
        P(None, "clip", "seq"),
        P(None, "seq"),
        P(None, "clip", "seq"),
        P(None, "seq"),
        P(None, "clip", "seq"),
        P(None, "seq"),
        P(None, None, "seq"),
        P(None, None, "seq"),
    )
    return jax.shard_map(
        build(mesh), mesh=mesh, in_specs=in_specs, out_specs=out_specs, check_vma=False
    )
```

```python
from copy import copy as duplicate
import functools

import jax
import jax.numpy as jnp
from jax import lax
from jax.experimental import pallas as pl
from jax.experimental.pallas import tpu as pltpu
from jax.sharding import PartitionSpec as P

HEADS = 12
HEAD_DIM = 64
CORES = 2
LANES = 128
SCALE = HEAD_DIM**-0.5
SQRT_HALF = 0.5**0.5
GAUSS = 0.3989422804014327
LOG2E = 1.4426950408889634
EPS = 1e-05
VMEM = 56 * 1024 * 1024
VMEM_BACK = 63 * 1024 * 1024

f32 = jnp.float32
b16 = jnp.bfloat16


def dot(a, b):
    return lax.dot_general(a, b, (((1,), (0,)), ((), ())), preferred_element_type=f32)


def dot_nt(a, b):
    return lax.dot_general(a, b, (((1,), (1,)), ((), ())), preferred_element_type=f32)


def dot_tn(a, b):
    return lax.dot_general(a, b, (((0,), (0,)), ((), ())), preferred_element_type=f32)


def norm_parts(values):
    center = values - jnp.mean(values, -1, keepdims=True)
    inverse = lax.rsqrt(jnp.mean(center * center, -1, keepdims=True) + EPS)
    return center * inverse, inverse


def norm_back(unit, inverse, gain, grad):
    scaled = grad * gain
    mean_one = jnp.mean(scaled, -1, keepdims=True)
    mean_two = jnp.mean(scaled * unit, -1, keepdims=True)
    back = inverse * (scaled - mean_one - unit * mean_two)
    return back, jnp.sum(grad * unit, 0, keepdims=True), jnp.sum(grad, 0, keepdims=True)


def call(kernel, core, grid, ins, outs, scratch, flops, moved):
    in_specs = [pl.BlockSpec(block, lambda g, c, at=at: at(g, c[0])) for unused, block, at in ins]
    out_specs = [pl.BlockSpec(block, lambda g, c, at=at: at(g, c[0])) for s, d, block, at in outs]
    return pl.pallas_call(
        kernel,
        grid_spec=pltpu.PrefetchScalarGridSpec(
            num_scalar_prefetch=1,
            grid=(grid,),
            in_specs=in_specs,
            out_specs=out_specs,
            scratch_shapes=scratch,
        ),
        out_shape=[jax.ShapeDtypeStruct(shape, dtype) for shape, dtype, b, at in outs],
        compiler_params=pltpu.CompilerParams(
            dimension_semantics=("arbitrary",), vmem_limit_bytes=VMEM
        ),
        cost_estimate=pl.CostEstimate(flops=flops, bytes_accessed=moved, transcendentals=0),
    )(core, *[array for array, b, at in ins])


def all_of(array):
    zeros = (0,) * array.ndim
    return (array, array.shape, lambda g, c: zeros)


def full(shape, dtype):
    zeros = (0,) * len(shape)
    return (shape, dtype, shape, lambda g, c: zeros)


class Geometry:
    def __init__(self, mesh, tokens, ffn):
        self.clip_size, self.seq_size = mesh.shape["clip"], mesh.shape["seq"]
        self.columns = self.clip_size // CORES
        self.held, self.slots, self.width = tokens.shape
        self.ffn = ffn
        self.posts = self.held * CORES
        self.lines = self.seq_size // self.posts
        self.tile = CORES * self.slots
        self.rows = self.held * self.tile
        self.count = self.rows * self.lines
        self.half = self.width // CORES
        self.pairs = self.half // LANES
        self.heads = 2 * self.pairs
        self.quarter = ffn // 4
        self.depth = self.width // self.clip_size
        self.aligned = self.columns == 2 and (ffn // self.seq_size) % LANES == 0

    def locate(self):
        self.clip = lax.axis_index("clip")
        self.seq = lax.axis_index("seq")
        self.core = self.clip % CORES
        self.column = self.clip // CORES
        self.post = self.seq // self.lines
        self.line = self.seq % self.lines
        self.parity = self.post % self.held

    def sibling(self):
        return self.clip + 1 - 2 * self.core, self.seq

    def on_line(self, shift):
        return self.clip, self.post * self.lines + (self.line + shift) % self.lines

    def on_post(self, shift):
        return self.clip, (self.post + shift) % self.posts * self.lines + self.line

    def on_column(self, shift):
        return (self.column + shift) % self.columns * CORES + self.core, self.seq

    def goal(self, turn):
        post = self.held * self.core + (self.post + turn) % self.held
        return self.column * CORES + self.post // self.held, post * self.lines + self.line

    def origin(self, turn, who):
        post = self.held * who + (self.parity + turn) % self.held
        return self.column * CORES + self.post // self.held, post * self.lines + self.line

    def blocked(self, turn):
        return jnp.logical_and(self.post // self.held == self.core, turn == 0)


def remote(source, target, send, receive, device):
    return pltpu.make_async_remote_copy(
        src_ref=source, dst_ref=target, send_sem=send, recv_sem=receive,
        device_id=device, device_id_type=pl.DeviceIdType.MESH,
    )


def meet(geo, devices):
    barrier = pltpu.get_barrier_semaphore()
    total = 0
    for device in devices:
        other = jnp.logical_or(device[0] != geo.clip, device[1] != geo.seq)

        @pl.when(other)
        def greet(device=device):
            pl.semaphore_signal(
                barrier, inc=1, device_id=device, device_id_type=pl.DeviceIdType.MESH
            )

        total = total + other.astype(jnp.int32)
    pl.semaphore_wait(barrier, total)


def loop(count, body):
    def step(at, carry):
        body(at)
        return carry

    lax.fori_loop(0, count, step, 0)


def gelu_parts(inner):
    bell = jnp.exp2((inner * inner) * (-0.5 * LOG2E))
    phi = 0.5 + 0.5 * lax.erf(inner * SQRT_HALF)
    return phi, phi + inner * (GAUSS * bell)


KEPT = ("xall", "kx", "v", "q", "ot", "lse", "o", "z1", "hrt", "act", "slope", "z2")


def kept_shapes(geo):
    rows, width, half, count = geo.rows, geo.width, geo.half, geo.count
    return {
        "xall": ((count, width), b16),
        "kx": ((geo.pairs, count, 2 * LANES), b16),
        "v": ((count, half), b16),
        "q": ((rows, half), b16),
        "ot": ((half, rows), f32),
        "lse": ((geo.heads, 8, rows), f32),
        "o": ((rows, half), b16),
        "z1": ((rows, width), f32),
        "hrt": ((width, rows), b16),
        "act": ((rows, geo.ffn // CORES), b16),
        "slope": ((rows, geo.ffn // CORES), b16),
        "z2": ((rows, width), f32),
    }


def forward_kernel(geo, layers, *refs):
    refs = list(refs)

    def take(count):
        taken = refs[:count]
        del refs[:count]
        return taken

    tokens, cotangent, w_in, w_out, w_up, w_down = take(6)
    lengths, in_bias, out_bias, up_bias, down_bias, gains, shifts = take(7)
    (cot_rows,) = take(1)
    stored = [dict(zip(KEPT, take(len(KEPT)))) for unused in range(layers)]
    kept = [dict(zip(KEPT, take(len(KEPT)))) for unused in range(layers)]
    wq, wkv, wout, wup, wdown = take(5)
    qx, vt, state, hidden, lens, lens_there, psend, precv, running = take(9)
    (load_sem, save_sem, tok_sem, tok_send, tok_recv, cot_sem, cot_send, cot_recv, sib_send,
     sib_recv, line_send, line_recv, pass_send, pass_recv, part_send, part_recv,
     len_sem) = take(17)

    geo = duplicate(geo)
    geo.locate()
    core, tile, slots = geo.core, geo.tile, geo.slots
    held, lines, rows, width, half = geo.held, geo.lines, geo.rows, geo.width, geo.half
    quarter, pairs = geo.quarter, geo.pairs
    sibling = geo.sibling()

    loads = []
    for layer in range(layers):
        targets = (wq.at[layer], wkv.at[layer, :, :half], wkv.at[layer, :, half:])
        parts = [
            (w_in.at[layer, :, pl.ds(pl.multiple_of((kind * CORES + core) * half, half), half)],
             targets[kind])
            for kind in range(3)
        ]
        parts.append((w_out.at[layer, pl.ds(pl.multiple_of(core * half, half), half), :], wout.at[layer]))
        for block in range(2):
            at = pl.ds(pl.multiple_of((2 * block + core) * quarter, quarter), quarter)
            span = slice(block * quarter, (block + 1) * quarter)
            parts.append((w_up.at[layer, :, at], wup.at[layer, :, span]))
            parts.append((w_down.at[layer, at, :], wdown.at[layer, span, :]))
        loads.append([
            pltpu.make_async_copy(source, target, load_sem.at[layer, at])
            for at, (source, target) in enumerate(parts)
        ])
    for copy in loads[0]:
        copy.start()

    sources = [geo.origin(turn, who) for turn in range(held) for who in range(CORES)]
    goals = [geo.goal(turn) for turn in range(held)]
    goals = goals + [(device[0] + 1 - 2 * (device[0] % CORES), device[1]) for device in goals]
    near = [sibling] + [geo.on_line(shift) for shift in range(1, lines)]
    meet(geo, near + sources + goals)

    first = kept[0]["xall"]

    def block_at(turn, who, shift=0):
        start = shift * rows + turn * tile + who * slots
        return pl.ds(start if isinstance(start, int) else pl.multiple_of(start, slots), slots)

    def token_copies(turn, who):
        mine = tokens.at[(geo.post + turn) % held]
        place = first.at[block_at(turn, who)]
        own = pltpu.make_async_copy(mine, place, tok_sem.at[turn])
        return own, remote(mine, place, tok_send.at[turn], tok_recv.at[turn], geo.goal(turn))

    def token_start(turn):
        own, there = token_copies(turn, geo.post // held)
        pl.when(geo.blocked(turn))(own.start)
        pl.when(jnp.logical_not(geo.blocked(turn)))(there.start)

    def token_wait(turn):
        own, there = token_copies(turn, core)
        pl.when(geo.blocked(turn))(own.wait)
        pl.when(jnp.logical_not(geo.blocked(turn)))(there.wait)

    def to_sibling(array, turn, who, shift, send, receive):
        place = array.at[block_at(turn, who, shift)]
        return remote(place, place, send, receive, sibling)

    def to_line(layer, turn, shift):
        array = kept[layer]["xall"]
        source = array.at[block_at(turn, core)]
        target = array.at[block_at(turn, core, shift)]
        return remote(
            source, target, line_send.at[layer, turn, shift - 1], line_recv.at[layer, turn, shift - 1],
            geo.on_line(shift),
        )

    for turn in range(held):
        token_start(turn)
    clip_row = lax.broadcasted_iota(jnp.int32, lens.shape, 0)
    filled = jnp.full(lens.shape, lengths[0], jnp.int32)
    for clip in range(1, held):
        filled = jnp.where(clip_row == clip, lengths[clip], filled)
    lens[...] = filled
    len_copy = remote(lens, lens_there, len_sem.at[0], len_sem.at[1], sibling)
    len_copy.start()

    def clear(at):
        qx[at] = jnp.zeros(qx.shape[1:], b16)
        qx[at, LANES : LANES + 16, :] = (
            lax.broadcasted_iota(jnp.int32, (16, rows), 0) == 0
        ).astype(f32).astype(b16)

    loop(geo.heads, clear)
    len_copy.wait()
    known = jnp.where(geo.post // held == core, lens[...], lens_there[...])
    length = known[0:1, :]
    for clip in range(1, held):
        length = jnp.where(geo.parity == clip, known[clip : clip + 1, :], length)
    lane = lax.broadcasted_iota(jnp.int32, (slots, LANES), 1)
    slot = lax.broadcasted_iota(jnp.int32, (slots, LANES), 0)
    for shift in range(lines):
        for turn in range(held):
            for who in range(CORES):
                post = held * who + (geo.parity + turn) % held
                line = (geo.line + lines - shift) % lines
                outside = (post * lines + line) * slots + slot >= length
                mask = jnp.where(jnp.logical_and(lane == 0, outside), -1e30, 0.0)
                mask = jnp.where(jnp.logical_and(lane > 0, lane < 4), 1.0, mask).astype(b16)
                for layer in range(layers):
                    for pair in range(pairs):
                        kept[layer]["kx"][pair, block_at(turn, who, shift), LANES:] = mask

    for turn in range(held):
        token_wait(turn)
        to_sibling(first, turn, core, 0, sib_send.at[turn], sib_recv.at[turn]).start()
        for shift in range(1, lines):
            to_line(0, turn, shift).start()
    for copy in loads[0]:
        copy.wait()
    for copy in loads[1]:
        copy.start()

    def cot_copies(turn, flip):
        mine = cotangent.at[(geo.post + turn) % held]
        place = cot_rows.at[block_at(turn, geo.post // held)]
        goal = geo.goal(turn)
        if flip:
            goal = (goal[0] + 1 - 2 * (goal[0] % CORES), goal[1])
        own = pltpu.make_async_copy(mine, place, cot_sem.at[turn, flip])
        there = remote(
            mine, place, cot_send.at[turn, flip], cot_recv.at[turn, geo.post // held], goal
        )
        here = jnp.logical_and(goal[0] == geo.clip, goal[1] == geo.seq)
        return own, there, here

    def cot_start():
        for turn in range(held):
            for flip in range(CORES):
                own, there, here = cot_copies(turn, flip)
                pl.when(here)(own.start)
                pl.when(jnp.logical_not(here))(there.start)

    def cot_wait():
        for turn in range(held):
            for flip in range(CORES):
                own, there, here = cot_copies(turn, flip)
                pl.when(here)(own.wait)
                pl.when(jnp.logical_not(here))(there.wait_send)
            for who in range(CORES):
                source = geo.origin(turn, who)
                place = cot_rows.at[block_at(turn, who)]
                there = remote(
                    cotangent.at[0], place, cot_send.at[turn, 0], cot_recv.at[turn, who], source
                )
                here = jnp.logical_and(source[0] == geo.clip, source[1] == geo.seq)
                pl.when(jnp.logical_not(here))(there.wait_recv)

    def key_tile(layer, at):
        keep = kept[layer]
        now = pl.ds(pl.multiple_of(at, tile), tile)
        both = dot(keep["xall"][now, :], wkv[layer])
        key = both[:, :half].astype(b16)
        for pair in range(pairs):
            keep["kx"][pair, now, :LANES] = key[:, pair * LANES : (pair + 1) * LANES]
        bias = in_bias[layer : layer + 1, pl.ds(pl.multiple_of(width + core * half, half), half)]
        value = (both[:, half:] + bias).astype(b16)
        keep["v"][now, :] = value
        vt[:, now] = value.astype(f32).T.astype(b16)

    def query_tile(layer, at):
        keep = kept[layer]
        now = pl.ds(pl.multiple_of(at, tile), tile)
        bias = in_bias[layer : layer + 1, pl.ds(pl.multiple_of(core * half, half), half)]
        query = (dot(keep["xall"][now, :], wq[layer]) + bias).astype(b16)
        query = (query * SCALE).astype(b16)
        keep["q"][now, :] = query
        turned = (query.astype(f32) * LOG2E).T.astype(b16)
        for head in range(geo.heads):
            inside = head % 2 * HEAD_DIM
            qx[head, inside : inside + HEAD_DIM, now] = (
                turned[head * HEAD_DIM : (head + 1) * HEAD_DIM]
            )

    def attend_block(layer, shift):
        keep = kept[layer]
        span = slice(shift * rows, (shift + 1) * rows)

        size = min(256, rows)
        cuts = [slice(start, start + size) for start in range(shift * rows, (shift + 1) * rows, size)]

        def pair_step(pair):
            heads = [2 * pair, 2 * pair + 1]
            scores = [
                [dot(keep["kx"][pair, cut, :], qx[head]) for cut in cuts] for head in heads
            ]
            for head, pieces in zip(heads, scores):
                here = pl.ds(pl.multiple_of(head * HEAD_DIM, HEAD_DIM), HEAD_DIM)
                top = functools.reduce(
                    jnp.maximum, [jnp.max(piece, 0, keepdims=True) for piece in pieces]
                )
                if shift > 0:
                    before = keep["lse"][head, 0:1, :]
                    top = jnp.maximum(top, before)
                    shrink = jnp.exp2(before - top)
                total = attended = None
                for piece, cut in zip(pieces, cuts):
                    weights = jnp.exp2(piece - top)
                    sums = jnp.sum(weights, 0, keepdims=True)
                    values = dot(vt[here, cut], weights.astype(b16))
                    total = sums if total is None else total + sums
                    attended = values if attended is None else attended + values
                if shift > 0:
                    total = total + shrink * running[head, 0:1, :]
                    attended = attended + shrink * keep["ot"][here, :]
                if shift < lines - 1:
                    running[head, 0:1, :] = total
                    keep["ot"][here, :] = attended
                    keep["lse"][head, 0:1, :] = top
                else:
                    keep["ot"][here, :] = attended / total
                    keep["lse"][head, 0:1, :] = top + jnp.log(total) * LOG2E

        loop(pairs, pair_step)

    def project_tile(layer, turn):
        keep = kept[layer]
        now = pl.ds(pl.multiple_of(turn * tile, tile), tile)
        attended = keep["ot"][:, now].T.astype(b16)
        keep["o"][now, :] = attended
        share(2 * layer, turn, dot(attended, wout[layer]))

    def part_copy(which, turn):
        now = pl.ds(pl.multiple_of(turn * tile, tile), tile)
        return remote(
            psend.at[which, now, :], precv.at[which, now, :], part_send.at[which, turn],
            part_recv.at[which, turn], sibling,
        )

    def share(which, turn, part):
        now = pl.ds(pl.multiple_of(turn * tile, tile), tile)
        psend[which, now, :] = part.astype(b16)
        part_copy(which, turn).start()

    def collect(which, turn):
        now = pl.ds(pl.multiple_of(turn * tile, tile), tile)
        part_copy(which, turn).wait()
        return psend[which, now, :].astype(f32) + precv[which, now, :].astype(f32)

    def feed_tile(layer, turn):
        keep = kept[layer]
        now = pl.ds(pl.multiple_of(turn * tile, tile), tile)
        x = first[now, :].astype(f32) if layer == 0 else state[now, :]
        summed = x + collect(2 * layer, turn) + out_bias[layer : layer + 1, :]
        keep["z1"][now, :] = summed
        unit, unused = norm_parts(summed)
        normal = unit * gains[layer, 0:1, :] + shifts[layer, 0:1, :]
        hidden[now, :] = normal
        low = normal.astype(b16)
        keep["hrt"][:, now] = low.astype(f32).T.astype(b16)
        size = min(256, quarter)
        for at in range(0, 2 * quarter, size):
            block, start = at // quarter, at % quarter
            bias = up_bias[
                layer : layer + 1,
                pl.ds(pl.multiple_of((2 * block + core) * quarter + start, size), size),
            ]
            inner = dot(low, wup[layer, :, at : at + size]) + bias
            phi, slope = gelu_parts(inner)
            keep["act"][now, at : at + size] = (inner * phi).astype(b16)
            keep["slope"][now, at : at + size] = slope.astype(b16)
        total = dot(keep["act"][now, :], wdown[layer])
        share(2 * layer + 1, turn, total)

    def norm_tile(layer, turn):
        keep = kept[layer]
        now = pl.ds(pl.multiple_of(turn * tile, tile), tile)
        summed = hidden[now, :] + collect(2 * layer + 1, turn) + down_bias[layer : layer + 1, :]
        keep["z2"][now, :] = summed
        if layer < layers - 1:
            unit, unused = norm_parts(summed)
            result = unit * gains[layer, 1:2, :] + shifts[layer, 1:2, :]
            state[now, :] = result
            kept[layer + 1]["xall"][now, :] = result.astype(b16)

    saves = []

    def save(layer, names):
        for name in names:
            copy = pltpu.make_async_copy(
                kept[layer][name], stored[layer][name], save_sem.at[layer, KEPT.index(name)]
            )
            copy.start()
            saves.append(copy)

    for layer in range(layers):
        x_all = kept[layer]["xall"]
        if layer == 0:
            for turn in range(held):
                to_sibling(x_all, turn, core, 0, sib_send.at[turn], sib_recv.at[turn]).wait_send()
                to_sibling(x_all, turn, 1 - core, 0, sib_send.at[turn], sib_recv.at[turn]).wait_recv()
                key_tile(layer, turn * tile)
                query_tile(layer, turn * tile)
        for shift in range(lines):
            if shift > 0:
                for turn in range(held):
                    to_line(layer, turn, shift).wait()
                    to_sibling(
                        x_all, turn, core, shift,
                        pass_send.at[layer, turn, shift - 1], pass_recv.at[layer, turn, shift - 1],
                    ).start()
                for turn in range(held):
                    send = pass_send.at[layer, turn, shift - 1]
                    receive = pass_recv.at[layer, turn, shift - 1]
                    to_sibling(x_all, turn, core, shift, send, receive).wait_send()
                    to_sibling(x_all, turn, 1 - core, shift, send, receive).wait_recv()
                    key_tile(layer, shift * rows + turn * tile)
            if shift == lines - 1:
                save(layer, ("xall", "kx", "v", "q"))
                if layer == 0:
                    cot_start()

            attend_block(layer, shift)
        loop(held, functools.partial(project_tile, layer))
        save(layer, ("ot", "lse", "o"))
        loop(held, functools.partial(feed_tile, layer))
        save(layer, ("z1", "hrt", "act", "slope"))
        for turn in range(held):
            norm_tile(layer, turn)
            if layer < layers - 1:
                for shift in range(1, lines):
                    to_line(layer + 1, turn, shift).start()
                if turn == 0:
                    for copy in loads[layer + 1]:
                        copy.wait()
                key_tile(layer + 1, turn * tile)
                query_tile(layer + 1, turn * tile)
        save(layer, ("z2",))

    cot_wait()
    for copy in saves:
        copy.wait()


def forward(geo, layers, tokens, cotangent, lengths, weights, vectors):
    width, rows, half, ffn = geo.width, geo.rows, geo.half, geo.ffn
    shapes = kept_shapes(geo)
    any_spec = pl.BlockSpec(memory_space=pl.ANY)
    vmem_spec = pl.BlockSpec(memory_space=pltpu.VMEM)
    out_shape = [
        jax.ShapeDtypeStruct((rows, width), b16),
    ]
    out_shape += [jax.ShapeDtypeStruct(*shapes[name]) for unused in range(layers) for name in KEPT]
    scratch = [pltpu.VMEM(*shapes[name]) for unused in range(layers) for name in KEPT]
    scratch += [
        pltpu.VMEM((layers, width, half), b16),
        pltpu.VMEM((layers, width, 2 * half), b16),
        pltpu.VMEM((layers, half, width), b16),
        pltpu.VMEM((layers, width, 2 * geo.quarter), b16),
        pltpu.VMEM((layers, 2 * geo.quarter, width), b16),
        pltpu.VMEM((geo.heads, 2 * LANES, rows), b16),
        pltpu.VMEM((half, geo.count), b16),
        pltpu.VMEM((rows, width), f32),
        pltpu.VMEM((rows, width), f32),
        pltpu.VMEM((8, LANES), jnp.int32),
        pltpu.VMEM((8, LANES), jnp.int32),
        pltpu.VMEM((2 * layers, rows, width), b16),
        pltpu.VMEM((2 * layers, rows, width), b16),
        pltpu.VMEM((geo.heads, 8, rows), f32),
    ]
    held, lines = geo.held, max(geo.lines - 1, 1)
    dma = pltpu.SemaphoreType.DMA
    scratch += [dma(shape) for shape in (
        (layers, 8), (layers, len(KEPT)), (held,), (held,), (held,),
        (held, CORES), (held, CORES), (held, CORES), (held,), (held,),
        (layers, held, lines), (layers, held, lines), (layers, held, lines), (layers, held, lines),
        (2 * layers, held), (2 * layers, held), (2,),
    )]
    results = pl.pallas_call(
        functools.partial(forward_kernel, geo, layers),
        out_shape=out_shape,
        in_specs=[any_spec] * 6 + [pl.BlockSpec(memory_space=pltpu.SMEM)] + [vmem_spec] * 6,
        out_specs=[any_spec] * len(out_shape),
        scratch_shapes=scratch,
        compiler_params=pltpu.CompilerParams(
            collective_id=0, has_side_effects=True, vmem_limit_bytes=VMEM
        ),
        cost_estimate=pl.CostEstimate(flops=3 * 10**10, bytes_accessed=4 * 10**7, transcendentals=0),
    )(tokens, cotangent, *weights, lengths, *vectors)
    count = len(KEPT)
    kept = [
        dict(zip(KEPT, results[1 + layer * count : 1 + (layer + 1) * count]))
        for layer in range(layers)
    ]
    return results[0], kept


QUERY_BIAS, VALUE_BIAS, UP_BIAS, OUT_BIAS, DOWN_BIAS, GAIN, SHIFT = 0, 1, 2, 6, 7, 8, 10
SUMS = 16
UP, DOWN = 0, 1
INTO, PROJ = 0, 1
PAIRS = ("pair0", "pair1", "pair2")
UP_AFTER = (1, 1)


def backward_kernel(geo, layers, *refs):
    refs = list(refs)

    def take(count):
        taken = refs[:count]
        del refs[:count]
        return taken

    cot_rows, w_in, w_out, w_up, w_down = take(5)
    stored = [dict(zip(KEPT, take(len(KEPT)))) for unused in range(layers)]
    gains, shifts = take(2)
    out_tokens, grad_tokens, sums = take(3)
    if geo.aligned:
        feed_out, attend_out = take(2)
    else:
        plain = [take(6) for unused in range(layers)]
    keep = dict(zip(KEPT, take(len(KEPT))))
    wq, wkv, wout, wup, wdown = take(5)
    (o_there, low_grad, turned, du_there, psend, precv, do, qx, dox, dq, dkv, dq_there,
     dkv_there, probs_all, grads_all, do_stack, q_stack, dqt, mine_dx, dx_recv, line_in) = take(21)
    out_low = mine_dx
    (load_sem, o_send, o_recv, du_send, du_recv, part_send, part_recv, qkv_send, qkv_recv,
     dx_ssem, dx_rsem, line_send, line_recv, more_send, more_recv, tok_sem, tok_send,
     tok_recv, plain_sem, out_sem, out_send, out_recv) = take(22)
    if geo.aligned:
        (other, mine, from_x, y_first, y_last, z_first, z_last, into_cell, proj_cell, into_y, proj_y, into_z, proj_z,
         a_send, a_x, sum_in) = take(16)
        from_y, from_z = (y_first, y_last), (z_first, z_last)
        cells = [[into_cell] * layers, [proj_cell.at[layer] for layer in range(layers)]]
        cells_z = (into_z, proj_z)
        (fx_send, fx_recv, fy_send, fy_recv, fz_send, fz_recv, ay_send, ay_recv, az_send, az_recv,
         ax_send, ax_recv, sum_send, sum_recv) = take(14)
        credit, into_credit = take(2)

    geo = duplicate(geo)
    geo.locate()
    core, tile, slots = geo.core, geo.tile, geo.slots
    held, lines, rows, width, half = geo.held, geo.lines, geo.rows, geo.width, geo.half
    quarter, pairs, posts, depth = geo.quarter, geo.pairs, geo.posts, geo.depth
    post, line, column = geo.post, geo.line, geo.column
    unit = width // geo.seq_size
    sibling = geo.sibling()

    def tile_at(turn):
        return pl.ds(pl.multiple_of(turn * tile, tile), tile)

    def block_at(turn, who, shift=0):
        start = shift * rows + turn * tile + who * slots
        return pl.ds(start if isinstance(start, int) else pl.multiple_of(start, slots), slots)

    NAMES = KEPT + ("win", "wout", "wup", "wdown", "cot")

    def load_copies(layer, name):
        where = load_sem.at[layer, NAMES.index(name)]
        if name == "win":
            targets = (wq, wkv.at[:, :half], wkv.at[:, half:])
            return [
                pltpu.make_async_copy(
                    w_in.at[layer, :, pl.ds(pl.multiple_of((kind * CORES + core) * half, half), half)],
                    targets[kind], load_sem.at[layer, len(NAMES) + kind],
                )
                for kind in range(3)
            ]
        if name == "wout":
            at = pl.ds(pl.multiple_of(core * half, half), half)
            return [pltpu.make_async_copy(w_out.at[layer, at, :], wout, where)]
        if name in ("wup", "wdown"):
            copies = []
            for block in range(2):
                at = pl.ds(pl.multiple_of((2 * block + core) * quarter, quarter), quarter)
                slot = len(NAMES) + 3 + 2 * (name == "wdown") + block
                if name == "wup":
                    pair = w_up.at[layer, :, at], wup.at[:, block * quarter : (block + 1) * quarter]
                else:
                    pair = w_down.at[layer, at, :], wdown.at[block * quarter : (block + 1) * quarter, :]
                copies.append(pltpu.make_async_copy(*pair, load_sem.at[layer, slot]))
            return copies
        if name == "hrt" and geo.aligned:
            return [
                pltpu.make_async_copy(
                    stored[layer][name].at[pl.ds(pl.multiple_of((2 * which + core) * depth, depth), depth), :],
                    keep[name].at[which * depth : (which + 1) * depth, :],
                    load_sem.at[layer, len(NAMES) + 7 + which],
                )
                for which in range(2)
            ]
        if name == "cot":
            return [pltpu.make_async_copy(cot_rows, low_grad, where)]
        return [pltpu.make_async_copy(stored[layer][name], keep[name], where)]

    def load(layer, *names):
        for name in names:
            for copy in load_copies(layer, name):
                copy.start()

    def loaded(layer, *names):
        for name in names:
            for copy in load_copies(layer, name):
                copy.wait()

    top = layers - 1
    load(top, "z2", "cot", "wdown", "slope", "wup", "act", "z1", "wout", "q", "kx", "v", "ot",
         "lse", "win", "hrt", "xall", "o")

    sources = [geo.origin(turn, who) for turn in range(held) for who in range(CORES)]
    goals = [geo.goal(turn) for turn in range(held)]
    near = [sibling] + [geo.on_line(shift) for shift in range(1, lines)]
    if geo.aligned:
        near += [geo.on_post(shift) for shift in range(1, posts)]
        near += [geo.on_column(shift) for shift in range(1, geo.columns)]
    goals = goals + [(device[0] + 1 - 2 * (device[0] % CORES), device[1]) for device in goals]
    meet(geo, near + sources + goals)

    def o_copy(layer):
        return remote(stored[layer]["o"], o_there, o_send.at[layer], o_recv.at[layer], sibling)

    def clear(at):
        qx[at] = jnp.zeros(qx.shape[1:], b16)
        dox[at] = jnp.zeros(dox.shape[1:], b16)

    loop(2, clear)
    sums[...] = jnp.zeros_like(sums)

    def add_sum(layer, row, lanes, value):
        sums[layer, pl.ds(row, 1), lanes] += value

    everywhere = slice(None)


    def x_copy(layer, kind, z):
        return remote(
            other.at[kind, z], from_x.at[kind, z], fx_send.at[layer, kind, z],
            fx_recv.at[layer, kind, z], geo.on_column(1),
        )

    pair_post = post + 1 - 2 * (post % 2)
    far_post = (post + 2) % posts

    landed = {}

    def all_landed(hop, kind):
        landed[hop, kind] = landed.get((hop, kind), 0) + 1
        return landed[hop, kind] == posts

    def order(step):
        return (pair_post + step // 2 * (far_post - pair_post) + step % 2 * 2) % posts

    def at_post(which):
        return geo.clip, which * lines + line

    def y_copy(layer, kind, z, shift):
        there = from_y[layer].at[kind, shift - 1] if layer else from_y[layer].at[kind, z, shift - 1]
        at = 0 if layer else z
        return remote(
            mine.at[layer, kind, z, (line + shift) % lines], there,
            fy_send.at[layer, kind, at, shift - 1], fy_recv.at[layer, kind, at, shift - 1],
            geo.on_line(shift),
        )

    def z_copy(layer, kind, hop):
        block = mine.at[layer, kind, order(hop)]
        return remote(
            block if layer else block.at[line], from_z[layer].at[kind, hop],
            fz_send.at[layer, kind, hop], fz_recv.at[layer, kind, hop],
            at_post(far_post if hop == 2 else pair_post),
        )

    def land_x(layer, kind, step):
        z = order(step)
        x_copy(layer, kind, z).wait()
        total = mine[layer, kind, z].astype(f32) + from_x[kind, z].astype(f32)
        mine[layer, kind, z] = total.astype(b16)
        if layer == 0:
            for shift in range(1, lines):
                y_copy(layer, kind, z, shift).start()
            return
        if step < 2:
            z_copy(layer, kind, step).start()
        if all_landed("x", kind):
            device = geo.on_column(1)
            pl.semaphore_signal(
                credit.at[kind], inc=1, device_id=device, device_id_type=pl.DeviceIdType.MESH
            )

    def land_y(layer, kind, step):
        z = order(step)
        total = mine[layer, kind, z, line].astype(f32)
        for shift in range(1, lines):
            y_copy(layer, kind, z, shift).wait()
            total = total + from_y[layer][kind, z, shift - 1].astype(f32)
        mine[layer, kind, z, line] = total.astype(b16)
        if step < 2:
            z_copy(layer, kind, step).start()

    def land_near(layer, kind):
        z_copy(layer, kind, 1).wait()
        here = (layer, kind, far_post) if layer else (layer, kind, far_post, line)
        total = mine[here].astype(f32) + from_z[layer][kind, 1].astype(f32)
        mine[here] = total.astype(b16)
        z_copy(layer, kind, 2).start()

    def land_far(layer, kind):
        here = (layer, kind, post) if layer else (layer, kind, post, line)
        total = mine[here].astype(f32)
        for hop in (0, 2):
            z_copy(layer, kind, hop).wait()
            total = total + from_z[layer][kind, hop].astype(f32)
        if layer == 0:
            feed_out[layer, kind] = total
            return
        mine[here] = total.astype(b16)
        for shift in range(1, lines):
            y_copy(layer, kind, post, shift).start()

    def land_end(layer, kind):
        total = mine[layer, kind, post, line].astype(f32)
        for shift in range(1, lines):
            y_copy(layer, kind, post, shift).wait()
            total = total + from_y[layer][kind, shift - 1].astype(f32)
        feed_out[layer, kind] = total

    def landing(layer, kind, z, shift):
        if kind == INTO:
            return into_y.at[z, shift - 1]
        return proj_y.at[layer, z, shift - 1]

    def ay_copy(layer, kind, z, shift):
        return remote(
            cells[kind][layer].at[(line + shift) % lines, z], landing(layer, kind, z, shift),
            ay_send.at[layer, kind, z, shift - 1], ay_recv.at[layer, kind, z, shift - 1],
            geo.on_line(shift),
        )

    def az_copy(layer, kind, hop):
        return remote(
            cells[kind][layer].at[line, order(hop)], cells_z[kind].at[layer, hop],
            az_send.at[layer, kind, hop], az_recv.at[layer, kind, hop],
            at_post(far_post if hop == 2 else pair_post),
        )

    def ax_copy(layer, kind):
        span = slice(0, 3 * unit) if kind == INTO else slice(3 * unit, 4 * unit)
        return remote(
            a_send.at[layer, span], a_x.at[layer, span], ax_send.at[layer, kind],
            ax_recv.at[layer, kind], geo.on_column(1),
        )

    def send_ay(layer, kind):
        if layer < top and kind == INTO:
            pl.semaphore_wait(into_credit, lines - 1)
        for step in range(posts):
            for shift in range(1, lines):
                ay_copy(layer, kind, order(step), shift).start()

    def land_ay(layer, kind, step):
        z = order(step)
        cell = cells[kind][layer]
        total = cell[line, z].astype(f32)
        for shift in range(1, lines):
            ay_copy(layer, kind, z, shift).wait()
            total = total + landing(layer, kind, z, shift)[...].astype(f32)
        cell[line, z] = total.astype(b16)
        if step < 2:
            az_copy(layer, kind, step).start()

        if layer > 0 and kind == INTO and all_landed("into", kind):
            for shift in range(1, lines):
                pl.semaphore_signal(
                    into_credit, inc=1, device_id=geo.on_line(shift),
                    device_id_type=pl.DeviceIdType.MESH,
                )

    def land_anear(layer, kind):
        cell = cells[kind][layer]
        az_copy(layer, kind, 1).wait()
        total = cell[line, far_post].astype(f32) + cells_z[kind][layer, 1].astype(f32)
        cell[line, far_post] = total.astype(b16)
        az_copy(layer, kind, 2).start()

    def land_afar(layer, kind):
        total = cells[kind][layer][line, post].astype(f32)
        for hop in (0, 2):
            az_copy(layer, kind, hop).wait()
            total = total + cells_z[kind][layer, hop].astype(f32)
        low, high = total[:, :depth], total[:, depth:]
        span = slice(0, 3 * unit) if kind == INTO else slice(3 * unit, 4 * unit)
        attend_out[layer, span] = jnp.where(column == 0, low, high)
        a_send[layer, span] = jnp.where(column == 0, high, low).astype(b16)
        ax_copy(layer, kind).start()

    def land_ax(layer, kind):
        ax_copy(layer, kind).wait()
        span = slice(0, 3 * unit) if kind == INTO else slice(3 * unit, 4 * unit)
        attend_out[layer, span] = attend_out[layer, span] + a_x[layer, span].astype(f32)

    def sum_copies(layer, hop):
        near = ([sibling], [geo.on_line(shift) for shift in range(1, lines)],
                [at_post(pair_post)], [at_post(far_post)], [geo.on_column(1)])
        first = (0, 1, lines, lines + 1, lines + 2)[hop]
        return [
            (remote(
                sums.at[layer], sum_in.at[layer, first + at], sum_send.at[layer, first + at],
                sum_recv.at[layer, first + at], device,
            ), first + at)
            for at, device in enumerate(near[hop])
        ]

    def start_sum(layer):
        shared = lax.broadcasted_iota(jnp.int32, sums.shape[1:], 0) >= OUT_BIAS
        sums[layer] = jnp.where(shared, 0.5 * sums[layer], sums[layer])
        for copy, unused in sum_copies(layer, 0):
            copy.start()

    def land_sum(layer, hop):
        total = sums[layer]
        for copy, at in sum_copies(layer, hop):
            copy.wait()
            total = total + sum_in[layer, at]
        sums[layer] = total
        if hop < 4:
            for copy, unused in sum_copies(layer, hop + 1):
                copy.start()

    schedule = {
        (1, "up"): (
            (land_x, 1, DOWN, 1),
        ),
        (1, "dx"): (
            (land_ay, 1, PROJ, 1), (land_x, 1, DOWN, 0), (land_x, 1, DOWN, 2), (land_sum, 1, 0),
            (land_ay, 1, PROJ, 2),
        ),
        (1, "own"): (
            (land_anear, 1, PROJ),
        ),
        (1, "into"): (
            (land_x, 1, DOWN, 3), (land_near, 1, DOWN), (land_sum, 1, 1), (land_ay, 1, PROJ, 0),
            (land_x, 1, UP, 0),
        ),
        (0, "feed"): (
            (land_ay, 1, INTO, 0),
        ),
        (0, "up"): (
            (land_x, 0, DOWN, 1), (land_near, 1, UP),
        ),
        (0, "proj"): (
            (land_ay, 1, INTO, 1), (land_x, 1, UP, 1), (land_ay, 1, INTO, 2),
            (land_far, 1, DOWN),
        ),
        (0, "pair0"): (
            (land_x, 1, UP, 3), (land_anear, 1, INTO), (land_x, 1, UP, 2), (land_x, 0, DOWN, 0),
        ),
        (0, "dx"): (
            (land_sum, 1, 2), (land_ay, 1, INTO, 3), (land_ay, 0, PROJ, 2), (land_x, 0, DOWN, 2),
            (land_ay, 0, PROJ, 1), (land_ay, 0, PROJ, 0), (land_y, 0, DOWN, 0),
            (land_afar, 1, INTO),
        ),
        (0, "own"): (
            (land_y, 0, DOWN, 1), (land_anear, 0, PROJ),
        ),
        (0, "end"): (
            (land_x, 0, UP, 1), (land_y, 0, DOWN, 2), (land_near, 0, DOWN),
            (land_ay, 0, INTO, 1), (land_sum, 0, 0), (land_x, 0, UP, 2), (land_ay, 0, INTO, 2),
            (land_ay, 0, INTO, 0), (land_anear, 0, INTO), (land_x, 0, UP, 0),
            (land_ay, 0, INTO, 3), (land_sum, 0, 1), (land_ay, 0, PROJ, 3), (land_sum, 1, 3),
            (land_y, 0, UP, 1), (land_far, 1, UP), (land_ay, 1, PROJ, 3), (land_y, 0, UP, 2),
            (land_x, 0, DOWN, 3), (land_sum, 0, 2), (land_sum, 1, 4), (land_x, 0, UP, 3),
            (land_afar, 0, INTO), (land_end, 1, DOWN), (land_y, 0, UP, 0), (land_ax, 1, INTO),
            (land_near, 0, UP), (land_afar, 1, PROJ), (land_sum, 0, 3), (land_afar, 0, PROJ),
            (land_ax, 0, INTO), (land_end, 1, UP), (land_y, 0, DOWN, 3), (land_ax, 1, PROJ),
            (land_sum, 0, 4), (land_far, 0, DOWN), (land_ax, 0, PROJ), (land_y, 0, UP, 3),
            (land_far, 0, UP),
        ),
    }

    def progress(layer, phase):
        if geo.aligned:
            for function, *given in schedule.get((layer, phase), ()):
                function(*given)


    def part_copy(layer, turn):
        return remote(
            psend.at[tile_at(turn), :], precv.at[tile_at(turn), :], part_send.at[layer, turn],
            part_recv.at[layer, turn], sibling,
        )

    def du_copy(layer, turn):
        return remote(
            keep["slope"].at[tile_at(turn), :], du_there.at[tile_at(turn), :],
            du_send.at[layer, turn], du_recv.at[layer, turn], sibling,
        )

    def out_copies(turn, place):
        own = pltpu.make_async_copy(out_low.at[turn], place, out_sem.at[turn])
        there = remote(
            out_low.at[turn], place, out_send.at[turn], out_recv.at[turn], geo.origin(turn, core)
        )
        return own, there

    def send_home(copies, turn, target):
        own, there = copies(turn, target.at[geo.parity])
        pl.when(geo.blocked(turn))(own.start)
        pl.when(jnp.logical_not(geo.blocked(turn)))(there.start)

    def wait_home(copies, turn, target):
        own, there = copies(turn, target.at[(post + turn) % held])
        pl.when(geo.blocked(turn))(own.wait)
        pl.when(jnp.logical_not(geo.blocked(turn)))(there.wait)

    def norm_grads(layer, which, values, grad, turn):
        unit, inverse = norm_parts(values)
        gain = gains[layer, which : which + 1, :]
        if layer == top and which == 1:
            result = unit * gain + shifts[layer, which : which + 1, :]
            out_low[turn] = jnp.where(core == 0, result[:slots], result[slots:]).astype(b16)
            send_home(out_copies, turn, out_tokens)
        back, gain_grad, shift_grad = norm_back(unit, inverse, gain, grad)
        add_sum(layer, GAIN + which, everywhere, gain_grad)
        add_sum(layer, SHIFT + which, everywhere, shift_grad)
        return back

    def feed_back_tile(layer, turn):
        now = tile_at(turn)
        grad = low_grad[now, :].astype(f32)
        if layer < top:
            grad = grad + keep["z1"][now, :]
        back = norm_grads(layer, 1, keep["z2"][now, :], grad, turn)
        keep["z2"][now, :] = back
        low = back.astype(b16)
        wide = low.astype(f32)
        turned[:, now] = wide.T.astype(b16)
        add_sum(layer, DOWN_BIAS, everywhere, jnp.sum(wide, 0, keepdims=True))
        size = min(256, quarter)
        for at in range(0, 2 * quarter, size):
            block, start = at // quarter, at % quarter
            lanes = slice(at, at + size)
            grads = dot_nt(low, wdown[lanes, :])
            grads = (grads * keep["slope"][now, lanes].astype(f32)).astype(b16)
            keep["slope"][now, lanes] = grads
            add_sum(
                layer, UP_BIAS + 2 * block + core, slice(start, start + size),
                jnp.sum(grads.astype(f32), 0, keepdims=True),
            )
        total = dot_nt(keep["slope"][now, :], wup[...])
        psend[now, :] = total.astype(b16)
        part_copy(layer, turn).start()
        du_copy(layer, turn).start()

    def down_grads(layer, which, start):
        lanes = pl.ds(pl.multiple_of(which * quarter, quarter), quarter)
        size = lines * unit

        def chunk(at):
            steps = (2 * at, 2 * at + 1)
            left = [
                turned[pl.ds(pl.multiple_of(order(step) * size, size), size), :] for step in steps
            ]
            result = dot(jnp.concatenate(left, 0), keep["act"][:, lanes]).astype(b16)
            for index, step in enumerate(steps):
                z = order(step)
                for row in range(lines):
                    top = index * size + row * unit
                    for piece in range(2):
                        block = result[
                            top : top + unit, piece * quarter // 2 : (piece + 1) * quarter // 2
                        ]
                        span = slice(piece * unit, (piece + 1) * unit)
                        if start:
                            other[DOWN, z, row, span, :] = block
                        else:
                            mine[layer, DOWN, z, row, span, :] = block
                if start:
                    x_copy(layer, DOWN, z).start()

        loop(posts // 2, chunk)

    def up_grads(layer):
        left = [
            keep["hrt"][pl.ds(pl.multiple_of(which * depth, depth), depth), :]
            for which in (1 - column, column)
        ]
        left = jnp.concatenate(left, 0)
        size = quarter // lines
        for block in range(2):
            lanes = slice(block * quarter, (block + 1) * quarter)
            for there, array in ((0, keep["slope"]), (1, du_there)):
                z = 2 * block + core + there * (1 - 2 * core)
                result = dot(left, array[:, lanes]).astype(b16)
                for row in range(lines):
                    span = slice(row * size, (row + 1) * size)
                    other[UP, z, row] = result[:depth, span]
                    mine[layer, UP, z, row] = result[depth:, span]
        for step in range(posts):
            x_copy(layer, UP, order(step)).start()

    def feed_grads(layer, kind):
        if layer < top:
            pl.semaphore_wait(credit.at[kind], 1)
        if kind == UP:
            loaded(layer, "hrt")
            for turn in range(held):
                du_copy(layer, turn).wait()
            up_grads(layer)
        else:
            down_grads(layer, 1 - column, True)
            down_grads(layer, column, False)

    def proj_back_tile(layer, turn):
        now = tile_at(turn)
        part_copy(layer, turn).wait()
        grad = keep["z2"][now, :] + (psend[now, :].astype(f32) + precv[now, :].astype(f32))
        back = norm_grads(layer, 0, keep["z1"][now, :], grad, turn)
        keep["z1"][now, :] = back
        low = back.astype(b16)
        wide = low.astype(f32)
        turned[:, now] = wide.T.astype(b16)
        add_sum(layer, OUT_BIAS, everywhere, jnp.sum(wide, 0, keepdims=True))
        do[now, :] = dot_nt(low, wout[...]).astype(b16)

    lane_head = lax.broadcasted_iota(jnp.int32, (tile, LANES), 1) // HEAD_DIM

    def attend_back_pair(layer, pair):
        lanes = pl.ds(pl.multiple_of(pair * LANES, LANES), LANES)
        key_t = keep["kx"][pair, :, :LANES].astype(f32).T.astype(b16)
        query_t = (keep["q"][:, lanes].astype(f32) * LOG2E).T.astype(b16)
        grad_t = do[:, lanes].astype(f32).T.astype(b16)
        for head in range(2):
            here = slice(head * HEAD_DIM, (head + 1) * HEAD_DIM)
            qx[head, here, :] = query_t[here]
            dox[head, here, :] = grad_t[here]
            rest = -keep["lse"][2 * pair + head, 0:1, :]
            row = lax.broadcasted_iota(jnp.int32, (16, rows), 0)
            extra = jnp.where(row == 0, 1.0, 0.0)
            for part in range(1, 4):
                piece = rest.astype(b16).astype(f32)
                rest = rest - piece
                extra = jnp.where(row == part, piece, extra)
            qx[head, LANES : LANES + 16, :] = extra.astype(b16)

        def turn_step(turn):
            now = tile_at(turn)
            query = keep["q"][now, lanes].astype(f32)
            outgrad = do[now, lanes].astype(f32)
            for head in range(2):
                here = slice(head * HEAD_DIM, (head + 1) * HEAD_DIM)
                chosen = (lane_head == head).astype(f32)
                place = pl.ds(pl.multiple_of((2 * turn + head) * tile, tile), tile)
                do_stack[place, :] = (outgrad * chosen).astype(b16)
                q_stack[place, :] = (query * chosen).astype(b16)
                scores = dot(keep["kx"][pair], qx[head, :, now])
                probs = jnp.exp2(scores)
                probs_all[:, place] = probs.astype(b16)
                grads = dot(keep["v"][:, lanes], dox[head, :, now])
                own = pl.ds(pl.multiple_of(pair * LANES + head * HEAD_DIM, HEAD_DIM), HEAD_DIM)
                delta = jnp.sum(
                    dox[head, here, now].astype(f32) * keep["ot"][own, now], 0, keepdims=True
                )
                score_grads = (probs * (grads - delta)).astype(b16)
                grads_all[:, place] = score_grads
                dqt[here, now] = dot(key_t[here], score_grads)

        loop(held, turn_step)
        query_grad = (dqt[...].T * SCALE).astype(b16)
        value_grad = dot(probs_all[...], do_stack[...]).astype(b16)
        dq[:, lanes] = query_grad
        dkv[:, lanes] = dot(grads_all[...], q_stack[...]).astype(b16)
        dkv[:, pl.ds(pl.multiple_of(half + pair * LANES, LANES), LANES)] = value_grad
        spot = pl.ds(pl.multiple_of(core * half + pair * LANES, LANES), LANES)
        add_sum(layer, QUERY_BIAS, spot, jnp.sum(query_grad.astype(f32), 0, keepdims=True))
        add_sum(layer, VALUE_BIAS, spot, jnp.sum(value_grad.astype(f32), 0, keepdims=True))

    def qkv_copies(layer):
        return [
            remote(source, target, qkv_send.at[layer, at], qkv_recv.at[layer, at], sibling)
            for at, (source, target) in enumerate(((dq, dq_there), (dkv, dkv_there)))
        ]

    def dx_send(shift, turn):
        start = pl.multiple_of((shift * held + turn) * slots, slots)
        return psend.at[pl.ds(start, slots), :]

    def dx_copy(layer, shift, turn):
        return remote(
            dx_send(shift, turn), dx_recv.at[shift * held + turn],
            dx_ssem.at[layer, shift * held + turn], dx_rsem.at[layer, shift * held + turn], sibling,
        )

    def dx_tile(layer, shift, turn):
        now = pl.ds(pl.multiple_of(shift * rows + turn * tile, tile), tile)
        total = dot_nt(dkv[now, :], wkv[...])
        if shift == 0:
            total = total + dot_nt(dq[now, :], wq[...])
        first, second = total[:slots], total[slots:]
        mine_dx[shift * held + turn] = jnp.where(core == 0, first, second).astype(b16)
        dx_send(shift, turn)[...] = jnp.where(core == 0, second, first).astype(b16)
        dx_copy(layer, shift, turn).start()

    def line_copy(layer, shift, turn):
        return remote(
            dx_recv.at[shift * held + turn], line_in.at[layer, shift - 1, turn],
            line_send.at[layer, shift - 1, turn], line_recv.at[layer, shift - 1, turn],
            geo.on_line(lines - shift),
        )

    def more_copy(layer, turn, who):
        place = low_grad.at[block_at(turn, who)]
        return remote(place, place, more_send.at[layer, turn], more_recv.at[layer, turn], sibling)

    def token_copies(turn, place):
        own = pltpu.make_async_copy(low_grad.at[block_at(turn, core)], place, tok_sem.at[turn])
        there = remote(
            low_grad.at[block_at(turn, core)], place, tok_send.at[turn], tok_recv.at[turn],
            geo.origin(turn, core),
        )
        return own, there

    def mine_lanes(x):
        cuts = [x[:, at * depth : (at + 1) * depth] for at in range(2 * CORES)]
        return jnp.where(
            core == 0, jnp.concatenate([cuts[0], cuts[2]], 1), jnp.concatenate([cuts[1], cuts[3]], 1)
        )

    def into_grads(layer, there):
        units = half // unit
        x = mine_lanes(keep["xall"][...])
        owner = core + there * (1 - 2 * core)
        for first, ref in ((0, (dq, dq_there)[there]), (1, (dkv, dkv_there)[there])):
            result = dot_tn(ref[...], x[: ref.shape[0]]).astype(b16)
            for at in range(result.shape[0] // unit):
                kind = first + at // units
                index = (2 * kind + owner) * units + at % units
                seq = index // 3
                where = pl.ds(pl.multiple_of(index % 3 * unit, unit), unit)
                into_cell[seq % lines, seq // lines, where, :] = result[at * unit : (at + 1) * unit]
        if there:
            send_ay(layer, INTO)

    def own_total(layer, turn):
        dx_copy(layer, 0, turn).wait_recv()
        total = mine_dx[turn].astype(f32) + dx_recv[turn].astype(f32)
        for shift in range(1, lines):
            line_copy(layer, shift, turn).wait()
            total = total + line_in[layer, shift - 1, turn].astype(f32)
        return total

    def take_grad(layer, turn):
        low_grad[block_at(turn, core), :] = own_total(layer, turn).astype(b16)
        more_copy(layer, turn, core).start()
        more_copy(layer, turn, core).wait_send()
        more_copy(layer, turn, 1 - core).wait_recv()

    def proj_grads(layer):
        here, there = keep["o"][...], o_there[...]
        features = jnp.where(
            core == 0,
            jnp.concatenate([here[:, :depth], there[:, :depth]], 1),
            jnp.concatenate([there[:, depth:], here[:, depth:]], 1),
        )
        result = dot(turned[...], features).astype(b16)
        for seq in range(geo.seq_size):
            proj_cell[layer, seq % lines, seq // lines] = result[seq * unit : (seq + 1) * unit]
        send_ay(layer, PROJ)

    def plain_out(layer, names):
        sources = {"du": keep["slope"], "dft": turned, "dat": turned, "dq": dq, "dk": dkv.at[:, :half], "dv": dkv.at[:, half:]}
        order = ("du", "dft", "dat", "dq", "dk", "dv")
        copies = [
            pltpu.make_async_copy(sources[name], plain[layer][order.index(name)], plain_sem.at[order.index(name)])
            for name in names
        ]
        for copy in copies:
            copy.start()
        for copy in copies:
            copy.wait()

    for layer in range(layers - 1, -1, -1):
        last = layer == 0
        below = layer - 1
        if layer == top:
            loaded(layer, "cot")
        loaded(layer, "z2", "wdown", "slope", "wup")

        def feed_step(turn):
            if layer < top:
                take_grad(layer + 1, turn)
            feed_back_tile(layer, turn)

        if layer < top:
            for turn in range(held):
                dx_copy(layer + 1, 0, turn).wait_send()
        loop(held, feed_step)
        o_copy(layer).start()
        progress(layer, "feed")
        if not last:
            load(below, "wdown", "wup")
        else:
            load(layer, "z1")
        loaded(layer, "act")
        if geo.aligned:
            feed_grads(layer, DOWN)
            progress(layer, "down")
            if UP_AFTER[layer] is None:
                feed_grads(layer, UP)
                progress(layer, "up")
        else:
            plain_out(layer, ("dft",))
        if not last:
            load(below, "act")
        loaded(layer, "z1", "wout")
        loop(held, functools.partial(proj_back_tile, layer))
        progress(layer, "proj")
        if not last:
            load(below, "wout", "z2")
        if geo.aligned:
            loaded(layer, "o")
            o_copy(layer).wait()
            proj_grads(layer)
        loaded(layer, "q", "kx", "v", "ot", "lse")

        def pair_step(pair):
            attend_back_pair(layer, pair)
            for index in range(pairs if geo.aligned else 0):

                @pl.when(pair == index)
                def after_pair(index=index):
                    progress(layer, PAIRS[index])
                    if index == UP_AFTER[layer]:
                        feed_grads(layer, UP)
                        progress(layer, "up")

        loop(pairs, pair_step)
        if not last:
            load(below, "q", "kx", "v", "ot", "lse")
        for copy in qkv_copies(layer):
            copy.start()
        if geo.aligned:
            start_sum(layer)
        loaded(layer, "win")
        if layer == top:
            for turn in range(held):
                wait_home(out_copies, turn, out_tokens)
        for shift in range(1, lines):
            loop(held, functools.partial(dx_tile, layer, shift))
        progress(layer, "dx")
        if geo.aligned and last:
            loaded(layer, "xall")
            into_grads(layer, 0)
        for shift in range(1, lines):
            for turn in range(held):
                dx_copy(layer, shift, turn).wait()
                at = shift * held + turn
                dx_recv[at] = (mine_dx[at].astype(f32) + dx_recv[at].astype(f32)).astype(b16)
                line_copy(layer, shift, turn).start()

        def own_rows():
            loop(held, functools.partial(dx_tile, layer, 0))
            progress(layer, "own")

        if not last:
            own_rows()
            load(below, "win")
        if geo.aligned:
            if not last:
                loaded(layer, "xall")
                into_grads(layer, 0)
            for copy in qkv_copies(layer):
                copy.wait()
            into_grads(layer, 1)
            progress(layer, "into")
        else:
            for turn in range(held):
                du_copy(layer, turn).wait()
            for copy in qkv_copies(layer):
                copy.wait()
            loaded(layer, "hrt", "xall", "o")
            o_copy(layer).wait()
            plain_out(layer, ("du", "dat", "dq", "dk", "dv"))
        if not last:
            load(below, "hrt", "slope", "xall", "o")
        else:
            own_rows()
            for turn in range(held):
                dx_copy(layer, 0, turn).wait_send()
                total = own_total(layer, turn) + keep["z1"][block_at(turn, core), :]
                low_grad[block_at(turn, core), :] = total.astype(b16)
                send_home(token_copies, turn, grad_tokens)

    progress(0, "end")
    for turn in range(held):
        wait_home(token_copies, turn, grad_tokens)


def backward(geo, layers, cot_rows, weights, kept, gains, shifts):
    width, rows, half, ffn, count = geo.width, geo.rows, geo.half, geo.ffn, geo.count
    held, lines, posts, slots, quarter = geo.held, geo.lines, geo.posts, geo.slots, geo.quarter
    shapes = kept_shapes(geo)
    any_spec = pl.BlockSpec(memory_space=pl.ANY)
    vmem_spec = pl.BlockSpec(memory_space=pltpu.VMEM)
    unit = width // geo.seq_size
    out = [((held, slots, width), b16)] * 2 + [((layers, SUMS, width), f32)]
    out_specs = [any_spec] * 2 + [vmem_spec]
    if geo.aligned:
        out += [
            ((layers, 2, geo.depth, quarter // lines), f32),
            ((layers, 4 * unit, geo.depth), f32),
        ]
        out_specs += [vmem_spec] * 2
    else:
        for unused in range(layers):
            out += [
                ((rows, ffn // CORES), b16), ((width, rows), b16), ((width, rows), b16),
                ((rows, half), b16), ((count, half), b16), ((count, half), b16),
            ]
            out_specs += [any_spec] * 6
    vmem = pltpu.VMEM
    if geo.aligned:
        shapes["hrt"] = (2 * geo.depth, rows), b16
    scratch = [vmem(*shapes[name]) for name in KEPT]
    scratch += [
        vmem((width, half), b16), vmem((width, 2 * half), b16), vmem((half, width), b16),
        vmem((width, 2 * quarter), b16), vmem((2 * quarter, width), b16),
        vmem((rows, half), b16),
        vmem((rows, width), b16),
        vmem((width, rows), b16),
        vmem((rows, ffn // CORES), b16),
        vmem((max(rows, lines * held * slots), width), b16), vmem((rows, width), b16),
        vmem((rows, half), b16),
        vmem((2, 2 * LANES, rows), b16), vmem((2, LANES, rows), b16),
        vmem((rows, half), b16), vmem((count, 2 * half), b16),
        vmem((rows, half), b16), vmem((count, 2 * half), b16),
        vmem((count, 2 * rows), b16), vmem((count, 2 * rows), b16),
        vmem((2 * rows, LANES), b16), vmem((2 * rows, LANES), b16), vmem((LANES, rows), f32),
        vmem((lines * held, slots, width), b16), vmem((lines * held, slots, width), b16),
        vmem((layers, lines - 1, held, slots, width), b16),
    ]
    dma = pltpu.SemaphoreType.DMA
    scratch += [dma(shape) for shape in (
        (layers, len(KEPT) + 16), (layers,), (layers,), (layers, held), (layers, held),
        (layers, held), (layers, held), (layers, 3), (layers, 3),
        (layers, lines * held), (layers, lines * held),
        (layers, lines - 1, held), (layers, lines - 1, held),
        (layers, held), (layers, held), (held,), (held,), (held,), (6,),
        (held,), (held,), (held,),
    )]
    if geo.aligned:
        block = (geo.depth, quarter // lines)
        into, proj = (3 * unit, 2 * geo.depth), (unit, 2 * geo.depth)
        hops = lines + 3
        scratch += [
            vmem((2, posts, lines, *block), b16), vmem((layers, 2, posts, lines, *block), b16),
            vmem((2, posts, lines, *block), b16),
            vmem((2, posts, lines - 1, *block), b16), vmem((2, lines - 1, *block), b16),
            vmem((2, 3, *block), b16), vmem((2, 3, lines, *block), b16),
            vmem((lines, posts, *into), b16), vmem((layers, lines, posts, *proj), b16),
            vmem((posts, lines - 1, *into), b16), vmem((layers, posts, lines - 1, *proj), b16),
            vmem((layers, 3, *into), b16), vmem((layers, 3, *proj), b16),
            vmem((layers, 4 * unit, geo.depth), b16), vmem((layers, 4 * unit, geo.depth), b16),
            vmem((layers, hops, SUMS, width), f32),
        ]
        scratch += [dma(shape) for shape in (
            (layers, 2, posts), (layers, 2, posts),
            (layers, 2, posts, lines - 1), (layers, 2, posts, lines - 1),
            (layers, 2, 3), (layers, 2, 3),
            (layers, 2, posts, lines - 1), (layers, 2, posts, lines - 1),
            (layers, 2, 3), (layers, 2, 3), (layers, 2), (layers, 2),
            (layers, hops), (layers, hops),
        )]
        scratch += [pltpu.SemaphoreType.REGULAR((2,)), pltpu.SemaphoreType.REGULAR]
    stored = [kept[layer][name] for layer in range(layers) for name in KEPT]
    return pl.pallas_call(
        functools.partial(backward_kernel, geo, layers),
        out_shape=[jax.ShapeDtypeStruct(*shape) for shape in out],
        in_specs=[any_spec] * (5 + len(stored)) + [vmem_spec] * 2,
        out_specs=out_specs,
        scratch_shapes=scratch,
        compiler_params=pltpu.CompilerParams(
            collective_id=1, has_side_effects=True, vmem_limit_bytes=VMEM_BACK
        ),
        cost_estimate=pl.CostEstimate(flops=8 * 10**10, bytes_accessed=6 * 10**7, transcendentals=0),
    )(cot_rows, *weights, *stored, gains, shifts)


def finish_kernel(
    geo, core_ref, sums_ref, feed_ref, attend_ref, out_in_ref, grad_in_ref,
    out_ref, grad_ref, into_ref, in_bias_ref, proj_ref, out_bias_ref, up_ref, up_bias_ref, down_ref, down_bias_ref,
    gain_ref, shift_ref,
):
    seq = core_ref[0]
    out_ref[...] = out_in_ref[...]
    grad_ref[...] = grad_in_ref[...]
    layers = feed_ref.shape[0]
    unit = geo.width // geo.seq_size
    wide, span = 2 * unit, geo.ffn // geo.seq_size
    per_row, per_quarter = geo.width // wide, geo.quarter // span

    def turn(rows, amount):
        return pltpu.roll(rows, (geo.width - amount) % geo.width, 1)

    for layer in range(layers):
        up_ref[layer] = feed_ref[layer, UP]
        down = feed_ref[layer, DOWN]
        down_ref[layer] = jnp.concatenate([down[:unit], down[unit:]], 1)
        both = attend_ref[layer].T
        into_ref[layer] = both[:, : 3 * unit]
        proj_ref[layer] = both[:, 3 * unit :]
        sums = sums_ref[layer]
        narrow = turn(sums, seq * unit)
        out_bias_ref[layer : layer + 1, :] = narrow[OUT_BIAS : OUT_BIAS + 1, :unit]
        down_bias_ref[layer : layer + 1, :] = narrow[DOWN_BIAS : DOWN_BIAS + 1, :unit]
        gain_ref[layer] = narrow[GAIN : GAIN + 2, :unit]
        shift_ref[layer] = narrow[SHIFT : SHIFT + 2, :unit]
        middle = turn(sums, seq % per_row * wide)
        first = middle[QUERY_BIAS : QUERY_BIAS + 1, :wide]
        second = middle[VALUE_BIAS : VALUE_BIAS + 1, :wide]
        in_bias_ref[layer : layer + 1, :] = jnp.where(seq < per_row, first, second)
        large = turn(sums, seq % per_quarter * span)
        chosen = large[UP_BIAS : UP_BIAS + 1, :span]
        for block in range(1, 4):
            chosen = jnp.where(
                seq // per_quarter == block, large[UP_BIAS + block : UP_BIAS + block + 1, :span], chosen
            )
        up_bias_ref[layer : layer + 1, :] = chosen


def finish(geo, layers, seq, sums, feed_out, attend_out, out_tokens, grad_tokens):
    unit, width = geo.width // geo.seq_size, geo.width
    span = geo.ffn // geo.seq_size
    depth = geo.depth
    shapes = [
        (layers, depth, 3 * unit), (layers, 2 * unit), (layers, depth, unit), (layers, unit),
        (layers, depth, span), (layers, span), (layers, unit, geo.ffn // geo.clip_size),
        (layers, unit), (layers, 2, unit), (layers, 2, unit),
    ]
    results = list(call(
        functools.partial(finish_kernel, geo), seq, 1,
        [all_of(array) for array in (sums, feed_out, attend_out, out_tokens, grad_tokens)],
        [full(out_tokens.shape, b16)] * 2 + [full(shape, f32) for shape in shapes], [],
        10**7, 10**7,
    ))
    results[8] = jnp.swapaxes(results[8], 1, 2)
    return results


def build(mesh):
    clip_size, seq_size = mesh.shape["clip"], mesh.shape["seq"]

    def shards(
        tokens, lengths, attn_in, in_bias, attn_out, out_bias, ffn_in, ffn_in_bias,
        ffn_out, ffn_out_bias, norm_gain, norm_bias, cotangent,
    ):
        layers = attn_in.shape[0]
        geo = Geometry(mesh, tokens, ffn_in.shape[2])
        geo.locate()
        held, width, ffn, half, quarter = geo.held, geo.width, geo.ffn, geo.half, geo.quarter
        aligned, core = geo.aligned, geo.core
        seq_at = geo.seq

        weights = (attn_in, attn_out, ffn_in, ffn_out)
        cot_rows, kept = forward(
            geo, layers, tokens, cotangent, lengths, weights,
            (in_bias, out_bias, ffn_in_bias, ffn_out_bias, norm_gain, norm_bias),
        )
        out_tokens, grad_tokens, sums, *results = backward(
            geo, layers, cot_rows, weights, kept, norm_gain, norm_bias
        )
        if aligned:
            seq_arg = jnp.reshape(seq_at, (1,)).astype(jnp.int32)
            return tuple(finish(geo, layers, seq_arg, sums, *results, out_tokens, grad_tokens))

        def swap(array):
            pairs = [(at, at ^ 1) for at in range(clip_size)]
            return lax.ppermute(array, "clip", pairs)

        def spread(array):
            array = lax.psum_scatter(
                array.astype(b16), "seq", scatter_dimension=1, tiled=True
            ).astype(b16)
            return lax.psum_scatter(array, "clip", scatter_dimension=0, tiled=True).astype(f32)

        matrices = []
        for layer in range(layers):
            du, df_t, da_t, dq, dk, dv = results[6 * layer : 6 * layer + 6]
            keep = kept[layer]
            x_all = keep["xall"]
            into = [
                jnp.concatenate([jnp.where(core == 0, a, b), jnp.where(core == 0, b, a)], 1)
                for a, b in (
                    (dot_tn(x_all[: array.shape[0]], array), dot_tn(x_all[: array.shape[0]], swap(array)))
                    for array in (dq, dk, dv)
                )
            ]
            proj = jnp.zeros((CORES, half, width), f32)
            proj = lax.dynamic_update_slice_in_dim(proj, dot(da_t, keep["o"]).T[None], core, 0)
            up = jnp.zeros((2, CORES, width, quarter), f32)
            own_up = dot(keep["hrt"], du).reshape(width, 2, 1, quarter).transpose(1, 2, 0, 3)
            up = lax.dynamic_update_slice_in_dim(up, own_up, core, 1)
            down = jnp.zeros((2, CORES, quarter, width), f32)
            own_down = dot(df_t, keep["act"]).T.reshape(2, 1, quarter, width)
            down = lax.dynamic_update_slice_in_dim(down, own_down, core, 1)
            matrices.append((
                spread(jnp.concatenate(into, 1) * 0.5),
                spread(proj.reshape(width, width)),
                spread(up.transpose(2, 0, 1, 3).reshape(width, ffn)),
                spread(down.reshape(ffn, width)),
            ))
        halves = jnp.arange(SUMS)[None, :, None] >= OUT_BIAS
        summed = lax.psum(jnp.where(halves, 0.5 * sums, sums), ("clip", "seq"))

        def share(row, count):
            piece = summed[:, row : row + count].reshape(layers, count * width)
            size = count * width // seq_size
            return lax.dynamic_slice_in_dim(piece, seq_at * size, size, 1)

        into, proj, up, down = (
            jnp.stack([matrices[layer][which] for layer in range(layers)]) for which in range(4)
        )
        return (
            out_tokens, grad_tokens, into, share(QUERY_BIAS, 2), proj, share(OUT_BIAS, 1),
            up, share(UP_BIAS, 4), down, share(DOWN_BIAS, 1),
            jnp.stack([share(GAIN, 1), share(GAIN + 1, 1)], 1),
            jnp.stack([share(SHIFT, 1), share(SHIFT + 1, 1)], 1),
        )

    return shards


def solution(mesh):
    rowed = P("clip", "seq", None)
    in_specs = (rowed, P("clip")) + (P(),) * 10 + (rowed,)
    out_specs = (
        rowed,
        rowed,
        P(None, "clip", "seq"),
        P(None, "seq"),
        P(None, "clip", "seq"),
        P(None, "seq"),
        P(None, "clip", "seq"),
        P(None, "seq"),
        P(None, "clip", "seq"),
        P(None, "seq"),
        P(None, None, "seq"),
        P(None, None, "seq"),
    )
    return jax.shard_map(
        build(mesh), mesh=mesh, in_specs=in_specs, out_specs=out_specs, check_vma=False
    )
```

```python
from copy import copy as duplicate
import functools

import jax
import jax.numpy as jnp
from jax import lax
from jax.experimental import pallas as pl
from jax.experimental.pallas import tpu as pltpu
from jax.sharding import PartitionSpec as P

HEADS = 12
HEAD_DIM = 64
CORES = 2
LANES = 128
SCALE = HEAD_DIM**-0.5
SQRT_HALF = 0.5**0.5
GAUSS = 0.3989422804014327
LOG2E = 1.4426950408889634
EPS = 1e-05
VMEM = 56 * 1024 * 1024
VMEM_BACK = 63 * 1024 * 1024

f32 = jnp.float32
b16 = jnp.bfloat16


def dot(a, b):
    return lax.dot_general(a, b, (((1,), (0,)), ((), ())), preferred_element_type=f32)


def dot_nt(a, b):
    return lax.dot_general(a, b, (((1,), (1,)), ((), ())), preferred_element_type=f32)


def dot_tn(a, b):
    return lax.dot_general(a, b, (((0,), (0,)), ((), ())), preferred_element_type=f32)


def norm_parts(values):
    center = values - jnp.mean(values, -1, keepdims=True)
    inverse = lax.rsqrt(jnp.mean(center * center, -1, keepdims=True) + EPS)
    return center * inverse, inverse


def norm_back(unit, inverse, gain, grad):
    scaled = grad * gain
    mean_one = jnp.mean(scaled, -1, keepdims=True)
    mean_two = jnp.mean(scaled * unit, -1, keepdims=True)
    back = inverse * (scaled - mean_one - unit * mean_two)
    return back, jnp.sum(grad * unit, 0, keepdims=True), jnp.sum(grad, 0, keepdims=True)


def call(kernel, core, grid, ins, outs, scratch, flops, moved):
    in_specs = [pl.BlockSpec(block, lambda g, c, at=at: at(g, c[0])) for unused, block, at in ins]
    out_specs = [pl.BlockSpec(block, lambda g, c, at=at: at(g, c[0])) for s, d, block, at in outs]
    return pl.pallas_call(
        kernel,
        grid_spec=pltpu.PrefetchScalarGridSpec(
            num_scalar_prefetch=1,
            grid=(grid,),
            in_specs=in_specs,
            out_specs=out_specs,
            scratch_shapes=scratch,
        ),
        out_shape=[jax.ShapeDtypeStruct(shape, dtype) for shape, dtype, b, at in outs],
        compiler_params=pltpu.CompilerParams(
            dimension_semantics=("arbitrary",), vmem_limit_bytes=VMEM
        ),
        cost_estimate=pl.CostEstimate(flops=flops, bytes_accessed=moved, transcendentals=0),
    )(core, *[array for array, b, at in ins])


def all_of(array):
    zeros = (0,) * array.ndim
    return (array, array.shape, lambda g, c: zeros)


def full(shape, dtype):
    zeros = (0,) * len(shape)
    return (shape, dtype, shape, lambda g, c: zeros)


class Geometry:
    def __init__(self, mesh, tokens, ffn):
        self.clip_size, self.seq_size = mesh.shape["clip"], mesh.shape["seq"]
        self.columns = self.clip_size // CORES
        self.held, self.slots, self.width = tokens.shape
        self.ffn = ffn
        self.posts = self.held * CORES
        self.lines = self.seq_size // self.posts
        self.tile = CORES * self.slots
        self.rows = self.held * self.tile
        self.count = self.rows * self.lines
        self.half = self.width // CORES
        self.pairs = self.half // LANES
        self.heads = 2 * self.pairs
        self.quarter = ffn // 4
        self.depth = self.width // self.clip_size
        self.aligned = self.columns == 2 and (ffn // self.seq_size) % LANES == 0

    def locate(self):
        self.clip = lax.axis_index("clip")
        self.seq = lax.axis_index("seq")
        self.core = self.clip % CORES
        self.column = self.clip // CORES
        self.post = self.seq // self.lines
        self.line = self.seq % self.lines
        self.parity = self.post % self.held

    def sibling(self):
        return self.clip + 1 - 2 * self.core, self.seq

    def on_line(self, shift):
        return self.clip, self.post * self.lines + (self.line + shift) % self.lines

    def on_post(self, shift):
        return self.clip, (self.post + shift) % self.posts * self.lines + self.line

    def on_column(self, shift):
        return (self.column + shift) % self.columns * CORES + self.core, self.seq

    def goal(self, turn):
        post = self.held * self.core + (self.post + turn) % self.held
        return self.column * CORES + self.post // self.held, post * self.lines + self.line

    def origin(self, turn, who):
        post = self.held * who + (self.parity + turn) % self.held
        return self.column * CORES + self.post // self.held, post * self.lines + self.line

    def blocked(self, turn):
        return jnp.logical_and(self.post // self.held == self.core, turn == 0)


def remote(source, target, send, receive, device):
    return pltpu.make_async_remote_copy(
        src_ref=source, dst_ref=target, send_sem=send, recv_sem=receive,
        device_id=device, device_id_type=pl.DeviceIdType.MESH,
    )


def meet(geo, devices):
    barrier = pltpu.get_barrier_semaphore()
    total = 0
    for device in devices:
        other = jnp.logical_or(device[0] != geo.clip, device[1] != geo.seq)

        @pl.when(other)
        def greet(device=device):
            pl.semaphore_signal(
                barrier, inc=1, device_id=device, device_id_type=pl.DeviceIdType.MESH
            )

        total = total + other.astype(jnp.int32)
    pl.semaphore_wait(barrier, total)


def loop(count, body):
    def step(at, carry):
        body(at)
        return carry

    lax.fori_loop(0, count, step, 0)


def gelu_parts(inner):
    bell = jnp.exp2((inner * inner) * (-0.5 * LOG2E))
    phi = 0.5 + 0.5 * lax.erf(inner * SQRT_HALF)
    return phi, phi + inner * (GAUSS * bell)


KEPT = ("xall", "kx", "v", "q", "ot", "lse", "o", "z1", "hrt", "act", "slope", "z2")


def kept_shapes(geo):
    rows, width, half, count = geo.rows, geo.width, geo.half, geo.count
    return {
        "xall": ((count, width), b16),
        "kx": ((geo.pairs, count, 2 * LANES), b16),
        "v": ((count, half), b16),
        "q": ((rows, half), b16),
        "ot": ((half, rows), f32),
        "lse": ((geo.heads, 8, rows), f32),
        "o": ((rows, half), b16),
        "z1": ((rows, width), f32),
        "hrt": ((width, rows), b16),
        "act": ((rows, geo.ffn // CORES), b16),
        "slope": ((rows, geo.ffn // CORES), b16),
        "z2": ((rows, width), f32),
    }


def forward_kernel(geo, layers, *refs):
    refs = list(refs)

    def take(count):
        taken = refs[:count]
        del refs[:count]
        return taken

    tokens, cotangent, w_in, w_out, w_up, w_down = take(6)
    lengths, in_bias, out_bias, up_bias, down_bias, gains, shifts = take(7)
    (cot_rows,) = take(1)
    stored = [dict(zip(KEPT, take(len(KEPT)))) for unused in range(layers)]
    kept = [dict(zip(KEPT, take(len(KEPT)))) for unused in range(layers)]
    wq, wkv, wout, wup, wdown = take(5)
    qx, vt, state, hidden, lens, lens_there, psend, precv, running = take(9)
    (load_sem, save_sem, tok_sem, tok_send, tok_recv, cot_sem, cot_send, cot_recv, sib_send,
     sib_recv, line_send, line_recv, pass_send, pass_recv, part_send, part_recv,
     len_sem) = take(17)

    geo = duplicate(geo)
    geo.locate()
    core, tile, slots = geo.core, geo.tile, geo.slots
    held, lines, rows, width, half = geo.held, geo.lines, geo.rows, geo.width, geo.half
    quarter, pairs = geo.quarter, geo.pairs
    sibling = geo.sibling()

    loads = []
    for layer in range(layers):
        targets = (wq.at[layer], wkv.at[layer, :, :half], wkv.at[layer, :, half:])
        parts = [
            (w_in.at[layer, :, pl.ds(pl.multiple_of((kind * CORES + core) * half, half), half)],
             targets[kind])
            for kind in range(3)
        ]
        parts.append((w_out.at[layer, pl.ds(pl.multiple_of(core * half, half), half), :], wout.at[layer]))
        for block in range(2):
            at = pl.ds(pl.multiple_of((2 * block + core) * quarter, quarter), quarter)
            span = slice(block * quarter, (block + 1) * quarter)
            parts.append((w_up.at[layer, :, at], wup.at[layer, :, span]))
            parts.append((w_down.at[layer, at, :], wdown.at[layer, span, :]))
        loads.append([
            pltpu.make_async_copy(source, target, load_sem.at[layer, at])
            for at, (source, target) in enumerate(parts)
        ])
    for copy in loads[0]:
        copy.start()

    sources = [geo.origin(turn, who) for turn in range(held) for who in range(CORES)]
    goals = [geo.goal(turn) for turn in range(held)]
    goals = goals + [(device[0] + 1 - 2 * (device[0] % CORES), device[1]) for device in goals]
    near = [sibling] + [geo.on_line(shift) for shift in range(1, lines)]
    meet(geo, near + sources + goals)

    first = kept[0]["xall"]

    def block_at(turn, who, shift=0):
        start = shift * rows + turn * tile + who * slots
        return pl.ds(start if isinstance(start, int) else pl.multiple_of(start, slots), slots)

    def token_copies(turn, who):
        mine = tokens.at[(geo.post + turn) % held]
        place = first.at[block_at(turn, who)]
        own = pltpu.make_async_copy(mine, place, tok_sem.at[turn])
        return own, remote(mine, place, tok_send.at[turn], tok_recv.at[turn], geo.goal(turn))

    def token_start(turn):
        own, there = token_copies(turn, geo.post // held)
        pl.when(geo.blocked(turn))(own.start)
        pl.when(jnp.logical_not(geo.blocked(turn)))(there.start)

    def token_wait(turn):
        own, there = token_copies(turn, core)
        pl.when(geo.blocked(turn))(own.wait)
        pl.when(jnp.logical_not(geo.blocked(turn)))(there.wait)

    def to_sibling(array, turn, who, shift, send, receive):
        place = array.at[block_at(turn, who, shift)]
        return remote(place, place, send, receive, sibling)

    def to_line(layer, turn, shift):
        array = kept[layer]["xall"]
        source = array.at[block_at(turn, core)]
        target = array.at[block_at(turn, core, shift)]
        return remote(
            source, target, line_send.at[layer, turn, shift - 1], line_recv.at[layer, turn, shift - 1],
            geo.on_line(shift),
        )

    for turn in range(held):
        token_start(turn)
    clip_row = lax.broadcasted_iota(jnp.int32, lens.shape, 0)
    filled = jnp.full(lens.shape, lengths[0], jnp.int32)
    for clip in range(1, held):
        filled = jnp.where(clip_row == clip, lengths[clip], filled)
    lens[...] = filled
    len_copy = remote(lens, lens_there, len_sem.at[0], len_sem.at[1], sibling)
    len_copy.start()

    def clear(at):
        qx[at] = jnp.zeros(qx.shape[1:], b16)
        qx[at, LANES : LANES + 16, :] = (
            lax.broadcasted_iota(jnp.int32, (16, rows), 0) == 0
        ).astype(f32).astype(b16)

    loop(geo.heads, clear)
    len_copy.wait()
    known = jnp.where(geo.post // held == core, lens[...], lens_there[...])
    length = known[0:1, :]
    for clip in range(1, held):
        length = jnp.where(geo.parity == clip, known[clip : clip + 1, :], length)
    lane = lax.broadcasted_iota(jnp.int32, (slots, LANES), 1)
    slot = lax.broadcasted_iota(jnp.int32, (slots, LANES), 0)
    for shift in range(lines):
        for turn in range(held):
            for who in range(CORES):
                post = held * who + (geo.parity + turn) % held
                line = (geo.line + lines - shift) % lines
                outside = (post * lines + line) * slots + slot >= length
                mask = jnp.where(jnp.logical_and(lane == 0, outside), -1e30, 0.0)
                mask = jnp.where(jnp.logical_and(lane > 0, lane < 4), 1.0, mask).astype(b16)
                for layer in range(layers):
                    for pair in range(pairs):
                        kept[layer]["kx"][pair, block_at(turn, who, shift), LANES:] = mask

    def cot_copies(turn, flip):
        mine = cotangent.at[(geo.post + turn) % held]
        place = cot_rows.at[block_at(turn, geo.post // held)]
        goal = geo.goal(turn)
        if flip:
            goal = (goal[0] + 1 - 2 * (goal[0] % CORES), goal[1])
        own = pltpu.make_async_copy(mine, place, cot_sem.at[turn, flip])
        there = remote(
            mine, place, cot_send.at[turn, flip], cot_recv.at[turn, geo.post // held], goal
        )
        here = jnp.logical_and(goal[0] == geo.clip, goal[1] == geo.seq)
        return own, there, here

    def cot_start():
        for turn in range(held):
            for flip in range(CORES):
                own, there, here = cot_copies(turn, flip)
                pl.when(here)(own.start)
                pl.when(jnp.logical_not(here))(there.start)

    def cot_wait():
        for turn in range(held):
            for flip in range(CORES):
                own, there, here = cot_copies(turn, flip)
                pl.when(here)(own.wait)
                pl.when(jnp.logical_not(here))(there.wait_send)
            for who in range(CORES):
                source = geo.origin(turn, who)
                place = cot_rows.at[block_at(turn, who)]
                there = remote(
                    cotangent.at[0], place, cot_send.at[turn, 0], cot_recv.at[turn, who], source
                )
                here = jnp.logical_and(source[0] == geo.clip, source[1] == geo.seq)
                pl.when(jnp.logical_not(here))(there.wait_recv)

    def key_tile(layer, at):
        keep = kept[layer]
        now = pl.ds(pl.multiple_of(at, tile), tile)
        both = dot(keep["xall"][now, :], wkv[layer])
        key = both[:, :half].astype(b16)
        for pair in range(pairs):
            keep["kx"][pair, now, :LANES] = key[:, pair * LANES : (pair + 1) * LANES]
        bias = in_bias[layer : layer + 1, pl.ds(pl.multiple_of(width + core * half, half), half)]
        value = (both[:, half:] + bias).astype(b16)
        keep["v"][now, :] = value
        vt[:, now] = value.astype(f32).T.astype(b16)

    def query_tile(layer, at):
        keep = kept[layer]
        now = pl.ds(pl.multiple_of(at, tile), tile)
        bias = in_bias[layer : layer + 1, pl.ds(pl.multiple_of(core * half, half), half)]
        query = (dot(keep["xall"][now, :], wq[layer]) + bias).astype(b16)
        query = (query * SCALE).astype(b16)
        keep["q"][now, :] = query
        turned = (query.astype(f32) * LOG2E).T.astype(b16)
        for head in range(geo.heads):
            inside = head % 2 * HEAD_DIM
            qx[head, inside : inside + HEAD_DIM, now] = (
                turned[head * HEAD_DIM : (head + 1) * HEAD_DIM]
            )

    def attend_block(layer, shift):
        keep = kept[layer]
        span = slice(shift * rows, (shift + 1) * rows)

        size = min(512, rows)
        cuts = [slice(start, start + size) for start in range(shift * rows, (shift + 1) * rows, size)]

        def pair_step(pair):
            heads = [2 * pair, 2 * pair + 1]
            scores = [
                [dot(keep["kx"][pair, cut, :], qx[head]) for cut in cuts] for head in heads
            ]
            for head, pieces in zip(heads, scores):
                here = pl.ds(pl.multiple_of(head * HEAD_DIM, HEAD_DIM), HEAD_DIM)
                top = functools.reduce(
                    jnp.maximum, [jnp.max(piece, 0, keepdims=True) for piece in pieces]
                )
                if shift > 0:
                    before = keep["lse"][head, 0:1, :]
                    top = jnp.maximum(top, before)
                    shrink = jnp.exp2(before - top)
                total = attended = None
                for piece, cut in zip(pieces, cuts):
                    weights = jnp.exp2(piece - top)
                    sums = jnp.sum(weights, 0, keepdims=True)
                    values = dot(vt[here, cut], weights.astype(b16))
                    total = sums if total is None else total + sums
                    attended = values if attended is None else attended + values
                if shift > 0:
                    total = total + shrink * running[head, 0:1, :]
                    attended = attended + shrink * keep["ot"][here, :]
                if shift < lines - 1:
                    running[head, 0:1, :] = total
                    keep["ot"][here, :] = attended
                    keep["lse"][head, 0:1, :] = top
                else:
                    keep["ot"][here, :] = attended / total
                    keep["lse"][head, 0:1, :] = top + jnp.log(total) * LOG2E

        loop(pairs, pair_step)

    def project_tile(layer, turn):
        keep = kept[layer]
        now = pl.ds(pl.multiple_of(turn * tile, tile), tile)
        attended = keep["ot"][:, now].T.astype(b16)
        keep["o"][now, :] = attended
        share(2 * layer, turn, dot(attended, wout[layer]))

    def part_copy(which, turn):
        now = pl.ds(pl.multiple_of(turn * tile, tile), tile)
        return remote(
            psend.at[which, now, :], precv.at[which, now, :], part_send.at[which, turn],
            part_recv.at[which, turn], sibling,
        )

    def share(which, turn, part):
        now = pl.ds(pl.multiple_of(turn * tile, tile), tile)
        psend[which, now, :] = part.astype(b16)
        part_copy(which, turn).start()

    def collect(which, turn):
        now = pl.ds(pl.multiple_of(turn * tile, tile), tile)
        part_copy(which, turn).wait()
        return psend[which, now, :].astype(f32) + precv[which, now, :].astype(f32)

    def feed_tile(layer, turn):
        keep = kept[layer]
        now = pl.ds(pl.multiple_of(turn * tile, tile), tile)
        x = first[now, :].astype(f32) if layer == 0 else state[now, :]
        summed = x + collect(2 * layer, turn) + out_bias[layer : layer + 1, :]
        keep["z1"][now, :] = summed
        unit, unused = norm_parts(summed)
        normal = unit * gains[layer, 0:1, :] + shifts[layer, 0:1, :]
        hidden[now, :] = normal
        low = normal.astype(b16)
        keep["hrt"][:, now] = low.astype(f32).T.astype(b16)
        size = min(256, quarter)
        for at in range(0, 2 * quarter, size):
            block, start = at // quarter, at % quarter
            bias = up_bias[
                layer : layer + 1,
                pl.ds(pl.multiple_of((2 * block + core) * quarter + start, size), size),
            ]
            inner = dot(low, wup[layer, :, at : at + size]) + bias
            phi, slope = gelu_parts(inner)
            keep["act"][now, at : at + size] = (inner * phi).astype(b16)
            keep["slope"][now, at : at + size] = slope.astype(b16)
        total = dot(keep["act"][now, :], wdown[layer])
        share(2 * layer + 1, turn, total)

    def norm_tile(layer, turn):
        keep = kept[layer]
        now = pl.ds(pl.multiple_of(turn * tile, tile), tile)
        summed = hidden[now, :] + collect(2 * layer + 1, turn) + down_bias[layer : layer + 1, :]
        keep["z2"][now, :] = summed
        if layer < layers - 1:
            unit, unused = norm_parts(summed)
            result = unit * gains[layer, 1:2, :] + shifts[layer, 1:2, :]
            state[now, :] = result
            kept[layer + 1]["xall"][now, :] = result.astype(b16)

    saves = []

    def save(layer, names):
        for name in names:
            copy = pltpu.make_async_copy(
                kept[layer][name], stored[layer][name], save_sem.at[layer, KEPT.index(name)]
            )
            copy.start()
            saves.append(copy)

    for layer in range(layers):
        x_all = kept[layer]["xall"]
        for turn in range(held if layer == 0 else 0):
            token_wait(turn)
            mine = to_sibling(x_all, turn, core, 0, sib_send.at[turn], sib_recv.at[turn])
            mine.start()
            for shift in range(1, lines):
                to_line(0, turn, shift).start()
            if turn == 0:
                for copy in loads[0]:
                    copy.wait()
                for copy in loads[1]:
                    copy.start()
            mine.wait_send()
            to_sibling(x_all, turn, 1 - core, 0, sib_send.at[turn], sib_recv.at[turn]).wait_recv()
            key_tile(layer, turn * tile)
            query_tile(layer, turn * tile)
        for shift in range(lines):
            if shift > 0:
                for turn in range(held):
                    to_line(layer, turn, shift).wait()
                    to_sibling(
                        x_all, turn, core, shift,
                        pass_send.at[layer, turn, shift - 1], pass_recv.at[layer, turn, shift - 1],
                    ).start()
                for turn in range(held):
                    send = pass_send.at[layer, turn, shift - 1]
                    receive = pass_recv.at[layer, turn, shift - 1]
                    to_sibling(x_all, turn, core, shift, send, receive).wait_send()
                    to_sibling(x_all, turn, 1 - core, shift, send, receive).wait_recv()
                    key_tile(layer, shift * rows + turn * tile)
            if shift == lines - 1:
                save(layer, ("xall", "kx", "v", "q"))
                if layer == 0:
                    cot_start()

            attend_block(layer, shift)
        loop(held, functools.partial(project_tile, layer))
        save(layer, ("ot", "lse", "o"))
        loop(held, functools.partial(feed_tile, layer))
        save(layer, ("z1", "hrt", "act", "slope"))
        for turn in range(held):
            norm_tile(layer, turn)
            if layer < layers - 1:
                for shift in range(1, lines):
                    to_line(layer + 1, turn, shift).start()
                if turn == 0:
                    for copy in loads[layer + 1]:
                        copy.wait()
                key_tile(layer + 1, turn * tile)
                query_tile(layer + 1, turn * tile)
        save(layer, ("z2",))

    cot_wait()
    for copy in saves:
        copy.wait()


def forward(geo, layers, tokens, cotangent, lengths, weights, vectors):
    width, rows, half, ffn = geo.width, geo.rows, geo.half, geo.ffn
    shapes = kept_shapes(geo)
    any_spec = pl.BlockSpec(memory_space=pl.ANY)
    vmem_spec = pl.BlockSpec(memory_space=pltpu.VMEM)
    out_shape = [
        jax.ShapeDtypeStruct((rows, width), b16),
    ]
    out_shape += [jax.ShapeDtypeStruct(*shapes[name]) for unused in range(layers) for name in KEPT]
    scratch = [pltpu.VMEM(*shapes[name]) for unused in range(layers) for name in KEPT]
    scratch += [
        pltpu.VMEM((layers, width, half), b16),
        pltpu.VMEM((layers, width, 2 * half), b16),
        pltpu.VMEM((layers, half, width), b16),
        pltpu.VMEM((layers, width, 2 * geo.quarter), b16),
        pltpu.VMEM((layers, 2 * geo.quarter, width), b16),
        pltpu.VMEM((geo.heads, 2 * LANES, rows), b16),
        pltpu.VMEM((half, geo.count), b16),
        pltpu.VMEM((rows, width), f32),
        pltpu.VMEM((rows, width), f32),
        pltpu.VMEM((8, LANES), jnp.int32),
        pltpu.VMEM((8, LANES), jnp.int32),
        pltpu.VMEM((2 * layers, rows, width), b16),
        pltpu.VMEM((2 * layers, rows, width), b16),
        pltpu.VMEM((geo.heads, 8, rows), f32),
    ]
    held, lines = geo.held, max(geo.lines - 1, 1)
    dma = pltpu.SemaphoreType.DMA
    scratch += [dma(shape) for shape in (
        (layers, 8), (layers, len(KEPT)), (held,), (held,), (held,),
        (held, CORES), (held, CORES), (held, CORES), (held,), (held,),
        (layers, held, lines), (layers, held, lines), (layers, held, lines), (layers, held, lines),
        (2 * layers, held), (2 * layers, held), (2,),
    )]
    results = pl.pallas_call(
        functools.partial(forward_kernel, geo, layers),
        out_shape=out_shape,
        in_specs=[any_spec] * 6 + [pl.BlockSpec(memory_space=pltpu.SMEM)] + [vmem_spec] * 6,
        out_specs=[any_spec] * len(out_shape),
        scratch_shapes=scratch,
        compiler_params=pltpu.CompilerParams(
            collective_id=0, has_side_effects=True, vmem_limit_bytes=VMEM
        ),
        cost_estimate=pl.CostEstimate(flops=3 * 10**10, bytes_accessed=4 * 10**7, transcendentals=0),
    )(tokens, cotangent, *weights, lengths, *vectors)
    count = len(KEPT)
    kept = [
        dict(zip(KEPT, results[1 + layer * count : 1 + (layer + 1) * count]))
        for layer in range(layers)
    ]
    return results[0], kept


QUERY_BIAS, VALUE_BIAS, UP_BIAS, OUT_BIAS, DOWN_BIAS, GAIN, SHIFT = 0, 1, 2, 6, 7, 8, 10
SUMS = 16
UP, DOWN = 0, 1
INTO, PROJ = 0, 1
PAIRS = ("pair0", "pair1", "pair2")
UP_AFTER = (1, 1)


def backward_kernel(geo, layers, *refs):
    refs = list(refs)

    def take(count):
        taken = refs[:count]
        del refs[:count]
        return taken

    cot_rows, w_in, w_out, w_up, w_down = take(5)
    stored = [dict(zip(KEPT, take(len(KEPT)))) for unused in range(layers)]
    gains, shifts = take(2)
    out_tokens, grad_tokens, sums = take(3)
    if geo.aligned:
        feed_out, attend_out = take(2)
    else:
        plain = [take(6) for unused in range(layers)]
    keep = dict(zip(KEPT, take(len(KEPT))))
    wq, wkv, wout, wup, wdown = take(5)
    (o_there, low_grad, turned, du_there, psend, precv, do, qx, dox, dq, dkv, dq_there,
     dkv_there, probs_all, grads_all, do_stack, q_stack, dqt, mine_dx, dx_recv, line_in) = take(21)
    out_low = mine_dx
    (load_sem, o_send, o_recv, du_send, du_recv, part_send, part_recv, qkv_send, qkv_recv,
     dx_ssem, dx_rsem, line_send, line_recv, more_send, more_recv, tok_sem, tok_send,
     tok_recv, plain_sem, out_sem, out_send, out_recv) = take(22)
    if geo.aligned:
        (other, mine, from_x, y_first, y_last, z_first, z_last, into_cell, proj_cell, into_y, proj_y, into_z, proj_z,
         a_send, a_x, sum_in) = take(16)
        from_y, from_z = (y_first, y_last), (z_first, z_last)
        cells = [[into_cell] * layers, [proj_cell.at[layer] for layer in range(layers)]]
        cells_z = (into_z, proj_z)
        (fx_send, fx_recv, fy_send, fy_recv, fz_send, fz_recv, ay_send, ay_recv, az_send, az_recv,
         ax_send, ax_recv, sum_send, sum_recv) = take(14)
        credit, into_credit = take(2)

    geo = duplicate(geo)
    geo.locate()
    core, tile, slots = geo.core, geo.tile, geo.slots
    held, lines, rows, width, half = geo.held, geo.lines, geo.rows, geo.width, geo.half
    quarter, pairs, posts, depth = geo.quarter, geo.pairs, geo.posts, geo.depth
    post, line, column = geo.post, geo.line, geo.column
    unit = width // geo.seq_size
    sibling = geo.sibling()

    def tile_at(turn):
        return pl.ds(pl.multiple_of(turn * tile, tile), tile)

    def block_at(turn, who, shift=0):
        start = shift * rows + turn * tile + who * slots
        return pl.ds(start if isinstance(start, int) else pl.multiple_of(start, slots), slots)

    NAMES = KEPT + ("win", "wout", "wup", "wdown", "cot")

    def load_copies(layer, name):
        where = load_sem.at[layer, NAMES.index(name)]
        if name == "win":
            targets = (wq, wkv.at[:, :half], wkv.at[:, half:])
            return [
                pltpu.make_async_copy(
                    w_in.at[layer, :, pl.ds(pl.multiple_of((kind * CORES + core) * half, half), half)],
                    targets[kind], load_sem.at[layer, len(NAMES) + kind],
                )
                for kind in range(3)
            ]
        if name == "wout":
            at = pl.ds(pl.multiple_of(core * half, half), half)
            return [pltpu.make_async_copy(w_out.at[layer, at, :], wout, where)]
        if name in ("wup", "wdown"):
            copies = []
            for block in range(2):
                at = pl.ds(pl.multiple_of((2 * block + core) * quarter, quarter), quarter)
                slot = len(NAMES) + 3 + 2 * (name == "wdown") + block
                if name == "wup":
                    pair = w_up.at[layer, :, at], wup.at[:, block * quarter : (block + 1) * quarter]
                else:
                    pair = w_down.at[layer, at, :], wdown.at[block * quarter : (block + 1) * quarter, :]
                copies.append(pltpu.make_async_copy(*pair, load_sem.at[layer, slot]))
            return copies
        if name == "hrt" and geo.aligned:
            return [
                pltpu.make_async_copy(
                    stored[layer][name].at[pl.ds(pl.multiple_of((2 * which + core) * depth, depth), depth), :],
                    keep[name].at[which * depth : (which + 1) * depth, :],
                    load_sem.at[layer, len(NAMES) + 7 + which],
                )
                for which in range(2)
            ]
        if name == "cot":
            return [pltpu.make_async_copy(cot_rows, low_grad, where)]
        return [pltpu.make_async_copy(stored[layer][name], keep[name], where)]

    def load(layer, *names):
        for name in names:
            for copy in load_copies(layer, name):
                copy.start()

    def loaded(layer, *names):
        for name in names:
            for copy in load_copies(layer, name):
                copy.wait()

    top = layers - 1
    load(top, "z2", "cot", "wdown", "slope", "wup", "act", "z1", "wout", "q", "kx", "v", "ot",
         "lse", "win", "hrt", "xall", "o")

    sources = [geo.origin(turn, who) for turn in range(held) for who in range(CORES)]
    goals = [geo.goal(turn) for turn in range(held)]
    near = [sibling] + [geo.on_line(shift) for shift in range(1, lines)]
    if geo.aligned:
        near += [geo.on_post(shift) for shift in range(1, posts)]
        near += [geo.on_column(shift) for shift in range(1, geo.columns)]
    goals = goals + [(device[0] + 1 - 2 * (device[0] % CORES), device[1]) for device in goals]
    meet(geo, near + sources + goals)

    def o_copy(layer):
        return remote(stored[layer]["o"], o_there, o_send.at[layer], o_recv.at[layer], sibling)

    def clear(at):
        qx[at] = jnp.zeros(qx.shape[1:], b16)
        dox[at] = jnp.zeros(dox.shape[1:], b16)

    loop(2, clear)
    sums[...] = jnp.zeros_like(sums)

    def add_sum(layer, row, lanes, value):
        sums[layer, pl.ds(row, 1), lanes] += value

    everywhere = slice(None)


    def x_copy(layer, kind, z):
        return remote(
            other.at[kind, z], from_x.at[kind, z], fx_send.at[layer, kind, z],
            fx_recv.at[layer, kind, z], geo.on_column(1),
        )

    pair_post = post + 1 - 2 * (post % 2)
    far_post = (post + 2) % posts

    landed = {}

    def all_landed(hop, kind):
        landed[hop, kind] = landed.get((hop, kind), 0) + 1
        return landed[hop, kind] == posts

    def order(step):
        return (pair_post + step // 2 * (far_post - pair_post) + step % 2 * 2) % posts

    def at_post(which):
        return geo.clip, which * lines + line

    def y_copy(layer, kind, z, shift):
        there = from_y[layer].at[kind, shift - 1] if layer else from_y[layer].at[kind, z, shift - 1]
        at = 0 if layer else z
        return remote(
            mine.at[layer, kind, z, (line + shift) % lines], there,
            fy_send.at[layer, kind, at, shift - 1], fy_recv.at[layer, kind, at, shift - 1],
            geo.on_line(shift),
        )

    def z_copy(layer, kind, hop):
        block = mine.at[layer, kind, order(hop)]
        return remote(
            block if layer else block.at[line], from_z[layer].at[kind, hop],
            fz_send.at[layer, kind, hop], fz_recv.at[layer, kind, hop],
            at_post(far_post if hop == 2 else pair_post),
        )

    def land_x(layer, kind, step):
        z = order(step)
        x_copy(layer, kind, z).wait()
        total = mine[layer, kind, z].astype(f32) + from_x[kind, z].astype(f32)
        mine[layer, kind, z] = total.astype(b16)
        if layer == 0:
            for shift in range(1, lines):
                y_copy(layer, kind, z, shift).start()
            return
        if step < 2:
            z_copy(layer, kind, step).start()
        if all_landed("x", kind):
            device = geo.on_column(1)
            pl.semaphore_signal(
                credit.at[kind], inc=1, device_id=device, device_id_type=pl.DeviceIdType.MESH
            )

    def land_y(layer, kind, step):
        z = order(step)
        total = mine[layer, kind, z, line].astype(f32)
        for shift in range(1, lines):
            y_copy(layer, kind, z, shift).wait()
            total = total + from_y[layer][kind, z, shift - 1].astype(f32)
        mine[layer, kind, z, line] = total.astype(b16)
        if step < 2:
            z_copy(layer, kind, step).start()

    def land_near(layer, kind):
        z_copy(layer, kind, 1).wait()
        here = (layer, kind, far_post) if layer else (layer, kind, far_post, line)
        total = mine[here].astype(f32) + from_z[layer][kind, 1].astype(f32)
        mine[here] = total.astype(b16)
        z_copy(layer, kind, 2).start()

    def land_far(layer, kind):
        here = (layer, kind, post) if layer else (layer, kind, post, line)
        total = mine[here].astype(f32)
        for hop in (0, 2):
            z_copy(layer, kind, hop).wait()
            total = total + from_z[layer][kind, hop].astype(f32)
        if layer == 0:
            feed_out[layer, kind] = total
            return
        mine[here] = total.astype(b16)
        for shift in range(1, lines):
            y_copy(layer, kind, post, shift).start()

    def land_end(layer, kind):
        total = mine[layer, kind, post, line].astype(f32)
        for shift in range(1, lines):
            y_copy(layer, kind, post, shift).wait()
            total = total + from_y[layer][kind, shift - 1].astype(f32)
        feed_out[layer, kind] = total

    def landing(layer, kind, z, shift):
        if kind == INTO:
            return into_y.at[z, shift - 1]
        return proj_y.at[layer, z, shift - 1]

    def ay_copy(layer, kind, z, shift):
        return remote(
            cells[kind][layer].at[(line + shift) % lines, z], landing(layer, kind, z, shift),
            ay_send.at[layer, kind, z, shift - 1], ay_recv.at[layer, kind, z, shift - 1],
            geo.on_line(shift),
        )

    def az_copy(layer, kind, hop):
        return remote(
            cells[kind][layer].at[line, order(hop)], cells_z[kind].at[layer, hop],
            az_send.at[layer, kind, hop], az_recv.at[layer, kind, hop],
            at_post(far_post if hop == 2 else pair_post),
        )

    def ax_copy(layer, kind):
        span = slice(0, 3 * unit) if kind == INTO else slice(3 * unit, 4 * unit)
        return remote(
            a_send.at[layer, span], a_x.at[layer, span], ax_send.at[layer, kind],
            ax_recv.at[layer, kind], geo.on_column(1),
        )

    def send_ay(layer, kind):
        if layer < top and kind == INTO:
            pl.semaphore_wait(into_credit, lines - 1)
        for step in range(posts):
            for shift in range(1, lines):
                ay_copy(layer, kind, order(step), shift).start()

    def land_ay(layer, kind, step):
        z = order(step)
        cell = cells[kind][layer]
        total = cell[line, z].astype(f32)
        for shift in range(1, lines):
            ay_copy(layer, kind, z, shift).wait()
            total = total + landing(layer, kind, z, shift)[...].astype(f32)
        cell[line, z] = total.astype(b16)
        if step < 2:
            az_copy(layer, kind, step).start()

        if layer > 0 and kind == INTO and all_landed("into", kind):
            for shift in range(1, lines):
                pl.semaphore_signal(
                    into_credit, inc=1, device_id=geo.on_line(shift),
                    device_id_type=pl.DeviceIdType.MESH,
                )

    def land_anear(layer, kind):
        cell = cells[kind][layer]
        az_copy(layer, kind, 1).wait()
        total = cell[line, far_post].astype(f32) + cells_z[kind][layer, 1].astype(f32)
        cell[line, far_post] = total.astype(b16)
        az_copy(layer, kind, 2).start()

    def land_afar(layer, kind):
        total = cells[kind][layer][line, post].astype(f32)
        for hop in (0, 2):
            az_copy(layer, kind, hop).wait()
            total = total + cells_z[kind][layer, hop].astype(f32)
        low, high = total[:, :depth], total[:, depth:]
        span = slice(0, 3 * unit) if kind == INTO else slice(3 * unit, 4 * unit)
        attend_out[layer, span] = jnp.where(column == 0, low, high)
        a_send[layer, span] = jnp.where(column == 0, high, low).astype(b16)
        ax_copy(layer, kind).start()

    def land_ax(layer, kind):
        ax_copy(layer, kind).wait()
        span = slice(0, 3 * unit) if kind == INTO else slice(3 * unit, 4 * unit)
        attend_out[layer, span] = attend_out[layer, span] + a_x[layer, span].astype(f32)

    def sum_copies(layer, hop):
        near = ([sibling], [geo.on_line(shift) for shift in range(1, lines)],
                [at_post(pair_post)], [at_post(far_post)], [geo.on_column(1)])
        first = (0, 1, lines, lines + 1, lines + 2)[hop]
        return [
            (remote(
                sums.at[layer], sum_in.at[layer, first + at], sum_send.at[layer, first + at],
                sum_recv.at[layer, first + at], device,
            ), first + at)
            for at, device in enumerate(near[hop])
        ]

    def start_sum(layer):
        shared = lax.broadcasted_iota(jnp.int32, sums.shape[1:], 0) >= OUT_BIAS
        sums[layer] = jnp.where(shared, 0.5 * sums[layer], sums[layer])
        for copy, unused in sum_copies(layer, 0):
            copy.start()

    def land_sum(layer, hop):
        total = sums[layer]
        for copy, at in sum_copies(layer, hop):
            copy.wait()
            total = total + sum_in[layer, at]
        sums[layer] = total
        if hop < 4:
            for copy, unused in sum_copies(layer, hop + 1):
                copy.start()

    schedule = {
        (1, "up"): (
            (land_x, 1, DOWN, 1),
        ),
        (1, "dx"): (
            (land_ay, 1, PROJ, 1), (land_x, 1, DOWN, 0), (land_x, 1, DOWN, 2), (land_sum, 1, 0),
            (land_ay, 1, PROJ, 2),
        ),
        (1, "own"): (
            (land_anear, 1, PROJ),
        ),
        (1, "into"): (
            (land_x, 1, DOWN, 3), (land_near, 1, DOWN), (land_sum, 1, 1), (land_ay, 1, PROJ, 0),
            (land_x, 1, UP, 0),
        ),
        (0, "feed"): (
            (land_ay, 1, INTO, 0),
        ),
        (0, "up"): (
            (land_x, 0, DOWN, 1), (land_near, 1, UP),
        ),
        (0, "proj"): (
            (land_ay, 1, INTO, 1), (land_x, 1, UP, 1), (land_ay, 1, INTO, 2),
            (land_far, 1, DOWN),
        ),
        (0, "pair0"): (
            (land_x, 1, UP, 3), (land_anear, 1, INTO), (land_x, 1, UP, 2), (land_x, 0, DOWN, 0),
        ),
        (0, "dx"): (
            (land_sum, 1, 2), (land_ay, 1, INTO, 3), (land_ay, 0, PROJ, 2), (land_x, 0, DOWN, 2),
            (land_ay, 0, PROJ, 1), (land_ay, 0, PROJ, 0), (land_y, 0, DOWN, 0),
            (land_afar, 1, INTO),
        ),
        (0, "own"): (
            (land_y, 0, DOWN, 1), (land_anear, 0, PROJ),
        ),
        (0, "end"): (
            (land_x, 0, UP, 1), (land_y, 0, DOWN, 2), (land_near, 0, DOWN),
            (land_ay, 0, INTO, 1), (land_sum, 0, 0), (land_x, 0, UP, 2), (land_ay, 0, INTO, 2),
            (land_ay, 0, INTO, 0), (land_anear, 0, INTO), (land_x, 0, UP, 0),
            (land_ay, 0, INTO, 3), (land_sum, 0, 1), (land_ay, 0, PROJ, 3), (land_sum, 1, 3),
            (land_y, 0, UP, 1), (land_far, 1, UP), (land_ay, 1, PROJ, 3), (land_y, 0, UP, 2),
            (land_x, 0, DOWN, 3), (land_sum, 0, 2), (land_sum, 1, 4), (land_x, 0, UP, 3),
            (land_afar, 0, INTO), (land_end, 1, DOWN), (land_y, 0, UP, 0), (land_ax, 1, INTO),
            (land_near, 0, UP), (land_afar, 1, PROJ), (land_sum, 0, 3), (land_afar, 0, PROJ),
            (land_ax, 0, INTO), (land_end, 1, UP), (land_y, 0, DOWN, 3), (land_ax, 1, PROJ),
            (land_sum, 0, 4), (land_far, 0, DOWN), (land_ax, 0, PROJ), (land_y, 0, UP, 3),
            (land_far, 0, UP),
        ),
    }

    def progress(layer, phase):
        if geo.aligned:
            for function, *given in schedule.get((layer, phase), ()):
                function(*given)


    def part_copy(layer, turn):
        return remote(
            psend.at[tile_at(turn), :], precv.at[tile_at(turn), :], part_send.at[layer, turn],
            part_recv.at[layer, turn], sibling,
        )

    def du_copy(layer, turn):
        return remote(
            keep["slope"].at[tile_at(turn), :], du_there.at[tile_at(turn), :],
            du_send.at[layer, turn], du_recv.at[layer, turn], sibling,
        )

    def out_copies(turn, place):
        own = pltpu.make_async_copy(out_low.at[turn], place, out_sem.at[turn])
        there = remote(
            out_low.at[turn], place, out_send.at[turn], out_recv.at[turn], geo.origin(turn, core)
        )
        return own, there

    def send_home(copies, turn, target):
        own, there = copies(turn, target.at[geo.parity])
        pl.when(geo.blocked(turn))(own.start)
        pl.when(jnp.logical_not(geo.blocked(turn)))(there.start)

    def wait_home(copies, turn, target):
        own, there = copies(turn, target.at[(post + turn) % held])
        pl.when(geo.blocked(turn))(own.wait)
        pl.when(jnp.logical_not(geo.blocked(turn)))(there.wait)

    def norm_grads(layer, which, values, grad, turn):
        unit, inverse = norm_parts(values)
        gain = gains[layer, which : which + 1, :]
        if layer == top and which == 1:
            result = unit * gain + shifts[layer, which : which + 1, :]
            out_low[turn] = jnp.where(core == 0, result[:slots], result[slots:]).astype(b16)
            send_home(out_copies, turn, out_tokens)
        back, gain_grad, shift_grad = norm_back(unit, inverse, gain, grad)
        add_sum(layer, GAIN + which, everywhere, gain_grad)
        add_sum(layer, SHIFT + which, everywhere, shift_grad)
        return back

    def feed_back_tile(layer, turn):
        now = tile_at(turn)
        grad = low_grad[now, :].astype(f32)
        if layer < top:
            grad = grad + keep["z1"][now, :]
        back = norm_grads(layer, 1, keep["z2"][now, :], grad, turn)
        keep["z2"][now, :] = back
        low = back.astype(b16)
        wide = low.astype(f32)
        turned[:, now] = wide.T.astype(b16)
        add_sum(layer, DOWN_BIAS, everywhere, jnp.sum(wide, 0, keepdims=True))
        size = min(256, quarter)
        for at in range(0, 2 * quarter, size):
            block, start = at // quarter, at % quarter
            lanes = slice(at, at + size)
            grads = dot_nt(low, wdown[lanes, :])
            grads = (grads * keep["slope"][now, lanes].astype(f32)).astype(b16)
            keep["slope"][now, lanes] = grads
            add_sum(
                layer, UP_BIAS + 2 * block + core, slice(start, start + size),
                jnp.sum(grads.astype(f32), 0, keepdims=True),
            )
        total = dot_nt(keep["slope"][now, :], wup[...])
        psend[now, :] = total.astype(b16)
        part_copy(layer, turn).start()
        du_copy(layer, turn).start()

    def down_grads(layer, which, start):
        lanes = pl.ds(pl.multiple_of(which * quarter, quarter), quarter)
        size = lines * unit

        def chunk(at):
            steps = (2 * at, 2 * at + 1)
            left = [
                turned[pl.ds(pl.multiple_of(order(step) * size, size), size), :] for step in steps
            ]
            result = dot(jnp.concatenate(left, 0), keep["act"][:, lanes]).astype(b16)
            for index, step in enumerate(steps):
                z = order(step)
                for row in range(lines):
                    top = index * size + row * unit
                    for piece in range(2):
                        block = result[
                            top : top + unit, piece * quarter // 2 : (piece + 1) * quarter // 2
                        ]
                        span = slice(piece * unit, (piece + 1) * unit)
                        if start:
                            other[DOWN, z, row, span, :] = block
                        else:
                            mine[layer, DOWN, z, row, span, :] = block
                if start:
                    x_copy(layer, DOWN, z).start()

        loop(posts // 2, chunk)

    def up_grads(layer):
        left = [
            keep["hrt"][pl.ds(pl.multiple_of(which * depth, depth), depth), :]
            for which in (1 - column, column)
        ]
        left = jnp.concatenate(left, 0)
        size = quarter // lines
        for block in range(2):
            lanes = slice(block * quarter, (block + 1) * quarter)
            for there, array in ((0, keep["slope"]), (1, du_there)):
                z = 2 * block + core + there * (1 - 2 * core)
                result = dot(left, array[:, lanes]).astype(b16)
                for row in range(lines):
                    span = slice(row * size, (row + 1) * size)
                    other[UP, z, row] = result[:depth, span]
                    mine[layer, UP, z, row] = result[depth:, span]
        for step in range(posts):
            x_copy(layer, UP, order(step)).start()

    def feed_grads(layer, kind):
        if layer < top:
            pl.semaphore_wait(credit.at[kind], 1)
        if kind == UP:
            loaded(layer, "hrt")
            for turn in range(held):
                du_copy(layer, turn).wait()
            up_grads(layer)
        else:
            down_grads(layer, 1 - column, True)
            down_grads(layer, column, False)

    def proj_back_tile(layer, turn):
        now = tile_at(turn)
        part_copy(layer, turn).wait()
        grad = keep["z2"][now, :] + (psend[now, :].astype(f32) + precv[now, :].astype(f32))
        back = norm_grads(layer, 0, keep["z1"][now, :], grad, turn)
        keep["z1"][now, :] = back
        low = back.astype(b16)
        wide = low.astype(f32)
        turned[:, now] = wide.T.astype(b16)
        add_sum(layer, OUT_BIAS, everywhere, jnp.sum(wide, 0, keepdims=True))
        do[now, :] = dot_nt(low, wout[...]).astype(b16)

    lane_head = lax.broadcasted_iota(jnp.int32, (tile, LANES), 1) // HEAD_DIM

    def attend_back_pair(layer, pair):
        lanes = pl.ds(pl.multiple_of(pair * LANES, LANES), LANES)
        key_t = keep["kx"][pair, :, :LANES].astype(f32).T.astype(b16)
        query_t = (keep["q"][:, lanes].astype(f32) * LOG2E).T.astype(b16)
        grad_t = do[:, lanes].astype(f32).T.astype(b16)
        for head in range(2):
            here = slice(head * HEAD_DIM, (head + 1) * HEAD_DIM)
            qx[head, here, :] = query_t[here]
            dox[head, here, :] = grad_t[here]
            rest = -keep["lse"][2 * pair + head, 0:1, :]
            row = lax.broadcasted_iota(jnp.int32, (16, rows), 0)
            extra = jnp.where(row == 0, 1.0, 0.0)
            for part in range(1, 4):
                piece = rest.astype(b16).astype(f32)
                rest = rest - piece
                extra = jnp.where(row == part, piece, extra)
            qx[head, LANES : LANES + 16, :] = extra.astype(b16)

        def turn_step(turn):
            now = tile_at(turn)
            query = keep["q"][now, lanes].astype(f32)
            outgrad = do[now, lanes].astype(f32)
            for head in range(2):
                here = slice(head * HEAD_DIM, (head + 1) * HEAD_DIM)
                chosen = (lane_head == head).astype(f32)
                place = pl.ds(pl.multiple_of((2 * turn + head) * tile, tile), tile)
                do_stack[place, :] = (outgrad * chosen).astype(b16)
                q_stack[place, :] = (query * chosen).astype(b16)
                scores = dot(keep["kx"][pair], qx[head, :, now])
                probs = jnp.exp2(scores)
                probs_all[:, place] = probs.astype(b16)
                grads = dot(keep["v"][:, lanes], dox[head, :, now])
                own = pl.ds(pl.multiple_of(pair * LANES + head * HEAD_DIM, HEAD_DIM), HEAD_DIM)
                delta = jnp.sum(
                    dox[head, here, now].astype(f32) * keep["ot"][own, now], 0, keepdims=True
                )
                score_grads = (probs * (grads - delta)).astype(b16)
                grads_all[:, place] = score_grads
                dqt[here, now] = dot(key_t[here], score_grads)

        loop(held, turn_step)
        query_grad = (dqt[...].T * SCALE).astype(b16)
        value_grad = dot(probs_all[...], do_stack[...]).astype(b16)
        dq[:, lanes] = query_grad
        dkv[:, lanes] = dot(grads_all[...], q_stack[...]).astype(b16)
        dkv[:, pl.ds(pl.multiple_of(half + pair * LANES, LANES), LANES)] = value_grad
        spot = pl.ds(pl.multiple_of(core * half + pair * LANES, LANES), LANES)
        add_sum(layer, QUERY_BIAS, spot, jnp.sum(query_grad.astype(f32), 0, keepdims=True))
        add_sum(layer, VALUE_BIAS, spot, jnp.sum(value_grad.astype(f32), 0, keepdims=True))

    def qkv_copies(layer):
        return [
            remote(source, target, qkv_send.at[layer, at], qkv_recv.at[layer, at], sibling)
            for at, (source, target) in enumerate(((dq, dq_there), (dkv, dkv_there)))
        ]

    def dx_send(shift, turn):
        start = pl.multiple_of((shift * held + turn) * slots, slots)
        return psend.at[pl.ds(start, slots), :]

    def dx_copy(layer, shift, turn):
        return remote(
            dx_send(shift, turn), dx_recv.at[shift * held + turn],
            dx_ssem.at[layer, shift * held + turn], dx_rsem.at[layer, shift * held + turn], sibling,
        )

    def dx_tile(layer, shift, turn):
        now = pl.ds(pl.multiple_of(shift * rows + turn * tile, tile), tile)
        total = dot_nt(dkv[now, :], wkv[...])
        if shift == 0:
            total = total + dot_nt(dq[now, :], wq[...])
        first, second = total[:slots], total[slots:]
        mine_dx[shift * held + turn] = jnp.where(core == 0, first, second).astype(b16)
        dx_send(shift, turn)[...] = jnp.where(core == 0, second, first).astype(b16)
        dx_copy(layer, shift, turn).start()

    def line_copy(layer, shift, turn):
        return remote(
            dx_recv.at[shift * held + turn], line_in.at[layer, shift - 1, turn],
            line_send.at[layer, shift - 1, turn], line_recv.at[layer, shift - 1, turn],
            geo.on_line(lines - shift),
        )

    def more_copy(layer, turn, who):
        place = low_grad.at[block_at(turn, who)]
        return remote(place, place, more_send.at[layer, turn], more_recv.at[layer, turn], sibling)

    def token_copies(turn, place):
        own = pltpu.make_async_copy(low_grad.at[block_at(turn, core)], place, tok_sem.at[turn])
        there = remote(
            low_grad.at[block_at(turn, core)], place, tok_send.at[turn], tok_recv.at[turn],
            geo.origin(turn, core),
        )
        return own, there

    def mine_lanes(x):
        cuts = [x[:, at * depth : (at + 1) * depth] for at in range(2 * CORES)]
        return jnp.where(
            core == 0, jnp.concatenate([cuts[0], cuts[2]], 1), jnp.concatenate([cuts[1], cuts[3]], 1)
        )

    def into_grads(layer, there):
        units = half // unit
        x = mine_lanes(keep["xall"][...])
        owner = core + there * (1 - 2 * core)
        for first, ref in ((0, (dq, dq_there)[there]), (1, (dkv, dkv_there)[there])):
            result = dot_tn(ref[...], x[: ref.shape[0]]).astype(b16)
            for at in range(result.shape[0] // unit):
                kind = first + at // units
                index = (2 * kind + owner) * units + at % units
                seq = index // 3
                where = pl.ds(pl.multiple_of(index % 3 * unit, unit), unit)
                into_cell[seq % lines, seq // lines, where, :] = result[at * unit : (at + 1) * unit]
        if there:
            send_ay(layer, INTO)

    def own_total(layer, turn):
        dx_copy(layer, 0, turn).wait_recv()
        total = mine_dx[turn].astype(f32) + dx_recv[turn].astype(f32)
        for shift in range(1, lines):
            line_copy(layer, shift, turn).wait()
            total = total + line_in[layer, shift - 1, turn].astype(f32)
        return total

    def take_grad(layer, turn):
        low_grad[block_at(turn, core), :] = own_total(layer, turn).astype(b16)
        more_copy(layer, turn, core).start()
        more_copy(layer, turn, core).wait_send()
        more_copy(layer, turn, 1 - core).wait_recv()

    def proj_grads(layer):
        here, there = keep["o"][...], o_there[...]
        features = jnp.where(
            core == 0,
            jnp.concatenate([here[:, :depth], there[:, :depth]], 1),
            jnp.concatenate([there[:, depth:], here[:, depth:]], 1),
        )
        result = dot(turned[...], features).astype(b16)
        for seq in range(geo.seq_size):
            proj_cell[layer, seq % lines, seq // lines] = result[seq * unit : (seq + 1) * unit]
        send_ay(layer, PROJ)

    def plain_out(layer, names):
        sources = {"du": keep["slope"], "dft": turned, "dat": turned, "dq": dq, "dk": dkv.at[:, :half], "dv": dkv.at[:, half:]}
        order = ("du", "dft", "dat", "dq", "dk", "dv")
        copies = [
            pltpu.make_async_copy(sources[name], plain[layer][order.index(name)], plain_sem.at[order.index(name)])
            for name in names
        ]
        for copy in copies:
            copy.start()
        for copy in copies:
            copy.wait()

    for layer in range(layers - 1, -1, -1):
        last = layer == 0
        below = layer - 1
        if layer == top:
            loaded(layer, "cot")
        loaded(layer, "z2", "wdown", "slope", "wup")

        def feed_step(turn):
            if layer < top:
                take_grad(layer + 1, turn)
            feed_back_tile(layer, turn)

        if layer < top:
            for turn in range(held):
                dx_copy(layer + 1, 0, turn).wait_send()
        loop(held, feed_step)
        o_copy(layer).start()
        progress(layer, "feed")
        if not last:
            load(below, "wdown", "wup")
        else:
            load(layer, "z1")
        loaded(layer, "act")
        if geo.aligned:
            feed_grads(layer, DOWN)
            progress(layer, "down")
            if UP_AFTER[layer] is None:
                feed_grads(layer, UP)
                progress(layer, "up")
        else:
            plain_out(layer, ("dft",))
        if not last:
            load(below, "act")
        loaded(layer, "z1", "wout")
        loop(held, functools.partial(proj_back_tile, layer))
        progress(layer, "proj")
        if not last:
            load(below, "wout", "z2")
        if geo.aligned:
            loaded(layer, "o")
            o_copy(layer).wait()
            proj_grads(layer)
        loaded(layer, "q", "kx", "v", "ot", "lse")

        def pair_step(pair):
            attend_back_pair(layer, pair)
            for index in range(pairs if geo.aligned else 0):

                @pl.when(pair == index)
                def after_pair(index=index):
                    progress(layer, PAIRS[index])
                    if index == UP_AFTER[layer]:
                        feed_grads(layer, UP)
                        progress(layer, "up")

        loop(pairs, pair_step)
        if not last:
            load(below, "q", "kx", "v", "ot", "lse")
        for copy in qkv_copies(layer):
            copy.start()
        if geo.aligned:
            start_sum(layer)
        loaded(layer, "win")
        if layer == top:
            for turn in range(held):
                wait_home(out_copies, turn, out_tokens)
        for shift in range(1, lines):
            loop(held, functools.partial(dx_tile, layer, shift))
        progress(layer, "dx")
        if geo.aligned and last:
            loaded(layer, "xall")
            into_grads(layer, 0)
        for shift in range(1, lines):
            for turn in range(held):
                dx_copy(layer, shift, turn).wait()
                at = shift * held + turn
                dx_recv[at] = (mine_dx[at].astype(f32) + dx_recv[at].astype(f32)).astype(b16)
                line_copy(layer, shift, turn).start()

        def own_rows():
            loop(held, functools.partial(dx_tile, layer, 0))
            progress(layer, "own")

        if not last:
            own_rows()
            load(below, "win")
        if geo.aligned:
            if not last:
                loaded(layer, "xall")
                into_grads(layer, 0)
            for copy in qkv_copies(layer):
                copy.wait()
            into_grads(layer, 1)
            progress(layer, "into")
        else:
            for turn in range(held):
                du_copy(layer, turn).wait()
            for copy in qkv_copies(layer):
                copy.wait()
            loaded(layer, "hrt", "xall", "o")
            o_copy(layer).wait()
            plain_out(layer, ("du", "dat", "dq", "dk", "dv"))
        if not last:
            load(below, "hrt", "slope", "xall", "o")
        else:
            own_rows()
            for turn in range(held):
                dx_copy(layer, 0, turn).wait_send()
                total = own_total(layer, turn) + keep["z1"][block_at(turn, core), :]
                low_grad[block_at(turn, core), :] = total.astype(b16)
                send_home(token_copies, turn, grad_tokens)

    progress(0, "end")
    for turn in range(held):
        wait_home(token_copies, turn, grad_tokens)


def backward(geo, layers, cot_rows, weights, kept, gains, shifts):
    width, rows, half, ffn, count = geo.width, geo.rows, geo.half, geo.ffn, geo.count
    held, lines, posts, slots, quarter = geo.held, geo.lines, geo.posts, geo.slots, geo.quarter
    shapes = kept_shapes(geo)
    any_spec = pl.BlockSpec(memory_space=pl.ANY)
    vmem_spec = pl.BlockSpec(memory_space=pltpu.VMEM)
    unit = width // geo.seq_size
    out = [((held, slots, width), b16)] * 2 + [((layers, SUMS, width), f32)]
    out_specs = [any_spec] * 2 + [vmem_spec]
    if geo.aligned:
        out += [
            ((layers, 2, geo.depth, quarter // lines), f32),
            ((layers, 4 * unit, geo.depth), f32),
        ]
        out_specs += [vmem_spec] * 2
    else:
        for unused in range(layers):
            out += [
                ((rows, ffn // CORES), b16), ((width, rows), b16), ((width, rows), b16),
                ((rows, half), b16), ((count, half), b16), ((count, half), b16),
            ]
            out_specs += [any_spec] * 6
    vmem = pltpu.VMEM
    if geo.aligned:
        shapes["hrt"] = (2 * geo.depth, rows), b16
    scratch = [vmem(*shapes[name]) for name in KEPT]
    scratch += [
        vmem((width, half), b16), vmem((width, 2 * half), b16), vmem((half, width), b16),
        vmem((width, 2 * quarter), b16), vmem((2 * quarter, width), b16),
        vmem((rows, half), b16),
        vmem((rows, width), b16),
        vmem((width, rows), b16),
        vmem((rows, ffn // CORES), b16),
        vmem((max(rows, lines * held * slots), width), b16), vmem((rows, width), b16),
        vmem((rows, half), b16),
        vmem((2, 2 * LANES, rows), b16), vmem((2, LANES, rows), b16),
        vmem((rows, half), b16), vmem((count, 2 * half), b16),
        vmem((rows, half), b16), vmem((count, 2 * half), b16),
        vmem((count, 2 * rows), b16), vmem((count, 2 * rows), b16),
        vmem((2 * rows, LANES), b16), vmem((2 * rows, LANES), b16), vmem((LANES, rows), f32),
        vmem((lines * held, slots, width), b16), vmem((lines * held, slots, width), b16),
        vmem((layers, lines - 1, held, slots, width), b16),
    ]
    dma = pltpu.SemaphoreType.DMA
    scratch += [dma(shape) for shape in (
        (layers, len(KEPT) + 16), (layers,), (layers,), (layers, held), (layers, held),
        (layers, held), (layers, held), (layers, 3), (layers, 3),
        (layers, lines * held), (layers, lines * held),
        (layers, lines - 1, held), (layers, lines - 1, held),
        (layers, held), (layers, held), (held,), (held,), (held,), (6,),
        (held,), (held,), (held,),
    )]
    if geo.aligned:
        block = (geo.depth, quarter // lines)
        into, proj = (3 * unit, 2 * geo.depth), (unit, 2 * geo.depth)
        hops = lines + 3
        scratch += [
            vmem((2, posts, lines, *block), b16), vmem((layers, 2, posts, lines, *block), b16),
            vmem((2, posts, lines, *block), b16),
            vmem((2, posts, lines - 1, *block), b16), vmem((2, lines - 1, *block), b16),
            vmem((2, 3, *block), b16), vmem((2, 3, lines, *block), b16),
            vmem((lines, posts, *into), b16), vmem((layers, lines, posts, *proj), b16),
            vmem((posts, lines - 1, *into), b16), vmem((layers, posts, lines - 1, *proj), b16),
            vmem((layers, 3, *into), b16), vmem((layers, 3, *proj), b16),
            vmem((layers, 4 * unit, geo.depth), b16), vmem((layers, 4 * unit, geo.depth), b16),
            vmem((layers, hops, SUMS, width), f32),
        ]
        scratch += [dma(shape) for shape in (
            (layers, 2, posts), (layers, 2, posts),
            (layers, 2, posts, lines - 1), (layers, 2, posts, lines - 1),
            (layers, 2, 3), (layers, 2, 3),
            (layers, 2, posts, lines - 1), (layers, 2, posts, lines - 1),
            (layers, 2, 3), (layers, 2, 3), (layers, 2), (layers, 2),
            (layers, hops), (layers, hops),
        )]
        scratch += [pltpu.SemaphoreType.REGULAR((2,)), pltpu.SemaphoreType.REGULAR]
    stored = [kept[layer][name] for layer in range(layers) for name in KEPT]
    return pl.pallas_call(
        functools.partial(backward_kernel, geo, layers),
        out_shape=[jax.ShapeDtypeStruct(*shape) for shape in out],
        in_specs=[any_spec] * (5 + len(stored)) + [vmem_spec] * 2,
        out_specs=out_specs,
        scratch_shapes=scratch,
        compiler_params=pltpu.CompilerParams(
            collective_id=1, has_side_effects=True, vmem_limit_bytes=VMEM_BACK
        ),
        cost_estimate=pl.CostEstimate(flops=8 * 10**10, bytes_accessed=6 * 10**7, transcendentals=0),
    )(cot_rows, *weights, *stored, gains, shifts)


def finish_kernel(
    geo, core_ref, sums_ref, feed_ref, attend_ref, out_in_ref, grad_in_ref,
    out_ref, grad_ref, into_ref, in_bias_ref, proj_ref, out_bias_ref, up_ref, up_bias_ref, down_ref, down_bias_ref,
    gain_ref, shift_ref,
):
    seq = core_ref[0]
    layer = pl.program_id(0)
    unit = geo.width // geo.seq_size
    wide, span = 2 * unit, geo.ffn // geo.seq_size
    per_row, per_quarter = geo.width // wide, geo.quarter // span

    def turn(rows, amount):
        return pltpu.roll(rows, (geo.width - amount) % geo.width, 1)

    out_ref[...] = out_in_ref[...]
    grad_ref[...] = grad_in_ref[...]
    up_ref[0] = feed_ref[0, UP]
    down = feed_ref[0, DOWN]
    down_ref[0] = jnp.concatenate([down[:unit], down[unit:]], 1)
    both = attend_ref[0].T
    into_ref[0] = both[:, : 3 * unit]
    proj_ref[0] = both[:, 3 * unit :]
    sums = sums_ref[0]
    narrow = turn(sums, seq * unit)
    out_bias_ref[pl.ds(layer, 1), :] = narrow[OUT_BIAS : OUT_BIAS + 1, :unit]
    down_bias_ref[pl.ds(layer, 1), :] = narrow[DOWN_BIAS : DOWN_BIAS + 1, :unit]
    gain_ref[0] = narrow[GAIN : GAIN + 2, :unit]
    shift_ref[0] = narrow[SHIFT : SHIFT + 2, :unit]
    middle = turn(sums, seq % per_row * wide)
    first = middle[QUERY_BIAS : QUERY_BIAS + 1, :wide]
    second = middle[VALUE_BIAS : VALUE_BIAS + 1, :wide]
    in_bias_ref[pl.ds(layer, 1), :] = jnp.where(seq < per_row, first, second)
    large = turn(sums, seq % per_quarter * span)
    chosen = large[UP_BIAS : UP_BIAS + 1, :span]
    for block in range(1, 4):
        chosen = jnp.where(
            seq // per_quarter == block, large[UP_BIAS + block : UP_BIAS + block + 1, :span], chosen
        )
    up_bias_ref[pl.ds(layer, 1), :] = chosen


def finish(geo, layers, seq, sums, feed_out, attend_out, out_tokens, grad_tokens):
    unit, width = geo.width // geo.seq_size, geo.width
    span = geo.ffn // geo.seq_size
    depth = geo.depth
    shapes = [
        (layers, depth, 3 * unit), (layers, 2 * unit), (layers, depth, unit), (layers, unit),
        (layers, depth, span), (layers, span), (layers, unit, geo.ffn // geo.clip_size),
        (layers, unit), (layers, 2, unit), (layers, 2, unit),
    ]

    def by_layer(shape):
        rest = (0,) * (len(shape) - 1)
        return (1, *shape[1:]), lambda g, c: (g, *rest)

    results = list(call(
        functools.partial(finish_kernel, geo), seq, layers,
        [
            (array, *by_layer(array.shape))
            for array in (sums, feed_out, attend_out, out_tokens, grad_tokens)
        ],
        [(out_tokens.shape, b16, *by_layer(out_tokens.shape))] * 2
        + [
            (shape, f32, *by_layer(shape)) if len(shape) > 2 else full(shape, f32)
            for shape in shapes
        ],
        [], 10**7, 10**7,
    ))
    results[8] = jnp.swapaxes(results[8], 1, 2)
    return results


def build(mesh):
    clip_size, seq_size = mesh.shape["clip"], mesh.shape["seq"]

    def shards(
        tokens, lengths, attn_in, in_bias, attn_out, out_bias, ffn_in, ffn_in_bias,
        ffn_out, ffn_out_bias, norm_gain, norm_bias, cotangent,
    ):
        layers = attn_in.shape[0]
        geo = Geometry(mesh, tokens, ffn_in.shape[2])
        geo.locate()
        held, width, ffn, half, quarter = geo.held, geo.width, geo.ffn, geo.half, geo.quarter
        aligned, core = geo.aligned, geo.core
        seq_at = geo.seq

        weights = (attn_in, attn_out, ffn_in, ffn_out)
        cot_rows, kept = forward(
            geo, layers, tokens, cotangent, lengths, weights,
            (in_bias, out_bias, ffn_in_bias, ffn_out_bias, norm_gain, norm_bias),
        )
        out_tokens, grad_tokens, sums, *results = backward(
            geo, layers, cot_rows, weights, kept, norm_gain, norm_bias
        )
        if aligned:
            seq_arg = jnp.reshape(seq_at, (1,)).astype(jnp.int32)
            return tuple(finish(geo, layers, seq_arg, sums, *results, out_tokens, grad_tokens))

        def swap(array):
            pairs = [(at, at ^ 1) for at in range(clip_size)]
            return lax.ppermute(array, "clip", pairs)

        def spread(array):
            array = lax.psum_scatter(
                array.astype(b16), "seq", scatter_dimension=1, tiled=True
            ).astype(b16)
            return lax.psum_scatter(array, "clip", scatter_dimension=0, tiled=True).astype(f32)

        matrices = []
        for layer in range(layers):
            du, df_t, da_t, dq, dk, dv = results[6 * layer : 6 * layer + 6]
            keep = kept[layer]
            x_all = keep["xall"]
            into = [
                jnp.concatenate([jnp.where(core == 0, a, b), jnp.where(core == 0, b, a)], 1)
                for a, b in (
                    (dot_tn(x_all[: array.shape[0]], array), dot_tn(x_all[: array.shape[0]], swap(array)))
                    for array in (dq, dk, dv)
                )
            ]
            proj = jnp.zeros((CORES, half, width), f32)
            proj = lax.dynamic_update_slice_in_dim(proj, dot(da_t, keep["o"]).T[None], core, 0)
            up = jnp.zeros((2, CORES, width, quarter), f32)
            own_up = dot(keep["hrt"], du).reshape(width, 2, 1, quarter).transpose(1, 2, 0, 3)
            up = lax.dynamic_update_slice_in_dim(up, own_up, core, 1)
            down = jnp.zeros((2, CORES, quarter, width), f32)
            own_down = dot(df_t, keep["act"]).T.reshape(2, 1, quarter, width)
            down = lax.dynamic_update_slice_in_dim(down, own_down, core, 1)
            matrices.append((
                spread(jnp.concatenate(into, 1) * 0.5),
                spread(proj.reshape(width, width)),
                spread(up.transpose(2, 0, 1, 3).reshape(width, ffn)),
                spread(down.reshape(ffn, width)),
            ))
        halves = jnp.arange(SUMS)[None, :, None] >= OUT_BIAS
        summed = lax.psum(jnp.where(halves, 0.5 * sums, sums), ("clip", "seq"))

        def share(row, count):
            piece = summed[:, row : row + count].reshape(layers, count * width)
            size = count * width // seq_size
            return lax.dynamic_slice_in_dim(piece, seq_at * size, size, 1)

        into, proj, up, down = (
            jnp.stack([matrices[layer][which] for layer in range(layers)]) for which in range(4)
        )
        return (
            out_tokens, grad_tokens, into, share(QUERY_BIAS, 2), proj, share(OUT_BIAS, 1),
            up, share(UP_BIAS, 4), down, share(DOWN_BIAS, 1),
            jnp.stack([share(GAIN, 1), share(GAIN + 1, 1)], 1),
            jnp.stack([share(SHIFT, 1), share(SHIFT + 1, 1)], 1),
        )

    return shards


def solution(mesh):
    rowed = P("clip", "seq", None)
    in_specs = (rowed, P("clip")) + (P(),) * 10 + (rowed,)
    out_specs = (
        rowed,
        rowed,
        P(None, "clip", "seq"),
        P(None, "seq"),
        P(None, "clip", "seq"),
        P(None, "seq"),
        P(None, "clip", "seq"),
        P(None, "seq"),
        P(None, "clip", "seq"),
        P(None, "seq"),
        P(None, None, "seq"),
        P(None, None, "seq"),
    )
    return jax.shard_map(
        build(mesh), mesh=mesh, in_specs=in_specs, out_specs=out_specs, check_vma=False
    )
```

```python
from copy import copy as duplicate
import functools

import jax
import jax.numpy as jnp
from jax import lax
from jax.experimental import pallas as pl
from jax.experimental.pallas import tpu as pltpu
from jax.sharding import PartitionSpec as P

HEADS = 12
HEAD_DIM = 64
CORES = 2
LANES = 128
SCALE = HEAD_DIM**-0.5
SQRT_HALF = 0.5**0.5
GAUSS = 0.3989422804014327
LOG2E = 1.4426950408889634
EPS = 1e-05
VMEM = 56 * 1024 * 1024
VMEM_BACK = 63 * 1024 * 1024

f32 = jnp.float32
b16 = jnp.bfloat16


def dot(a, b):
    return lax.dot_general(a, b, (((1,), (0,)), ((), ())), preferred_element_type=f32)


def dot_nt(a, b):
    return lax.dot_general(a, b, (((1,), (1,)), ((), ())), preferred_element_type=f32)


def dot_tn(a, b):
    return lax.dot_general(a, b, (((0,), (0,)), ((), ())), preferred_element_type=f32)


def norm_parts(values):
    center = values - jnp.mean(values, -1, keepdims=True)
    inverse = lax.rsqrt(jnp.mean(center * center, -1, keepdims=True) + EPS)
    return center * inverse, inverse


def norm_back(unit, inverse, gain, grad):
    scaled = grad * gain
    mean_one = jnp.mean(scaled, -1, keepdims=True)
    mean_two = jnp.mean(scaled * unit, -1, keepdims=True)
    back = inverse * (scaled - mean_one - unit * mean_two)
    return back, jnp.sum(grad * unit, 0, keepdims=True), jnp.sum(grad, 0, keepdims=True)


def call(kernel, core, grid, ins, outs, scratch, flops, moved):
    in_specs = [pl.BlockSpec(block, lambda g, c, at=at: at(g, c[0])) for unused, block, at in ins]
    out_specs = [pl.BlockSpec(block, lambda g, c, at=at: at(g, c[0])) for s, d, block, at in outs]
    return pl.pallas_call(
        kernel,
        grid_spec=pltpu.PrefetchScalarGridSpec(
            num_scalar_prefetch=1,
            grid=(grid,),
            in_specs=in_specs,
            out_specs=out_specs,
            scratch_shapes=scratch,
        ),
        out_shape=[jax.ShapeDtypeStruct(shape, dtype) for shape, dtype, b, at in outs],
        compiler_params=pltpu.CompilerParams(
            dimension_semantics=("arbitrary",), vmem_limit_bytes=VMEM
        ),
        cost_estimate=pl.CostEstimate(flops=flops, bytes_accessed=moved, transcendentals=0),
    )(core, *[array for array, b, at in ins])


def all_of(array):
    zeros = (0,) * array.ndim
    return (array, array.shape, lambda g, c: zeros)


def full(shape, dtype):
    zeros = (0,) * len(shape)
    return (shape, dtype, shape, lambda g, c: zeros)


class Geometry:
    def __init__(self, mesh, tokens, ffn):
        self.clip_size, self.seq_size = mesh.shape["clip"], mesh.shape["seq"]
        self.columns = self.clip_size // CORES
        self.held, self.slots, self.width = tokens.shape
        self.ffn = ffn
        self.posts = self.held * CORES
        self.lines = self.seq_size // self.posts
        self.tile = CORES * self.slots
        self.rows = self.held * self.tile
        self.count = self.rows * self.lines
        self.half = self.width // CORES
        self.pairs = self.half // LANES
        self.heads = 2 * self.pairs
        self.quarter = ffn // 4
        self.depth = self.width // self.clip_size
        self.aligned = self.columns == 2 and (ffn // self.seq_size) % LANES == 0

    def locate(self):
        self.clip = lax.axis_index("clip")
        self.seq = lax.axis_index("seq")
        self.core = self.clip % CORES
        self.column = self.clip // CORES
        self.post = self.seq // self.lines
        self.line = self.seq % self.lines
        self.parity = self.post % self.held

    def sibling(self):
        return self.clip + 1 - 2 * self.core, self.seq

    def on_line(self, shift):
        return self.clip, self.post * self.lines + (self.line + shift) % self.lines

    def on_post(self, shift):
        return self.clip, (self.post + shift) % self.posts * self.lines + self.line

    def on_column(self, shift):
        return (self.column + shift) % self.columns * CORES + self.core, self.seq

    def goal(self, turn):
        post = self.held * self.core + (self.post + turn) % self.held
        return self.column * CORES + self.post // self.held, post * self.lines + self.line

    def origin(self, turn, who):
        post = self.held * who + (self.parity + turn) % self.held
        return self.column * CORES + self.post // self.held, post * self.lines + self.line

    def blocked(self, turn):
        return jnp.logical_and(self.post // self.held == self.core, turn == 0)


def remote(source, target, send, receive, device):
    return pltpu.make_async_remote_copy(
        src_ref=source, dst_ref=target, send_sem=send, recv_sem=receive,
        device_id=device, device_id_type=pl.DeviceIdType.MESH,
    )


def meet(geo, devices):
    barrier = pltpu.get_barrier_semaphore()
    total = 0
    for device in devices:
        other = jnp.logical_or(device[0] != geo.clip, device[1] != geo.seq)

        @pl.when(other)
        def greet(device=device):
            pl.semaphore_signal(
                barrier, inc=1, device_id=device, device_id_type=pl.DeviceIdType.MESH
            )

        total = total + other.astype(jnp.int32)
    pl.semaphore_wait(barrier, total)


def loop(count, body):
    def step(at, carry):
        body(at)
        return carry

    lax.fori_loop(0, count, step, 0)


def gelu_parts(inner):
    bell = jnp.exp2((inner * inner) * (-0.5 * LOG2E))
    phi = 0.5 + 0.5 * lax.erf(inner * SQRT_HALF)
    return phi, phi + inner * (GAUSS * bell)


KEPT = ("xall", "kx", "v", "q", "ot", "lse", "o", "z1", "hrt", "act", "slope", "z2")


def kept_shapes(geo):
    rows, width, half, count = geo.rows, geo.width, geo.half, geo.count
    return {
        "xall": ((count, width), b16),
        "kx": ((geo.pairs, count, 2 * LANES), b16),
        "v": ((count, half), b16),
        "q": ((rows, half), b16),
        "ot": ((half, rows), f32),
        "lse": ((geo.heads, 8, rows), f32),
        "o": ((rows, half), b16),
        "z1": ((rows, width), f32),
        "hrt": ((width, rows), b16),
        "act": ((rows, geo.ffn // CORES), b16),
        "slope": ((rows, geo.ffn // CORES), b16),
        "z2": ((rows, width), f32),
    }


def forward_kernel(geo, layers, *refs):
    refs = list(refs)

    def take(count):
        taken = refs[:count]
        del refs[:count]
        return taken

    tokens, cotangent, w_in, w_out, w_up, w_down = take(6)
    lengths, in_bias, out_bias, up_bias, down_bias, gains, shifts = take(7)
    (cot_rows,) = take(1)
    stored = [dict(zip(KEPT, take(len(KEPT)))) for unused in range(layers)]
    kept = [dict(zip(KEPT, take(len(KEPT)))) for unused in range(layers)]
    wq, wkv, wout, wup, wdown = take(5)
    qx, vt, state, hidden, lens, lens_there, psend, precv, running = take(9)
    (load_sem, save_sem, tok_sem, tok_send, tok_recv, cot_sem, cot_send, cot_recv, sib_send,
     sib_recv, line_send, line_recv, pass_send, pass_recv, part_send, part_recv,
     len_sem) = take(17)

    geo = duplicate(geo)
    geo.locate()
    core, tile, slots = geo.core, geo.tile, geo.slots
    held, lines, rows, width, half = geo.held, geo.lines, geo.rows, geo.width, geo.half
    quarter, pairs = geo.quarter, geo.pairs
    sibling = geo.sibling()

    loads = []
    for layer in range(layers):
        targets = (wq.at[layer], wkv.at[layer, :, :half], wkv.at[layer, :, half:])
        parts = [
            (w_in.at[layer, :, pl.ds(pl.multiple_of((kind * CORES + core) * half, half), half)],
             targets[kind])
            for kind in range(3)
        ]
        parts.append((w_out.at[layer, pl.ds(pl.multiple_of(core * half, half), half), :], wout.at[layer]))
        for block in range(2):
            at = pl.ds(pl.multiple_of((2 * block + core) * quarter, quarter), quarter)
            span = slice(block * quarter, (block + 1) * quarter)
            parts.append((w_up.at[layer, :, at], wup.at[layer, :, span]))
            parts.append((w_down.at[layer, at, :], wdown.at[layer, span, :]))
        loads.append([
            pltpu.make_async_copy(source, target, load_sem.at[layer, at])
            for at, (source, target) in enumerate(parts)
        ])
    for copy in loads[0]:
        copy.start()

    sources = [geo.origin(turn, who) for turn in range(held) for who in range(CORES)]
    goals = [geo.goal(turn) for turn in range(held)]
    goals = goals + [(device[0] + 1 - 2 * (device[0] % CORES), device[1]) for device in goals]
    near = [sibling] + [geo.on_line(shift) for shift in range(1, lines)]
    meet(geo, near + sources + goals)

    first = kept[0]["xall"]

    def block_at(turn, who, shift=0):
        start = shift * rows + turn * tile + who * slots
        return pl.ds(start if isinstance(start, int) else pl.multiple_of(start, slots), slots)

    def token_copies(turn, who):
        mine = tokens.at[(geo.post + turn) % held]
        place = first.at[block_at(turn, who)]
        own = pltpu.make_async_copy(mine, place, tok_sem.at[turn])
        return own, remote(mine, place, tok_send.at[turn], tok_recv.at[turn], geo.goal(turn))

    def token_start(turn):
        own, there = token_copies(turn, geo.post // held)
        pl.when(geo.blocked(turn))(own.start)
        pl.when(jnp.logical_not(geo.blocked(turn)))(there.start)

    def token_wait(turn):
        own, there = token_copies(turn, core)
        pl.when(geo.blocked(turn))(own.wait)
        pl.when(jnp.logical_not(geo.blocked(turn)))(there.wait)

    def to_sibling(array, turn, who, shift, send, receive):
        place = array.at[block_at(turn, who, shift)]
        return remote(place, place, send, receive, sibling)

    def to_line(layer, turn, shift):
        array = kept[layer]["xall"]
        source = array.at[block_at(turn, core)]
        target = array.at[block_at(turn, core, shift)]
        return remote(
            source, target, line_send.at[layer, turn, shift - 1], line_recv.at[layer, turn, shift - 1],
            geo.on_line(shift),
        )

    for turn in range(held):
        token_start(turn)
    clip_row = lax.broadcasted_iota(jnp.int32, lens.shape, 0)
    filled = jnp.full(lens.shape, lengths[0], jnp.int32)
    for clip in range(1, held):
        filled = jnp.where(clip_row == clip, lengths[clip], filled)
    lens[...] = filled
    len_copy = remote(lens, lens_there, len_sem.at[0], len_sem.at[1], sibling)
    len_copy.start()

    def clear(at):
        qx[at] = jnp.zeros(qx.shape[1:], b16)
        qx[at, LANES : LANES + 16, :] = (
            lax.broadcasted_iota(jnp.int32, (16, rows), 0) == 0
        ).astype(f32).astype(b16)

    loop(geo.heads, clear)
    len_copy.wait()
    known = jnp.where(geo.post // held == core, lens[...], lens_there[...])
    length = known[0:1, :]
    for clip in range(1, held):
        length = jnp.where(geo.parity == clip, known[clip : clip + 1, :], length)
    lane = lax.broadcasted_iota(jnp.int32, (slots, LANES), 1)
    slot = lax.broadcasted_iota(jnp.int32, (slots, LANES), 0)
    for shift in range(lines):
        for turn in range(held):
            for who in range(CORES):
                post = held * who + (geo.parity + turn) % held
                line = (geo.line + lines - shift) % lines
                outside = (post * lines + line) * slots + slot >= length
                mask = jnp.where(jnp.logical_and(lane == 0, outside), -1e30, 0.0)
                mask = jnp.where(jnp.logical_and(lane > 0, lane < 4), 1.0, mask).astype(b16)
                for layer in range(layers):
                    for pair in range(pairs):
                        kept[layer]["kx"][pair, block_at(turn, who, shift), LANES:] = mask

    for turn in range(held):
        token_wait(turn)
        to_sibling(first, turn, core, 0, sib_send.at[turn], sib_recv.at[turn]).start()
        for shift in range(1, lines):
            to_line(0, turn, shift).start()
    for copy in loads[0]:
        copy.wait()
    for copy in loads[1]:
        copy.start()

    def cot_copies(turn, flip):
        mine = cotangent.at[(geo.post + turn) % held]
        place = cot_rows.at[block_at(turn, geo.post // held)]
        goal = geo.goal(turn)
        if flip:
            goal = (goal[0] + 1 - 2 * (goal[0] % CORES), goal[1])
        own = pltpu.make_async_copy(mine, place, cot_sem.at[turn, flip])
        there = remote(
            mine, place, cot_send.at[turn, flip], cot_recv.at[turn, geo.post // held], goal
        )
        here = jnp.logical_and(goal[0] == geo.clip, goal[1] == geo.seq)
        return own, there, here

    def cot_start():
        for turn in range(held):
            for flip in range(CORES):
                own, there, here = cot_copies(turn, flip)
                pl.when(here)(own.start)
                pl.when(jnp.logical_not(here))(there.start)

    def cot_wait():
        for turn in range(held):
            for flip in range(CORES):
                own, there, here = cot_copies(turn, flip)
                pl.when(here)(own.wait)
                pl.when(jnp.logical_not(here))(there.wait_send)
            for who in range(CORES):
                source = geo.origin(turn, who)
                place = cot_rows.at[block_at(turn, who)]
                there = remote(
                    cotangent.at[0], place, cot_send.at[turn, 0], cot_recv.at[turn, who], source
                )
                here = jnp.logical_and(source[0] == geo.clip, source[1] == geo.seq)
                pl.when(jnp.logical_not(here))(there.wait_recv)

    def key_tile(layer, at):
        keep = kept[layer]
        now = pl.ds(pl.multiple_of(at, tile), tile)
        both = dot(keep["xall"][now, :], wkv[layer])
        key = both[:, :half].astype(b16)
        for pair in range(pairs):
            keep["kx"][pair, now, :LANES] = key[:, pair * LANES : (pair + 1) * LANES]
        bias = in_bias[layer : layer + 1, pl.ds(pl.multiple_of(width + core * half, half), half)]
        value = (both[:, half:] + bias).astype(b16)
        keep["v"][now, :] = value
        vt[:, now] = value.astype(f32).T.astype(b16)

    def query_tile(layer, at):
        keep = kept[layer]
        now = pl.ds(pl.multiple_of(at, tile), tile)
        bias = in_bias[layer : layer + 1, pl.ds(pl.multiple_of(core * half, half), half)]
        query = (dot(keep["xall"][now, :], wq[layer]) + bias).astype(b16)
        query = (query * SCALE).astype(b16)
        keep["q"][now, :] = query
        turned = (query.astype(f32) * LOG2E).T.astype(b16)
        for head in range(geo.heads):
            inside = head % 2 * HEAD_DIM
            qx[head, inside : inside + HEAD_DIM, now] = (
                turned[head * HEAD_DIM : (head + 1) * HEAD_DIM]
            )

    def attend_block(layer, shift):
        keep = kept[layer]
        span = slice(shift * rows, (shift + 1) * rows)

        size = min(256, rows)
        cuts = [slice(start, start + size) for start in range(shift * rows, (shift + 1) * rows, size)]

        def pair_step(pair):
            heads = [2 * pair, 2 * pair + 1]
            scores = [
                [dot(keep["kx"][pair, cut, :], qx[head]) for cut in cuts] for head in heads
            ]
            for head, pieces in zip(heads, scores):
                here = pl.ds(pl.multiple_of(head * HEAD_DIM, HEAD_DIM), HEAD_DIM)
                top = functools.reduce(
                    jnp.maximum, [jnp.max(piece, 0, keepdims=True) for piece in pieces]
                )
                if shift > 0:
                    before = keep["lse"][head, 0:1, :]
                    top = jnp.maximum(top, before)
                    shrink = jnp.exp2(before - top)
                total = attended = None
                for piece, cut in zip(pieces, cuts):
                    weights = jnp.exp2(piece - top)
                    sums = jnp.sum(weights, 0, keepdims=True)
                    values = dot(vt[here, cut], weights.astype(b16))
                    total = sums if total is None else total + sums
                    attended = values if attended is None else attended + values
                if shift > 0:
                    total = total + shrink * running[head, 0:1, :]
                    attended = attended + shrink * keep["ot"][here, :]
                if shift < lines - 1:
                    running[head, 0:1, :] = total
                    keep["ot"][here, :] = attended
                    keep["lse"][head, 0:1, :] = top
                else:
                    keep["ot"][here, :] = attended / total
                    keep["lse"][head, 0:1, :] = top + jnp.log(total) * LOG2E

        loop(pairs, pair_step)

    def project_tile(layer, turn):
        keep = kept[layer]
        now = pl.ds(pl.multiple_of(turn * tile, tile), tile)
        attended = keep["ot"][:, now].T.astype(b16)
        keep["o"][now, :] = attended
        share(2 * layer, turn, dot(attended, wout[layer]))

    def part_copy(which, turn):
        now = pl.ds(pl.multiple_of(turn * tile, tile), tile)
        return remote(
            psend.at[which, now, :], precv.at[which, now, :], part_send.at[which, turn],
            part_recv.at[which, turn], sibling,
        )

    def share(which, turn, part):
        now = pl.ds(pl.multiple_of(turn * tile, tile), tile)
        psend[which, now, :] = part.astype(b16)
        part_copy(which, turn).start()

    def collect(which, turn):
        now = pl.ds(pl.multiple_of(turn * tile, tile), tile)
        part_copy(which, turn).wait()
        return psend[which, now, :].astype(f32) + precv[which, now, :].astype(f32)

    def feed_tile(layer, turn):
        keep = kept[layer]
        now = pl.ds(pl.multiple_of(turn * tile, tile), tile)
        x = first[now, :].astype(f32) if layer == 0 else state[now, :]
        summed = x + collect(2 * layer, turn) + out_bias[layer : layer + 1, :]
        keep["z1"][now, :] = summed
        unit, unused = norm_parts(summed)
        normal = unit * gains[layer, 0:1, :] + shifts[layer, 0:1, :]
        hidden[now, :] = normal
        low = normal.astype(b16)
        keep["hrt"][:, now] = low.astype(f32).T.astype(b16)
        size = min(256, quarter)
        for at in range(0, 2 * quarter, size):
            block, start = at // quarter, at % quarter
            bias = up_bias[
                layer : layer + 1,
                pl.ds(pl.multiple_of((2 * block + core) * quarter + start, size), size),
            ]
            inner = dot(low, wup[layer, :, at : at + size]) + bias
            phi, slope = gelu_parts(inner)
            keep["act"][now, at : at + size] = (inner * phi).astype(b16)
            keep["slope"][now, at : at + size] = slope.astype(b16)
        total = dot(keep["act"][now, :], wdown[layer])
        share(2 * layer + 1, turn, total)

    def norm_tile(layer, turn):
        keep = kept[layer]
        now = pl.ds(pl.multiple_of(turn * tile, tile), tile)
        summed = hidden[now, :] + collect(2 * layer + 1, turn) + down_bias[layer : layer + 1, :]
        keep["z2"][now, :] = summed
        if layer < layers - 1:
            unit, unused = norm_parts(summed)
            result = unit * gains[layer, 1:2, :] + shifts[layer, 1:2, :]
            state[now, :] = result
            kept[layer + 1]["xall"][now, :] = result.astype(b16)

    saves = []

    def save(layer, names):
        for name in names:
            copy = pltpu.make_async_copy(
                kept[layer][name], stored[layer][name], save_sem.at[layer, KEPT.index(name)]
            )
            copy.start()
            saves.append(copy)

    for layer in range(layers):
        x_all = kept[layer]["xall"]
        if layer == 0:
            for turn in range(held):
                to_sibling(x_all, turn, core, 0, sib_send.at[turn], sib_recv.at[turn]).wait_send()
                to_sibling(x_all, turn, 1 - core, 0, sib_send.at[turn], sib_recv.at[turn]).wait_recv()
                key_tile(layer, turn * tile)
                query_tile(layer, turn * tile)
        for shift in range(lines):
            if shift > 0:
                for turn in range(held):
                    to_line(layer, turn, shift).wait()
                    to_sibling(
                        x_all, turn, core, shift,
                        pass_send.at[layer, turn, shift - 1], pass_recv.at[layer, turn, shift - 1],
                    ).start()
                for turn in range(held):
                    send = pass_send.at[layer, turn, shift - 1]
                    receive = pass_recv.at[layer, turn, shift - 1]
                    to_sibling(x_all, turn, core, shift, send, receive).wait_send()
                    to_sibling(x_all, turn, 1 - core, shift, send, receive).wait_recv()
                    key_tile(layer, shift * rows + turn * tile)
            if shift == lines - 1:
                save(layer, ("xall", "kx", "v", "q"))
                if layer == 0:
                    cot_start()

            attend_block(layer, shift)
        loop(held, functools.partial(project_tile, layer))
        save(layer, ("ot", "lse", "o"))
        loop(held, functools.partial(feed_tile, layer))
        save(layer, ("z1", "hrt", "act", "slope"))
        for turn in range(held):
            norm_tile(layer, turn)
            if layer < layers - 1:
                for shift in range(1, lines):
                    to_line(layer + 1, turn, shift).start()
                if turn == 0:
                    for copy in loads[layer + 1]:
                        copy.wait()
                key_tile(layer + 1, turn * tile)
                query_tile(layer + 1, turn * tile)
        save(layer, ("z2",))

    cot_wait()
    for copy in saves:
        copy.wait()


def forward(geo, layers, tokens, cotangent, lengths, weights, vectors):
    width, rows, half, ffn = geo.width, geo.rows, geo.half, geo.ffn
    shapes = kept_shapes(geo)
    any_spec = pl.BlockSpec(memory_space=pl.ANY)
    vmem_spec = pl.BlockSpec(memory_space=pltpu.VMEM)
    out_shape = [
        jax.ShapeDtypeStruct((rows, width), b16),
    ]
    out_shape += [jax.ShapeDtypeStruct(*shapes[name]) for unused in range(layers) for name in KEPT]
    scratch = [pltpu.VMEM(*shapes[name]) for unused in range(layers) for name in KEPT]
    scratch += [
        pltpu.VMEM((layers, width, half), b16),
        pltpu.VMEM((layers, width, 2 * half), b16),
        pltpu.VMEM((layers, half, width), b16),
        pltpu.VMEM((layers, width, 2 * geo.quarter), b16),
        pltpu.VMEM((layers, 2 * geo.quarter, width), b16),
        pltpu.VMEM((geo.heads, 2 * LANES, rows), b16),
        pltpu.VMEM((half, geo.count), b16),
        pltpu.VMEM((rows, width), f32),
        pltpu.VMEM((rows, width), f32),
        pltpu.VMEM((8, LANES), jnp.int32),
        pltpu.VMEM((8, LANES), jnp.int32),
        pltpu.VMEM((2 * layers, rows, width), b16),
        pltpu.VMEM((2 * layers, rows, width), b16),
        pltpu.VMEM((geo.heads, 8, rows), f32),
    ]
    held, lines = geo.held, max(geo.lines - 1, 1)
    dma = pltpu.SemaphoreType.DMA
    scratch += [dma(shape) for shape in (
        (layers, 8), (layers, len(KEPT)), (held,), (held,), (held,),
        (held, CORES), (held, CORES), (held, CORES), (held,), (held,),
        (layers, held, lines), (layers, held, lines), (layers, held, lines), (layers, held, lines),
        (2 * layers, held), (2 * layers, held), (2,),
    )]
    results = pl.pallas_call(
        functools.partial(forward_kernel, geo, layers),
        out_shape=out_shape,
        in_specs=[any_spec] * 6 + [pl.BlockSpec(memory_space=pltpu.SMEM)] + [vmem_spec] * 6,
        out_specs=[any_spec] * len(out_shape),
        scratch_shapes=scratch,
        compiler_params=pltpu.CompilerParams(
            collective_id=0, has_side_effects=True, vmem_limit_bytes=VMEM
        ),
        cost_estimate=pl.CostEstimate(flops=3 * 10**10, bytes_accessed=4 * 10**7, transcendentals=0),
    )(tokens, cotangent, *weights, lengths, *vectors)
    count = len(KEPT)
    kept = [
        dict(zip(KEPT, results[1 + layer * count : 1 + (layer + 1) * count]))
        for layer in range(layers)
    ]
    return results[0], kept


QUERY_BIAS, VALUE_BIAS, UP_BIAS, OUT_BIAS, DOWN_BIAS, GAIN, SHIFT = 0, 1, 2, 6, 7, 8, 10
SUMS = 16
UP, DOWN = 0, 1
INTO, PROJ = 0, 1
PAIRS = ("pair0", "pair1", "pair2")
UP_AFTER = (1, 1)


def backward_kernel(geo, layers, *refs):
    refs = list(refs)

    def take(count):
        taken = refs[:count]
        del refs[:count]
        return taken

    cot_rows, w_in, w_out, w_up, w_down = take(5)
    stored = [dict(zip(KEPT, take(len(KEPT)))) for unused in range(layers)]
    gains, shifts = take(2)
    out_tokens, grad_tokens, sums = take(3)
    if geo.aligned:
        feed_out, attend_out = take(2)
    else:
        plain = [take(6) for unused in range(layers)]
    keep = dict(zip(KEPT, take(len(KEPT))))
    wq, wkv, wout, wup, wdown = take(5)
    (o_there, low_grad, turned, du_there, psend, precv, do, qx, dox, dq, dkv, dq_there,
     dkv_there, probs_all, grads_all, do_stack, q_stack, dqt, mine_dx, dx_recv, line_in) = take(21)
    out_low = mine_dx
    (load_sem, o_send, o_recv, du_send, du_recv, part_send, part_recv, qkv_send, qkv_recv,
     dx_ssem, dx_rsem, line_send, line_recv, more_send, more_recv, tok_sem, tok_send,
     tok_recv, plain_sem, out_sem, out_send, out_recv) = take(22)
    if geo.aligned:
        (other, mine, from_x, y_first, y_last, z_first, z_last, into_cell, proj_cell, into_y, proj_y, into_z, proj_z,
         a_send, a_x, sum_in) = take(16)
        from_y, from_z = (y_first, y_last), (z_first, z_last)
        cells = [[into_cell] * layers, [proj_cell.at[layer] for layer in range(layers)]]
        cells_z = (into_z, proj_z)
        (fx_send, fx_recv, fy_send, fy_recv, fz_send, fz_recv, ay_send, ay_recv, az_send, az_recv,
         ax_send, ax_recv, sum_send, sum_recv) = take(14)
        credit, into_credit = take(2)

    geo = duplicate(geo)
    geo.locate()
    core, tile, slots = geo.core, geo.tile, geo.slots
    held, lines, rows, width, half = geo.held, geo.lines, geo.rows, geo.width, geo.half
    quarter, pairs, posts, depth = geo.quarter, geo.pairs, geo.posts, geo.depth
    post, line, column = geo.post, geo.line, geo.column
    unit = width // geo.seq_size
    sibling = geo.sibling()

    def tile_at(turn):
        return pl.ds(pl.multiple_of(turn * tile, tile), tile)

    def block_at(turn, who, shift=0):
        start = shift * rows + turn * tile + who * slots
        return pl.ds(start if isinstance(start, int) else pl.multiple_of(start, slots), slots)

    NAMES = KEPT + ("win", "wout", "wup", "wdown", "cot")

    def load_copies(layer, name):
        where = load_sem.at[layer, NAMES.index(name)]
        if name == "win":
            targets = (wq, wkv.at[:, :half], wkv.at[:, half:])
            return [
                pltpu.make_async_copy(
                    w_in.at[layer, :, pl.ds(pl.multiple_of((kind * CORES + core) * half, half), half)],
                    targets[kind], load_sem.at[layer, len(NAMES) + kind],
                )
                for kind in range(3)
            ]
        if name == "wout":
            at = pl.ds(pl.multiple_of(core * half, half), half)
            return [pltpu.make_async_copy(w_out.at[layer, at, :], wout, where)]
        if name in ("wup", "wdown"):
            copies = []
            for block in range(2):
                at = pl.ds(pl.multiple_of((2 * block + core) * quarter, quarter), quarter)
                slot = len(NAMES) + 3 + 2 * (name == "wdown") + block
                if name == "wup":
                    pair = w_up.at[layer, :, at], wup.at[:, block * quarter : (block + 1) * quarter]
                else:
                    pair = w_down.at[layer, at, :], wdown.at[block * quarter : (block + 1) * quarter, :]
                copies.append(pltpu.make_async_copy(*pair, load_sem.at[layer, slot]))
            return copies
        if name == "hrt" and geo.aligned:
            return [
                pltpu.make_async_copy(
                    stored[layer][name].at[pl.ds(pl.multiple_of((2 * which + core) * depth, depth), depth), :],
                    keep[name].at[which * depth : (which + 1) * depth, :],
                    load_sem.at[layer, len(NAMES) + 7 + which],
                )
                for which in range(2)
            ]
        if name == "cot":
            return [pltpu.make_async_copy(cot_rows, low_grad, where)]
        return [pltpu.make_async_copy(stored[layer][name], keep[name], where)]

    def load(layer, *names):
        for name in names:
            for copy in load_copies(layer, name):
                copy.start()

    def loaded(layer, *names):
        for name in names:
            for copy in load_copies(layer, name):
                copy.wait()

    top = layers - 1
    load(top, "z2", "cot", "wdown", "slope", "wup", "act", "z1", "wout", "q", "kx", "v", "ot",
         "lse", "win", "hrt", "xall", "o")

    sources = [geo.origin(turn, who) for turn in range(held) for who in range(CORES)]
    goals = [geo.goal(turn) for turn in range(held)]
    near = [sibling] + [geo.on_line(shift) for shift in range(1, lines)]
    if geo.aligned:
        near += [geo.on_post(shift) for shift in range(1, posts)]
        near += [geo.on_column(shift) for shift in range(1, geo.columns)]
    goals = goals + [(device[0] + 1 - 2 * (device[0] % CORES), device[1]) for device in goals]
    meet(geo, near + sources + goals)

    def o_copy(layer):
        return remote(stored[layer]["o"], o_there, o_send.at[layer], o_recv.at[layer], sibling)

    def clear(at):
        qx[at] = jnp.zeros(qx.shape[1:], b16)
        dox[at] = jnp.zeros(dox.shape[1:], b16)

    loop(2, clear)
    sums[...] = jnp.zeros_like(sums)

    def add_sum(layer, row, lanes, value):
        sums[layer, pl.ds(row, 1), lanes] += value

    everywhere = slice(None)


    def x_copy(layer, kind, z):
        return remote(
            other.at[kind, z], from_x.at[kind, z], fx_send.at[layer, kind, z],
            fx_recv.at[layer, kind, z], geo.on_column(1),
        )

    pair_post = post + 1 - 2 * (post % 2)
    far_post = (post + 2) % posts

    landed = {}

    def all_landed(hop, kind):
        landed[hop, kind] = landed.get((hop, kind), 0) + 1
        return landed[hop, kind] == posts

    def order(step):
        return (pair_post + step // 2 * (far_post - pair_post) + step % 2 * 2) % posts

    def at_post(which):
        return geo.clip, which * lines + line

    def y_copy(layer, kind, z, shift):
        there = from_y[layer].at[kind, shift - 1] if layer else from_y[layer].at[kind, z, shift - 1]
        at = 0 if layer else z
        return remote(
            mine.at[layer, kind, z, (line + shift) % lines], there,
            fy_send.at[layer, kind, at, shift - 1], fy_recv.at[layer, kind, at, shift - 1],
            geo.on_line(shift),
        )

    def z_copy(layer, kind, hop):
        block = mine.at[layer, kind, order(hop)]
        return remote(
            block if layer else block.at[line], from_z[layer].at[kind, hop],
            fz_send.at[layer, kind, hop], fz_recv.at[layer, kind, hop],
            at_post(far_post if hop == 2 else pair_post),
        )

    def land_x(layer, kind, step):
        z = order(step)
        x_copy(layer, kind, z).wait()
        total = mine[layer, kind, z].astype(f32) + from_x[kind, z].astype(f32)
        mine[layer, kind, z] = total.astype(b16)
        if layer == 0:
            for shift in range(1, lines):
                y_copy(layer, kind, z, shift).start()
            return
        if step < 2:
            z_copy(layer, kind, step).start()
        if all_landed("x", kind):
            device = geo.on_column(1)
            pl.semaphore_signal(
                credit.at[kind], inc=1, device_id=device, device_id_type=pl.DeviceIdType.MESH
            )

    def land_y(layer, kind, step):
        z = order(step)
        total = mine[layer, kind, z, line].astype(f32)
        for shift in range(1, lines):
            y_copy(layer, kind, z, shift).wait()
            total = total + from_y[layer][kind, z, shift - 1].astype(f32)
        mine[layer, kind, z, line] = total.astype(b16)
        if step < 2:
            z_copy(layer, kind, step).start()

    def land_near(layer, kind):
        z_copy(layer, kind, 1).wait()
        here = (layer, kind, far_post) if layer else (layer, kind, far_post, line)
        total = mine[here].astype(f32) + from_z[layer][kind, 1].astype(f32)
        mine[here] = total.astype(b16)
        z_copy(layer, kind, 2).start()

    def land_far(layer, kind):
        here = (layer, kind, post) if layer else (layer, kind, post, line)
        total = mine[here].astype(f32)
        for hop in (0, 2):
            z_copy(layer, kind, hop).wait()
            total = total + from_z[layer][kind, hop].astype(f32)
        if layer == 0:
            feed_out[layer, kind] = total
            return
        mine[here] = total.astype(b16)
        for shift in range(1, lines):
            y_copy(layer, kind, post, shift).start()

    def land_end(layer, kind):
        total = mine[layer, kind, post, line].astype(f32)
        for shift in range(1, lines):
            y_copy(layer, kind, post, shift).wait()
            total = total + from_y[layer][kind, shift - 1].astype(f32)
        feed_out[layer, kind] = total

    def landing(layer, kind, z, shift):
        if kind == INTO:
            return into_y.at[z, shift - 1]
        return proj_y.at[layer, z, shift - 1]

    def ay_copy(layer, kind, z, shift):
        return remote(
            cells[kind][layer].at[(line + shift) % lines, z], landing(layer, kind, z, shift),
            ay_send.at[layer, kind, z, shift - 1], ay_recv.at[layer, kind, z, shift - 1],
            geo.on_line(shift),
        )

    def az_copy(layer, kind, hop):
        return remote(
            cells[kind][layer].at[line, order(hop)], cells_z[kind].at[layer, hop],
            az_send.at[layer, kind, hop], az_recv.at[layer, kind, hop],
            at_post(far_post if hop == 2 else pair_post),
        )

    def ax_copy(layer, kind):
        span = slice(0, 3 * unit) if kind == INTO else slice(3 * unit, 4 * unit)
        return remote(
            a_send.at[layer, span], a_x.at[layer, span], ax_send.at[layer, kind],
            ax_recv.at[layer, kind], geo.on_column(1),
        )

    def send_ay(layer, kind):
        if layer < top and kind == INTO:
            pl.semaphore_wait(into_credit, lines - 1)
        for step in range(posts):
            for shift in range(1, lines):
                ay_copy(layer, kind, order(step), shift).start()

    def land_ay(layer, kind, step):
        z = order(step)
        cell = cells[kind][layer]
        total = cell[line, z].astype(f32)
        for shift in range(1, lines):
            ay_copy(layer, kind, z, shift).wait()
            total = total + landing(layer, kind, z, shift)[...].astype(f32)
        cell[line, z] = total.astype(b16)
        if step < 2:
            az_copy(layer, kind, step).start()

        if layer > 0 and kind == INTO and all_landed("into", kind):
            for shift in range(1, lines):
                pl.semaphore_signal(
                    into_credit, inc=1, device_id=geo.on_line(shift),
                    device_id_type=pl.DeviceIdType.MESH,
                )

    def land_anear(layer, kind):
        cell = cells[kind][layer]
        az_copy(layer, kind, 1).wait()
        total = cell[line, far_post].astype(f32) + cells_z[kind][layer, 1].astype(f32)
        cell[line, far_post] = total.astype(b16)
        az_copy(layer, kind, 2).start()

    def land_afar(layer, kind):
        total = cells[kind][layer][line, post].astype(f32)
        for hop in (0, 2):
            az_copy(layer, kind, hop).wait()
            total = total + cells_z[kind][layer, hop].astype(f32)
        low, high = total[:, :depth], total[:, depth:]
        span = slice(0, 3 * unit) if kind == INTO else slice(3 * unit, 4 * unit)
        attend_out[layer, span] = jnp.where(column == 0, low, high)
        a_send[layer, span] = jnp.where(column == 0, high, low).astype(b16)
        ax_copy(layer, kind).start()

    def land_ax(layer, kind):
        ax_copy(layer, kind).wait()
        span = slice(0, 3 * unit) if kind == INTO else slice(3 * unit, 4 * unit)
        attend_out[layer, span] = attend_out[layer, span] + a_x[layer, span].astype(f32)

    def sum_copies(layer, hop):
        near = ([sibling], [geo.on_line(shift) for shift in range(1, lines)],
                [at_post(pair_post)], [at_post(far_post)], [geo.on_column(1)])
        first = (0, 1, lines, lines + 1, lines + 2)[hop]
        return [
            (remote(
                sums.at[layer], sum_in.at[layer, first + at], sum_send.at[layer, first + at],
                sum_recv.at[layer, first + at], device,
            ), first + at)
            for at, device in enumerate(near[hop])
        ]

    def start_sum(layer):
        shared = lax.broadcasted_iota(jnp.int32, sums.shape[1:], 0) >= OUT_BIAS
        sums[layer] = jnp.where(shared, 0.5 * sums[layer], sums[layer])
        for copy, unused in sum_copies(layer, 0):
            copy.start()

    def land_sum(layer, hop):
        total = sums[layer]
        for copy, at in sum_copies(layer, hop):
            copy.wait()
            total = total + sum_in[layer, at]
        sums[layer] = total
        if hop < 4:
            for copy, unused in sum_copies(layer, hop + 1):
                copy.start()

    schedule = {
        (1, "up"): (
            (land_x, 1, DOWN, 1),
        ),
        (1, "dx"): (
            (land_x, 1, DOWN, 2), (land_ay, 1, PROJ, 1), (land_x, 1, DOWN, 0),
            (land_ay, 1, PROJ, 0),
        ),
        (1, "own"): (
            (land_near, 1, DOWN), (land_x, 1, DOWN, 3),
        ),
        (1, "into"): (
            (land_ay, 1, PROJ, 2), (land_anear, 1, PROJ), (land_x, 1, UP, 0),
        ),
        (0, "feed"): (
            (land_ay, 1, INTO, 0), (land_ay, 1, INTO, 1), (land_far, 1, DOWN),
        ),
        (0, "down"): (
            (land_x, 1, UP, 1),
        ),
        (0, "up"): (
            (land_x, 0, DOWN, 0), (land_near, 1, UP), (land_x, 0, DOWN, 1),
        ),
        (0, "pair0"): (
            (land_ay, 1, INTO, 2), (land_x, 1, UP, 3), (land_anear, 1, INTO),
        ),
        (0, "pair1"): (
            (land_x, 1, UP, 2),
        ),
        (0, "dx"): (
            (land_ay, 1, INTO, 3), (land_sum, 1, 0), (land_ay, 0, PROJ, 3), (land_afar, 1, INTO),
            (land_ay, 0, PROJ, 1), (land_x, 0, DOWN, 2), (land_y, 0, DOWN, 1),
            (land_y, 0, DOWN, 0), (land_ay, 0, PROJ, 2),
        ),
        (0, "into"): (
            (land_sum, 1, 1),
        ),
        (0, "own"): (
            (land_anear, 0, PROJ),
        ),
        (0, "end"): (
            (land_y, 0, DOWN, 2), (land_sum, 1, 2), (land_near, 0, DOWN), (land_ay, 0, INTO, 1),
            (land_sum, 0, 0), (land_x, 0, UP, 1), (land_ay, 0, INTO, 0), (land_ay, 0, INTO, 2),
            (land_x, 0, UP, 3), (land_anear, 0, INTO), (land_ay, 1, PROJ, 3), (land_sum, 1, 3),
            (land_sum, 0, 1), (land_sum, 1, 4), (land_y, 0, UP, 1), (land_x, 0, UP, 2),
            (land_afar, 1, PROJ), (land_ax, 1, INTO), (land_x, 0, UP, 0), (land_x, 0, DOWN, 3),
            (land_ay, 0, INTO, 3), (land_sum, 0, 2), (land_far, 1, UP), (land_ay, 0, PROJ, 0),
            (land_y, 0, UP, 2), (land_afar, 0, INTO), (land_near, 0, UP), (land_y, 0, UP, 0),
            (land_ax, 1, PROJ), (land_afar, 0, PROJ), (land_y, 0, UP, 3), (land_sum, 0, 3),
            (land_end, 1, DOWN), (land_ax, 0, PROJ), (land_y, 0, DOWN, 3), (land_far, 0, DOWN),
            (land_ax, 0, INTO), (land_end, 1, UP), (land_sum, 0, 4), (land_far, 0, UP),
        ),
    }

    def progress(layer, phase):
        if geo.aligned:
            for function, *given in schedule.get((layer, phase), ()):
                function(*given)


    def part_copy(layer, turn):
        return remote(
            psend.at[tile_at(turn), :], precv.at[tile_at(turn), :], part_send.at[layer, turn],
            part_recv.at[layer, turn], sibling,
        )

    def du_copy(layer, turn):
        return remote(
            keep["slope"].at[tile_at(turn), :], du_there.at[tile_at(turn), :],
            du_send.at[layer, turn], du_recv.at[layer, turn], sibling,
        )

    def out_copies(turn, place):
        own = pltpu.make_async_copy(out_low.at[turn], place, out_sem.at[turn])
        there = remote(
            out_low.at[turn], place, out_send.at[turn], out_recv.at[turn], geo.origin(turn, core)
        )
        return own, there

    def send_home(copies, turn, target):
        own, there = copies(turn, target.at[geo.parity])
        pl.when(geo.blocked(turn))(own.start)
        pl.when(jnp.logical_not(geo.blocked(turn)))(there.start)

    def wait_home(copies, turn, target):
        own, there = copies(turn, target.at[(post + turn) % held])
        pl.when(geo.blocked(turn))(own.wait)
        pl.when(jnp.logical_not(geo.blocked(turn)))(there.wait)

    def norm_grads(layer, which, values, grad, turn):
        unit, inverse = norm_parts(values)
        gain = gains[layer, which : which + 1, :]
        if layer == top and which == 1:
            result = unit * gain + shifts[layer, which : which + 1, :]
            out_low[turn] = jnp.where(core == 0, result[:slots], result[slots:]).astype(b16)
            send_home(out_copies, turn, out_tokens)
        back, gain_grad, shift_grad = norm_back(unit, inverse, gain, grad)
        add_sum(layer, GAIN + which, everywhere, gain_grad)
        add_sum(layer, SHIFT + which, everywhere, shift_grad)
        return back

    def feed_back_tile(layer, turn):
        now = tile_at(turn)
        grad = low_grad[now, :].astype(f32)
        if layer < top:
            grad = grad + keep["z1"][now, :]
        back = norm_grads(layer, 1, keep["z2"][now, :], grad, turn)
        keep["z2"][now, :] = back
        low = back.astype(b16)
        wide = low.astype(f32)
        turned[:, now] = wide.T.astype(b16)
        add_sum(layer, DOWN_BIAS, everywhere, jnp.sum(wide, 0, keepdims=True))
        size = min(256, quarter)
        for at in range(0, 2 * quarter, size):
            block, start = at // quarter, at % quarter
            lanes = slice(at, at + size)
            grads = dot_nt(low, wdown[lanes, :])
            grads = (grads * keep["slope"][now, lanes].astype(f32)).astype(b16)
            keep["slope"][now, lanes] = grads
            add_sum(
                layer, UP_BIAS + 2 * block + core, slice(start, start + size),
                jnp.sum(grads.astype(f32), 0, keepdims=True),
            )
        total = dot_nt(keep["slope"][now, :], wup[...])
        psend[now, :] = total.astype(b16)
        part_copy(layer, turn).start()
        du_copy(layer, turn).start()

    def down_grads(layer, which, start):
        lanes = pl.ds(pl.multiple_of(which * quarter, quarter), quarter)
        size = lines * unit

        def chunk(at):
            steps = (2 * at, 2 * at + 1)
            left = [
                turned[pl.ds(pl.multiple_of(order(step) * size, size), size), :] for step in steps
            ]
            result = dot(jnp.concatenate(left, 0), keep["act"][:, lanes]).astype(b16)
            for index, step in enumerate(steps):
                z = order(step)
                for row in range(lines):
                    top = index * size + row * unit
                    for piece in range(2):
                        block = result[
                            top : top + unit, piece * quarter // 2 : (piece + 1) * quarter // 2
                        ]
                        span = slice(piece * unit, (piece + 1) * unit)
                        if start:
                            other[DOWN, z, row, span, :] = block
                        else:
                            mine[layer, DOWN, z, row, span, :] = block
                if start:
                    x_copy(layer, DOWN, z).start()

        loop(posts // 2, chunk)

    def up_grads(layer):
        left = [
            keep["hrt"][pl.ds(pl.multiple_of(which * depth, depth), depth), :]
            for which in (1 - column, column)
        ]
        left = jnp.concatenate(left, 0)
        size = quarter // lines
        for block in range(2):
            lanes = slice(block * quarter, (block + 1) * quarter)
            for there, array in ((0, keep["slope"]), (1, du_there)):
                z = 2 * block + core + there * (1 - 2 * core)
                result = dot(left, array[:, lanes]).astype(b16)
                for row in range(lines):
                    span = slice(row * size, (row + 1) * size)
                    other[UP, z, row] = result[:depth, span]
                    mine[layer, UP, z, row] = result[depth:, span]
        for step in range(posts):
            x_copy(layer, UP, order(step)).start()

    def feed_grads(layer, kind):
        if layer < top:
            pl.semaphore_wait(credit.at[kind], 1)
        if kind == UP:
            loaded(layer, "hrt")
            for turn in range(held):
                du_copy(layer, turn).wait()
            up_grads(layer)
        else:
            down_grads(layer, 1 - column, True)
            down_grads(layer, column, False)

    def proj_back_tile(layer, turn):
        now = tile_at(turn)
        part_copy(layer, turn).wait()
        grad = keep["z2"][now, :] + (psend[now, :].astype(f32) + precv[now, :].astype(f32))
        back = norm_grads(layer, 0, keep["z1"][now, :], grad, turn)
        keep["z1"][now, :] = back
        low = back.astype(b16)
        wide = low.astype(f32)
        turned[:, now] = wide.T.astype(b16)
        add_sum(layer, OUT_BIAS, everywhere, jnp.sum(wide, 0, keepdims=True))
        do[now, :] = dot_nt(low, wout[...]).astype(b16)

    lane_head = lax.broadcasted_iota(jnp.int32, (tile, LANES), 1) // HEAD_DIM

    def attend_back_pair(layer, pair):
        lanes = pl.ds(pl.multiple_of(pair * LANES, LANES), LANES)
        key_t = keep["kx"][pair, :, :LANES].astype(f32).T.astype(b16)
        query_t = (keep["q"][:, lanes].astype(f32) * LOG2E).T.astype(b16)
        grad_t = do[:, lanes].astype(f32).T.astype(b16)
        for head in range(2):
            here = slice(head * HEAD_DIM, (head + 1) * HEAD_DIM)
            qx[head, here, :] = query_t[here]
            dox[head, here, :] = grad_t[here]
            rest = -keep["lse"][2 * pair + head, 0:1, :]
            row = lax.broadcasted_iota(jnp.int32, (16, rows), 0)
            extra = jnp.where(row == 0, 1.0, 0.0)
            for part in range(1, 4):
                piece = rest.astype(b16).astype(f32)
                rest = rest - piece
                extra = jnp.where(row == part, piece, extra)
            qx[head, LANES : LANES + 16, :] = extra.astype(b16)

        def turn_step(turn):
            now = tile_at(turn)
            query = keep["q"][now, lanes].astype(f32)
            outgrad = do[now, lanes].astype(f32)
            for head in range(2):
                here = slice(head * HEAD_DIM, (head + 1) * HEAD_DIM)
                chosen = (lane_head == head).astype(f32)
                place = pl.ds(pl.multiple_of((2 * turn + head) * tile, tile), tile)
                do_stack[place, :] = (outgrad * chosen).astype(b16)
                q_stack[place, :] = (query * chosen).astype(b16)
                scores = dot(keep["kx"][pair], qx[head, :, now])
                probs = jnp.exp2(scores)
                probs_all[:, place] = probs.astype(b16)
                grads = dot(keep["v"][:, lanes], dox[head, :, now])
                own = pl.ds(pl.multiple_of(pair * LANES + head * HEAD_DIM, HEAD_DIM), HEAD_DIM)
                delta = jnp.sum(
                    dox[head, here, now].astype(f32) * keep["ot"][own, now], 0, keepdims=True
                )
                score_grads = (probs * (grads - delta)).astype(b16)
                grads_all[:, place] = score_grads
                dqt[here, now] = dot(key_t[here], score_grads)

        loop(held, turn_step)
        query_grad = (dqt[...].T * SCALE).astype(b16)
        value_grad = dot(probs_all[...], do_stack[...]).astype(b16)
        dq[:, lanes] = query_grad
        dkv[:, lanes] = dot(grads_all[...], q_stack[...]).astype(b16)
        dkv[:, pl.ds(pl.multiple_of(half + pair * LANES, LANES), LANES)] = value_grad
        spot = pl.ds(pl.multiple_of(core * half + pair * LANES, LANES), LANES)
        add_sum(layer, QUERY_BIAS, spot, jnp.sum(query_grad.astype(f32), 0, keepdims=True))
        add_sum(layer, VALUE_BIAS, spot, jnp.sum(value_grad.astype(f32), 0, keepdims=True))

    def qkv_copies(layer):
        return [
            remote(source, target, qkv_send.at[layer, at], qkv_recv.at[layer, at], sibling)
            for at, (source, target) in enumerate(((dq, dq_there), (dkv, dkv_there)))
        ]

    def dx_send(shift, turn):
        start = pl.multiple_of((shift * held + turn) * slots, slots)
        return psend.at[pl.ds(start, slots), :]

    def dx_copy(layer, shift, turn):
        return remote(
            dx_send(shift, turn), dx_recv.at[shift * held + turn],
            dx_ssem.at[layer, shift * held + turn], dx_rsem.at[layer, shift * held + turn], sibling,
        )

    def dx_tile(layer, shift, turn):
        now = pl.ds(pl.multiple_of(shift * rows + turn * tile, tile), tile)
        total = dot_nt(dkv[now, :], wkv[...])
        if shift == 0:
            total = total + dot_nt(dq[now, :], wq[...])
        first, second = total[:slots], total[slots:]
        mine_dx[shift * held + turn] = jnp.where(core == 0, first, second).astype(b16)
        dx_send(shift, turn)[...] = jnp.where(core == 0, second, first).astype(b16)
        dx_copy(layer, shift, turn).start()

    def line_copy(layer, shift, turn):
        return remote(
            dx_recv.at[shift * held + turn], line_in.at[layer, shift - 1, turn],
            line_send.at[layer, shift - 1, turn], line_recv.at[layer, shift - 1, turn],
            geo.on_line(lines - shift),
        )

    def more_copy(layer, turn, who):
        place = low_grad.at[block_at(turn, who)]
        return remote(place, place, more_send.at[layer, turn], more_recv.at[layer, turn], sibling)

    def token_copies(turn, place):
        own = pltpu.make_async_copy(low_grad.at[block_at(turn, core)], place, tok_sem.at[turn])
        there = remote(
            low_grad.at[block_at(turn, core)], place, tok_send.at[turn], tok_recv.at[turn],
            geo.origin(turn, core),
        )
        return own, there

    def mine_lanes(x):
        cuts = [x[:, at * depth : (at + 1) * depth] for at in range(2 * CORES)]
        return jnp.where(
            core == 0, jnp.concatenate([cuts[0], cuts[2]], 1), jnp.concatenate([cuts[1], cuts[3]], 1)
        )

    def into_grads(layer, there):
        units = half // unit
        x = mine_lanes(keep["xall"][...])
        owner = core + there * (1 - 2 * core)
        for first, ref in ((0, (dq, dq_there)[there]), (1, (dkv, dkv_there)[there])):
            result = dot_tn(ref[...], x[: ref.shape[0]]).astype(b16)
            for at in range(result.shape[0] // unit):
                kind = first + at // units
                index = (2 * kind + owner) * units + at % units
                seq = index // 3
                where = pl.ds(pl.multiple_of(index % 3 * unit, unit), unit)
                into_cell[seq % lines, seq // lines, where, :] = result[at * unit : (at + 1) * unit]
        if there:
            send_ay(layer, INTO)

    def own_total(layer, turn):
        dx_copy(layer, 0, turn).wait_recv()
        total = mine_dx[turn].astype(f32) + dx_recv[turn].astype(f32)
        for shift in range(1, lines):
            line_copy(layer, shift, turn).wait()
            total = total + line_in[layer, shift - 1, turn].astype(f32)
        return total

    def take_grad(layer, turn):
        low_grad[block_at(turn, core), :] = own_total(layer, turn).astype(b16)
        more_copy(layer, turn, core).start()
        more_copy(layer, turn, core).wait_send()
        more_copy(layer, turn, 1 - core).wait_recv()

    def proj_grads(layer):
        here, there = keep["o"][...], o_there[...]
        features = jnp.where(
            core == 0,
            jnp.concatenate([here[:, :depth], there[:, :depth]], 1),
            jnp.concatenate([there[:, depth:], here[:, depth:]], 1),
        )
        result = dot(turned[...], features).astype(b16)
        for seq in range(geo.seq_size):
            proj_cell[layer, seq % lines, seq // lines] = result[seq * unit : (seq + 1) * unit]
        send_ay(layer, PROJ)

    def plain_out(layer, names):
        sources = {"du": keep["slope"], "dft": turned, "dat": turned, "dq": dq, "dk": dkv.at[:, :half], "dv": dkv.at[:, half:]}
        order = ("du", "dft", "dat", "dq", "dk", "dv")
        copies = [
            pltpu.make_async_copy(sources[name], plain[layer][order.index(name)], plain_sem.at[order.index(name)])
            for name in names
        ]
        for copy in copies:
            copy.start()
        for copy in copies:
            copy.wait()

    for layer in range(layers - 1, -1, -1):
        last = layer == 0
        below = layer - 1
        if layer == top:
            loaded(layer, "cot")
        loaded(layer, "z2", "wdown", "slope", "wup")

        def feed_step(turn):
            if layer < top:
                take_grad(layer + 1, turn)
            feed_back_tile(layer, turn)

        if layer < top:
            for turn in range(held):
                dx_copy(layer + 1, 0, turn).wait_send()
        loop(held, feed_step)
        o_copy(layer).start()
        progress(layer, "feed")
        if not last:
            load(below, "wdown", "wup")
        else:
            load(layer, "z1")
        loaded(layer, "act")
        if geo.aligned:
            feed_grads(layer, DOWN)
            progress(layer, "down")
            if UP_AFTER[layer] is None:
                feed_grads(layer, UP)
                progress(layer, "up")
        else:
            plain_out(layer, ("dft",))
        if not last:
            load(below, "act")
        loaded(layer, "z1", "wout")
        loop(held, functools.partial(proj_back_tile, layer))
        progress(layer, "proj")
        if not last:
            load(below, "wout", "z2")
        if geo.aligned:
            loaded(layer, "o")
            o_copy(layer).wait()
            proj_grads(layer)
        loaded(layer, "q", "kx", "v", "ot", "lse")

        def pair_step(pair):
            attend_back_pair(layer, pair)
            for index in range(pairs if geo.aligned else 0):

                @pl.when(pair == index)
                def after_pair(index=index):
                    progress(layer, PAIRS[index])
                    if index == UP_AFTER[layer]:
                        feed_grads(layer, UP)
                        progress(layer, "up")

        loop(pairs, pair_step)
        if not last:
            load(below, "q", "kx", "v", "ot", "lse")
        for copy in qkv_copies(layer):
            copy.start()
        if geo.aligned:
            start_sum(layer)
        loaded(layer, "win")
        if layer == top:
            for turn in range(held):
                wait_home(out_copies, turn, out_tokens)
        for shift in range(1, lines):
            loop(held, functools.partial(dx_tile, layer, shift))
        progress(layer, "dx")
        if geo.aligned and last:
            loaded(layer, "xall")
            into_grads(layer, 0)
        for shift in range(1, lines):
            for turn in range(held):
                dx_copy(layer, shift, turn).wait()
                at = shift * held + turn
                dx_recv[at] = (mine_dx[at].astype(f32) + dx_recv[at].astype(f32)).astype(b16)
                line_copy(layer, shift, turn).start()

        def own_rows():
            loop(held, functools.partial(dx_tile, layer, 0))
            progress(layer, "own")

        if not last:
            own_rows()
            load(below, "win")
        if geo.aligned:
            if not last:
                loaded(layer, "xall")
                into_grads(layer, 0)
            for copy in qkv_copies(layer):
                copy.wait()
            into_grads(layer, 1)
            progress(layer, "into")
        else:
            for turn in range(held):
                du_copy(layer, turn).wait()
            for copy in qkv_copies(layer):
                copy.wait()
            loaded(layer, "hrt", "xall", "o")
            o_copy(layer).wait()
            plain_out(layer, ("du", "dat", "dq", "dk", "dv"))
        if not last:
            load(below, "hrt", "slope", "xall", "o")
        else:
            own_rows()
            for turn in range(held):
                dx_copy(layer, 0, turn).wait_send()
                total = own_total(layer, turn) + keep["z1"][block_at(turn, core), :]
                low_grad[block_at(turn, core), :] = total.astype(b16)
                send_home(token_copies, turn, grad_tokens)

    progress(0, "end")
    for turn in range(held):
        wait_home(token_copies, turn, grad_tokens)


def backward(geo, layers, cot_rows, weights, kept, gains, shifts):
    width, rows, half, ffn, count = geo.width, geo.rows, geo.half, geo.ffn, geo.count
    held, lines, posts, slots, quarter = geo.held, geo.lines, geo.posts, geo.slots, geo.quarter
    shapes = kept_shapes(geo)
    any_spec = pl.BlockSpec(memory_space=pl.ANY)
    vmem_spec = pl.BlockSpec(memory_space=pltpu.VMEM)
    unit = width // geo.seq_size
    out = [((held, slots, width), b16)] * 2 + [((layers, SUMS, width), f32)]
    out_specs = [any_spec] * 2 + [vmem_spec]
    if geo.aligned:
        out += [
            ((layers, 2, geo.depth, quarter // lines), f32),
            ((layers, 4 * unit, geo.depth), f32),
        ]
        out_specs += [vmem_spec] * 2
    else:
        for unused in range(layers):
            out += [
                ((rows, ffn // CORES), b16), ((width, rows), b16), ((width, rows), b16),
                ((rows, half), b16), ((count, half), b16), ((count, half), b16),
            ]
            out_specs += [any_spec] * 6
    vmem = pltpu.VMEM
    if geo.aligned:
        shapes["hrt"] = (2 * geo.depth, rows), b16
    scratch = [vmem(*shapes[name]) for name in KEPT]
    scratch += [
        vmem((width, half), b16), vmem((width, 2 * half), b16), vmem((half, width), b16),
        vmem((width, 2 * quarter), b16), vmem((2 * quarter, width), b16),
        vmem((rows, half), b16),
        vmem((rows, width), b16),
        vmem((width, rows), b16),
        vmem((rows, ffn // CORES), b16),
        vmem((max(rows, lines * held * slots), width), b16), vmem((rows, width), b16),
        vmem((rows, half), b16),
        vmem((2, 2 * LANES, rows), b16), vmem((2, LANES, rows), b16),
        vmem((rows, half), b16), vmem((count, 2 * half), b16),
        vmem((rows, half), b16), vmem((count, 2 * half), b16),
        vmem((count, 2 * rows), b16), vmem((count, 2 * rows), b16),
        vmem((2 * rows, LANES), b16), vmem((2 * rows, LANES), b16), vmem((LANES, rows), f32),
        vmem((lines * held, slots, width), b16), vmem((lines * held, slots, width), b16),
        vmem((layers, lines - 1, held, slots, width), b16),
    ]
    dma = pltpu.SemaphoreType.DMA
    scratch += [dma(shape) for shape in (
        (layers, len(KEPT) + 16), (layers,), (layers,), (layers, held), (layers, held),
        (layers, held), (layers, held), (layers, 3), (layers, 3),
        (layers, lines * held), (layers, lines * held),
        (layers, lines - 1, held), (layers, lines - 1, held),
        (layers, held), (layers, held), (held,), (held,), (held,), (6,),
        (held,), (held,), (held,),
    )]
    if geo.aligned:
        block = (geo.depth, quarter // lines)
        into, proj = (3 * unit, 2 * geo.depth), (unit, 2 * geo.depth)
        hops = lines + 3
        scratch += [
            vmem((2, posts, lines, *block), b16), vmem((layers, 2, posts, lines, *block), b16),
            vmem((2, posts, lines, *block), b16),
            vmem((2, posts, lines - 1, *block), b16), vmem((2, lines - 1, *block), b16),
            vmem((2, 3, *block), b16), vmem((2, 3, lines, *block), b16),
            vmem((lines, posts, *into), b16), vmem((layers, lines, posts, *proj), b16),
            vmem((posts, lines - 1, *into), b16), vmem((layers, posts, lines - 1, *proj), b16),
            vmem((layers, 3, *into), b16), vmem((layers, 3, *proj), b16),
            vmem((layers, 4 * unit, geo.depth), b16), vmem((layers, 4 * unit, geo.depth), b16),
            vmem((layers, hops, SUMS, width), f32),
        ]
        scratch += [dma(shape) for shape in (
            (layers, 2, posts), (layers, 2, posts),
            (layers, 2, posts, lines - 1), (layers, 2, posts, lines - 1),
            (layers, 2, 3), (layers, 2, 3),
            (layers, 2, posts, lines - 1), (layers, 2, posts, lines - 1),
            (layers, 2, 3), (layers, 2, 3), (layers, 2), (layers, 2),
            (layers, hops), (layers, hops),
        )]
        scratch += [pltpu.SemaphoreType.REGULAR((2,)), pltpu.SemaphoreType.REGULAR]
    stored = [kept[layer][name] for layer in range(layers) for name in KEPT]
    return pl.pallas_call(
        functools.partial(backward_kernel, geo, layers),
        out_shape=[jax.ShapeDtypeStruct(*shape) for shape in out],
        in_specs=[any_spec] * (5 + len(stored)) + [vmem_spec] * 2,
        out_specs=out_specs,
        scratch_shapes=scratch,
        compiler_params=pltpu.CompilerParams(
            collective_id=1, has_side_effects=True, vmem_limit_bytes=VMEM_BACK
        ),
        cost_estimate=pl.CostEstimate(flops=8 * 10**10, bytes_accessed=6 * 10**7, transcendentals=0),
    )(cot_rows, *weights, *stored, gains, shifts)


def finish_kernel(
    geo, core_ref, sums_ref, feed_ref, attend_ref, out_in_ref, grad_in_ref,
    out_ref, grad_ref, into_ref, in_bias_ref, proj_ref, out_bias_ref, up_ref, up_bias_ref, down_ref, down_bias_ref,
    gain_ref, shift_ref,
):
    seq = core_ref[0]
    layer = pl.program_id(0)
    unit = geo.width // geo.seq_size
    wide, span = 2 * unit, geo.ffn // geo.seq_size
    per_row, per_quarter = geo.width // wide, geo.quarter // span

    def turn(rows, amount):
        return pltpu.roll(rows, (geo.width - amount) % geo.width, 1)

    out_ref[...] = out_in_ref[...]
    grad_ref[...] = grad_in_ref[...]
    up_ref[0] = feed_ref[0, UP]
    down = feed_ref[0, DOWN]
    down_ref[0] = jnp.concatenate([down[:unit], down[unit:]], 1)
    both = attend_ref[0].T
    into_ref[0] = both[:, : 3 * unit]
    proj_ref[0] = both[:, 3 * unit :]
    sums = sums_ref[0]
    narrow = turn(sums, seq * unit)
    out_bias_ref[pl.ds(layer, 1), :] = narrow[OUT_BIAS : OUT_BIAS + 1, :unit]
    down_bias_ref[pl.ds(layer, 1), :] = narrow[DOWN_BIAS : DOWN_BIAS + 1, :unit]
    gain_ref[0] = narrow[GAIN : GAIN + 2, :unit]
    shift_ref[0] = narrow[SHIFT : SHIFT + 2, :unit]
    middle = turn(sums, seq % per_row * wide)
    first = middle[QUERY_BIAS : QUERY_BIAS + 1, :wide]
    second = middle[VALUE_BIAS : VALUE_BIAS + 1, :wide]
    in_bias_ref[pl.ds(layer, 1), :] = jnp.where(seq < per_row, first, second)
    large = turn(sums, seq % per_quarter * span)
    chosen = large[UP_BIAS : UP_BIAS + 1, :span]
    for block in range(1, 4):
        chosen = jnp.where(
            seq // per_quarter == block, large[UP_BIAS + block : UP_BIAS + block + 1, :span], chosen
        )
    up_bias_ref[pl.ds(layer, 1), :] = chosen


def finish(geo, layers, seq, sums, feed_out, attend_out, out_tokens, grad_tokens):
    unit, width = geo.width // geo.seq_size, geo.width
    span = geo.ffn // geo.seq_size
    depth = geo.depth
    shapes = [
        (layers, depth, 3 * unit), (layers, 2 * unit), (layers, depth, unit), (layers, unit),
        (layers, depth, span), (layers, span), (layers, unit, geo.ffn // geo.clip_size),
        (layers, unit), (layers, 2, unit), (layers, 2, unit),
    ]

    def by_layer(shape):
        rest = (0,) * (len(shape) - 1)
        return (1, *shape[1:]), lambda g, c: (g, *rest)

    results = list(call(
        functools.partial(finish_kernel, geo), seq, layers,
        [
            (array, *by_layer(array.shape))
            for array in (sums, feed_out, attend_out, out_tokens, grad_tokens)
        ],
        [(out_tokens.shape, b16, *by_layer(out_tokens.shape))] * 2
        + [
            (shape, f32, *by_layer(shape)) if len(shape) > 2 else full(shape, f32)
            for shape in shapes
        ],
        [], 10**7, 10**7,
    ))
    results[8] = jnp.swapaxes(results[8], 1, 2)
    return results


def build(mesh):
    clip_size, seq_size = mesh.shape["clip"], mesh.shape["seq"]

    def shards(
        tokens, lengths, attn_in, in_bias, attn_out, out_bias, ffn_in, ffn_in_bias,
        ffn_out, ffn_out_bias, norm_gain, norm_bias, cotangent,
    ):
        layers = attn_in.shape[0]
        geo = Geometry(mesh, tokens, ffn_in.shape[2])
        geo.locate()
        held, width, ffn, half, quarter = geo.held, geo.width, geo.ffn, geo.half, geo.quarter
        aligned, core = geo.aligned, geo.core
        seq_at = geo.seq

        weights = (attn_in, attn_out, ffn_in, ffn_out)
        cot_rows, kept = forward(
            geo, layers, tokens, cotangent, lengths, weights,
            (in_bias, out_bias, ffn_in_bias, ffn_out_bias, norm_gain, norm_bias),
        )
        out_tokens, grad_tokens, sums, *results = backward(
            geo, layers, cot_rows, weights, kept, norm_gain, norm_bias
        )
        if aligned:
            seq_arg = jnp.reshape(seq_at, (1,)).astype(jnp.int32)
            return tuple(finish(geo, layers, seq_arg, sums, *results, out_tokens, grad_tokens))

        def swap(array):
            pairs = [(at, at ^ 1) for at in range(clip_size)]
            return lax.ppermute(array, "clip", pairs)

        def spread(array):
            array = lax.psum_scatter(
                array.astype(b16), "seq", scatter_dimension=1, tiled=True
            ).astype(b16)
            return lax.psum_scatter(array, "clip", scatter_dimension=0, tiled=True).astype(f32)

        matrices = []
        for layer in range(layers):
            du, df_t, da_t, dq, dk, dv = results[6 * layer : 6 * layer + 6]
            keep = kept[layer]
            x_all = keep["xall"]
            into = [
                jnp.concatenate([jnp.where(core == 0, a, b), jnp.where(core == 0, b, a)], 1)
                for a, b in (
                    (dot_tn(x_all[: array.shape[0]], array), dot_tn(x_all[: array.shape[0]], swap(array)))
                    for array in (dq, dk, dv)
                )
            ]
            proj = jnp.zeros((CORES, half, width), f32)
            proj = lax.dynamic_update_slice_in_dim(proj, dot(da_t, keep["o"]).T[None], core, 0)
            up = jnp.zeros((2, CORES, width, quarter), f32)
            own_up = dot(keep["hrt"], du).reshape(width, 2, 1, quarter).transpose(1, 2, 0, 3)
            up = lax.dynamic_update_slice_in_dim(up, own_up, core, 1)
            down = jnp.zeros((2, CORES, quarter, width), f32)
            own_down = dot(df_t, keep["act"]).T.reshape(2, 1, quarter, width)
            down = lax.dynamic_update_slice_in_dim(down, own_down, core, 1)
            matrices.append((
                spread(jnp.concatenate(into, 1) * 0.5),
                spread(proj.reshape(width, width)),
                spread(up.transpose(2, 0, 1, 3).reshape(width, ffn)),
                spread(down.reshape(ffn, width)),
            ))
        halves = jnp.arange(SUMS)[None, :, None] >= OUT_BIAS
        summed = lax.psum(jnp.where(halves, 0.5 * sums, sums), ("clip", "seq"))

        def share(row, count):
            piece = summed[:, row : row + count].reshape(layers, count * width)
            size = count * width // seq_size
            return lax.dynamic_slice_in_dim(piece, seq_at * size, size, 1)

        into, proj, up, down = (
            jnp.stack([matrices[layer][which] for layer in range(layers)]) for which in range(4)
        )
        return (
            out_tokens, grad_tokens, into, share(QUERY_BIAS, 2), proj, share(OUT_BIAS, 1),
            up, share(UP_BIAS, 4), down, share(DOWN_BIAS, 1),
            jnp.stack([share(GAIN, 1), share(GAIN + 1, 1)], 1),
            jnp.stack([share(SHIFT, 1), share(SHIFT + 1, 1)], 1),
        )

    return shards


def solution(mesh):
    rowed = P("clip", "seq", None)
    in_specs = (rowed, P("clip")) + (P(),) * 10 + (rowed,)
    out_specs = (
        rowed,
        rowed,
        P(None, "clip", "seq"),
        P(None, "seq"),
        P(None, "clip", "seq"),
        P(None, "seq"),
        P(None, "clip", "seq"),
        P(None, "seq"),
        P(None, "clip", "seq"),
        P(None, "seq"),
        P(None, None, "seq"),
        P(None, None, "seq"),
    )
    return jax.shard_map(
        build(mesh), mesh=mesh, in_specs=in_specs, out_specs=out_specs, check_vma=False
    )
```
